32 devices in a mesh: dp: 16 (over z, y, core), tensor: 2 (over x).
Axes of the slice: x: 2, y: 2, z: 4, core: 2. Of those that a mesh axis runs over, the one named last changes fastest.
Arguments:
- block_input: bfloat16 [4096, 2048], P(('dp', 'tensor')), may hold values from -6 to 6
- segments: int32 [16, 256], P('dp'), may hold values from 0 to 3, never falling along the last dimension, each value on 1 to 128 neighbouring positions
- counts: int32 [16], P('dp'), may hold values from 128 to 256, as said below
- routes: int32 [4096, 6], P('dp'), may hold values from 0 to 15, all different within a row; in each aligned block of 256 rows (0 to 255, 256 to 511, ...) at most 192 rows name the same one
- attn_gain: bfloat16 [2048], P('dp'), may hold values from 0.5 to 1.5
- w_query: bfloat16 [2048, 3072], P('dp', 'tensor'), may hold values from -0.125 to 0.125
- w_latent: bfloat16 [2048, 576], P('dp'), may hold values from -0.125 to 0.125
- latent_gain: bfloat16 [512], P('dp'), may hold values from 0.5 to 1.5
- w_keyval: bfloat16 [512, 4096], P('dp', 'tensor'), may hold values from -0.25 to 0.25
- w_output: bfloat16 [2048, 2048], P('tensor', 'dp'), may hold values from -1.25 to 1.25
- ffn_gain: bfloat16 [2048], P('dp'), may hold values from 0.5 to 1.5
- w_router: bfloat16 [2048, 16], P('dp'), may hold values from -0.15625 to 0.15625
- shared_gate_up: bfloat16 [2, 2048, 2816], P(None, 'dp', 'tensor'), may hold values from -0.125 to 0.125
- shared_down: bfloat16 [2816, 2048], P('tensor', 'dp'), may hold values from -0.109375 to 0.109375
- expert_gate_up: bfloat16 [16, 2, 2048, 1408], P('dp', None, None, 'tensor'), may hold values from -0.125 to 0.125
- expert_down: bfloat16 [16, 1408, 2048], P('dp', 'tensor'), may hold values from -3 to 3
- cotangent: bfloat16 [4096, 2048], P(('dp', 'tensor')), may hold values from -6 to 6
Outputs:
- block_output: float32 [4096, 2048], P(('dp', 'tensor'))
- grad_input: float32 [4096, 2048], P(('dp', 'tensor'))
- grad_attn_gain: float32 [2048], P('dp')
- grad_w_query: float32 [2048, 3072], P('dp', 'tensor')
- grad_w_latent: float32 [2048, 576], P('dp')
- grad_latent_gain: float32 [512], P('dp')
- grad_w_keyval: float32 [512, 4096], P('dp', 'tensor')
- grad_w_output: float32 [2048, 2048], P('tensor', 'dp')
- grad_ffn_gain: float32 [2048], P('dp')
- grad_w_router: float32 [2048, 16], P('dp')
- grad_shared_gate_up: float32 [2, 2048, 2816], P(None, 'dp', 'tensor')
- grad_shared_down: float32 [2816, 2048], P('tensor', 'dp')
- grad_expert_gate_up: float32 [16, 2, 2048, 1408], P('dp', None, None, 'tensor')
- grad_expert_down: float32 [16, 1408, 2048], P('dp', 'tensor')
The draws below stay inside these ranges and needn't reach their ends.
Inputs may be any that keep to these rules, and one draw needn't show every extreme that they name: `routes`: each row names 6 different experts; in each aligned block of 256 rows no expert is named by more than 192 rows, a bound that some block reaches. `segments`: along a row the ids never fall; every id of the range is used in every row. `counts`: some block has all 256 slots live.
All inputs are finite; a program needn't handle non-finite values.
Results may differ from the reference program's by a relative error of at most 0.018.
Values may be sent and summed in bfloat16 or wider, within the bound.
No kernel may reach another device: no remote copies, remote signals or barrier semaphores. Data moves between devices by JAX's collectives and lax.ppermute only.
A program may use at most 384 MiB of HBM per device.

```python
import math
import jax
import jax.numpy as jnp
import numpy as np
from jax import lax

D = 2048
H = 16
NOPE = 128
ROPE = 64
VD = 128
KVR = 512
FE = 1408
FS = 2816
TOP = 6
TOK_DEV = 256
EXPERTS = 16
CAP = 192
TOKENS = 4096
N_DP = 16


def draw_counts(key, part):
    lowest = TOK_DEV // 2
    drawn = jax.random.randint(key, (N_DP,), lowest, TOK_DEV + 1, dtype=jnp.int32)
    chosen = jax.random.randint(jax.random.fold_in(key, 7), (), 0, N_DP, dtype=jnp.int32)
    filled = jnp.arange(N_DP, dtype=jnp.int32) == chosen
    return jnp.where(filled, TOK_DEV, drawn).astype(jnp.int32)


def steps_of(own_key, dims, split, least, largest):
    loudness, own = 1.0, jax.random.fold_in(own_key, 6)
    for dim, blocks in split:
        draws = jnp.exp(jax.random.uniform(jax.random.fold_in(own, dim), (blocks,), jnp.float32, least / len(split), largest / len(split)))
        loudness = loudness * jnp.repeat(draws, dims[dim] // blocks).reshape([-1 if axis == dim else 1 for axis in range(len(dims))])
    return loudness


def length_profile(number_of, total, most, slope):
    loads = [(1 << 20) // math.isqrt(standing ** slope) + 1 for standing in range(2, number_of + 1)]
    spare, given = total - most - (number_of - 1), [1] * (number_of - 1)
    while spare > 0:
        candidates = [i for i in range(number_of - 1) if given[i] < most]
        mass, budget = sum([loads[i] for i in candidates]), spare
        for i in candidates:
            extra = min(most - given[i], max(1, budget * loads[i] // mass), spare)
            given[i] = given[i] + extra
            spare = spare - extra
    return np.array([most] + given)


def uneven(own_key, amount, total, bound, lean):
    if amount == 2:
        one = jax.random.randint(own_key, (), max(1, total - bound), min(bound, total - 1) + 1)
        return jnp.stack([one, total - one])
    tallies = jnp.asarray(length_profile(amount, total, bound, lean), jnp.int32)
    pairs = (amount - 1) // 2
    donor, taker = tallies[1:1 + 2 * pairs:2], tallies[2:2 + 2 * pairs:2]
    room = jnp.minimum(donor - 1, bound - taker)
    moved = jax.random.randint(jax.random.fold_in(own_key, 1), (pairs,), 0, 1 << 20) % (room + 1)
    tallies = tallies.at[1:1 + 2 * pairs:2].set(donor - moved).at[2:2 + 2 * pairs:2].set(taker + moved)
    return tallies[jax.random.permutation(jax.random.fold_in(own_key, 2), amount)]


def routed_block(own_key, own, number, rows, count, top, reach, lean):
    ranking = jax.random.permutation(own_key, count)
    packed, ordinary = shares(count, rows * top, reach, lean, True), shares(count, rows * top, reach, lean, False)
    places = jnp.arange(count)

    def named(sizes, offset_by):
        used = int((sizes > 0).sum())
        fixed = max(1, used // 4)
        passed = fixed + (places - fixed + offset_by * (used - fixed)) % max(1, count - fixed)
        return jnp.zeros((count,), jnp.int32).at[ranking[jnp.where(places < fixed, places, passed)]].set(jnp.asarray(sizes, jnp.int32))

    sizes = jnp.where(number % 4 == 0, named(packed, number // 4), named(ordinary, number - number // 4 - 1))
    mixed = jax.random.permutation(jax.random.fold_in(own, 3), count)
    donor, taker = mixed[0:count // 2 * 2:2], mixed[1:count // 2 * 2:2]
    margin = jnp.minimum(sizes[donor] - 1, reach - sizes[taker]) // 2
    margin = jnp.where((donor == ranking[0]) | (taker == ranking[0]) | (sizes[taker] == 0), 0, jnp.maximum(margin, 0))
    passed = jax.random.randint(jax.random.fold_in(own, 4), (count // 2,), 0, 1 << 20) % (margin + 1)
    sizes = sizes.at[donor].add(-passed).at[taker].add(passed)
    members = jnp.searchsorted(jnp.cumsum(sizes), jnp.arange(rows * top), side="right").astype(jnp.int32)
    grid = members.reshape(top, rows).T
    grid = grid[jax.random.permutation(jax.random.fold_in(own, 1), rows)]
    offset_by = jax.random.randint(jax.random.fold_in(own, 2), (rows, 1), 0, top)
    return jnp.take_along_axis(grid, (jnp.arange(top)[None, :] + offset_by) % top, axis=1)


def shares(number_of, total, limit, lean, full):
    loads = [(1 << 20) // math.isqrt(standing ** lean) + 1 for standing in range(1, number_of + 1)]
    largest = limit if full else min(limit, max(-(-total // number_of), total * loads[0] // sum(loads)))
    least = 1 if total - largest >= number_of - 1 else 0
    given, surplus = [largest] + [least] * (number_of - 1), total - largest - least * (number_of - 1)
    while surplus > 0:
        candidates = [i for i in range(1, number_of) if given[i] < largest] or [i for i in range(1, number_of) if given[i] < limit]
        pool, remaining = sum([loads[i] for i in candidates]), surplus
        for i in candidates:
            more = min(limit - given[i], max(1, remaining * loads[i] // pool), surplus)
            given[i] = given[i] + more
            surplus = surplus - more
    return np.array(given)


def scatter_about(stream_key, shape, deviation, reach, split=(), kind=jnp.bfloat16):
    values = jax.random.normal(stream_key, shape, jnp.float32) * deviation
    if len(split) > 0:
        values = steps_of(stream_key, shape, split, -0.22, 0.18) * values
    return jnp.clip(values, min=-reach, max=reach).astype(kind)


def setup_inputs(seed: int = 0) -> dict:
    splits = jax.random.split(jax.random.key(seed), 18)
    block_input = scatter_about(splits[0], (TOKENS, D), 1.0, 6.0, ((0, 32),))
    segments = jax.vmap(lambda own: jnp.searchsorted(jnp.cumsum(uneven(own, 4, TOK_DEV, TOK_DEV // 2, 2)), jnp.arange(TOK_DEV), side="right"))(jax.random.split(splits[1], N_DP)).reshape((N_DP, TOK_DEV)).astype(jnp.int32)
    counts = draw_counts(jax.random.fold_in(splits[17], 71), 0)
    routes_keys = jax.random.split(jax.random.fold_in(splits[3], 1), TOKENS // TOK_DEV)
    routes_turns = jax.random.permutation(jax.random.fold_in(splits[3], 3), TOKENS // TOK_DEV)
    routes = jax.vmap(lambda own, number: routed_block(jax.random.fold_in(splits[3], 2), own, number, TOK_DEV, EXPERTS, TOP, CAP, 2))(routes_keys, routes_turns).reshape((TOKENS, TOP))
    attn_gain = jnp.clip(1.0 + 0.1 * jax.random.normal(splits[4], (D,), jnp.float32), 0.5, 1.5).astype(jnp.bfloat16)
    w_query = scatter_about(splits[5], (D, H * (NOPE + ROPE)), D ** -0.5, 0.125, ((0, 16), (1, 2)))
    w_latent = scatter_about(splits[6], (D, KVR + ROPE), D ** -0.5, 0.125, ((0, 16),))
    latent_gain = jnp.clip(1.0 + 0.1 * jax.random.normal(splits[7], (KVR,), jnp.float32), 0.5, 1.5).astype(jnp.bfloat16)
    w_keyval = scatter_about(splits[8], (KVR, H * (NOPE + VD)), KVR ** -0.5, 0.25, ((0, 16), (1, 2)))
    w_output = scatter_about(splits[9], (H * VD, D), (4.0 / (H * VD) ** 0.5), 1.25, ((0, 2), (1, 16)))
    ffn_gain = jnp.clip(1.0 + 0.1 * jax.random.normal(splits[10], (D,), jnp.float32), 0.5, 1.5).astype(jnp.bfloat16)
    w_router = scatter_about(splits[11], (D, EXPERTS), (0.5 / D ** 0.5), 0.15625, ((0, 16),))
    shared_gate_up = scatter_about(splits[12], (2, D, FS), D ** -0.5, 0.125, ((1, 16), (2, 2)))
    shared_down = scatter_about(splits[13], (FS, D), FS ** -0.5, 0.109375, ((0, 2), (1, 16)))
    expert_gate_up = scatter_about(splits[14], (EXPERTS, 2, D, FE), D ** -0.5, 0.125, ((0, 16), (3, 2)))
    expert_down = scatter_about(splits[15], (EXPERTS, FE, D), (EXPERTS / (2.0 * FE ** 0.5)), 3.0, ((0, 16), (1, 2)))
    cotangent = scatter_about(splits[16], (TOKENS, D), 1.0, 6.0, ((0, 32),))
    return {"block_input": block_input, "segments": segments, "counts": counts, "routes": routes, "attn_gain": attn_gain, "w_query": w_query, "w_latent": w_latent, "latent_gain": latent_gain, "w_keyval": w_keyval, "w_output": w_output, "ffn_gain": ffn_gain, "w_router": w_router, "shared_gate_up": shared_gate_up, "shared_down": shared_down, "expert_gate_up": expert_gate_up, "expert_down": expert_down, "cotangent": cotangent}


EPSILON = 1e-06
HIGHEST = lax.Precision.HIGHEST

@jax.custom_vjp
def low(v):
    return lax.optimization_barrier(v.astype(jnp.bfloat16)).astype(jnp.float32)

@jax.custom_vjp
def low_back(v):
    return v

def low_keep(v):
    return (low(v), None)

def low_pass(kept, grad):
    return (grad,)

def back_keep(v):
    return (v, None)

def back_low(kept, grad):
    return (low(grad),)
low.defvjp(low_keep, low_pass)
low_back.defvjp(back_keep, back_low)

def rounded_both(values):
    return low(low_back(values))

def rms_scale(values):
    return lax.rsqrt(lax.optimization_barrier(jnp.mean(values * values, axis=-1, keepdims=True)) + EPSILON)

def rotary_tables(segment_row, width):
    count = segment_row.shape[0]
    position = jnp.arange(count, dtype=jnp.int32)
    same = segment_row[:, None] == segment_row[None, :]
    start = lax.optimization_barrier(jnp.min(jnp.where(same, position[None, :], count), axis=1)).astype(jnp.int32)
    offset = (position - start).astype(jnp.float32)
    freq = jnp.exp(jnp.arange(width // 2, dtype=jnp.float32) * (-2.0 * math.log(10000.0) / width))
    angle = offset[:, None] * freq[None, :]
    return (jnp.cos(angle), jnp.sin(angle))

def rotate(values, cosine, sine):
    half = values.shape[-1] // 2
    first = values[..., :half]
    second = values[..., half:]
    return jnp.concatenate([first * cosine - second * sine, second * cosine + first * sine], axis=-1)

def allowed_pairs(segment_row, count):
    position = jnp.arange(segment_row.shape[0], dtype=jnp.int32)
    live = position < count
    same = segment_row[:, None] == segment_row[None, :]
    causal = position[None, :] <= position[:, None]
    return same & causal & live[:, None] & live[None, :] | (position[:, None] == position[None, :])

def slot_tables(routes):
    blocks = routes.reshape(N_DP, TOK_DEV * TOP)
    expert_ids = jnp.arange(EXPERTS, dtype=jnp.int32)

    def block_slots(flat):
        onehot = (flat[:, None] == expert_ids[None, :]).astype(jnp.int32)
        before = jnp.cumsum(onehot, axis=0).astype(jnp.int32) - onehot
        return lax.optimization_barrier(jnp.sum(before * onehot, axis=1)).astype(jnp.int32)
    slots = jax.vmap(block_slots)(blocks)
    block_ids = jnp.arange(N_DP, dtype=jnp.int32)[:, None]
    target = (blocks * (N_DP * CAP) + block_ids * CAP + slots).astype(jnp.int32)
    token_ids = (block_ids * TOK_DEV + jnp.arange(TOK_DEV * TOP, dtype=jnp.int32)[None, :] // TOP).astype(jnp.int32)
    owner = jnp.full((EXPERTS * N_DP * CAP,), TOKENS, jnp.int32).at[target.reshape(-1)].set(token_ids.reshape(-1))
    return (target.reshape(TOKENS, TOP), owner.reshape(EXPERTS, N_DP * CAP))

def reference(block_input, segments, counts, routes, attn_gain, w_query, w_latent, latent_gain, w_keyval, w_output, ffn_gain, w_router, shared_gate_up, shared_down, expert_gate_up, expert_down, cotangent):
    target, owner = slot_tables(routes)
    cosine, sine = jax.vmap(lambda row: rotary_tables(row, ROPE))(segments)
    cosine = cosine.reshape(TOKENS, ROPE // 2)
    sine = sine.reshape(TOKENS, ROPE // 2)
    scale = (NOPE + ROPE) ** (-0.5)

    def attend(block):
        query_rows, key_nope, key_rope, values, segment_row, count = block
        allowed = allowed_pairs(segment_row, count)
        raw = jnp.einsum('ihd,jhd->hij', query_rows[..., :NOPE], key_nope, precision=HIGHEST)
        raw = raw + jnp.einsum('ihd,jd->hij', query_rows[..., NOPE:], key_rope, precision=HIGHEST)
        scores = jnp.where(allowed[None], low_back(raw * scale), -1e+30)
        row_max = lax.optimization_barrier(jnp.max(scores, axis=-1, keepdims=True))
        log_total = row_max + jnp.log(lax.optimization_barrier(jnp.sum(jnp.exp(scores - row_max), axis=-1, keepdims=True)))
        weights = jnp.exp(scores - log_total)
        return jnp.einsum('hij,jhd->ihd', low(weights), values, precision=HIGHEST)

    def forward(inputs, gain_attn, query_weight, latent_weight, gain_latent, keyval_weight, output_weight, gain_ffn, router_weight, shared_in, shared_out, expert_in, expert_out):
        first_unit = inputs * rms_scale(inputs)
        first_normed = low(first_unit * gain_attn)
        query = low_back(jnp.dot(first_normed, query_weight, precision=HIGHEST)).reshape(TOKENS, H, NOPE + ROPE)
        query_rows = low(jnp.concatenate([query[..., :NOPE], rotate(query[..., NOPE:], cosine[:, None, :], sine[:, None, :])], axis=-1))
        latent_all = low_back(jnp.dot(first_normed, latent_weight, precision=HIGHEST))
        latent = latent_all[:, :KVR]
        key_rope = low(rotate(latent_all[:, KVR:], cosine, sine))
        latent_normed = low(latent * rms_scale(latent) * gain_latent)
        keyval = rounded_both(jnp.dot(latent_normed, keyval_weight, precision=HIGHEST)).reshape(TOKENS, H, NOPE + VD)
        attended = lax.map(jax.checkpoint(attend), (query_rows.reshape(N_DP, TOK_DEV, H, NOPE + ROPE), keyval[..., :NOPE].reshape(N_DP, TOK_DEV, H, NOPE), key_rope.reshape(N_DP, TOK_DEV, ROPE), keyval[..., NOPE:].reshape(N_DP, TOK_DEV, H, VD), segments, counts))
        attended = rounded_both(attended.reshape(TOKENS, H * VD))
        mixed = inputs + low_back(jnp.dot(attended, output_weight, precision=HIGHEST))
        second_normed = low(mixed * rms_scale(mixed) * gain_ffn)
        logits = low_back(jnp.dot(second_normed, router_weight, precision=HIGHEST))
        probabilities = jax.nn.softmax(logits, axis=-1)
        gate_values = jnp.take_along_axis(probabilities, routes, axis=1)
        shared_pre = low_back(jnp.einsum('td,gdf->tgf', second_normed, shared_in, precision=HIGHEST))
        shared_hidden = low(jax.nn.silu(shared_pre[:, 0]) * shared_pre[:, 1])
        shared_term = low_back(jnp.dot(shared_hidden, shared_out, precision=HIGHEST))
        gate_slots = jnp.zeros((EXPERTS * N_DP * CAP,), jnp.float32).at[target.reshape(-1)].set(gate_values.reshape(-1)).reshape(EXPERTS, N_DP * CAP)
        padded_rows = jnp.concatenate([second_normed, jnp.zeros((1, D), jnp.float32)], axis=0)

        def expert(item):
            rows_index, weight_in, weight_out = item
            rows = padded_rows[rows_index]
            expert_pre = low_back(jnp.einsum('rd,gdf->rgf', rows, weight_in, precision=HIGHEST))
            expert_hidden = low(jax.nn.silu(expert_pre[:, 0]) * expert_pre[:, 1])
            return low_back(jnp.dot(expert_hidden, weight_out, precision=HIGHEST))
        expert_results = lax.map(jax.checkpoint(expert), (owner, expert_in, expert_out))
        weighted = (gate_slots[..., None] * expert_results).reshape(-1, D)
        routed = jnp.zeros((TOKENS + 1, D), jnp.float32).at[owner.reshape(-1)].add(weighted)[:TOKENS]
        return mixed + shared_term + routed
    floats = (block_input, attn_gain, w_query, w_latent, latent_gain, w_keyval, w_output, ffn_gain, w_router, shared_gate_up, shared_down, expert_gate_up, expert_down)
    floats = tuple((value.astype(jnp.float32) for value in floats))
    block_output, pullback = jax.vjp(forward, *floats)
    grads = pullback(cotangent.astype(jnp.float32))
    return (block_output, grads[0], grads[1], grads[2], grads[3], grads[4], grads[5], grads[6], grads[7], grads[8], grads[9], grads[10], grads[11], grads[12])
```

```python
import functools
import math

import jax
import jax.numpy as jnp
from jax import lax
from jax.experimental import pallas as pl
from jax.experimental.pallas import tpu as pltpu
from jax.sharding import PartitionSpec as P

D = 2048
NOPE = 128
ROPE = 64
VD = 128
KVR = 512
TOP = 6


EPSILON = 1e-06


def rms_scale(values):
    return lax.rsqrt(jnp.mean(values * values, axis=-1, keepdims=True) + EPSILON)


def rms_back(grad_unit, unit_rows, row_scale):
    return row_scale * (
        grad_unit - unit_rows * jnp.mean(grad_unit * unit_rows, axis=-1, keepdims=True)
    )


def rotary_tables(segment_row, width):
    count = segment_row.shape[0]
    position = jnp.arange(count, dtype=jnp.int32)
    same = segment_row[:, None] == segment_row[None, :]
    start = jnp.min(jnp.where(same, position[None, :], count), axis=1)
    offset = (position - start).astype(jnp.float32)
    freq = jnp.exp(jnp.arange(width // 2, dtype=jnp.float32) * (-2.0 * math.log(10000.0) / width))
    angle = offset[:, None] * freq[None, :]
    return (jnp.cos(angle), jnp.sin(angle))


def rotate(values, cosine, sine):
    half = values.shape[-1] // 2
    first = values[..., :half]
    second = values[..., half:]
    return jnp.concatenate(
        [first * cosine - second * sine, second * cosine + first * sine], axis=-1
    )


def rotate_back(grads, cosine, sine):
    half = grads.shape[-1] // 2
    first = grads[..., :half]
    second = grads[..., half:]
    return jnp.concatenate(
        [first * cosine + second * sine, second * cosine - first * sine], axis=-1
    )


def allowed_pairs(segment_row, count):
    position = jnp.arange(segment_row.shape[0], dtype=jnp.int32)
    live = position < count
    same = segment_row[:, None] == segment_row[None, :]
    causal = position[None, :] <= position[:, None]
    return same & causal & live[:, None] & live[None, :] | (position[:, None] == position[None, :])


def attention_scores(query_rows, key_nope, key_rope, allowed, scale):
    scores = jnp.einsum(
        "ihd,jhd->hij", query_rows[..., :NOPE], key_nope, preferred_element_type=jnp.float32
    )
    scores = scores + jnp.einsum(
        "ihd,jd->hij", query_rows[..., NOPE:], key_rope, preferred_element_type=jnp.float32
    )
    return jnp.where(allowed[None], scores * scale, -1e30)


def swiglu_back(gate, upper, grad_hidden, axis):
    sigmoid = jax.nn.sigmoid(gate)
    grad_gate = grad_hidden * upper * sigmoid * (1.0 + gate * (1.0 - sigmoid))
    grad_upper = grad_hidden * gate * sigmoid
    return jnp.stack([grad_gate, grad_upper], axis=axis)


def slot_layout(routes, experts, capacity):
    tokens = routes.shape[0]
    flat = routes.reshape(-1)
    onehot = (flat[:, None] == jnp.arange(experts, dtype=jnp.int32)[None, :]).astype(jnp.int32)
    rank = jnp.arange(flat.shape[0], dtype=jnp.int32)
    earlier = (rank[None, :] < rank[:, None]).astype(jnp.bfloat16)
    before = jnp.dot(
        earlier, onehot.astype(jnp.bfloat16), preferred_element_type=jnp.float32
    ).astype(jnp.int32)
    slot_index = jnp.sum(before * onehot, axis=1)
    target = flat * capacity + slot_index
    token_ids = jnp.arange(flat.shape[0], dtype=jnp.int32) // routes.shape[1]
    owner = jnp.full((experts * capacity,), tokens, jnp.int32).at[target].set(token_ids)
    return (slot_index, target, owner)


def to_expert_major(arrived, groups, local_experts):
    capacity = arrived.shape[1]
    width = arrived.shape[2]
    return (
        arrived.reshape(groups, local_experts, capacity, width)
        .transpose(1, 0, 2, 3)
        .reshape(local_experts, groups * capacity, width)
    )


def from_expert_major(results, groups):
    local_experts = results.shape[0]
    width = results.shape[2]
    capacity = results.shape[1] // groups
    return (
        results.reshape(local_experts, groups, capacity, width)
        .transpose(1, 0, 2, 3)
        .reshape(groups * local_experts, capacity, width)
    )


def exchange_body(
    block_input,
    segments,
    counts,
    routes,
    attn_gain,
    w_query,
    w_latent,
    latent_gain,
    w_keyval,
    w_output,
    ffn_gain,
    w_router,
    shared_gate_up,
    shared_down,
    expert_gate_up,
    expert_down,
    cotangent,
):
    gathered = (
        lax.all_gather(attn_gain, "dp", axis=0, tiled=True),
        lax.all_gather(w_query, "dp", axis=0, tiled=True),
        lax.all_gather(w_latent, "dp", axis=0, tiled=True),
        lax.all_gather(latent_gain, "dp", axis=0, tiled=True),
        lax.all_gather(w_keyval, "dp", axis=0, tiled=True),
        lax.all_gather(w_output, "dp", axis=1, tiled=True),
        lax.all_gather(ffn_gain, "dp", axis=0, tiled=True),
        lax.all_gather(w_router, "dp", axis=0, tiled=True),
        lax.all_gather(shared_gate_up, "dp", axis=1, tiled=True),
        lax.all_gather(shared_down, "dp", axis=1, tiled=True),
    )
    (
        full_attn_gain,
        query_weight,
        latent_weight,
        full_latent_gain,
        keyval_weight,
        output_weight,
        full_ffn_gain,
        router_weight,
        shared_in,
        shared_out,
    ) = gathered
    tensor_rank = lax.axis_index("tensor")
    dp_size = lax.axis_size("dp")
    rows_all = lax.all_gather(block_input, "tensor", axis=0, tiled=True)
    tokens = rows_all.shape[0]
    local_rows = block_input.shape[0]
    heads = query_weight.shape[1] // (NOPE + ROPE)
    experts = router_weight.shape[1]
    local_experts = expert_gate_up.shape[0]
    capacity = 2 * tokens * TOP // experts
    scale = (NOPE + ROPE) ** (-0.5)
    start = tensor_rank * local_rows
    cosine, sine = rotary_tables(segments[0], ROPE)
    allowed = allowed_pairs(segments[0], counts[0])
    attn_gain_wide = full_attn_gain.astype(jnp.float32)
    latent_gain_wide = full_latent_gain.astype(jnp.float32)
    ffn_gain_wide = full_ffn_gain.astype(jnp.float32)
    inputs = rows_all.astype(jnp.float32)
    first_scale = rms_scale(inputs)
    first_unit = inputs * first_scale
    first_normed = (first_unit * attn_gain_wide).astype(jnp.bfloat16)
    query = jnp.dot(first_normed, query_weight, preferred_element_type=jnp.float32).reshape(
        tokens, heads, NOPE + ROPE
    )
    query_rows = jnp.concatenate(
        [query[..., :NOPE], rotate(query[..., NOPE:], cosine[:, None, :], sine[:, None, :])],
        axis=-1,
    ).astype(jnp.bfloat16)
    latent_all = jnp.dot(first_normed, latent_weight, preferred_element_type=jnp.float32)
    latent = latent_all[:, :KVR]
    key_rope = rotate(latent_all[:, KVR:], cosine, sine).astype(jnp.bfloat16)
    latent_scale = rms_scale(latent)
    latent_unit = latent * latent_scale
    latent_normed = (latent_unit * latent_gain_wide).astype(jnp.bfloat16)
    keyval = (
        jnp.dot(latent_normed, keyval_weight, preferred_element_type=jnp.float32)
        .astype(jnp.bfloat16)
        .reshape(tokens, heads, NOPE + VD)
    )
    key_nope = keyval[..., :NOPE]
    values = keyval[..., NOPE:]
    scores = attention_scores(query_rows, key_nope, key_rope, allowed, scale)
    row_max = jnp.max(scores, axis=-1, keepdims=True)
    log_total = row_max + jnp.log(jnp.sum(jnp.exp(scores - row_max), axis=-1, keepdims=True))
    weights_low = jnp.exp(scores - log_total).astype(jnp.bfloat16)
    attended = (
        jnp.einsum("hij,jhd->ihd", weights_low, values, preferred_element_type=jnp.float32)
        .astype(jnp.bfloat16)
        .reshape(tokens, heads * VD)
    )
    attn_part = jnp.dot(attended, output_weight, preferred_element_type=jnp.float32)
    mixed = inputs + lax.psum(attn_part, "tensor")
    second_scale = rms_scale(mixed)
    second_unit = mixed * second_scale
    second_normed = (second_unit * ffn_gain_wide).astype(jnp.bfloat16)
    logits = jnp.dot(second_normed, router_weight, preferred_element_type=jnp.float32)
    probabilities = jax.nn.softmax(logits, axis=-1)
    gate_values = jnp.take_along_axis(probabilities, routes, axis=1)
    shared_pre = jnp.einsum(
        "td,gdf->tgf", second_normed, shared_in, preferred_element_type=jnp.float32
    )
    shared_hidden = (jax.nn.silu(shared_pre[:, 0]) * shared_pre[:, 1]).astype(jnp.bfloat16)
    shared_part = jnp.dot(shared_hidden, shared_out, preferred_element_type=jnp.float32)
    slot_index, target, owner = slot_layout(routes, experts, capacity)
    owner_grid = owner.reshape(experts, capacity)
    padded_rows = jnp.concatenate([second_normed, jnp.zeros((1, D), jnp.bfloat16)], axis=0)
    outgoing = padded_rows[owner_grid]
    arrived = lax.all_to_all(outgoing, "dp", split_axis=0, concat_axis=0, tiled=True)
    expert_rows = to_expert_major(arrived, dp_size, local_experts)
    expert_pre = jnp.einsum(
        "erd,egdf->ergf", expert_rows, expert_gate_up, preferred_element_type=jnp.float32
    )
    expert_hidden = (jax.nn.silu(expert_pre[:, :, 0]) * expert_pre[:, :, 1]).astype(jnp.bfloat16)
    expert_result = jnp.einsum(
        "erf,efd->erd", expert_hidden, expert_down, preferred_element_type=jnp.float32
    )
    returning = from_expert_major(expert_result, dp_size)
    returned = lax.all_to_all(
        returning.astype(jnp.bfloat16), "dp", split_axis=0, concat_axis=0, tiled=True
    ).astype(returning.dtype)
    padded_back = jnp.concatenate([returned.reshape(-1, D), jnp.zeros((1, D), jnp.float32)], axis=0)
    picked = padded_back[target].reshape(tokens, TOP, D)
    routed_part = jnp.sum(gate_values[:, :, None] * picked, axis=1)
    branch_sum = lax.psum_scatter(
        (shared_part + routed_part).astype(jnp.bfloat16), "tensor", scatter_dimension=0, tiled=True
    ).astype(jnp.float32)
    block_output = lax.dynamic_slice_in_dim(mixed, start, local_rows, 0) + branch_sum
    grad_rows = lax.all_gather(cotangent, "tensor", axis=0, tiled=True)
    grad_out = grad_rows.astype(jnp.float32)
    grad_shared_hidden = jnp.dot(grad_rows, shared_out.T, preferred_element_type=jnp.float32)
    grad_shared_out = jnp.dot(shared_hidden.T, grad_rows, preferred_element_type=jnp.float32)
    grad_shared_pre = swiglu_back(shared_pre[:, 0], shared_pre[:, 1], grad_shared_hidden, 1).astype(
        jnp.bfloat16
    )
    grad_shared_in = jnp.einsum(
        "td,tgf->gdf", second_normed, grad_shared_pre, preferred_element_type=jnp.float32
    )
    grad_second = jnp.einsum(
        "tgf,gdf->td", grad_shared_pre, shared_in, preferred_element_type=jnp.float32
    )
    gate_by_slot = (
        jnp.zeros((experts * capacity + 1,), jnp.float32).at[target].set(gate_values.reshape(-1))
    )
    slot_ids = jnp.arange(experts * capacity, dtype=jnp.int32).reshape(experts, capacity)
    padded_grad = jnp.concatenate([grad_out, jnp.zeros((1, D), jnp.float32)], axis=0)
    grad_outgoing = (gate_by_slot[slot_ids][..., None] * padded_grad[owner_grid]).astype(
        jnp.bfloat16
    )
    grad_arrived = lax.all_to_all(grad_outgoing, "dp", split_axis=0, concat_axis=0, tiled=True)
    grad_expert_rows = to_expert_major(grad_arrived, dp_size, local_experts)
    grad_expert_hidden = jnp.einsum(
        "erd,efd->erf", grad_expert_rows, expert_down, preferred_element_type=jnp.float32
    )
    grad_expert_down = jnp.einsum(
        "erf,erd->efd", expert_hidden, grad_expert_rows, preferred_element_type=jnp.float32
    )
    grad_expert_pre = swiglu_back(
        expert_pre[:, :, 0], expert_pre[:, :, 1], grad_expert_hidden, 2
    ).astype(jnp.bfloat16)
    grad_expert_gate_up = jnp.einsum(
        "erd,ergf->egdf", expert_rows, grad_expert_pre, preferred_element_type=jnp.float32
    )
    grad_expert_input = jnp.einsum(
        "ergf,egdf->erd", grad_expert_pre, expert_gate_up, preferred_element_type=jnp.float32
    )
    grad_returning = from_expert_major(grad_expert_input, dp_size)
    grad_returned = lax.all_to_all(
        grad_returning.astype(jnp.bfloat16), "dp", split_axis=0, concat_axis=0, tiled=True
    ).astype(grad_returning.dtype)
    padded_grad_back = jnp.concatenate(
        [grad_returned.reshape(-1, D), jnp.zeros((1, D), jnp.float32)], axis=0
    )
    grad_second = grad_second + jnp.sum(padded_grad_back[target].reshape(tokens, TOP, D), axis=1)
    grad_gates = jnp.sum(grad_out[:, None, :] * picked, axis=-1)
    grad_second, grad_gates = (
        lax.psum(grad_second.astype(jnp.bfloat16), "tensor").astype(jnp.float32),
        lax.psum(grad_gates.astype(jnp.bfloat16), "tensor").astype(jnp.float32),
    )
    chosen = (routes[:, :, None] == jnp.arange(experts, dtype=jnp.int32)[None, None, :]).astype(
        jnp.float32
    )
    grad_probabilities = jnp.sum(chosen * grad_gates[:, :, None], axis=1)
    grad_logits = probabilities * (
        grad_probabilities - jnp.sum(probabilities * grad_probabilities, axis=-1, keepdims=True)
    )
    grad_logits_low = grad_logits.astype(jnp.bfloat16)
    grad_router = jnp.dot(second_normed.T, grad_logits_low, preferred_element_type=jnp.float32)
    grad_second = grad_second + jnp.dot(
        grad_logits_low, router_weight.T, preferred_element_type=jnp.float32
    )
    gain_ffn_grad = jnp.sum(grad_second * second_unit, axis=0)
    grad_mixed = grad_out + rms_back(grad_second * ffn_gain_wide, second_unit, second_scale)
    grad_attn_low = grad_mixed.astype(jnp.bfloat16)
    grad_output_weight = jnp.dot(attended.T, grad_attn_low, preferred_element_type=jnp.float32)
    grad_attended = (
        jnp.dot(grad_attn_low, output_weight.T, preferred_element_type=jnp.float32)
        .astype(jnp.bfloat16)
        .reshape(tokens, heads, VD)
    )
    scores = attention_scores(query_rows, key_nope, key_rope, allowed, scale)
    weights = jnp.exp(scores - log_total)
    weights_low = weights.astype(jnp.bfloat16)
    grad_weights = jnp.einsum(
        "ihd,jhd->hij", grad_attended, values, preferred_element_type=jnp.float32
    )
    grad_values = jnp.einsum(
        "hij,ihd->jhd", weights_low, grad_attended, preferred_element_type=jnp.float32
    )
    grad_scores = (
        weights * (grad_weights - jnp.sum(weights * grad_weights, axis=-1, keepdims=True))
    ).astype(jnp.bfloat16)
    grad_query_nope = (
        jnp.einsum("hij,jhd->ihd", grad_scores, key_nope, preferred_element_type=jnp.float32)
        * scale
    )
    grad_query_rope = (
        jnp.einsum("hij,jd->ihd", grad_scores, key_rope, preferred_element_type=jnp.float32) * scale
    )
    grad_key_nope = (
        jnp.einsum(
            "hij,ihd->jhd", grad_scores, query_rows[..., :NOPE], preferred_element_type=jnp.float32
        )
        * scale
    )
    grad_key_rope = (
        jnp.einsum(
            "hij,ihd->jd", grad_scores, query_rows[..., NOPE:], preferred_element_type=jnp.float32
        )
        * scale
    )
    grad_query = (
        jnp.concatenate(
            [grad_query_nope, rotate_back(grad_query_rope, cosine[:, None, :], sine[:, None, :])],
            axis=-1,
        )
        .astype(jnp.bfloat16)
        .reshape(tokens, heads * (NOPE + ROPE))
    )
    grad_query_weight = jnp.dot(first_normed.T, grad_query, preferred_element_type=jnp.float32)
    grad_first = jnp.dot(grad_query, query_weight.T, preferred_element_type=jnp.float32)
    grad_keyval = (
        jnp.concatenate([grad_key_nope, grad_values], axis=-1)
        .astype(jnp.bfloat16)
        .reshape(tokens, heads * (NOPE + VD))
    )
    grad_keyval_weight = jnp.dot(latent_normed.T, grad_keyval, preferred_element_type=jnp.float32)
    grad_latent_normed = jnp.dot(grad_keyval, keyval_weight.T, preferred_element_type=jnp.float32)
    gain_latent_part = jnp.sum(grad_latent_normed * latent_unit, axis=0)
    grad_latent = rms_back(grad_latent_normed * latent_gain_wide, latent_unit, latent_scale)
    grad_latent_all = jnp.concatenate(
        [grad_latent, rotate_back(grad_key_rope, cosine, sine)], axis=-1
    )
    grad_first, grad_latent_all, gain_latent_grad = (
        lax.psum(grad_first.astype(jnp.bfloat16), "tensor").astype(jnp.float32),
        lax.psum(grad_latent_all.astype(jnp.bfloat16), "tensor").astype(jnp.float32),
        lax.psum(gain_latent_part.astype(jnp.bfloat16), "tensor").astype(jnp.float32),
    )
    grad_latent_low = grad_latent_all.astype(jnp.bfloat16)
    grad_latent_weight = jnp.dot(
        first_normed.T, grad_latent_low, preferred_element_type=jnp.float32
    )
    grad_first = grad_first + jnp.dot(
        grad_latent_low, latent_weight.T, preferred_element_type=jnp.float32
    )
    gain_attn_grad = jnp.sum(grad_first * first_unit, axis=0)
    grad_inputs = grad_mixed + rms_back(grad_first * attn_gain_wide, first_unit, first_scale)
    grad_local = lax.dynamic_slice_in_dim(grad_inputs, start, local_rows, 0)
    summed = (
        lax.psum_scatter(gain_attn_grad, "dp", scatter_dimension=0, tiled=True),
        lax.psum_scatter(grad_query_weight, "dp", scatter_dimension=0, tiled=True),
        lax.psum_scatter(grad_latent_weight, "dp", scatter_dimension=0, tiled=True),
        lax.psum_scatter(gain_latent_grad, "dp", scatter_dimension=0, tiled=True),
        lax.psum_scatter(grad_keyval_weight, "dp", scatter_dimension=0, tiled=True),
        lax.psum_scatter(grad_output_weight, "dp", scatter_dimension=1, tiled=True),
        lax.psum_scatter(gain_ffn_grad, "dp", scatter_dimension=0, tiled=True),
        lax.psum_scatter(grad_router, "dp", scatter_dimension=0, tiled=True),
        lax.psum_scatter(grad_shared_in, "dp", scatter_dimension=1, tiled=True),
        lax.psum_scatter(grad_shared_out, "dp", scatter_dimension=1, tiled=True),
    )
    return (
        block_output,
        grad_local,
        summed[0],
        summed[1],
        summed[2],
        summed[3],
        summed[4],
        summed[5],
        summed[6],
        summed[7],
        summed[8],
        summed[9],
        grad_expert_gate_up,
        grad_expert_down,
    )


RINGS = 4


def ring_step(values):
    return lax.ppermute(values, "dp", [(i, (i + RINGS) % 16) for i in range(16)])


def other_y(values):
    return lax.ppermute(values, "dp", [(i, i ^ 2) for i in range(16)])


def other_core(values):
    return lax.ppermute(values, "dp", [(i, i ^ 1) for i in range(16)])


def other_x(values):
    return lax.ppermute(values, "tensor", [(0, 1), (1, 0)])


def gather_rows(rows):
    half = rows.shape[0] // 2
    planes = []
    current = rows
    for distance in range(RINGS):
        if distance:
            current = ring_step(current)
        beside = other_y(current)
        across = other_x(current)
        plane = jnp.concatenate(
            [current, beside, across, other_y(across[:half]), other_x(beside[half:])], axis=0
        )
        planes.append((plane, other_core(plane)))
    return planes


def add_low(first, second):
    return (first.astype(jnp.float32) + second.astype(jnp.float32)).astype(jnp.bfloat16)


def plane_sum(mine, theirs):
    size = mine.shape[0] // 4
    half = size // 2
    total = add_low(mine, other_core(theirs))
    own, beside, across = total[:size], total[size : 2 * size], total[2 * size : 3 * size]
    corner_y = other_y(total[3 * size : 3 * size + half])
    corner_x = other_x(total[3 * size + half :])
    across = jnp.concatenate([add_low(across[:half], corner_y), across[half:]], axis=0)
    beside = jnp.concatenate([beside[:half], add_low(beside[half:], corner_x)], axis=0)
    return (
        own.astype(jnp.float32)
        + other_x(across).astype(jnp.float32)
        + other_y(beside).astype(jnp.float32)
    )


def ring_sum(parts):
    moving = parts[1]
    for distance in (2, 3, 0):
        moving = ring_step(moving.astype(jnp.bfloat16)).astype(jnp.float32) + parts[distance]
    return moving


def gather_weight(shard):
    chunks = []
    current = shard
    for distance in range(RINGS):
        if distance:
            current = ring_step(current)
        beside = other_y(current)
        for flip_y, chunk in ((0, current), (1, beside)):
            for flip_core, piece in ((0, chunk), (1, other_core(chunk))):
                chunks.append(((distance, flip_y, flip_core), piece))
    return chunks


def place_of(coords, key):
    z, y, core = coords
    distance, flip_y, flip_core = key
    return (
        lax.rem(z + RINGS - distance, RINGS) * 4
        + (1 - y if flip_y else y) * 2
        + (1 - core if flip_core else core)
    )


def place_kernel(keys, moves, coords_ref, *refs):
    chunks = refs[: len(keys)]
    outs = refs[len(keys) : -1]
    semaphores = refs[-1]
    coords = (coords_ref[0], coords_ref[1], coords_ref[2])
    copies = []
    for key, chunk in zip(keys, chunks):
        block = place_of(coords, key)
        for source_rows, source_columns, out, rows, columns in moves:
            start = pl.multiple_of(block * rows, rows)
            copies.append(
                pltpu.make_async_copy(
                    chunk.at[source_rows, source_columns],
                    outs[out].at[pl.ds(start, rows), columns],
                    semaphores.at[len(copies)],
                )
            )
    for copy in copies:
        copy.start()
    for copy in copies:
        copy.wait()


def place_chunks(coords, chunks, moves, shapes):
    keys = [key for key, _ in chunks]
    anywhere = pl.BlockSpec(memory_space=pl.ANY)
    return pl.pallas_call(
        functools.partial(place_kernel, keys, moves),
        out_shape=[jax.ShapeDtypeStruct(shape, jnp.bfloat16) for shape in shapes],
        in_specs=[pl.BlockSpec(memory_space=pltpu.SMEM)] + [anywhere] * len(chunks),
        out_specs=[anywhere] * len(shapes),
        scratch_shapes=[pltpu.SemaphoreType.DMA((len(chunks) * len(moves),))],
        cost_estimate=pl.CostEstimate(
            flops=0,
            bytes_accessed=4 * sum(shape[0] * shape[1] for shape in shapes),
            transcendentals=0,
        ),
    )(coords, *[piece for _, piece in chunks])


def weight_keys():
    return [
        (distance, flip_y, flip_core)
        for flip_core in (0, 1)
        for flip_y in (0, 1)
        for distance in range(RINGS)
    ]


def scatter_weight(grads):
    half = grads.shape[0] // 2
    total = add_low(grads[:half], other_core(grads[half:]))
    quarter = half // 2
    total = total[:quarter].astype(jnp.float32) + other_y(total[quarter:]).astype(jnp.float32)
    size = quarter // RINGS
    return ring_sum([total[r * size : (r + 1) * size] for r in range(RINGS)])


def attend_forward(query_rows, key_nope, key_rope, values, allowed, scale):
    scores = attention_scores(query_rows, key_nope, key_rope, allowed, scale)
    row_max = jnp.max(scores, axis=-1, keepdims=True)
    log_total = row_max + jnp.log(jnp.sum(jnp.exp(scores - row_max), axis=-1, keepdims=True))
    weights_low = jnp.exp(scores - log_total).astype(jnp.bfloat16)
    attended = jnp.einsum("hij,jhd->ihd", weights_low, values, preferred_element_type=jnp.float32)
    return attended.astype(jnp.bfloat16), log_total


def wide_dot(left, right):
    return jnp.dot(left, right, preferred_element_type=jnp.float32)


def dot_turned(left, right):
    return lax.dot_general(left, right, (((1,), (1,)), ((), ())), preferred_element_type=jnp.float32)


def dot_rows(left, right):
    return lax.dot_general(left, right, (((0,), (0,)), ((), ())), preferred_element_type=jnp.float32)


def mlp_rows(rows, grad_rows, routed, expert, sizes, gate_weight, up_weight, down_weight):
    units, shared, experts = sizes
    width = gate_weight.shape[1]
    pre_gate = wide_dot(rows, gate_weight)
    pre_up = wide_dot(rows, up_weight)
    down_grad = dot_turned(grad_rows, down_weight)
    column = lax.broadcasted_iota(jnp.int32, (1, width), 1)
    logits = pre_gate[:, units + shared : units + shared + experts]
    probabilities = jax.nn.softmax(logits, axis=-1)
    mine = lax.broadcasted_iota(jnp.int32, (1, experts), 1) == expert
    gate = routed[:, None] * jnp.sum(jnp.where(mine, probabilities, 0.0), axis=1, keepdims=True)
    sigmoid = jax.nn.sigmoid(pre_gate)
    hidden = (pre_gate * sigmoid * pre_up).astype(jnp.bfloat16).astype(jnp.float32)
    scale = jnp.where(column < units, gate, jnp.where(column < units + shared, 1.0, 0.0))
    scaled_hidden = (scale * hidden).astype(jnp.bfloat16)
    grad_gate_value = jnp.sum(
        jnp.where(column < units, hidden * down_grad, 0.0), axis=1, keepdims=True
    )
    grad_hidden = scale * down_grad
    grad_gate = grad_hidden * pre_up * sigmoid * (1.0 + pre_gate * (1.0 - sigmoid))
    grad_up = (grad_hidden * pre_gate * sigmoid).astype(jnp.bfloat16)
    grad_logits = (gate * grad_gate_value) * (jnp.where(mine, 1.0, 0.0) - probabilities)
    grad_logits = jnp.pad(
        grad_logits, ((0, 0), (units + shared, width - units - shared - experts))
    )
    router_column = (column >= units + shared) & (column < units + shared + experts)
    grad_gate = jnp.where(router_column, grad_logits, grad_gate).astype(jnp.bfloat16)
    out = wide_dot(scaled_hidden, down_weight).astype(jnp.bfloat16)
    grad_input = (dot_turned(grad_gate, gate_weight) + dot_turned(grad_up, up_weight)).astype(
        jnp.bfloat16
    )
    return scaled_hidden, grad_gate, grad_up, out, grad_input


def gather_body(
    block_input,
    segments,
    counts,
    routes,
    attn_gain,
    w_query,
    w_latent,
    latent_gain,
    w_keyval,
    w_output,
    ffn_gain,
    w_router,
    shared_gate_up,
    shared_down,
    expert_gate_up,
    expert_down,
    cotangent,
):
    f32 = jnp.float32
    bf16 = jnp.bfloat16
    blocks = 16
    index = lax.axis_index("dp")
    x = lax.axis_index("tensor")
    coords = jnp.stack([index // 4, (index // 2) % 2, index % 2]).astype(jnp.int32)
    z, y, core = coords[0], coords[1], coords[2]
    local_rows = block_input.shape[0]
    tokens = 2 * local_rows
    depth = w_query.shape[0]
    query_width = w_query.shape[1]
    heads = query_width // (NOPE + ROPE)
    experts = w_router.shape[1]
    units = expert_gate_up.shape[3]
    shared = shared_gate_up.shape[2] // blocks
    width = -(-(units + shared + experts) // 128) * 128
    latent_depth = w_keyval.shape[0]
    scale = (NOPE + ROPE) ** (-0.5)

    def both_halves(own, other):
        return jnp.concatenate(
            [jnp.where(x == 0, own, other), jnp.where(x == 0, other, own)], axis=0
        )

    small = jnp.concatenate(
        [
            attn_gain[:, None],
            ffn_gain[:, None],
            w_router,
            jnp.pad(latent_gain, (0, depth - latent_depth))[:, None],
            routes.reshape(depth, -1).astype(bf16),
        ],
        axis=1,
    )
    small = lax.all_gather(small, "dp", axis=0, tiled=True)
    attn_gain_wide = small[:, 0].astype(f32)
    ffn_gain_wide = small[:, 1].astype(f32)
    router_weight = small[:, 2 : 2 + experts]
    latent_gain_wide = (
        small[:, 2 + experts].reshape(blocks, depth)[:, :latent_depth].reshape(-1).astype(f32)
    )
    routes_all = small[:, 3 + experts :].reshape(blocks * tokens, TOP)
    routed_all = jnp.any(routes_all == index.astype(bf16), axis=1).astype(f32)
    order = jnp.stack(
        [
            place_of(coords, (distance, flip_y, flip_core)) * 2 + (1 - x if flip_x else x)
            for distance in range(RINGS)
            for flip_core in (0, 1)
            for flip_x, flip_y in ((0, 0), (0, 1), (1, 0), (1, 1))
        ]
    )
    routed = routed_all.reshape(blocks * 2, local_rows)[order].reshape(
        RINGS, 2, 4 * local_rows
    )

    rows_all = both_halves(block_input, other_x(block_input))
    first_chunks = gather_weight(jnp.concatenate([w_query, w_latent], axis=1))
    parts = depth // latent_depth
    keyval_part = w_keyval.shape[1] // parts
    keyval_packed = (
        w_keyval.reshape(latent_depth, parts, keyval_part).transpose(1, 0, 2).reshape(depth, -1)
    )
    second_chunks = gather_weight(jnp.concatenate([keyval_packed, w_output.T], axis=1))
    (first_weight,) = place_chunks(
        coords,
        first_chunks,
        [(pl.ds(0, depth), pl.ds(0, query_width + KVR + ROPE), 0, depth, pl.ds(0, query_width + KVR + ROPE))],
        [(D, query_width + KVR + ROPE)],
    )
    keyval_weight, output_turned = place_chunks(
        coords,
        second_chunks,
        [
            (
                pl.ds(k * latent_depth, latent_depth),
                pl.ds(0, keyval_part),
                0,
                latent_depth,
                pl.ds(k * keyval_part, keyval_part),
            )
            for k in range(parts)
        ]
        + [
            (
                pl.ds(0, depth),
                pl.ds(keyval_part, w_output.shape[0]),
                1,
                depth,
                pl.ds(0, w_output.shape[0]),
            )
        ],
        [(KVR, w_keyval.shape[1]), (D, w_output.shape[0])],
    )

    shared_in = lax.all_to_all(
        shared_gate_up.reshape(2, depth, blocks, shared).transpose(2, 0, 1, 3).reshape(
            blocks, 2 * depth, shared
        ),
        "dp",
        split_axis=0,
        concat_axis=0,
        tiled=True,
    ).reshape(blocks, 2, depth, shared)
    shared_out = lax.all_to_all(
        shared_down.reshape(blocks, shared, depth),
        "dp",
        split_axis=0,
        concat_axis=0,
        tiled=True,
    )
    shared_gate = shared_in[:, 0].reshape(D, shared)
    shared_up = shared_in[:, 1].reshape(D, shared)
    spare = width - units - shared
    gate_weight = jnp.concatenate(
        [
            expert_gate_up[0, 0],
            shared_gate,
            router_weight,
            jnp.zeros((D, spare - experts), bf16),
        ],
        axis=1,
    )
    up_weight = jnp.concatenate(
        [expert_gate_up[0, 1], shared_up, jnp.zeros((D, spare), bf16)], axis=1
    )
    down_weight = jnp.concatenate(
        [
            expert_down[0],
            shared_out.transpose(1, 0, 2).reshape(shared, D),
            jnp.zeros((spare, D), bf16),
        ],
        axis=0,
    )

    cosine, sine = rotary_tables(segments[0], ROPE)
    allowed = allowed_pairs(segments[0], counts[0])
    inputs = rows_all.astype(f32)
    first_scale = rms_scale(inputs)
    first_unit = inputs * first_scale
    first_normed = (first_unit * attn_gain_wide).astype(bf16)
    projected = wide_dot(first_normed, first_weight)
    query = projected[:, :query_width].reshape(tokens, heads, NOPE + ROPE)
    query_rows = jnp.concatenate(
        [query[..., :NOPE], rotate(query[..., NOPE:], cosine[:, None, :], sine[:, None, :])],
        axis=-1,
    ).astype(bf16)
    latent = projected[:, query_width : query_width + KVR]
    key_rope = rotate(projected[:, query_width + KVR :], cosine, sine).astype(bf16)
    latent_scale = rms_scale(latent)
    latent_unit = latent * latent_scale
    latent_normed = (latent_unit * latent_gain_wide).astype(bf16)
    keyval = wide_dot(latent_normed, keyval_weight).astype(bf16).reshape(tokens, heads, NOPE + VD)
    key_nope = keyval[..., :NOPE]
    values = keyval[..., NOPE:]
    attended, log_total = attend_forward(query_rows, key_nope, key_rope, values, allowed, scale)
    attended = attended.reshape(tokens, heads * VD)
    attn_part = dot_turned(attended, output_turned)
    low_rows, high_rows = attn_part[:local_rows], attn_part[local_rows:]
    own_part = jnp.where(x == 0, low_rows, high_rows)
    sent_part = jnp.where(x == 0, high_rows, low_rows).astype(bf16)
    mixed = block_input.astype(f32) + own_part + other_x(sent_part).astype(f32)
    second_scale = rms_scale(mixed)
    second_unit = mixed * second_scale
    second_normed = (second_unit * ffn_gain_wide).astype(bf16)

    grad_planes = gather_rows(cotangent)
    row_planes = gather_rows(second_normed)
    hiddens, gate_grads, up_grads, grad_sums, out_sums = [], [], [], [], []
    for distance in range(RINGS):
        results = [
            mlp_rows(
                row_planes[distance][side],
                grad_planes[distance][side],
                routed[distance, side],
                index,
                (units, shared, experts),
                gate_weight,
                up_weight,
                down_weight,
            )
            for side in (0, 1)
        ]
        for side in (0, 1):
            hiddens.append(results[side][0])
            gate_grads.append(results[side][1])
            up_grads.append(results[side][2])
        out_sums.append(plane_sum(results[0][3], results[1][3]))
        grad_sums.append(plane_sum(results[0][4], results[1][4]))
    grad_second = ring_sum(grad_sums)
    block_output = mixed + ring_sum(out_sums)

    every_row = jnp.concatenate([plane for pair in row_planes for plane in pair], axis=0)
    every_grad = jnp.concatenate([plane for pair in grad_planes for plane in pair], axis=0)
    every_hidden = jnp.concatenate(hiddens, axis=0)
    every_gate_grad = jnp.concatenate(gate_grads, axis=0)
    every_up_grad = jnp.concatenate(up_grads, axis=0)
    grad_expert_gate_up = jnp.stack(
        [
            dot_rows(every_row, every_gate_grad[:, :units]),
            dot_rows(every_row, every_up_grad[:, :units]),
        ]
    )[None]
    side_grads = dot_rows(
        every_row, jnp.concatenate([every_gate_grad[:, units:], every_up_grad[:, units:]], axis=1)
    )
    spare_width = width - units
    grad_router = side_grads[:, shared : shared + experts]
    shared_in_grads = jnp.stack(
        [side_grads[:, :shared], side_grads[:, spare_width : spare_width + shared]]
    )
    grad_expert_down = dot_rows(every_hidden[:, :units], every_grad)[None]
    shared_down_grads = dot_rows(every_hidden[:, units:], every_grad)[:shared]
    grad_shared_in = (
        lax.all_to_all(
            shared_in_grads.astype(bf16)
            .reshape(2, blocks, depth, shared)
            .transpose(1, 0, 2, 3)
            .reshape(blocks, 2 * depth, shared),
            "dp",
            split_axis=0,
            concat_axis=0,
            tiled=True,
        )
        .astype(f32)
        .reshape(blocks, 2, depth, shared)
        .transpose(1, 2, 0, 3)
        .reshape(2, depth, blocks * shared)
    )
    grad_shared_down = (
        lax.all_to_all(
            shared_down_grads.astype(bf16).reshape(shared, blocks, depth).transpose(1, 0, 2),
            "dp",
            split_axis=0,
            concat_axis=0,
            tiled=True,
        )
        .astype(f32)
        .reshape(blocks * shared, depth)
    )

    gain_ffn_part = jnp.sum(grad_second * second_unit, axis=0)
    grad_mixed = cotangent.astype(f32) + rms_back(
        grad_second * ffn_gain_wide, second_unit, second_scale
    )
    grad_mixed_low = grad_mixed.astype(bf16)
    grad_attn = both_halves(grad_mixed_low, other_x(grad_mixed_low))

    keys = weight_keys()
    places = [place_of(coords, key) for key in keys]

    def in_key_order(values):
        return jnp.concatenate(
            [lax.dynamic_slice_in_dim(values, place * depth, depth, 1) for place in places], axis=1
        )

    grad_output_weight = scatter_weight(
        dot_rows(in_key_order(grad_attn), attended).astype(bf16)
    ).T
    grad_attended = (
        wide_dot(grad_attn, output_turned).astype(bf16).reshape(tokens, heads, VD)
    )
    scores = attention_scores(query_rows, key_nope, key_rope, allowed, scale)
    weights = jnp.exp(scores - log_total)
    weights_low = weights.astype(bf16)
    grad_weights = jnp.einsum("ihd,jhd->hij", grad_attended, values, preferred_element_type=f32)
    grad_values = jnp.einsum("hij,ihd->jhd", weights_low, grad_attended, preferred_element_type=f32)
    grad_scores = (
        weights * (grad_weights - jnp.sum(weights * grad_weights, axis=-1, keepdims=True))
    ).astype(bf16)
    grad_query_nope = scale * jnp.einsum(
        "hij,jhd->ihd", grad_scores, key_nope, preferred_element_type=f32
    )
    grad_query_rope = scale * jnp.einsum(
        "hij,jd->ihd", grad_scores, key_rope, preferred_element_type=f32
    )
    grad_key_nope = scale * jnp.einsum(
        "hij,ihd->jhd", grad_scores, query_rows[..., :NOPE], preferred_element_type=f32
    )
    grad_key_rope = scale * jnp.einsum(
        "hij,ihd->jd", grad_scores, query_rows[..., NOPE:], preferred_element_type=f32
    )
    grad_query = (
        jnp.concatenate(
            [grad_query_nope, rotate_back(grad_query_rope, cosine[:, None, :], sine[:, None, :])],
            axis=-1,
        )
        .astype(bf16)
        .reshape(tokens, heads * (NOPE + ROPE))
    )
    grad_keyval = (
        jnp.concatenate([grad_key_nope, grad_values], axis=-1)
        .astype(bf16)
        .reshape(tokens, heads * (NOPE + VD))
    )
    key_order = jnp.stack(places)
    latent_column = jnp.arange(KVR, dtype=jnp.int32)
    wanted = key_order[latent_column // latent_depth] * latent_depth + latent_column % latent_depth
    shuffle = (latent_column[:, None] == wanted[None, :]).astype(bf16)
    latent_in_order = wide_dot(latent_normed, shuffle).astype(bf16)
    grad_keyval_weight = scatter_weight(dot_rows(latent_in_order, grad_keyval).astype(bf16))
    grad_latent_normed = dot_turned(grad_keyval, keyval_weight)
    gain_latent_part = jnp.sum(grad_latent_normed * latent_unit, axis=0)
    grad_latent = rms_back(grad_latent_normed * latent_gain_wide, latent_unit, latent_scale)
    grad_latent_all = jnp.concatenate(
        [grad_latent, rotate_back(grad_key_rope, cosine, sine)], axis=-1
    ).astype(bf16)
    grad_projected = jnp.concatenate([grad_query, grad_latent_all], axis=1)
    grad_first_weight = scatter_weight(
        dot_rows(in_key_order(first_normed), grad_projected).astype(bf16)
    )
    grad_latent_part = grad_first_weight[:, query_width:]
    grad_latent_weight = grad_latent_part + other_x(grad_latent_part)
    grad_first_part = dot_turned(grad_projected, first_weight)
    low_rows, high_rows = grad_first_part[:local_rows], grad_first_part[local_rows:]
    sent_part = jnp.where(x == 0, high_rows, low_rows).astype(bf16)
    grad_first = jnp.where(x == 0, low_rows, high_rows) + other_x(sent_part).astype(f32)
    own_inputs = block_input.astype(f32)
    own_scale = rms_scale(own_inputs)
    own_unit = own_inputs * own_scale
    gain_attn_part = jnp.sum(grad_first * own_unit, axis=0)
    grad_input = grad_mixed + rms_back(grad_first * attn_gain_wide, own_unit, own_scale)

    small_grads = jnp.concatenate(
        [
            gain_attn_part.reshape(blocks, 1, depth),
            gain_ffn_part.reshape(blocks, 1, depth),
            grad_router.reshape(blocks, experts, depth),
            jnp.pad(
                gain_latent_part.reshape(blocks, 1, latent_depth),
                ((0, 0), (0, 0), (0, depth - latent_depth)),
            ),
        ],
        axis=1,
    )
    small_grads = lax.dynamic_index_in_dim(
        lax.psum(small_grads, ("dp", "tensor")), index, 0, keepdims=False
    )
    return (
        block_output,
        grad_input,
        small_grads[0],
        grad_first_weight[:, :query_width],
        grad_latent_weight,
        small_grads[2 + experts, :latent_depth],
        grad_keyval_weight,
        grad_output_weight,
        small_grads[1],
        small_grads[2 : 2 + experts].reshape(depth, experts),
        grad_shared_in,
        grad_shared_down,
        grad_expert_gate_up,
        grad_expert_down,
    )


def solution(mesh):
    in_specs = (
        P(("dp", "tensor"), None),
        P("dp", None),
        P("dp"),
        P("dp", None),
        P("dp"),
        P("dp", "tensor"),
        P("dp", None),
        P("dp"),
        P("dp", "tensor"),
        P("tensor", "dp"),
        P("dp"),
        P("dp", None),
        P(None, "dp", "tensor"),
        P("tensor", "dp"),
        P("dp", None, None, "tensor"),
        P("dp", "tensor", None),
        P(("dp", "tensor"), None),
    )
    out_specs = (
        P(("dp", "tensor"), None),
        P(("dp", "tensor"), None),
        P("dp"),
        P("dp", "tensor"),
        P("dp", None),
        P("dp"),
        P("dp", "tensor"),
        P("tensor", "dp"),
        P("dp"),
        P("dp", None),
        P(None, "dp", "tensor"),
        P("tensor", "dp"),
        P("dp", None, None, "tensor"),
        P("dp", "tensor", None),
    )
    body = gather_body if mesh.shape["dp"] == 16 else exchange_body
    return jax.shard_map(body, mesh=mesh, in_specs=in_specs, out_specs=out_specs, check_vma=False)
```

```python
import functools
import math

import jax
import jax.numpy as jnp
from jax import lax
from jax.experimental import pallas as pl
from jax.experimental.pallas import tpu as pltpu
from jax.sharding import PartitionSpec as P

D = 2048
NOPE = 128
ROPE = 64
VD = 128
KVR = 512
TOP = 6


EPSILON = 1e-06


def rms_scale(values):
    return lax.rsqrt(jnp.mean(values * values, axis=-1, keepdims=True) + EPSILON)


def rms_back(grad_unit, unit_rows, row_scale):
    return row_scale * (
        grad_unit - unit_rows * jnp.mean(grad_unit * unit_rows, axis=-1, keepdims=True)
    )


def rotary_tables(segment_row, width):
    count = segment_row.shape[0]
    position = jnp.arange(count, dtype=jnp.int32)
    same = segment_row[:, None] == segment_row[None, :]
    start = jnp.min(jnp.where(same, position[None, :], count), axis=1)
    offset = (position - start).astype(jnp.float32)
    freq = jnp.exp(jnp.arange(width // 2, dtype=jnp.float32) * (-2.0 * math.log(10000.0) / width))
    angle = offset[:, None] * freq[None, :]
    return (jnp.cos(angle), jnp.sin(angle))


def rotate(values, cosine, sine):
    half = values.shape[-1] // 2
    first = values[..., :half]
    second = values[..., half:]
    return jnp.concatenate(
        [first * cosine - second * sine, second * cosine + first * sine], axis=-1
    )


def rotate_back(grads, cosine, sine):
    half = grads.shape[-1] // 2
    first = grads[..., :half]
    second = grads[..., half:]
    return jnp.concatenate(
        [first * cosine + second * sine, second * cosine - first * sine], axis=-1
    )


def allowed_pairs(segment_row, count):
    position = jnp.arange(segment_row.shape[0], dtype=jnp.int32)
    live = position < count
    same = segment_row[:, None] == segment_row[None, :]
    causal = position[None, :] <= position[:, None]
    return same & causal & live[:, None] & live[None, :] | (position[:, None] == position[None, :])


def attention_scores(query_rows, key_nope, key_rope, allowed, scale):
    scores = jnp.einsum(
        "ihd,jhd->hij", query_rows[..., :NOPE], key_nope, preferred_element_type=jnp.float32
    )
    scores = scores + jnp.einsum(
        "ihd,jd->hij", query_rows[..., NOPE:], key_rope, preferred_element_type=jnp.float32
    )
    return jnp.where(allowed[None], scores * scale, -1e30)


def swiglu_back(gate, upper, grad_hidden, axis):
    sigmoid = jax.nn.sigmoid(gate)
    grad_gate = grad_hidden * upper * sigmoid * (1.0 + gate * (1.0 - sigmoid))
    grad_upper = grad_hidden * gate * sigmoid
    return jnp.stack([grad_gate, grad_upper], axis=axis)


def slot_layout(routes, experts, capacity):
    tokens = routes.shape[0]
    flat = routes.reshape(-1)
    onehot = (flat[:, None] == jnp.arange(experts, dtype=jnp.int32)[None, :]).astype(jnp.int32)
    rank = jnp.arange(flat.shape[0], dtype=jnp.int32)
    earlier = (rank[None, :] < rank[:, None]).astype(jnp.bfloat16)
    before = jnp.dot(
        earlier, onehot.astype(jnp.bfloat16), preferred_element_type=jnp.float32
    ).astype(jnp.int32)
    slot_index = jnp.sum(before * onehot, axis=1)
    target = flat * capacity + slot_index
    token_ids = jnp.arange(flat.shape[0], dtype=jnp.int32) // routes.shape[1]
    owner = jnp.full((experts * capacity,), tokens, jnp.int32).at[target].set(token_ids)
    return (slot_index, target, owner)


def to_expert_major(arrived, groups, local_experts):
    capacity = arrived.shape[1]
    width = arrived.shape[2]
    return (
        arrived.reshape(groups, local_experts, capacity, width)
        .transpose(1, 0, 2, 3)
        .reshape(local_experts, groups * capacity, width)
    )


def from_expert_major(results, groups):
    local_experts = results.shape[0]
    width = results.shape[2]
    capacity = results.shape[1] // groups
    return (
        results.reshape(local_experts, groups, capacity, width)
        .transpose(1, 0, 2, 3)
        .reshape(groups * local_experts, capacity, width)
    )


def exchange_body(
    block_input,
    segments,
    counts,
    routes,
    attn_gain,
    w_query,
    w_latent,
    latent_gain,
    w_keyval,
    w_output,
    ffn_gain,
    w_router,
    shared_gate_up,
    shared_down,
    expert_gate_up,
    expert_down,
    cotangent,
):
    gathered = (
        lax.all_gather(attn_gain, "dp", axis=0, tiled=True),
        lax.all_gather(w_query, "dp", axis=0, tiled=True),
        lax.all_gather(w_latent, "dp", axis=0, tiled=True),
        lax.all_gather(latent_gain, "dp", axis=0, tiled=True),
        lax.all_gather(w_keyval, "dp", axis=0, tiled=True),
        lax.all_gather(w_output, "dp", axis=1, tiled=True),
        lax.all_gather(ffn_gain, "dp", axis=0, tiled=True),
        lax.all_gather(w_router, "dp", axis=0, tiled=True),
        lax.all_gather(shared_gate_up, "dp", axis=1, tiled=True),
        lax.all_gather(shared_down, "dp", axis=1, tiled=True),
    )
    (
        full_attn_gain,
        query_weight,
        latent_weight,
        full_latent_gain,
        keyval_weight,
        output_weight,
        full_ffn_gain,
        router_weight,
        shared_in,
        shared_out,
    ) = gathered
    tensor_rank = lax.axis_index("tensor")
    dp_size = lax.axis_size("dp")
    rows_all = lax.all_gather(block_input, "tensor", axis=0, tiled=True)
    tokens = rows_all.shape[0]
    local_rows = block_input.shape[0]
    heads = query_weight.shape[1] // (NOPE + ROPE)
    experts = router_weight.shape[1]
    local_experts = expert_gate_up.shape[0]
    capacity = 2 * tokens * TOP // experts
    scale = (NOPE + ROPE) ** (-0.5)
    start = tensor_rank * local_rows
    cosine, sine = rotary_tables(segments[0], ROPE)
    allowed = allowed_pairs(segments[0], counts[0])
    attn_gain_wide = full_attn_gain.astype(jnp.float32)
    latent_gain_wide = full_latent_gain.astype(jnp.float32)
    ffn_gain_wide = full_ffn_gain.astype(jnp.float32)
    inputs = rows_all.astype(jnp.float32)
    first_scale = rms_scale(inputs)
    first_unit = inputs * first_scale
    first_normed = (first_unit * attn_gain_wide).astype(jnp.bfloat16)
    query = jnp.dot(first_normed, query_weight, preferred_element_type=jnp.float32).reshape(
        tokens, heads, NOPE + ROPE
    )
    query_rows = jnp.concatenate(
        [query[..., :NOPE], rotate(query[..., NOPE:], cosine[:, None, :], sine[:, None, :])],
        axis=-1,
    ).astype(jnp.bfloat16)
    latent_all = jnp.dot(first_normed, latent_weight, preferred_element_type=jnp.float32)
    latent = latent_all[:, :KVR]
    key_rope = rotate(latent_all[:, KVR:], cosine, sine).astype(jnp.bfloat16)
    latent_scale = rms_scale(latent)
    latent_unit = latent * latent_scale
    latent_normed = (latent_unit * latent_gain_wide).astype(jnp.bfloat16)
    keyval = (
        jnp.dot(latent_normed, keyval_weight, preferred_element_type=jnp.float32)
        .astype(jnp.bfloat16)
        .reshape(tokens, heads, NOPE + VD)
    )
    key_nope = keyval[..., :NOPE]
    values = keyval[..., NOPE:]
    scores = attention_scores(query_rows, key_nope, key_rope, allowed, scale)
    row_max = jnp.max(scores, axis=-1, keepdims=True)
    log_total = row_max + jnp.log(jnp.sum(jnp.exp(scores - row_max), axis=-1, keepdims=True))
    weights_low = jnp.exp(scores - log_total).astype(jnp.bfloat16)
    attended = (
        jnp.einsum("hij,jhd->ihd", weights_low, values, preferred_element_type=jnp.float32)
        .astype(jnp.bfloat16)
        .reshape(tokens, heads * VD)
    )
    attn_part = jnp.dot(attended, output_weight, preferred_element_type=jnp.float32)
    mixed = inputs + lax.psum(attn_part, "tensor")
    second_scale = rms_scale(mixed)
    second_unit = mixed * second_scale
    second_normed = (second_unit * ffn_gain_wide).astype(jnp.bfloat16)
    logits = jnp.dot(second_normed, router_weight, preferred_element_type=jnp.float32)
    probabilities = jax.nn.softmax(logits, axis=-1)
    gate_values = jnp.take_along_axis(probabilities, routes, axis=1)
    shared_pre = jnp.einsum(
        "td,gdf->tgf", second_normed, shared_in, preferred_element_type=jnp.float32
    )
    shared_hidden = (jax.nn.silu(shared_pre[:, 0]) * shared_pre[:, 1]).astype(jnp.bfloat16)
    shared_part = jnp.dot(shared_hidden, shared_out, preferred_element_type=jnp.float32)
    slot_index, target, owner = slot_layout(routes, experts, capacity)
    owner_grid = owner.reshape(experts, capacity)
    padded_rows = jnp.concatenate([second_normed, jnp.zeros((1, D), jnp.bfloat16)], axis=0)
    outgoing = padded_rows[owner_grid]
    arrived = lax.all_to_all(outgoing, "dp", split_axis=0, concat_axis=0, tiled=True)
    expert_rows = to_expert_major(arrived, dp_size, local_experts)
    expert_pre = jnp.einsum(
        "erd,egdf->ergf", expert_rows, expert_gate_up, preferred_element_type=jnp.float32
    )
    expert_hidden = (jax.nn.silu(expert_pre[:, :, 0]) * expert_pre[:, :, 1]).astype(jnp.bfloat16)
    expert_result = jnp.einsum(
        "erf,efd->erd", expert_hidden, expert_down, preferred_element_type=jnp.float32
    )
    returning = from_expert_major(expert_result, dp_size)
    returned = lax.all_to_all(
        returning.astype(jnp.bfloat16), "dp", split_axis=0, concat_axis=0, tiled=True
    ).astype(returning.dtype)
    padded_back = jnp.concatenate([returned.reshape(-1, D), jnp.zeros((1, D), jnp.float32)], axis=0)
    picked = padded_back[target].reshape(tokens, TOP, D)
    routed_part = jnp.sum(gate_values[:, :, None] * picked, axis=1)
    branch_sum = lax.psum_scatter(
        (shared_part + routed_part).astype(jnp.bfloat16), "tensor", scatter_dimension=0, tiled=True
    ).astype(jnp.float32)
    block_output = lax.dynamic_slice_in_dim(mixed, start, local_rows, 0) + branch_sum
    grad_rows = lax.all_gather(cotangent, "tensor", axis=0, tiled=True)
    grad_out = grad_rows.astype(jnp.float32)
    grad_shared_hidden = jnp.dot(grad_rows, shared_out.T, preferred_element_type=jnp.float32)
    grad_shared_out = jnp.dot(shared_hidden.T, grad_rows, preferred_element_type=jnp.float32)
    grad_shared_pre = swiglu_back(shared_pre[:, 0], shared_pre[:, 1], grad_shared_hidden, 1).astype(
        jnp.bfloat16
    )
    grad_shared_in = jnp.einsum(
        "td,tgf->gdf", second_normed, grad_shared_pre, preferred_element_type=jnp.float32
    )
    grad_second = jnp.einsum(
        "tgf,gdf->td", grad_shared_pre, shared_in, preferred_element_type=jnp.float32
    )
    gate_by_slot = (
        jnp.zeros((experts * capacity + 1,), jnp.float32).at[target].set(gate_values.reshape(-1))
    )
    slot_ids = jnp.arange(experts * capacity, dtype=jnp.int32).reshape(experts, capacity)
    padded_grad = jnp.concatenate([grad_out, jnp.zeros((1, D), jnp.float32)], axis=0)
    grad_outgoing = (gate_by_slot[slot_ids][..., None] * padded_grad[owner_grid]).astype(
        jnp.bfloat16
    )
    grad_arrived = lax.all_to_all(grad_outgoing, "dp", split_axis=0, concat_axis=0, tiled=True)
    grad_expert_rows = to_expert_major(grad_arrived, dp_size, local_experts)
    grad_expert_hidden = jnp.einsum(
        "erd,efd->erf", grad_expert_rows, expert_down, preferred_element_type=jnp.float32
    )
    grad_expert_down = jnp.einsum(
        "erf,erd->efd", expert_hidden, grad_expert_rows, preferred_element_type=jnp.float32
    )
    grad_expert_pre = swiglu_back(
        expert_pre[:, :, 0], expert_pre[:, :, 1], grad_expert_hidden, 2
    ).astype(jnp.bfloat16)
    grad_expert_gate_up = jnp.einsum(
        "erd,ergf->egdf", expert_rows, grad_expert_pre, preferred_element_type=jnp.float32
    )
    grad_expert_input = jnp.einsum(
        "ergf,egdf->erd", grad_expert_pre, expert_gate_up, preferred_element_type=jnp.float32
    )
    grad_returning = from_expert_major(grad_expert_input, dp_size)
    grad_returned = lax.all_to_all(
        grad_returning.astype(jnp.bfloat16), "dp", split_axis=0, concat_axis=0, tiled=True
    ).astype(grad_returning.dtype)
    padded_grad_back = jnp.concatenate(
        [grad_returned.reshape(-1, D), jnp.zeros((1, D), jnp.float32)], axis=0
    )
    grad_second = grad_second + jnp.sum(padded_grad_back[target].reshape(tokens, TOP, D), axis=1)
    grad_gates = jnp.sum(grad_out[:, None, :] * picked, axis=-1)
    grad_second, grad_gates = (
        lax.psum(grad_second.astype(jnp.bfloat16), "tensor").astype(jnp.float32),
        lax.psum(grad_gates.astype(jnp.bfloat16), "tensor").astype(jnp.float32),
    )
    chosen = (routes[:, :, None] == jnp.arange(experts, dtype=jnp.int32)[None, None, :]).astype(
        jnp.float32
    )
    grad_probabilities = jnp.sum(chosen * grad_gates[:, :, None], axis=1)
    grad_logits = probabilities * (
        grad_probabilities - jnp.sum(probabilities * grad_probabilities, axis=-1, keepdims=True)
    )
    grad_logits_low = grad_logits.astype(jnp.bfloat16)
    grad_router = jnp.dot(second_normed.T, grad_logits_low, preferred_element_type=jnp.float32)
    grad_second = grad_second + jnp.dot(
        grad_logits_low, router_weight.T, preferred_element_type=jnp.float32
    )
    gain_ffn_grad = jnp.sum(grad_second * second_unit, axis=0)
    grad_mixed = grad_out + rms_back(grad_second * ffn_gain_wide, second_unit, second_scale)
    grad_attn_low = grad_mixed.astype(jnp.bfloat16)
    grad_output_weight = jnp.dot(attended.T, grad_attn_low, preferred_element_type=jnp.float32)
    grad_attended = (
        jnp.dot(grad_attn_low, output_weight.T, preferred_element_type=jnp.float32)
        .astype(jnp.bfloat16)
        .reshape(tokens, heads, VD)
    )
    scores = attention_scores(query_rows, key_nope, key_rope, allowed, scale)
    weights = jnp.exp(scores - log_total)
    weights_low = weights.astype(jnp.bfloat16)
    grad_weights = jnp.einsum(
        "ihd,jhd->hij", grad_attended, values, preferred_element_type=jnp.float32
    )
    grad_values = jnp.einsum(
        "hij,ihd->jhd", weights_low, grad_attended, preferred_element_type=jnp.float32
    )
    grad_scores = (
        weights * (grad_weights - jnp.sum(weights * grad_weights, axis=-1, keepdims=True))
    ).astype(jnp.bfloat16)
    grad_query_nope = (
        jnp.einsum("hij,jhd->ihd", grad_scores, key_nope, preferred_element_type=jnp.float32)
        * scale
    )
    grad_query_rope = (
        jnp.einsum("hij,jd->ihd", grad_scores, key_rope, preferred_element_type=jnp.float32) * scale
    )
    grad_key_nope = (
        jnp.einsum(
            "hij,ihd->jhd", grad_scores, query_rows[..., :NOPE], preferred_element_type=jnp.float32
        )
        * scale
    )
    grad_key_rope = (
        jnp.einsum(
            "hij,ihd->jd", grad_scores, query_rows[..., NOPE:], preferred_element_type=jnp.float32
        )
        * scale
    )
    grad_query = (
        jnp.concatenate(
            [grad_query_nope, rotate_back(grad_query_rope, cosine[:, None, :], sine[:, None, :])],
            axis=-1,
        )
        .astype(jnp.bfloat16)
        .reshape(tokens, heads * (NOPE + ROPE))
    )
    grad_query_weight = jnp.dot(first_normed.T, grad_query, preferred_element_type=jnp.float32)
    grad_first = jnp.dot(grad_query, query_weight.T, preferred_element_type=jnp.float32)
    grad_keyval = (
        jnp.concatenate([grad_key_nope, grad_values], axis=-1)
        .astype(jnp.bfloat16)
        .reshape(tokens, heads * (NOPE + VD))
    )
    grad_keyval_weight = jnp.dot(latent_normed.T, grad_keyval, preferred_element_type=jnp.float32)
    grad_latent_normed = jnp.dot(grad_keyval, keyval_weight.T, preferred_element_type=jnp.float32)
    gain_latent_part = jnp.sum(grad_latent_normed * latent_unit, axis=0)
    grad_latent = rms_back(grad_latent_normed * latent_gain_wide, latent_unit, latent_scale)
    grad_latent_all = jnp.concatenate(
        [grad_latent, rotate_back(grad_key_rope, cosine, sine)], axis=-1
    )
    grad_first, grad_latent_all, gain_latent_grad = (
        lax.psum(grad_first.astype(jnp.bfloat16), "tensor").astype(jnp.float32),
        lax.psum(grad_latent_all.astype(jnp.bfloat16), "tensor").astype(jnp.float32),
        lax.psum(gain_latent_part.astype(jnp.bfloat16), "tensor").astype(jnp.float32),
    )
    grad_latent_low = grad_latent_all.astype(jnp.bfloat16)
    grad_latent_weight = jnp.dot(
        first_normed.T, grad_latent_low, preferred_element_type=jnp.float32
    )
    grad_first = grad_first + jnp.dot(
        grad_latent_low, latent_weight.T, preferred_element_type=jnp.float32
    )
    gain_attn_grad = jnp.sum(grad_first * first_unit, axis=0)
    grad_inputs = grad_mixed + rms_back(grad_first * attn_gain_wide, first_unit, first_scale)
    grad_local = lax.dynamic_slice_in_dim(grad_inputs, start, local_rows, 0)
    summed = (
        lax.psum_scatter(gain_attn_grad, "dp", scatter_dimension=0, tiled=True),
        lax.psum_scatter(grad_query_weight, "dp", scatter_dimension=0, tiled=True),
        lax.psum_scatter(grad_latent_weight, "dp", scatter_dimension=0, tiled=True),
        lax.psum_scatter(gain_latent_grad, "dp", scatter_dimension=0, tiled=True),
        lax.psum_scatter(grad_keyval_weight, "dp", scatter_dimension=0, tiled=True),
        lax.psum_scatter(grad_output_weight, "dp", scatter_dimension=1, tiled=True),
        lax.psum_scatter(gain_ffn_grad, "dp", scatter_dimension=0, tiled=True),
        lax.psum_scatter(grad_router, "dp", scatter_dimension=0, tiled=True),
        lax.psum_scatter(grad_shared_in, "dp", scatter_dimension=1, tiled=True),
        lax.psum_scatter(grad_shared_out, "dp", scatter_dimension=1, tiled=True),
    )
    return (
        block_output,
        grad_local,
        summed[0],
        summed[1],
        summed[2],
        summed[3],
        summed[4],
        summed[5],
        summed[6],
        summed[7],
        summed[8],
        summed[9],
        grad_expert_gate_up,
        grad_expert_down,
    )


RINGS = 4


def ring_step(values):
    return lax.ppermute(values, "dp", [(i, (i + RINGS) % 16) for i in range(16)])


def other_y(values):
    return lax.ppermute(values, "dp", [(i, i ^ 2) for i in range(16)])


def other_core(values):
    return lax.ppermute(values, "dp", [(i, i ^ 1) for i in range(16)])


def other_x(values):
    return lax.ppermute(values, "tensor", [(0, 1), (1, 0)])


def gather_rows(rows):
    planes = []
    current = rows
    for distance in range(RINGS):
        if distance:
            current = ring_step(current)
        beside = other_y(current)
        across = other_x(current)
        corner = other_x(beside) if distance % 2 else other_y(across)
        planes.append((current, beside, across, corner))
    return planes


def add_low(first, second):
    return (first.astype(jnp.float32) + second.astype(jnp.float32)).astype(jnp.bfloat16)


def scatter_rows(planes):
    moving = None
    for distance in (1, 2, 3, 0):
        own, beside, across, corner = planes[distance]
        if distance % 2:
            beside = add_low(beside, other_x(corner))
        else:
            across = add_low(across, other_y(corner))
        total = own.astype(jnp.float32)
        total = total + other_x(across).astype(jnp.float32) + other_y(beside).astype(jnp.float32)
        if moving is not None:
            total = total + ring_step(moving).astype(jnp.float32)
        moving = total.astype(jnp.bfloat16)
    return total


def ring_sum(parts, low):
    moving = parts[1]
    for distance in (2, 3, 0):
        moving = ring_step(moving.astype(low)).astype(jnp.float32) + parts[distance]
    return moving


def gather_weight(shard):
    chunks = []
    current = shard
    for distance in range(RINGS):
        if distance:
            current = ring_step(current)
        beside = other_y(current)
        for flip_y, chunk in ((0, current), (1, beside)):
            for flip_core, piece in ((0, chunk), (1, other_core(chunk))):
                chunks.append(((distance, flip_y, flip_core), piece))
    return chunks


def place_of(coords, key):
    z, y, core = coords
    distance, flip_y, flip_core = key
    return (
        lax.rem(z + RINGS - distance, RINGS) * 4
        + (1 - y if flip_y else y) * 2
        + (1 - core if flip_core else core)
    )


def place_kernel(keys, moves, coords_ref, *refs):
    chunks = refs[: len(keys)]
    outs = refs[len(keys) : -1]
    semaphores = refs[-1]
    coords = (coords_ref[0], coords_ref[1], coords_ref[2])
    copies = []
    for key, chunk in zip(keys, chunks):
        block = place_of(coords, key)
        for source_rows, source_columns, out, rows, columns in moves:
            start = pl.multiple_of(block * rows, rows)
            copies.append(
                pltpu.make_async_copy(
                    chunk.at[source_rows, source_columns],
                    outs[out].at[pl.ds(start, rows), columns],
                    semaphores.at[len(copies)],
                )
            )
    for copy in copies:
        copy.start()
    for copy in copies:
        copy.wait()


def place_chunks(coords, chunks, moves, shapes):
    keys = [key for key, _ in chunks]
    anywhere = pl.BlockSpec(memory_space=pl.ANY)
    return pl.pallas_call(
        functools.partial(place_kernel, keys, moves),
        out_shape=[jax.ShapeDtypeStruct(shape, jnp.bfloat16) for shape in shapes],
        in_specs=[pl.BlockSpec(memory_space=pltpu.SMEM)] + [anywhere] * len(chunks),
        out_specs=[pl.BlockSpec(memory_space=pltpu.VMEM)] * len(shapes),
        scratch_shapes=[pltpu.SemaphoreType.DMA((len(chunks) * len(moves),))],
        compiler_params=pltpu.CompilerParams(vmem_limit_bytes=24 * 1024 * 1024),
        cost_estimate=pl.CostEstimate(
            flops=0,
            bytes_accessed=4 * sum(shape[0] * shape[1] for shape in shapes),
            transcendentals=0,
        ),
    )(coords, *[piece for _, piece in chunks])


def weight_keys():
    return [
        (distance, flip_y, flip_core)
        for flip_core in (0, 1)
        for flip_y in (0, 1)
        for distance in range(RINGS)
    ]


def scatter_blocks(grads, low):
    half = grads.shape[0] // 2
    total = grads[:half].astype(jnp.float32) + other_core(grads[half:].astype(low)).astype(
        jnp.float32
    )
    quarter = half // 2
    total = total[:quarter] + other_y(total[quarter:].astype(low)).astype(jnp.float32)
    size = quarter // RINGS
    return ring_sum([total[r * size : (r + 1) * size] for r in range(RINGS)], low)


def pick_blocks(values, order):
    chosen = order[:, None] == jnp.arange(values.shape[0], dtype=jnp.int32)[None, :]
    chosen = chosen.reshape(chosen.shape + (1,) * (values.ndim - 1))
    return jnp.sum(jnp.where(chosen, values[None], 0.0), axis=1)


def attend_forward(query_rows, key_nope, key_rope, values, allowed, scale):
    scores = attention_scores(query_rows, key_nope, key_rope, allowed, scale)
    row_max = jnp.max(scores, axis=-1, keepdims=True)
    log_total = row_max + jnp.log(jnp.sum(jnp.exp(scores - row_max), axis=-1, keepdims=True))
    weights_low = jnp.exp(scores - log_total).astype(jnp.bfloat16)
    attended = jnp.einsum("hij,jhd->ihd", weights_low, values, preferred_element_type=jnp.float32)
    return attended.astype(jnp.bfloat16), log_total


def wide_dot(left, right):
    return jnp.dot(left, right, preferred_element_type=jnp.float32)


def dot_turned(left, right):
    return lax.dot_general(left, right, (((1,), (1,)), ((), ())), preferred_element_type=jnp.float32)


def dot_rows(left, right):
    return lax.dot_general(left, right, (((0,), (0,)), ((), ())), preferred_element_type=jnp.float32)


TILE = 256


def mlp_kernel(tiles, steps, pieces, *refs):
    experts_ref, routed_ref = refs[:2]
    row_refs = refs[2 : 2 + pieces]
    cot_refs = refs[2 + pieces : 2 + 2 * pieces]
    router_ref, gate_col, up_col, down_row, gate_row, up_row, down_col = refs[
        2 + 2 * pieces : 9 + 2 * pieces
    ]
    outs = refs[9 + 2 * pieces + 6 :]
    grad_refs, out_refs = outs[:pieces], outs[pieces : 2 * pieces]
    rows_out, cots_out, hidden_out, gate_out, up_out, logit_out = outs[2 * pieces : 2 * pieces + 6]
    hidden_all, gate_all, up_all, prob_ref, scale_ref, sum_ref = outs[2 * pieces + 6 :]
    step = pl.program_id(0)
    third = tiles // 2
    size = row_refs[0].shape[0]
    lane = lax.broadcasted_iota(jnp.int32, (1, router_ref.shape[1]), 1)

    @pl.when(step == 0)
    def _():
        for k in range(pieces):
            rows_out[k * size : (k + 1) * size, :] = row_refs[k][...]
            cots_out[k * size : (k + 1) * size, :] = cot_refs[k][...]
        logits = wide_dot(rows_out[...], router_ref[...])
        logits = jnp.where(lane < experts_ref[2], logits, -1e30)
        raised = jnp.exp(logits - jnp.max(logits, axis=1, keepdims=True))
        chances = raised / jnp.sum(raised, axis=1, keepdims=True)
        prob_ref[...] = chances
        for k in (0, 1):
            chance = jnp.sum(jnp.where(lane == experts_ref[k], chances, 0.0), axis=1, keepdims=True)
            scale_ref[k] = routed_ref[:, k : k + 1] * chance
        scale_ref[2] = jnp.ones_like(scale_ref[2])
        sum_ref[...] = jnp.zeros_like(sum_ref)

    @pl.when(step < tiles)
    def _():
        pre_gate = wide_dot(rows_out[...], gate_col[...])
        pre_up = wide_dot(rows_out[...], up_col[...])
        down_grad = dot_turned(cots_out[...], down_row[...])
        part = step // third
        scale = scale_ref[part]
        sigmoid = 1.0 / (1.0 + jnp.exp(-pre_gate))
        silu = pre_gate * sigmoid
        hidden = (silu * pre_up).astype(jnp.bfloat16).astype(jnp.float32)
        sum_ref[part] += jnp.sum(hidden * down_grad, axis=1, keepdims=True)
        grad_hidden = scale * down_grad
        columns = pl.ds(pl.multiple_of(step * TILE, TILE), TILE)
        low_hidden = (scale * hidden).astype(jnp.bfloat16)
        low_gate = (grad_hidden * pre_up * (sigmoid + silu * (1.0 - sigmoid))).astype(jnp.bfloat16)
        low_up = (grad_hidden * silu).astype(jnp.bfloat16)
        hidden_all[:, columns] = low_hidden
        gate_all[:, columns] = low_gate
        up_all[:, columns] = low_up
        hidden_out[...] = low_hidden
        gate_out[...] = low_gate
        up_out[...] = low_up

    @pl.when(step == tiles - 1)
    def _():
        grad_logits = jnp.zeros_like(prob_ref)
        for k in (0, 1):
            own = jnp.where(lane == experts_ref[k], 1.0, 0.0)
            grad_logits += scale_ref[k] * sum_ref[k] * (own - prob_ref[...])
        logit_out[...] = grad_logits.astype(jnp.bfloat16)

    @pl.when(step >= tiles)
    def _():
        some = pl.ds(pl.multiple_of((step - tiles) * TILE, TILE), TILE)
        grads = dot_turned(gate_all[...], gate_row[...]) + dot_turned(up_all[...], up_row[...])
        grads += dot_turned(logit_out[...], router_ref[some, :])
        grads = grads.astype(jnp.bfloat16)
        result = wide_dot(hidden_all[...], down_col[...]).astype(jnp.bfloat16)
        for k in range(pieces):
            grad_refs[k][...] = grads[k * size : (k + 1) * size]
            out_refs[k][...] = result[k * size : (k + 1) * size]


def mlp_plane(distance, experts, routed, rows, cots, router, gate, up, down, kept):
    pieces = len(rows)
    size, depth = rows[0].shape
    width = gate.shape[1]
    tiles, columns = width // TILE, depth // TILE
    total = pieces * size

    def whole(array):
        return pl.BlockSpec(array.shape, lambda i: (0,) * array.ndim)

    def early(i):
        return jnp.minimum(i, tiles - 1)

    def late(i):
        return jnp.maximum(i - tiles, 0)

    low = jnp.bfloat16
    piece_spec = pl.BlockSpec((size, TILE), lambda i: (0, late(i)))
    tile_spec = pl.BlockSpec((total, TILE), lambda i: (distance, early(i)))
    kept_specs = [
        pl.BlockSpec((total, depth), lambda i: (distance, 0)),
        pl.BlockSpec((total, depth), lambda i: (distance, 0)),
        tile_spec,
        tile_spec,
        tile_spec,
        pl.BlockSpec((total, router.shape[1]), lambda i: (distance, 0)),
    ]
    first_kept = 9 + 2 * pieces
    aliases = {first_kept + k: 2 * pieces + k for k in range(6)}
    results = pl.pallas_call(
        functools.partial(mlp_kernel, tiles, tiles + columns, pieces),
        grid=(tiles + columns,),
        in_specs=[pl.BlockSpec(memory_space=pltpu.SMEM), whole(routed)]
        + [whole(piece) for piece in rows]
        + [whole(piece) for piece in cots]
        + [
            whole(router),
            pl.BlockSpec((depth, TILE), lambda i: (0, early(i))),
            pl.BlockSpec((depth, TILE), lambda i: (0, early(i))),
            pl.BlockSpec((TILE, depth), lambda i: (early(i), 0)),
            pl.BlockSpec((TILE, width), lambda i: (late(i), 0)),
            pl.BlockSpec((TILE, width), lambda i: (late(i), 0)),
            pl.BlockSpec((width, TILE), lambda i: (0, late(i))),
        ]
        + [pl.BlockSpec(memory_space=pl.ANY)] * 6,
        out_specs=[piece_spec] * (2 * pieces) + kept_specs,
        out_shape=[jax.ShapeDtypeStruct((size, depth), low)] * (2 * pieces)
        + [jax.ShapeDtypeStruct(array.shape, array.dtype) for array in kept],
        scratch_shapes=[pltpu.VMEM((total, width), low)] * 3
        + [
            pltpu.VMEM((total, router.shape[1]), jnp.float32),
            pltpu.VMEM((3, total, 1), jnp.float32),
            pltpu.VMEM((3, total, 1), jnp.float32),
        ],
        input_output_aliases=aliases,
        compiler_params=pltpu.CompilerParams(vmem_limit_bytes=60 * 1024 * 1024),
        cost_estimate=pl.CostEstimate(
            flops=2 * total * depth * width * 6,
            bytes_accessed=2 * (6 * depth * width + 6 * total * depth + 3 * total * width),
            transcendentals=total * width,
        ),
    )(experts, routed, *rows, *cots, router, gate, up, down, gate, up, down, *kept)
    return results[:pieces], results[pieces : 2 * pieces], results[2 * pieces :]


def gather_body(
    block_input,
    segments,
    counts,
    routes,
    attn_gain,
    w_query,
    w_latent,
    latent_gain,
    w_keyval,
    w_output,
    ffn_gain,
    w_router,
    shared_gate_up,
    shared_down,
    expert_gate_up,
    expert_down,
    cotangent,
):
    f32 = jnp.float32
    bf16 = jnp.bfloat16
    blocks = 16
    index = lax.axis_index("dp")
    x = lax.axis_index("tensor")
    coords = jnp.stack([index // 4, (index // 2) % 2, index % 2]).astype(jnp.int32)
    z, y, core = coords[0], coords[1], coords[2]
    local_rows = block_input.shape[0]
    tokens = 2 * local_rows
    depth = w_query.shape[0]
    query_width = w_query.shape[1]
    heads = query_width // (NOPE + ROPE)
    experts = w_router.shape[1]
    units = expert_gate_up.shape[3]
    shared = shared_gate_up.shape[2] // blocks
    latent_depth = w_keyval.shape[0]
    scale = (NOPE + ROPE) ** (-0.5)

    def both_halves(own, other):
        return jnp.concatenate(
            [jnp.where(x == 0, own, other), jnp.where(x == 0, other, own)], axis=0
        )

    small = jnp.concatenate(
        [
            attn_gain[:, None],
            ffn_gain[:, None],
            w_router,
            jnp.pad(latent_gain, (0, depth - latent_depth))[:, None],
            routes.reshape(depth, -1).astype(bf16),
        ],
        axis=1,
    )
    rows_all = both_halves(block_input, other_x(block_input))
    used = query_width + KVR + ROPE
    first_width = -(-(used + small.shape[1]) // 128) * 128
    first_chunks = gather_weight(
        jnp.pad(
            jnp.concatenate([w_query, w_latent, small], axis=1),
            ((0, 0), (0, first_width - used - small.shape[1])),
        )
    )
    parts = depth // latent_depth
    keyval_part = w_keyval.shape[1] // parts
    keyval_packed = (
        w_keyval.reshape(latent_depth, parts, keyval_part).transpose(1, 0, 2).reshape(depth, -1)
    )
    second_chunks = gather_weight(jnp.concatenate([keyval_packed, w_output.T], axis=1))
    (first_weight,) = place_chunks(
        coords,
        first_chunks,
        [(pl.ds(0, depth), pl.ds(0, first_width), 0, depth, pl.ds(0, first_width))],
        [(D, first_width)],
    )
    small = first_weight[:, used:]
    attn_gain_wide = small[:, 0].astype(f32)
    ffn_gain_wide = small[:, 1].astype(f32)
    router_weight = small[:, 2 : 2 + experts]
    latent_gain_wide = (
        small[:, 2 + experts].reshape(blocks, depth)[:, :latent_depth].reshape(-1).astype(f32)
    )
    routes_all = small[:, 3 + experts : 3 + experts + 2 * TOP].reshape(blocks * tokens, TOP)
    chip_experts = jnp.stack([index, index + 1 - 2 * core])
    routed_all = jnp.any(
        routes_all[None] == chip_experts[:, None, None].astype(bf16), axis=2
    ).astype(f32)
    order = jnp.stack(
        [
            place_of(coords, (distance, flip_y, 0)) * 2 + (1 - x if flip_x else x)
            for distance in range(RINGS)
            for flip_x, flip_y in ((0, 0), (0, 1), (1, 0), (1, 1))
        ]
    )
    routed = jnp.stack(
        [
            pick_blocks(one.reshape(blocks * 2, local_rows), order).reshape(RINGS, -1)
            for one in routed_all
        ],
        axis=2,
    )
    keyval_weight, output_turned = place_chunks(
        coords,
        second_chunks,
        [
            (
                pl.ds(k * latent_depth, latent_depth),
                pl.ds(0, keyval_part),
                0,
                latent_depth,
                pl.ds(k * keyval_part, keyval_part),
            )
            for k in range(parts)
        ]
        + [
            (
                pl.ds(0, depth),
                pl.ds(keyval_part, w_output.shape[0]),
                1,
                depth,
                pl.ds(0, w_output.shape[0]),
            )
        ],
        [(KVR, w_keyval.shape[1]), (D, w_output.shape[0])],
    )

    shared_in = lax.all_to_all(
        shared_gate_up.reshape(2, depth, blocks, shared).transpose(2, 0, 1, 3).reshape(
            blocks, 2 * depth, shared
        ),
        "dp",
        split_axis=0,
        concat_axis=0,
        tiled=True,
    ).reshape(blocks, 2, depth, shared)
    shared_out = lax.all_to_all(
        shared_down.reshape(blocks, shared, depth),
        "dp",
        split_axis=0,
        concat_axis=0,
        tiled=True,
    )
    shared_other = other_core(shared_in)
    shared_out_other = other_core(shared_out)
    expert_in_other = other_core(expert_gate_up[0])
    expert_out_other = other_core(expert_down[0])
    hole = -(-units // TILE) * TILE - units

    def side_columns(k):
        return jnp.concatenate(
            [
                expert_gate_up[0, k],
                jnp.zeros((D, hole), bf16),
                expert_in_other[k],
                jnp.zeros((D, hole), bf16),
                shared_in[:, k].reshape(D, shared),
                shared_other[:, k].reshape(D, shared),
                jnp.zeros((D, TILE - 2 * shared), bf16),
            ],
            axis=1,
        )

    gate_weight = side_columns(0)
    up_weight = side_columns(1)
    down_weight = jnp.concatenate(
        [
            expert_down[0],
            jnp.zeros((hole, D), bf16),
            expert_out_other,
            jnp.zeros((hole, D), bf16),
            shared_out.transpose(1, 0, 2).reshape(shared, D),
            shared_out_other.transpose(1, 0, 2).reshape(shared, D),
            jnp.zeros((TILE - 2 * shared, D), bf16),
        ],
        axis=0,
    )
    router_wide = jnp.pad(router_weight, ((0, 0), (0, 128 - experts)))

    cosine, sine = rotary_tables(segments[0], ROPE)
    allowed = allowed_pairs(segments[0], counts[0])
    inputs = rows_all.astype(f32)
    first_scale = rms_scale(inputs)
    first_unit = inputs * first_scale
    first_normed = (first_unit * attn_gain_wide).astype(bf16)
    projected = wide_dot(first_normed, first_weight)
    query = projected[:, :query_width].reshape(tokens, heads, NOPE + ROPE)
    query_rows = jnp.concatenate(
        [query[..., :NOPE], rotate(query[..., NOPE:], cosine[:, None, :], sine[:, None, :])],
        axis=-1,
    ).astype(bf16)
    latent = projected[:, query_width : query_width + KVR]
    key_rope = rotate(projected[:, query_width + KVR : used], cosine, sine).astype(bf16)
    latent_scale = rms_scale(latent)
    latent_unit = latent * latent_scale
    latent_normed = (latent_unit * latent_gain_wide).astype(bf16)
    keyval = wide_dot(latent_normed, keyval_weight).astype(bf16).reshape(tokens, heads, NOPE + VD)
    key_nope = keyval[..., :NOPE]
    values = keyval[..., NOPE:]
    attended, log_total = attend_forward(query_rows, key_nope, key_rope, values, allowed, scale)
    attended = attended.reshape(tokens, heads * VD)
    attn_part = dot_turned(attended, output_turned)
    low_rows, high_rows = attn_part[:local_rows], attn_part[local_rows:]
    own_part = jnp.where(x == 0, low_rows, high_rows)
    sent_part = jnp.where(x == 0, high_rows, low_rows).astype(bf16)
    mixed = block_input.astype(f32) + own_part + other_x(sent_part).astype(f32)
    second_scale = rms_scale(mixed)
    second_unit = mixed * second_scale
    second_normed = (second_unit * ffn_gain_wide).astype(bf16)

    grad_planes = gather_rows(cotangent)
    row_planes = gather_rows(second_normed)
    width = gate_weight.shape[1]
    total_rows = 16 * local_rows
    kept = [
        jnp.zeros((total_rows, columns), bf16)
        for columns in (D, D, width, width, width, router_wide.shape[1])
    ]
    expert_ids = jnp.concatenate([chip_experts, jnp.array([experts], jnp.int32)])
    grad_parts, out_parts = [], []
    for distance in range(RINGS):
        grads, outs, kept = mlp_plane(
            distance,
            expert_ids,
            routed[distance],
            row_planes[distance],
            grad_planes[distance],
            router_wide,
            gate_weight,
            up_weight,
            down_weight,
            kept,
        )
        grad_parts.append(grads)
        out_parts.append(outs)
    grad_second = scatter_rows(grad_parts)
    block_output = mixed + scatter_rows(out_parts)

    every_row, every_grad, every_hidden, every_gate_grad, every_up_grad, logit_grads = kept
    far = units + hole

    def both_in(grads):
        sent = other_core(dot_rows(every_row, grads[:, far : far + units]).astype(bf16))
        return dot_rows(every_row, grads[:, :units]) + sent.astype(f32)

    grad_expert_gate_up = jnp.stack([both_in(every_gate_grad), both_in(every_up_grad)])[None]
    sent_down = other_core(dot_rows(every_hidden[:, far : far + units], every_grad).astype(bf16))
    grad_expert_down = (
        dot_rows(every_hidden[:, :units], every_grad) + sent_down.astype(f32)
    )[None]
    side_grads = dot_rows(
        every_row,
        jnp.concatenate(
            [every_gate_grad[:, 2 * far :], every_up_grad[:, 2 * far :], logit_grads], axis=1
        ),
    )
    grad_router = side_grads[:, 2 * TILE : 2 * TILE + experts]
    shared_in_grads = jnp.stack(
        [
            side_grads[:, k * TILE : k * TILE + shared]
            + other_core(
                side_grads[:, k * TILE + shared : k * TILE + 2 * shared].astype(bf16)
            ).astype(f32)
            for k in (0, 1)
        ]
    )
    side_down = dot_rows(every_hidden[:, 2 * far :], every_grad)
    shared_down_grads = side_down[:shared] + other_core(
        side_down[shared : 2 * shared].astype(bf16)
    ).astype(f32)
    grad_shared_in = (
        lax.all_to_all(
            shared_in_grads.astype(bf16)
            .reshape(2, blocks, depth, shared)
            .transpose(1, 0, 2, 3)
            .reshape(blocks, 2 * depth, shared),
            "dp",
            split_axis=0,
            concat_axis=0,
            tiled=True,
        )
        .astype(f32)
        .reshape(blocks, 2, depth, shared)
        .transpose(1, 2, 0, 3)
        .reshape(2, depth, blocks * shared)
    )
    grad_shared_down = (
        lax.all_to_all(
            shared_down_grads.astype(bf16).reshape(shared, blocks, depth).transpose(1, 0, 2),
            "dp",
            split_axis=0,
            concat_axis=0,
            tiled=True,
        )
        .astype(f32)
        .reshape(blocks * shared, depth)
    )

    gain_ffn_part = jnp.sum(grad_second * second_unit, axis=0)
    grad_mixed = cotangent.astype(f32) + rms_back(
        grad_second * ffn_gain_wide, second_unit, second_scale
    )
    grad_mixed_low = grad_mixed.astype(bf16)
    grad_attn = both_halves(grad_mixed_low, other_x(grad_mixed_low))

    keys = weight_keys()
    places = [place_of(coords, key) for key in keys]

    def in_key_order(values):
        return jnp.concatenate(
            [lax.dynamic_slice_in_dim(values, place * depth, depth, 1) for place in places], axis=1
        )

    grad_output_weight = scatter_blocks(
        dot_rows(in_key_order(grad_attn), attended).astype(bf16), bf16
    ).T
    grad_attended = (
        wide_dot(grad_attn, output_turned).astype(bf16).reshape(tokens, heads, VD)
    )
    scores = attention_scores(query_rows, key_nope, key_rope, allowed, scale)
    weights = jnp.exp(scores - log_total)
    weights_low = weights.astype(bf16)
    grad_weights = jnp.einsum("ihd,jhd->hij", grad_attended, values, preferred_element_type=f32)
    grad_values = jnp.einsum("hij,ihd->jhd", weights_low, grad_attended, preferred_element_type=f32)
    grad_scores = (
        weights * (grad_weights - jnp.sum(weights * grad_weights, axis=-1, keepdims=True))
    ).astype(bf16)
    grad_query_nope = scale * jnp.einsum(
        "hij,jhd->ihd", grad_scores, key_nope, preferred_element_type=f32
    )
    grad_query_rope = scale * jnp.einsum(
        "hij,jd->ihd", grad_scores, key_rope, preferred_element_type=f32
    )
    grad_key_nope = scale * jnp.einsum(
        "hij,ihd->jhd", grad_scores, query_rows[..., :NOPE], preferred_element_type=f32
    )
    grad_key_rope = scale * jnp.einsum(
        "hij,ihd->jd", grad_scores, query_rows[..., NOPE:], preferred_element_type=f32
    )
    grad_query = (
        jnp.concatenate(
            [grad_query_nope, rotate_back(grad_query_rope, cosine[:, None, :], sine[:, None, :])],
            axis=-1,
        )
        .astype(bf16)
        .reshape(tokens, heads * (NOPE + ROPE))
    )
    grad_keyval = (
        jnp.concatenate([grad_key_nope, grad_values], axis=-1)
        .astype(bf16)
        .reshape(tokens, heads * (NOPE + VD))
    )
    key_order = jnp.stack(places)
    latent_column = jnp.arange(KVR, dtype=jnp.int32)
    wanted = key_order[latent_column // latent_depth] * latent_depth + latent_column % latent_depth
    shuffle = (latent_column[:, None] == wanted[None, :]).astype(bf16)
    latent_in_order = wide_dot(latent_normed, shuffle).astype(bf16)
    grad_keyval_weight = scatter_blocks(dot_rows(latent_in_order, grad_keyval).astype(bf16), bf16)
    grad_latent_normed = dot_turned(grad_keyval, keyval_weight)
    gain_latent_part = jnp.sum(grad_latent_normed * latent_unit, axis=0)
    grad_latent = rms_back(grad_latent_normed * latent_gain_wide, latent_unit, latent_scale)
    grad_latent_all = jnp.concatenate(
        [grad_latent, rotate_back(grad_key_rope, cosine, sine)], axis=-1
    ).astype(bf16)
    grad_projected = jnp.concatenate([grad_query, grad_latent_all], axis=1)
    grad_first_weight = scatter_blocks(
        dot_rows(in_key_order(first_normed), grad_projected).astype(bf16), bf16
    )
    grad_latent_part = grad_first_weight[:, query_width:]
    grad_latent_weight = grad_latent_part + other_x(grad_latent_part)
    grad_first_part = dot_turned(grad_projected, first_weight[:, :used])
    low_rows, high_rows = grad_first_part[:local_rows], grad_first_part[local_rows:]
    sent_part = jnp.where(x == 0, high_rows, low_rows).astype(bf16)
    grad_first = jnp.where(x == 0, low_rows, high_rows) + other_x(sent_part).astype(f32)
    own_inputs = block_input.astype(f32)
    own_scale = rms_scale(own_inputs)
    own_unit = own_inputs * own_scale
    gain_attn_part = jnp.sum(grad_first * own_unit, axis=0)
    grad_input = grad_mixed + rms_back(grad_first * attn_gain_wide, own_unit, own_scale)

    small_grads = jnp.concatenate(
        [
            gain_attn_part.reshape(blocks, 1, depth),
            gain_ffn_part.reshape(blocks, 1, depth),
            grad_router.reshape(blocks, experts, depth),
            jnp.pad(
                gain_latent_part.reshape(blocks, 1, latent_depth),
                ((0, 0), (0, 0), (0, depth - latent_depth)),
            ),
        ],
        axis=1,
    )
    small_grads = scatter_blocks(pick_blocks(small_grads, key_order), f32)[0]
    small_grads = small_grads + other_x(small_grads)
    return (
        block_output,
        grad_input,
        small_grads[0],
        grad_first_weight[:, :query_width],
        grad_latent_weight,
        small_grads[2 + experts, :latent_depth],
        grad_keyval_weight,
        grad_output_weight,
        small_grads[1],
        small_grads[2 : 2 + experts].reshape(depth, experts),
        grad_shared_in,
        grad_shared_down,
        grad_expert_gate_up,
        grad_expert_down,
    )


def solution(mesh):
    in_specs = (
        P(("dp", "tensor"), None),
        P("dp", None),
        P("dp"),
        P("dp", None),
        P("dp"),
        P("dp", "tensor"),
        P("dp", None),
        P("dp"),
        P("dp", "tensor"),
        P("tensor", "dp"),
        P("dp"),
        P("dp", None),
        P(None, "dp", "tensor"),
        P("tensor", "dp"),
        P("dp", None, None, "tensor"),
        P("dp", "tensor", None),
        P(("dp", "tensor"), None),
    )
    out_specs = (
        P(("dp", "tensor"), None),
        P(("dp", "tensor"), None),
        P("dp"),
        P("dp", "tensor"),
        P("dp", None),
        P("dp"),
        P("dp", "tensor"),
        P("tensor", "dp"),
        P("dp"),
        P("dp", None),
        P(None, "dp", "tensor"),
        P("tensor", "dp"),
        P("dp", None, None, "tensor"),
        P("dp", "tensor", None),
    )
    body = gather_body if mesh.shape["dp"] == 16 else exchange_body
    return jax.shard_map(body, mesh=mesh, in_specs=in_specs, out_specs=out_specs, check_vma=False)
```

```python
import functools
import math

import jax
import jax.numpy as jnp
from jax import lax
from jax.experimental import pallas as pl
from jax.experimental.pallas import tpu as pltpu
from jax.sharding import PartitionSpec as P

D = 2048
NOPE = 128
ROPE = 64
VD = 128
KVR = 512
TOP = 6


EPSILON = 1e-06


def rms_scale(values):
    return lax.rsqrt(jnp.mean(values * values, axis=-1, keepdims=True) + EPSILON)


def rms_back(grad_unit, unit_rows, row_scale):
    return row_scale * (
        grad_unit - unit_rows * jnp.mean(grad_unit * unit_rows, axis=-1, keepdims=True)
    )


def rotary_tables(segment_row, width):
    count = segment_row.shape[0]
    position = jnp.arange(count, dtype=jnp.int32)
    same = segment_row[:, None] == segment_row[None, :]
    start = jnp.min(jnp.where(same, position[None, :], count), axis=1)
    offset = (position - start).astype(jnp.float32)
    freq = jnp.exp(jnp.arange(width // 2, dtype=jnp.float32) * (-2.0 * math.log(10000.0) / width))
    angle = offset[:, None] * freq[None, :]
    return (jnp.cos(angle), jnp.sin(angle))


def rotate(values, cosine, sine):
    half = values.shape[-1] // 2
    first = values[..., :half]
    second = values[..., half:]
    return jnp.concatenate(
        [first * cosine - second * sine, second * cosine + first * sine], axis=-1
    )


def rotate_back(grads, cosine, sine):
    half = grads.shape[-1] // 2
    first = grads[..., :half]
    second = grads[..., half:]
    return jnp.concatenate(
        [first * cosine + second * sine, second * cosine - first * sine], axis=-1
    )


def allowed_pairs(segment_row, count):
    position = jnp.arange(segment_row.shape[0], dtype=jnp.int32)
    live = position < count
    same = segment_row[:, None] == segment_row[None, :]
    causal = position[None, :] <= position[:, None]
    return same & causal & live[:, None] & live[None, :] | (position[:, None] == position[None, :])


def attention_scores(query_rows, key_nope, key_rope, allowed, scale):
    scores = jnp.einsum(
        "ihd,jhd->hij", query_rows[..., :NOPE], key_nope, preferred_element_type=jnp.float32
    )
    scores = scores + jnp.einsum(
        "ihd,jd->hij", query_rows[..., NOPE:], key_rope, preferred_element_type=jnp.float32
    )
    return jnp.where(allowed[None], scores * scale, -1e30)


def swiglu_back(gate, upper, grad_hidden, axis):
    sigmoid = jax.nn.sigmoid(gate)
    grad_gate = grad_hidden * upper * sigmoid * (1.0 + gate * (1.0 - sigmoid))
    grad_upper = grad_hidden * gate * sigmoid
    return jnp.stack([grad_gate, grad_upper], axis=axis)


def slot_layout(routes, experts, capacity):
    tokens = routes.shape[0]
    flat = routes.reshape(-1)
    onehot = (flat[:, None] == jnp.arange(experts, dtype=jnp.int32)[None, :]).astype(jnp.int32)
    rank = jnp.arange(flat.shape[0], dtype=jnp.int32)
    earlier = (rank[None, :] < rank[:, None]).astype(jnp.bfloat16)
    before = jnp.dot(
        earlier, onehot.astype(jnp.bfloat16), preferred_element_type=jnp.float32
    ).astype(jnp.int32)
    slot_index = jnp.sum(before * onehot, axis=1)
    target = flat * capacity + slot_index
    token_ids = jnp.arange(flat.shape[0], dtype=jnp.int32) // routes.shape[1]
    owner = jnp.full((experts * capacity,), tokens, jnp.int32).at[target].set(token_ids)
    return (slot_index, target, owner)


def to_expert_major(arrived, groups, local_experts):
    capacity = arrived.shape[1]
    width = arrived.shape[2]
    return (
        arrived.reshape(groups, local_experts, capacity, width)
        .transpose(1, 0, 2, 3)
        .reshape(local_experts, groups * capacity, width)
    )


def from_expert_major(results, groups):
    local_experts = results.shape[0]
    width = results.shape[2]
    capacity = results.shape[1] // groups
    return (
        results.reshape(local_experts, groups, capacity, width)
        .transpose(1, 0, 2, 3)
        .reshape(groups * local_experts, capacity, width)
    )


def exchange_body(
    block_input,
    segments,
    counts,
    routes,
    attn_gain,
    w_query,
    w_latent,
    latent_gain,
    w_keyval,
    w_output,
    ffn_gain,
    w_router,
    shared_gate_up,
    shared_down,
    expert_gate_up,
    expert_down,
    cotangent,
):
    gathered = (
        lax.all_gather(attn_gain, "dp", axis=0, tiled=True),
        lax.all_gather(w_query, "dp", axis=0, tiled=True),
        lax.all_gather(w_latent, "dp", axis=0, tiled=True),
        lax.all_gather(latent_gain, "dp", axis=0, tiled=True),
        lax.all_gather(w_keyval, "dp", axis=0, tiled=True),
        lax.all_gather(w_output, "dp", axis=1, tiled=True),
        lax.all_gather(ffn_gain, "dp", axis=0, tiled=True),
        lax.all_gather(w_router, "dp", axis=0, tiled=True),
        lax.all_gather(shared_gate_up, "dp", axis=1, tiled=True),
        lax.all_gather(shared_down, "dp", axis=1, tiled=True),
    )
    (
        full_attn_gain,
        query_weight,
        latent_weight,
        full_latent_gain,
        keyval_weight,
        output_weight,
        full_ffn_gain,
        router_weight,
        shared_in,
        shared_out,
    ) = gathered
    tensor_rank = lax.axis_index("tensor")
    dp_size = lax.axis_size("dp")
    rows_all = lax.all_gather(block_input, "tensor", axis=0, tiled=True)
    tokens = rows_all.shape[0]
    local_rows = block_input.shape[0]
    heads = query_weight.shape[1] // (NOPE + ROPE)
    experts = router_weight.shape[1]
    local_experts = expert_gate_up.shape[0]
    capacity = 2 * tokens * TOP // experts
    scale = (NOPE + ROPE) ** (-0.5)
    start = tensor_rank * local_rows
    cosine, sine = rotary_tables(segments[0], ROPE)
    allowed = allowed_pairs(segments[0], counts[0])
    attn_gain_wide = full_attn_gain.astype(jnp.float32)
    latent_gain_wide = full_latent_gain.astype(jnp.float32)
    ffn_gain_wide = full_ffn_gain.astype(jnp.float32)
    inputs = rows_all.astype(jnp.float32)
    first_scale = rms_scale(inputs)
    first_unit = inputs * first_scale
    first_normed = (first_unit * attn_gain_wide).astype(jnp.bfloat16)
    query = jnp.dot(first_normed, query_weight, preferred_element_type=jnp.float32).reshape(
        tokens, heads, NOPE + ROPE
    )
    query_rows = jnp.concatenate(
        [query[..., :NOPE], rotate(query[..., NOPE:], cosine[:, None, :], sine[:, None, :])],
        axis=-1,
    ).astype(jnp.bfloat16)
    latent_all = jnp.dot(first_normed, latent_weight, preferred_element_type=jnp.float32)
    latent = latent_all[:, :KVR]
    key_rope = rotate(latent_all[:, KVR:], cosine, sine).astype(jnp.bfloat16)
    latent_scale = rms_scale(latent)
    latent_unit = latent * latent_scale
    latent_normed = (latent_unit * latent_gain_wide).astype(jnp.bfloat16)
    keyval = (
        jnp.dot(latent_normed, keyval_weight, preferred_element_type=jnp.float32)
        .astype(jnp.bfloat16)
        .reshape(tokens, heads, NOPE + VD)
    )
    key_nope = keyval[..., :NOPE]
    values = keyval[..., NOPE:]
    scores = attention_scores(query_rows, key_nope, key_rope, allowed, scale)
    row_max = jnp.max(scores, axis=-1, keepdims=True)
    log_total = row_max + jnp.log(jnp.sum(jnp.exp(scores - row_max), axis=-1, keepdims=True))
    weights_low = jnp.exp(scores - log_total).astype(jnp.bfloat16)
    attended = (
        jnp.einsum("hij,jhd->ihd", weights_low, values, preferred_element_type=jnp.float32)
        .astype(jnp.bfloat16)
        .reshape(tokens, heads * VD)
    )
    attn_part = jnp.dot(attended, output_weight, preferred_element_type=jnp.float32)
    mixed = inputs + lax.psum(attn_part, "tensor")
    second_scale = rms_scale(mixed)
    second_unit = mixed * second_scale
    second_normed = (second_unit * ffn_gain_wide).astype(jnp.bfloat16)
    logits = jnp.dot(second_normed, router_weight, preferred_element_type=jnp.float32)
    probabilities = jax.nn.softmax(logits, axis=-1)
    gate_values = jnp.take_along_axis(probabilities, routes, axis=1)
    shared_pre = jnp.einsum(
        "td,gdf->tgf", second_normed, shared_in, preferred_element_type=jnp.float32
    )
    shared_hidden = (jax.nn.silu(shared_pre[:, 0]) * shared_pre[:, 1]).astype(jnp.bfloat16)
    shared_part = jnp.dot(shared_hidden, shared_out, preferred_element_type=jnp.float32)
    slot_index, target, owner = slot_layout(routes, experts, capacity)
    owner_grid = owner.reshape(experts, capacity)
    padded_rows = jnp.concatenate([second_normed, jnp.zeros((1, D), jnp.bfloat16)], axis=0)
    outgoing = padded_rows[owner_grid]
    arrived = lax.all_to_all(outgoing, "dp", split_axis=0, concat_axis=0, tiled=True)
    expert_rows = to_expert_major(arrived, dp_size, local_experts)
    expert_pre = jnp.einsum(
        "erd,egdf->ergf", expert_rows, expert_gate_up, preferred_element_type=jnp.float32
    )
    expert_hidden = (jax.nn.silu(expert_pre[:, :, 0]) * expert_pre[:, :, 1]).astype(jnp.bfloat16)
    expert_result = jnp.einsum(
        "erf,efd->erd", expert_hidden, expert_down, preferred_element_type=jnp.float32
    )
    returning = from_expert_major(expert_result, dp_size)
    returned = lax.all_to_all(
        returning.astype(jnp.bfloat16), "dp", split_axis=0, concat_axis=0, tiled=True
    ).astype(returning.dtype)
    padded_back = jnp.concatenate([returned.reshape(-1, D), jnp.zeros((1, D), jnp.float32)], axis=0)
    picked = padded_back[target].reshape(tokens, TOP, D)
    routed_part = jnp.sum(gate_values[:, :, None] * picked, axis=1)
    branch_sum = lax.psum_scatter(
        (shared_part + routed_part).astype(jnp.bfloat16), "tensor", scatter_dimension=0, tiled=True
    ).astype(jnp.float32)
    block_output = lax.dynamic_slice_in_dim(mixed, start, local_rows, 0) + branch_sum
    grad_rows = lax.all_gather(cotangent, "tensor", axis=0, tiled=True)
    grad_out = grad_rows.astype(jnp.float32)
    grad_shared_hidden = jnp.dot(grad_rows, shared_out.T, preferred_element_type=jnp.float32)
    grad_shared_out = jnp.dot(shared_hidden.T, grad_rows, preferred_element_type=jnp.float32)
    grad_shared_pre = swiglu_back(shared_pre[:, 0], shared_pre[:, 1], grad_shared_hidden, 1).astype(
        jnp.bfloat16
    )
    grad_shared_in = jnp.einsum(
        "td,tgf->gdf", second_normed, grad_shared_pre, preferred_element_type=jnp.float32
    )
    grad_second = jnp.einsum(
        "tgf,gdf->td", grad_shared_pre, shared_in, preferred_element_type=jnp.float32
    )
    gate_by_slot = (
        jnp.zeros((experts * capacity + 1,), jnp.float32).at[target].set(gate_values.reshape(-1))
    )
    slot_ids = jnp.arange(experts * capacity, dtype=jnp.int32).reshape(experts, capacity)
    padded_grad = jnp.concatenate([grad_out, jnp.zeros((1, D), jnp.float32)], axis=0)
    grad_outgoing = (gate_by_slot[slot_ids][..., None] * padded_grad[owner_grid]).astype(
        jnp.bfloat16
    )
    grad_arrived = lax.all_to_all(grad_outgoing, "dp", split_axis=0, concat_axis=0, tiled=True)
    grad_expert_rows = to_expert_major(grad_arrived, dp_size, local_experts)
    grad_expert_hidden = jnp.einsum(
        "erd,efd->erf", grad_expert_rows, expert_down, preferred_element_type=jnp.float32
    )
    grad_expert_down = jnp.einsum(
        "erf,erd->efd", expert_hidden, grad_expert_rows, preferred_element_type=jnp.float32
    )
    grad_expert_pre = swiglu_back(
        expert_pre[:, :, 0], expert_pre[:, :, 1], grad_expert_hidden, 2
    ).astype(jnp.bfloat16)
    grad_expert_gate_up = jnp.einsum(
        "erd,ergf->egdf", expert_rows, grad_expert_pre, preferred_element_type=jnp.float32
    )
    grad_expert_input = jnp.einsum(
        "ergf,egdf->erd", grad_expert_pre, expert_gate_up, preferred_element_type=jnp.float32
    )
    grad_returning = from_expert_major(grad_expert_input, dp_size)
    grad_returned = lax.all_to_all(
        grad_returning.astype(jnp.bfloat16), "dp", split_axis=0, concat_axis=0, tiled=True
    ).astype(grad_returning.dtype)
    padded_grad_back = jnp.concatenate(
        [grad_returned.reshape(-1, D), jnp.zeros((1, D), jnp.float32)], axis=0
    )
    grad_second = grad_second + jnp.sum(padded_grad_back[target].reshape(tokens, TOP, D), axis=1)
    grad_gates = jnp.sum(grad_out[:, None, :] * picked, axis=-1)
    grad_second, grad_gates = (
        lax.psum(grad_second.astype(jnp.bfloat16), "tensor").astype(jnp.float32),
        lax.psum(grad_gates.astype(jnp.bfloat16), "tensor").astype(jnp.float32),
    )
    chosen = (routes[:, :, None] == jnp.arange(experts, dtype=jnp.int32)[None, None, :]).astype(
        jnp.float32
    )
    grad_probabilities = jnp.sum(chosen * grad_gates[:, :, None], axis=1)
    grad_logits = probabilities * (
        grad_probabilities - jnp.sum(probabilities * grad_probabilities, axis=-1, keepdims=True)
    )
    grad_logits_low = grad_logits.astype(jnp.bfloat16)
    grad_router = jnp.dot(second_normed.T, grad_logits_low, preferred_element_type=jnp.float32)
    grad_second = grad_second + jnp.dot(
        grad_logits_low, router_weight.T, preferred_element_type=jnp.float32
    )
    gain_ffn_grad = jnp.sum(grad_second * second_unit, axis=0)
    grad_mixed = grad_out + rms_back(grad_second * ffn_gain_wide, second_unit, second_scale)
    grad_attn_low = grad_mixed.astype(jnp.bfloat16)
    grad_output_weight = jnp.dot(attended.T, grad_attn_low, preferred_element_type=jnp.float32)
    grad_attended = (
        jnp.dot(grad_attn_low, output_weight.T, preferred_element_type=jnp.float32)
        .astype(jnp.bfloat16)
        .reshape(tokens, heads, VD)
    )
    scores = attention_scores(query_rows, key_nope, key_rope, allowed, scale)
    weights = jnp.exp(scores - log_total)
    weights_low = weights.astype(jnp.bfloat16)
    grad_weights = jnp.einsum(
        "ihd,jhd->hij", grad_attended, values, preferred_element_type=jnp.float32
    )
    grad_values = jnp.einsum(
        "hij,ihd->jhd", weights_low, grad_attended, preferred_element_type=jnp.float32
    )
    grad_scores = (
        weights * (grad_weights - jnp.sum(weights * grad_weights, axis=-1, keepdims=True))
    ).astype(jnp.bfloat16)
    grad_query_nope = (
        jnp.einsum("hij,jhd->ihd", grad_scores, key_nope, preferred_element_type=jnp.float32)
        * scale
    )
    grad_query_rope = (
        jnp.einsum("hij,jd->ihd", grad_scores, key_rope, preferred_element_type=jnp.float32) * scale
    )
    grad_key_nope = (
        jnp.einsum(
            "hij,ihd->jhd", grad_scores, query_rows[..., :NOPE], preferred_element_type=jnp.float32
        )
        * scale
    )
    grad_key_rope = (
        jnp.einsum(
            "hij,ihd->jd", grad_scores, query_rows[..., NOPE:], preferred_element_type=jnp.float32
        )
        * scale
    )
    grad_query = (
        jnp.concatenate(
            [grad_query_nope, rotate_back(grad_query_rope, cosine[:, None, :], sine[:, None, :])],
            axis=-1,
        )
        .astype(jnp.bfloat16)
        .reshape(tokens, heads * (NOPE + ROPE))
    )
    grad_query_weight = jnp.dot(first_normed.T, grad_query, preferred_element_type=jnp.float32)
    grad_first = jnp.dot(grad_query, query_weight.T, preferred_element_type=jnp.float32)
    grad_keyval = (
        jnp.concatenate([grad_key_nope, grad_values], axis=-1)
        .astype(jnp.bfloat16)
        .reshape(tokens, heads * (NOPE + VD))
    )
    grad_keyval_weight = jnp.dot(latent_normed.T, grad_keyval, preferred_element_type=jnp.float32)
    grad_latent_normed = jnp.dot(grad_keyval, keyval_weight.T, preferred_element_type=jnp.float32)
    gain_latent_part = jnp.sum(grad_latent_normed * latent_unit, axis=0)
    grad_latent = rms_back(grad_latent_normed * latent_gain_wide, latent_unit, latent_scale)
    grad_latent_all = jnp.concatenate(
        [grad_latent, rotate_back(grad_key_rope, cosine, sine)], axis=-1
    )
    grad_first, grad_latent_all, gain_latent_grad = (
        lax.psum(grad_first.astype(jnp.bfloat16), "tensor").astype(jnp.float32),
        lax.psum(grad_latent_all.astype(jnp.bfloat16), "tensor").astype(jnp.float32),
        lax.psum(gain_latent_part.astype(jnp.bfloat16), "tensor").astype(jnp.float32),
    )
    grad_latent_low = grad_latent_all.astype(jnp.bfloat16)
    grad_latent_weight = jnp.dot(
        first_normed.T, grad_latent_low, preferred_element_type=jnp.float32
    )
    grad_first = grad_first + jnp.dot(
        grad_latent_low, latent_weight.T, preferred_element_type=jnp.float32
    )
    gain_attn_grad = jnp.sum(grad_first * first_unit, axis=0)
    grad_inputs = grad_mixed + rms_back(grad_first * attn_gain_wide, first_unit, first_scale)
    grad_local = lax.dynamic_slice_in_dim(grad_inputs, start, local_rows, 0)
    summed = (
        lax.psum_scatter(gain_attn_grad, "dp", scatter_dimension=0, tiled=True),
        lax.psum_scatter(grad_query_weight, "dp", scatter_dimension=0, tiled=True),
        lax.psum_scatter(grad_latent_weight, "dp", scatter_dimension=0, tiled=True),
        lax.psum_scatter(gain_latent_grad, "dp", scatter_dimension=0, tiled=True),
        lax.psum_scatter(grad_keyval_weight, "dp", scatter_dimension=0, tiled=True),
        lax.psum_scatter(grad_output_weight, "dp", scatter_dimension=1, tiled=True),
        lax.psum_scatter(gain_ffn_grad, "dp", scatter_dimension=0, tiled=True),
        lax.psum_scatter(grad_router, "dp", scatter_dimension=0, tiled=True),
        lax.psum_scatter(grad_shared_in, "dp", scatter_dimension=1, tiled=True),
        lax.psum_scatter(grad_shared_out, "dp", scatter_dimension=1, tiled=True),
    )
    return (
        block_output,
        grad_local,
        summed[0],
        summed[1],
        summed[2],
        summed[3],
        summed[4],
        summed[5],
        summed[6],
        summed[7],
        summed[8],
        summed[9],
        grad_expert_gate_up,
        grad_expert_down,
    )


RINGS = 4


def ring_step(values):
    return lax.ppermute(values, "dp", [(i, (i + RINGS) % 16) for i in range(16)])


def other_y(values):
    return lax.ppermute(values, "dp", [(i, i ^ 2) for i in range(16)])


def other_core(values):
    return lax.ppermute(values, "dp", [(i, i ^ 1) for i in range(16)])


def other_x(values):
    return lax.ppermute(values, "tensor", [(0, 1), (1, 0)])


def fence_kernel(*refs):
    pass


def after(values, *others):
    anywhere = pl.BlockSpec(memory_space=pl.ANY)
    return pl.pallas_call(
        fence_kernel,
        out_shape=jax.ShapeDtypeStruct(values.shape, values.dtype),
        in_specs=[anywhere] * (1 + len(others)),
        out_specs=anywhere,
        input_output_aliases={0: 0},
    )(values, *others)


def gather_rows(rows, corners):
    planes = []
    current = rows
    for distance in range(RINGS):
        if distance:
            current = ring_step(current)
        beside = other_y(current)
        across = other_x(current)
        corner = other_x(beside) if corners[distance] == "x" else other_y(across)
        planes.append((current, beside, across, corner))
    return planes


def add_low(first, second):
    return (first.astype(jnp.float32) + second.astype(jnp.float32)).astype(jnp.bfloat16)


def turn_corner(plane, direction):
    own, beside, across, corner = plane
    if direction == "x":
        return own, add_low(beside, other_x(corner)), across
    return own, beside, add_low(across, other_y(corner))


def close_plane(turned):
    own, beside, across = turned
    return own, other_y(beside), other_x(across)


def ring_rows(closed):
    moving = None
    for distance in (1, 2, 3, 0):
        own, from_y, from_x = closed[distance]
        total = own.astype(jnp.float32) + from_y.astype(jnp.float32) + from_x.astype(jnp.float32)
        if moving is not None:
            total = total + ring_step(moving).astype(jnp.float32)
        moving = total.astype(jnp.bfloat16)
    return total


def ring_sum(parts, low):
    moving = parts[1]
    for distance in (2, 3, 0):
        moving = ring_step(moving.astype(low)).astype(jnp.float32) + parts[distance]
    return moving


def ring_shards(shard):
    held = [shard]
    for _ in range(RINGS - 1):
        held.append(ring_step(held[-1]))
    return held


def gather_weight(held):
    chunks = []
    for distance, current in enumerate(held):
        beside = other_y(current)
        for flip_y, chunk in ((0, current), (1, beside)):
            for flip_core, piece in ((0, chunk), (1, other_core(chunk))):
                chunks.append(((distance, flip_y, flip_core), piece))
    return chunks


def place_of(coords, key):
    z, y, core = coords
    distance, flip_y, flip_core = key
    return (
        lax.rem(z + RINGS - distance, RINGS) * 4
        + (1 - y if flip_y else y) * 2
        + (1 - core if flip_core else core)
    )


def place_kernel(keys, moves, outputs, coords_ref, *refs):
    chunks = refs[: len(keys)]
    outs = refs[-1 - outputs : -1]
    semaphores = refs[-1]
    coords = (coords_ref[0], coords_ref[1], coords_ref[2])
    copies = []
    for key, chunk in zip(keys, chunks):
        block = place_of(coords, key)
        for source_rows, source_columns, out, rows, columns in moves:
            start = pl.multiple_of(block * rows, rows)
            copies.append(
                pltpu.make_async_copy(
                    chunk.at[source_rows, source_columns],
                    outs[out].at[pl.ds(start, rows), columns],
                    semaphores.at[len(copies)],
                )
            )
    for copy in copies:
        copy.start()
    for copy in copies:
        copy.wait()


def place_chunks(coords, chunks, moves, shapes, others=()):
    keys = [key for key, _ in chunks]
    anywhere = pl.BlockSpec(memory_space=pl.ANY)
    return pl.pallas_call(
        functools.partial(place_kernel, keys, moves, len(shapes)),
        out_shape=[jax.ShapeDtypeStruct(shape, jnp.bfloat16) for shape in shapes],
        in_specs=[pl.BlockSpec(memory_space=pltpu.SMEM)] + [anywhere] * (len(chunks) + len(others)),
        out_specs=[pl.BlockSpec(memory_space=pltpu.VMEM)] * len(shapes),
        scratch_shapes=[pltpu.SemaphoreType.DMA((len(chunks) * len(moves),))],
        compiler_params=pltpu.CompilerParams(vmem_limit_bytes=24 * 1024 * 1024),
        cost_estimate=pl.CostEstimate(
            flops=0,
            bytes_accessed=4 * sum(shape[0] * shape[1] for shape in shapes),
            transcendentals=0,
        ),
    )(coords, *[piece for _, piece in chunks], *others)


def weight_keys():
    return [
        (distance, flip_y, flip_core)
        for flip_core in (0, 1)
        for flip_y in (0, 1)
        for distance in range(RINGS)
    ]


def scatter_blocks(grads, low):
    half = grads.shape[0] // 2
    total = grads[:half].astype(jnp.float32) + other_core(grads[half:].astype(low)).astype(
        jnp.float32
    )
    quarter = half // 2
    total = total[:quarter] + other_y(total[quarter:].astype(low)).astype(jnp.float32)
    size = quarter // RINGS
    return ring_sum([total[r * size : (r + 1) * size] for r in range(RINGS)], low)


def pick_blocks(values, order):
    chosen = order[:, None] == jnp.arange(values.shape[0], dtype=jnp.int32)[None, :]
    chosen = chosen.reshape(chosen.shape + (1,) * (values.ndim - 1))
    return jnp.sum(jnp.where(chosen, values[None], 0.0), axis=1)


def attend_forward(query_rows, key_nope, key_rope, values, allowed, scale):
    scores = attention_scores(query_rows, key_nope, key_rope, allowed, scale)
    row_max = jnp.max(scores, axis=-1, keepdims=True)
    log_total = row_max + jnp.log(jnp.sum(jnp.exp(scores - row_max), axis=-1, keepdims=True))
    weights_low = jnp.exp(scores - log_total).astype(jnp.bfloat16)
    attended = jnp.einsum("hij,jhd->ihd", weights_low, values, preferred_element_type=jnp.float32)
    return attended.astype(jnp.bfloat16), log_total


def wide_dot(left, right):
    return jnp.dot(left, right, preferred_element_type=jnp.float32)


def dot_turned(left, right):
    return lax.dot_general(left, right, (((1,), (1,)), ((), ())), preferred_element_type=jnp.float32)


def dot_rows(left, right):
    return lax.dot_general(left, right, (((0,), (0,)), ((), ())), preferred_element_type=jnp.float32)


TILE = 256


def whole(array):
    return pl.BlockSpec(array.shape, lambda i: (0,) * array.ndim)


def load_pieces(pieces, target, semaphores):
    size = pieces[0].shape[0]
    copies = [
        pltpu.make_async_copy(piece, target.at[pl.ds(k * size, size)], semaphores.at[k])
        for k, piece in enumerate(pieces)
    ]
    for copy in copies:
        copy.start()
    for copy in copies:
        copy.wait()


def down_kernel(count, *refs):
    pieces, (weight_ref, grads_ref, rows_ref, semaphores) = refs[:count], refs[count:]

    @pl.when(pl.program_id(0) == 0)
    def _():
        load_pieces(pieces, rows_ref, semaphores)

    size = rows_ref.shape[0] // 4
    for k in range(4):
        part = slice(k * size, (k + 1) * size)
        grads_ref[part, :] = dot_turned(rows_ref[part, :], weight_ref[...]).astype(jnp.bfloat16)


def down_grads(pieces, down):
    count = len(pieces)
    size, depth = pieces[0].shape
    width = down.shape[0]
    rows = count * size
    return pl.pallas_call(
        functools.partial(down_kernel, count),
        grid=(width // TILE,),
        in_specs=[pl.BlockSpec(memory_space=pl.ANY)] * count
        + [pl.BlockSpec((TILE, depth), lambda i: (i, 0))],
        out_specs=[
            pl.BlockSpec((rows, TILE), lambda i: (0, i)),
            pl.BlockSpec((rows, depth), lambda i: (0, 0)),
        ],
        out_shape=[
            jax.ShapeDtypeStruct((rows, width), jnp.bfloat16),
            jax.ShapeDtypeStruct((rows, depth), jnp.bfloat16),
        ],
        scratch_shapes=[pltpu.SemaphoreType.DMA((count,))],
        compiler_params=pltpu.CompilerParams(vmem_limit_bytes=48 * 1024 * 1024),
        cost_estimate=pl.CostEstimate(
            flops=2 * rows * depth * width,
            bytes_accessed=2 * (2 * rows * depth + depth * width + rows * width),
            transcendentals=0,
        ),
    )(*pieces, down)


def out_kernel(count, *refs):
    hidden_ref, weight_ref = refs[:2]
    outs = refs[2:]
    size = outs[0].shape[0]
    for k in range(0, count, 4):
        part = hidden_ref[k * size : (k + 4) * size, :]
        result = wide_dot(part, weight_ref[...]).astype(jnp.bfloat16)
        for j in range(4):
            outs[k + j][...] = result[j * size : (j + 1) * size]


def out_rows(count, hidden, down):
    rows, width = hidden.shape
    depth = down.shape[1]
    size = rows // count
    return pl.pallas_call(
        functools.partial(out_kernel, count),
        grid=(depth // TILE,),
        in_specs=[whole(hidden), pl.BlockSpec((width, TILE), lambda i: (0, i))],
        out_specs=[pl.BlockSpec((size, TILE), lambda i: (0, i))] * count,
        out_shape=[jax.ShapeDtypeStruct((size, depth), jnp.bfloat16)] * count,
        compiler_params=pltpu.CompilerParams(vmem_limit_bytes=48 * 1024 * 1024),
        cost_estimate=pl.CostEstimate(
            flops=2 * rows * depth * width,
            bytes_accessed=2 * (rows * depth + depth * width + rows * width),
            transcendentals=0,
        ),
    )(hidden, down)


def mlp_kernel(tiles, pieces, others, experts_ref, routed_ref, *refs):
    row_refs = refs[:pieces]
    router_ref, gate_col, up_col, down_grad, gate_row, up_row = refs[pieces : pieces + 6]
    outs = refs[pieces + 6 + others :]
    grad_refs = outs[:pieces]
    rows_out, hidden_out, gate_out, up_out, logit_out = outs[pieces : pieces + 5]
    gate_all, up_all, prob_ref, scale_ref, sum_ref, semaphores = outs[pieces + 5 :]
    step = pl.program_id(0)
    third = tiles // 2
    total = rows_out.shape[0]
    size = total // pieces
    lane = lax.broadcasted_iota(jnp.int32, (1, router_ref.shape[1]), 1)

    @pl.when(step == 0)
    def _():
        load_pieces(row_refs, rows_out, semaphores)
        logits = wide_dot(rows_out[...], router_ref[...])
        logits = jnp.where(lane < experts_ref[2], logits, -1e30)
        raised = jnp.exp(logits - jnp.max(logits, axis=1, keepdims=True))
        chances = raised / jnp.sum(raised, axis=1, keepdims=True)
        prob_ref[...] = chances
        for k in (0, 1):
            chance = jnp.sum(jnp.where(lane == experts_ref[k], chances, 0.0), axis=1, keepdims=True)
            scale_ref[k] = routed_ref[:, k : k + 1] * chance
        scale_ref[2] = jnp.ones_like(scale_ref[2])
        sum_ref[...] = jnp.zeros_like(sum_ref)

    @pl.when(step < tiles)
    def _():
        columns = pl.ds(pl.multiple_of(step * TILE, TILE), TILE)
        kind = step // third
        half = total // 2
        for k in (0, 1):
            part = slice(k * half, (k + 1) * half)
            pre_gate = wide_dot(rows_out[part, :], gate_col[...])
            pre_up = wide_dot(rows_out[part, :], up_col[...])
            grads = down_grad[part, :].astype(jnp.float32)
            scale = scale_ref[kind, part, :]
            sigmoid = 1.0 / (1.0 + jnp.exp(-pre_gate))
            silu = pre_gate * sigmoid
            hidden = (silu * pre_up).astype(jnp.bfloat16).astype(jnp.float32)
            sum_ref[kind, part, :] += jnp.sum(hidden * grads, axis=1, keepdims=True)
            grad_hidden = scale * grads
            low_gate = (grad_hidden * pre_up * (sigmoid + silu * (1.0 - sigmoid))).astype(
                jnp.bfloat16
            )
            low_up = (grad_hidden * silu).astype(jnp.bfloat16)
            gate_all[part, columns] = low_gate
            up_all[part, columns] = low_up
            hidden_out[part, :] = (scale * hidden).astype(jnp.bfloat16)
            gate_out[part, :] = low_gate
            up_out[part, :] = low_up

    @pl.when(step == tiles - 1)
    def _():
        grad_logits = jnp.zeros_like(prob_ref)
        for k in (0, 1):
            own = jnp.where(lane == experts_ref[k], 1.0, 0.0)
            grad_logits += scale_ref[k] * sum_ref[k] * (own - prob_ref[...])
        logit_out[...] = grad_logits.astype(jnp.bfloat16)

    @pl.when(step >= tiles)
    def _():
        some = pl.ds(pl.multiple_of((step - tiles) * TILE, TILE), TILE)
        grads = dot_turned(gate_all[...], gate_row[...]) + dot_turned(up_all[...], up_row[...])
        grads += dot_turned(logit_out[...], router_ref[some, :])
        grads = grads.astype(jnp.bfloat16)
        for k in range(pieces):
            grad_refs[k][...] = grads[k * size : (k + 1) * size]


def mlp_plane(distance, experts, routed, rows, down_grad, router, gate, up, kept, others):
    pieces = len(rows)
    size, depth = rows[0].shape
    width = gate.shape[1]
    tiles, columns = width // TILE, depth // TILE
    total = pieces * size
    low = jnp.bfloat16

    def early(i):
        return jnp.minimum(i, tiles - 1)

    def late(i):
        return jnp.maximum(i - tiles, 0)

    tile_spec = pl.BlockSpec((total, TILE), lambda i: (distance, early(i)))
    anywhere = pl.BlockSpec(memory_space=pl.ANY)
    first_kept = 2 + pieces + 6
    results = pl.pallas_call(
        functools.partial(mlp_kernel, tiles, pieces, len(kept) + len(others)),
        grid=(tiles + columns,),
        in_specs=[pl.BlockSpec(memory_space=pltpu.SMEM), whole(routed)]
        + [anywhere] * pieces
        + [
            whole(router),
            pl.BlockSpec((depth, TILE), lambda i: (0, early(i))),
            pl.BlockSpec((depth, TILE), lambda i: (0, early(i))),
            tile_spec,
            pl.BlockSpec((TILE, width), lambda i: (late(i), 0)),
            pl.BlockSpec((TILE, width), lambda i: (late(i), 0)),
        ]
        + [anywhere] * (len(kept) + len(others)),
        out_specs=[pl.BlockSpec((size, TILE), lambda i: (0, late(i)))] * pieces
        + [
            pl.BlockSpec((total, depth), lambda i: (distance, 0)),
            tile_spec,
            tile_spec,
            tile_spec,
            pl.BlockSpec((total, router.shape[1]), lambda i: (distance, 0)),
        ],
        out_shape=[jax.ShapeDtypeStruct((size, depth), low)] * pieces
        + [
            jax.ShapeDtypeStruct((RINGS * total, many), low)
            for many in (depth, width, width, width, router.shape[1])
        ],
        scratch_shapes=[pltpu.VMEM((total, width), low)] * 2
        + [
            pltpu.VMEM((total, router.shape[1]), jnp.float32),
            pltpu.VMEM((3, total, 1), jnp.float32),
            pltpu.VMEM((3, total, 1), jnp.float32),
            pltpu.SemaphoreType.DMA((pieces,)),
        ],
        input_output_aliases={first_kept + k: pieces + k for k in range(len(kept))},
        compiler_params=pltpu.CompilerParams(vmem_limit_bytes=48 * 1024 * 1024),
        cost_estimate=pl.CostEstimate(
            flops=2 * total * depth * width * 4,
            bytes_accessed=2 * (4 * depth * width + 3 * total * depth + 4 * total * width),
            transcendentals=total * width,
        ),
    )(experts, routed, *rows, router, gate, up, down_grad, gate, up, *kept, *others)
    return results[:pieces], results[pieces:]


def gather_body(
    block_input,
    segments,
    counts,
    routes,
    attn_gain,
    w_query,
    w_latent,
    latent_gain,
    w_keyval,
    w_output,
    ffn_gain,
    w_router,
    shared_gate_up,
    shared_down,
    expert_gate_up,
    expert_down,
    cotangent,
):
    f32 = jnp.float32
    bf16 = jnp.bfloat16
    blocks = 16
    index = lax.axis_index("dp")
    x = lax.axis_index("tensor")
    coords = jnp.stack([index // 4, (index // 2) % 2, index % 2]).astype(jnp.int32)
    z, y, core = coords[0], coords[1], coords[2]
    local_rows = block_input.shape[0]
    tokens = 2 * local_rows
    depth = w_query.shape[0]
    query_width = w_query.shape[1]
    heads = query_width // (NOPE + ROPE)
    experts = w_router.shape[1]
    units = expert_gate_up.shape[3]
    shared = shared_gate_up.shape[2] // blocks
    latent_depth = w_keyval.shape[0]
    scale = (NOPE + ROPE) ** (-0.5)

    def both_halves(own, other):
        return jnp.concatenate(
            [jnp.where(x == 0, own, other), jnp.where(x == 0, other, own)], axis=0
        )

    small = jnp.concatenate(
        [
            attn_gain[:, None],
            ffn_gain[:, None],
            w_router,
            jnp.pad(latent_gain, (0, depth - latent_depth))[:, None],
            routes.reshape(depth, -1).astype(bf16),
        ],
        axis=1,
    )
    rows_all = both_halves(block_input, other_x(block_input))
    used = query_width + KVR + ROPE
    first_width = -(-(used + small.shape[1]) // 128) * 128
    first_held = ring_shards(
        jnp.pad(
            jnp.concatenate([w_query, w_latent, small], axis=1),
            ((0, 0), (0, first_width - used - small.shape[1])),
        )
    )
    first_chunks = gather_weight(first_held)
    parts = depth // latent_depth
    keyval_part = w_keyval.shape[1] // parts
    keyval_packed = (
        w_keyval.reshape(latent_depth, parts, keyval_part).transpose(1, 0, 2).reshape(depth, -1)
    )
    second_held = ring_shards(
        after(jnp.concatenate([keyval_packed, w_output.T], axis=1), first_held[3])
    )
    second_chunks = gather_weight(second_held)
    grad_planes = gather_rows(after(cotangent, second_held[3]), "xxxx")
    shared_in = lax.all_to_all(
        after(
            shared_gate_up.reshape(2, depth, blocks, shared)
            .transpose(2, 0, 1, 3)
            .reshape(blocks, 2 * depth, shared),
            first_held[1],
        ),
        "dp",
        split_axis=0,
        concat_axis=0,
        tiled=True,
    ).reshape(blocks, 2, depth, shared)
    shared_out = lax.all_to_all(
        after(shared_down.reshape(blocks, shared, depth), first_held[1]),
        "dp",
        split_axis=0,
        concat_axis=0,
        tiled=True,
    )
    shared_other = other_core(shared_in)
    shared_out_other = other_core(shared_out)
    expert_in_other = other_core(expert_gate_up[0])
    expert_out_other = other_core(expert_down[0])
    hole = -(-units // TILE) * TILE - units

    def side_columns(k):
        return jnp.concatenate(
            [
                expert_gate_up[0, k],
                jnp.zeros((D, hole), bf16),
                expert_in_other[k],
                jnp.zeros((D, hole), bf16),
                shared_in[:, k].reshape(D, shared),
                shared_other[:, k].reshape(D, shared),
                jnp.zeros((D, TILE - 2 * shared), bf16),
            ],
            axis=1,
        )

    gate_weight = side_columns(0)
    up_weight = side_columns(1)
    down_weight = jnp.concatenate(
        [
            expert_down[0],
            jnp.zeros((hole, D), bf16),
            expert_out_other,
            jnp.zeros((hole, D), bf16),
            shared_out.transpose(1, 0, 2).reshape(shared, D),
            shared_out_other.transpose(1, 0, 2).reshape(shared, D),
            jnp.zeros((TILE - 2 * shared, D), bf16),
        ],
        axis=0,
    )
    (first_weight,) = place_chunks(
        coords,
        first_chunks,
        [(pl.ds(0, depth), pl.ds(0, first_width), 0, depth, pl.ds(0, first_width))],
        [(D, first_width)],
        (gate_weight, up_weight, down_weight),
    )
    small = first_weight[:, used:]
    attn_gain_wide = small[:, 0].astype(f32)
    ffn_gain_wide = small[:, 1].astype(f32)
    router_weight = small[:, 2 : 2 + experts]
    latent_gain_wide = (
        small[:, 2 + experts].reshape(blocks, depth)[:, :latent_depth].reshape(-1).astype(f32)
    )
    routes_all = small[:, 3 + experts : 3 + experts + 2 * TOP].reshape(blocks * tokens, TOP)
    chip_experts = jnp.stack([index, index + 1 - 2 * core])
    routed_all = jnp.any(
        routes_all[None] == chip_experts[:, None, None].astype(bf16), axis=2
    ).astype(f32)
    order = jnp.stack(
        [
            place_of(coords, (distance, flip_y, 0)) * 2 + (1 - x if flip_x else x)
            for distance in range(RINGS)
            for flip_x, flip_y in ((0, 0), (0, 1), (1, 0), (1, 1))
        ]
    )
    routed = jnp.stack(
        [
            pick_blocks(one.reshape(blocks * 2, local_rows), order).reshape(RINGS, -1)
            for one in routed_all
        ],
        axis=2,
    )
    keyval_weight, output_turned = place_chunks(
        coords,
        second_chunks,
        [
            (
                pl.ds(k * latent_depth, latent_depth),
                pl.ds(0, keyval_part),
                0,
                latent_depth,
                pl.ds(k * keyval_part, keyval_part),
            )
            for k in range(parts)
        ]
        + [
            (
                pl.ds(0, depth),
                pl.ds(keyval_part, w_output.shape[0]),
                1,
                depth,
                pl.ds(0, w_output.shape[0]),
            )
        ],
        [(KVR, w_keyval.shape[1]), (D, w_output.shape[0])],
    )

    router_wide = jnp.pad(router_weight, ((0, 0), (0, 128 - experts)))

    cosine, sine = rotary_tables(segments[0], ROPE)
    allowed = allowed_pairs(segments[0], counts[0])
    inputs = rows_all.astype(f32)
    first_scale = rms_scale(inputs)
    first_unit = inputs * first_scale
    first_normed = (first_unit * attn_gain_wide).astype(bf16)
    projected = wide_dot(first_normed, first_weight)
    query = projected[:, :query_width].reshape(tokens, heads, NOPE + ROPE)
    query_rows = jnp.concatenate(
        [query[..., :NOPE], rotate(query[..., NOPE:], cosine[:, None, :], sine[:, None, :])],
        axis=-1,
    ).astype(bf16)
    latent = projected[:, query_width : query_width + KVR]
    key_rope = rotate(projected[:, query_width + KVR : used], cosine, sine).astype(bf16)
    latent_scale = rms_scale(latent)
    latent_unit = latent * latent_scale
    latent_normed = (latent_unit * latent_gain_wide).astype(bf16)
    keyval = wide_dot(latent_normed, keyval_weight).astype(bf16).reshape(tokens, heads, NOPE + VD)
    key_nope = keyval[..., :NOPE]
    values = keyval[..., NOPE:]
    attended, log_total = attend_forward(query_rows, key_nope, key_rope, values, allowed, scale)
    attended = attended.reshape(tokens, heads * VD)
    attn_part = dot_turned(attended, output_turned)
    low_rows, high_rows = attn_part[:local_rows], attn_part[local_rows:]
    own_part = jnp.where(x == 0, low_rows, high_rows)
    sent_part = jnp.where(x == 0, high_rows, low_rows).astype(bf16)
    mixed = block_input.astype(f32) + own_part + other_x(sent_part).astype(f32)
    second_scale = rms_scale(mixed)
    second_unit = mixed * second_scale
    second_normed = (second_unit * ffn_gain_wide).astype(bf16)

    down_grad, every_grad = down_grads(
        [piece for plane in grad_planes for piece in plane], down_weight
    )
    row_planes = gather_rows(second_normed, "yxyx")
    expert_ids = jnp.concatenate([chip_experts, jnp.array([experts], jnp.int32)])
    kept = []
    turned, closed = [], []
    for distance in range(RINGS):
        others = list(turned[distance - 2][1:]) if distance > 1 else []
        if distance > 2:
            others += list(closed[distance - 3][1:])
        grads, kept = mlp_plane(
            distance,
            expert_ids,
            routed[distance],
            row_planes[distance],
            down_grad,
            router_wide,
            gate_weight,
            up_weight,
            kept,
            others,
        )
        turned.append(turn_corner(grads, "yxyx"[distance]))
        closed.append(close_plane(turned[distance]))
    grad_second = ring_rows(closed)
    every_row, every_hidden, every_gate_grad, every_up_grad, logit_grads = kept
    out_pieces = out_rows(4 * RINGS, every_hidden, down_weight)
    out_closed = []
    for distance in range(RINGS):
        plane = list(out_pieces[4 * distance : 4 * distance + 4])
        plane[3] = after(plane[3], grad_second)
        plane[2] = after(plane[2], grad_second)
        out_closed.append(close_plane(turn_corner(plane, "x")))
    block_output = mixed + ring_rows(out_closed)

    far = units + hole

    def both_in(grads):
        sent = other_core(dot_rows(every_row, grads[:, far : far + units]).astype(bf16))
        return dot_rows(every_row, grads[:, :units]) + sent.astype(f32)

    grad_expert_gate_up = jnp.stack([both_in(every_gate_grad), both_in(every_up_grad)])[None]
    sent_down = other_core(dot_rows(every_hidden[:, far : far + units], every_grad).astype(bf16))
    grad_expert_down = (
        dot_rows(every_hidden[:, :units], every_grad) + sent_down.astype(f32)
    )[None]
    side_grads = dot_rows(
        every_row,
        jnp.concatenate(
            [every_gate_grad[:, 2 * far :], every_up_grad[:, 2 * far :], logit_grads], axis=1
        ),
    )
    grad_router = side_grads[:, 2 * TILE : 2 * TILE + experts]
    shared_in_grads = jnp.stack(
        [
            side_grads[:, k * TILE : k * TILE + shared]
            + other_core(
                side_grads[:, k * TILE + shared : k * TILE + 2 * shared].astype(bf16)
            ).astype(f32)
            for k in (0, 1)
        ]
    )
    side_down = dot_rows(every_hidden[:, 2 * far :], every_grad)
    shared_down_grads = side_down[:shared] + other_core(
        side_down[shared : 2 * shared].astype(bf16)
    ).astype(f32)
    grad_shared_in = (
        lax.all_to_all(
            shared_in_grads.astype(bf16)
            .reshape(2, blocks, depth, shared)
            .transpose(1, 0, 2, 3)
            .reshape(blocks, 2 * depth, shared),
            "dp",
            split_axis=0,
            concat_axis=0,
            tiled=True,
        )
        .astype(f32)
        .reshape(blocks, 2, depth, shared)
        .transpose(1, 2, 0, 3)
        .reshape(2, depth, blocks * shared)
    )
    grad_shared_down = (
        lax.all_to_all(
            shared_down_grads.astype(bf16).reshape(shared, blocks, depth).transpose(1, 0, 2),
            "dp",
            split_axis=0,
            concat_axis=0,
            tiled=True,
        )
        .astype(f32)
        .reshape(blocks * shared, depth)
    )

    gain_ffn_part = jnp.sum(grad_second * second_unit, axis=0)
    grad_mixed = cotangent.astype(f32) + rms_back(
        grad_second * ffn_gain_wide, second_unit, second_scale
    )
    grad_mixed_low = grad_mixed.astype(bf16)
    grad_attn = both_halves(grad_mixed_low, other_x(grad_mixed_low))

    keys = weight_keys()
    places = [place_of(coords, key) for key in keys]

    def in_key_order(values):
        return jnp.concatenate(
            [lax.dynamic_slice_in_dim(values, place * depth, depth, 1) for place in places], axis=1
        )

    grad_output_weight = scatter_blocks(
        dot_rows(in_key_order(grad_attn), attended).astype(bf16), bf16
    ).T
    grad_attended = (
        wide_dot(grad_attn, output_turned).astype(bf16).reshape(tokens, heads, VD)
    )
    scores = attention_scores(query_rows, key_nope, key_rope, allowed, scale)
    weights = jnp.exp(scores - log_total)
    weights_low = weights.astype(bf16)
    grad_weights = jnp.einsum("ihd,jhd->hij", grad_attended, values, preferred_element_type=f32)
    grad_values = jnp.einsum("hij,ihd->jhd", weights_low, grad_attended, preferred_element_type=f32)
    grad_scores = (
        weights * (grad_weights - jnp.sum(weights * grad_weights, axis=-1, keepdims=True))
    ).astype(bf16)
    grad_query_nope = scale * jnp.einsum(
        "hij,jhd->ihd", grad_scores, key_nope, preferred_element_type=f32
    )
    grad_query_rope = scale * jnp.einsum(
        "hij,jd->ihd", grad_scores, key_rope, preferred_element_type=f32
    )
    grad_key_nope = scale * jnp.einsum(
        "hij,ihd->jhd", grad_scores, query_rows[..., :NOPE], preferred_element_type=f32
    )
    grad_key_rope = scale * jnp.einsum(
        "hij,ihd->jd", grad_scores, query_rows[..., NOPE:], preferred_element_type=f32
    )
    grad_query = (
        jnp.concatenate(
            [grad_query_nope, rotate_back(grad_query_rope, cosine[:, None, :], sine[:, None, :])],
            axis=-1,
        )
        .astype(bf16)
        .reshape(tokens, heads * (NOPE + ROPE))
    )
    grad_keyval = (
        jnp.concatenate([grad_key_nope, grad_values], axis=-1)
        .astype(bf16)
        .reshape(tokens, heads * (NOPE + VD))
    )
    key_order = jnp.stack(places)
    latent_column = jnp.arange(KVR, dtype=jnp.int32)
    wanted = key_order[latent_column // latent_depth] * latent_depth + latent_column % latent_depth
    shuffle = (latent_column[:, None] == wanted[None, :]).astype(bf16)
    latent_in_order = wide_dot(latent_normed, shuffle).astype(bf16)
    grad_keyval_weight = scatter_blocks(dot_rows(latent_in_order, grad_keyval).astype(bf16), bf16)
    grad_latent_normed = dot_turned(grad_keyval, keyval_weight)
    gain_latent_part = jnp.sum(grad_latent_normed * latent_unit, axis=0)
    grad_latent = rms_back(grad_latent_normed * latent_gain_wide, latent_unit, latent_scale)
    grad_latent_all = jnp.concatenate(
        [grad_latent, rotate_back(grad_key_rope, cosine, sine)], axis=-1
    ).astype(bf16)
    grad_projected = jnp.concatenate([grad_query, grad_latent_all], axis=1)
    grad_first_weight = scatter_blocks(
        dot_rows(in_key_order(first_normed), grad_projected).astype(bf16), bf16
    )
    grad_latent_part = grad_first_weight[:, query_width:]
    grad_latent_weight = grad_latent_part + other_x(grad_latent_part)
    grad_first_part = dot_turned(grad_projected, first_weight[:, :used])
    low_rows, high_rows = grad_first_part[:local_rows], grad_first_part[local_rows:]
    sent_part = jnp.where(x == 0, high_rows, low_rows).astype(bf16)
    grad_first = jnp.where(x == 0, low_rows, high_rows) + other_x(sent_part).astype(f32)
    own_inputs = block_input.astype(f32)
    own_scale = rms_scale(own_inputs)
    own_unit = own_inputs * own_scale
    gain_attn_part = jnp.sum(grad_first * own_unit, axis=0)
    grad_input = grad_mixed + rms_back(grad_first * attn_gain_wide, own_unit, own_scale)

    small_grads = jnp.concatenate(
        [
            gain_attn_part.reshape(blocks, 1, depth),
            gain_ffn_part.reshape(blocks, 1, depth),
            grad_router.reshape(blocks, experts, depth),
            jnp.pad(
                gain_latent_part.reshape(blocks, 1, latent_depth),
                ((0, 0), (0, 0), (0, depth - latent_depth)),
            ),
        ],
        axis=1,
    )
    small_grads = scatter_blocks(pick_blocks(small_grads, key_order), f32)[0]
    small_grads = small_grads + other_x(small_grads)
    return (
        block_output,
        grad_input,
        small_grads[0],
        grad_first_weight[:, :query_width],
        grad_latent_weight,
        small_grads[2 + experts, :latent_depth],
        grad_keyval_weight,
        grad_output_weight,
        small_grads[1],
        small_grads[2 : 2 + experts].reshape(depth, experts),
        grad_shared_in,
        grad_shared_down,
        grad_expert_gate_up,
        grad_expert_down,
    )


def solution(mesh):
    in_specs = (
        P(("dp", "tensor"), None),
        P("dp", None),
        P("dp"),
        P("dp", None),
        P("dp"),
        P("dp", "tensor"),
        P("dp", None),
        P("dp"),
        P("dp", "tensor"),
        P("tensor", "dp"),
        P("dp"),
        P("dp", None),
        P(None, "dp", "tensor"),
        P("tensor", "dp"),
        P("dp", None, None, "tensor"),
        P("dp", "tensor", None),
        P(("dp", "tensor"), None),
    )
    out_specs = (
        P(("dp", "tensor"), None),
        P(("dp", "tensor"), None),
        P("dp"),
        P("dp", "tensor"),
        P("dp", None),
        P("dp"),
        P("dp", "tensor"),
        P("tensor", "dp"),
        P("dp"),
        P("dp", None),
        P(None, "dp", "tensor"),
        P("tensor", "dp"),
        P("dp", None, None, "tensor"),
        P("dp", "tensor", None),
    )
    body = gather_body if mesh.shape["dp"] == 16 else exchange_body
    return jax.shard_map(body, mesh=mesh, in_specs=in_specs, out_specs=out_specs, check_vma=False)
```

```python
import functools
import math

import jax
import jax.numpy as jnp
from jax import lax
from jax.experimental import pallas as pl
from jax.experimental.pallas import tpu as pltpu
from jax.sharding import PartitionSpec as P

D = 2048
NOPE = 128
ROPE = 64
VD = 128
KVR = 512
TOP = 6


EPSILON = 1e-06


def rms_scale(values):
    return lax.rsqrt(jnp.mean(values * values, axis=-1, keepdims=True) + EPSILON)


def rms_back(grad_unit, unit_rows, row_scale):
    return row_scale * (
        grad_unit - unit_rows * jnp.mean(grad_unit * unit_rows, axis=-1, keepdims=True)
    )


def rotary_tables(segment_row, width):
    count = segment_row.shape[0]
    position = jnp.arange(count, dtype=jnp.int32)
    same = segment_row[:, None] == segment_row[None, :]
    start = jnp.min(jnp.where(same, position[None, :], count), axis=1)
    offset = (position - start).astype(jnp.float32)
    freq = jnp.exp(jnp.arange(width // 2, dtype=jnp.float32) * (-2.0 * math.log(10000.0) / width))
    angle = offset[:, None] * freq[None, :]
    return (jnp.cos(angle), jnp.sin(angle))


def rotate(values, cosine, sine):
    half = values.shape[-1] // 2
    first = values[..., :half]
    second = values[..., half:]
    return jnp.concatenate(
        [first * cosine - second * sine, second * cosine + first * sine], axis=-1
    )


def rotate_back(grads, cosine, sine):
    half = grads.shape[-1] // 2
    first = grads[..., :half]
    second = grads[..., half:]
    return jnp.concatenate(
        [first * cosine + second * sine, second * cosine - first * sine], axis=-1
    )


def allowed_pairs(segment_row, count):
    position = jnp.arange(segment_row.shape[0], dtype=jnp.int32)
    live = position < count
    same = segment_row[:, None] == segment_row[None, :]
    causal = position[None, :] <= position[:, None]
    return same & causal & live[:, None] & live[None, :] | (position[:, None] == position[None, :])


def attention_scores(query_rows, key_nope, key_rope, allowed, scale):
    scores = jnp.einsum(
        "ihd,jhd->hij", query_rows[..., :NOPE], key_nope, preferred_element_type=jnp.float32
    )
    scores = scores + jnp.einsum(
        "ihd,jd->hij", query_rows[..., NOPE:], key_rope, preferred_element_type=jnp.float32
    )
    return jnp.where(allowed[None], scores * scale, -1e30)


def swiglu_back(gate, upper, grad_hidden, axis):
    sigmoid = jax.nn.sigmoid(gate)
    grad_gate = grad_hidden * upper * sigmoid * (1.0 + gate * (1.0 - sigmoid))
    grad_upper = grad_hidden * gate * sigmoid
    return jnp.stack([grad_gate, grad_upper], axis=axis)


def slot_layout(routes, experts, capacity):
    tokens = routes.shape[0]
    flat = routes.reshape(-1)
    onehot = (flat[:, None] == jnp.arange(experts, dtype=jnp.int32)[None, :]).astype(jnp.int32)
    rank = jnp.arange(flat.shape[0], dtype=jnp.int32)
    earlier = (rank[None, :] < rank[:, None]).astype(jnp.bfloat16)
    before = jnp.dot(
        earlier, onehot.astype(jnp.bfloat16), preferred_element_type=jnp.float32
    ).astype(jnp.int32)
    slot_index = jnp.sum(before * onehot, axis=1)
    target = flat * capacity + slot_index
    token_ids = jnp.arange(flat.shape[0], dtype=jnp.int32) // routes.shape[1]
    owner = jnp.full((experts * capacity,), tokens, jnp.int32).at[target].set(token_ids)
    return (slot_index, target, owner)


def to_expert_major(arrived, groups, local_experts):
    capacity = arrived.shape[1]
    width = arrived.shape[2]
    return (
        arrived.reshape(groups, local_experts, capacity, width)
        .transpose(1, 0, 2, 3)
        .reshape(local_experts, groups * capacity, width)
    )


def from_expert_major(results, groups):
    local_experts = results.shape[0]
    width = results.shape[2]
    capacity = results.shape[1] // groups
    return (
        results.reshape(local_experts, groups, capacity, width)
        .transpose(1, 0, 2, 3)
        .reshape(groups * local_experts, capacity, width)
    )


def exchange_body(
    block_input,
    segments,
    counts,
    routes,
    attn_gain,
    w_query,
    w_latent,
    latent_gain,
    w_keyval,
    w_output,
    ffn_gain,
    w_router,
    shared_gate_up,
    shared_down,
    expert_gate_up,
    expert_down,
    cotangent,
):
    gathered = (
        lax.all_gather(attn_gain, "dp", axis=0, tiled=True),
        lax.all_gather(w_query, "dp", axis=0, tiled=True),
        lax.all_gather(w_latent, "dp", axis=0, tiled=True),
        lax.all_gather(latent_gain, "dp", axis=0, tiled=True),
        lax.all_gather(w_keyval, "dp", axis=0, tiled=True),
        lax.all_gather(w_output, "dp", axis=1, tiled=True),
        lax.all_gather(ffn_gain, "dp", axis=0, tiled=True),
        lax.all_gather(w_router, "dp", axis=0, tiled=True),
        lax.all_gather(shared_gate_up, "dp", axis=1, tiled=True),
        lax.all_gather(shared_down, "dp", axis=1, tiled=True),
    )
    (
        full_attn_gain,
        query_weight,
        latent_weight,
        full_latent_gain,
        keyval_weight,
        output_weight,
        full_ffn_gain,
        router_weight,
        shared_in,
        shared_out,
    ) = gathered
    tensor_rank = lax.axis_index("tensor")
    dp_size = lax.axis_size("dp")
    rows_all = lax.all_gather(block_input, "tensor", axis=0, tiled=True)
    tokens = rows_all.shape[0]
    local_rows = block_input.shape[0]
    heads = query_weight.shape[1] // (NOPE + ROPE)
    experts = router_weight.shape[1]
    local_experts = expert_gate_up.shape[0]
    capacity = 2 * tokens * TOP // experts
    scale = (NOPE + ROPE) ** (-0.5)
    start = tensor_rank * local_rows
    cosine, sine = rotary_tables(segments[0], ROPE)
    allowed = allowed_pairs(segments[0], counts[0])
    attn_gain_wide = full_attn_gain.astype(jnp.float32)
    latent_gain_wide = full_latent_gain.astype(jnp.float32)
    ffn_gain_wide = full_ffn_gain.astype(jnp.float32)
    inputs = rows_all.astype(jnp.float32)
    first_scale = rms_scale(inputs)
    first_unit = inputs * first_scale
    first_normed = (first_unit * attn_gain_wide).astype(jnp.bfloat16)
    query = jnp.dot(first_normed, query_weight, preferred_element_type=jnp.float32).reshape(
        tokens, heads, NOPE + ROPE
    )
    query_rows = jnp.concatenate(
        [query[..., :NOPE], rotate(query[..., NOPE:], cosine[:, None, :], sine[:, None, :])],
        axis=-1,
    ).astype(jnp.bfloat16)
    latent_all = jnp.dot(first_normed, latent_weight, preferred_element_type=jnp.float32)
    latent = latent_all[:, :KVR]
    key_rope = rotate(latent_all[:, KVR:], cosine, sine).astype(jnp.bfloat16)
    latent_scale = rms_scale(latent)
    latent_unit = latent * latent_scale
    latent_normed = (latent_unit * latent_gain_wide).astype(jnp.bfloat16)
    keyval = (
        jnp.dot(latent_normed, keyval_weight, preferred_element_type=jnp.float32)
        .astype(jnp.bfloat16)
        .reshape(tokens, heads, NOPE + VD)
    )
    key_nope = keyval[..., :NOPE]
    values = keyval[..., NOPE:]
    scores = attention_scores(query_rows, key_nope, key_rope, allowed, scale)
    row_max = jnp.max(scores, axis=-1, keepdims=True)
    log_total = row_max + jnp.log(jnp.sum(jnp.exp(scores - row_max), axis=-1, keepdims=True))
    weights_low = jnp.exp(scores - log_total).astype(jnp.bfloat16)
    attended = (
        jnp.einsum("hij,jhd->ihd", weights_low, values, preferred_element_type=jnp.float32)
        .astype(jnp.bfloat16)
        .reshape(tokens, heads * VD)
    )
    attn_part = jnp.dot(attended, output_weight, preferred_element_type=jnp.float32)
    mixed = inputs + lax.psum(attn_part, "tensor")
    second_scale = rms_scale(mixed)
    second_unit = mixed * second_scale
    second_normed = (second_unit * ffn_gain_wide).astype(jnp.bfloat16)
    logits = jnp.dot(second_normed, router_weight, preferred_element_type=jnp.float32)
    probabilities = jax.nn.softmax(logits, axis=-1)
    gate_values = jnp.take_along_axis(probabilities, routes, axis=1)
    shared_pre = jnp.einsum(
        "td,gdf->tgf", second_normed, shared_in, preferred_element_type=jnp.float32
    )
    shared_hidden = (jax.nn.silu(shared_pre[:, 0]) * shared_pre[:, 1]).astype(jnp.bfloat16)
    shared_part = jnp.dot(shared_hidden, shared_out, preferred_element_type=jnp.float32)
    slot_index, target, owner = slot_layout(routes, experts, capacity)
    owner_grid = owner.reshape(experts, capacity)
    padded_rows = jnp.concatenate([second_normed, jnp.zeros((1, D), jnp.bfloat16)], axis=0)
    outgoing = padded_rows[owner_grid]
    arrived = lax.all_to_all(outgoing, "dp", split_axis=0, concat_axis=0, tiled=True)
    expert_rows = to_expert_major(arrived, dp_size, local_experts)
    expert_pre = jnp.einsum(
        "erd,egdf->ergf", expert_rows, expert_gate_up, preferred_element_type=jnp.float32
    )
    expert_hidden = (jax.nn.silu(expert_pre[:, :, 0]) * expert_pre[:, :, 1]).astype(jnp.bfloat16)
    expert_result = jnp.einsum(
        "erf,efd->erd", expert_hidden, expert_down, preferred_element_type=jnp.float32
    )
    returning = from_expert_major(expert_result, dp_size)
    returned = lax.all_to_all(
        returning.astype(jnp.bfloat16), "dp", split_axis=0, concat_axis=0, tiled=True
    ).astype(returning.dtype)
    padded_back = jnp.concatenate([returned.reshape(-1, D), jnp.zeros((1, D), jnp.float32)], axis=0)
    picked = padded_back[target].reshape(tokens, TOP, D)
    routed_part = jnp.sum(gate_values[:, :, None] * picked, axis=1)
    branch_sum = lax.psum_scatter(
        (shared_part + routed_part).astype(jnp.bfloat16), "tensor", scatter_dimension=0, tiled=True
    ).astype(jnp.float32)
    block_output = lax.dynamic_slice_in_dim(mixed, start, local_rows, 0) + branch_sum
    grad_rows = lax.all_gather(cotangent, "tensor", axis=0, tiled=True)
    grad_out = grad_rows.astype(jnp.float32)
    grad_shared_hidden = jnp.dot(grad_rows, shared_out.T, preferred_element_type=jnp.float32)
    grad_shared_out = jnp.dot(shared_hidden.T, grad_rows, preferred_element_type=jnp.float32)
    grad_shared_pre = swiglu_back(shared_pre[:, 0], shared_pre[:, 1], grad_shared_hidden, 1).astype(
        jnp.bfloat16
    )
    grad_shared_in = jnp.einsum(
        "td,tgf->gdf", second_normed, grad_shared_pre, preferred_element_type=jnp.float32
    )
    grad_second = jnp.einsum(
        "tgf,gdf->td", grad_shared_pre, shared_in, preferred_element_type=jnp.float32
    )
    gate_by_slot = (
        jnp.zeros((experts * capacity + 1,), jnp.float32).at[target].set(gate_values.reshape(-1))
    )
    slot_ids = jnp.arange(experts * capacity, dtype=jnp.int32).reshape(experts, capacity)
    padded_grad = jnp.concatenate([grad_out, jnp.zeros((1, D), jnp.float32)], axis=0)
    grad_outgoing = (gate_by_slot[slot_ids][..., None] * padded_grad[owner_grid]).astype(
        jnp.bfloat16
    )
    grad_arrived = lax.all_to_all(grad_outgoing, "dp", split_axis=0, concat_axis=0, tiled=True)
    grad_expert_rows = to_expert_major(grad_arrived, dp_size, local_experts)
    grad_expert_hidden = jnp.einsum(
        "erd,efd->erf", grad_expert_rows, expert_down, preferred_element_type=jnp.float32
    )
    grad_expert_down = jnp.einsum(
        "erf,erd->efd", expert_hidden, grad_expert_rows, preferred_element_type=jnp.float32
    )
    grad_expert_pre = swiglu_back(
        expert_pre[:, :, 0], expert_pre[:, :, 1], grad_expert_hidden, 2
    ).astype(jnp.bfloat16)
    grad_expert_gate_up = jnp.einsum(
        "erd,ergf->egdf", expert_rows, grad_expert_pre, preferred_element_type=jnp.float32
    )
    grad_expert_input = jnp.einsum(
        "ergf,egdf->erd", grad_expert_pre, expert_gate_up, preferred_element_type=jnp.float32
    )
    grad_returning = from_expert_major(grad_expert_input, dp_size)
    grad_returned = lax.all_to_all(
        grad_returning.astype(jnp.bfloat16), "dp", split_axis=0, concat_axis=0, tiled=True
    ).astype(grad_returning.dtype)
    padded_grad_back = jnp.concatenate(
        [grad_returned.reshape(-1, D), jnp.zeros((1, D), jnp.float32)], axis=0
    )
    grad_second = grad_second + jnp.sum(padded_grad_back[target].reshape(tokens, TOP, D), axis=1)
    grad_gates = jnp.sum(grad_out[:, None, :] * picked, axis=-1)
    grad_second, grad_gates = (
        lax.psum(grad_second.astype(jnp.bfloat16), "tensor").astype(jnp.float32),
        lax.psum(grad_gates.astype(jnp.bfloat16), "tensor").astype(jnp.float32),
    )
    chosen = (routes[:, :, None] == jnp.arange(experts, dtype=jnp.int32)[None, None, :]).astype(
        jnp.float32
    )
    grad_probabilities = jnp.sum(chosen * grad_gates[:, :, None], axis=1)
    grad_logits = probabilities * (
        grad_probabilities - jnp.sum(probabilities * grad_probabilities, axis=-1, keepdims=True)
    )
    grad_logits_low = grad_logits.astype(jnp.bfloat16)
    grad_router = jnp.dot(second_normed.T, grad_logits_low, preferred_element_type=jnp.float32)
    grad_second = grad_second + jnp.dot(
        grad_logits_low, router_weight.T, preferred_element_type=jnp.float32
    )
    gain_ffn_grad = jnp.sum(grad_second * second_unit, axis=0)
    grad_mixed = grad_out + rms_back(grad_second * ffn_gain_wide, second_unit, second_scale)
    grad_attn_low = grad_mixed.astype(jnp.bfloat16)
    grad_output_weight = jnp.dot(attended.T, grad_attn_low, preferred_element_type=jnp.float32)
    grad_attended = (
        jnp.dot(grad_attn_low, output_weight.T, preferred_element_type=jnp.float32)
        .astype(jnp.bfloat16)
        .reshape(tokens, heads, VD)
    )
    scores = attention_scores(query_rows, key_nope, key_rope, allowed, scale)
    weights = jnp.exp(scores - log_total)
    weights_low = weights.astype(jnp.bfloat16)
    grad_weights = jnp.einsum(
        "ihd,jhd->hij", grad_attended, values, preferred_element_type=jnp.float32
    )
    grad_values = jnp.einsum(
        "hij,ihd->jhd", weights_low, grad_attended, preferred_element_type=jnp.float32
    )
    grad_scores = (
        weights * (grad_weights - jnp.sum(weights * grad_weights, axis=-1, keepdims=True))
    ).astype(jnp.bfloat16)
    grad_query_nope = (
        jnp.einsum("hij,jhd->ihd", grad_scores, key_nope, preferred_element_type=jnp.float32)
        * scale
    )
    grad_query_rope = (
        jnp.einsum("hij,jd->ihd", grad_scores, key_rope, preferred_element_type=jnp.float32) * scale
    )
    grad_key_nope = (
        jnp.einsum(
            "hij,ihd->jhd", grad_scores, query_rows[..., :NOPE], preferred_element_type=jnp.float32
        )
        * scale
    )
    grad_key_rope = (
        jnp.einsum(
            "hij,ihd->jd", grad_scores, query_rows[..., NOPE:], preferred_element_type=jnp.float32
        )
        * scale
    )
    grad_query = (
        jnp.concatenate(
            [grad_query_nope, rotate_back(grad_query_rope, cosine[:, None, :], sine[:, None, :])],
            axis=-1,
        )
        .astype(jnp.bfloat16)
        .reshape(tokens, heads * (NOPE + ROPE))
    )
    grad_query_weight = jnp.dot(first_normed.T, grad_query, preferred_element_type=jnp.float32)
    grad_first = jnp.dot(grad_query, query_weight.T, preferred_element_type=jnp.float32)
    grad_keyval = (
        jnp.concatenate([grad_key_nope, grad_values], axis=-1)
        .astype(jnp.bfloat16)
        .reshape(tokens, heads * (NOPE + VD))
    )
    grad_keyval_weight = jnp.dot(latent_normed.T, grad_keyval, preferred_element_type=jnp.float32)
    grad_latent_normed = jnp.dot(grad_keyval, keyval_weight.T, preferred_element_type=jnp.float32)
    gain_latent_part = jnp.sum(grad_latent_normed * latent_unit, axis=0)
    grad_latent = rms_back(grad_latent_normed * latent_gain_wide, latent_unit, latent_scale)
    grad_latent_all = jnp.concatenate(
        [grad_latent, rotate_back(grad_key_rope, cosine, sine)], axis=-1
    )
    grad_first, grad_latent_all, gain_latent_grad = (
        lax.psum(grad_first.astype(jnp.bfloat16), "tensor").astype(jnp.float32),
        lax.psum(grad_latent_all.astype(jnp.bfloat16), "tensor").astype(jnp.float32),
        lax.psum(gain_latent_part.astype(jnp.bfloat16), "tensor").astype(jnp.float32),
    )
    grad_latent_low = grad_latent_all.astype(jnp.bfloat16)
    grad_latent_weight = jnp.dot(
        first_normed.T, grad_latent_low, preferred_element_type=jnp.float32
    )
    grad_first = grad_first + jnp.dot(
        grad_latent_low, latent_weight.T, preferred_element_type=jnp.float32
    )
    gain_attn_grad = jnp.sum(grad_first * first_unit, axis=0)
    grad_inputs = grad_mixed + rms_back(grad_first * attn_gain_wide, first_unit, first_scale)
    grad_local = lax.dynamic_slice_in_dim(grad_inputs, start, local_rows, 0)
    summed = (
        lax.psum_scatter(gain_attn_grad, "dp", scatter_dimension=0, tiled=True),
        lax.psum_scatter(grad_query_weight, "dp", scatter_dimension=0, tiled=True),
        lax.psum_scatter(grad_latent_weight, "dp", scatter_dimension=0, tiled=True),
        lax.psum_scatter(gain_latent_grad, "dp", scatter_dimension=0, tiled=True),
        lax.psum_scatter(grad_keyval_weight, "dp", scatter_dimension=0, tiled=True),
        lax.psum_scatter(grad_output_weight, "dp", scatter_dimension=1, tiled=True),
        lax.psum_scatter(gain_ffn_grad, "dp", scatter_dimension=0, tiled=True),
        lax.psum_scatter(grad_router, "dp", scatter_dimension=0, tiled=True),
        lax.psum_scatter(grad_shared_in, "dp", scatter_dimension=1, tiled=True),
        lax.psum_scatter(grad_shared_out, "dp", scatter_dimension=1, tiled=True),
    )
    return (
        block_output,
        grad_local,
        summed[0],
        summed[1],
        summed[2],
        summed[3],
        summed[4],
        summed[5],
        summed[6],
        summed[7],
        summed[8],
        summed[9],
        grad_expert_gate_up,
        grad_expert_down,
    )


RINGS = 4


def ring_step(values):
    return lax.ppermute(values, "dp", [(i, (i + RINGS) % 16) for i in range(16)])


def other_y(values):
    return lax.ppermute(values, "dp", [(i, i ^ 2) for i in range(16)])


def other_core(values):
    return lax.ppermute(values, "dp", [(i, i ^ 1) for i in range(16)])


def other_x(values):
    return lax.ppermute(values, "tensor", [(0, 1), (1, 0)])


def fence_kernel(*refs):
    pass


def after(values, *others):
    anywhere = pl.BlockSpec(memory_space=pl.ANY)
    return pl.pallas_call(
        fence_kernel,
        out_shape=jax.ShapeDtypeStruct(values.shape, values.dtype),
        in_specs=[anywhere] * (1 + len(others)),
        out_specs=anywhere,
        input_output_aliases={0: 0},
    )(values, *others)


def gather_rows(rows, corners):
    planes = []
    current = rows
    for distance in range(RINGS):
        if distance:
            current = ring_step(current)
        beside = other_y(current)
        across = other_x(current)
        corner = other_x(beside) if corners[distance] == "x" else other_y(across)
        planes.append((current, beside, across, corner))
    return planes


def add_low(first, second):
    return (first.astype(jnp.float32) + second.astype(jnp.float32)).astype(jnp.bfloat16)


def turn_corner(plane, direction):
    own, beside, across, corner = plane
    if direction == "x":
        return own, add_low(beside, other_x(corner)), across
    return own, beside, add_low(across, other_y(corner))


def close_plane(turned):
    own, beside, across = turned
    return own, other_y(beside), other_x(across)


def ring_rows(closed):
    moving = None
    for distance in (1, 2, 3, 0):
        own, from_y, from_x = closed[distance]
        total = own.astype(jnp.float32) + from_y.astype(jnp.float32) + from_x.astype(jnp.float32)
        if moving is not None:
            total = total + ring_step(moving).astype(jnp.float32)
        moving = total.astype(jnp.bfloat16)
    return total


def ring_sum(parts, low):
    moving = parts[1]
    for distance in (2, 3, 0):
        moving = ring_step(moving.astype(low)).astype(jnp.float32) + parts[distance]
    return moving


def ring_shards(shard):
    held = [shard]
    for _ in range(RINGS - 1):
        held.append(ring_step(held[-1]))
    return held


def gather_weight(held, others):
    chunks = []
    for distance, current in enumerate(held):
        beside = other_y(after(current, *others) if distance == RINGS - 1 else current)
        for flip_y, chunk in ((0, current), (1, beside)):
            for flip_core, piece in ((0, chunk), (1, other_core(chunk))):
                chunks.append(((distance, flip_y, flip_core), piece))
    return chunks


def place_of(coords, key):
    z, y, core = coords
    distance, flip_y, flip_core = key
    return (
        lax.rem(z + RINGS - distance, RINGS) * 4
        + (1 - y if flip_y else y) * 2
        + (1 - core if flip_core else core)
    )


def weight_keys():
    return [
        (distance, flip_y, flip_core)
        for flip_core in (0, 1)
        for flip_y in (0, 1)
        for distance in range(RINGS)
    ]


def scatter_blocks(grads, low):
    half = grads.shape[0] // 2
    total = grads[:half].astype(jnp.float32) + other_core(grads[half:].astype(low)).astype(
        jnp.float32
    )
    quarter = half // 2
    total = total[:quarter] + other_y(total[quarter:].astype(low)).astype(jnp.float32)
    size = quarter // RINGS
    return ring_sum([total[r * size : (r + 1) * size] for r in range(RINGS)], low)


def pick_blocks(values, order):
    chosen = order[:, None] == jnp.arange(values.shape[0], dtype=jnp.int32)[None, :]
    chosen = chosen.reshape(chosen.shape + (1,) * (values.ndim - 1))
    return jnp.sum(jnp.where(chosen, values[None], 0.0), axis=1)


def wide_dot(left, right):
    return jnp.dot(left, right, preferred_element_type=jnp.float32)


def dot_turned(left, right):
    return lax.dot_general(left, right, (((1,), (1,)), ((), ())), preferred_element_type=jnp.float32)


def dot_rows(left, right):
    return lax.dot_general(left, right, (((0,), (0,)), ((), ())), preferred_element_type=jnp.float32)


TILE = 256


def whole(array):
    return pl.BlockSpec(array.shape, lambda *i: (0,) * array.ndim)


def in_vmem(count):
    return [pl.BlockSpec(memory_space=pltpu.VMEM)] * count


def in_place(count):
    return [pl.BlockSpec(memory_space=pl.ANY)] * count


def head_scores(heads, h, nope_ref, turned_ref, keyval_ref, key_ref, masks):
    span = ROPE // 2 * heads
    column = pl.ds(pl.multiple_of(h * NOPE, NOPE), NOPE)
    key_column = pl.ds(pl.multiple_of(h * (NOPE + VD), NOPE), NOPE)
    scores = dot_turned(nope_ref[:, column], keyval_ref[:, key_column])
    for k in (0, 1):
        part = turned_ref[:, k * span : (k + 1) * span]
        part = jnp.where(masks, part, jnp.zeros_like(part))
        scores += dot_turned(part, key_ref[:, k * span : (k + 1) * span])
    return scores * (NOPE + ROPE) ** (-0.5)


def head_lanes(heads, h):
    span = ROPE // 2 * heads
    lane = lax.broadcasted_iota(jnp.int32, (1, span), 1)
    return (lane >= h * (ROPE // 2)) & (lane < (h + 1) * (ROPE // 2))


def allowed_rows(count, segment_row, segment_column):
    tokens = segment_row.shape[1]
    column = lax.broadcasted_iota(jnp.int32, (tokens, tokens), 0)
    row = lax.broadcasted_iota(jnp.int32, (tokens, tokens), 1)
    live = (column < count) & (row < count) & (row <= column)
    return (segment_row == segment_column) & live | (column == row)


def attend_kernel(
    keys,
    heads,
    sizes,
    place_ref,
    segment_row_ref,
    segment_column_ref,
    cosine_ref,
    sine_ref,
    own_ref,
    other_ref,
    *refs,
):
    depth, query_width, used, latent_depth, keyval_part, first_width = sizes
    chunks = refs[: len(keys)]
    (
        own_out,
        sent_out,
        first_ref,
        keyval_weight_ref,
        output_ref,
        normed_ref,
        nope_ref,
        turned_ref,
        latent_ref,
        key_ref,
        keyval_ref,
        total_ref,
        attended_ref,
        gains_ref,
        latent_gain_ref,
        semaphores,
    ) = refs[len(keys) :]
    f32, bf16 = jnp.float32, jnp.bfloat16
    local_rows = own_ref.shape[0]
    tokens = 2 * local_rows
    coords = (place_ref[0], place_ref[1], place_ref[2])
    x = place_ref[3]
    copies = []
    parts = depth // latent_depth
    for key, chunk in zip(keys, chunks):
        block = place_of(coords, key)
        rows = pl.ds(pl.multiple_of(block * depth, depth), depth)
        small_rows = pl.ds(pl.multiple_of(block * latent_depth, latent_depth), latent_depth)
        moves = [(chunk.at[:, pl.ds(0, first_width)], first_ref.at[rows])]
        for k in range(parts):
            moves.append(
                (
                    chunk.at[
                        pl.ds(k * latent_depth, latent_depth), pl.ds(first_width, keyval_part)
                    ],
                    keyval_weight_ref.at[small_rows, pl.ds(k * keyval_part, keyval_part)],
                )
            )
        moves.append(
            (
                chunk.at[:, pl.ds(first_width + keyval_part, heads * VD)],
                output_ref.at[rows],
            )
        )
        for source, target in moves:
            copies.append(pltpu.make_async_copy(source, target, semaphores.at[len(copies)]))
    for copy in copies:
        copy.start()
    for copy in copies:
        copy.wait()

    edge = query_width + KVR
    spread = jnp.transpose(first_ref[:, edge:].astype(f32))[used - edge : used - edge + 8]
    gains_ref[...] = spread
    gain = spread[0:1]
    source = lax.broadcasted_iota(jnp.int32, (D, KVR), 0)
    target = lax.broadcasted_iota(jnp.int32, (D, KVR), 1)
    wanted = target // latent_depth * depth + target % latent_depth
    chosen = jnp.where(source == wanted, 1.0, 0.0).astype(bf16)
    latent_gain = wide_dot(spread.astype(bf16), chosen)[2:3]
    latent_gain_ref[...] = latent_gain
    for ref, start in ((own_ref, x * local_rows), (other_ref, (1 - x) * local_rows)):
        rows = ref[...].astype(f32)
        unit = rows * lax.rsqrt(jnp.mean(rows * rows, axis=1, keepdims=True) + EPSILON)
        normed_ref[pl.ds(pl.multiple_of(start, local_rows), local_rows), :] = (unit * gain).astype(
            bf16
        )
    nope_width = heads * NOPE
    span = heads * (ROPE // 2)
    half = nope_width // 2
    for k in (0, 1):
        nope_ref[:, k * half : (k + 1) * half] = wide_dot(
            normed_ref[...], first_ref[:, k * half : (k + 1) * half]
        ).astype(bf16)
    turning = wide_dot(normed_ref[...], first_ref[:, nope_width : nope_width + 2 * span])
    cosine, sine = cosine_ref[...], sine_ref[...]
    first, second = turning[:, :span], turning[:, span:]
    turned_ref[:, :span] = (first * cosine - second * sine).astype(bf16)
    turned_ref[:, span:] = (second * cosine + first * sine).astype(bf16)
    latent = wide_dot(normed_ref[...], first_ref[:, query_width : query_width + KVR])
    latent_ref[...] = latent
    tail = wide_dot(normed_ref[...], first_ref[:, query_width + KVR :])
    lane = lax.broadcasted_iota(jnp.int32, (1, tail.shape[1]), 1)
    swapped = jnp.where(
        lane < ROPE // 2,
        -pltpu.roll(tail, tail.shape[1] - ROPE // 2, 1),
        pltpu.roll(tail, ROPE // 2, 1),
    )
    width = tail.shape[1]
    turned_key = tail * cosine[:, :width] + swapped * sine[:, :width]
    turned_key = jnp.where(lane < ROPE, turned_key, 0.0).astype(bf16)
    source = lax.broadcasted_iota(jnp.int32, (width, 2 * span), 0)
    target = lax.broadcasted_iota(jnp.int32, (width, 2 * span), 1)
    wanted = target % (ROPE // 2) + jnp.where(target < span, 0, ROPE // 2)
    key_ref[...] = wide_dot(turned_key, (source == wanted).astype(bf16)).astype(bf16)
    unit = latent * lax.rsqrt(jnp.mean(latent * latent, axis=1, keepdims=True) + EPSILON)
    latent_normed = (unit * latent_gain).astype(bf16)
    half = keyval_ref.shape[1] // 4
    for k in range(4):
        keyval_ref[:, k * half : (k + 1) * half] = wide_dot(
            latent_normed, keyval_weight_ref[:, k * half : (k + 1) * half]
        ).astype(bf16)
    allowed = allowed_rows(place_ref[4], segment_row_ref[...], segment_column_ref[...])
    total_lane = lax.broadcasted_iota(jnp.int32, total_ref.shape, 1)
    total_ref[...] = jnp.zeros_like(total_ref)

    def one_head(h, _):
        scores = head_scores(
            heads, h, nope_ref, turned_ref, keyval_ref, key_ref, head_lanes(heads, h)
        )
        scores = jnp.where(allowed, scores, -1e30)
        most = jnp.max(scores, axis=1, keepdims=True)
        total = most + jnp.log(jnp.sum(jnp.exp(scores - most), axis=1, keepdims=True))
        weights = jnp.exp(scores - total).astype(bf16)
        total_ref[...] += jnp.where(total_lane == h, total, 0.0)
        value_column = pl.ds(pl.multiple_of(h * (NOPE + VD) + NOPE, NOPE), VD)
        attended_ref[:, pl.ds(pl.multiple_of(h * VD, VD), VD)] = wide_dot(
            weights, keyval_ref[:, value_column]
        ).astype(bf16)
        return 0

    lax.fori_loop(0, heads, one_head, 0)
    own = pl.ds(pl.multiple_of(x * local_rows, local_rows), local_rows)
    other = pl.ds(pl.multiple_of((1 - x) * local_rows, local_rows), local_rows)
    pieces = 4
    size = output_ref.shape[0] // pieces
    for k in range(pieces):
        columns = slice(k * size, (k + 1) * size)
        own_out[:, columns] = dot_turned(attended_ref[own, :], output_ref[columns, :])
        sent_out[:, columns] = dot_turned(attended_ref[other, :], output_ref[columns, :]).astype(
            bf16
        )


def attend_forward(place, segments, cosine, sine, own, other, chunks, heads, sizes):
    depth, query_width, used, latent_depth, keyval_part, first_width = sizes
    f32, bf16 = jnp.float32, jnp.bfloat16
    keys = [key for key, _ in chunks]
    local_rows = own.shape[0]
    tokens = 2 * local_rows
    span = heads * (ROPE // 2)
    shapes = [
        ((local_rows, D), f32),
        ((local_rows, D), bf16),
        ((D, first_width), bf16),
        ((KVR, heads * (NOPE + VD)), bf16),
        ((D, heads * VD), bf16),
        ((tokens, D), bf16),
        ((tokens, heads * NOPE), bf16),
        ((tokens, 2 * span), bf16),
        ((tokens, KVR), f32),
        ((tokens, 2 * span), bf16),
        ((tokens, heads * (NOPE + VD)), bf16),
        ((tokens, 128), f32),
        ((tokens, heads * VD), bf16),
        ((8, D), f32),
        ((1, KVR), f32),
    ]
    return pl.pallas_call(
        functools.partial(attend_kernel, keys, heads, sizes),
        out_shape=[jax.ShapeDtypeStruct(*shape) for shape in shapes],
        in_specs=[pl.BlockSpec(memory_space=pltpu.SMEM)] + in_vmem(6) + in_place(len(chunks)),
        out_specs=in_vmem(len(shapes)),
        scratch_shapes=[
            pltpu.SemaphoreType.DMA((len(chunks) * (2 + depth // latent_depth),))
        ],
        compiler_params=pltpu.CompilerParams(vmem_limit_bytes=48 * 1024 * 1024),
        cost_estimate=pl.CostEstimate(
            flops=2 * tokens * D * (first_width + heads * VD + 1024),
            bytes_accessed=4 * D * (first_width + 1536),
            transcendentals=2 * heads * tokens * tokens,
        ),
    )(place, segments, segments.T, cosine, sine, own, other, *[piece for _, piece in chunks])


def attend_back_kernel(
    heads,
    place_ref,
    segment_row_ref,
    segment_column_ref,
    cosine_ref,
    sine_ref,
    own_ref,
    other_ref,
    keyval_weight_ref,
    output_ref,
    nope_ref,
    turned_ref,
    latent_ref,
    key_ref,
    keyval_ref,
    total_ref,
    latent_gain_ref,
    projected_ref,
    keyval_grad_ref,
    latent_out,
    gain_ref,
    grad_ref,
    turn_ref,
    back_ref,
):
    f32, bf16 = jnp.float32, jnp.bfloat16
    local_rows = own_ref.shape[0]
    x = place_ref[3]
    span = heads * (ROPE // 2)
    nope_width = heads * NOPE
    query_width = nope_width + 2 * span
    scale = (NOPE + ROPE) ** (-0.5)
    for ref, start in ((own_ref, x * local_rows), (other_ref, (1 - x) * local_rows)):
        rows = pl.ds(pl.multiple_of(start, local_rows), local_rows)
        for k in (0, 1):
            half = slice(k * nope_width // 2, (k + 1) * nope_width // 2)
            grad_ref[rows, half] = wide_dot(ref[...], output_ref[:, half]).astype(bf16)
    allowed = allowed_rows(place_ref[4], segment_row_ref[...], segment_column_ref[...])
    total_lane = lax.broadcasted_iota(jnp.int32, total_ref.shape, 1)
    turn_ref[...] = jnp.zeros_like(turn_ref)
    back_ref[...] = jnp.zeros_like(back_ref)

    def one_head(h, _):
        mask = head_lanes(heads, h)
        scores = head_scores(heads, h, nope_ref, turned_ref, keyval_ref, key_ref, mask)
        total = jnp.sum(jnp.where(total_lane == h, total_ref[...], 0.0), axis=1, keepdims=True)
        weights = jnp.exp(jnp.where(allowed, scores, -1e30) - total)
        weights_low = weights.astype(bf16)
        column = pl.ds(pl.multiple_of(h * NOPE, NOPE), NOPE)
        key_column = pl.ds(pl.multiple_of(h * (NOPE + VD), NOPE), NOPE)
        value_column = pl.ds(pl.multiple_of(h * (NOPE + VD) + NOPE, NOPE), VD)
        grads = grad_ref[:, column]
        grad_weights = dot_turned(grads, keyval_ref[:, value_column])
        keyval_grad_ref[:, value_column] = dot_rows(weights_low, grads).astype(bf16)
        grad_scores = (
            weights * (grad_weights - jnp.sum(weights * grad_weights, axis=1, keepdims=True))
        ).astype(bf16)
        projected_ref[:, column] = (
            scale * wide_dot(grad_scores, keyval_ref[:, key_column])
        ).astype(bf16)
        keyval_grad_ref[:, key_column] = (
            scale * dot_rows(grad_scores, nope_ref[:, column])
        ).astype(bf16)
        for k in (0, 1):
            part = slice(k * span, (k + 1) * span)
            turn = wide_dot(grad_scores, key_ref[:, part])
            turn_ref[:, part] += jnp.where(mask, turn, 0.0)
            own = turned_ref[:, part]
            own = jnp.where(mask, own, jnp.zeros_like(own))
            back_ref[:, part] += dot_rows(grad_scores, own)
        return 0

    lax.fori_loop(0, heads, one_head, 0)
    cosine, sine = cosine_ref[...], sine_ref[...]
    first, second = scale * turn_ref[:, :span], scale * turn_ref[:, span:]
    projected_ref[:, nope_width : nope_width + span] = (first * cosine + second * sine).astype(bf16)
    projected_ref[:, nope_width + span : query_width] = (second * cosine - first * sine).astype(
        bf16
    )
    folded = []
    for k in (0, 1):
        part = scale * back_ref[:, k * span : (k + 1) * span]
        shift = span // 2
        while shift >= ROPE // 2:
            part = part + pltpu.roll(part, shift, 1)
            shift //= 2
        folded.append(part)
    width = projected_ref.shape[1] - query_width - KVR
    lane = lax.broadcasted_iota(jnp.int32, (1, width), 1)
    first = (folded[0] * cosine + folded[1] * sine)[:, :width]
    second = (folded[1] * cosine - folded[0] * sine)[:, :width]
    projected_ref[:, query_width + KVR :] = jnp.where(
        lane < ROPE // 2, first, jnp.where(lane < ROPE, second, 0.0)
    ).astype(bf16)
    gain = latent_gain_ref[...]
    latent = latent_ref[...]
    row_scale = lax.rsqrt(jnp.mean(latent * latent, axis=1, keepdims=True) + EPSILON)
    unit = latent * row_scale
    latent_out[...] = (unit * gain).astype(bf16)
    grad_normed = dot_turned(keyval_grad_ref[...], keyval_weight_ref[...])
    gain_ref[...] = jnp.sum(grad_normed * unit, axis=0, keepdims=True)
    grad_unit = grad_normed * gain
    projected_ref[:, query_width : query_width + KVR] = (
        row_scale * (grad_unit - unit * jnp.mean(grad_unit * unit, axis=1, keepdims=True))
    ).astype(bf16)


def attend_back(place, segments, cosine, sine, own, other, saved, heads, first_width):
    f32, bf16 = jnp.float32, jnp.bfloat16
    keyval = saved[6]
    tokens = 2 * own.shape[0]
    span = heads * (ROPE // 2)
    return pl.pallas_call(
        functools.partial(attend_back_kernel, heads),
        out_shape=[
            jax.ShapeDtypeStruct((tokens, first_width), bf16),
            jax.ShapeDtypeStruct((tokens, keyval.shape[1]), bf16),
            jax.ShapeDtypeStruct((tokens, KVR), bf16),
            jax.ShapeDtypeStruct((1, KVR), f32),
        ],
        in_specs=[pl.BlockSpec(memory_space=pltpu.SMEM)] + in_vmem(15),
        out_specs=in_vmem(4),
        scratch_shapes=[
            pltpu.VMEM((tokens, heads * NOPE), bf16),
            pltpu.VMEM((tokens, 2 * span), f32),
            pltpu.VMEM((tokens, 2 * span), f32),
        ],
        compiler_params=pltpu.CompilerParams(vmem_limit_bytes=48 * 1024 * 1024),
        cost_estimate=pl.CostEstimate(
            flops=2 * tokens * D * 3000,
            bytes_accessed=2 * D * 1536,
            transcendentals=heads * tokens * tokens,
        ),
    )(
        place,
        segments,
        segments.T,
        cosine,
        sine,
        own,
        other,
        *saved,
    )


def block_grads_kernel(places_ref, left_ref, right_ref, *refs):
    result = dot_rows(left_ref[...], right_ref[...])
    if len(refs) > 1:
        result += refs[0][...].astype(jnp.float32)
    refs[-1][...] = result.astype(jnp.bfloat16)


def block_grads(left, right, places, first, count, arrived=None, others=()):
    rows, width = right.shape
    size = left.shape[1] // places.shape[0]
    block = pl.BlockSpec((size, width), lambda i, where: (i, 0))
    extra = [] if arrived is None else [arrived]
    return pl.pallas_call(
        lambda places_ref, left_ref, right_ref, *refs: block_grads_kernel(
            places_ref, left_ref, right_ref, *refs[: len(extra)], refs[-1]
        ),
        grid_spec=pltpu.PrefetchScalarGridSpec(
            num_scalar_prefetch=1,
            grid=(count,),
            in_specs=[
                pl.BlockSpec((rows, size), lambda i, where: (0, where[first + i])),
                pl.BlockSpec((rows, width), lambda i, where: (0, 0)),
            ]
            + [pl.BlockSpec((size, width), lambda i, where: (first + i, 0))] * len(extra)
            + [pl.BlockSpec(memory_space=pl.ANY)] * len(others),
            out_specs=block,
        ),
        out_shape=jax.ShapeDtypeStruct((count * size, width), jnp.bfloat16),
        cost_estimate=pl.CostEstimate(
            flops=2 * rows * count * size * width,
            bytes_accessed=2 * (count * size * width + rows * width),
            transcendentals=0,
        ),
    )(places, left, right, *extra, *others)


def close_ring(near, arrived):
    size = near.shape[0] // RINGS
    total = near.astype(jnp.float32) + arrived.astype(jnp.float32)
    return ring_sum([total[r * size : (r + 1) * size] for r in range(RINGS)], jnp.bfloat16)


def scatter_product(left, right, places):
    sent = block_grads(left, right, places, 2 * RINGS, 2 * RINGS)
    arrived = other_core(sent)
    far = block_grads(left, right, places, RINGS, RINGS, arrived)
    from_y = other_y(far)
    near = block_grads(left, right, places, 0, RINGS, arrived)
    return close_ring(near, from_y)


def latent_blocks_kernel(places_ref, left_ref, right_ref, out_ref, whole_ref):
    blocks = places_ref.shape[0]
    size = left_ref.shape[1] // blocks
    pieces = 4
    part = right_ref.shape[1] // pieces
    for k in range(pieces):
        columns = slice(k * part, (k + 1) * part)
        whole_ref[:, columns] = dot_rows(left_ref[...], right_ref[:, columns])
    for k in range(blocks):
        start = pl.multiple_of(places_ref[k] * size, size)
        out_ref[k * size : (k + 1) * size, :] = whole_ref[pl.ds(start, size), :].astype(
            jnp.bfloat16
        )


def latent_blocks(left, right, places):
    shape = (left.shape[1], right.shape[1])
    return pl.pallas_call(
        latent_blocks_kernel,
        out_shape=jax.ShapeDtypeStruct(shape, jnp.bfloat16),
        in_specs=[pl.BlockSpec(memory_space=pltpu.SMEM)] + in_vmem(2),
        out_specs=pl.BlockSpec(memory_space=pltpu.VMEM),
        scratch_shapes=[pltpu.VMEM(shape, jnp.float32)],
        compiler_params=pltpu.CompilerParams(vmem_limit_bytes=32 * 1024 * 1024),
    )(places, left, right)


def pack_kernel(heads, query_ref, latent_ref, small_ref, keyval_ref, output_ref, out_ref):
    half = ROPE // 2
    head = NOPE + ROPE
    nope_width = heads * NOPE
    for h in range(heads):
        start = h * head
        out_ref[:, h * NOPE : (h + 1) * NOPE] = query_ref[:, start : start + NOPE]
        for k in (0, 1):
            to = nope_width + k * heads * half + h * half
            out_ref[:, to : to + half] = query_ref[
                :, start + NOPE + k * half : start + NOPE + (k + 1) * half
            ]
    at = heads * head
    edge = at + KVR
    out_ref[:, at:edge] = latent_ref[:, :KVR]
    out_ref[:, edge : edge + 128] = jnp.concatenate([latent_ref[:, KVR:], small_ref[...]], axis=1)
    at = edge + 128
    size = keyval_ref.shape[0]
    parts = out_ref.shape[0] // size
    part = keyval_ref.shape[1] // parts
    for k in range(parts):
        out_ref[k * size : (k + 1) * size, at : at + part] = keyval_ref[
            :, k * part : (k + 1) * part
        ]
    out_ref[:, at + part :] = jnp.transpose(output_ref[...].astype(jnp.float32)).astype(
        jnp.bfloat16
    )


def pack_weights(query, latent, small, keyval, output):
    depth, query_width = query.shape
    heads = query_width // (NOPE + ROPE)
    width = query_width + KVR + 128 + keyval.size // depth + output.shape[0]
    return pl.pallas_call(
        functools.partial(pack_kernel, heads),
        out_shape=jax.ShapeDtypeStruct((depth, width), jnp.bfloat16),
        in_specs=in_vmem(5),
        out_specs=pl.BlockSpec(memory_space=pltpu.VMEM),
    )(query, latent, small, keyval, output)


def load_pieces(pieces, target, semaphores):
    size = pieces[0].shape[0]
    copies = [
        pltpu.make_async_copy(piece, target.at[pl.ds(k * size, size)], semaphores.at[k])
        for k, piece in enumerate(pieces)
    ]
    for copy in copies:
        copy.start()
    for copy in copies:
        copy.wait()


def pack_sides_kernel(units, shared, own_ref, other_ref, near_ref, far_ref, *refs):
    gate_out, up_out = refs[-2:]
    hole = -(-units // TILE) * TILE
    rows = gate_out.shape[0]
    gap = -(-shared // 32) * 32
    for k, out in ((0, gate_out), (1, up_out)):
        part = slice(k * rows, (k + 1) * rows)
        out[:, :units] = own_ref[0, k]
        out[:, units:hole] = jnp.zeros((rows, hole - units), jnp.bfloat16)
        out[:, hole : hole + units] = other_ref[0, k]
        out[:, hole + units : 2 * hole] = jnp.zeros((rows, hole - units), jnp.bfloat16)
        out[:, 2 * hole :] = jnp.zeros((rows, TILE), jnp.bfloat16)
        out[:, 2 * hole : 2 * hole + shared] = near_ref[0, part]
        out[:, 2 * hole + gap : 2 * hole + gap + shared] = far_ref[0, part]


def pack_sides(own, other, near, far, others):
    depth, units = own.shape[2:]
    blocks, rows, shared = near.shape
    rows //= 2
    width = 2 * (-(-units // TILE) * TILE) + TILE
    wide = pl.BlockSpec((1, 2, rows, units), lambda i: (0, 0, i, 0))
    narrow = pl.BlockSpec((1, 2 * rows, shared), lambda i: (i, 0, 0))
    out = pl.BlockSpec((rows, width), lambda i: (i, 0))
    return pl.pallas_call(
        functools.partial(pack_sides_kernel, units, shared),
        grid=(blocks,),
        in_specs=[wide, wide, narrow, narrow] + in_place(len(others)),
        out_specs=[out, out],
        out_shape=[jax.ShapeDtypeStruct((depth, width), jnp.bfloat16)] * 2,
        compiler_params=pltpu.CompilerParams(vmem_limit_bytes=32 * 1024 * 1024),
    )(own, other, near, far, *others)


def pack_down_kernel(units, shared, own_ref, other_ref, near_ref, far_ref, *refs):
    out = refs[-1]
    hole = -(-units // TILE) * TILE
    columns = out.shape[1]
    gap = -(-shared // 32) * 32
    out[:units] = own_ref[0]
    out[units:hole] = jnp.zeros((hole - units, columns), jnp.bfloat16)
    out[hole : hole + units] = other_ref[0]
    out[hole + units : 2 * hole] = jnp.zeros((hole - units, columns), jnp.bfloat16)
    out[2 * hole :] = jnp.zeros((TILE, columns), jnp.bfloat16)
    size = near_ref.shape[2]
    for k in range(columns // size):
        part = slice(k * size, (k + 1) * size)
        out[2 * hole : 2 * hole + shared, part] = near_ref[k]
        out[2 * hole + gap : 2 * hole + gap + shared, part] = far_ref[k]


def pack_down(own, other, near, far, others):
    units, depth = own.shape[1:]
    blocks, shared, size = near.shape
    height = 2 * (-(-units // TILE) * TILE) + TILE
    columns = 4 * size
    wide = pl.BlockSpec((1, units, columns), lambda i: (0, 0, i))
    narrow = pl.BlockSpec((4, shared, size), lambda i: (i, 0, 0))
    return pl.pallas_call(
        functools.partial(pack_down_kernel, units, shared),
        grid=(depth // columns,),
        in_specs=[wide, wide, narrow, narrow] + in_place(len(others)),
        out_specs=pl.BlockSpec((height, columns), lambda i: (0, i)),
        out_shape=jax.ShapeDtypeStruct((height, depth), jnp.bfloat16),
        compiler_params=pltpu.CompilerParams(vmem_limit_bytes=32 * 1024 * 1024),
    )(own, other, near, far, *others)


def expert_grads_kernel(units, extra, rows_ref, gate_ref, up_ref, *refs):
    out = refs[-1]
    for k, grads in ((0, gate_ref), (1, up_ref)):

        @pl.when(pl.program_id(0) == k)
        def _():
            result = dot_rows(rows_ref[...], grads[...])[:, :units]
            if extra:
                result += refs[0][0, 0].astype(jnp.float32)
            out[0, 0] = result.astype(out.dtype)


def expert_grads(rows, gate, up, units, column, arrived, kind, others=()):
    total, depth = rows.shape
    wide = -(-units // TILE) * TILE
    extra = [] if arrived is None else [arrived]
    out = pl.BlockSpec((1, 1, 2 * TILE, units), lambda k, i: (0, k, i, 0))
    side = pl.BlockSpec((total, wide), lambda k, i: (0, column))
    return pl.pallas_call(
        functools.partial(expert_grads_kernel, units, len(extra)),
        grid=(2, depth // (2 * TILE)),
        in_specs=[pl.BlockSpec((total, 2 * TILE), lambda k, i: (0, i)), side, side]
        + [out] * len(extra)
        + in_place(len(others)),
        out_specs=out,
        out_shape=jax.ShapeDtypeStruct((1, 2, depth, units), kind),
        compiler_params=pltpu.CompilerParams(vmem_limit_bytes=48 * 1024 * 1024),
        cost_estimate=pl.CostEstimate(
            flops=4 * total * depth * wide,
            bytes_accessed=4 * total * (depth + wide) + 8 * depth * units,
            transcendentals=0,
        ),
    )(rows, gate, up, *extra, *others)


def down_kernel(count, *refs):
    pieces, (weight_ref, grads_ref, rows_ref, semaphores) = refs[:count], refs[count:]

    @pl.when(pl.program_id(0) == 0)
    def _():
        load_pieces(pieces, rows_ref, semaphores)

    size = rows_ref.shape[0] // 4
    for k in range(4):
        part = slice(k * size, (k + 1) * size)
        grads_ref[part, :] = dot_turned(rows_ref[part, :], weight_ref[...]).astype(jnp.bfloat16)


def down_grads(pieces, down):
    count = len(pieces)
    size, depth = pieces[0].shape
    width = down.shape[0]
    rows = count * size
    return pl.pallas_call(
        functools.partial(down_kernel, count),
        grid=(width // TILE,),
        in_specs=[pl.BlockSpec(memory_space=pl.ANY)] * count
        + [pl.BlockSpec((TILE, depth), lambda i: (i, 0))],
        out_specs=[
            pl.BlockSpec((rows, TILE), lambda i: (0, i)),
            pl.BlockSpec((rows, depth), lambda i: (0, 0)),
        ],
        out_shape=[
            jax.ShapeDtypeStruct((rows, width), jnp.bfloat16),
            jax.ShapeDtypeStruct((rows, depth), jnp.bfloat16),
        ],
        scratch_shapes=[pltpu.SemaphoreType.DMA((count,))],
        compiler_params=pltpu.CompilerParams(vmem_limit_bytes=48 * 1024 * 1024),
        cost_estimate=pl.CostEstimate(
            flops=2 * rows * depth * width,
            bytes_accessed=2 * (2 * rows * depth + depth * width + rows * width),
            transcendentals=0,
        ),
    )(*pieces, down)


def out_kernel(count, *refs):
    hidden_ref, weight_ref = refs[:2]
    outs = refs[2:]
    size = outs[0].shape[0]
    for k in range(0, count, 4):
        part = hidden_ref[k * size : (k + 4) * size, :]
        result = wide_dot(part, weight_ref[...]).astype(jnp.bfloat16)
        for j in range(4):
            outs[k + j][...] = result[j * size : (j + 1) * size]


def out_rows(count, hidden, down):
    rows, width = hidden.shape
    depth = down.shape[1]
    size = rows // count
    return pl.pallas_call(
        functools.partial(out_kernel, count),
        grid=(depth // TILE,),
        in_specs=[whole(hidden), pl.BlockSpec((width, TILE), lambda i: (0, i))],
        out_specs=[pl.BlockSpec((size, TILE), lambda i: (0, i))] * count,
        out_shape=[jax.ShapeDtypeStruct((size, depth), jnp.bfloat16)] * count,
        compiler_params=pltpu.CompilerParams(vmem_limit_bytes=48 * 1024 * 1024),
        cost_estimate=pl.CostEstimate(
            flops=2 * rows * depth * width,
            bytes_accessed=2 * (rows * depth + depth * width + rows * width),
            transcendentals=0,
        ),
    )(hidden, down)


def mlp_kernel(tiles, pieces, others, experts_ref, routed_ref, *refs):
    row_refs = refs[:pieces]
    router_ref, gate_col, up_col, down_grad, gate_row, up_row = refs[pieces : pieces + 6]
    outs = refs[pieces + 6 + others :]
    grad_refs = outs[:pieces]
    rows_out, hidden_out, gate_out, up_out, logit_out = outs[pieces : pieces + 5]
    gate_all, up_all, prob_ref, scale_ref, sum_ref, semaphores = outs[pieces + 5 :]
    step = pl.program_id(0)
    third = tiles // 2
    total = rows_out.shape[0]
    size = total // pieces
    lane = lax.broadcasted_iota(jnp.int32, (1, router_ref.shape[1]), 1) - experts_ref[3]

    @pl.when(step == 0)
    def _():
        load_pieces(row_refs, rows_out, semaphores)
        logits = wide_dot(rows_out[...], router_ref[...])
        logits = jnp.where((lane >= 0) & (lane < experts_ref[2]), logits, -1e30)
        raised = jnp.exp(logits - jnp.max(logits, axis=1, keepdims=True))
        chances = raised / jnp.sum(raised, axis=1, keepdims=True)
        prob_ref[...] = chances
        for k in (0, 1):
            chance = jnp.sum(jnp.where(lane == experts_ref[k], chances, 0.0), axis=1, keepdims=True)
            scale_ref[k] = routed_ref[:, k : k + 1] * chance
        scale_ref[2] = jnp.ones_like(scale_ref[2])
        sum_ref[...] = jnp.zeros_like(sum_ref)

    @pl.when(step < tiles)
    def _():
        columns = pl.ds(pl.multiple_of(step * TILE, TILE), TILE)
        kind = step // third
        half = total // 2
        for k in (0, 1):
            part = slice(k * half, (k + 1) * half)
            pre_gate = wide_dot(rows_out[part, :], gate_col[...])
            pre_up = wide_dot(rows_out[part, :], up_col[...])
            grads = down_grad[part, :].astype(jnp.float32)
            scale = scale_ref[kind, part, :]
            sigmoid = 1.0 / (1.0 + jnp.exp(-pre_gate))
            silu = pre_gate * sigmoid
            hidden = (silu * pre_up).astype(jnp.bfloat16).astype(jnp.float32)
            sum_ref[kind, part, :] += jnp.sum(hidden * grads, axis=1, keepdims=True)
            grad_hidden = scale * grads
            low_gate = (grad_hidden * pre_up * (sigmoid + silu * (1.0 - sigmoid))).astype(
                jnp.bfloat16
            )
            low_up = (grad_hidden * silu).astype(jnp.bfloat16)
            gate_all[part, columns] = low_gate
            up_all[part, columns] = low_up
            hidden_out[part, :] = (scale * hidden).astype(jnp.bfloat16)
            gate_out[part, :] = low_gate
            up_out[part, :] = low_up

    @pl.when(step == tiles - 1)
    def _():
        grad_logits = jnp.zeros_like(prob_ref)
        for k in (0, 1):
            own = jnp.where(lane == experts_ref[k], 1.0, 0.0)
            grad_logits += scale_ref[k] * sum_ref[k] * (own - prob_ref[...])
        logit_out[...] = grad_logits.astype(jnp.bfloat16)

    @pl.when(step >= tiles)
    def _():
        some = pl.ds(pl.multiple_of((step - tiles) * 2 * TILE, TILE), 2 * TILE)
        grads = dot_turned(gate_all[...], gate_row[...]) + dot_turned(up_all[...], up_row[...])
        grads += dot_turned(logit_out[...], router_ref[some, :])
        grads = grads.astype(jnp.bfloat16)
        for k in range(pieces):
            grad_refs[k][...] = grads[k * size : (k + 1) * size]


def mlp_plane(distance, experts, routed, rows, down_grad, router, gate, up, kept, others):
    pieces = len(rows)
    size, depth = rows[0].shape
    width = gate.shape[1]
    tiles, columns = width // TILE, depth // (2 * TILE)
    total = pieces * size
    low = jnp.bfloat16

    def early(i):
        return jnp.minimum(i, tiles - 1)

    def late(i):
        return jnp.maximum(i - tiles, 0)

    tile_spec = pl.BlockSpec((total, TILE), lambda i: (distance, early(i)))
    anywhere = pl.BlockSpec(memory_space=pl.ANY)
    first_kept = 2 + pieces + 6
    results = pl.pallas_call(
        functools.partial(mlp_kernel, tiles, pieces, len(kept) + len(others)),
        grid=(tiles + columns,),
        in_specs=[pl.BlockSpec(memory_space=pltpu.SMEM), whole(routed)]
        + [anywhere] * pieces
        + [
            pl.BlockSpec((depth, 128), lambda i: (0, router.shape[1] // 128 - 1)),
            pl.BlockSpec((depth, TILE), lambda i: (0, early(i))),
            pl.BlockSpec((depth, TILE), lambda i: (0, early(i))),
            tile_spec,
            pl.BlockSpec((2 * TILE, width), lambda i: (late(i), 0)),
            pl.BlockSpec((2 * TILE, width), lambda i: (late(i), 0)),
        ]
        + [anywhere] * (len(kept) + len(others)),
        out_specs=[pl.BlockSpec((size, 2 * TILE), lambda i: (0, late(i)))] * pieces
        + [
            pl.BlockSpec((total, depth), lambda i: (distance, 0)),
            tile_spec,
            tile_spec,
            tile_spec,
            pl.BlockSpec((total, 128), lambda i: (distance, 0)),
        ],
        out_shape=[jax.ShapeDtypeStruct((size, depth), low)] * pieces
        + [
            jax.ShapeDtypeStruct((RINGS * total, many), low)
            for many in (depth, width, width, width, 128)
        ],
        scratch_shapes=[pltpu.VMEM((total, width), low)] * 2
        + [
            pltpu.VMEM((total, 128), jnp.float32),
            pltpu.VMEM((3, total, 1), jnp.float32),
            pltpu.VMEM((3, total, 1), jnp.float32),
            pltpu.SemaphoreType.DMA((pieces,)),
        ],
        input_output_aliases={first_kept + k: pieces + k for k in range(len(kept))},
        compiler_params=pltpu.CompilerParams(vmem_limit_bytes=48 * 1024 * 1024),
        cost_estimate=pl.CostEstimate(
            flops=2 * total * depth * width * 4,
            bytes_accessed=2 * (4 * depth * width + 3 * total * depth + 4 * total * width),
            transcendentals=total * width,
        ),
    )(experts, routed, *rows, router, gate, up, down_grad, gate, up, *kept, *others)
    return results[:pieces], results[pieces:]


def gather_body(
    block_input,
    segments,
    counts,
    routes,
    attn_gain,
    w_query,
    w_latent,
    latent_gain,
    w_keyval,
    w_output,
    ffn_gain,
    w_router,
    shared_gate_up,
    shared_down,
    expert_gate_up,
    expert_down,
    cotangent,
):
    f32 = jnp.float32
    bf16 = jnp.bfloat16
    blocks = 16
    index = lax.axis_index("dp")
    x = lax.axis_index("tensor")
    coords = jnp.stack([index // 4, (index // 2) % 2, index % 2]).astype(jnp.int32)
    core = coords[2]
    place = jnp.concatenate([coords, x.astype(jnp.int32)[None], counts])
    local_rows = block_input.shape[0]
    tokens = 2 * local_rows
    depth = w_query.shape[0]
    query_width = w_query.shape[1]
    heads = query_width // (NOPE + ROPE)
    experts = w_router.shape[1]
    units = expert_gate_up.shape[3]
    shared = shared_gate_up.shape[2] // blocks
    latent_depth = w_keyval.shape[0]

    used = query_width + KVR + ROPE
    small = jnp.concatenate(
        [
            attn_gain[:, None],
            ffn_gain[:, None],
            jnp.pad(latent_gain, (0, depth - latent_depth))[:, None],
            w_router,
            routes.reshape(depth, -1).astype(bf16),
            jnp.zeros((depth, 128 - ROPE - 3 - experts - 2 * TOP), bf16),
        ],
        axis=1,
    )
    first_width = query_width + KVR + 128
    shards = pack_weights(w_query, w_latent, small, w_keyval, w_output)
    held = ring_shards(shards)
    other_input = other_x(block_input)
    expert_in_other = other_core(expert_gate_up)
    expert_out_other = other_core(expert_down)

    shared_in = lax.all_to_all(
        after(
            shared_gate_up.reshape(2, depth, blocks, shared)
            .transpose(2, 0, 1, 3)
            .reshape(blocks, 2 * depth, shared),
            held[1],
        ),
        "dp",
        split_axis=0,
        concat_axis=0,
        tiled=True,
    )
    shared_out = lax.all_to_all(
        after(shared_down.reshape(blocks, shared, depth), held[1]),
        "dp",
        split_axis=0,
        concat_axis=0,
        tiled=True,
    )
    gate_weight, up_weight = pack_sides(
        expert_gate_up, expert_in_other, shared_in, other_core(shared_in), (held[2],)
    )
    down_weight = pack_down(
        expert_down, expert_out_other, shared_out, other_core(shared_out), (held[2],)
    )
    chunks = gather_weight(held, (gate_weight, up_weight, down_weight))
    grad_planes = gather_rows(after(cotangent, held[3]), "xyxy")

    cosine, sine = rotary_tables(segments[0], ROPE)
    cosine = jnp.tile(cosine, (1, heads))
    sine = jnp.tile(sine, (1, heads))
    sizes = (depth, query_width, used, latent_depth, w_keyval.shape[1] * latent_depth // depth, first_width)
    (
        own_part,
        sent_part,
        first_weight,
        keyval_weight,
        output_turned,
        first_normed,
        nope,
        turned_query,
        latent,
        key,
        keyval,
        total,
        attended,
        gains,
        latent_gain_row,
    ) = attend_forward(
        place, segments, cosine, sine, block_input, other_input, chunks, heads, sizes
    )
    attn_gain_wide, ffn_gain_wide = gains[0], gains[1]
    mixed = block_input.astype(f32) + own_part + other_x(sent_part).astype(f32)
    second_scale = rms_scale(mixed)
    second_unit = mixed * second_scale
    second_normed = (second_unit * ffn_gain_wide).astype(bf16)

    routes_at = used + 3 + experts
    routes_all = first_weight[:, routes_at : routes_at + 2 * TOP].reshape(blocks * tokens, TOP)
    chip_experts = jnp.stack([index, index + 1 - 2 * core]).astype(jnp.int32)
    routed_all = jnp.any(
        routes_all[None] == chip_experts[:, None, None].astype(bf16), axis=2
    ).astype(f32)
    order = jnp.stack(
        [
            place_of(coords, (distance, flip_y, 0)) * 2 + (1 - x if flip_x else x)
            for distance in range(RINGS)
            for flip_x, flip_y in ((0, 0), (0, 1), (1, 0), (1, 1))
        ]
    )
    routed = jnp.stack(
        [
            pick_blocks(one.reshape(blocks * 2, local_rows), order).reshape(RINGS, -1)
            for one in routed_all
        ],
        axis=2,
    )

    down_grad, every_grad = down_grads(
        [piece for plane in grad_planes for piece in plane], down_weight
    )
    corners = "yxyx"
    row_planes = gather_rows(second_normed, corners)
    expert_ids = jnp.concatenate(
        [chip_experts, jnp.array([experts, used + 3 - query_width - KVR], jnp.int32)]
    )
    kept = []
    turned, closed = [], []
    for distance in range(RINGS):
        others = list(turned[distance - 2][1:]) if distance > 1 else []
        if distance > 2:
            others += list(closed[distance - 3][1:])
        grads, kept = mlp_plane(
            distance,
            expert_ids,
            routed[distance],
            row_planes[distance],
            down_grad,
            first_weight,
            gate_weight,
            up_weight,
            kept,
            others,
        )
        turned.append(turn_corner(grads, corners[distance]))
        if distance < RINGS - 1:
            closed.append(close_plane(turned[distance]))
    every_row, every_hidden, every_gate_grad, every_up_grad, logit_grads = kept
    out_pieces = out_rows(4 * RINGS, every_hidden, down_weight)
    own, beside, across = turned[3]
    closed.append(close_plane((own, after(beside, out_pieces[0]), after(across, out_pieces[0]))))
    grad_second = ring_rows(closed)
    out_closed = []
    for distance in range(RINGS):
        plane = list(out_pieces[4 * distance : 4 * distance + 4])
        plane[3] = after(plane[3], grad_second)
        plane[2] = after(plane[2], grad_second)
        out_closed.append(close_plane(turn_corner(plane, "x")))
    block_output = mixed + ring_rows(out_closed)

    wide = -(-units // TILE) * TILE
    arrived_in = other_core(
        expert_grads(every_row, every_gate_grad, every_up_grad, units, 1, None, bf16)
    )
    arrived_down = other_core(
        dot_rows(every_hidden[:, wide : wide + units], every_grad).astype(bf16)
    )
    side_grads = dot_rows(
        every_row,
        jnp.concatenate(
            [every_gate_grad[:, 2 * wide :], every_up_grad[:, 2 * wide :], logit_grads], axis=1
        ),
    )
    router_at = 2 * TILE + used + 3 - query_width - KVR
    grad_router = side_grads[:, router_at : router_at + experts]
    gap = -(-shared // 32) * 32
    shared_in_grads = jnp.stack(
        [
            side_grads[:, k * TILE : k * TILE + shared]
            + other_core(
                side_grads[:, k * TILE + gap : k * TILE + gap + shared].astype(bf16)
            ).astype(f32)
            for k in (0, 1)
        ]
    )
    side_down = dot_rows(every_hidden[:, 2 * wide :], every_grad)
    shared_down_grads = side_down[:shared] + other_core(
        side_down[gap : gap + shared].astype(bf16)
    ).astype(f32)
    grad_shared_in = (
        lax.all_to_all(
            shared_in_grads.astype(bf16)
            .reshape(2, blocks, depth, shared)
            .transpose(1, 0, 2, 3)
            .reshape(blocks, 2 * depth, shared),
            "dp",
            split_axis=0,
            concat_axis=0,
            tiled=True,
        )
        .astype(f32)
        .reshape(blocks, 2, depth, shared)
        .transpose(1, 2, 0, 3)
        .reshape(2, depth, blocks * shared)
    )
    grad_shared_down = (
        lax.all_to_all(
            shared_down_grads.astype(bf16).reshape(shared, blocks, depth).transpose(1, 0, 2),
            "dp",
            split_axis=0,
            concat_axis=0,
            tiled=True,
        )
        .astype(f32)
        .reshape(blocks * shared, depth)
    )

    gain_ffn_part = jnp.sum(grad_second * second_unit, axis=0)
    grad_mixed = cotangent.astype(f32) + rms_back(
        grad_second * ffn_gain_wide, second_unit, second_scale
    )
    grad_mixed_low = grad_mixed.astype(bf16)
    other_grad = other_x(grad_mixed_low)

    places = jnp.stack([place_of(coords, key_of) for key_of in weight_keys()]).astype(jnp.int32)
    projected_grad, keyval_grad, latent_normed, gain_latent_part = attend_back(
        place,
        segments,
        cosine,
        sine,
        grad_mixed_low,
        other_grad,
        (keyval_weight, output_turned, nope, turned_query, latent, key, keyval, total, latent_gain_row),
        heads,
        first_width,
    )
    grad_attn = jnp.concatenate(
        [
            jnp.where(x == 0, grad_mixed_low, other_grad),
            jnp.where(x == 0, other_grad, grad_mixed_low),
        ],
        axis=0,
    )
    grad_output_weight = scatter_product(grad_attn, attended, places).T
    grad_keyval_weight = scatter_blocks(latent_blocks(latent_normed, keyval_grad, places), bf16)

    sent = block_grads(first_normed, projected_grad, places, 2 * RINGS, 2 * RINGS)
    arrived = other_core(sent)
    far = block_grads(first_normed, projected_grad, places, RINGS, RINGS, arrived)
    from_y = other_y(far)
    grad_expert_gate_up = expert_grads(
        every_row, every_gate_grad, every_up_grad, units, 0, arrived_in, f32, (arrived,)
    )
    grad_expert_down = (
        dot_rows(every_hidden[:, :units], every_grad) + arrived_down.astype(f32)
    )[None]
    near = block_grads(
        first_normed, projected_grad, places, 0, RINGS, arrived, (grad_expert_gate_up,)
    )
    grad_first_weight = close_ring(near, from_y)
    nope_width = heads * NOPE
    span = heads * (ROPE // 2)
    grad_query_weight = jnp.concatenate(
        [
            grad_first_weight[:, :nope_width].reshape(depth, heads, NOPE),
            grad_first_weight[:, nope_width : nope_width + span].reshape(depth, heads, -1),
            grad_first_weight[:, nope_width + span : query_width].reshape(depth, heads, -1),
        ],
        axis=2,
    ).reshape(depth, query_width)
    grad_latent_part = grad_first_weight[:, query_width:used]
    grad_latent_weight = grad_latent_part + other_x(grad_latent_part)
    grad_first_part = dot_turned(projected_grad, first_weight)
    low_rows, high_rows = grad_first_part[:local_rows], grad_first_part[local_rows:]
    sent_rows = jnp.where(x == 0, high_rows, low_rows).astype(bf16)
    grad_first = jnp.where(x == 0, low_rows, high_rows) + other_x(sent_rows).astype(f32)
    own_inputs = block_input.astype(f32)
    own_scale = rms_scale(own_inputs)
    own_unit = own_inputs * own_scale
    gain_attn_part = jnp.sum(grad_first * own_unit, axis=0)
    grad_input = grad_mixed + rms_back(grad_first * attn_gain_wide, own_unit, own_scale)

    small_grads = jnp.concatenate(
        [
            gain_attn_part.reshape(blocks, 1, depth),
            gain_ffn_part.reshape(blocks, 1, depth),
            grad_router.reshape(blocks, experts, depth),
            jnp.pad(
                gain_latent_part.reshape(blocks, 1, latent_depth),
                ((0, 0), (0, 0), (0, depth - latent_depth)),
            ),
        ],
        axis=1,
    )
    small_grads = scatter_blocks(pick_blocks(small_grads, places), f32)[0]
    small_grads = small_grads + other_x(small_grads)
    return (
        block_output,
        grad_input,
        small_grads[0],
        grad_query_weight,
        grad_latent_weight,
        small_grads[2 + experts, :latent_depth],
        grad_keyval_weight,
        grad_output_weight,
        small_grads[1],
        small_grads[2 : 2 + experts].reshape(depth, experts),
        grad_shared_in,
        grad_shared_down,
        grad_expert_gate_up,
        grad_expert_down,
    )


def solution(mesh):
    in_specs = (
        P(("dp", "tensor"), None),
        P("dp", None),
        P("dp"),
        P("dp", None),
        P("dp"),
        P("dp", "tensor"),
        P("dp", None),
        P("dp"),
        P("dp", "tensor"),
        P("tensor", "dp"),
        P("dp"),
        P("dp", None),
        P(None, "dp", "tensor"),
        P("tensor", "dp"),
        P("dp", None, None, "tensor"),
        P("dp", "tensor", None),
        P(("dp", "tensor"), None),
    )
    out_specs = (
        P(("dp", "tensor"), None),
        P(("dp", "tensor"), None),
        P("dp"),
        P("dp", "tensor"),
        P("dp", None),
        P("dp"),
        P("dp", "tensor"),
        P("tensor", "dp"),
        P("dp"),
        P("dp", None),
        P(None, "dp", "tensor"),
        P("tensor", "dp"),
        P("dp", None, None, "tensor"),
        P("dp", "tensor", None),
    )
    body = gather_body if mesh.shape["dp"] == 16 else exchange_body
    return jax.shard_map(body, mesh=mesh, in_specs=in_specs, out_specs=out_specs, check_vma=False)
```

```python
import functools
import math

import jax
import jax.numpy as jnp
from jax import lax
from jax.experimental import pallas as pl
from jax.experimental.pallas import tpu as pltpu
from jax.sharding import PartitionSpec as P

D = 2048
NOPE = 128
ROPE = 64
VD = 128
KVR = 512
TOP = 6


EPSILON = 1e-06


def rms_scale(values):
    return lax.rsqrt(jnp.mean(values * values, axis=-1, keepdims=True) + EPSILON)


def rms_back(grad_unit, unit_rows, row_scale):
    return row_scale * (
        grad_unit - unit_rows * jnp.mean(grad_unit * unit_rows, axis=-1, keepdims=True)
    )


def rotary_tables(segment_row, width):
    count = segment_row.shape[0]
    position = jnp.arange(count, dtype=jnp.int32)
    same = segment_row[:, None] == segment_row[None, :]
    start = jnp.min(jnp.where(same, position[None, :], count), axis=1)
    offset = (position - start).astype(jnp.float32)
    freq = jnp.exp(jnp.arange(width // 2, dtype=jnp.float32) * (-2.0 * math.log(10000.0) / width))
    angle = offset[:, None] * freq[None, :]
    return (jnp.cos(angle), jnp.sin(angle))


def rotate(values, cosine, sine):
    half = values.shape[-1] // 2
    first = values[..., :half]
    second = values[..., half:]
    return jnp.concatenate(
        [first * cosine - second * sine, second * cosine + first * sine], axis=-1
    )


def rotate_back(grads, cosine, sine):
    half = grads.shape[-1] // 2
    first = grads[..., :half]
    second = grads[..., half:]
    return jnp.concatenate(
        [first * cosine + second * sine, second * cosine - first * sine], axis=-1
    )


def allowed_pairs(segment_row, count):
    position = jnp.arange(segment_row.shape[0], dtype=jnp.int32)
    live = position < count
    same = segment_row[:, None] == segment_row[None, :]
    causal = position[None, :] <= position[:, None]
    return same & causal & live[:, None] & live[None, :] | (position[:, None] == position[None, :])


def attention_scores(query_rows, key_nope, key_rope, allowed, scale):
    scores = jnp.einsum(
        "ihd,jhd->hij", query_rows[..., :NOPE], key_nope, preferred_element_type=jnp.float32
    )
    scores = scores + jnp.einsum(
        "ihd,jd->hij", query_rows[..., NOPE:], key_rope, preferred_element_type=jnp.float32
    )
    return jnp.where(allowed[None], scores * scale, -1e30)


def swiglu_back(gate, upper, grad_hidden, axis):
    sigmoid = jax.nn.sigmoid(gate)
    grad_gate = grad_hidden * upper * sigmoid * (1.0 + gate * (1.0 - sigmoid))
    grad_upper = grad_hidden * gate * sigmoid
    return jnp.stack([grad_gate, grad_upper], axis=axis)


def slot_layout(routes, experts, capacity):
    tokens = routes.shape[0]
    flat = routes.reshape(-1)
    onehot = (flat[:, None] == jnp.arange(experts, dtype=jnp.int32)[None, :]).astype(jnp.int32)
    rank = jnp.arange(flat.shape[0], dtype=jnp.int32)
    earlier = (rank[None, :] < rank[:, None]).astype(jnp.bfloat16)
    before = jnp.dot(
        earlier, onehot.astype(jnp.bfloat16), preferred_element_type=jnp.float32
    ).astype(jnp.int32)
    slot_index = jnp.sum(before * onehot, axis=1)
    target = flat * capacity + slot_index
    token_ids = jnp.arange(flat.shape[0], dtype=jnp.int32) // routes.shape[1]
    owner = jnp.full((experts * capacity,), tokens, jnp.int32).at[target].set(token_ids)
    return (slot_index, target, owner)


def to_expert_major(arrived, groups, local_experts):
    capacity = arrived.shape[1]
    width = arrived.shape[2]
    return (
        arrived.reshape(groups, local_experts, capacity, width)
        .transpose(1, 0, 2, 3)
        .reshape(local_experts, groups * capacity, width)
    )


def from_expert_major(results, groups):
    local_experts = results.shape[0]
    width = results.shape[2]
    capacity = results.shape[1] // groups
    return (
        results.reshape(local_experts, groups, capacity, width)
        .transpose(1, 0, 2, 3)
        .reshape(groups * local_experts, capacity, width)
    )


def exchange_body(
    block_input,
    segments,
    counts,
    routes,
    attn_gain,
    w_query,
    w_latent,
    latent_gain,
    w_keyval,
    w_output,
    ffn_gain,
    w_router,
    shared_gate_up,
    shared_down,
    expert_gate_up,
    expert_down,
    cotangent,
):
    gathered = (
        lax.all_gather(attn_gain, "dp", axis=0, tiled=True),
        lax.all_gather(w_query, "dp", axis=0, tiled=True),
        lax.all_gather(w_latent, "dp", axis=0, tiled=True),
        lax.all_gather(latent_gain, "dp", axis=0, tiled=True),
        lax.all_gather(w_keyval, "dp", axis=0, tiled=True),
        lax.all_gather(w_output, "dp", axis=1, tiled=True),
        lax.all_gather(ffn_gain, "dp", axis=0, tiled=True),
        lax.all_gather(w_router, "dp", axis=0, tiled=True),
        lax.all_gather(shared_gate_up, "dp", axis=1, tiled=True),
        lax.all_gather(shared_down, "dp", axis=1, tiled=True),
    )
    (
        full_attn_gain,
        query_weight,
        latent_weight,
        full_latent_gain,
        keyval_weight,
        output_weight,
        full_ffn_gain,
        router_weight,
        shared_in,
        shared_out,
    ) = gathered
    tensor_rank = lax.axis_index("tensor")
    dp_size = lax.axis_size("dp")
    rows_all = lax.all_gather(block_input, "tensor", axis=0, tiled=True)
    tokens = rows_all.shape[0]
    local_rows = block_input.shape[0]
    heads = query_weight.shape[1] // (NOPE + ROPE)
    experts = router_weight.shape[1]
    local_experts = expert_gate_up.shape[0]
    capacity = 2 * tokens * TOP // experts
    scale = (NOPE + ROPE) ** (-0.5)
    start = tensor_rank * local_rows
    cosine, sine = rotary_tables(segments[0], ROPE)
    allowed = allowed_pairs(segments[0], counts[0])
    attn_gain_wide = full_attn_gain.astype(jnp.float32)
    latent_gain_wide = full_latent_gain.astype(jnp.float32)
    ffn_gain_wide = full_ffn_gain.astype(jnp.float32)
    inputs = rows_all.astype(jnp.float32)
    first_scale = rms_scale(inputs)
    first_unit = inputs * first_scale
    first_normed = (first_unit * attn_gain_wide).astype(jnp.bfloat16)
    query = jnp.dot(first_normed, query_weight, preferred_element_type=jnp.float32).reshape(
        tokens, heads, NOPE + ROPE
    )
    query_rows = jnp.concatenate(
        [query[..., :NOPE], rotate(query[..., NOPE:], cosine[:, None, :], sine[:, None, :])],
        axis=-1,
    ).astype(jnp.bfloat16)
    latent_all = jnp.dot(first_normed, latent_weight, preferred_element_type=jnp.float32)
    latent = latent_all[:, :KVR]
    key_rope = rotate(latent_all[:, KVR:], cosine, sine).astype(jnp.bfloat16)
    latent_scale = rms_scale(latent)
    latent_unit = latent * latent_scale
    latent_normed = (latent_unit * latent_gain_wide).astype(jnp.bfloat16)
    keyval = (
        jnp.dot(latent_normed, keyval_weight, preferred_element_type=jnp.float32)
        .astype(jnp.bfloat16)
        .reshape(tokens, heads, NOPE + VD)
    )
    key_nope = keyval[..., :NOPE]
    values = keyval[..., NOPE:]
    scores = attention_scores(query_rows, key_nope, key_rope, allowed, scale)
    row_max = jnp.max(scores, axis=-1, keepdims=True)
    log_total = row_max + jnp.log(jnp.sum(jnp.exp(scores - row_max), axis=-1, keepdims=True))
    weights_low = jnp.exp(scores - log_total).astype(jnp.bfloat16)
    attended = (
        jnp.einsum("hij,jhd->ihd", weights_low, values, preferred_element_type=jnp.float32)
        .astype(jnp.bfloat16)
        .reshape(tokens, heads * VD)
    )
    attn_part = jnp.dot(attended, output_weight, preferred_element_type=jnp.float32)
    mixed = inputs + lax.psum(attn_part, "tensor")
    second_scale = rms_scale(mixed)
    second_unit = mixed * second_scale
    second_normed = (second_unit * ffn_gain_wide).astype(jnp.bfloat16)
    logits = jnp.dot(second_normed, router_weight, preferred_element_type=jnp.float32)
    probabilities = jax.nn.softmax(logits, axis=-1)
    gate_values = jnp.take_along_axis(probabilities, routes, axis=1)
    shared_pre = jnp.einsum(
        "td,gdf->tgf", second_normed, shared_in, preferred_element_type=jnp.float32
    )
    shared_hidden = (jax.nn.silu(shared_pre[:, 0]) * shared_pre[:, 1]).astype(jnp.bfloat16)
    shared_part = jnp.dot(shared_hidden, shared_out, preferred_element_type=jnp.float32)
    slot_index, target, owner = slot_layout(routes, experts, capacity)
    owner_grid = owner.reshape(experts, capacity)
    padded_rows = jnp.concatenate([second_normed, jnp.zeros((1, D), jnp.bfloat16)], axis=0)
    outgoing = padded_rows[owner_grid]
    arrived = lax.all_to_all(outgoing, "dp", split_axis=0, concat_axis=0, tiled=True)
    expert_rows = to_expert_major(arrived, dp_size, local_experts)
    expert_pre = jnp.einsum(
        "erd,egdf->ergf", expert_rows, expert_gate_up, preferred_element_type=jnp.float32
    )
    expert_hidden = (jax.nn.silu(expert_pre[:, :, 0]) * expert_pre[:, :, 1]).astype(jnp.bfloat16)
    expert_result = jnp.einsum(
        "erf,efd->erd", expert_hidden, expert_down, preferred_element_type=jnp.float32
    )
    returning = from_expert_major(expert_result, dp_size)
    returned = lax.all_to_all(
        returning.astype(jnp.bfloat16), "dp", split_axis=0, concat_axis=0, tiled=True
    ).astype(returning.dtype)
    padded_back = jnp.concatenate([returned.reshape(-1, D), jnp.zeros((1, D), jnp.float32)], axis=0)
    picked = padded_back[target].reshape(tokens, TOP, D)
    routed_part = jnp.sum(gate_values[:, :, None] * picked, axis=1)
    branch_sum = lax.psum_scatter(
        (shared_part + routed_part).astype(jnp.bfloat16), "tensor", scatter_dimension=0, tiled=True
    ).astype(jnp.float32)
    block_output = lax.dynamic_slice_in_dim(mixed, start, local_rows, 0) + branch_sum
    grad_rows = lax.all_gather(cotangent, "tensor", axis=0, tiled=True)
    grad_out = grad_rows.astype(jnp.float32)
    grad_shared_hidden = jnp.dot(grad_rows, shared_out.T, preferred_element_type=jnp.float32)
    grad_shared_out = jnp.dot(shared_hidden.T, grad_rows, preferred_element_type=jnp.float32)
    grad_shared_pre = swiglu_back(shared_pre[:, 0], shared_pre[:, 1], grad_shared_hidden, 1).astype(
        jnp.bfloat16
    )
    grad_shared_in = jnp.einsum(
        "td,tgf->gdf", second_normed, grad_shared_pre, preferred_element_type=jnp.float32
    )
    grad_second = jnp.einsum(
        "tgf,gdf->td", grad_shared_pre, shared_in, preferred_element_type=jnp.float32
    )
    gate_by_slot = (
        jnp.zeros((experts * capacity + 1,), jnp.float32).at[target].set(gate_values.reshape(-1))
    )
    slot_ids = jnp.arange(experts * capacity, dtype=jnp.int32).reshape(experts, capacity)
    padded_grad = jnp.concatenate([grad_out, jnp.zeros((1, D), jnp.float32)], axis=0)
    grad_outgoing = (gate_by_slot[slot_ids][..., None] * padded_grad[owner_grid]).astype(
        jnp.bfloat16
    )
    grad_arrived = lax.all_to_all(grad_outgoing, "dp", split_axis=0, concat_axis=0, tiled=True)
    grad_expert_rows = to_expert_major(grad_arrived, dp_size, local_experts)
    grad_expert_hidden = jnp.einsum(
        "erd,efd->erf", grad_expert_rows, expert_down, preferred_element_type=jnp.float32
    )
    grad_expert_down = jnp.einsum(
        "erf,erd->efd", expert_hidden, grad_expert_rows, preferred_element_type=jnp.float32
    )
    grad_expert_pre = swiglu_back(
        expert_pre[:, :, 0], expert_pre[:, :, 1], grad_expert_hidden, 2
    ).astype(jnp.bfloat16)
    grad_expert_gate_up = jnp.einsum(
        "erd,ergf->egdf", expert_rows, grad_expert_pre, preferred_element_type=jnp.float32
    )
    grad_expert_input = jnp.einsum(
        "ergf,egdf->erd", grad_expert_pre, expert_gate_up, preferred_element_type=jnp.float32
    )
    grad_returning = from_expert_major(grad_expert_input, dp_size)
    grad_returned = lax.all_to_all(
        grad_returning.astype(jnp.bfloat16), "dp", split_axis=0, concat_axis=0, tiled=True
    ).astype(grad_returning.dtype)
    padded_grad_back = jnp.concatenate(
        [grad_returned.reshape(-1, D), jnp.zeros((1, D), jnp.float32)], axis=0
    )
    grad_second = grad_second + jnp.sum(padded_grad_back[target].reshape(tokens, TOP, D), axis=1)
    grad_gates = jnp.sum(grad_out[:, None, :] * picked, axis=-1)
    grad_second, grad_gates = (
        lax.psum(grad_second.astype(jnp.bfloat16), "tensor").astype(jnp.float32),
        lax.psum(grad_gates.astype(jnp.bfloat16), "tensor").astype(jnp.float32),
    )
    chosen = (routes[:, :, None] == jnp.arange(experts, dtype=jnp.int32)[None, None, :]).astype(
        jnp.float32
    )
    grad_probabilities = jnp.sum(chosen * grad_gates[:, :, None], axis=1)
    grad_logits = probabilities * (
        grad_probabilities - jnp.sum(probabilities * grad_probabilities, axis=-1, keepdims=True)
    )
    grad_logits_low = grad_logits.astype(jnp.bfloat16)
    grad_router = jnp.dot(second_normed.T, grad_logits_low, preferred_element_type=jnp.float32)
    grad_second = grad_second + jnp.dot(
        grad_logits_low, router_weight.T, preferred_element_type=jnp.float32
    )
    gain_ffn_grad = jnp.sum(grad_second * second_unit, axis=0)
    grad_mixed = grad_out + rms_back(grad_second * ffn_gain_wide, second_unit, second_scale)
    grad_attn_low = grad_mixed.astype(jnp.bfloat16)
    grad_output_weight = jnp.dot(attended.T, grad_attn_low, preferred_element_type=jnp.float32)
    grad_attended = (
        jnp.dot(grad_attn_low, output_weight.T, preferred_element_type=jnp.float32)
        .astype(jnp.bfloat16)
        .reshape(tokens, heads, VD)
    )
    scores = attention_scores(query_rows, key_nope, key_rope, allowed, scale)
    weights = jnp.exp(scores - log_total)
    weights_low = weights.astype(jnp.bfloat16)
    grad_weights = jnp.einsum(
        "ihd,jhd->hij", grad_attended, values, preferred_element_type=jnp.float32
    )
    grad_values = jnp.einsum(
        "hij,ihd->jhd", weights_low, grad_attended, preferred_element_type=jnp.float32
    )
    grad_scores = (
        weights * (grad_weights - jnp.sum(weights * grad_weights, axis=-1, keepdims=True))
    ).astype(jnp.bfloat16)
    grad_query_nope = (
        jnp.einsum("hij,jhd->ihd", grad_scores, key_nope, preferred_element_type=jnp.float32)
        * scale
    )
    grad_query_rope = (
        jnp.einsum("hij,jd->ihd", grad_scores, key_rope, preferred_element_type=jnp.float32) * scale
    )
    grad_key_nope = (
        jnp.einsum(
            "hij,ihd->jhd", grad_scores, query_rows[..., :NOPE], preferred_element_type=jnp.float32
        )
        * scale
    )
    grad_key_rope = (
        jnp.einsum(
            "hij,ihd->jd", grad_scores, query_rows[..., NOPE:], preferred_element_type=jnp.float32
        )
        * scale
    )
    grad_query = (
        jnp.concatenate(
            [grad_query_nope, rotate_back(grad_query_rope, cosine[:, None, :], sine[:, None, :])],
            axis=-1,
        )
        .astype(jnp.bfloat16)
        .reshape(tokens, heads * (NOPE + ROPE))
    )
    grad_query_weight = jnp.dot(first_normed.T, grad_query, preferred_element_type=jnp.float32)
    grad_first = jnp.dot(grad_query, query_weight.T, preferred_element_type=jnp.float32)
    grad_keyval = (
        jnp.concatenate([grad_key_nope, grad_values], axis=-1)
        .astype(jnp.bfloat16)
        .reshape(tokens, heads * (NOPE + VD))
    )
    grad_keyval_weight = jnp.dot(latent_normed.T, grad_keyval, preferred_element_type=jnp.float32)
    grad_latent_normed = jnp.dot(grad_keyval, keyval_weight.T, preferred_element_type=jnp.float32)
    gain_latent_part = jnp.sum(grad_latent_normed * latent_unit, axis=0)
    grad_latent = rms_back(grad_latent_normed * latent_gain_wide, latent_unit, latent_scale)
    grad_latent_all = jnp.concatenate(
        [grad_latent, rotate_back(grad_key_rope, cosine, sine)], axis=-1
    )
    grad_first, grad_latent_all, gain_latent_grad = (
        lax.psum(grad_first.astype(jnp.bfloat16), "tensor").astype(jnp.float32),
        lax.psum(grad_latent_all.astype(jnp.bfloat16), "tensor").astype(jnp.float32),
        lax.psum(gain_latent_part.astype(jnp.bfloat16), "tensor").astype(jnp.float32),
    )
    grad_latent_low = grad_latent_all.astype(jnp.bfloat16)
    grad_latent_weight = jnp.dot(
        first_normed.T, grad_latent_low, preferred_element_type=jnp.float32
    )
    grad_first = grad_first + jnp.dot(
        grad_latent_low, latent_weight.T, preferred_element_type=jnp.float32
    )
    gain_attn_grad = jnp.sum(grad_first * first_unit, axis=0)
    grad_inputs = grad_mixed + rms_back(grad_first * attn_gain_wide, first_unit, first_scale)
    grad_local = lax.dynamic_slice_in_dim(grad_inputs, start, local_rows, 0)
    summed = (
        lax.psum_scatter(gain_attn_grad, "dp", scatter_dimension=0, tiled=True),
        lax.psum_scatter(grad_query_weight, "dp", scatter_dimension=0, tiled=True),
        lax.psum_scatter(grad_latent_weight, "dp", scatter_dimension=0, tiled=True),
        lax.psum_scatter(gain_latent_grad, "dp", scatter_dimension=0, tiled=True),
        lax.psum_scatter(grad_keyval_weight, "dp", scatter_dimension=0, tiled=True),
        lax.psum_scatter(grad_output_weight, "dp", scatter_dimension=1, tiled=True),
        lax.psum_scatter(gain_ffn_grad, "dp", scatter_dimension=0, tiled=True),
        lax.psum_scatter(grad_router, "dp", scatter_dimension=0, tiled=True),
        lax.psum_scatter(grad_shared_in, "dp", scatter_dimension=1, tiled=True),
        lax.psum_scatter(grad_shared_out, "dp", scatter_dimension=1, tiled=True),
    )
    return (
        block_output,
        grad_local,
        summed[0],
        summed[1],
        summed[2],
        summed[3],
        summed[4],
        summed[5],
        summed[6],
        summed[7],
        summed[8],
        summed[9],
        grad_expert_gate_up,
        grad_expert_down,
    )


RINGS = 4


def ring_step(values):
    return lax.ppermute(values, "dp", [(i, (i + RINGS) % 16) for i in range(16)])


def other_y(values):
    return lax.ppermute(values, "dp", [(i, i ^ 2) for i in range(16)])


def other_core(values):
    return lax.ppermute(values, "dp", [(i, i ^ 1) for i in range(16)])


def other_x(values):
    return lax.ppermute(values, "tensor", [(0, 1), (1, 0)])


def fence_kernel(*refs):
    pass


def after(values, *others):
    anywhere = pl.BlockSpec(memory_space=pl.ANY)
    return pl.pallas_call(
        fence_kernel,
        out_shape=jax.ShapeDtypeStruct(values.shape, values.dtype),
        in_specs=[anywhere] * (1 + len(others)),
        out_specs=anywhere,
        input_output_aliases={0: 0},
    )(values, *others)


def gather_rows(rows, corners):
    planes = []
    current = rows
    for distance in range(RINGS):
        if distance:
            current = ring_step(current)
        beside = other_y(current)
        across = other_x(current)
        corner = other_x(beside) if corners[distance] == "x" else other_y(across)
        planes.append((current, beside, across, corner))
    return planes


def add_low(first, second):
    return (first.astype(jnp.float32) + second.astype(jnp.float32)).astype(jnp.bfloat16)


def turn_corner(plane, direction):
    own, beside, across, corner = plane
    if direction == "x":
        return own, add_low(beside, other_x(corner)), across
    return own, beside, add_low(across, other_y(corner))


def close_plane(turned):
    own, beside, across = turned
    return own, other_y(beside), other_x(across)


def ring_rows(closed):
    moving = None
    for distance in (1, 2, 3, 0):
        own, from_y, from_x = closed[distance]
        total = own.astype(jnp.float32) + from_y.astype(jnp.float32) + from_x.astype(jnp.float32)
        if moving is not None:
            total = total + ring_step(moving).astype(jnp.float32)
        moving = total.astype(jnp.bfloat16)
    return total


def ring_sum(parts, low):
    moving = parts[1]
    for distance in (2, 3, 0):
        moving = ring_step(moving.astype(low)).astype(jnp.float32) + parts[distance]
    return moving


def ring_shards(shard):
    held = [shard]
    for _ in range(RINGS - 1):
        held.append(ring_step(held[-1]))
    return held


def gather_weight(held):
    chunks = []
    for distance, current in enumerate(held):
        beside = other_y(current)
        for flip_y, chunk in ((0, current), (1, beside)):
            for flip_core, piece in ((0, chunk), (1, other_core(chunk))):
                chunks.append(((distance, flip_y, flip_core), piece))
    return chunks


def place_of(coords, key):
    z, y, core = coords
    distance, flip_y, flip_core = key
    return (
        lax.rem(z + RINGS - distance, RINGS) * 4
        + (1 - y if flip_y else y) * 2
        + (1 - core if flip_core else core)
    )


def weight_keys():
    return [
        (distance, flip_y, flip_core)
        for flip_core in (0, 1)
        for flip_y in (0, 1)
        for distance in range(RINGS)
    ]


def scatter_blocks(grads, low):
    half = grads.shape[0] // 2
    total = grads[:half].astype(jnp.float32) + other_core(grads[half:].astype(low)).astype(
        jnp.float32
    )
    quarter = half // 2
    total = total[:quarter] + other_y(total[quarter:].astype(low)).astype(jnp.float32)
    size = quarter // RINGS
    return ring_sum([total[r * size : (r + 1) * size] for r in range(RINGS)], low)


def pick_blocks(values, order):
    chosen = order[:, None] == jnp.arange(values.shape[0], dtype=jnp.int32)[None, :]
    chosen = chosen.reshape(chosen.shape + (1,) * (values.ndim - 1))
    return jnp.sum(jnp.where(chosen, values[None], 0.0), axis=1)


def wide_dot(left, right):
    return jnp.dot(left, right, preferred_element_type=jnp.float32)


def dot_turned(left, right):
    return lax.dot_general(left, right, (((1,), (1,)), ((), ())), preferred_element_type=jnp.float32)


def dot_rows(left, right):
    return lax.dot_general(left, right, (((0,), (0,)), ((), ())), preferred_element_type=jnp.float32)


TILE = 256


def whole(array):
    return pl.BlockSpec(array.shape, lambda *i: (0,) * array.ndim)


def in_vmem(count):
    return [pl.BlockSpec(memory_space=pltpu.VMEM)] * count


def in_place(count):
    return [pl.BlockSpec(memory_space=pl.ANY)] * count


def head_scores(heads, h, nope_ref, turned_ref, keyval_ref, key_ref, masks):
    span = ROPE // 2 * heads
    column = pl.ds(pl.multiple_of(h * NOPE, NOPE), NOPE)
    key_column = pl.ds(pl.multiple_of(h * (NOPE + VD), NOPE), NOPE)
    scores = dot_turned(nope_ref[:, column], keyval_ref[:, key_column])
    for k in (0, 1):
        part = turned_ref[:, k * span : (k + 1) * span]
        part = jnp.where(masks, part, jnp.zeros_like(part))
        scores += dot_turned(part, key_ref[:, k * span : (k + 1) * span])
    return scores * (NOPE + ROPE) ** (-0.5)


def head_lanes(heads, h):
    span = ROPE // 2 * heads
    lane = lax.broadcasted_iota(jnp.int32, (1, span), 1)
    return (lane >= h * (ROPE // 2)) & (lane < (h + 1) * (ROPE // 2))


def allowed_rows(count, segment_row, segment_column):
    tokens = segment_row.shape[1]
    column = lax.broadcasted_iota(jnp.int32, (tokens, tokens), 0)
    row = lax.broadcasted_iota(jnp.int32, (tokens, tokens), 1)
    live = (column < count) & (row < count) & (row <= column)
    return (segment_row == segment_column) & live | (column == row)


def attend_kernel(
    keys,
    extra,
    heads,
    sizes,
    place_ref,
    segment_row_ref,
    segment_column_ref,
    cosine_ref,
    sine_ref,
    own_ref,
    other_ref,
    *refs,
):
    depth, query_width, used, latent_depth, keyval_part, first_width = sizes
    chunks = refs[: len(keys)]
    (
        own_out,
        sent_out,
        first_ref,
        keyval_weight_ref,
        output_ref,
        normed_ref,
        nope_ref,
        turned_ref,
        latent_ref,
        key_ref,
        keyval_ref,
        total_ref,
        attended_ref,
        gains_ref,
        latent_gain_ref,
        semaphores,
    ) = refs[len(keys) + extra :]
    f32, bf16 = jnp.float32, jnp.bfloat16
    local_rows = own_ref.shape[0]
    tokens = 2 * local_rows
    coords = (place_ref[0], place_ref[1], place_ref[2])
    x = place_ref[3]
    copies = []
    parts = depth // latent_depth
    for key, chunk in zip(keys, chunks):
        block = place_of(coords, key)
        rows = pl.ds(pl.multiple_of(block * depth, depth), depth)
        small_rows = pl.ds(pl.multiple_of(block * latent_depth, latent_depth), latent_depth)
        moves = [(chunk.at[:, pl.ds(0, first_width)], first_ref.at[rows])]
        for k in range(parts):
            moves.append(
                (
                    chunk.at[
                        pl.ds(k * latent_depth, latent_depth), pl.ds(first_width, keyval_part)
                    ],
                    keyval_weight_ref.at[small_rows, pl.ds(k * keyval_part, keyval_part)],
                )
            )
        moves.append(
            (
                chunk.at[:, pl.ds(first_width + keyval_part, heads * VD)],
                output_ref.at[rows],
            )
        )
        for source, target in moves:
            copies.append(pltpu.make_async_copy(source, target, semaphores.at[len(copies)]))
    for copy in copies:
        copy.start()
    for copy in copies:
        copy.wait()

    edge = query_width + KVR
    spread = jnp.transpose(first_ref[:, edge:].astype(f32))[used - edge : used - edge + 8]
    gains_ref[...] = spread
    gain = spread[0:1]
    source = lax.broadcasted_iota(jnp.int32, (D, KVR), 0)
    target = lax.broadcasted_iota(jnp.int32, (D, KVR), 1)
    wanted = target // latent_depth * depth + target % latent_depth
    chosen = jnp.where(source == wanted, 1.0, 0.0).astype(bf16)
    latent_gain = wide_dot(spread.astype(bf16), chosen)[2:3]
    latent_gain_ref[...] = latent_gain
    for ref, start in ((own_ref, x * local_rows), (other_ref, (1 - x) * local_rows)):
        rows = ref[...].astype(f32)
        unit = rows * lax.rsqrt(jnp.mean(rows * rows, axis=1, keepdims=True) + EPSILON)
        normed_ref[pl.ds(pl.multiple_of(start, local_rows), local_rows), :] = (unit * gain).astype(
            bf16
        )
    nope_width = heads * NOPE
    span = heads * (ROPE // 2)
    half = nope_width // 2
    for k in (0, 1):
        nope_ref[:, k * half : (k + 1) * half] = wide_dot(
            normed_ref[...], first_ref[:, k * half : (k + 1) * half]
        ).astype(bf16)
    turning = wide_dot(normed_ref[...], first_ref[:, nope_width : nope_width + 2 * span])
    cosine, sine = cosine_ref[...], sine_ref[...]
    first, second = turning[:, :span], turning[:, span:]
    turned_ref[:, :span] = (first * cosine - second * sine).astype(bf16)
    turned_ref[:, span:] = (second * cosine + first * sine).astype(bf16)
    latent = wide_dot(normed_ref[...], first_ref[:, query_width : query_width + KVR])
    latent_ref[...] = latent
    tail = wide_dot(normed_ref[...], first_ref[:, query_width + KVR :])
    lane = lax.broadcasted_iota(jnp.int32, (1, tail.shape[1]), 1)
    swapped = jnp.where(
        lane < ROPE // 2,
        -pltpu.roll(tail, tail.shape[1] - ROPE // 2, 1),
        pltpu.roll(tail, ROPE // 2, 1),
    )
    width = tail.shape[1]
    turned_key = tail * cosine[:, :width] + swapped * sine[:, :width]
    turned_key = jnp.where(lane < ROPE, turned_key, 0.0).astype(bf16)
    source = lax.broadcasted_iota(jnp.int32, (width, 2 * span), 0)
    target = lax.broadcasted_iota(jnp.int32, (width, 2 * span), 1)
    wanted = target % (ROPE // 2) + jnp.where(target < span, 0, ROPE // 2)
    key_ref[...] = wide_dot(turned_key, (source == wanted).astype(bf16)).astype(bf16)
    unit = latent * lax.rsqrt(jnp.mean(latent * latent, axis=1, keepdims=True) + EPSILON)
    latent_normed = (unit * latent_gain).astype(bf16)
    half = keyval_ref.shape[1] // 4
    for k in range(4):
        keyval_ref[:, k * half : (k + 1) * half] = wide_dot(
            latent_normed, keyval_weight_ref[:, k * half : (k + 1) * half]
        ).astype(bf16)
    allowed = allowed_rows(place_ref[4], segment_row_ref[...], segment_column_ref[...])
    total_lane = lax.broadcasted_iota(jnp.int32, total_ref.shape, 1)
    total_ref[...] = jnp.zeros_like(total_ref)

    def one_head(h, _):
        scores = head_scores(
            heads, h, nope_ref, turned_ref, keyval_ref, key_ref, head_lanes(heads, h)
        )
        scores = jnp.where(allowed, scores, -1e30)
        most = jnp.max(scores, axis=1, keepdims=True)
        total = most + jnp.log(jnp.sum(jnp.exp(scores - most), axis=1, keepdims=True))
        weights = jnp.exp(scores - total).astype(bf16)
        total_ref[...] += jnp.where(total_lane == h, total, 0.0)
        value_column = pl.ds(pl.multiple_of(h * (NOPE + VD) + NOPE, NOPE), VD)
        attended_ref[:, pl.ds(pl.multiple_of(h * VD, VD), VD)] = wide_dot(
            weights, keyval_ref[:, value_column]
        ).astype(bf16)
        return 0

    lax.fori_loop(0, heads, one_head, 0)
    own = pl.ds(pl.multiple_of(x * local_rows, local_rows), local_rows)
    other = pl.ds(pl.multiple_of((1 - x) * local_rows, local_rows), local_rows)
    pieces = 4
    size = output_ref.shape[0] // pieces
    for k in range(pieces):
        columns = slice(k * size, (k + 1) * size)
        own_out[:, columns] = dot_turned(attended_ref[own, :], output_ref[columns, :])
        sent_out[:, columns] = dot_turned(attended_ref[other, :], output_ref[columns, :]).astype(
            bf16
        )


def attend_forward(place, segments, cosine, sine, own, other, chunks, heads, sizes, others):
    depth, query_width, used, latent_depth, keyval_part, first_width = sizes
    f32, bf16 = jnp.float32, jnp.bfloat16
    keys = [key for key, _ in chunks]
    local_rows = own.shape[0]
    tokens = 2 * local_rows
    span = heads * (ROPE // 2)
    shapes = [
        ((local_rows, D), f32),
        ((local_rows, D), bf16),
        ((D, first_width), bf16),
        ((KVR, heads * (NOPE + VD)), bf16),
        ((D, heads * VD), bf16),
        ((tokens, D), bf16),
        ((tokens, heads * NOPE), bf16),
        ((tokens, 2 * span), bf16),
        ((tokens, KVR), f32),
        ((tokens, 2 * span), bf16),
        ((tokens, heads * (NOPE + VD)), bf16),
        ((tokens, 128), f32),
        ((tokens, heads * VD), bf16),
        ((8, D), f32),
        ((1, KVR), f32),
    ]
    return pl.pallas_call(
        functools.partial(attend_kernel, keys, len(others), heads, sizes),
        out_shape=[jax.ShapeDtypeStruct(*shape) for shape in shapes],
        in_specs=[pl.BlockSpec(memory_space=pltpu.SMEM)]
        + in_vmem(6)
        + in_place(len(chunks) + len(others)),
        out_specs=in_vmem(len(shapes)),
        scratch_shapes=[
            pltpu.SemaphoreType.DMA((len(chunks) * (2 + depth // latent_depth),))
        ],
        compiler_params=pltpu.CompilerParams(vmem_limit_bytes=48 * 1024 * 1024),
        cost_estimate=pl.CostEstimate(
            flops=2 * tokens * D * (first_width + heads * VD + 1024),
            bytes_accessed=4 * D * (first_width + 1536),
            transcendentals=2 * heads * tokens * tokens,
        ),
    )(
        place,
        segments,
        segments.T,
        cosine,
        sine,
        own,
        other,
        *[piece for _, piece in chunks],
        *others,
    )


def attend_back_kernel(
    heads,
    place_ref,
    segment_row_ref,
    segment_column_ref,
    cosine_ref,
    sine_ref,
    own_ref,
    other_ref,
    keyval_weight_ref,
    output_ref,
    nope_ref,
    turned_ref,
    latent_ref,
    key_ref,
    keyval_ref,
    total_ref,
    latent_gain_ref,
    projected_ref,
    keyval_grad_ref,
    latent_out,
    gain_ref,
    grad_ref,
    turn_ref,
    back_ref,
):
    f32, bf16 = jnp.float32, jnp.bfloat16
    local_rows = own_ref.shape[0]
    x = place_ref[3]
    span = heads * (ROPE // 2)
    nope_width = heads * NOPE
    query_width = nope_width + 2 * span
    scale = (NOPE + ROPE) ** (-0.5)
    for ref, start in ((own_ref, x * local_rows), (other_ref, (1 - x) * local_rows)):
        rows = pl.ds(pl.multiple_of(start, local_rows), local_rows)
        for k in (0, 1):
            half = slice(k * nope_width // 2, (k + 1) * nope_width // 2)
            grad_ref[rows, half] = wide_dot(ref[...], output_ref[:, half]).astype(bf16)
    allowed = allowed_rows(place_ref[4], segment_row_ref[...], segment_column_ref[...])
    total_lane = lax.broadcasted_iota(jnp.int32, total_ref.shape, 1)
    turn_ref[...] = jnp.zeros_like(turn_ref)
    back_ref[...] = jnp.zeros_like(back_ref)

    def one_head(h, _):
        mask = head_lanes(heads, h)
        scores = head_scores(heads, h, nope_ref, turned_ref, keyval_ref, key_ref, mask)
        total = jnp.sum(jnp.where(total_lane == h, total_ref[...], 0.0), axis=1, keepdims=True)
        weights = jnp.exp(jnp.where(allowed, scores, -1e30) - total)
        weights_low = weights.astype(bf16)
        column = pl.ds(pl.multiple_of(h * NOPE, NOPE), NOPE)
        key_column = pl.ds(pl.multiple_of(h * (NOPE + VD), NOPE), NOPE)
        value_column = pl.ds(pl.multiple_of(h * (NOPE + VD) + NOPE, NOPE), VD)
        grads = grad_ref[:, column]
        grad_weights = dot_turned(grads, keyval_ref[:, value_column])
        keyval_grad_ref[:, value_column] = dot_rows(weights_low, grads).astype(bf16)
        grad_scores = (
            weights * (grad_weights - jnp.sum(weights * grad_weights, axis=1, keepdims=True))
        ).astype(bf16)
        projected_ref[:, column] = (
            scale * wide_dot(grad_scores, keyval_ref[:, key_column])
        ).astype(bf16)
        keyval_grad_ref[:, key_column] = (
            scale * dot_rows(grad_scores, nope_ref[:, column])
        ).astype(bf16)
        for k in (0, 1):
            part = slice(k * span, (k + 1) * span)
            turn = wide_dot(grad_scores, key_ref[:, part])
            turn_ref[:, part] += jnp.where(mask, turn, 0.0)
            own = turned_ref[:, part]
            own = jnp.where(mask, own, jnp.zeros_like(own))
            back_ref[:, part] += dot_rows(grad_scores, own)
        return 0

    lax.fori_loop(0, heads, one_head, 0)
    cosine, sine = cosine_ref[...], sine_ref[...]
    first, second = scale * turn_ref[:, :span], scale * turn_ref[:, span:]
    projected_ref[:, nope_width : nope_width + span] = (first * cosine + second * sine).astype(bf16)
    projected_ref[:, nope_width + span : query_width] = (second * cosine - first * sine).astype(
        bf16
    )
    folded = []
    for k in (0, 1):
        part = scale * back_ref[:, k * span : (k + 1) * span]
        shift = span // 2
        while shift >= ROPE // 2:
            part = part + pltpu.roll(part, shift, 1)
            shift //= 2
        folded.append(part)
    width = projected_ref.shape[1] - query_width - KVR
    lane = lax.broadcasted_iota(jnp.int32, (1, width), 1)
    first = (folded[0] * cosine + folded[1] * sine)[:, :width]
    second = (folded[1] * cosine - folded[0] * sine)[:, :width]
    projected_ref[:, query_width + KVR :] = jnp.where(
        lane < ROPE // 2, first, jnp.where(lane < ROPE, second, 0.0)
    ).astype(bf16)
    gain = latent_gain_ref[...]
    latent = latent_ref[...]
    row_scale = lax.rsqrt(jnp.mean(latent * latent, axis=1, keepdims=True) + EPSILON)
    unit = latent * row_scale
    latent_out[...] = (unit * gain).astype(bf16)
    grad_normed = dot_turned(keyval_grad_ref[...], keyval_weight_ref[...])
    gain_ref[...] = jnp.sum(grad_normed * unit, axis=0, keepdims=True)
    grad_unit = grad_normed * gain
    projected_ref[:, query_width : query_width + KVR] = (
        row_scale * (grad_unit - unit * jnp.mean(grad_unit * unit, axis=1, keepdims=True))
    ).astype(bf16)


def attend_back(place, segments, cosine, sine, own, other, saved, heads, first_width):
    f32, bf16 = jnp.float32, jnp.bfloat16
    keyval = saved[6]
    tokens = 2 * own.shape[0]
    span = heads * (ROPE // 2)
    return pl.pallas_call(
        functools.partial(attend_back_kernel, heads),
        out_shape=[
            jax.ShapeDtypeStruct((tokens, first_width), bf16),
            jax.ShapeDtypeStruct((tokens, keyval.shape[1]), bf16),
            jax.ShapeDtypeStruct((tokens, KVR), bf16),
            jax.ShapeDtypeStruct((1, KVR), f32),
        ],
        in_specs=[pl.BlockSpec(memory_space=pltpu.SMEM)] + in_vmem(15),
        out_specs=in_vmem(4),
        scratch_shapes=[
            pltpu.VMEM((tokens, heads * NOPE), bf16),
            pltpu.VMEM((tokens, 2 * span), f32),
            pltpu.VMEM((tokens, 2 * span), f32),
        ],
        compiler_params=pltpu.CompilerParams(vmem_limit_bytes=48 * 1024 * 1024),
        cost_estimate=pl.CostEstimate(
            flops=2 * tokens * D * 3000,
            bytes_accessed=2 * D * 1536,
            transcendentals=heads * tokens * tokens,
        ),
    )(
        place,
        segments,
        segments.T,
        cosine,
        sine,
        own,
        other,
        *saved,
    )


def block_grads_kernel(places_ref, left_ref, right_ref, *refs):
    result = dot_rows(left_ref[...], right_ref[...])
    if len(refs) > 1:
        result += refs[0][...].astype(jnp.float32)
    refs[-1][...] = result.astype(jnp.bfloat16)


def block_grads(left, right, places, first, count, arrived=None, others=()):
    rows, width = right.shape
    size = left.shape[1] // places.shape[0]
    block = pl.BlockSpec((size, width), lambda i, where: (i, 0))
    extra = [] if arrived is None else [arrived]
    return pl.pallas_call(
        lambda places_ref, left_ref, right_ref, *refs: block_grads_kernel(
            places_ref, left_ref, right_ref, *refs[: len(extra)], refs[-1]
        ),
        grid_spec=pltpu.PrefetchScalarGridSpec(
            num_scalar_prefetch=1,
            grid=(count,),
            in_specs=[
                pl.BlockSpec((rows, size), lambda i, where: (0, where[first + i])),
                pl.BlockSpec((rows, width), lambda i, where: (0, 0)),
            ]
            + [pl.BlockSpec((size, width), lambda i, where: (first + i, 0))] * len(extra)
            + [pl.BlockSpec(memory_space=pl.ANY)] * len(others),
            out_specs=block,
        ),
        out_shape=jax.ShapeDtypeStruct((count * size, width), jnp.bfloat16),
        cost_estimate=pl.CostEstimate(
            flops=2 * rows * count * size * width,
            bytes_accessed=2 * (count * size * width + rows * width),
            transcendentals=0,
        ),
    )(places, left, right, *extra, *others)


def close_ring(near, arrived):
    size = near.shape[0] // RINGS
    total = near.astype(jnp.float32) + arrived.astype(jnp.float32)
    return ring_sum([total[r * size : (r + 1) * size] for r in range(RINGS)], jnp.bfloat16)


def scatter_product(left, right, places, others):
    sent = block_grads(left, right, places, 2 * RINGS, 2 * RINGS, None, others)
    arrived = other_core(sent)
    far = block_grads(left, right, places, RINGS, RINGS, arrived)
    from_y = other_y(far)
    near = block_grads(left, right, places, 0, RINGS, arrived)
    return close_ring(near, from_y)


def latent_blocks_kernel(places_ref, left_ref, right_ref, out_ref, whole_ref):
    blocks = places_ref.shape[0]
    size = left_ref.shape[1] // blocks
    pieces = 4
    part = right_ref.shape[1] // pieces
    for k in range(pieces):
        columns = slice(k * part, (k + 1) * part)
        whole_ref[:, columns] = dot_rows(left_ref[...], right_ref[:, columns])
    for k in range(blocks):
        start = pl.multiple_of(places_ref[k] * size, size)
        out_ref[k * size : (k + 1) * size, :] = whole_ref[pl.ds(start, size), :].astype(
            jnp.bfloat16
        )


def latent_blocks(left, right, places, others):
    shape = (left.shape[1], right.shape[1])
    return pl.pallas_call(
        lambda places_ref, left_ref, right_ref, *refs: latent_blocks_kernel(
            places_ref, left_ref, right_ref, *refs[len(others) :]
        ),
        out_shape=jax.ShapeDtypeStruct(shape, jnp.bfloat16),
        in_specs=[pl.BlockSpec(memory_space=pltpu.SMEM)] + in_vmem(2) + in_place(len(others)),
        out_specs=pl.BlockSpec(memory_space=pltpu.VMEM),
        scratch_shapes=[pltpu.VMEM(shape, jnp.float32)],
        compiler_params=pltpu.CompilerParams(vmem_limit_bytes=32 * 1024 * 1024),
    )(places, left, right, *others)


def pack_kernel(heads, query_ref, latent_ref, small_ref, keyval_ref, output_ref, out_ref):
    half = ROPE // 2
    head = NOPE + ROPE
    nope_width = heads * NOPE
    for h in range(heads):
        start = h * head
        out_ref[:, h * NOPE : (h + 1) * NOPE] = query_ref[:, start : start + NOPE]
        for k in (0, 1):
            to = nope_width + k * heads * half + h * half
            out_ref[:, to : to + half] = query_ref[
                :, start + NOPE + k * half : start + NOPE + (k + 1) * half
            ]
    at = heads * head
    edge = at + KVR
    out_ref[:, at:edge] = latent_ref[:, :KVR]
    out_ref[:, edge : edge + 128] = jnp.concatenate([latent_ref[:, KVR:], small_ref[...]], axis=1)
    at = edge + 128
    size = keyval_ref.shape[0]
    parts = out_ref.shape[0] // size
    part = keyval_ref.shape[1] // parts
    for k in range(parts):
        out_ref[k * size : (k + 1) * size, at : at + part] = keyval_ref[
            :, k * part : (k + 1) * part
        ]
    out_ref[:, at + part :] = jnp.transpose(output_ref[...].astype(jnp.float32)).astype(
        jnp.bfloat16
    )


def pack_weights(query, latent, small, keyval, output):
    depth, query_width = query.shape
    heads = query_width // (NOPE + ROPE)
    width = query_width + KVR + 128 + keyval.size // depth + output.shape[0]
    return pl.pallas_call(
        functools.partial(pack_kernel, heads),
        out_shape=jax.ShapeDtypeStruct((depth, width), jnp.bfloat16),
        in_specs=in_vmem(5),
        out_specs=pl.BlockSpec(memory_space=pltpu.VMEM),
    )(query, latent, small, keyval, output)


def load_pieces(pieces, target, semaphores):
    size = pieces[0].shape[0]
    copies = [
        pltpu.make_async_copy(piece, target.at[pl.ds(k * size, size)], semaphores.at[k])
        for k, piece in enumerate(pieces)
    ]
    for copy in copies:
        copy.start()
    for copy in copies:
        copy.wait()


def shared_stride(shared):
    return -(-shared // 32) * 32


def pack_shared_kernel(blocks, shared, in_ref, down_ref, out_ref):
    stride = shared_stride(shared)
    out_ref[...] = jnp.zeros_like(out_ref)
    for k in range(3):
        if k < 2:
            units = jnp.transpose(in_ref[k].astype(jnp.float32)).astype(jnp.bfloat16)
        else:
            units = down_ref[...]
        for b in range(blocks):
            out_ref[b, k * stride : k * stride + shared] = units[b * shared : (b + 1) * shared]


def pack_shared(shared_in, shared_down, blocks, others):
    depth = shared_in.shape[1]
    shared = shared_down.shape[0] // blocks
    return pl.pallas_call(
        lambda in_ref, down_ref, *refs: pack_shared_kernel(
            blocks, shared, in_ref, down_ref, refs[-1]
        ),
        out_shape=jax.ShapeDtypeStruct((blocks, 3 * shared_stride(shared), depth), jnp.bfloat16),
        in_specs=in_vmem(2) + in_place(len(others)),
        out_specs=pl.BlockSpec(memory_space=pltpu.VMEM),
    )(shared_in, shared_down, *others)


def unpack_shared_kernel(shared, packed_ref, in_ref, down_ref, units_ref):
    stride = shared_stride(shared)
    blocks = packed_ref.shape[0]
    for k in range(3):
        target = down_ref if k == 2 else units_ref
        for b in range(blocks):
            target[b * shared : (b + 1) * shared, :] = packed_ref[
                b, k * stride : k * stride + shared
            ].astype(jnp.float32)
        if k < 2:
            in_ref[k] = jnp.transpose(units_ref[...])


def unpack_shared(packed, shared):
    blocks, _, depth = packed.shape
    return pl.pallas_call(
        functools.partial(unpack_shared_kernel, shared),
        out_shape=[
            jax.ShapeDtypeStruct((2, depth, blocks * shared), jnp.float32),
            jax.ShapeDtypeStruct((blocks * shared, depth), jnp.float32),
        ],
        in_specs=in_vmem(1),
        out_specs=in_vmem(2),
        scratch_shapes=[pltpu.VMEM((blocks * shared, depth), jnp.float32)],
    )(packed)


def pack_units_kernel(units, shared, own_in, other_in, own_down, other_down, near, far, *refs):
    outs = refs[-3:]
    hole = -(-units // TILE) * TILE
    stride = shared_stride(shared)
    columns = outs[0].shape[1]
    size = near.shape[2]
    for k, out in enumerate(outs):
        first = own_in[0, k] if k < 2 else own_down[0]
        second = other_in[0, k] if k < 2 else other_down[0]
        out[:units] = first
        out[units:hole] = jnp.zeros((hole - units, columns), jnp.bfloat16)
        out[hole : hole + units] = second
        out[hole + units : 2 * hole] = jnp.zeros((hole - units, columns), jnp.bfloat16)
        out[2 * hole :] = jnp.zeros((TILE, columns), jnp.bfloat16)
        for b in range(columns // size):
            part = slice(b * size, (b + 1) * size)
            for at, ref in ((2 * hole, near), (2 * hole + stride, far)):
                out[at : at + shared, part] = ref[b, k * stride : k * stride + shared]


def pack_units(own_in, other_in, own_down, other_down, near, far, shared, others):
    units, depth = own_down.shape[1:]
    size = near.shape[2]
    height = 2 * (-(-units // TILE) * TILE) + TILE
    columns = 2 * size
    in_spec = pl.BlockSpec((1, 2, units, columns), lambda i: (0, 0, 0, i))
    down_spec = pl.BlockSpec((1, units, columns), lambda i: (0, 0, i))
    narrow = pl.BlockSpec((2,) + near.shape[1:], lambda i: (i, 0, 0))
    return pl.pallas_call(
        functools.partial(pack_units_kernel, units, shared),
        grid=(depth // columns,),
        in_specs=[in_spec, in_spec, down_spec, down_spec, narrow, narrow]
        + in_place(len(others)),
        out_specs=[pl.BlockSpec((height, columns), lambda i: (0, i))] * 3,
        out_shape=[jax.ShapeDtypeStruct((height, depth), jnp.bfloat16)] * 3,
        compiler_params=pltpu.CompilerParams(vmem_limit_bytes=32 * 1024 * 1024),
        cost_estimate=pl.CostEstimate(
            flops=0, bytes_accessed=12 * height * depth, transcendentals=0
        ),
    )(own_in, other_in, own_down, other_down, near, far, *others)


def expert_grads_kernel(units, count, extra, right_ref, *refs):
    out = refs[-1]
    for k in range(count):

        @pl.when(pl.program_id(0) == k)
        def _():
            result = dot_rows(refs[k][...], right_ref[...])[:units]
            if extra:
                result += refs[count][0, 0].astype(jnp.float32)
            out[0, 0] = result.astype(out.dtype)


def expert_grads(lefts, right, units, column, arrived, kind, others=()):
    total, depth = right.shape
    wide = -(-units // TILE) * TILE
    extra = [] if arrived is None else [arrived]
    out = pl.BlockSpec((1, 1, units, 2 * TILE), lambda k, i: (0, k, 0, i))
    side = pl.BlockSpec((total, wide), lambda k, i: (0, column))
    return pl.pallas_call(
        functools.partial(expert_grads_kernel, units, len(lefts), len(extra)),
        grid=(len(lefts), depth // (2 * TILE)),
        in_specs=[pl.BlockSpec((total, 2 * TILE), lambda k, i: (0, i))]
        + [side] * len(lefts)
        + [out] * len(extra)
        + in_place(len(others)),
        out_specs=out,
        out_shape=jax.ShapeDtypeStruct((1, len(lefts), units, depth), kind),
        compiler_params=pltpu.CompilerParams(vmem_limit_bytes=48 * 1024 * 1024),
        cost_estimate=pl.CostEstimate(
            flops=2 * len(lefts) * total * depth * wide,
            bytes_accessed=2 * len(lefts) * total * (depth + wide) + 8 * depth * units,
            transcendentals=0,
        ),
    )(right, *lefts, *extra, *others)


def side_grads_kernel(shared, rows_ref, cots_ref, gate_ref, up_ref, hidden_ref, logit_ref, *outs):
    kept_ref, sent_ref, router_ref = outs
    stride = shared_stride(shared)
    size = kept_ref.shape[2]
    for k, (left, right) in enumerate(
        ((gate_ref, rows_ref), (up_ref, rows_ref), (hidden_ref, cots_ref))
    ):
        result = dot_rows(left[...], right[...])
        for b in range(kept_ref.shape[0]):
            part = slice(b * size, (b + 1) * size)
            kept_ref[b, k * stride : (k + 1) * stride] = result[:stride, part]
            sent_ref[b, k * stride : (k + 1) * stride] = result[
                stride : 2 * stride, part
            ].astype(jnp.bfloat16)
    router_ref[...] = dot_rows(logit_ref[...], rows_ref[...])


def side_grads(rows, cots, gate, up, hidden, logits, shared, blocks):
    total, depth = rows.shape
    column = gate.shape[1] // TILE - 1
    size = depth // blocks
    stride = shared_stride(shared)
    wide = pl.BlockSpec((total, 2 * TILE), lambda i: (0, i))
    side = pl.BlockSpec((total, TILE), lambda i: (0, column))
    packed = pl.BlockSpec((2 * TILE // size, 3 * stride, size), lambda i: (i, 0, 0))
    return pl.pallas_call(
        functools.partial(side_grads_kernel, shared),
        grid=(depth // (2 * TILE),),
        in_specs=[wide, wide, side, side, side, whole(logits)],
        out_specs=[packed, packed, pl.BlockSpec((logits.shape[1], 2 * TILE), lambda i: (0, i))],
        out_shape=[
            jax.ShapeDtypeStruct((blocks, 3 * stride, size), jnp.float32),
            jax.ShapeDtypeStruct((blocks, 3 * stride, size), jnp.bfloat16),
            jax.ShapeDtypeStruct((logits.shape[1], depth), jnp.float32),
        ],
        compiler_params=pltpu.CompilerParams(vmem_limit_bytes=48 * 1024 * 1024),
        cost_estimate=pl.CostEstimate(
            flops=8 * total * depth * TILE,
            bytes_accessed=4 * total * depth,
            transcendentals=0,
        ),
    )(rows, cots, gate, up, hidden, logits)


def down_kernel(count, *refs):
    pieces, weight_ref = refs[:count], refs[count]
    grads_ref, rows_ref, semaphores = refs[-3:]

    @pl.when(pl.program_id(0) == 0)
    def _():
        load_pieces(pieces, rows_ref, semaphores)

    size = rows_ref.shape[0] // 2
    for k in range(2):
        part = slice(k * size, (k + 1) * size)
        grads_ref[part, :] = dot_turned(rows_ref[part, :], weight_ref[...]).astype(jnp.bfloat16)


def down_grads(part, pieces, down, kept, others):
    count = len(pieces)
    size, depth = pieces[0].shape
    width = down.shape[0]
    rows = count * size
    return pl.pallas_call(
        functools.partial(down_kernel, count),
        grid=(width // TILE,),
        in_specs=in_place(count)
        + [pl.BlockSpec((TILE, depth), lambda i: (i, 0))]
        + in_place(len(kept) + len(others)),
        out_specs=[
            pl.BlockSpec((rows, TILE), lambda i: (part, i)),
            pl.BlockSpec((rows, depth), lambda i: (part, 0)),
        ],
        out_shape=[
            jax.ShapeDtypeStruct((2 * rows, width), jnp.bfloat16),
            jax.ShapeDtypeStruct((2 * rows, depth), jnp.bfloat16),
        ],
        scratch_shapes=[pltpu.SemaphoreType.DMA((count,))],
        input_output_aliases={count + 1 + k: k for k in range(len(kept))},
        compiler_params=pltpu.CompilerParams(vmem_limit_bytes=48 * 1024 * 1024),
        cost_estimate=pl.CostEstimate(
            flops=2 * rows * depth * width,
            bytes_accessed=2 * (2 * rows * depth + depth * width + rows * width),
            transcendentals=0,
        ),
    )(*pieces, down, *kept, *others)


def out_kernel(count, *refs):
    hidden_ref, weight_ref = refs[:2]
    outs = refs[2:]
    size = outs[0].shape[0]
    for k in range(0, count, 4):
        part = hidden_ref[k * size : (k + 4) * size, :]
        result = wide_dot(part, weight_ref[...]).astype(jnp.bfloat16)
        for j in range(4):
            outs[k + j][...] = result[j * size : (j + 1) * size]


def out_rows(count, hidden, down):
    rows, width = hidden.shape
    depth = down.shape[1]
    size = rows // count
    return pl.pallas_call(
        functools.partial(out_kernel, count),
        grid=(depth // TILE,),
        in_specs=[whole(hidden), pl.BlockSpec((width, TILE), lambda i: (0, i))],
        out_specs=[pl.BlockSpec((size, TILE), lambda i: (0, i))] * count,
        out_shape=[jax.ShapeDtypeStruct((size, depth), jnp.bfloat16)] * count,
        compiler_params=pltpu.CompilerParams(vmem_limit_bytes=48 * 1024 * 1024),
        cost_estimate=pl.CostEstimate(
            flops=2 * rows * depth * width,
            bytes_accessed=2 * (rows * depth + depth * width + rows * width),
            transcendentals=0,
        ),
    )(hidden, down)


def mlp_kernel(tiles, pieces, others, experts_ref, routed_ref, *refs):
    row_refs = refs[:pieces]
    router_ref, gate_col, up_col, down_grad, gate_row, up_row = refs[pieces : pieces + 6]
    outs = refs[pieces + 6 + others :]
    grad_refs = outs[:pieces]
    rows_out, hidden_out, gate_out, up_out, logit_out = outs[pieces : pieces + 5]
    gate_all, up_all, prob_ref, scale_ref, sum_ref, semaphores = outs[pieces + 5 :]
    step = pl.program_id(0)
    third = tiles // 2
    total = rows_out.shape[0]
    size = total // pieces
    lane = lax.broadcasted_iota(jnp.int32, (1, router_ref.shape[1]), 1) - experts_ref[3]

    @pl.when(step == 0)
    def _():
        load_pieces(row_refs, rows_out, semaphores)
        logits = wide_dot(rows_out[...], router_ref[...])
        logits = jnp.where((lane >= 0) & (lane < experts_ref[2]), logits, -1e30)
        raised = jnp.exp(logits - jnp.max(logits, axis=1, keepdims=True))
        chances = raised / jnp.sum(raised, axis=1, keepdims=True)
        prob_ref[...] = chances
        for k in (0, 1):
            chance = jnp.sum(jnp.where(lane == experts_ref[k], chances, 0.0), axis=1, keepdims=True)
            scale_ref[k] = routed_ref[:, k : k + 1] * chance
        scale_ref[2] = jnp.ones_like(scale_ref[2])
        sum_ref[...] = jnp.zeros_like(sum_ref)

    @pl.when(step < tiles)
    def _():
        columns = pl.ds(pl.multiple_of(step * TILE, TILE), TILE)
        kind = step // third
        half = total // 2
        for k in (0, 1):
            part = slice(k * half, (k + 1) * half)
            pre_gate = dot_turned(rows_out[part, :], gate_col[...])
            pre_up = dot_turned(rows_out[part, :], up_col[...])
            grads = down_grad[part, :].astype(jnp.float32)
            scale = scale_ref[kind, part, :]
            sigmoid = 1.0 / (1.0 + jnp.exp(-pre_gate))
            silu = pre_gate * sigmoid
            hidden = (silu * pre_up).astype(jnp.bfloat16).astype(jnp.float32)
            sum_ref[kind, part, :] += jnp.sum(hidden * grads, axis=1, keepdims=True)
            grad_hidden = scale * grads
            low_gate = (grad_hidden * pre_up * (sigmoid + silu * (1.0 - sigmoid))).astype(
                jnp.bfloat16
            )
            low_up = (grad_hidden * silu).astype(jnp.bfloat16)
            gate_all[part, columns] = low_gate
            up_all[part, columns] = low_up
            hidden_out[part, :] = (scale * hidden).astype(jnp.bfloat16)
            gate_out[part, :] = low_gate
            up_out[part, :] = low_up

    @pl.when(step == tiles - 1)
    def _():
        grad_logits = jnp.zeros_like(prob_ref)
        for k in (0, 1):
            own = jnp.where(lane == experts_ref[k], 1.0, 0.0)
            grad_logits += scale_ref[k] * sum_ref[k] * (own - prob_ref[...])
        logit_out[...] = grad_logits.astype(jnp.bfloat16)

    @pl.when(step >= tiles)
    def _():
        some = pl.ds(pl.multiple_of((step - tiles) * 2 * TILE, TILE), 2 * TILE)
        grads = wide_dot(gate_all[...], gate_row[...]) + wide_dot(up_all[...], up_row[...])
        grads += dot_turned(logit_out[...], router_ref[some, :])
        grads = grads.astype(jnp.bfloat16)
        for k in range(pieces):
            grad_refs[k][...] = grads[k * size : (k + 1) * size]


def mlp_plane(distance, experts, routed, rows, down_grad, router, gate, up, kept, others):
    pieces = len(rows)
    size, depth = rows[0].shape
    width = gate.shape[0]
    tiles, columns = width // TILE, depth // (2 * TILE)
    total = pieces * size
    low = jnp.bfloat16

    def early(i):
        return jnp.minimum(i, tiles - 1)

    def late(i):
        return jnp.maximum(i - tiles, 0)

    tile_spec = pl.BlockSpec((total, TILE), lambda i: (distance, early(i)))
    anywhere = pl.BlockSpec(memory_space=pl.ANY)
    first_kept = 2 + pieces + 6
    results = pl.pallas_call(
        functools.partial(mlp_kernel, tiles, pieces, len(kept) + len(others)),
        grid=(tiles + columns,),
        in_specs=[pl.BlockSpec(memory_space=pltpu.SMEM), whole(routed)]
        + [anywhere] * pieces
        + [
            pl.BlockSpec((depth, 128), lambda i: (0, router.shape[1] // 128 - 1)),
            pl.BlockSpec((TILE, depth), lambda i: (early(i), 0)),
            pl.BlockSpec((TILE, depth), lambda i: (early(i), 0)),
            tile_spec,
            pl.BlockSpec((width, 2 * TILE), lambda i: (0, late(i))),
            pl.BlockSpec((width, 2 * TILE), lambda i: (0, late(i))),
        ]
        + [anywhere] * (len(kept) + len(others)),
        out_specs=[pl.BlockSpec((size, 2 * TILE), lambda i: (0, late(i)))] * pieces
        + [
            pl.BlockSpec((total, depth), lambda i: (distance, 0)),
            tile_spec,
            tile_spec,
            tile_spec,
            pl.BlockSpec((total, 128), lambda i: (distance, 0)),
        ],
        out_shape=[jax.ShapeDtypeStruct((size, depth), low)] * pieces
        + [
            jax.ShapeDtypeStruct((RINGS * total, many), low)
            for many in (depth, width, width, width, 128)
        ],
        scratch_shapes=[pltpu.VMEM((total, width), low)] * 2
        + [
            pltpu.VMEM((total, 128), jnp.float32),
            pltpu.VMEM((3, total, 1), jnp.float32),
            pltpu.VMEM((3, total, 1), jnp.float32),
            pltpu.SemaphoreType.DMA((pieces,)),
        ],
        input_output_aliases={first_kept + k: pieces + k for k in range(len(kept))},
        compiler_params=pltpu.CompilerParams(vmem_limit_bytes=48 * 1024 * 1024),
        cost_estimate=pl.CostEstimate(
            flops=2 * total * depth * width * 4,
            bytes_accessed=2 * (4 * depth * width + 3 * total * depth + 4 * total * width),
            transcendentals=total * width,
        ),
    )(experts, routed, *rows, router, gate, up, down_grad, gate, up, *kept, *others)
    return results[:pieces], results[pieces:]


def gather_body(
    block_input,
    segments,
    counts,
    routes,
    attn_gain,
    w_query,
    w_latent,
    latent_gain,
    w_keyval,
    w_output,
    ffn_gain,
    w_router,
    shared_gate_up,
    shared_down,
    expert_gate_up,
    expert_down,
    cotangent,
):
    f32 = jnp.float32
    bf16 = jnp.bfloat16
    blocks = 16
    index = lax.axis_index("dp")
    x = lax.axis_index("tensor")
    coords = jnp.stack([index // 4, (index // 2) % 2, index % 2]).astype(jnp.int32)
    core = coords[2]
    place = jnp.concatenate([coords, x.astype(jnp.int32)[None], counts])
    local_rows = block_input.shape[0]
    tokens = 2 * local_rows
    depth = w_query.shape[0]
    query_width = w_query.shape[1]
    heads = query_width // (NOPE + ROPE)
    experts = w_router.shape[1]
    units = expert_gate_up.shape[3]
    shared = shared_gate_up.shape[2] // blocks
    latent_depth = w_keyval.shape[0]

    used = query_width + KVR + ROPE
    small = jnp.concatenate(
        [
            attn_gain[:, None],
            ffn_gain[:, None],
            jnp.pad(latent_gain, (0, depth - latent_depth))[:, None],
            w_router,
            routes.reshape(depth, -1).astype(bf16),
            jnp.zeros((depth, 128 - ROPE - 3 - experts - 2 * TOP), bf16),
        ],
        axis=1,
    )
    first_width = query_width + KVR + 128
    shards = pack_weights(w_query, w_latent, small, w_keyval, w_output)
    held = ring_shards(shards)
    other_input = other_x(block_input)
    expert_in = expert_gate_up.swapaxes(2, 3)
    expert_in_other = other_core(expert_in)
    expert_down_other = other_core(expert_down)
    chunks = gather_weight(held)
    grad_planes = gather_rows(after(cotangent, held[3]), "xyxy")

    shared_near = lax.all_to_all(
        pack_shared(shared_gate_up, shared_down, blocks, (held[3],)),
        "dp",
        split_axis=0,
        concat_axis=0,
        tiled=True,
    )
    shared_far = other_core(shared_near)

    cosine, sine = rotary_tables(segments[0], ROPE)
    cosine = jnp.tile(cosine, (1, heads))
    sine = jnp.tile(sine, (1, heads))
    sizes = (depth, query_width, used, latent_depth, w_keyval.shape[1] * latent_depth // depth, first_width)
    (
        own_part,
        sent_part,
        first_weight,
        keyval_weight,
        output_turned,
        first_normed,
        nope,
        turned_query,
        latent,
        key,
        keyval,
        total,
        attended,
        gains,
        latent_gain_row,
    ) = attend_forward(
        place,
        segments,
        cosine,
        sine,
        block_input,
        other_input,
        chunks,
        heads,
        sizes,
        (grad_planes[1][0], grad_planes[0][2]),
    )
    attn_gain_wide, ffn_gain_wide = gains[0], gains[1]
    mixed = block_input.astype(f32) + own_part + other_x(sent_part).astype(f32)
    second_scale = rms_scale(mixed)
    second_unit = mixed * second_scale
    second_normed = (second_unit * ffn_gain_wide).astype(bf16)

    routes_at = used + 3 + experts
    routes_all = first_weight[:, routes_at : routes_at + 2 * TOP].reshape(blocks * tokens, TOP)
    chip_experts = jnp.stack([index, index + 1 - 2 * core]).astype(jnp.int32)
    routed_all = jnp.any(
        routes_all[None] == chip_experts[:, None, None].astype(bf16), axis=2
    ).astype(f32)
    order = jnp.stack(
        [
            place_of(coords, (distance, flip_y, 0)) * 2 + (1 - x if flip_x else x)
            for distance in range(RINGS)
            for flip_x, flip_y in ((0, 0), (0, 1), (1, 0), (1, 1))
        ]
    )
    routed = jnp.stack(
        [
            pick_blocks(one.reshape(blocks * 2, local_rows), order).reshape(RINGS, -1)
            for one in routed_all
        ],
        axis=2,
    )

    corners = "yxyx"
    row_planes = gather_rows(second_normed, corners)
    gate_weight, up_weight, down_weight = pack_units(
        expert_in,
        expert_in_other,
        expert_down,
        expert_down_other,
        shared_near,
        shared_far,
        shared,
        (second_normed,),
    )
    half_kept = down_grads(
        0, [piece for plane in grad_planes[:2] for piece in plane], down_weight, (), ()
    )
    down_grad, every_grad = down_grads(
        1,
        [piece for plane in grad_planes[2:] for piece in plane],
        down_weight,
        half_kept,
        (row_planes[1][0],),
    )
    expert_ids = jnp.concatenate(
        [chip_experts, jnp.array([experts, used + 3 - query_width - KVR], jnp.int32)]
    )
    kept = []
    turned, closed = [], []
    for distance in range(RINGS):
        others = list(turned[distance - 2][1:]) if distance > 1 else []
        if distance > 2:
            others += list(closed[distance - 3][1:])
        grads, kept = mlp_plane(
            distance,
            expert_ids,
            routed[distance],
            row_planes[distance],
            down_grad,
            first_weight,
            gate_weight,
            up_weight,
            kept,
            others,
        )
        turned.append(turn_corner(grads, corners[distance]))
        if distance < RINGS - 1:
            closed.append(close_plane(turned[distance]))
    every_row, every_hidden, every_gate_grad, every_up_grad, logit_grads = kept
    out_pieces = out_rows(4 * RINGS, every_hidden, down_weight)
    own, beside, across = turned[3]
    closed.append(close_plane((own, after(beside, out_pieces[0]), after(across, out_pieces[0]))))
    grad_second = ring_rows(closed)
    out_closed = []
    for distance in range(RINGS):
        plane = list(out_pieces[4 * distance : 4 * distance + 4])
        plane[3] = after(plane[3], grad_second)
        plane[2] = after(plane[2], grad_second)
        out_closed.append(close_plane(turn_corner(plane, "x")))
    block_output = mixed + ring_rows(out_closed)

    arrived_in = other_core(
        expert_grads((every_gate_grad, every_up_grad), every_row, units, 1, None, bf16)
    )
    arrived_down = other_core(expert_grads((every_hidden,), every_grad, units, 1, None, bf16))
    shared_kept, shared_sent, logit_rows = side_grads(
        every_row,
        every_grad,
        every_gate_grad,
        every_up_grad,
        every_hidden,
        logit_grads,
        shared,
        blocks,
    )
    router_at = used + 3 - query_width - KVR
    grad_router = logit_rows[router_at : router_at + experts].reshape(experts, blocks, depth)
    grad_shared_in, grad_shared_down = unpack_shared(
        lax.all_to_all(
            add_low(shared_kept, other_core(shared_sent)),
            "dp",
            split_axis=0,
            concat_axis=0,
            tiled=True,
        ),
        shared,
    )

    gain_ffn_part = jnp.sum(grad_second * second_unit, axis=0)
    grad_mixed = cotangent.astype(f32) + rms_back(
        grad_second * ffn_gain_wide, second_unit, second_scale
    )
    grad_mixed_low = grad_mixed.astype(bf16)
    other_grad = other_x(grad_mixed_low)

    places = jnp.stack([place_of(coords, key_of) for key_of in weight_keys()]).astype(jnp.int32)
    projected_grad, keyval_grad, latent_normed, gain_latent_part = attend_back(
        place,
        segments,
        cosine,
        sine,
        grad_mixed_low,
        other_grad,
        (keyval_weight, output_turned, nope, turned_query, latent, key, keyval, total, latent_gain_row),
        heads,
        first_width,
    )
    grad_attn = jnp.concatenate(
        [
            jnp.where(x == 0, grad_mixed_low, other_grad),
            jnp.where(x == 0, other_grad, grad_mixed_low),
        ],
        axis=0,
    )
    middle = heads * NOPE
    edges = ((0, middle), (middle, first_width))
    parts = [projected_grad[:, start:end] for start, end in edges]
    arrived = [
        other_core(block_grads(first_normed, part, places, 2 * RINGS, 2 * RINGS))
        for part in parts
    ]
    far = [
        block_grads(first_normed, part, places, RINGS, RINGS, came)
        for part, came in zip(parts, arrived)
    ]
    from_y = [other_y(far[0]), other_y(far[1])]
    grad_expert_in = expert_grads(
        (every_gate_grad, every_up_grad), every_row, units, 0, arrived_in, f32, tuple(far)
    )
    near = [
        block_grads(first_normed, part, places, 0, RINGS, came)
        for part, came in zip(parts, arrived)
    ]
    first_closed = close_ring(after(near[0], grad_expert_in), from_y[0])
    grad_expert_down = expert_grads(
        (every_hidden,), every_grad, units, 0, arrived_down, f32, (from_y[0],)
    )
    second_closed = close_ring(near[1], from_y[1])
    grad_expert_gate_up = grad_expert_in.swapaxes(2, 3)
    grad_expert_down = grad_expert_down[0]
    grad_output_weight = scatter_product(grad_attn, attended, places, (arrived[1],)).T
    grad_keyval_weight = scatter_blocks(
        latent_blocks(latent_normed, keyval_grad, places, (arrived[1],)), bf16
    )
    grad_first_weight = jnp.concatenate([first_closed, second_closed], axis=1)
    nope_width = heads * NOPE
    span = heads * (ROPE // 2)
    grad_query_weight = jnp.concatenate(
        [
            grad_first_weight[:, :nope_width].reshape(depth, heads, NOPE),
            grad_first_weight[:, nope_width : nope_width + span].reshape(depth, heads, -1),
            grad_first_weight[:, nope_width + span : query_width].reshape(depth, heads, -1),
        ],
        axis=2,
    ).reshape(depth, query_width)
    grad_latent_part = grad_first_weight[:, query_width:used]
    grad_latent_weight = grad_latent_part + other_x(grad_latent_part)
    grad_first_part = dot_turned(projected_grad, first_weight)
    low_rows, high_rows = grad_first_part[:local_rows], grad_first_part[local_rows:]
    sent_rows = jnp.where(x == 0, high_rows, low_rows).astype(bf16)
    grad_first = jnp.where(x == 0, low_rows, high_rows) + other_x(sent_rows).astype(f32)
    own_inputs = block_input.astype(f32)
    own_scale = rms_scale(own_inputs)
    own_unit = own_inputs * own_scale
    gain_attn_part = jnp.sum(grad_first * own_unit, axis=0)
    grad_input = grad_mixed + rms_back(grad_first * attn_gain_wide, own_unit, own_scale)

    small_grads = jnp.concatenate(
        [
            gain_attn_part.reshape(blocks, 1, depth),
            gain_ffn_part.reshape(blocks, 1, depth),
            grad_router.swapaxes(0, 1),
            jnp.pad(
                gain_latent_part.reshape(blocks, 1, latent_depth),
                ((0, 0), (0, 0), (0, depth - latent_depth)),
            ),
        ],
        axis=1,
    )
    small_grads = scatter_blocks(
        pick_blocks(after(small_grads, far[1]), places), f32
    )[0]
    small_grads = small_grads + other_x(small_grads)
    return (
        block_output,
        grad_input,
        small_grads[0],
        grad_query_weight,
        grad_latent_weight,
        small_grads[2 + experts, :latent_depth],
        grad_keyval_weight,
        grad_output_weight,
        small_grads[1],
        small_grads[2 : 2 + experts].T,
        grad_shared_in,
        grad_shared_down,
        grad_expert_gate_up,
        grad_expert_down,
    )


def solution(mesh):
    in_specs = (
        P(("dp", "tensor"), None),
        P("dp", None),
        P("dp"),
        P("dp", None),
        P("dp"),
        P("dp", "tensor"),
        P("dp", None),
        P("dp"),
        P("dp", "tensor"),
        P("tensor", "dp"),
        P("dp"),
        P("dp", None),
        P(None, "dp", "tensor"),
        P("tensor", "dp"),
        P("dp", None, None, "tensor"),
        P("dp", "tensor", None),
        P(("dp", "tensor"), None),
    )
    out_specs = (
        P(("dp", "tensor"), None),
        P(("dp", "tensor"), None),
        P("dp"),
        P("dp", "tensor"),
        P("dp", None),
        P("dp"),
        P("dp", "tensor"),
        P("tensor", "dp"),
        P("dp"),
        P("dp", None),
        P(None, "dp", "tensor"),
        P("tensor", "dp"),
        P("dp", None, None, "tensor"),
        P("dp", "tensor", None),
    )
    body = gather_body if mesh.shape["dp"] == 16 else exchange_body
    return jax.shard_map(body, mesh=mesh, in_specs=in_specs, out_specs=out_specs, check_vma=False)
```

```python
import functools
import math

import jax
import jax.numpy as jnp
from jax import lax
from jax.experimental import pallas as pl
from jax.experimental.pallas import tpu as pltpu
from jax.sharding import PartitionSpec as P

D = 2048
NOPE = 128
ROPE = 64
VD = 128
KVR = 512
TOP = 6


EPSILON = 1e-06


def rms_scale(values):
    return lax.rsqrt(jnp.mean(values * values, axis=-1, keepdims=True) + EPSILON)


def rms_back(grad_unit, unit_rows, row_scale):
    return row_scale * (
        grad_unit - unit_rows * jnp.mean(grad_unit * unit_rows, axis=-1, keepdims=True)
    )


def rotary_tables(segment_row, width):
    count = segment_row.shape[0]
    position = jnp.arange(count, dtype=jnp.int32)
    same = segment_row[:, None] == segment_row[None, :]
    start = jnp.min(jnp.where(same, position[None, :], count), axis=1)
    offset = (position - start).astype(jnp.float32)
    freq = jnp.exp(jnp.arange(width // 2, dtype=jnp.float32) * (-2.0 * math.log(10000.0) / width))
    angle = offset[:, None] * freq[None, :]
    return (jnp.cos(angle), jnp.sin(angle))


def rotate(values, cosine, sine):
    half = values.shape[-1] // 2
    first = values[..., :half]
    second = values[..., half:]
    return jnp.concatenate(
        [first * cosine - second * sine, second * cosine + first * sine], axis=-1
    )


def rotate_back(grads, cosine, sine):
    half = grads.shape[-1] // 2
    first = grads[..., :half]
    second = grads[..., half:]
    return jnp.concatenate(
        [first * cosine + second * sine, second * cosine - first * sine], axis=-1
    )


def allowed_pairs(segment_row, count):
    position = jnp.arange(segment_row.shape[0], dtype=jnp.int32)
    live = position < count
    same = segment_row[:, None] == segment_row[None, :]
    causal = position[None, :] <= position[:, None]
    return same & causal & live[:, None] & live[None, :] | (position[:, None] == position[None, :])


def attention_scores(query_rows, key_nope, key_rope, allowed, scale):
    scores = jnp.einsum(
        "ihd,jhd->hij", query_rows[..., :NOPE], key_nope, preferred_element_type=jnp.float32
    )
    scores = scores + jnp.einsum(
        "ihd,jd->hij", query_rows[..., NOPE:], key_rope, preferred_element_type=jnp.float32
    )
    return jnp.where(allowed[None], scores * scale, -1e30)


def swiglu_back(gate, upper, grad_hidden, axis):
    sigmoid = jax.nn.sigmoid(gate)
    grad_gate = grad_hidden * upper * sigmoid * (1.0 + gate * (1.0 - sigmoid))
    grad_upper = grad_hidden * gate * sigmoid
    return jnp.stack([grad_gate, grad_upper], axis=axis)


def slot_layout(routes, experts, capacity):
    tokens = routes.shape[0]
    flat = routes.reshape(-1)
    onehot = (flat[:, None] == jnp.arange(experts, dtype=jnp.int32)[None, :]).astype(jnp.int32)
    rank = jnp.arange(flat.shape[0], dtype=jnp.int32)
    earlier = (rank[None, :] < rank[:, None]).astype(jnp.bfloat16)
    before = jnp.dot(
        earlier, onehot.astype(jnp.bfloat16), preferred_element_type=jnp.float32
    ).astype(jnp.int32)
    slot_index = jnp.sum(before * onehot, axis=1)
    target = flat * capacity + slot_index
    token_ids = jnp.arange(flat.shape[0], dtype=jnp.int32) // routes.shape[1]
    owner = jnp.full((experts * capacity,), tokens, jnp.int32).at[target].set(token_ids)
    return (slot_index, target, owner)


def to_expert_major(arrived, groups, local_experts):
    capacity = arrived.shape[1]
    width = arrived.shape[2]
    return (
        arrived.reshape(groups, local_experts, capacity, width)
        .transpose(1, 0, 2, 3)
        .reshape(local_experts, groups * capacity, width)
    )


def from_expert_major(results, groups):
    local_experts = results.shape[0]
    width = results.shape[2]
    capacity = results.shape[1] // groups
    return (
        results.reshape(local_experts, groups, capacity, width)
        .transpose(1, 0, 2, 3)
        .reshape(groups * local_experts, capacity, width)
    )


def exchange_body(
    block_input,
    segments,
    counts,
    routes,
    attn_gain,
    w_query,
    w_latent,
    latent_gain,
    w_keyval,
    w_output,
    ffn_gain,
    w_router,
    shared_gate_up,
    shared_down,
    expert_gate_up,
    expert_down,
    cotangent,
):
    gathered = (
        lax.all_gather(attn_gain, "dp", axis=0, tiled=True),
        lax.all_gather(w_query, "dp", axis=0, tiled=True),
        lax.all_gather(w_latent, "dp", axis=0, tiled=True),
        lax.all_gather(latent_gain, "dp", axis=0, tiled=True),
        lax.all_gather(w_keyval, "dp", axis=0, tiled=True),
        lax.all_gather(w_output, "dp", axis=1, tiled=True),
        lax.all_gather(ffn_gain, "dp", axis=0, tiled=True),
        lax.all_gather(w_router, "dp", axis=0, tiled=True),
        lax.all_gather(shared_gate_up, "dp", axis=1, tiled=True),
        lax.all_gather(shared_down, "dp", axis=1, tiled=True),
    )
    (
        full_attn_gain,
        query_weight,
        latent_weight,
        full_latent_gain,
        keyval_weight,
        output_weight,
        full_ffn_gain,
        router_weight,
        shared_in,
        shared_out,
    ) = gathered
    tensor_rank = lax.axis_index("tensor")
    dp_size = lax.axis_size("dp")
    rows_all = lax.all_gather(block_input, "tensor", axis=0, tiled=True)
    tokens = rows_all.shape[0]
    local_rows = block_input.shape[0]
    heads = query_weight.shape[1] // (NOPE + ROPE)
    experts = router_weight.shape[1]
    local_experts = expert_gate_up.shape[0]
    capacity = 2 * tokens * TOP // experts
    scale = (NOPE + ROPE) ** (-0.5)
    start = tensor_rank * local_rows
    cosine, sine = rotary_tables(segments[0], ROPE)
    allowed = allowed_pairs(segments[0], counts[0])
    attn_gain_wide = full_attn_gain.astype(jnp.float32)
    latent_gain_wide = full_latent_gain.astype(jnp.float32)
    ffn_gain_wide = full_ffn_gain.astype(jnp.float32)
    inputs = rows_all.astype(jnp.float32)
    first_scale = rms_scale(inputs)
    first_unit = inputs * first_scale
    first_normed = (first_unit * attn_gain_wide).astype(jnp.bfloat16)
    query = jnp.dot(first_normed, query_weight, preferred_element_type=jnp.float32).reshape(
        tokens, heads, NOPE + ROPE
    )
    query_rows = jnp.concatenate(
        [query[..., :NOPE], rotate(query[..., NOPE:], cosine[:, None, :], sine[:, None, :])],
        axis=-1,
    ).astype(jnp.bfloat16)
    latent_all = jnp.dot(first_normed, latent_weight, preferred_element_type=jnp.float32)
    latent = latent_all[:, :KVR]
    key_rope = rotate(latent_all[:, KVR:], cosine, sine).astype(jnp.bfloat16)
    latent_scale = rms_scale(latent)
    latent_unit = latent * latent_scale
    latent_normed = (latent_unit * latent_gain_wide).astype(jnp.bfloat16)
    keyval = (
        jnp.dot(latent_normed, keyval_weight, preferred_element_type=jnp.float32)
        .astype(jnp.bfloat16)
        .reshape(tokens, heads, NOPE + VD)
    )
    key_nope = keyval[..., :NOPE]
    values = keyval[..., NOPE:]
    scores = attention_scores(query_rows, key_nope, key_rope, allowed, scale)
    row_max = jnp.max(scores, axis=-1, keepdims=True)
    log_total = row_max + jnp.log(jnp.sum(jnp.exp(scores - row_max), axis=-1, keepdims=True))
    weights_low = jnp.exp(scores - log_total).astype(jnp.bfloat16)
    attended = (
        jnp.einsum("hij,jhd->ihd", weights_low, values, preferred_element_type=jnp.float32)
        .astype(jnp.bfloat16)
        .reshape(tokens, heads * VD)
    )
    attn_part = jnp.dot(attended, output_weight, preferred_element_type=jnp.float32)
    mixed = inputs + lax.psum(attn_part, "tensor")
    second_scale = rms_scale(mixed)
    second_unit = mixed * second_scale
    second_normed = (second_unit * ffn_gain_wide).astype(jnp.bfloat16)
    logits = jnp.dot(second_normed, router_weight, preferred_element_type=jnp.float32)
    probabilities = jax.nn.softmax(logits, axis=-1)
    gate_values = jnp.take_along_axis(probabilities, routes, axis=1)
    shared_pre = jnp.einsum(
        "td,gdf->tgf", second_normed, shared_in, preferred_element_type=jnp.float32
    )
    shared_hidden = (jax.nn.silu(shared_pre[:, 0]) * shared_pre[:, 1]).astype(jnp.bfloat16)
    shared_part = jnp.dot(shared_hidden, shared_out, preferred_element_type=jnp.float32)
    slot_index, target, owner = slot_layout(routes, experts, capacity)
    owner_grid = owner.reshape(experts, capacity)
    padded_rows = jnp.concatenate([second_normed, jnp.zeros((1, D), jnp.bfloat16)], axis=0)
    outgoing = padded_rows[owner_grid]
    arrived = lax.all_to_all(outgoing, "dp", split_axis=0, concat_axis=0, tiled=True)
    expert_rows = to_expert_major(arrived, dp_size, local_experts)
    expert_pre = jnp.einsum(
        "erd,egdf->ergf", expert_rows, expert_gate_up, preferred_element_type=jnp.float32
    )
    expert_hidden = (jax.nn.silu(expert_pre[:, :, 0]) * expert_pre[:, :, 1]).astype(jnp.bfloat16)
    expert_result = jnp.einsum(
        "erf,efd->erd", expert_hidden, expert_down, preferred_element_type=jnp.float32
    )
    returning = from_expert_major(expert_result, dp_size)
    returned = lax.all_to_all(
        returning.astype(jnp.bfloat16), "dp", split_axis=0, concat_axis=0, tiled=True
    ).astype(returning.dtype)
    padded_back = jnp.concatenate([returned.reshape(-1, D), jnp.zeros((1, D), jnp.float32)], axis=0)
    picked = padded_back[target].reshape(tokens, TOP, D)
    routed_part = jnp.sum(gate_values[:, :, None] * picked, axis=1)
    branch_sum = lax.psum_scatter(
        (shared_part + routed_part).astype(jnp.bfloat16), "tensor", scatter_dimension=0, tiled=True
    ).astype(jnp.float32)
    block_output = lax.dynamic_slice_in_dim(mixed, start, local_rows, 0) + branch_sum
    grad_rows = lax.all_gather(cotangent, "tensor", axis=0, tiled=True)
    grad_out = grad_rows.astype(jnp.float32)
    grad_shared_hidden = jnp.dot(grad_rows, shared_out.T, preferred_element_type=jnp.float32)
    grad_shared_out = jnp.dot(shared_hidden.T, grad_rows, preferred_element_type=jnp.float32)
    grad_shared_pre = swiglu_back(shared_pre[:, 0], shared_pre[:, 1], grad_shared_hidden, 1).astype(
        jnp.bfloat16
    )
    grad_shared_in = jnp.einsum(
        "td,tgf->gdf", second_normed, grad_shared_pre, preferred_element_type=jnp.float32
    )
    grad_second = jnp.einsum(
        "tgf,gdf->td", grad_shared_pre, shared_in, preferred_element_type=jnp.float32
    )
    gate_by_slot = (
        jnp.zeros((experts * capacity + 1,), jnp.float32).at[target].set(gate_values.reshape(-1))
    )
    slot_ids = jnp.arange(experts * capacity, dtype=jnp.int32).reshape(experts, capacity)
    padded_grad = jnp.concatenate([grad_out, jnp.zeros((1, D), jnp.float32)], axis=0)
    grad_outgoing = (gate_by_slot[slot_ids][..., None] * padded_grad[owner_grid]).astype(
        jnp.bfloat16
    )
    grad_arrived = lax.all_to_all(grad_outgoing, "dp", split_axis=0, concat_axis=0, tiled=True)
    grad_expert_rows = to_expert_major(grad_arrived, dp_size, local_experts)
    grad_expert_hidden = jnp.einsum(
        "erd,efd->erf", grad_expert_rows, expert_down, preferred_element_type=jnp.float32
    )
    grad_expert_down = jnp.einsum(
        "erf,erd->efd", expert_hidden, grad_expert_rows, preferred_element_type=jnp.float32
    )
    grad_expert_pre = swiglu_back(
        expert_pre[:, :, 0], expert_pre[:, :, 1], grad_expert_hidden, 2
    ).astype(jnp.bfloat16)
    grad_expert_gate_up = jnp.einsum(
        "erd,ergf->egdf", expert_rows, grad_expert_pre, preferred_element_type=jnp.float32
    )
    grad_expert_input = jnp.einsum(
        "ergf,egdf->erd", grad_expert_pre, expert_gate_up, preferred_element_type=jnp.float32
    )
    grad_returning = from_expert_major(grad_expert_input, dp_size)
    grad_returned = lax.all_to_all(
        grad_returning.astype(jnp.bfloat16), "dp", split_axis=0, concat_axis=0, tiled=True
    ).astype(grad_returning.dtype)
    padded_grad_back = jnp.concatenate(
        [grad_returned.reshape(-1, D), jnp.zeros((1, D), jnp.float32)], axis=0
    )
    grad_second = grad_second + jnp.sum(padded_grad_back[target].reshape(tokens, TOP, D), axis=1)
    grad_gates = jnp.sum(grad_out[:, None, :] * picked, axis=-1)
    grad_second, grad_gates = (
        lax.psum(grad_second.astype(jnp.bfloat16), "tensor").astype(jnp.float32),
        lax.psum(grad_gates.astype(jnp.bfloat16), "tensor").astype(jnp.float32),
    )
    chosen = (routes[:, :, None] == jnp.arange(experts, dtype=jnp.int32)[None, None, :]).astype(
        jnp.float32
    )
    grad_probabilities = jnp.sum(chosen * grad_gates[:, :, None], axis=1)
    grad_logits = probabilities * (
        grad_probabilities - jnp.sum(probabilities * grad_probabilities, axis=-1, keepdims=True)
    )
    grad_logits_low = grad_logits.astype(jnp.bfloat16)
    grad_router = jnp.dot(second_normed.T, grad_logits_low, preferred_element_type=jnp.float32)
    grad_second = grad_second + jnp.dot(
        grad_logits_low, router_weight.T, preferred_element_type=jnp.float32
    )
    gain_ffn_grad = jnp.sum(grad_second * second_unit, axis=0)
    grad_mixed = grad_out + rms_back(grad_second * ffn_gain_wide, second_unit, second_scale)
    grad_attn_low = grad_mixed.astype(jnp.bfloat16)
    grad_output_weight = jnp.dot(attended.T, grad_attn_low, preferred_element_type=jnp.float32)
    grad_attended = (
        jnp.dot(grad_attn_low, output_weight.T, preferred_element_type=jnp.float32)
        .astype(jnp.bfloat16)
        .reshape(tokens, heads, VD)
    )
    scores = attention_scores(query_rows, key_nope, key_rope, allowed, scale)
    weights = jnp.exp(scores - log_total)
    weights_low = weights.astype(jnp.bfloat16)
    grad_weights = jnp.einsum(
        "ihd,jhd->hij", grad_attended, values, preferred_element_type=jnp.float32
    )
    grad_values = jnp.einsum(
        "hij,ihd->jhd", weights_low, grad_attended, preferred_element_type=jnp.float32
    )
    grad_scores = (
        weights * (grad_weights - jnp.sum(weights * grad_weights, axis=-1, keepdims=True))
    ).astype(jnp.bfloat16)
    grad_query_nope = (
        jnp.einsum("hij,jhd->ihd", grad_scores, key_nope, preferred_element_type=jnp.float32)
        * scale
    )
    grad_query_rope = (
        jnp.einsum("hij,jd->ihd", grad_scores, key_rope, preferred_element_type=jnp.float32) * scale
    )
    grad_key_nope = (
        jnp.einsum(
            "hij,ihd->jhd", grad_scores, query_rows[..., :NOPE], preferred_element_type=jnp.float32
        )
        * scale
    )
    grad_key_rope = (
        jnp.einsum(
            "hij,ihd->jd", grad_scores, query_rows[..., NOPE:], preferred_element_type=jnp.float32
        )
        * scale
    )
    grad_query = (
        jnp.concatenate(
            [grad_query_nope, rotate_back(grad_query_rope, cosine[:, None, :], sine[:, None, :])],
            axis=-1,
        )
        .astype(jnp.bfloat16)
        .reshape(tokens, heads * (NOPE + ROPE))
    )
    grad_query_weight = jnp.dot(first_normed.T, grad_query, preferred_element_type=jnp.float32)
    grad_first = jnp.dot(grad_query, query_weight.T, preferred_element_type=jnp.float32)
    grad_keyval = (
        jnp.concatenate([grad_key_nope, grad_values], axis=-1)
        .astype(jnp.bfloat16)
        .reshape(tokens, heads * (NOPE + VD))
    )
    grad_keyval_weight = jnp.dot(latent_normed.T, grad_keyval, preferred_element_type=jnp.float32)
    grad_latent_normed = jnp.dot(grad_keyval, keyval_weight.T, preferred_element_type=jnp.float32)
    gain_latent_part = jnp.sum(grad_latent_normed * latent_unit, axis=0)
    grad_latent = rms_back(grad_latent_normed * latent_gain_wide, latent_unit, latent_scale)
    grad_latent_all = jnp.concatenate(
        [grad_latent, rotate_back(grad_key_rope, cosine, sine)], axis=-1
    )
    grad_first, grad_latent_all, gain_latent_grad = (
        lax.psum(grad_first.astype(jnp.bfloat16), "tensor").astype(jnp.float32),
        lax.psum(grad_latent_all.astype(jnp.bfloat16), "tensor").astype(jnp.float32),
        lax.psum(gain_latent_part.astype(jnp.bfloat16), "tensor").astype(jnp.float32),
    )
    grad_latent_low = grad_latent_all.astype(jnp.bfloat16)
    grad_latent_weight = jnp.dot(
        first_normed.T, grad_latent_low, preferred_element_type=jnp.float32
    )
    grad_first = grad_first + jnp.dot(
        grad_latent_low, latent_weight.T, preferred_element_type=jnp.float32
    )
    gain_attn_grad = jnp.sum(grad_first * first_unit, axis=0)
    grad_inputs = grad_mixed + rms_back(grad_first * attn_gain_wide, first_unit, first_scale)
    grad_local = lax.dynamic_slice_in_dim(grad_inputs, start, local_rows, 0)
    summed = (
        lax.psum_scatter(gain_attn_grad, "dp", scatter_dimension=0, tiled=True),
        lax.psum_scatter(grad_query_weight, "dp", scatter_dimension=0, tiled=True),
        lax.psum_scatter(grad_latent_weight, "dp", scatter_dimension=0, tiled=True),
        lax.psum_scatter(gain_latent_grad, "dp", scatter_dimension=0, tiled=True),
        lax.psum_scatter(grad_keyval_weight, "dp", scatter_dimension=0, tiled=True),
        lax.psum_scatter(grad_output_weight, "dp", scatter_dimension=1, tiled=True),
        lax.psum_scatter(gain_ffn_grad, "dp", scatter_dimension=0, tiled=True),
        lax.psum_scatter(grad_router, "dp", scatter_dimension=0, tiled=True),
        lax.psum_scatter(grad_shared_in, "dp", scatter_dimension=1, tiled=True),
        lax.psum_scatter(grad_shared_out, "dp", scatter_dimension=1, tiled=True),
    )
    return (
        block_output,
        grad_local,
        summed[0],
        summed[1],
        summed[2],
        summed[3],
        summed[4],
        summed[5],
        summed[6],
        summed[7],
        summed[8],
        summed[9],
        grad_expert_gate_up,
        grad_expert_down,
    )


RINGS = 4


def ring_step(values):
    return lax.ppermute(values, "dp", [(i, (i + RINGS) % 16) for i in range(16)])


def other_y(values):
    return lax.ppermute(values, "dp", [(i, i ^ 2) for i in range(16)])


def other_core(values):
    return lax.ppermute(values, "dp", [(i, i ^ 1) for i in range(16)])


def other_x(values):
    return lax.ppermute(values, "tensor", [(0, 1), (1, 0)])


def fence_kernel(*refs):
    pass


def after(values, *others):
    anywhere = pl.BlockSpec(memory_space=pl.ANY)
    return pl.pallas_call(
        fence_kernel,
        out_shape=jax.ShapeDtypeStruct(values.shape, values.dtype),
        in_specs=[anywhere] * (1 + len(others)),
        out_specs=anywhere,
        input_output_aliases={0: 0},
    )(values, *others)


def gather_rows(rows, corners):
    planes = []
    current = rows
    for distance in range(RINGS):
        if distance:
            current = ring_step(current)
        beside = other_y(current)
        across = other_x(current)
        corner = other_x(beside) if corners[distance] == "x" else other_y(across)
        planes.append((current, beside, across, corner))
    return planes


def add_low(first, second):
    return (first.astype(jnp.float32) + second.astype(jnp.float32)).astype(jnp.bfloat16)


def turn_corner(plane, direction):
    own, beside, across, corner = plane
    if direction == "x":
        return own, add_low(beside, other_x(corner)), across
    return own, beside, add_low(across, other_y(corner))


def close_plane(turned):
    own, beside, across = turned
    return own, other_y(beside), other_x(across)


def wide_sum(*values):
    total = values[0].astype(jnp.float32)
    for value in values[1:]:
        total = total + value.astype(jnp.float32)
    return total


def ring_sum(parts, low):
    moving = parts[1]
    for distance in (2, 3, 0):
        moving = ring_step(moving.astype(low)).astype(jnp.float32) + parts[distance]
    return moving


def ring_shards(shard):
    held = [shard]
    for _ in range(RINGS - 1):
        held.append(ring_step(held[-1]))
    return held


def gather_weight(held):
    chunks = []
    beside = None
    for distance, current in enumerate(held):
        beside = other_y(current if beside is None else after(current, beside))
        for flip_y, chunk in ((0, current), (1, beside)):
            for flip_core, piece in ((0, chunk), (1, other_core(chunk))):
                chunks.append(((distance, flip_y, flip_core), piece))
    return chunks


def place_of(coords, key):
    z, y, core = coords
    distance, flip_y, flip_core = key
    return (
        lax.rem(z + RINGS - distance, RINGS) * 4
        + (1 - y if flip_y else y) * 2
        + (1 - core if flip_core else core)
    )


def weight_keys():
    return [
        (distance, flip_y, flip_core)
        for flip_core in (0, 1)
        for flip_y in (0, 1)
        for distance in range(RINGS)
    ]


def scatter_blocks(grads, low):
    half = grads.shape[0] // 2
    total = grads[:half].astype(jnp.float32) + other_core(grads[half:].astype(low)).astype(
        jnp.float32
    )
    quarter = half // 2
    total = total[:quarter] + other_y(total[quarter:].astype(low)).astype(jnp.float32)
    size = quarter // RINGS
    return ring_sum([total[r * size : (r + 1) * size] for r in range(RINGS)], low)


def pick_blocks(values, order):
    chosen = order[:, None] == jnp.arange(values.shape[0], dtype=jnp.int32)[None, :]
    chosen = chosen.reshape(chosen.shape + (1,) * (values.ndim - 1))
    return jnp.sum(jnp.where(chosen, values[None], 0.0), axis=1)


def wide_dot(left, right):
    return jnp.dot(left, right, preferred_element_type=jnp.float32)


def dot_turned(left, right):
    return lax.dot_general(left, right, (((1,), (1,)), ((), ())), preferred_element_type=jnp.float32)


def dot_rows(left, right):
    return lax.dot_general(left, right, (((0,), (0,)), ((), ())), preferred_element_type=jnp.float32)


TILE = 256


def whole(array):
    return pl.BlockSpec(array.shape, lambda *i: (0,) * array.ndim)


def in_vmem(count):
    return [pl.BlockSpec(memory_space=pltpu.VMEM)] * count


def in_place(count):
    return [pl.BlockSpec(memory_space=pl.ANY)] * count


def head_scores(heads, h, nope_ref, turned_ref, keyval_ref, key_ref, masks):
    span = ROPE // 2 * heads
    column = pl.ds(pl.multiple_of(h * NOPE, NOPE), NOPE)
    key_column = pl.ds(pl.multiple_of(h * (NOPE + VD), NOPE), NOPE)
    scores = dot_turned(nope_ref[:, column], keyval_ref[:, key_column])
    for k in (0, 1):
        part = turned_ref[:, k * span : (k + 1) * span]
        part = jnp.where(masks, part, jnp.zeros_like(part))
        scores += dot_turned(part, key_ref[:, k * span : (k + 1) * span])
    return scores * (NOPE + ROPE) ** (-0.5)


def head_lanes(heads, h):
    span = ROPE // 2 * heads
    lane = lax.broadcasted_iota(jnp.int32, (1, span), 1)
    return (lane >= h * (ROPE // 2)) & (lane < (h + 1) * (ROPE // 2))


def allowed_rows(count, segment_row, segment_column):
    tokens = segment_row.shape[1]
    column = lax.broadcasted_iota(jnp.int32, (tokens, tokens), 0)
    row = lax.broadcasted_iota(jnp.int32, (tokens, tokens), 1)
    live = (column < count) & (row < count) & (row <= column)
    return (segment_row == segment_column) & live | (column == row)


def attend_kernel(
    keys,
    extra,
    heads,
    sizes,
    place_ref,
    segment_row_ref,
    segment_column_ref,
    cosine_ref,
    sine_ref,
    own_ref,
    other_ref,
    *refs,
):
    depth, query_width, used, latent_depth, keyval_part, first_width = sizes
    chunks = refs[: len(keys)]
    (
        own_out,
        sent_out,
        first_ref,
        keyval_weight_ref,
        output_ref,
        normed_ref,
        nope_ref,
        turned_ref,
        latent_ref,
        key_ref,
        keyval_ref,
        total_ref,
        attended_ref,
        gains_ref,
        latent_gain_ref,
        semaphores,
    ) = refs[len(keys) + extra :]
    f32, bf16 = jnp.float32, jnp.bfloat16
    local_rows = own_ref.shape[0]
    tokens = 2 * local_rows
    coords = (place_ref[0], place_ref[1], place_ref[2])
    x = place_ref[3]
    copies = []
    parts = depth // latent_depth
    for key, chunk in zip(keys, chunks):
        block = place_of(coords, key)
        rows = pl.ds(pl.multiple_of(block * depth, depth), depth)
        small_rows = pl.ds(pl.multiple_of(block * latent_depth, latent_depth), latent_depth)
        moves = [(chunk.at[:, pl.ds(0, first_width)], first_ref.at[rows])]
        for k in range(parts):
            moves.append(
                (
                    chunk.at[
                        pl.ds(k * latent_depth, latent_depth), pl.ds(first_width, keyval_part)
                    ],
                    keyval_weight_ref.at[small_rows, pl.ds(k * keyval_part, keyval_part)],
                )
            )
        moves.append(
            (
                chunk.at[:, pl.ds(first_width + keyval_part, heads * VD)],
                output_ref.at[rows],
            )
        )
        for source, target in moves:
            copies.append(pltpu.make_async_copy(source, target, semaphores.at[len(copies)]))
    for copy in copies:
        copy.start()
    for copy in copies:
        copy.wait()

    edge = query_width + KVR
    spread = jnp.transpose(first_ref[:, edge:].astype(f32))[used - edge : used - edge + 8]
    gains_ref[...] = spread
    gain = spread[0:1]
    source = lax.broadcasted_iota(jnp.int32, (D, KVR), 0)
    target = lax.broadcasted_iota(jnp.int32, (D, KVR), 1)
    wanted = target // latent_depth * depth + target % latent_depth
    chosen = jnp.where(source == wanted, 1.0, 0.0).astype(bf16)
    latent_gain = wide_dot(spread.astype(bf16), chosen)[2:3]
    latent_gain_ref[...] = latent_gain
    for ref, start in ((own_ref, x * local_rows), (other_ref, (1 - x) * local_rows)):
        rows = ref[...].astype(f32)
        unit = rows * lax.rsqrt(jnp.mean(rows * rows, axis=1, keepdims=True) + EPSILON)
        normed_ref[pl.ds(pl.multiple_of(start, local_rows), local_rows), :] = (unit * gain).astype(
            bf16
        )
    nope_width = heads * NOPE
    span = heads * (ROPE // 2)
    half = nope_width // 2
    for k in (0, 1):
        nope_ref[:, k * half : (k + 1) * half] = wide_dot(
            normed_ref[...], first_ref[:, k * half : (k + 1) * half]
        ).astype(bf16)
    turning = wide_dot(normed_ref[...], first_ref[:, nope_width : nope_width + 2 * span])
    cosine, sine = cosine_ref[...], sine_ref[...]
    first, second = turning[:, :span], turning[:, span:]
    turned_ref[:, :span] = (first * cosine - second * sine).astype(bf16)
    turned_ref[:, span:] = (second * cosine + first * sine).astype(bf16)
    latent = wide_dot(normed_ref[...], first_ref[:, query_width : query_width + KVR])
    latent_ref[...] = latent
    tail = wide_dot(normed_ref[...], first_ref[:, query_width + KVR :])
    lane = lax.broadcasted_iota(jnp.int32, (1, tail.shape[1]), 1)
    swapped = jnp.where(
        lane < ROPE // 2,
        -pltpu.roll(tail, tail.shape[1] - ROPE // 2, 1),
        pltpu.roll(tail, ROPE // 2, 1),
    )
    width = tail.shape[1]
    turned_key = tail * cosine[:, :width] + swapped * sine[:, :width]
    turned_key = jnp.where(lane < ROPE, turned_key, 0.0).astype(bf16)
    source = lax.broadcasted_iota(jnp.int32, (width, 2 * span), 0)
    target = lax.broadcasted_iota(jnp.int32, (width, 2 * span), 1)
    wanted = target % (ROPE // 2) + jnp.where(target < span, 0, ROPE // 2)
    key_ref[...] = wide_dot(turned_key, (source == wanted).astype(bf16)).astype(bf16)
    unit = latent * lax.rsqrt(jnp.mean(latent * latent, axis=1, keepdims=True) + EPSILON)
    latent_normed = (unit * latent_gain).astype(bf16)
    half = keyval_ref.shape[1] // 4
    for k in range(4):
        keyval_ref[:, k * half : (k + 1) * half] = wide_dot(
            latent_normed, keyval_weight_ref[:, k * half : (k + 1) * half]
        ).astype(bf16)
    allowed = allowed_rows(place_ref[4], segment_row_ref[...], segment_column_ref[...])
    total_lane = lax.broadcasted_iota(jnp.int32, total_ref.shape, 1)
    total_ref[...] = jnp.zeros_like(total_ref)

    def one_head(h, _):
        scores = head_scores(
            heads, h, nope_ref, turned_ref, keyval_ref, key_ref, head_lanes(heads, h)
        )
        scores = jnp.where(allowed, scores, -1e30)
        most = jnp.max(scores, axis=1, keepdims=True)
        total = most + jnp.log(jnp.sum(jnp.exp(scores - most), axis=1, keepdims=True))
        weights = jnp.exp(scores - total).astype(bf16)
        total_ref[...] += jnp.where(total_lane == h, total, 0.0)
        value_column = pl.ds(pl.multiple_of(h * (NOPE + VD) + NOPE, NOPE), VD)
        attended_ref[:, pl.ds(pl.multiple_of(h * VD, VD), VD)] = wide_dot(
            weights, keyval_ref[:, value_column]
        ).astype(bf16)
        return 0

    lax.fori_loop(0, heads, one_head, 0)
    own = pl.ds(pl.multiple_of(x * local_rows, local_rows), local_rows)
    other = pl.ds(pl.multiple_of((1 - x) * local_rows, local_rows), local_rows)
    pieces = 4
    size = output_ref.shape[0] // pieces
    for k in range(pieces):
        columns = slice(k * size, (k + 1) * size)
        own_out[:, columns] = dot_turned(attended_ref[own, :], output_ref[columns, :])
        sent_out[:, columns] = dot_turned(attended_ref[other, :], output_ref[columns, :]).astype(
            bf16
        )


def attend_forward(place, segments, cosine, sine, own, other, chunks, heads, sizes, others):
    depth, query_width, used, latent_depth, keyval_part, first_width = sizes
    f32, bf16 = jnp.float32, jnp.bfloat16
    keys = [key for key, _ in chunks]
    local_rows = own.shape[0]
    tokens = 2 * local_rows
    span = heads * (ROPE // 2)
    shapes = [
        ((local_rows, D), f32),
        ((local_rows, D), bf16),
        ((D, first_width), bf16),
        ((KVR, heads * (NOPE + VD)), bf16),
        ((D, heads * VD), bf16),
        ((tokens, D), bf16),
        ((tokens, heads * NOPE), bf16),
        ((tokens, 2 * span), bf16),
        ((tokens, KVR), f32),
        ((tokens, 2 * span), bf16),
        ((tokens, heads * (NOPE + VD)), bf16),
        ((tokens, 128), f32),
        ((tokens, heads * VD), bf16),
        ((8, D), f32),
        ((1, KVR), f32),
    ]
    return pl.pallas_call(
        functools.partial(attend_kernel, keys, len(others), heads, sizes),
        out_shape=[jax.ShapeDtypeStruct(*shape) for shape in shapes],
        in_specs=[pl.BlockSpec(memory_space=pltpu.SMEM)]
        + in_vmem(6)
        + in_place(len(chunks) + len(others)),
        out_specs=in_vmem(len(shapes)),
        scratch_shapes=[
            pltpu.SemaphoreType.DMA((len(chunks) * (2 + depth // latent_depth),))
        ],
        compiler_params=pltpu.CompilerParams(vmem_limit_bytes=48 * 1024 * 1024),
        cost_estimate=pl.CostEstimate(
            flops=2 * tokens * D * (first_width + heads * VD + 1024),
            bytes_accessed=4 * D * (first_width + 1536),
            transcendentals=2 * heads * tokens * tokens,
        ),
    )(
        place,
        segments,
        segments.T,
        cosine,
        sine,
        own,
        other,
        *[piece for _, piece in chunks],
        *others,
    )


def attend_back_kernel(
    heads,
    place_ref,
    segment_row_ref,
    segment_column_ref,
    cosine_ref,
    sine_ref,
    own_ref,
    other_ref,
    keyval_weight_ref,
    output_ref,
    nope_ref,
    turned_ref,
    latent_ref,
    key_ref,
    keyval_ref,
    total_ref,
    latent_gain_ref,
    projected_ref,
    keyval_grad_ref,
    latent_out,
    gain_ref,
    grad_ref,
    turn_ref,
    back_ref,
):
    f32, bf16 = jnp.float32, jnp.bfloat16
    local_rows = own_ref.shape[0]
    x = place_ref[3]
    span = heads * (ROPE // 2)
    nope_width = heads * NOPE
    query_width = nope_width + 2 * span
    scale = (NOPE + ROPE) ** (-0.5)
    for ref, start in ((own_ref, x * local_rows), (other_ref, (1 - x) * local_rows)):
        rows = pl.ds(pl.multiple_of(start, local_rows), local_rows)
        for k in (0, 1):
            half = slice(k * nope_width // 2, (k + 1) * nope_width // 2)
            grad_ref[rows, half] = wide_dot(ref[...], output_ref[:, half]).astype(bf16)
    allowed = allowed_rows(place_ref[4], segment_row_ref[...], segment_column_ref[...])
    total_lane = lax.broadcasted_iota(jnp.int32, total_ref.shape, 1)
    turn_ref[...] = jnp.zeros_like(turn_ref)
    back_ref[...] = jnp.zeros_like(back_ref)

    def one_head(h, _):
        mask = head_lanes(heads, h)
        scores = head_scores(heads, h, nope_ref, turned_ref, keyval_ref, key_ref, mask)
        total = jnp.sum(jnp.where(total_lane == h, total_ref[...], 0.0), axis=1, keepdims=True)
        weights = jnp.exp(jnp.where(allowed, scores, -1e30) - total)
        weights_low = weights.astype(bf16)
        column = pl.ds(pl.multiple_of(h * NOPE, NOPE), NOPE)
        key_column = pl.ds(pl.multiple_of(h * (NOPE + VD), NOPE), NOPE)
        value_column = pl.ds(pl.multiple_of(h * (NOPE + VD) + NOPE, NOPE), VD)
        grads = grad_ref[:, column]
        grad_weights = dot_turned(grads, keyval_ref[:, value_column])
        keyval_grad_ref[:, value_column] = dot_rows(weights_low, grads).astype(bf16)
        grad_scores = (
            weights * (grad_weights - jnp.sum(weights * grad_weights, axis=1, keepdims=True))
        ).astype(bf16)
        projected_ref[:, column] = (
            scale * wide_dot(grad_scores, keyval_ref[:, key_column])
        ).astype(bf16)
        keyval_grad_ref[:, key_column] = (
            scale * dot_rows(grad_scores, nope_ref[:, column])
        ).astype(bf16)
        for k in (0, 1):
            part = slice(k * span, (k + 1) * span)
            turn = wide_dot(grad_scores, key_ref[:, part])
            turn_ref[:, part] += jnp.where(mask, turn, 0.0)
            own = turned_ref[:, part]
            own = jnp.where(mask, own, jnp.zeros_like(own))
            back_ref[:, part] += dot_rows(grad_scores, own)
        return 0

    lax.fori_loop(0, heads, one_head, 0)
    cosine, sine = cosine_ref[...], sine_ref[...]
    first, second = scale * turn_ref[:, :span], scale * turn_ref[:, span:]
    projected_ref[:, nope_width : nope_width + span] = (first * cosine + second * sine).astype(bf16)
    projected_ref[:, nope_width + span : query_width] = (second * cosine - first * sine).astype(
        bf16
    )
    folded = []
    for k in (0, 1):
        part = scale * back_ref[:, k * span : (k + 1) * span]
        shift = span // 2
        while shift >= ROPE // 2:
            part = part + pltpu.roll(part, shift, 1)
            shift //= 2
        folded.append(part)
    width = projected_ref.shape[1] - query_width - KVR
    lane = lax.broadcasted_iota(jnp.int32, (1, width), 1)
    first = (folded[0] * cosine + folded[1] * sine)[:, :width]
    second = (folded[1] * cosine - folded[0] * sine)[:, :width]
    projected_ref[:, query_width + KVR :] = jnp.where(
        lane < ROPE // 2, first, jnp.where(lane < ROPE, second, 0.0)
    ).astype(bf16)
    gain = latent_gain_ref[...]
    latent = latent_ref[...]
    row_scale = lax.rsqrt(jnp.mean(latent * latent, axis=1, keepdims=True) + EPSILON)
    unit = latent * row_scale
    latent_out[...] = (unit * gain).astype(bf16)
    grad_normed = dot_turned(keyval_grad_ref[...], keyval_weight_ref[...])
    gain_ref[...] = jnp.sum(grad_normed * unit, axis=0, keepdims=True)
    grad_unit = grad_normed * gain
    projected_ref[:, query_width : query_width + KVR] = (
        row_scale * (grad_unit - unit * jnp.mean(grad_unit * unit, axis=1, keepdims=True))
    ).astype(bf16)


def attend_back(place, segments, cosine, sine, own, other, saved, heads, first_width):
    f32, bf16 = jnp.float32, jnp.bfloat16
    keyval = saved[6]
    tokens = 2 * own.shape[0]
    span = heads * (ROPE // 2)
    return pl.pallas_call(
        functools.partial(attend_back_kernel, heads),
        out_shape=[
            jax.ShapeDtypeStruct((tokens, first_width), bf16),
            jax.ShapeDtypeStruct((tokens, keyval.shape[1]), bf16),
            jax.ShapeDtypeStruct((tokens, KVR), bf16),
            jax.ShapeDtypeStruct((1, KVR), f32),
        ],
        in_specs=[pl.BlockSpec(memory_space=pltpu.SMEM)] + in_vmem(15),
        out_specs=in_vmem(4),
        scratch_shapes=[
            pltpu.VMEM((tokens, heads * NOPE), bf16),
            pltpu.VMEM((tokens, 2 * span), f32),
            pltpu.VMEM((tokens, 2 * span), f32),
        ],
        compiler_params=pltpu.CompilerParams(vmem_limit_bytes=48 * 1024 * 1024),
        cost_estimate=pl.CostEstimate(
            flops=2 * tokens * D * 3000,
            bytes_accessed=2 * D * 1536,
            transcendentals=heads * tokens * tokens,
        ),
    )(
        place,
        segments,
        segments.T,
        cosine,
        sine,
        own,
        other,
        *saved,
    )


def block_grads_kernel(extra, places_ref, left_ref, right_ref, *refs):
    result = dot_rows(left_ref[...], right_ref[...])
    if extra:
        result += refs[0][...].astype(jnp.float32)
    refs[-1][...] = result.astype(jnp.bfloat16)


def block_grads(left, right, width, places, first, count, arrived=None):
    rows = right.shape[0]
    size = left.shape[1] // places.shape[0]
    extra = [] if arrived is None else [arrived]
    return pl.pallas_call(
        functools.partial(block_grads_kernel, len(extra)),
        grid_spec=pltpu.PrefetchScalarGridSpec(
            num_scalar_prefetch=1,
            grid=(count,),
            in_specs=[
                pl.BlockSpec((rows, size), lambda i, where: (0, where[first + i])),
                pl.BlockSpec((rows, width), lambda i, where: (0, 0)),
            ]
            + [pl.BlockSpec((size, width), lambda i, where: (first + i, 0))] * len(extra),
            out_specs=pl.BlockSpec((size, width), lambda i, where: (i, 0)),
        ),
        out_shape=jax.ShapeDtypeStruct((count * size, width), jnp.bfloat16),
        cost_estimate=pl.CostEstimate(
            flops=2 * rows * count * size * width,
            bytes_accessed=2 * (count * size * width + rows * width),
            transcendentals=0,
        ),
    )(places, left, right, *extra)


def mixed_grads_kernel(first, extra, places_ref, *refs):
    normed_ref, right_ref, small_ref, latent_ref, keyval_ref, grad_ref, attended_ref = refs[:7]
    out_ref, keyval_all = refs[-2:]
    step = pl.program_id(0)
    size = normed_ref.shape[1]
    blocks = places_ref.shape[0]
    latent_size = latent_ref.shape[1] // blocks
    parts = size // latent_size
    columns = keyval_ref.shape[1] // parts

    @pl.when(step == 0)
    def _():
        for k in range(parts):
            some = slice(k * columns, (k + 1) * columns)
            keyval_all[:, some] = dot_rows(latent_ref[...], keyval_ref[:, some])

    low = jnp.bfloat16
    at = right_ref.shape[1]
    result = dot_rows(normed_ref[...], right_ref[...])
    small = jnp.transpose(small_ref[...])
    result = result + jnp.concatenate(
        [jnp.zeros((size, at - small.shape[1]), jnp.float32), small], axis=1
    )
    start = pl.multiple_of(places_ref[first + step] * latent_size, latent_size)
    strip = keyval_all[pl.ds(start, latent_size), :]
    keyval = jnp.concatenate([strip[:, k * columns : (k + 1) * columns] for k in range(parts)], axis=0)
    output = dot_rows(grad_ref[...], attended_ref[...])
    for value, begin in ((result, 0), (keyval, at), (output, at + columns)):
        end = begin + value.shape[1]
        if extra:
            value = value + refs[7][:, begin:end].astype(jnp.float32)
        out_ref[:, begin:end] = value.astype(low)


def mixed_grads(normed, right, small, latent, keyval, grad, attended, places, first, count, arrived=None):
    rows, width = right.shape
    blocks = places.shape[0]
    size = normed.shape[1] // blocks
    parts = size // (latent.shape[1] // blocks)
    total = width + keyval.shape[1] // parts + attended.shape[1]
    extra = [] if arrived is None else [arrived]

    def block(i, where):
        return (0, where[first + i])

    def still(array):
        return pl.BlockSpec(array.shape, lambda i, where: (0, 0))

    return pl.pallas_call(
        functools.partial(mixed_grads_kernel, first, len(extra)),
        grid_spec=pltpu.PrefetchScalarGridSpec(
            num_scalar_prefetch=1,
            grid=(count,),
            in_specs=[
                pl.BlockSpec((rows, size), block),
                still(right),
                pl.BlockSpec((small.shape[0], size), block),
                still(latent),
                still(keyval),
                pl.BlockSpec((rows, size), block),
                still(attended),
            ]
            + [pl.BlockSpec((size, total), lambda i, where: (first + i, 0))] * len(extra),
            out_specs=pl.BlockSpec((size, total), lambda i, where: (i, 0)),
            scratch_shapes=[pltpu.VMEM((latent.shape[1], keyval.shape[1]), jnp.float32)],
        ),
        out_shape=jax.ShapeDtypeStruct((count * size, total), jnp.bfloat16),
        compiler_params=pltpu.CompilerParams(vmem_limit_bytes=32 * 1024 * 1024),
        cost_estimate=pl.CostEstimate(
            flops=2 * rows * count * size * total,
            bytes_accessed=2 * (count * size * total + rows * total),
            transcendentals=0,
        ),
    )(places, normed, right, small, latent, keyval, grad, attended, *extra)


def first_back_kernel(place_ref, own_ref, other_ref, grad_ref, weight_ref, own_out, sent_out, gain_ref):
    local_rows = own_ref.shape[0]
    x = place_ref[3]
    size = weight_ref.shape[0] // 4
    for ref, start, out in (
        (own_ref, x * local_rows, own_out),
        (other_ref, (1 - x) * local_rows, sent_out),
    ):
        rows = ref[...].astype(jnp.float32)
        unit = rows * lax.rsqrt(jnp.mean(rows * rows, axis=1, keepdims=True) + EPSILON)
        grads = grad_ref[pl.ds(pl.multiple_of(start, local_rows), local_rows), :]
        for k in range(4):
            some = slice(k * size, (k + 1) * size)
            part = dot_turned(grads, weight_ref[some, :])
            out[:, some] = part.astype(out.dtype)
            gain = jnp.sum(part * unit[:, some], axis=0, keepdims=True)
            if ref is own_ref:
                gain_ref[:, some] = gain
            else:
                gain_ref[:, some] += gain


def first_back(place, own, other, grads, weight):
    f32, bf16 = jnp.float32, jnp.bfloat16
    depth = weight.shape[0]
    return pl.pallas_call(
        first_back_kernel,
        out_shape=[
            jax.ShapeDtypeStruct(own.shape, f32),
            jax.ShapeDtypeStruct(own.shape, bf16),
            jax.ShapeDtypeStruct((1, depth), f32),
        ],
        in_specs=[pl.BlockSpec(memory_space=pltpu.SMEM)] + in_vmem(4),
        out_specs=in_vmem(3),
        compiler_params=pltpu.CompilerParams(vmem_limit_bytes=32 * 1024 * 1024),
        cost_estimate=pl.CostEstimate(
            flops=4 * own.shape[0] * weight.shape[0] * weight.shape[1],
            bytes_accessed=2 * weight.shape[0] * weight.shape[1],
            transcendentals=0,
        ),
    )(place, own, other, grads, weight)


def close_ring(near, arrived):
    size = near.shape[0] // RINGS
    total = near.astype(jnp.float32) + arrived.astype(jnp.float32)
    return ring_sum([total[r * size : (r + 1) * size] for r in range(RINGS)], jnp.bfloat16)


def pack_kernel(heads, query_ref, latent_ref, small_ref, keyval_ref, output_ref, out_ref):
    half = ROPE // 2
    head = NOPE + ROPE
    nope_width = heads * NOPE
    for h in range(heads):
        start = h * head
        out_ref[:, h * NOPE : (h + 1) * NOPE] = query_ref[:, start : start + NOPE]
        for k in (0, 1):
            to = nope_width + k * heads * half + h * half
            out_ref[:, to : to + half] = query_ref[
                :, start + NOPE + k * half : start + NOPE + (k + 1) * half
            ]
    at = heads * head
    edge = at + KVR
    out_ref[:, at:edge] = latent_ref[:, :KVR]
    out_ref[:, edge : edge + 128] = jnp.concatenate([latent_ref[:, KVR:], small_ref[...]], axis=1)
    at = edge + 128
    size = keyval_ref.shape[0]
    parts = out_ref.shape[0] // size
    part = keyval_ref.shape[1] // parts
    for k in range(parts):
        out_ref[k * size : (k + 1) * size, at : at + part] = keyval_ref[
            :, k * part : (k + 1) * part
        ]
    out_ref[:, at + part :] = jnp.transpose(output_ref[...].astype(jnp.float32)).astype(
        jnp.bfloat16
    )


def pack_weights(query, latent, small, keyval, output):
    depth, query_width = query.shape
    heads = query_width // (NOPE + ROPE)
    width = query_width + KVR + 128 + keyval.size // depth + output.shape[0]
    return pl.pallas_call(
        functools.partial(pack_kernel, heads),
        out_shape=jax.ShapeDtypeStruct((depth, width), jnp.bfloat16),
        in_specs=in_vmem(5),
        out_specs=pl.BlockSpec(memory_space=pltpu.VMEM),
    )(query, latent, small, keyval, output)


def load_pieces(pieces, target, semaphores):
    size = pieces[0].shape[0]
    copies = [
        pltpu.make_async_copy(piece, target.at[pl.ds(k * size, size)], semaphores.at[k])
        for k, piece in enumerate(pieces)
    ]
    for copy in copies:
        copy.start()
    for copy in copies:
        copy.wait()


def shared_stride(shared):
    return -(-shared // 32) * 32


def pack_shared_kernel(blocks, shared, in_ref, down_ref, out_ref):
    stride = shared_stride(shared)
    out_ref[...] = jnp.zeros_like(out_ref)
    for k in range(3):
        if k < 2:
            units = jnp.transpose(in_ref[k].astype(jnp.float32)).astype(jnp.bfloat16)
        else:
            units = down_ref[...]
        for b in range(blocks):
            out_ref[b, k * stride : k * stride + shared] = units[b * shared : (b + 1) * shared]


def pack_shared(shared_in, shared_down, blocks, others):
    depth = shared_in.shape[1]
    shared = shared_down.shape[0] // blocks
    return pl.pallas_call(
        lambda in_ref, down_ref, *refs: pack_shared_kernel(
            blocks, shared, in_ref, down_ref, refs[-1]
        ),
        out_shape=jax.ShapeDtypeStruct((blocks, 3 * shared_stride(shared), depth), jnp.bfloat16),
        in_specs=in_vmem(2) + in_place(len(others)),
        out_specs=pl.BlockSpec(memory_space=pltpu.VMEM),
    )(shared_in, shared_down, *others)


def unpack_shared_kernel(shared, packed_ref, in_ref, down_ref, units_ref):
    stride = shared_stride(shared)
    blocks = packed_ref.shape[0]
    for k in range(3):
        target = down_ref if k == 2 else units_ref
        for b in range(blocks):
            target[b * shared : (b + 1) * shared, :] = packed_ref[
                b, k * stride : k * stride + shared
            ].astype(jnp.float32)
        if k < 2:
            in_ref[k] = jnp.transpose(units_ref[...])


def unpack_shared(packed, shared):
    blocks, _, depth = packed.shape
    return pl.pallas_call(
        functools.partial(unpack_shared_kernel, shared),
        out_shape=[
            jax.ShapeDtypeStruct((2, depth, blocks * shared), jnp.float32),
            jax.ShapeDtypeStruct((blocks * shared, depth), jnp.float32),
        ],
        in_specs=in_vmem(1),
        out_specs=in_vmem(2),
        scratch_shapes=[pltpu.VMEM((blocks * shared, depth), jnp.float32)],
    )(packed)


def pack_units_kernel(units, shared, own_in, other_in, own_down, other_down, near, far, *refs):
    outs = refs[-3:]
    hole = -(-units // TILE) * TILE
    stride = shared_stride(shared)
    columns = outs[0].shape[1]
    size = near.shape[2]
    for k, out in enumerate(outs):
        first = own_in[0, k] if k < 2 else own_down[0]
        second = other_in[0, k] if k < 2 else other_down[0]
        out[:units] = first
        out[units:hole] = jnp.zeros((hole - units, columns), jnp.bfloat16)
        out[hole : hole + units] = second
        out[hole + units : 2 * hole] = jnp.zeros((hole - units, columns), jnp.bfloat16)
        out[2 * hole :] = jnp.zeros((TILE, columns), jnp.bfloat16)
        for b in range(columns // size):
            part = slice(b * size, (b + 1) * size)
            for at, ref in ((2 * hole, near), (2 * hole + stride, far)):
                out[at : at + shared, part] = ref[b, k * stride : k * stride + shared]


def pack_units(own_in, other_in, own_down, other_down, near, far, shared, others):
    units, depth = own_down.shape[1:]
    size = near.shape[2]
    height = 2 * (-(-units // TILE) * TILE) + TILE
    columns = 2 * size
    in_spec = pl.BlockSpec((1, 2, units, columns), lambda i: (0, 0, 0, i))
    down_spec = pl.BlockSpec((1, units, columns), lambda i: (0, 0, i))
    narrow = pl.BlockSpec((2,) + near.shape[1:], lambda i: (i, 0, 0))
    return pl.pallas_call(
        functools.partial(pack_units_kernel, units, shared),
        grid=(depth // columns,),
        in_specs=[in_spec, in_spec, down_spec, down_spec, narrow, narrow]
        + in_place(len(others)),
        out_specs=[pl.BlockSpec((height, columns), lambda i: (0, i))] * 3,
        out_shape=[jax.ShapeDtypeStruct((height, depth), jnp.bfloat16)] * 3,
        compiler_params=pltpu.CompilerParams(vmem_limit_bytes=32 * 1024 * 1024),
        cost_estimate=pl.CostEstimate(
            flops=0, bytes_accessed=12 * height * depth, transcendentals=0
        ),
    )(own_in, other_in, own_down, other_down, near, far, *others)


def expert_grads_kernel(units, count, extra, right_ref, *refs):
    out = refs[-1]
    for k in range(count):

        @pl.when(pl.program_id(0) == k)
        def _():
            result = dot_rows(refs[k][...], right_ref[...])[:units]
            if extra:
                result += refs[count][0, 0].astype(jnp.float32)
            out[0, 0] = result.astype(out.dtype)


def expert_grads(lefts, right, units, column, arrived, kind, others=()):
    total, depth = right.shape
    wide = -(-units // TILE) * TILE
    extra = [] if arrived is None else [arrived]
    out = pl.BlockSpec((1, 1, units, 2 * TILE), lambda k, i: (0, k, 0, i))
    side = pl.BlockSpec((total, wide), lambda k, i: (0, column))
    return pl.pallas_call(
        functools.partial(expert_grads_kernel, units, len(lefts), len(extra)),
        grid=(len(lefts), depth // (2 * TILE)),
        in_specs=[pl.BlockSpec((total, 2 * TILE), lambda k, i: (0, i))]
        + [side] * len(lefts)
        + [out] * len(extra)
        + in_place(len(others)),
        out_specs=out,
        out_shape=jax.ShapeDtypeStruct((1, len(lefts), units, depth), kind),
        compiler_params=pltpu.CompilerParams(vmem_limit_bytes=48 * 1024 * 1024),
        cost_estimate=pl.CostEstimate(
            flops=2 * len(lefts) * total * depth * wide,
            bytes_accessed=2 * len(lefts) * total * (depth + wide) + 8 * depth * units,
            transcendentals=0,
        ),
    )(right, *lefts, *extra, *others)


def side_grads_kernel(shared, rows_ref, cots_ref, gate_ref, up_ref, hidden_ref, logit_ref, *outs):
    kept_ref, sent_ref, router_ref = outs
    stride = shared_stride(shared)
    size = kept_ref.shape[2]
    for k, (left, right) in enumerate(
        ((gate_ref, rows_ref), (up_ref, rows_ref), (hidden_ref, cots_ref))
    ):
        result = dot_rows(left[...], right[...])
        for b in range(kept_ref.shape[0]):
            part = slice(b * size, (b + 1) * size)
            kept_ref[b, k * stride : (k + 1) * stride] = result[:stride, part]
            sent_ref[b, k * stride : (k + 1) * stride] = result[
                stride : 2 * stride, part
            ].astype(jnp.bfloat16)
    router_ref[...] = dot_rows(logit_ref[...], rows_ref[...])


def side_grads(rows, cots, gate, up, hidden, logits, shared, blocks):
    total, depth = rows.shape
    column = gate.shape[1] // TILE - 1
    size = depth // blocks
    stride = shared_stride(shared)
    wide = pl.BlockSpec((total, 2 * TILE), lambda i: (0, i))
    side = pl.BlockSpec((total, TILE), lambda i: (0, column))
    packed = pl.BlockSpec((2 * TILE // size, 3 * stride, size), lambda i: (i, 0, 0))
    return pl.pallas_call(
        functools.partial(side_grads_kernel, shared),
        grid=(depth // (2 * TILE),),
        in_specs=[wide, wide, side, side, side, whole(logits)],
        out_specs=[packed, packed, pl.BlockSpec((logits.shape[1], 2 * TILE), lambda i: (0, i))],
        out_shape=[
            jax.ShapeDtypeStruct((blocks, 3 * stride, size), jnp.float32),
            jax.ShapeDtypeStruct((blocks, 3 * stride, size), jnp.bfloat16),
            jax.ShapeDtypeStruct((logits.shape[1], depth), jnp.float32),
        ],
        compiler_params=pltpu.CompilerParams(vmem_limit_bytes=48 * 1024 * 1024),
        cost_estimate=pl.CostEstimate(
            flops=8 * total * depth * TILE,
            bytes_accessed=4 * total * depth,
            transcendentals=0,
        ),
    )(rows, cots, gate, up, hidden, logits)


def down_kernel(count, *refs):
    pieces, weight_ref = refs[:count], refs[count]
    grads_ref, rows_ref, semaphores = refs[-3:]

    @pl.when(pl.program_id(0) == 0)
    def _():
        load_pieces(pieces, rows_ref, semaphores)

    size = rows_ref.shape[0] // 2
    for k in range(2):
        part = slice(k * size, (k + 1) * size)
        grads_ref[part, :] = dot_turned(rows_ref[part, :], weight_ref[...]).astype(jnp.bfloat16)


def down_grads(part, pieces, down, kept, others):
    count = len(pieces)
    size, depth = pieces[0].shape
    width = down.shape[0]
    rows = count * size
    return pl.pallas_call(
        functools.partial(down_kernel, count),
        grid=(width // TILE,),
        in_specs=in_place(count)
        + [pl.BlockSpec((TILE, depth), lambda i: (i, 0))]
        + in_place(len(kept) + len(others)),
        out_specs=[
            pl.BlockSpec((rows, TILE), lambda i: (part, i)),
            pl.BlockSpec((rows, depth), lambda i: (part, 0)),
        ],
        out_shape=[
            jax.ShapeDtypeStruct((2 * rows, width), jnp.bfloat16),
            jax.ShapeDtypeStruct((2 * rows, depth), jnp.bfloat16),
        ],
        scratch_shapes=[pltpu.SemaphoreType.DMA((count,))],
        input_output_aliases={count + 1 + k: k for k in range(len(kept))},
        compiler_params=pltpu.CompilerParams(vmem_limit_bytes=48 * 1024 * 1024),
        cost_estimate=pl.CostEstimate(
            flops=2 * rows * depth * width,
            bytes_accessed=2 * (2 * rows * depth + depth * width + rows * width),
            transcendentals=0,
        ),
    )(*pieces, down, *kept, *others)


def mlp_kernel(tiles, columns, joined, pieces, others, experts_ref, routed_ref, *refs):
    row_refs = refs[:pieces]
    router_ref, gate_col, up_col, down_grad, gate_row, up_row, down_row = refs[pieces : pieces + 7]
    outs = refs[pieces + 7 + others :]
    grad_refs, out_refs = outs[:pieces], outs[:pieces] if joined else outs[pieces : 2 * pieces]
    outs = outs[pieces if joined else 2 * pieces :]
    rows_out, hidden_out, gate_out, up_out, logit_out = outs[:5]
    hidden_all, gate_all, up_all, prob_ref, scale_ref, sum_ref, semaphores = outs[5:]
    step = pl.program_id(0)
    third = tiles // 2
    total = rows_out.shape[0]
    size = total // pieces
    lane = lax.broadcasted_iota(jnp.int32, (1, router_ref.shape[1]), 1) - experts_ref[3]

    @pl.when(step == 0)
    def _():
        load_pieces(row_refs, rows_out, semaphores)
        logits = wide_dot(rows_out[...], router_ref[...])
        logits = jnp.where((lane >= 0) & (lane < experts_ref[2]), logits, -1e30)
        raised = jnp.exp(logits - jnp.max(logits, axis=1, keepdims=True))
        chances = raised / jnp.sum(raised, axis=1, keepdims=True)
        prob_ref[...] = chances
        for k in (0, 1):
            chance = jnp.sum(jnp.where(lane == experts_ref[k], chances, 0.0), axis=1, keepdims=True)
            scale_ref[k] = routed_ref[:, k : k + 1] * chance
        scale_ref[2] = jnp.ones_like(scale_ref[2])
        sum_ref[...] = jnp.zeros_like(sum_ref)

    @pl.when(step < tiles)
    def _():
        columns_here = pl.ds(pl.multiple_of(step * TILE, TILE), TILE)
        kind = step // third
        half = total // 2
        for k in (0, 1):
            part = slice(k * half, (k + 1) * half)
            pre_gate = dot_turned(rows_out[part, :], gate_col[...])
            pre_up = dot_turned(rows_out[part, :], up_col[...])
            grads = down_grad[part, :].astype(jnp.float32)
            scale = scale_ref[kind, part, :]
            sigmoid = 1.0 / (1.0 + jnp.exp(-pre_gate))
            silu = pre_gate * sigmoid
            hidden = (silu * pre_up).astype(jnp.bfloat16).astype(jnp.float32)
            sum_ref[kind, part, :] += jnp.sum(hidden * grads, axis=1, keepdims=True)
            grad_hidden = scale * grads
            low_gate = (grad_hidden * pre_up * (sigmoid + silu * (1.0 - sigmoid))).astype(
                jnp.bfloat16
            )
            low_up = (grad_hidden * silu).astype(jnp.bfloat16)
            gate_all[part, columns_here] = low_gate
            up_all[part, columns_here] = low_up
            low_hidden = (scale * hidden).astype(jnp.bfloat16)
            hidden_all[part, columns_here] = low_hidden
            hidden_out[part, :] = low_hidden
            gate_out[part, :] = low_gate
            up_out[part, :] = low_up

    @pl.when(step == tiles - 1)
    def _():
        grad_logits = jnp.zeros_like(prob_ref)
        for k in (0, 1):
            own = jnp.where(lane == experts_ref[k], 1.0, 0.0)
            grad_logits += scale_ref[k] * sum_ref[k] * (own - prob_ref[...])
        logit_out[...] = grad_logits.astype(jnp.bfloat16)

    @pl.when((step >= tiles) & (step < tiles + columns))
    def _():
        some = pl.ds(pl.multiple_of((step - tiles) * 2 * TILE, TILE), 2 * TILE)
        grads = wide_dot(gate_all[...], gate_row[...]) + wide_dot(up_all[...], up_row[...])
        grads += dot_turned(logit_out[...], router_ref[some, :])
        grads = grads.astype(jnp.bfloat16)
        for k in range(pieces):
            grad_refs[k][...] = grads[k * size : (k + 1) * size]

    @pl.when(step >= tiles + columns)
    def _():
        result = wide_dot(hidden_all[...], down_row[...]).astype(jnp.bfloat16)
        for k in range(pieces):
            out_refs[k][...] = result[k * size : (k + 1) * size]


def mlp_plane(distance, joined, experts, routed, rows, down_grad, router, weights, kept, others):
    gate, up, down = weights
    pieces = len(rows)
    size, depth = rows[0].shape
    width = gate.shape[0]
    tiles, columns = width // TILE, depth // (2 * TILE)
    total = pieces * size
    low = jnp.bfloat16

    def early(i):
        return jnp.minimum(i, tiles - 1)

    def late(i):
        return jnp.clip(i - tiles, 0, columns - 1)

    def last(i):
        return jnp.maximum(i - tiles - columns, 0)

    tile_spec = pl.BlockSpec((total, TILE), lambda i: (distance, early(i)))
    weight_tile = pl.BlockSpec((TILE, depth), lambda i: (early(i), 0))
    if joined:
        result_specs = [
            pl.BlockSpec((size, 2 * TILE), lambda i: (0, jnp.maximum(i - tiles, 0)))
        ] * pieces
        result_shapes = [jax.ShapeDtypeStruct((size, 2 * depth), low)] * pieces
    else:
        result_specs = [pl.BlockSpec((size, 2 * TILE), lambda i: (0, late(i)))] * pieces + [
            pl.BlockSpec((size, 2 * TILE), lambda i: (0, last(i)))
        ] * pieces
        result_shapes = [jax.ShapeDtypeStruct((size, depth), low)] * (2 * pieces)
    first_kept = 2 + pieces + 7
    results = pl.pallas_call(
        functools.partial(
            mlp_kernel, tiles, columns, joined, pieces, len(kept) + len(others)
        ),
        grid=(tiles + 2 * columns,),
        in_specs=[pl.BlockSpec(memory_space=pltpu.SMEM), whole(routed)]
        + in_place(pieces)
        + [
            pl.BlockSpec((depth, 128), lambda i: (0, router.shape[1] // 128 - 1)),
            weight_tile,
            weight_tile,
            tile_spec,
            pl.BlockSpec((width, 2 * TILE), lambda i: (0, late(i))),
            pl.BlockSpec((width, 2 * TILE), lambda i: (0, late(i))),
            pl.BlockSpec((width, 2 * TILE), lambda i: (0, last(i))),
        ]
        + in_place(len(kept) + len(others)),
        out_specs=result_specs
        + [
            pl.BlockSpec((total, depth), lambda i: (distance, 0)),
            tile_spec,
            tile_spec,
            tile_spec,
            pl.BlockSpec((total, 128), lambda i: (distance, 0)),
        ],
        out_shape=result_shapes
        + [
            jax.ShapeDtypeStruct((RINGS * total, many), low)
            for many in (depth, width, width, width, 128)
        ],
        scratch_shapes=[pltpu.VMEM((total, width), low)] * 3
        + [
            pltpu.VMEM((total, 128), jnp.float32),
            pltpu.VMEM((3, total, 1), jnp.float32),
            pltpu.VMEM((3, total, 1), jnp.float32),
            pltpu.SemaphoreType.DMA((pieces,)),
        ],
        input_output_aliases={
            first_kept + k: len(result_shapes) + k for k in range(len(kept))
        },
        compiler_params=pltpu.CompilerParams(vmem_limit_bytes=56 * 1024 * 1024),
        cost_estimate=pl.CostEstimate(
            flops=2 * total * depth * width * 5,
            bytes_accessed=2 * (5 * depth * width + 4 * total * depth + 4 * total * width),
            transcendentals=total * width,
        ),
    )(experts, routed, *rows, router, gate, up, down_grad, gate, up, down, *kept, *others)
    count = len(result_shapes)
    return results[:pieces], results[pieces:count], results[count:]


def gather_body(
    block_input,
    segments,
    counts,
    routes,
    attn_gain,
    w_query,
    w_latent,
    latent_gain,
    w_keyval,
    w_output,
    ffn_gain,
    w_router,
    shared_gate_up,
    shared_down,
    expert_gate_up,
    expert_down,
    cotangent,
):
    f32 = jnp.float32
    bf16 = jnp.bfloat16
    blocks = 16
    index = lax.axis_index("dp")
    x = lax.axis_index("tensor")
    coords = jnp.stack([index // 4, (index // 2) % 2, index % 2]).astype(jnp.int32)
    core = coords[2]
    place = jnp.concatenate([coords, x.astype(jnp.int32)[None], counts])
    local_rows = block_input.shape[0]
    tokens = 2 * local_rows
    depth = w_query.shape[0]
    query_width = w_query.shape[1]
    heads = query_width // (NOPE + ROPE)
    experts = w_router.shape[1]
    units = expert_gate_up.shape[3]
    shared = shared_gate_up.shape[2] // blocks
    latent_depth = w_keyval.shape[0]

    used = query_width + KVR + ROPE
    small = jnp.concatenate(
        [
            attn_gain[:, None],
            ffn_gain[:, None],
            jnp.pad(latent_gain, (0, depth - latent_depth))[:, None],
            w_router,
            routes.reshape(depth, -1).astype(bf16),
            jnp.zeros((depth, 128 - ROPE - 3 - experts - 2 * TOP), bf16),
        ],
        axis=1,
    )
    first_width = query_width + KVR + 128
    shards = pack_weights(w_query, w_latent, small, w_keyval, w_output)
    held = ring_shards(shards)
    other_input = other_x(block_input)
    expert_in = expert_gate_up.swapaxes(2, 3)
    expert_in_other = other_core(expert_in)
    expert_down_other = other_core(expert_down)
    chunks = gather_weight(held)
    grad_planes = gather_rows(after(cotangent, held[3]), "xyxy")

    shared_near = lax.all_to_all(
        pack_shared(shared_gate_up, shared_down, blocks, (held[3],)),
        "dp",
        split_axis=0,
        concat_axis=0,
        tiled=True,
    )
    shared_far = other_core(shared_near)

    cosine, sine = rotary_tables(segments[0], ROPE)
    cosine = jnp.tile(cosine, (1, heads))
    sine = jnp.tile(sine, (1, heads))
    sizes = (depth, query_width, used, latent_depth, w_keyval.shape[1] * latent_depth // depth, first_width)
    (
        own_part,
        sent_part,
        first_weight,
        keyval_weight,
        output_turned,
        first_normed,
        nope,
        turned_query,
        latent,
        key,
        keyval,
        total,
        attended,
        gains,
        latent_gain_row,
    ) = attend_forward(
        place,
        segments,
        cosine,
        sine,
        block_input,
        other_input,
        chunks,
        heads,
        sizes,
        (grad_planes[2][0], grad_planes[0][1], grad_planes[0][2], grad_planes[1][2], shared_near),
    )
    attn_gain_wide, ffn_gain_wide = gains[0], gains[1]
    mixed = block_input.astype(f32) + own_part + other_x(sent_part).astype(f32)
    second_scale = rms_scale(mixed)
    second_unit = mixed * second_scale
    second_normed = (second_unit * ffn_gain_wide).astype(bf16)

    routes_at = used + 3 + experts
    routes_all = first_weight[:, routes_at : routes_at + 2 * TOP].reshape(blocks * tokens, TOP)
    chip_experts = jnp.stack([index, index + 1 - 2 * core]).astype(jnp.int32)
    routed_all = jnp.any(
        routes_all[None] == chip_experts[:, None, None].astype(bf16), axis=2
    ).astype(f32)
    order = jnp.stack(
        [
            place_of(coords, (distance, flip_y, 0)) * 2 + (1 - x if flip_x else x)
            for distance in range(RINGS)
            for flip_x, flip_y in ((0, 0), (0, 1), (1, 0), (1, 1))
        ]
    )
    routed = jnp.stack(
        [
            pick_blocks(one.reshape(blocks * 2, local_rows), order).reshape(RINGS, -1)
            for one in routed_all
        ],
        axis=2,
    )

    corners = "yxyx"
    row_planes = gather_rows(second_normed, corners)
    gate_weight, up_weight, down_weight = pack_units(
        expert_in,
        expert_in_other,
        expert_down,
        expert_down_other,
        shared_near,
        shared_far,
        shared,
        (second_normed,),
    )
    half_kept = down_grads(
        0,
        [piece for plane in grad_planes[:2] for piece in plane],
        down_weight,
        (),
        (row_planes[1][0], row_planes[0][1], row_planes[0][2]),
    )
    down_grad, every_grad = down_grads(
        1,
        [piece for plane in grad_planes[2:] for piece in plane],
        down_weight,
        half_kept,
        (row_planes[2][0], row_planes[0][3]),
    )
    expert_ids = jnp.concatenate(
        [chip_experts, jnp.array([experts, used + 3 - query_width - KVR], jnp.int32)]
    )
    kept = []
    turned, closed = [], []
    for distance in range(RINGS):
        others = [row_planes[3][0]] if distance == 0 else []
        if distance == 2:
            others = list(turned[0][1:])
        elif distance == 3:
            others = list(turned[1][1:]) + list(closed[0][1:])
        grads, outs, kept = mlp_plane(
            distance,
            distance < RINGS - 1,
            expert_ids,
            routed[distance],
            row_planes[distance],
            down_grad,
            first_weight,
            (gate_weight, up_weight, down_weight),
            kept,
            others,
        )
        turned.append(turn_corner(grads, corners[distance]))
        if distance < RINGS - 1:
            closed.append(close_plane(turned[distance]))
    every_row, every_hidden, every_gate_grad, every_up_grad, logit_grads = kept
    shared_kept, shared_sent, logit_rows = side_grads(
        every_row,
        every_grad,
        every_gate_grad,
        every_up_grad,
        every_hidden,
        logit_grads,
        shared,
        blocks,
    )
    sent_down = expert_grads((every_hidden,), every_grad, units, 1, None, bf16)
    moving = ring_step(wide_sum(*closed[1]).astype(bf16))
    moving = ring_step(wide_sum(moving, *closed[2]).astype(bf16))
    own, beside, across = turned[3]
    grad_close = close_plane((own, after(beside, shared_sent), across))
    grad_second = wide_sum(
        ring_step(
            after(wide_sum(moving[:, :D], *grad_close).astype(bf16), sent_down)
        ),
        *[part[:, :D] for part in closed[0]],
    )
    outs = list(outs)
    outs[3] = after(outs[3], grad_close[1])
    out_close = close_plane(turn_corner(outs, corners[3]))
    block_output = mixed + wide_sum(
        ring_step(wide_sum(moving[:, D:], *out_close).astype(bf16)),
        *[part[:, D:] for part in closed[0]],
    )

    arrived_down = other_core(sent_down)
    router_at = used + 3 - query_width - KVR
    grad_router = logit_rows[router_at : router_at + experts]
    grad_shared_in, grad_shared_down = unpack_shared(
        lax.all_to_all(
            add_low(shared_kept, other_core(shared_sent)),
            "dp",
            split_axis=0,
            concat_axis=0,
            tiled=True,
        ),
        shared,
    )

    gain_ffn_part = jnp.sum(grad_second * second_unit, axis=0)
    grad_mixed = cotangent.astype(f32) + rms_back(
        grad_second * ffn_gain_wide, second_unit, second_scale
    )
    grad_mixed_low = grad_mixed.astype(bf16)
    other_grad = other_x(grad_mixed_low)

    places = jnp.stack([place_of(coords, key_of) for key_of in weight_keys()]).astype(jnp.int32)
    projected_grad, keyval_grad, latent_normed, gain_latent_part = attend_back(
        place,
        segments,
        cosine,
        sine,
        grad_mixed_low,
        other_grad,
        (keyval_weight, output_turned, nope, turned_query, latent, key, keyval, total, latent_gain_row),
        heads,
        first_width,
    )
    grad_attn = jnp.concatenate(
        [
            jnp.where(x == 0, grad_mixed_low, other_grad),
            jnp.where(x == 0, other_grad, grad_mixed_low),
        ],
        axis=0,
    )
    cut = (query_width + KVR) // TILE * TILE - TILE
    arrived = [other_core(block_grads(first_normed, projected_grad, cut, places, 8, 8))]
    own_first, sent_first, gain_attn_part = first_back(
        place, block_input, other_input, projected_grad, first_weight
    )
    grad_first = own_first + other_x(sent_first).astype(f32)
    small_rows = jnp.concatenate(
        [
            jnp.zeros((ROPE, D), f32),
            gain_attn_part,
            gain_ffn_part[None],
            jnp.pad(
                gain_latent_part.reshape(blocks, latent_depth),
                ((0, 0), (0, depth - latent_depth)),
            ).reshape(1, D),
            grad_router,
            jnp.zeros((128 - ROPE - 3 - experts, D), f32),
        ],
        axis=0,
    )
    mixed_parts = (
        first_normed,
        projected_grad[:, cut:],
        small_rows,
        latent_normed,
        keyval_grad,
        grad_attn,
        attended,
        places,
    )
    arrived.append(other_core(mixed_grads(*mixed_parts, 8, 8)))
    far = [
        block_grads(first_normed, projected_grad, cut, places, 4, 4, arrived[0]),
        mixed_grads(*mixed_parts, 4, 4, arrived[1]),
    ]
    from_y = [other_y(part) for part in far]
    arrived_in = other_core(
        expert_grads((every_gate_grad, every_up_grad), every_row, units, 1, None, bf16, (far[1],))
    )
    near = [
        block_grads(first_normed, projected_grad, cut, places, 0, 4, arrived[0]),
        mixed_grads(*mixed_parts, 0, 4, arrived[1]),
    ]
    grad_expert_down = expert_grads(
        (every_hidden,), every_grad, units, 0, arrived_down, f32, (near[1],)
    )
    first_closed = close_ring(near[0], from_y[0])
    grad_expert_in = expert_grads(
        (every_gate_grad, every_up_grad), every_row, units, 0, arrived_in, f32
    )
    second_closed = close_ring(after(near[1], grad_expert_in), from_y[1])
    grad_expert_gate_up = grad_expert_in.swapaxes(2, 3)
    grad_expert_down = grad_expert_down[0]
    nope_width = heads * NOPE
    span = heads * (ROPE // 2)
    grad_query_weight = jnp.concatenate(
        [
            first_closed[:, :nope_width].reshape(depth, heads, NOPE),
            first_closed[:, nope_width : nope_width + span].reshape(depth, heads, -1),
            first_closed[:, nope_width + span : query_width].reshape(depth, heads, -1),
        ],
        axis=2,
    ).reshape(depth, query_width)
    at = first_width - cut
    both = jnp.concatenate([first_closed[:, query_width:], second_closed[:, :at]], axis=1)
    both = both + other_x(both)
    grad_latent_weight = both[:, : KVR + ROPE]
    small_grads = both[:, KVR + ROPE :].T
    keyval_columns = w_keyval.shape[1] * latent_depth // depth
    grad_keyval_weight = (
        second_closed[:, at : at + keyval_columns]
        .reshape(-1, latent_depth, keyval_columns)
        .transpose(1, 0, 2)
        .reshape(latent_depth, -1)
    )
    grad_output_weight = second_closed[:, at + keyval_columns :].T
    own_inputs = block_input.astype(f32)
    own_scale = rms_scale(own_inputs)
    own_unit = own_inputs * own_scale
    grad_input = grad_mixed + rms_back(grad_first * attn_gain_wide, own_unit, own_scale)
    return (
        block_output,
        grad_input,
        small_grads[0],
        grad_query_weight,
        grad_latent_weight,
        small_grads[2, :latent_depth],
        grad_keyval_weight,
        grad_output_weight,
        small_grads[1],
        small_grads[3 : 3 + experts].T,
        grad_shared_in,
        grad_shared_down,
        grad_expert_gate_up,
        grad_expert_down,
    )


def solution(mesh):
    in_specs = (
        P(("dp", "tensor"), None),
        P("dp", None),
        P("dp"),
        P("dp", None),
        P("dp"),
        P("dp", "tensor"),
        P("dp", None),
        P("dp"),
        P("dp", "tensor"),
        P("tensor", "dp"),
        P("dp"),
        P("dp", None),
        P(None, "dp", "tensor"),
        P("tensor", "dp"),
        P("dp", None, None, "tensor"),
        P("dp", "tensor", None),
        P(("dp", "tensor"), None),
    )
    out_specs = (
        P(("dp", "tensor"), None),
        P(("dp", "tensor"), None),
        P("dp"),
        P("dp", "tensor"),
        P("dp", None),
        P("dp"),
        P("dp", "tensor"),
        P("tensor", "dp"),
        P("dp"),
        P("dp", None),
        P(None, "dp", "tensor"),
        P("tensor", "dp"),
        P("dp", None, None, "tensor"),
        P("dp", "tensor", None),
    )
    body = gather_body if mesh.shape["dp"] == 16 else exchange_body
    return jax.shard_map(body, mesh=mesh, in_specs=in_specs, out_specs=out_specs, check_vma=False)
```

```python
import functools
import math

import jax
import jax.numpy as jnp
from jax import lax
from jax.experimental import pallas as pl
from jax.experimental.pallas import tpu as pltpu
from jax.sharding import PartitionSpec as P

D = 2048
NOPE = 128
ROPE = 64
VD = 128
KVR = 512
TOP = 6


EPSILON = 1e-06


def rms_scale(values):
    return lax.rsqrt(jnp.mean(values * values, axis=-1, keepdims=True) + EPSILON)


def rms_back(grad_unit, unit_rows, row_scale):
    return row_scale * (
        grad_unit - unit_rows * jnp.mean(grad_unit * unit_rows, axis=-1, keepdims=True)
    )


def rotary_tables(segment_row, width):
    count = segment_row.shape[0]
    position = jnp.arange(count, dtype=jnp.int32)
    same = segment_row[:, None] == segment_row[None, :]
    start = jnp.min(jnp.where(same, position[None, :], count), axis=1)
    offset = (position - start).astype(jnp.float32)
    freq = jnp.exp(jnp.arange(width // 2, dtype=jnp.float32) * (-2.0 * math.log(10000.0) / width))
    angle = offset[:, None] * freq[None, :]
    return (jnp.cos(angle), jnp.sin(angle))


def rotate(values, cosine, sine):
    half = values.shape[-1] // 2
    first = values[..., :half]
    second = values[..., half:]
    return jnp.concatenate(
        [first * cosine - second * sine, second * cosine + first * sine], axis=-1
    )


def rotate_back(grads, cosine, sine):
    half = grads.shape[-1] // 2
    first = grads[..., :half]
    second = grads[..., half:]
    return jnp.concatenate(
        [first * cosine + second * sine, second * cosine - first * sine], axis=-1
    )


def allowed_pairs(segment_row, count):
    position = jnp.arange(segment_row.shape[0], dtype=jnp.int32)
    live = position < count
    same = segment_row[:, None] == segment_row[None, :]
    causal = position[None, :] <= position[:, None]
    return same & causal & live[:, None] & live[None, :] | (position[:, None] == position[None, :])


def attention_scores(query_rows, key_nope, key_rope, allowed, scale):
    scores = jnp.einsum(
        "ihd,jhd->hij", query_rows[..., :NOPE], key_nope, preferred_element_type=jnp.float32
    )
    scores = scores + jnp.einsum(
        "ihd,jd->hij", query_rows[..., NOPE:], key_rope, preferred_element_type=jnp.float32
    )
    return jnp.where(allowed[None], scores * scale, -1e30)


def swiglu_back(gate, upper, grad_hidden, axis):
    sigmoid = jax.nn.sigmoid(gate)
    grad_gate = grad_hidden * upper * sigmoid * (1.0 + gate * (1.0 - sigmoid))
    grad_upper = grad_hidden * gate * sigmoid
    return jnp.stack([grad_gate, grad_upper], axis=axis)


def slot_layout(routes, experts, capacity):
    tokens = routes.shape[0]
    flat = routes.reshape(-1)
    onehot = (flat[:, None] == jnp.arange(experts, dtype=jnp.int32)[None, :]).astype(jnp.int32)
    rank = jnp.arange(flat.shape[0], dtype=jnp.int32)
    earlier = (rank[None, :] < rank[:, None]).astype(jnp.bfloat16)
    before = jnp.dot(
        earlier, onehot.astype(jnp.bfloat16), preferred_element_type=jnp.float32
    ).astype(jnp.int32)
    slot_index = jnp.sum(before * onehot, axis=1)
    target = flat * capacity + slot_index
    token_ids = jnp.arange(flat.shape[0], dtype=jnp.int32) // routes.shape[1]
    owner = jnp.full((experts * capacity,), tokens, jnp.int32).at[target].set(token_ids)
    return (slot_index, target, owner)


def to_expert_major(arrived, groups, local_experts):
    capacity = arrived.shape[1]
    width = arrived.shape[2]
    return (
        arrived.reshape(groups, local_experts, capacity, width)
        .transpose(1, 0, 2, 3)
        .reshape(local_experts, groups * capacity, width)
    )


def from_expert_major(results, groups):
    local_experts = results.shape[0]
    width = results.shape[2]
    capacity = results.shape[1] // groups
    return (
        results.reshape(local_experts, groups, capacity, width)
        .transpose(1, 0, 2, 3)
        .reshape(groups * local_experts, capacity, width)
    )


def exchange_body(
    block_input,
    segments,
    counts,
    routes,
    attn_gain,
    w_query,
    w_latent,
    latent_gain,
    w_keyval,
    w_output,
    ffn_gain,
    w_router,
    shared_gate_up,
    shared_down,
    expert_gate_up,
    expert_down,
    cotangent,
):
    gathered = (
        lax.all_gather(attn_gain, "dp", axis=0, tiled=True),
        lax.all_gather(w_query, "dp", axis=0, tiled=True),
        lax.all_gather(w_latent, "dp", axis=0, tiled=True),
        lax.all_gather(latent_gain, "dp", axis=0, tiled=True),
        lax.all_gather(w_keyval, "dp", axis=0, tiled=True),
        lax.all_gather(w_output, "dp", axis=1, tiled=True),
        lax.all_gather(ffn_gain, "dp", axis=0, tiled=True),
        lax.all_gather(w_router, "dp", axis=0, tiled=True),
        lax.all_gather(shared_gate_up, "dp", axis=1, tiled=True),
        lax.all_gather(shared_down, "dp", axis=1, tiled=True),
    )
    (
        full_attn_gain,
        query_weight,
        latent_weight,
        full_latent_gain,
        keyval_weight,
        output_weight,
        full_ffn_gain,
        router_weight,
        shared_in,
        shared_out,
    ) = gathered
    tensor_rank = lax.axis_index("tensor")
    dp_size = lax.axis_size("dp")
    rows_all = lax.all_gather(block_input, "tensor", axis=0, tiled=True)
    tokens = rows_all.shape[0]
    local_rows = block_input.shape[0]
    heads = query_weight.shape[1] // (NOPE + ROPE)
    experts = router_weight.shape[1]
    local_experts = expert_gate_up.shape[0]
    capacity = 2 * tokens * TOP // experts
    scale = (NOPE + ROPE) ** (-0.5)
    start = tensor_rank * local_rows
    cosine, sine = rotary_tables(segments[0], ROPE)
    allowed = allowed_pairs(segments[0], counts[0])
    attn_gain_wide = full_attn_gain.astype(jnp.float32)
    latent_gain_wide = full_latent_gain.astype(jnp.float32)
    ffn_gain_wide = full_ffn_gain.astype(jnp.float32)
    inputs = rows_all.astype(jnp.float32)
    first_scale = rms_scale(inputs)
    first_unit = inputs * first_scale
    first_normed = (first_unit * attn_gain_wide).astype(jnp.bfloat16)
    query = jnp.dot(first_normed, query_weight, preferred_element_type=jnp.float32).reshape(
        tokens, heads, NOPE + ROPE
    )
    query_rows = jnp.concatenate(
        [query[..., :NOPE], rotate(query[..., NOPE:], cosine[:, None, :], sine[:, None, :])],
        axis=-1,
    ).astype(jnp.bfloat16)
    latent_all = jnp.dot(first_normed, latent_weight, preferred_element_type=jnp.float32)
    latent = latent_all[:, :KVR]
    key_rope = rotate(latent_all[:, KVR:], cosine, sine).astype(jnp.bfloat16)
    latent_scale = rms_scale(latent)
    latent_unit = latent * latent_scale
    latent_normed = (latent_unit * latent_gain_wide).astype(jnp.bfloat16)
    keyval = (
        jnp.dot(latent_normed, keyval_weight, preferred_element_type=jnp.float32)
        .astype(jnp.bfloat16)
        .reshape(tokens, heads, NOPE + VD)
    )
    key_nope = keyval[..., :NOPE]
    values = keyval[..., NOPE:]
    scores = attention_scores(query_rows, key_nope, key_rope, allowed, scale)
    row_max = jnp.max(scores, axis=-1, keepdims=True)
    log_total = row_max + jnp.log(jnp.sum(jnp.exp(scores - row_max), axis=-1, keepdims=True))
    weights_low = jnp.exp(scores - log_total).astype(jnp.bfloat16)
    attended = (
        jnp.einsum("hij,jhd->ihd", weights_low, values, preferred_element_type=jnp.float32)
        .astype(jnp.bfloat16)
        .reshape(tokens, heads * VD)
    )
    attn_part = jnp.dot(attended, output_weight, preferred_element_type=jnp.float32)
    mixed = inputs + lax.psum(attn_part, "tensor")
    second_scale = rms_scale(mixed)
    second_unit = mixed * second_scale
    second_normed = (second_unit * ffn_gain_wide).astype(jnp.bfloat16)
    logits = jnp.dot(second_normed, router_weight, preferred_element_type=jnp.float32)
    probabilities = jax.nn.softmax(logits, axis=-1)
    gate_values = jnp.take_along_axis(probabilities, routes, axis=1)
    shared_pre = jnp.einsum(
        "td,gdf->tgf", second_normed, shared_in, preferred_element_type=jnp.float32
    )
    shared_hidden = (jax.nn.silu(shared_pre[:, 0]) * shared_pre[:, 1]).astype(jnp.bfloat16)
    shared_part = jnp.dot(shared_hidden, shared_out, preferred_element_type=jnp.float32)
    slot_index, target, owner = slot_layout(routes, experts, capacity)
    owner_grid = owner.reshape(experts, capacity)
    padded_rows = jnp.concatenate([second_normed, jnp.zeros((1, D), jnp.bfloat16)], axis=0)
    outgoing = padded_rows[owner_grid]
    arrived = lax.all_to_all(outgoing, "dp", split_axis=0, concat_axis=0, tiled=True)
    expert_rows = to_expert_major(arrived, dp_size, local_experts)
    expert_pre = jnp.einsum(
        "erd,egdf->ergf", expert_rows, expert_gate_up, preferred_element_type=jnp.float32
    )
    expert_hidden = (jax.nn.silu(expert_pre[:, :, 0]) * expert_pre[:, :, 1]).astype(jnp.bfloat16)
    expert_result = jnp.einsum(
        "erf,efd->erd", expert_hidden, expert_down, preferred_element_type=jnp.float32
    )
    returning = from_expert_major(expert_result, dp_size)
    returned = lax.all_to_all(
        returning.astype(jnp.bfloat16), "dp", split_axis=0, concat_axis=0, tiled=True
    ).astype(returning.dtype)
    padded_back = jnp.concatenate([returned.reshape(-1, D), jnp.zeros((1, D), jnp.float32)], axis=0)
    picked = padded_back[target].reshape(tokens, TOP, D)
    routed_part = jnp.sum(gate_values[:, :, None] * picked, axis=1)
    branch_sum = lax.psum_scatter(
        (shared_part + routed_part).astype(jnp.bfloat16), "tensor", scatter_dimension=0, tiled=True
    ).astype(jnp.float32)
    block_output = lax.dynamic_slice_in_dim(mixed, start, local_rows, 0) + branch_sum
    grad_rows = lax.all_gather(cotangent, "tensor", axis=0, tiled=True)
    grad_out = grad_rows.astype(jnp.float32)
    grad_shared_hidden = jnp.dot(grad_rows, shared_out.T, preferred_element_type=jnp.float32)
    grad_shared_out = jnp.dot(shared_hidden.T, grad_rows, preferred_element_type=jnp.float32)
    grad_shared_pre = swiglu_back(shared_pre[:, 0], shared_pre[:, 1], grad_shared_hidden, 1).astype(
        jnp.bfloat16
    )
    grad_shared_in = jnp.einsum(
        "td,tgf->gdf", second_normed, grad_shared_pre, preferred_element_type=jnp.float32
    )
    grad_second = jnp.einsum(
        "tgf,gdf->td", grad_shared_pre, shared_in, preferred_element_type=jnp.float32
    )
    gate_by_slot = (
        jnp.zeros((experts * capacity + 1,), jnp.float32).at[target].set(gate_values.reshape(-1))
    )
    slot_ids = jnp.arange(experts * capacity, dtype=jnp.int32).reshape(experts, capacity)
    padded_grad = jnp.concatenate([grad_out, jnp.zeros((1, D), jnp.float32)], axis=0)
    grad_outgoing = (gate_by_slot[slot_ids][..., None] * padded_grad[owner_grid]).astype(
        jnp.bfloat16
    )
    grad_arrived = lax.all_to_all(grad_outgoing, "dp", split_axis=0, concat_axis=0, tiled=True)
    grad_expert_rows = to_expert_major(grad_arrived, dp_size, local_experts)
    grad_expert_hidden = jnp.einsum(
        "erd,efd->erf", grad_expert_rows, expert_down, preferred_element_type=jnp.float32
    )
    grad_expert_down = jnp.einsum(
        "erf,erd->efd", expert_hidden, grad_expert_rows, preferred_element_type=jnp.float32
    )
    grad_expert_pre = swiglu_back(
        expert_pre[:, :, 0], expert_pre[:, :, 1], grad_expert_hidden, 2
    ).astype(jnp.bfloat16)
    grad_expert_gate_up = jnp.einsum(
        "erd,ergf->egdf", expert_rows, grad_expert_pre, preferred_element_type=jnp.float32
    )
    grad_expert_input = jnp.einsum(
        "ergf,egdf->erd", grad_expert_pre, expert_gate_up, preferred_element_type=jnp.float32
    )
    grad_returning = from_expert_major(grad_expert_input, dp_size)
    grad_returned = lax.all_to_all(
        grad_returning.astype(jnp.bfloat16), "dp", split_axis=0, concat_axis=0, tiled=True
    ).astype(grad_returning.dtype)
    padded_grad_back = jnp.concatenate(
        [grad_returned.reshape(-1, D), jnp.zeros((1, D), jnp.float32)], axis=0
    )
    grad_second = grad_second + jnp.sum(padded_grad_back[target].reshape(tokens, TOP, D), axis=1)
    grad_gates = jnp.sum(grad_out[:, None, :] * picked, axis=-1)
    grad_second, grad_gates = (
        lax.psum(grad_second.astype(jnp.bfloat16), "tensor").astype(jnp.float32),
        lax.psum(grad_gates.astype(jnp.bfloat16), "tensor").astype(jnp.float32),
    )
    chosen = (routes[:, :, None] == jnp.arange(experts, dtype=jnp.int32)[None, None, :]).astype(
        jnp.float32
    )
    grad_probabilities = jnp.sum(chosen * grad_gates[:, :, None], axis=1)
    grad_logits = probabilities * (
        grad_probabilities - jnp.sum(probabilities * grad_probabilities, axis=-1, keepdims=True)
    )
    grad_logits_low = grad_logits.astype(jnp.bfloat16)
    grad_router = jnp.dot(second_normed.T, grad_logits_low, preferred_element_type=jnp.float32)
    grad_second = grad_second + jnp.dot(
        grad_logits_low, router_weight.T, preferred_element_type=jnp.float32
    )
    gain_ffn_grad = jnp.sum(grad_second * second_unit, axis=0)
    grad_mixed = grad_out + rms_back(grad_second * ffn_gain_wide, second_unit, second_scale)
    grad_attn_low = grad_mixed.astype(jnp.bfloat16)
    grad_output_weight = jnp.dot(attended.T, grad_attn_low, preferred_element_type=jnp.float32)
    grad_attended = (
        jnp.dot(grad_attn_low, output_weight.T, preferred_element_type=jnp.float32)
        .astype(jnp.bfloat16)
        .reshape(tokens, heads, VD)
    )
    scores = attention_scores(query_rows, key_nope, key_rope, allowed, scale)
    weights = jnp.exp(scores - log_total)
    weights_low = weights.astype(jnp.bfloat16)
    grad_weights = jnp.einsum(
        "ihd,jhd->hij", grad_attended, values, preferred_element_type=jnp.float32
    )
    grad_values = jnp.einsum(
        "hij,ihd->jhd", weights_low, grad_attended, preferred_element_type=jnp.float32
    )
    grad_scores = (
        weights * (grad_weights - jnp.sum(weights * grad_weights, axis=-1, keepdims=True))
    ).astype(jnp.bfloat16)
    grad_query_nope = (
        jnp.einsum("hij,jhd->ihd", grad_scores, key_nope, preferred_element_type=jnp.float32)
        * scale
    )
    grad_query_rope = (
        jnp.einsum("hij,jd->ihd", grad_scores, key_rope, preferred_element_type=jnp.float32) * scale
    )
    grad_key_nope = (
        jnp.einsum(
            "hij,ihd->jhd", grad_scores, query_rows[..., :NOPE], preferred_element_type=jnp.float32
        )
        * scale
    )
    grad_key_rope = (
        jnp.einsum(
            "hij,ihd->jd", grad_scores, query_rows[..., NOPE:], preferred_element_type=jnp.float32
        )
        * scale
    )
    grad_query = (
        jnp.concatenate(
            [grad_query_nope, rotate_back(grad_query_rope, cosine[:, None, :], sine[:, None, :])],
            axis=-1,
        )
        .astype(jnp.bfloat16)
        .reshape(tokens, heads * (NOPE + ROPE))
    )
    grad_query_weight = jnp.dot(first_normed.T, grad_query, preferred_element_type=jnp.float32)
    grad_first = jnp.dot(grad_query, query_weight.T, preferred_element_type=jnp.float32)
    grad_keyval = (
        jnp.concatenate([grad_key_nope, grad_values], axis=-1)
        .astype(jnp.bfloat16)
        .reshape(tokens, heads * (NOPE + VD))
    )
    grad_keyval_weight = jnp.dot(latent_normed.T, grad_keyval, preferred_element_type=jnp.float32)
    grad_latent_normed = jnp.dot(grad_keyval, keyval_weight.T, preferred_element_type=jnp.float32)
    gain_latent_part = jnp.sum(grad_latent_normed * latent_unit, axis=0)
    grad_latent = rms_back(grad_latent_normed * latent_gain_wide, latent_unit, latent_scale)
    grad_latent_all = jnp.concatenate(
        [grad_latent, rotate_back(grad_key_rope, cosine, sine)], axis=-1
    )
    grad_first, grad_latent_all, gain_latent_grad = (
        lax.psum(grad_first.astype(jnp.bfloat16), "tensor").astype(jnp.float32),
        lax.psum(grad_latent_all.astype(jnp.bfloat16), "tensor").astype(jnp.float32),
        lax.psum(gain_latent_part.astype(jnp.bfloat16), "tensor").astype(jnp.float32),
    )
    grad_latent_low = grad_latent_all.astype(jnp.bfloat16)
    grad_latent_weight = jnp.dot(
        first_normed.T, grad_latent_low, preferred_element_type=jnp.float32
    )
    grad_first = grad_first + jnp.dot(
        grad_latent_low, latent_weight.T, preferred_element_type=jnp.float32
    )
    gain_attn_grad = jnp.sum(grad_first * first_unit, axis=0)
    grad_inputs = grad_mixed + rms_back(grad_first * attn_gain_wide, first_unit, first_scale)
    grad_local = lax.dynamic_slice_in_dim(grad_inputs, start, local_rows, 0)
    summed = (
        lax.psum_scatter(gain_attn_grad, "dp", scatter_dimension=0, tiled=True),
        lax.psum_scatter(grad_query_weight, "dp", scatter_dimension=0, tiled=True),
        lax.psum_scatter(grad_latent_weight, "dp", scatter_dimension=0, tiled=True),
        lax.psum_scatter(gain_latent_grad, "dp", scatter_dimension=0, tiled=True),
        lax.psum_scatter(grad_keyval_weight, "dp", scatter_dimension=0, tiled=True),
        lax.psum_scatter(grad_output_weight, "dp", scatter_dimension=1, tiled=True),
        lax.psum_scatter(gain_ffn_grad, "dp", scatter_dimension=0, tiled=True),
        lax.psum_scatter(grad_router, "dp", scatter_dimension=0, tiled=True),
        lax.psum_scatter(grad_shared_in, "dp", scatter_dimension=1, tiled=True),
        lax.psum_scatter(grad_shared_out, "dp", scatter_dimension=1, tiled=True),
    )
    return (
        block_output,
        grad_local,
        summed[0],
        summed[1],
        summed[2],
        summed[3],
        summed[4],
        summed[5],
        summed[6],
        summed[7],
        summed[8],
        summed[9],
        grad_expert_gate_up,
        grad_expert_down,
    )


RINGS = 4


def ring_step(values):
    return lax.ppermute(values, "dp", [(i, (i + RINGS) % 16) for i in range(16)])


def other_y(values):
    return lax.ppermute(values, "dp", [(i, i ^ 2) for i in range(16)])


def other_core(values):
    return lax.ppermute(values, "dp", [(i, i ^ 1) for i in range(16)])


def other_x(values):
    return lax.ppermute(values, "tensor", [(0, 1), (1, 0)])


def fence_kernel(*refs):
    pass


def after(values, *others):
    anywhere = pl.BlockSpec(memory_space=pl.ANY)
    return pl.pallas_call(
        fence_kernel,
        out_shape=jax.ShapeDtypeStruct(values.shape, values.dtype),
        in_specs=[anywhere] * (1 + len(others)),
        out_specs=anywhere,
        input_output_aliases={0: 0},
    )(values, *others)


def gather_rows(rows, corners, eager=False):
    planes = []
    current = rows
    for distance in range(RINGS):
        if distance > 1 and eager:
            current = after(current, *planes[distance - 2][1:3])
        if distance:
            current = ring_step(current)
        beside = other_y(current)
        across = other_x(current)
        corner = other_x(beside) if corners[distance] == "x" else other_y(across)
        planes.append((current, beside, across, corner))
    return planes


def add_low(first, second):
    return (first.astype(jnp.float32) + second.astype(jnp.float32)).astype(jnp.bfloat16)


def turn_corner(plane, direction):
    own, beside, across, corner = plane
    if direction == "x":
        return own, add_low(beside, other_x(corner)), across
    return own, beside, add_low(across, other_y(corner))


def close_plane(turned):
    own, beside, across = turned
    return own, other_y(beside), other_x(across)


def wide_sum(*values):
    total = values[0].astype(jnp.float32)
    for value in values[1:]:
        total = total + value.astype(jnp.float32)
    return total


def ring_sum(parts, low):
    moving = parts[1]
    for distance in (2, 3, 0):
        moving = ring_step(moving.astype(low)).astype(jnp.float32) + parts[distance].astype(
            jnp.float32
        )
    return moving


def ring_shards(shard):
    held = [shard]
    for _ in range(RINGS - 1):
        held.append(ring_step(held[-1]))
    return held


def gather_weight(held):
    chunks = []
    beside = None
    for distance, current in enumerate(held):
        beside = other_y(current if beside is None else after(current, beside))
        for flip_y, chunk in ((0, current), (1, beside)):
            for flip_core, piece in ((0, chunk), (1, other_core(chunk))):
                chunks.append(((distance, flip_y, flip_core), piece))
    return chunks


def place_of(coords, key):
    z, y, core = coords
    distance, flip_y, flip_core = key
    return (
        lax.rem(z + RINGS - distance, RINGS) * 4
        + (1 - y if flip_y else y) * 2
        + (1 - core if flip_core else core)
    )


def weight_keys():
    return [
        (distance, flip_y, flip_core)
        for flip_core in (0, 1)
        for flip_y in (0, 1)
        for distance in range(RINGS)
    ]


def scatter_blocks(grads, low):
    half = grads.shape[0] // 2
    total = grads[:half].astype(jnp.float32) + other_core(grads[half:].astype(low)).astype(
        jnp.float32
    )
    quarter = half // 2
    total = total[:quarter] + other_y(total[quarter:].astype(low)).astype(jnp.float32)
    size = quarter // RINGS
    return ring_sum([total[r * size : (r + 1) * size] for r in range(RINGS)], low)


def pick_blocks(values, order):
    chosen = order[:, None] == jnp.arange(values.shape[0], dtype=jnp.int32)[None, :]
    chosen = chosen.reshape(chosen.shape + (1,) * (values.ndim - 1))
    return jnp.sum(jnp.where(chosen, values[None], 0.0), axis=1)


def wide_dot(left, right):
    return jnp.dot(left, right, preferred_element_type=jnp.float32)


def dot_turned(left, right):
    return lax.dot_general(left, right, (((1,), (1,)), ((), ())), preferred_element_type=jnp.float32)


def dot_rows(left, right):
    return lax.dot_general(left, right, (((0,), (0,)), ((), ())), preferred_element_type=jnp.float32)


TILE = 256


def whole(array):
    return pl.BlockSpec(array.shape, lambda *i: (0,) * array.ndim)


def in_vmem(count):
    return [pl.BlockSpec(memory_space=pltpu.VMEM)] * count


def in_place(count):
    return [pl.BlockSpec(memory_space=pl.ANY)] * count


def head_scores(heads, h, nope_ref, turned_ref, keyval_ref, key_ref, masks):
    span = ROPE // 2 * heads
    column = pl.ds(pl.multiple_of(h * NOPE, NOPE), NOPE)
    key_column = pl.ds(pl.multiple_of(h * (NOPE + VD), NOPE), NOPE)
    scores = dot_turned(nope_ref[:, column], keyval_ref[:, key_column])
    for k in (0, 1):
        part = turned_ref[:, k * span : (k + 1) * span]
        part = jnp.where(masks, part, jnp.zeros_like(part))
        scores += dot_turned(part, key_ref[:, k * span : (k + 1) * span])
    return scores * (NOPE + ROPE) ** (-0.5)


def head_lanes(heads, h):
    span = ROPE // 2 * heads
    lane = lax.broadcasted_iota(jnp.int32, (1, span), 1)
    return (lane >= h * (ROPE // 2)) & (lane < (h + 1) * (ROPE // 2))


def allowed_rows(count, segment_row, segment_column):
    tokens = segment_row.shape[1]
    column = lax.broadcasted_iota(jnp.int32, (tokens, tokens), 0)
    row = lax.broadcasted_iota(jnp.int32, (tokens, tokens), 1)
    live = (column < count) & (row < count) & (row <= column)
    return (segment_row == segment_column) & live | (column == row)


def attend_kernel(
    keys,
    extra,
    heads,
    sizes,
    place_ref,
    segment_row_ref,
    segment_column_ref,
    cosine_ref,
    sine_ref,
    own_ref,
    other_ref,
    *refs,
):
    depth, query_width, used, latent_depth, keyval_part, first_width = sizes
    chunks = refs[: len(keys)]
    (
        own_out,
        sent_out,
        first_ref,
        keyval_weight_ref,
        output_ref,
        normed_ref,
        nope_ref,
        turned_ref,
        latent_ref,
        key_ref,
        keyval_ref,
        total_ref,
        attended_ref,
        gains_ref,
        latent_gain_ref,
        semaphores,
    ) = refs[len(keys) + extra :]
    f32, bf16 = jnp.float32, jnp.bfloat16
    local_rows = own_ref.shape[0]
    tokens = 2 * local_rows
    coords = (place_ref[0], place_ref[1], place_ref[2])
    x = place_ref[3]
    copies = []
    parts = depth // latent_depth
    for key, chunk in zip(keys, chunks):
        block = place_of(coords, key)
        rows = pl.ds(pl.multiple_of(block * depth, depth), depth)
        small_rows = pl.ds(pl.multiple_of(block * latent_depth, latent_depth), latent_depth)
        moves = [(chunk.at[:, pl.ds(0, first_width)], first_ref.at[rows])]
        for k in range(parts):
            moves.append(
                (
                    chunk.at[
                        pl.ds(k * latent_depth, latent_depth), pl.ds(first_width, keyval_part)
                    ],
                    keyval_weight_ref.at[small_rows, pl.ds(k * keyval_part, keyval_part)],
                )
            )
        moves.append(
            (
                chunk.at[:, pl.ds(first_width + keyval_part, heads * VD)],
                output_ref.at[rows],
            )
        )
        for source, target in moves:
            copies.append(pltpu.make_async_copy(source, target, semaphores.at[len(copies)]))
    for copy in copies:
        copy.start()
    for copy in copies:
        copy.wait()

    edge = query_width + KVR
    spread = jnp.transpose(first_ref[:, edge:].astype(f32))[used - edge : used - edge + 8]
    gains_ref[...] = spread
    gain = spread[0:1]
    source = lax.broadcasted_iota(jnp.int32, (D, KVR), 0)
    target = lax.broadcasted_iota(jnp.int32, (D, KVR), 1)
    wanted = target // latent_depth * depth + target % latent_depth
    chosen = jnp.where(source == wanted, 1.0, 0.0).astype(bf16)
    latent_gain = wide_dot(spread.astype(bf16), chosen)[2:3]
    latent_gain_ref[...] = latent_gain
    for ref, start in ((own_ref, x * local_rows), (other_ref, (1 - x) * local_rows)):
        rows = ref[...].astype(f32)
        unit = rows * lax.rsqrt(jnp.mean(rows * rows, axis=1, keepdims=True) + EPSILON)
        normed_ref[pl.ds(pl.multiple_of(start, local_rows), local_rows), :] = (unit * gain).astype(
            bf16
        )
    nope_width = heads * NOPE
    span = heads * (ROPE // 2)
    half = nope_width // 2
    for k in (0, 1):
        nope_ref[:, k * half : (k + 1) * half] = wide_dot(
            normed_ref[...], first_ref[:, k * half : (k + 1) * half]
        ).astype(bf16)
    turning = wide_dot(normed_ref[...], first_ref[:, nope_width : nope_width + 2 * span])
    cosine, sine = cosine_ref[...], sine_ref[...]
    first, second = turning[:, :span], turning[:, span:]
    turned_ref[:, :span] = (first * cosine - second * sine).astype(bf16)
    turned_ref[:, span:] = (second * cosine + first * sine).astype(bf16)
    latent = wide_dot(normed_ref[...], first_ref[:, query_width : query_width + KVR])
    latent_ref[...] = latent
    tail = wide_dot(normed_ref[...], first_ref[:, query_width + KVR :])
    lane = lax.broadcasted_iota(jnp.int32, (1, tail.shape[1]), 1)
    swapped = jnp.where(
        lane < ROPE // 2,
        -pltpu.roll(tail, tail.shape[1] - ROPE // 2, 1),
        pltpu.roll(tail, ROPE // 2, 1),
    )
    width = tail.shape[1]
    turned_key = tail * cosine[:, :width] + swapped * sine[:, :width]
    turned_key = jnp.where(lane < ROPE, turned_key, 0.0).astype(bf16)
    source = lax.broadcasted_iota(jnp.int32, (width, 2 * span), 0)
    target = lax.broadcasted_iota(jnp.int32, (width, 2 * span), 1)
    wanted = target % (ROPE // 2) + jnp.where(target < span, 0, ROPE // 2)
    key_ref[...] = wide_dot(turned_key, (source == wanted).astype(bf16)).astype(bf16)
    unit = latent * lax.rsqrt(jnp.mean(latent * latent, axis=1, keepdims=True) + EPSILON)
    latent_normed = (unit * latent_gain).astype(bf16)
    half = keyval_ref.shape[1] // 4
    for k in range(4):
        keyval_ref[:, k * half : (k + 1) * half] = wide_dot(
            latent_normed, keyval_weight_ref[:, k * half : (k + 1) * half]
        ).astype(bf16)
    allowed = allowed_rows(place_ref[4], segment_row_ref[...], segment_column_ref[...])
    total_lane = lax.broadcasted_iota(jnp.int32, total_ref.shape, 1)
    total_ref[...] = jnp.zeros_like(total_ref)

    def one_head(h, _):
        scores = head_scores(
            heads, h, nope_ref, turned_ref, keyval_ref, key_ref, head_lanes(heads, h)
        )
        scores = jnp.where(allowed, scores, -1e30)
        most = jnp.max(scores, axis=1, keepdims=True)
        total = most + jnp.log(jnp.sum(jnp.exp(scores - most), axis=1, keepdims=True))
        weights = jnp.exp(scores - total).astype(bf16)
        total_ref[...] += jnp.where(total_lane == h, total, 0.0)
        value_column = pl.ds(pl.multiple_of(h * (NOPE + VD) + NOPE, NOPE), VD)
        attended_ref[:, pl.ds(pl.multiple_of(h * VD, VD), VD)] = wide_dot(
            weights, keyval_ref[:, value_column]
        ).astype(bf16)
        return 0

    lax.fori_loop(0, heads, one_head, 0)
    own = pl.ds(pl.multiple_of(x * local_rows, local_rows), local_rows)
    other = pl.ds(pl.multiple_of((1 - x) * local_rows, local_rows), local_rows)
    pieces = 4
    size = output_ref.shape[0] // pieces
    for k in range(pieces):
        columns = slice(k * size, (k + 1) * size)
        own_out[:, columns] = dot_turned(attended_ref[own, :], output_ref[columns, :])
        sent_out[:, columns] = dot_turned(attended_ref[other, :], output_ref[columns, :]).astype(
            bf16
        )


def attend_forward(place, segments, cosine, sine, own, other, chunks, heads, sizes, others):
    depth, query_width, used, latent_depth, keyval_part, first_width = sizes
    f32, bf16 = jnp.float32, jnp.bfloat16
    keys = [key for key, _ in chunks]
    local_rows = own.shape[0]
    tokens = 2 * local_rows
    span = heads * (ROPE // 2)
    shapes = [
        ((local_rows, D), f32),
        ((local_rows, D), bf16),
        ((D, first_width), bf16),
        ((KVR, heads * (NOPE + VD)), bf16),
        ((D, heads * VD), bf16),
        ((tokens, D), bf16),
        ((tokens, heads * NOPE), bf16),
        ((tokens, 2 * span), bf16),
        ((tokens, KVR), f32),
        ((tokens, 2 * span), bf16),
        ((tokens, heads * (NOPE + VD)), bf16),
        ((tokens, 128), f32),
        ((tokens, heads * VD), bf16),
        ((8, D), f32),
        ((1, KVR), f32),
    ]
    return pl.pallas_call(
        functools.partial(attend_kernel, keys, len(others), heads, sizes),
        out_shape=[jax.ShapeDtypeStruct(*shape) for shape in shapes],
        in_specs=[pl.BlockSpec(memory_space=pltpu.SMEM)]
        + in_vmem(6)
        + in_place(len(chunks) + len(others)),
        out_specs=in_vmem(len(shapes)),
        scratch_shapes=[
            pltpu.SemaphoreType.DMA((len(chunks) * (2 + depth // latent_depth),))
        ],
        compiler_params=pltpu.CompilerParams(vmem_limit_bytes=48 * 1024 * 1024),
        cost_estimate=pl.CostEstimate(
            flops=2 * tokens * D * (first_width + heads * VD + 1024),
            bytes_accessed=4 * D * (first_width + 1536),
            transcendentals=2 * heads * tokens * tokens,
        ),
    )(
        place,
        segments,
        segments.T,
        cosine,
        sine,
        own,
        other,
        *[piece for _, piece in chunks],
        *others,
    )


def attend_back_kernel(
    heads,
    place_ref,
    segment_row_ref,
    segment_column_ref,
    cosine_ref,
    sine_ref,
    own_ref,
    other_ref,
    keyval_weight_ref,
    output_ref,
    nope_ref,
    turned_ref,
    latent_ref,
    key_ref,
    keyval_ref,
    total_ref,
    latent_gain_ref,
    projected_ref,
    keyval_grad_ref,
    latent_out,
    gain_ref,
    grad_ref,
    turn_ref,
    back_ref,
):
    f32, bf16 = jnp.float32, jnp.bfloat16
    local_rows = own_ref.shape[0]
    x = place_ref[3]
    span = heads * (ROPE // 2)
    nope_width = heads * NOPE
    query_width = nope_width + 2 * span
    scale = (NOPE + ROPE) ** (-0.5)
    for ref, start in ((own_ref, x * local_rows), (other_ref, (1 - x) * local_rows)):
        rows = pl.ds(pl.multiple_of(start, local_rows), local_rows)
        for k in (0, 1):
            half = slice(k * nope_width // 2, (k + 1) * nope_width // 2)
            grad_ref[rows, half] = wide_dot(ref[...], output_ref[:, half]).astype(bf16)
    allowed = allowed_rows(place_ref[4], segment_row_ref[...], segment_column_ref[...])
    total_lane = lax.broadcasted_iota(jnp.int32, total_ref.shape, 1)
    turn_ref[...] = jnp.zeros_like(turn_ref)
    back_ref[...] = jnp.zeros_like(back_ref)

    def one_head(h, _):
        mask = head_lanes(heads, h)
        scores = head_scores(heads, h, nope_ref, turned_ref, keyval_ref, key_ref, mask)
        total = jnp.sum(jnp.where(total_lane == h, total_ref[...], 0.0), axis=1, keepdims=True)
        weights = jnp.exp(jnp.where(allowed, scores, -1e30) - total)
        weights_low = weights.astype(bf16)
        column = pl.ds(pl.multiple_of(h * NOPE, NOPE), NOPE)
        key_column = pl.ds(pl.multiple_of(h * (NOPE + VD), NOPE), NOPE)
        value_column = pl.ds(pl.multiple_of(h * (NOPE + VD) + NOPE, NOPE), VD)
        grads = grad_ref[:, column]
        grad_weights = dot_turned(grads, keyval_ref[:, value_column])
        keyval_grad_ref[:, value_column] = dot_rows(weights_low, grads).astype(bf16)
        grad_scores = (
            weights * (grad_weights - jnp.sum(weights * grad_weights, axis=1, keepdims=True))
        ).astype(bf16)
        projected_ref[:, column] = (
            scale * wide_dot(grad_scores, keyval_ref[:, key_column])
        ).astype(bf16)
        keyval_grad_ref[:, key_column] = (
            scale * dot_rows(grad_scores, nope_ref[:, column])
        ).astype(bf16)
        for k in (0, 1):
            part = slice(k * span, (k + 1) * span)
            turn = wide_dot(grad_scores, key_ref[:, part])
            turn_ref[:, part] += jnp.where(mask, turn, 0.0)
            own = turned_ref[:, part]
            own = jnp.where(mask, own, jnp.zeros_like(own))
            back_ref[:, part] += dot_rows(grad_scores, own)
        return 0

    lax.fori_loop(0, heads, one_head, 0)
    cosine, sine = cosine_ref[...], sine_ref[...]
    first, second = scale * turn_ref[:, :span], scale * turn_ref[:, span:]
    projected_ref[:, nope_width : nope_width + span] = (first * cosine + second * sine).astype(bf16)
    projected_ref[:, nope_width + span : query_width] = (second * cosine - first * sine).astype(
        bf16
    )
    folded = []
    for k in (0, 1):
        part = scale * back_ref[:, k * span : (k + 1) * span]
        shift = span // 2
        while shift >= ROPE // 2:
            part = part + pltpu.roll(part, shift, 1)
            shift //= 2
        folded.append(part)
    width = projected_ref.shape[1] - query_width - KVR
    lane = lax.broadcasted_iota(jnp.int32, (1, width), 1)
    first = (folded[0] * cosine + folded[1] * sine)[:, :width]
    second = (folded[1] * cosine - folded[0] * sine)[:, :width]
    projected_ref[:, query_width + KVR :] = jnp.where(
        lane < ROPE // 2, first, jnp.where(lane < ROPE, second, 0.0)
    ).astype(bf16)
    gain = latent_gain_ref[...]
    latent = latent_ref[...]
    row_scale = lax.rsqrt(jnp.mean(latent * latent, axis=1, keepdims=True) + EPSILON)
    unit = latent * row_scale
    latent_out[...] = (unit * gain).astype(bf16)
    grad_normed = dot_turned(keyval_grad_ref[...], keyval_weight_ref[...])
    gain_ref[...] = jnp.sum(grad_normed * unit, axis=0, keepdims=True)
    grad_unit = grad_normed * gain
    projected_ref[:, query_width : query_width + KVR] = (
        row_scale * (grad_unit - unit * jnp.mean(grad_unit * unit, axis=1, keepdims=True))
    ).astype(bf16)


def attend_back(place, segments, cosine, sine, own, other, saved, heads, first_width):
    f32, bf16 = jnp.float32, jnp.bfloat16
    keyval = saved[6]
    tokens = 2 * own.shape[0]
    span = heads * (ROPE // 2)
    return pl.pallas_call(
        functools.partial(attend_back_kernel, heads),
        out_shape=[
            jax.ShapeDtypeStruct((tokens, first_width), bf16),
            jax.ShapeDtypeStruct((tokens, keyval.shape[1]), bf16),
            jax.ShapeDtypeStruct((tokens, KVR), bf16),
            jax.ShapeDtypeStruct((1, KVR), f32),
        ],
        in_specs=[pl.BlockSpec(memory_space=pltpu.SMEM)] + in_vmem(15),
        out_specs=in_vmem(4),
        scratch_shapes=[
            pltpu.VMEM((tokens, heads * NOPE), bf16),
            pltpu.VMEM((tokens, 2 * span), f32),
            pltpu.VMEM((tokens, 2 * span), f32),
        ],
        compiler_params=pltpu.CompilerParams(vmem_limit_bytes=48 * 1024 * 1024),
        cost_estimate=pl.CostEstimate(
            flops=2 * tokens * D * 3000,
            bytes_accessed=2 * D * 1536,
            transcendentals=heads * tokens * tokens,
        ),
    )(
        place,
        segments,
        segments.T,
        cosine,
        sine,
        own,
        other,
        *saved,
    )


def first_grads_kernel(extra, places_ref, left_ref, right_ref, small_ref, *refs):
    out_ref = refs[-1]
    size = left_ref.shape[1]
    edge = right_ref.shape[1] - small_ref.shape[0]
    result = dot_rows(left_ref[...], right_ref[...])
    for value, some in (
        (result[:, :edge], slice(0, edge)),
        (result[:, edge:] + jnp.transpose(small_ref[...]), slice(edge, right_ref.shape[1])),
    ):
        if extra:
            value = value + refs[0][:, some].astype(jnp.float32)
        out_ref[:, some] = value.astype(jnp.bfloat16)


def other_grads_kernel(first, extra, places_ref, latent_ref, keyval_ref, grad_ref, attended_ref, *refs):
    out_ref, keyval_all = refs[-2:]
    step = pl.program_id(0)
    size = grad_ref.shape[1]
    latent_size = latent_ref.shape[1] // places_ref.shape[0]
    parts = size // latent_size
    columns = keyval_ref.shape[1] // parts

    @pl.when(step == 0)
    def _():
        for k in range(parts):
            some = slice(k * columns, (k + 1) * columns)
            keyval_all[:, some] = dot_rows(latent_ref[...], keyval_ref[:, some])

    start = pl.multiple_of(places_ref[first + step] * latent_size, latent_size)
    strip = keyval_all[pl.ds(start, latent_size), :]
    keyval = jnp.concatenate([strip[:, k * columns : (k + 1) * columns] for k in range(parts)], axis=0)
    output = dot_rows(grad_ref[...], attended_ref[...])
    for value, some in (
        (keyval, slice(0, columns)),
        (output, slice(columns, columns + output.shape[1])),
    ):
        if extra:
            value = value + refs[0][:, some].astype(jnp.float32)
        out_ref[:, some] = value.astype(jnp.bfloat16)


def still(array):
    return pl.BlockSpec(array.shape, lambda i, where: (0, 0))


def grads_call(kernel, specs, operands, scratch, size, width, places, first, count, arrived):
    extra = [] if arrived is None else [arrived]
    return pl.pallas_call(
        functools.partial(kernel, len(extra)),
        grid_spec=pltpu.PrefetchScalarGridSpec(
            num_scalar_prefetch=1,
            grid=(count,),
            in_specs=specs
            + [pl.BlockSpec((size, width), lambda i, where: (first + i, 0))] * len(extra),
            out_specs=pl.BlockSpec((size, width), lambda i, where: (i, 0)),
            scratch_shapes=scratch,
        ),
        out_shape=jax.ShapeDtypeStruct((count * size, width), jnp.bfloat16),
        compiler_params=pltpu.CompilerParams(vmem_limit_bytes=32 * 1024 * 1024),
        cost_estimate=pl.CostEstimate(
            flops=1024 * count * size * width,
            bytes_accessed=4 * count * size * width,
            transcendentals=0,
        ),
    )(places, *operands, *extra)


def first_grads(left, right, small, places, first, count, arrived=None):
    rows, width = right.shape
    size = left.shape[1] // places.shape[0]
    specs = [
        pl.BlockSpec((rows, size), lambda i, where: (0, where[first + i])),
        still(right),
        pl.BlockSpec((small.shape[0], size), lambda i, where: (0, where[first + i])),
    ]
    return grads_call(
        first_grads_kernel, specs, (left, right, small), [], size, width, places, first, count, arrived
    )


def other_grads(latent, keyval, grad, attended, places, first, count, arrived=None):
    rows = grad.shape[0]
    blocks = places.shape[0]
    size = grad.shape[1] // blocks
    parts = size // (latent.shape[1] // blocks)
    width = keyval.shape[1] // parts + attended.shape[1]
    specs = [
        still(latent),
        still(keyval),
        pl.BlockSpec((rows, size), lambda i, where: (0, where[first + i])),
        still(attended),
    ]
    scratch = [pltpu.VMEM((latent.shape[1], keyval.shape[1]), jnp.float32)]
    return grads_call(
        functools.partial(other_grads_kernel, first),
        specs,
        (latent, keyval, grad, attended),
        scratch,
        size,
        width,
        places,
        first,
        count,
        arrived,
    )


def first_back_kernel(place_ref, own_ref, other_ref, grad_ref, weight_ref, own_out, sent_out, gain_ref):
    local_rows = own_ref.shape[0]
    x = place_ref[3]
    size = weight_ref.shape[0] // 4
    for ref, start, out in (
        (own_ref, x * local_rows, own_out),
        (other_ref, (1 - x) * local_rows, sent_out),
    ):
        rows = ref[...].astype(jnp.float32)
        unit = rows * lax.rsqrt(jnp.mean(rows * rows, axis=1, keepdims=True) + EPSILON)
        grads = grad_ref[pl.ds(pl.multiple_of(start, local_rows), local_rows), :]
        for k in range(4):
            some = slice(k * size, (k + 1) * size)
            part = dot_turned(grads, weight_ref[some, :])
            out[:, some] = part.astype(out.dtype)
            gain = jnp.sum(part * unit[:, some], axis=0, keepdims=True)
            if ref is own_ref:
                gain_ref[:, some] = gain
            else:
                gain_ref[:, some] += gain


def first_back(place, own, other, grads, weight):
    f32, bf16 = jnp.float32, jnp.bfloat16
    depth = weight.shape[0]
    return pl.pallas_call(
        first_back_kernel,
        out_shape=[
            jax.ShapeDtypeStruct(own.shape, f32),
            jax.ShapeDtypeStruct(own.shape, bf16),
            jax.ShapeDtypeStruct((1, depth), f32),
        ],
        in_specs=[pl.BlockSpec(memory_space=pltpu.SMEM)] + in_vmem(4),
        out_specs=in_vmem(3),
        compiler_params=pltpu.CompilerParams(vmem_limit_bytes=32 * 1024 * 1024),
        cost_estimate=pl.CostEstimate(
            flops=4 * own.shape[0] * weight.shape[0] * weight.shape[1],
            bytes_accessed=2 * weight.shape[0] * weight.shape[1],
            transcendentals=0,
        ),
    )(place, own, other, grads, weight)


def close_ring(near, arrived):
    size = near.shape[0] // RINGS
    total = near.astype(jnp.float32) + arrived.astype(jnp.float32)
    return ring_sum([total[r * size : (r + 1) * size] for r in range(RINGS)], jnp.bfloat16)


def pack_kernel(heads, query_ref, latent_ref, small_ref, keyval_ref, output_ref, out_ref):
    half = ROPE // 2
    head = NOPE + ROPE
    nope_width = heads * NOPE
    for h in range(heads):
        start = h * head
        out_ref[:, h * NOPE : (h + 1) * NOPE] = query_ref[:, start : start + NOPE]
        for k in (0, 1):
            to = nope_width + k * heads * half + h * half
            out_ref[:, to : to + half] = query_ref[
                :, start + NOPE + k * half : start + NOPE + (k + 1) * half
            ]
    at = heads * head
    edge = at + KVR
    out_ref[:, at:edge] = latent_ref[:, :KVR]
    out_ref[:, edge : edge + 128] = jnp.concatenate([latent_ref[:, KVR:], small_ref[...]], axis=1)
    at = edge + 128
    size = keyval_ref.shape[0]
    parts = out_ref.shape[0] // size
    part = keyval_ref.shape[1] // parts
    for k in range(parts):
        out_ref[k * size : (k + 1) * size, at : at + part] = keyval_ref[
            :, k * part : (k + 1) * part
        ]
    out_ref[:, at + part :] = jnp.transpose(output_ref[...].astype(jnp.float32)).astype(
        jnp.bfloat16
    )


def pack_weights(query, latent, small, keyval, output):
    depth, query_width = query.shape
    heads = query_width // (NOPE + ROPE)
    width = query_width + KVR + 128 + keyval.size // depth + output.shape[0]
    return pl.pallas_call(
        functools.partial(pack_kernel, heads),
        out_shape=jax.ShapeDtypeStruct((depth, width), jnp.bfloat16),
        in_specs=in_vmem(5),
        out_specs=pl.BlockSpec(memory_space=pltpu.VMEM),
    )(query, latent, small, keyval, output)


def load_pieces(pieces, target, semaphores):
    size = pieces[0].shape[0]
    copies = [
        pltpu.make_async_copy(piece, target.at[pl.ds(k * size, size)], semaphores.at[k])
        for k, piece in enumerate(pieces)
    ]
    for copy in copies:
        copy.start()
    for copy in copies:
        copy.wait()


def shared_stride(shared):
    return -(-shared // 32) * 32


def pack_shared_kernel(blocks, shared, in_ref, down_ref, out_ref):
    stride = shared_stride(shared)
    out_ref[...] = jnp.zeros_like(out_ref)
    for k in range(3):
        if k < 2:
            units = jnp.transpose(in_ref[k].astype(jnp.float32)).astype(jnp.bfloat16)
        else:
            units = down_ref[...]
        for b in range(blocks):
            out_ref[b, k * stride : k * stride + shared] = units[b * shared : (b + 1) * shared]


def pack_shared(shared_in, shared_down, blocks, others):
    depth = shared_in.shape[1]
    shared = shared_down.shape[0] // blocks
    return pl.pallas_call(
        lambda in_ref, down_ref, *refs: pack_shared_kernel(
            blocks, shared, in_ref, down_ref, refs[-1]
        ),
        out_shape=jax.ShapeDtypeStruct((blocks, 3 * shared_stride(shared), depth), jnp.bfloat16),
        in_specs=in_vmem(2) + in_place(len(others)),
        out_specs=pl.BlockSpec(memory_space=pltpu.VMEM),
    )(shared_in, shared_down, *others)


def unpack_shared_kernel(shared, packed_ref, in_ref, down_ref, units_ref):
    stride = shared_stride(shared)
    blocks = packed_ref.shape[0]
    for k in range(3):
        target = down_ref if k == 2 else units_ref
        for b in range(blocks):
            target[b * shared : (b + 1) * shared, :] = packed_ref[
                b, k * stride : k * stride + shared
            ].astype(jnp.float32)
        if k < 2:
            in_ref[k] = jnp.transpose(units_ref[...])


def unpack_shared(packed, shared, others):
    blocks, _, depth = packed.shape
    return pl.pallas_call(
        lambda packed_ref, *refs: unpack_shared_kernel(shared, packed_ref, *refs[len(others) :]),
        out_shape=[
            jax.ShapeDtypeStruct((2, depth, blocks * shared), jnp.float32),
            jax.ShapeDtypeStruct((blocks * shared, depth), jnp.float32),
        ],
        in_specs=in_vmem(1) + in_place(len(others)),
        out_specs=in_vmem(2),
        scratch_shapes=[pltpu.VMEM((blocks * shared, depth), jnp.float32)],
    )(packed, *others)


def pack_units_kernel(units, shared, own_in, other_in, own_down, other_down, near, far, *refs):
    outs = refs[-3:]
    hole = -(-units // TILE) * TILE
    stride = shared_stride(shared)
    columns = outs[0].shape[1]
    size = near.shape[2]
    for k, out in enumerate(outs):
        first = own_in[0, k] if k < 2 else own_down[0]
        second = other_in[0, k] if k < 2 else other_down[0]
        out[:units] = first
        out[units:hole] = jnp.zeros((hole - units, columns), jnp.bfloat16)
        out[hole : hole + units] = second
        out[hole + units : 2 * hole] = jnp.zeros((hole - units, columns), jnp.bfloat16)
        out[2 * hole :] = jnp.zeros((TILE, columns), jnp.bfloat16)
        for b in range(columns // size):
            part = slice(b * size, (b + 1) * size)
            for at, ref in ((2 * hole, near), (2 * hole + stride, far)):
                out[at : at + shared, part] = ref[b, k * stride : k * stride + shared]


def pack_units(own_in, other_in, own_down, other_down, near, far, shared, others):
    units, depth = own_down.shape[1:]
    size = near.shape[2]
    height = 2 * (-(-units // TILE) * TILE) + TILE
    columns = 2 * size
    in_spec = pl.BlockSpec((1, 2, units, columns), lambda i: (0, 0, 0, i))
    down_spec = pl.BlockSpec((1, units, columns), lambda i: (0, 0, i))
    narrow = pl.BlockSpec((2,) + near.shape[1:], lambda i: (i, 0, 0))
    return pl.pallas_call(
        functools.partial(pack_units_kernel, units, shared),
        grid=(depth // columns,),
        in_specs=[in_spec, in_spec, down_spec, down_spec, narrow, narrow]
        + in_place(len(others)),
        out_specs=[pl.BlockSpec((height, columns), lambda i: (0, i))] * 3,
        out_shape=[jax.ShapeDtypeStruct((height, depth), jnp.bfloat16)] * 3,
        compiler_params=pltpu.CompilerParams(vmem_limit_bytes=32 * 1024 * 1024),
        cost_estimate=pl.CostEstimate(
            flops=0, bytes_accessed=12 * height * depth, transcendentals=0
        ),
    )(own_in, other_in, own_down, other_down, near, far, *others)


def expert_grads_kernel(units, count, extra, right_ref, *refs):
    out = refs[-1]
    for k in range(count):

        @pl.when(pl.program_id(0) == k)
        def _():
            result = dot_rows(refs[k][...], right_ref[...])[:units]
            if extra:
                result += refs[count][0, 0].astype(jnp.float32)
            out[0, 0] = result.astype(out.dtype)


def expert_grads(lefts, right, units, column, arrived, kind, others=()):
    total, depth = right.shape
    wide = -(-units // TILE) * TILE
    extra = [] if arrived is None else [arrived]
    out = pl.BlockSpec((1, 1, units, 2 * TILE), lambda k, i: (0, k, 0, i))
    side = pl.BlockSpec((total, wide), lambda k, i: (0, column))
    return pl.pallas_call(
        functools.partial(expert_grads_kernel, units, len(lefts), len(extra)),
        grid=(len(lefts), depth // (2 * TILE)),
        in_specs=[pl.BlockSpec((total, 2 * TILE), lambda k, i: (0, i))]
        + [side] * len(lefts)
        + [out] * len(extra)
        + in_place(len(others)),
        out_specs=out,
        out_shape=jax.ShapeDtypeStruct((1, len(lefts), units, depth), kind),
        compiler_params=pltpu.CompilerParams(vmem_limit_bytes=48 * 1024 * 1024),
        cost_estimate=pl.CostEstimate(
            flops=2 * len(lefts) * total * depth * wide,
            bytes_accessed=2 * len(lefts) * total * (depth + wide) + 8 * depth * units,
            transcendentals=0,
        ),
    )(right, *lefts, *extra, *others)


def side_grads_kernel(shared, rows_ref, cots_ref, gate_ref, up_ref, hidden_ref, logit_ref, *outs):
    kept_ref, sent_ref, router_ref = outs
    stride = shared_stride(shared)
    size = kept_ref.shape[2]
    for k, (left, right) in enumerate(
        ((gate_ref, rows_ref), (up_ref, rows_ref), (hidden_ref, cots_ref))
    ):
        result = dot_rows(left[...], right[...])
        for b in range(kept_ref.shape[0]):
            part = slice(b * size, (b + 1) * size)
            kept_ref[b, k * stride : (k + 1) * stride] = result[:stride, part]
            sent_ref[b, k * stride : (k + 1) * stride] = result[
                stride : 2 * stride, part
            ].astype(jnp.bfloat16)
    router_ref[...] = dot_rows(logit_ref[...], rows_ref[...])


def side_grads(rows, cots, gate, up, hidden, logits, shared, blocks):
    total, depth = rows.shape
    column = gate.shape[1] // TILE - 1
    size = depth // blocks
    stride = shared_stride(shared)
    wide = pl.BlockSpec((total, 2 * TILE), lambda i: (0, i))
    side = pl.BlockSpec((total, TILE), lambda i: (0, column))
    packed = pl.BlockSpec((2 * TILE // size, 3 * stride, size), lambda i: (i, 0, 0))
    return pl.pallas_call(
        functools.partial(side_grads_kernel, shared),
        grid=(depth // (2 * TILE),),
        in_specs=[wide, wide, side, side, side, whole(logits)],
        out_specs=[packed, packed, pl.BlockSpec((logits.shape[1], 2 * TILE), lambda i: (0, i))],
        out_shape=[
            jax.ShapeDtypeStruct((blocks, 3 * stride, size), jnp.float32),
            jax.ShapeDtypeStruct((blocks, 3 * stride, size), jnp.bfloat16),
            jax.ShapeDtypeStruct((logits.shape[1], depth), jnp.float32),
        ],
        compiler_params=pltpu.CompilerParams(vmem_limit_bytes=48 * 1024 * 1024),
        cost_estimate=pl.CostEstimate(
            flops=8 * total * depth * TILE,
            bytes_accessed=4 * total * depth,
            transcendentals=0,
        ),
    )(rows, cots, gate, up, hidden, logits)


def down_kernel(count, *refs):
    pieces, weight_ref = refs[:count], refs[count]
    grads_ref, rows_ref, semaphores = refs[-3:]

    @pl.when(pl.program_id(0) == 0)
    def _():
        load_pieces(pieces, rows_ref, semaphores)

    size = rows_ref.shape[0] // 2
    for k in range(2):
        part = slice(k * size, (k + 1) * size)
        grads_ref[part, :] = dot_turned(rows_ref[part, :], weight_ref[...]).astype(jnp.bfloat16)


def down_grads(part, pieces, down, kept, others):
    count = len(pieces)
    size, depth = pieces[0].shape
    width = down.shape[0]
    rows = count * size
    return pl.pallas_call(
        functools.partial(down_kernel, count),
        grid=(width // TILE,),
        in_specs=in_place(count)
        + [pl.BlockSpec((TILE, depth), lambda i: (i, 0))]
        + in_place(len(kept) + len(others)),
        out_specs=[
            pl.BlockSpec((rows, TILE), lambda i: (part, i)),
            pl.BlockSpec((rows, depth), lambda i: (part, 0)),
        ],
        out_shape=[
            jax.ShapeDtypeStruct((2 * rows, width), jnp.bfloat16),
            jax.ShapeDtypeStruct((2 * rows, depth), jnp.bfloat16),
        ],
        scratch_shapes=[pltpu.SemaphoreType.DMA((count,))],
        input_output_aliases={count + 1 + k: k for k in range(len(kept))},
        compiler_params=pltpu.CompilerParams(vmem_limit_bytes=48 * 1024 * 1024),
        cost_estimate=pl.CostEstimate(
            flops=2 * rows * depth * width,
            bytes_accessed=2 * (2 * rows * depth + depth * width + rows * width),
            transcendentals=0,
        ),
    )(*pieces, down, *kept, *others)


def mlp_kernel(tiles, columns, joined, pieces, others, experts_ref, routed_ref, *refs):
    row_refs = refs[:pieces]
    router_ref, gate_col, up_col, down_grad, gate_row, up_row, down_row = refs[pieces : pieces + 7]
    outs = refs[pieces + 7 + others :]
    grad_refs, out_refs = outs[:pieces], outs[:pieces] if joined else outs[pieces : 2 * pieces]
    outs = outs[pieces if joined else 2 * pieces :]
    rows_out, hidden_out, gate_out, up_out, logit_out = outs[:5]
    hidden_all, gate_all, up_all, prob_ref, scale_ref, sum_ref, semaphores = outs[5:]
    step = pl.program_id(0)
    third = tiles // 2
    total = rows_out.shape[0]
    size = total // pieces
    lane = lax.broadcasted_iota(jnp.int32, (1, router_ref.shape[1]), 1) - experts_ref[3]

    @pl.when(step == 0)
    def _():
        load_pieces(row_refs, rows_out, semaphores)
        logits = wide_dot(rows_out[...], router_ref[...])
        logits = jnp.where((lane >= 0) & (lane < experts_ref[2]), logits, -1e30)
        raised = jnp.exp(logits - jnp.max(logits, axis=1, keepdims=True))
        chances = raised / jnp.sum(raised, axis=1, keepdims=True)
        prob_ref[...] = chances
        for k in (0, 1):
            chance = jnp.sum(jnp.where(lane == experts_ref[k], chances, 0.0), axis=1, keepdims=True)
            scale_ref[k] = routed_ref[:, k : k + 1] * chance
        scale_ref[2] = jnp.ones_like(scale_ref[2])
        sum_ref[...] = jnp.zeros_like(sum_ref)

    @pl.when(step < tiles)
    def _():
        columns_here = pl.ds(pl.multiple_of(step * TILE, TILE), TILE)
        kind = step // third
        half = total // 2
        for k in (0, 1):
            part = slice(k * half, (k + 1) * half)
            pre_gate = dot_turned(rows_out[part, :], gate_col[...])
            pre_up = dot_turned(rows_out[part, :], up_col[...])
            grads = down_grad[part, :].astype(jnp.float32)
            scale = scale_ref[kind, part, :]
            sigmoid = 1.0 / (1.0 + jnp.exp(-pre_gate))
            silu = pre_gate * sigmoid
            hidden = (silu * pre_up).astype(jnp.bfloat16).astype(jnp.float32)
            sum_ref[kind, part, :] += jnp.sum(hidden * grads, axis=1, keepdims=True)
            grad_hidden = scale * grads
            low_gate = (grad_hidden * pre_up * (sigmoid + silu * (1.0 - sigmoid))).astype(
                jnp.bfloat16
            )
            low_up = (grad_hidden * silu).astype(jnp.bfloat16)
            gate_all[part, columns_here] = low_gate
            up_all[part, columns_here] = low_up
            low_hidden = (scale * hidden).astype(jnp.bfloat16)
            hidden_all[part, columns_here] = low_hidden
            hidden_out[part, :] = low_hidden
            gate_out[part, :] = low_gate
            up_out[part, :] = low_up

    @pl.when(step == tiles - 1)
    def _():
        grad_logits = jnp.zeros_like(prob_ref)
        for k in (0, 1):
            own = jnp.where(lane == experts_ref[k], 1.0, 0.0)
            grad_logits += scale_ref[k] * sum_ref[k] * (own - prob_ref[...])
        logit_out[...] = grad_logits.astype(jnp.bfloat16)

    @pl.when((step >= tiles) & (step < tiles + columns))
    def _():
        some = pl.ds(pl.multiple_of((step - tiles) * 2 * TILE, TILE), 2 * TILE)
        grads = wide_dot(gate_all[...], gate_row[...]) + wide_dot(up_all[...], up_row[...])
        grads += dot_turned(logit_out[...], router_ref[some, :])
        grads = grads.astype(jnp.bfloat16)
        for k in range(pieces):
            grad_refs[k][...] = grads[k * size : (k + 1) * size]

    @pl.when(step >= tiles + columns)
    def _():
        result = wide_dot(hidden_all[...], down_row[...]).astype(jnp.bfloat16)
        for k in range(pieces):
            out_refs[k][...] = result[k * size : (k + 1) * size]


def mlp_plane(distance, joined, experts, routed, rows, down_grad, router, weights, kept, others):
    gate, up, down = weights
    pieces = len(rows)
    size, depth = rows[0].shape
    width = gate.shape[0]
    tiles, columns = width // TILE, depth // (2 * TILE)
    total = pieces * size
    low = jnp.bfloat16

    def early(i):
        return jnp.minimum(i, tiles - 1)

    def late(i):
        return jnp.clip(i - tiles, 0, columns - 1)

    def last(i):
        return jnp.maximum(i - tiles - columns, 0)

    tile_spec = pl.BlockSpec((total, TILE), lambda i: (distance, early(i)))
    weight_tile = pl.BlockSpec((TILE, depth), lambda i: (early(i), 0))
    if joined:
        result_specs = [
            pl.BlockSpec((size, 2 * TILE), lambda i: (0, jnp.maximum(i - tiles, 0)))
        ] * pieces
        result_shapes = [jax.ShapeDtypeStruct((size, 2 * depth), low)] * pieces
    else:
        result_specs = [pl.BlockSpec((size, 2 * TILE), lambda i: (0, late(i)))] * pieces + [
            pl.BlockSpec((size, 2 * TILE), lambda i: (0, last(i)))
        ] * pieces
        result_shapes = [jax.ShapeDtypeStruct((size, depth), low)] * (2 * pieces)
    first_kept = 2 + pieces + 7
    results = pl.pallas_call(
        functools.partial(
            mlp_kernel, tiles, columns, joined, pieces, len(kept) + len(others)
        ),
        grid=(tiles + 2 * columns,),
        in_specs=[pl.BlockSpec(memory_space=pltpu.SMEM), whole(routed)]
        + in_place(pieces)
        + [
            pl.BlockSpec((depth, 128), lambda i: (0, router.shape[1] // 128 - 1)),
            weight_tile,
            weight_tile,
            tile_spec,
            pl.BlockSpec((width, 2 * TILE), lambda i: (0, late(i))),
            pl.BlockSpec((width, 2 * TILE), lambda i: (0, late(i))),
            pl.BlockSpec((width, 2 * TILE), lambda i: (0, last(i))),
        ]
        + in_place(len(kept) + len(others)),
        out_specs=result_specs
        + [
            pl.BlockSpec((total, depth), lambda i: (distance, 0)),
            tile_spec,
            tile_spec,
            tile_spec,
            pl.BlockSpec((total, 128), lambda i: (distance, 0)),
        ],
        out_shape=result_shapes
        + [
            jax.ShapeDtypeStruct((RINGS * total, many), low)
            for many in (depth, width, width, width, 128)
        ],
        scratch_shapes=[pltpu.VMEM((total, width), low)] * 3
        + [
            pltpu.VMEM((total, 128), jnp.float32),
            pltpu.VMEM((3, total, 1), jnp.float32),
            pltpu.VMEM((3, total, 1), jnp.float32),
            pltpu.SemaphoreType.DMA((pieces,)),
        ],
        input_output_aliases={
            first_kept + k: len(result_shapes) + k for k in range(len(kept))
        },
        compiler_params=pltpu.CompilerParams(vmem_limit_bytes=56 * 1024 * 1024),
        cost_estimate=pl.CostEstimate(
            flops=2 * total * depth * width * 5,
            bytes_accessed=2 * (5 * depth * width + 4 * total * depth + 4 * total * width),
            transcendentals=total * width,
        ),
    )(experts, routed, *rows, router, gate, up, down_grad, gate, up, down, *kept, *others)
    count = len(result_shapes)
    return results[:pieces], results[pieces:count], results[count:]


def gather_body(
    block_input,
    segments,
    counts,
    routes,
    attn_gain,
    w_query,
    w_latent,
    latent_gain,
    w_keyval,
    w_output,
    ffn_gain,
    w_router,
    shared_gate_up,
    shared_down,
    expert_gate_up,
    expert_down,
    cotangent,
):
    f32 = jnp.float32
    bf16 = jnp.bfloat16
    blocks = 16
    index = lax.axis_index("dp")
    x = lax.axis_index("tensor")
    coords = jnp.stack([index // 4, (index // 2) % 2, index % 2]).astype(jnp.int32)
    core = coords[2]
    place = jnp.concatenate([coords, x.astype(jnp.int32)[None], counts])
    local_rows = block_input.shape[0]
    tokens = 2 * local_rows
    depth = w_query.shape[0]
    query_width = w_query.shape[1]
    heads = query_width // (NOPE + ROPE)
    experts = w_router.shape[1]
    units = expert_gate_up.shape[3]
    shared = shared_gate_up.shape[2] // blocks
    latent_depth = w_keyval.shape[0]

    used = query_width + KVR + ROPE
    small = jnp.concatenate(
        [
            attn_gain[:, None],
            ffn_gain[:, None],
            jnp.pad(latent_gain, (0, depth - latent_depth))[:, None],
            w_router,
            routes.reshape(depth, -1).astype(bf16),
            jnp.zeros((depth, 128 - ROPE - 3 - experts - 2 * TOP), bf16),
        ],
        axis=1,
    )
    first_width = query_width + KVR + 128
    shards = pack_weights(w_query, w_latent, small, w_keyval, w_output)
    held = ring_shards(shards)
    other_input = other_x(block_input)
    expert_in = expert_gate_up.swapaxes(2, 3)
    expert_in_other = other_core(expert_in)
    expert_down_other = other_core(expert_down)
    chunks = gather_weight(held)
    grad_planes = gather_rows(cotangent, "xxxx")

    shared_near = lax.all_to_all(
        pack_shared(shared_gate_up, shared_down, blocks, ()),
        "dp",
        split_axis=0,
        concat_axis=0,
        tiled=True,
    )
    shared_far = other_core(shared_near)

    gate_weight, up_weight, down_weight = pack_units(
        expert_in,
        expert_in_other,
        expert_down,
        expert_down_other,
        shared_near,
        shared_far,
        shared,
        (),
    )
    half_kept = down_grads(
        0,
        [piece for plane in grad_planes[:2] for piece in plane],
        down_weight,
        (),
        (),
    )
    down_grad, every_grad = down_grads(
        1,
        [piece for plane in grad_planes[2:] for piece in plane],
        down_weight,
        half_kept,
        (),
    )
    cosine, sine = rotary_tables(segments[0], ROPE)
    cosine = jnp.tile(cosine, (1, heads))
    sine = jnp.tile(sine, (1, heads))
    sizes = (depth, query_width, used, latent_depth, w_keyval.shape[1] * latent_depth // depth, first_width)
    (
        own_part,
        sent_part,
        first_weight,
        keyval_weight,
        output_turned,
        first_normed,
        nope,
        turned_query,
        latent,
        key,
        keyval,
        total,
        attended,
        gains,
        latent_gain_row,
    ) = attend_forward(
        place,
        segments,
        cosine,
        sine,
        block_input,
        other_input,
        chunks,
        heads,
        sizes,
        (down_grad,),
    )
    attn_gain_wide, ffn_gain_wide = gains[0], gains[1]
    mixed = block_input.astype(f32) + own_part + other_x(sent_part).astype(f32)
    second_scale = rms_scale(mixed)
    second_unit = mixed * second_scale
    second_normed = (second_unit * ffn_gain_wide).astype(bf16)

    routes_at = used + 3 + experts
    routes_all = first_weight[:, routes_at : routes_at + 2 * TOP].reshape(blocks * tokens, TOP)
    chip_experts = jnp.stack([index, index + 1 - 2 * core]).astype(jnp.int32)
    routed_all = jnp.any(
        routes_all[None] == chip_experts[:, None, None].astype(bf16), axis=2
    ).astype(f32)
    order = jnp.stack(
        [
            place_of(coords, (distance, flip_y, 0)) * 2 + (1 - x if flip_x else x)
            for distance in range(RINGS)
            for flip_x, flip_y in ((0, 0), (0, 1), (1, 0), (1, 1))
        ]
    )
    routed = jnp.stack(
        [
            pick_blocks(one.reshape(blocks * 2, local_rows), order).reshape(RINGS, -1)
            for one in routed_all
        ],
        axis=2,
    )

    corners = "yxyx"
    row_planes = gather_rows(second_normed, corners, True)
    expert_ids = jnp.concatenate(
        [chip_experts, jnp.array([experts, used + 3 - query_width - KVR], jnp.int32)]
    )
    kept = []
    turned, closed = [], []
    for distance in range(RINGS):
        others = [row_planes[3][0]] if distance == 0 else []
        if distance == 2:
            others = list(turned[0][1:])
        elif distance == 3:
            others = list(turned[1][1:]) + list(closed[0][1:])
        grads, outs, kept = mlp_plane(
            distance,
            distance < RINGS - 1,
            expert_ids,
            routed[distance],
            row_planes[distance],
            down_grad,
            first_weight,
            (gate_weight, up_weight, down_weight),
            kept,
            others,
        )
        turned.append(turn_corner(grads, corners[distance]))
        if distance < RINGS - 1:
            closed.append(close_plane(turned[distance]))
    every_row, every_hidden, every_gate_grad, every_up_grad, logit_grads = kept
    shared_kept, shared_sent, logit_rows = side_grads(
        every_row,
        every_grad,
        every_gate_grad,
        every_up_grad,
        every_hidden,
        logit_grads,
        shared,
        blocks,
    )
    sent_in = expert_grads((every_gate_grad, every_up_grad), every_row, units, 1, None, bf16)
    sent_down = expert_grads((every_hidden,), every_grad, units, 1, None, bf16)
    moving = ring_step(wide_sum(*closed[1]).astype(bf16))
    moving = ring_step(wide_sum(moving, *closed[2]).astype(bf16))
    own, beside, across = turned[3]
    own = after(own, sent_in)
    grad_close = close_plane((own, after(beside, shared_sent), across))
    grad_second = wide_sum(
        ring_step(wide_sum(moving[:, :D], *grad_close).astype(bf16)),
        after(closed[0][0], sent_down)[:, :D],
        *[part[:, :D] for part in closed[0][1:]],
    )
    outs = list(outs)
    outs[3] = after(outs[3], grad_close[1])
    out_close = close_plane(turn_corner(outs, corners[3]))
    block_output = mixed + wide_sum(
        ring_step(wide_sum(moving[:, D:], *out_close).astype(bf16)),
        *[part[:, D:] for part in closed[0]],
    )

    arrived_in = other_core(sent_in)
    arrived_down = other_core(sent_down)
    router_at = used + 3 - query_width - KVR
    grad_router = logit_rows[router_at : router_at + experts]
    shared_grads = lax.all_to_all(
        add_low(shared_kept, other_core(shared_sent)), "dp", split_axis=0, concat_axis=0, tiled=True
    )

    gain_ffn_part = jnp.sum(grad_second * second_unit, axis=0)
    grad_mixed = cotangent.astype(f32) + rms_back(
        grad_second * ffn_gain_wide, second_unit, second_scale
    )
    grad_mixed_low = grad_mixed.astype(bf16)
    other_grad = other_x(grad_mixed_low)

    places = jnp.stack([place_of(coords, key_of) for key_of in weight_keys()]).astype(jnp.int32)
    projected_grad, keyval_grad, latent_normed, gain_latent_part = attend_back(
        place,
        segments,
        cosine,
        sine,
        grad_mixed_low,
        other_grad,
        (keyval_weight, output_turned, nope, turned_query, latent, key, keyval, total, latent_gain_row),
        heads,
        first_width,
    )
    grad_attn = jnp.concatenate(
        [
            jnp.where(x == 0, grad_mixed_low, other_grad),
            jnp.where(x == 0, other_grad, grad_mixed_low),
        ],
        axis=0,
    )
    ring_places = places.reshape(2, 2, RINGS).swapaxes(1, 2).reshape(-1)
    other_parts = (latent_normed, keyval_grad, grad_attn, attended, ring_places)
    other_arrived = other_core(other_grads(*other_parts, 8, 8))
    own_first, sent_first, gain_attn_part = first_back(
        place, block_input, other_input, projected_grad, first_weight
    )
    grad_first = own_first + other_x(sent_first).astype(f32)
    small_rows = jnp.concatenate(
        [
            jnp.zeros((ROPE, D), f32),
            gain_attn_part,
            gain_ffn_part[None],
            jnp.pad(
                gain_latent_part.reshape(blocks, latent_depth),
                ((0, 0), (0, depth - latent_depth)),
            ).reshape(1, D),
            grad_router,
            jnp.zeros((128 - ROPE - 3 - experts, D), f32),
        ],
        axis=0,
    )
    first_parts = (first_normed, projected_grad, small_rows, places)
    first_arrived = other_core(first_grads(*first_parts, 8, 8))
    other_kept = other_grads(*other_parts, 0, 8, other_arrived)
    far = first_grads(*first_parts, 4, 4, first_arrived)
    from_y = other_y(far)
    near = first_grads(*first_parts, 0, 4, first_arrived)
    other_summed = ring_sum(
        [other_kept[2 * r * depth : 2 * (r + 1) * depth] for r in range(RINGS)], bf16
    )
    other_closed = other_summed[:depth] + other_y(other_summed[depth:].astype(bf16)).astype(f32)
    grad_expert_down = expert_grads(
        (every_hidden,), every_grad, units, 0, arrived_down, f32, (near,)
    )
    first_closed = close_ring(near, from_y)
    grad_expert_in = expert_grads(
        (every_gate_grad, every_up_grad), every_row, units, 0, arrived_in, f32, (from_y,)
    )
    grad_shared_in, grad_shared_down = unpack_shared(shared_grads, shared, (from_y,))
    grad_expert_gate_up = grad_expert_in.swapaxes(2, 3)
    grad_expert_down = grad_expert_down[0]
    nope_width = heads * NOPE
    span = heads * (ROPE // 2)
    grad_query_weight = jnp.concatenate(
        [
            first_closed[:, :nope_width].reshape(depth, heads, NOPE),
            first_closed[:, nope_width : nope_width + span].reshape(depth, heads, -1),
            first_closed[:, nope_width + span : query_width].reshape(depth, heads, -1),
        ],
        axis=2,
    ).reshape(depth, query_width)
    both = first_closed[:, query_width:]
    both = both + other_x(both)
    grad_latent_weight = both[:, : KVR + ROPE]
    small_grads = both[:, KVR + ROPE :].T
    keyval_columns = w_keyval.shape[1] * latent_depth // depth
    grad_keyval_weight = (
        other_closed[:, :keyval_columns]
        .reshape(-1, latent_depth, keyval_columns)
        .transpose(1, 0, 2)
        .reshape(latent_depth, -1)
    )
    grad_output_weight = other_closed[:, keyval_columns:].T
    own_inputs = block_input.astype(f32)
    own_scale = rms_scale(own_inputs)
    own_unit = own_inputs * own_scale
    grad_input = grad_mixed + rms_back(grad_first * attn_gain_wide, own_unit, own_scale)
    return (
        block_output,
        grad_input,
        small_grads[0],
        grad_query_weight,
        grad_latent_weight,
        small_grads[2, :latent_depth],
        grad_keyval_weight,
        grad_output_weight,
        small_grads[1],
        small_grads[3 : 3 + experts].T,
        grad_shared_in,
        grad_shared_down,
        grad_expert_gate_up,
        grad_expert_down,
    )


def solution(mesh):
    in_specs = (
        P(("dp", "tensor"), None),
        P("dp", None),
        P("dp"),
        P("dp", None),
        P("dp"),
        P("dp", "tensor"),
        P("dp", None),
        P("dp"),
        P("dp", "tensor"),
        P("tensor", "dp"),
        P("dp"),
        P("dp", None),
        P(None, "dp", "tensor"),
        P("tensor", "dp"),
        P("dp", None, None, "tensor"),
        P("dp", "tensor", None),
        P(("dp", "tensor"), None),
    )
    out_specs = (
        P(("dp", "tensor"), None),
        P(("dp", "tensor"), None),
        P("dp"),
        P("dp", "tensor"),
        P("dp", None),
        P("dp"),
        P("dp", "tensor"),
        P("tensor", "dp"),
        P("dp"),
        P("dp", None),
        P(None, "dp", "tensor"),
        P("tensor", "dp"),
        P("dp", None, None, "tensor"),
        P("dp", "tensor", None),
    )
    body = gather_body if mesh.shape["dp"] == 16 else exchange_body
    return jax.shard_map(body, mesh=mesh, in_specs=in_specs, out_specs=out_specs, check_vma=False)
```

```python
import functools
import math

import jax
import jax.numpy as jnp
from jax import lax
from jax.experimental import pallas as pl
from jax.experimental.pallas import tpu as pltpu
from jax.sharding import PartitionSpec as P

D = 2048
NOPE = 128
ROPE = 64
VD = 128
KVR = 512
TOP = 6


EPSILON = 1e-06


def rms_scale(values):
    return lax.rsqrt(jnp.mean(values * values, axis=-1, keepdims=True) + EPSILON)


def rms_back(grad_unit, unit_rows, row_scale):
    return row_scale * (
        grad_unit - unit_rows * jnp.mean(grad_unit * unit_rows, axis=-1, keepdims=True)
    )


def rotary_tables(segment_row, width):
    count = segment_row.shape[0]
    position = jnp.arange(count, dtype=jnp.int32)
    same = segment_row[:, None] == segment_row[None, :]
    start = jnp.min(jnp.where(same, position[None, :], count), axis=1)
    offset = (position - start).astype(jnp.float32)
    freq = jnp.exp(jnp.arange(width // 2, dtype=jnp.float32) * (-2.0 * math.log(10000.0) / width))
    angle = offset[:, None] * freq[None, :]
    return (jnp.cos(angle), jnp.sin(angle))


def rotate(values, cosine, sine):
    half = values.shape[-1] // 2
    first = values[..., :half]
    second = values[..., half:]
    return jnp.concatenate(
        [first * cosine - second * sine, second * cosine + first * sine], axis=-1
    )


def rotate_back(grads, cosine, sine):
    half = grads.shape[-1] // 2
    first = grads[..., :half]
    second = grads[..., half:]
    return jnp.concatenate(
        [first * cosine + second * sine, second * cosine - first * sine], axis=-1
    )


def allowed_pairs(segment_row, count):
    position = jnp.arange(segment_row.shape[0], dtype=jnp.int32)
    live = position < count
    same = segment_row[:, None] == segment_row[None, :]
    causal = position[None, :] <= position[:, None]
    return same & causal & live[:, None] & live[None, :] | (position[:, None] == position[None, :])


def attention_scores(query_rows, key_nope, key_rope, allowed, scale):
    scores = jnp.einsum(
        "ihd,jhd->hij", query_rows[..., :NOPE], key_nope, preferred_element_type=jnp.float32
    )
    scores = scores + jnp.einsum(
        "ihd,jd->hij", query_rows[..., NOPE:], key_rope, preferred_element_type=jnp.float32
    )
    return jnp.where(allowed[None], scores * scale, -1e30)


def swiglu_back(gate, upper, grad_hidden, axis):
    sigmoid = jax.nn.sigmoid(gate)
    grad_gate = grad_hidden * upper * sigmoid * (1.0 + gate * (1.0 - sigmoid))
    grad_upper = grad_hidden * gate * sigmoid
    return jnp.stack([grad_gate, grad_upper], axis=axis)


def slot_layout(routes, experts, capacity):
    tokens = routes.shape[0]
    flat = routes.reshape(-1)
    onehot = (flat[:, None] == jnp.arange(experts, dtype=jnp.int32)[None, :]).astype(jnp.int32)
    rank = jnp.arange(flat.shape[0], dtype=jnp.int32)
    earlier = (rank[None, :] < rank[:, None]).astype(jnp.bfloat16)
    before = jnp.dot(
        earlier, onehot.astype(jnp.bfloat16), preferred_element_type=jnp.float32
    ).astype(jnp.int32)
    slot_index = jnp.sum(before * onehot, axis=1)
    target = flat * capacity + slot_index
    token_ids = jnp.arange(flat.shape[0], dtype=jnp.int32) // routes.shape[1]
    owner = jnp.full((experts * capacity,), tokens, jnp.int32).at[target].set(token_ids)
    return (slot_index, target, owner)


def to_expert_major(arrived, groups, local_experts):
    capacity = arrived.shape[1]
    width = arrived.shape[2]
    return (
        arrived.reshape(groups, local_experts, capacity, width)
        .transpose(1, 0, 2, 3)
        .reshape(local_experts, groups * capacity, width)
    )


def from_expert_major(results, groups):
    local_experts = results.shape[0]
    width = results.shape[2]
    capacity = results.shape[1] // groups
    return (
        results.reshape(local_experts, groups, capacity, width)
        .transpose(1, 0, 2, 3)
        .reshape(groups * local_experts, capacity, width)
    )


def exchange_body(
    block_input,
    segments,
    counts,
    routes,
    attn_gain,
    w_query,
    w_latent,
    latent_gain,
    w_keyval,
    w_output,
    ffn_gain,
    w_router,
    shared_gate_up,
    shared_down,
    expert_gate_up,
    expert_down,
    cotangent,
):
    gathered = (
        lax.all_gather(attn_gain, "dp", axis=0, tiled=True),
        lax.all_gather(w_query, "dp", axis=0, tiled=True),
        lax.all_gather(w_latent, "dp", axis=0, tiled=True),
        lax.all_gather(latent_gain, "dp", axis=0, tiled=True),
        lax.all_gather(w_keyval, "dp", axis=0, tiled=True),
        lax.all_gather(w_output, "dp", axis=1, tiled=True),
        lax.all_gather(ffn_gain, "dp", axis=0, tiled=True),
        lax.all_gather(w_router, "dp", axis=0, tiled=True),
        lax.all_gather(shared_gate_up, "dp", axis=1, tiled=True),
        lax.all_gather(shared_down, "dp", axis=1, tiled=True),
    )
    (
        full_attn_gain,
        query_weight,
        latent_weight,
        full_latent_gain,
        keyval_weight,
        output_weight,
        full_ffn_gain,
        router_weight,
        shared_in,
        shared_out,
    ) = gathered
    tensor_rank = lax.axis_index("tensor")
    dp_size = lax.axis_size("dp")
    rows_all = lax.all_gather(block_input, "tensor", axis=0, tiled=True)
    tokens = rows_all.shape[0]
    local_rows = block_input.shape[0]
    heads = query_weight.shape[1] // (NOPE + ROPE)
    experts = router_weight.shape[1]
    local_experts = expert_gate_up.shape[0]
    capacity = 2 * tokens * TOP // experts
    scale = (NOPE + ROPE) ** (-0.5)
    start = tensor_rank * local_rows
    cosine, sine = rotary_tables(segments[0], ROPE)
    allowed = allowed_pairs(segments[0], counts[0])
    attn_gain_wide = full_attn_gain.astype(jnp.float32)
    latent_gain_wide = full_latent_gain.astype(jnp.float32)
    ffn_gain_wide = full_ffn_gain.astype(jnp.float32)
    inputs = rows_all.astype(jnp.float32)
    first_scale = rms_scale(inputs)
    first_unit = inputs * first_scale
    first_normed = (first_unit * attn_gain_wide).astype(jnp.bfloat16)
    query = jnp.dot(first_normed, query_weight, preferred_element_type=jnp.float32).reshape(
        tokens, heads, NOPE + ROPE
    )
    query_rows = jnp.concatenate(
        [query[..., :NOPE], rotate(query[..., NOPE:], cosine[:, None, :], sine[:, None, :])],
        axis=-1,
    ).astype(jnp.bfloat16)
    latent_all = jnp.dot(first_normed, latent_weight, preferred_element_type=jnp.float32)
    latent = latent_all[:, :KVR]
    key_rope = rotate(latent_all[:, KVR:], cosine, sine).astype(jnp.bfloat16)
    latent_scale = rms_scale(latent)
    latent_unit = latent * latent_scale
    latent_normed = (latent_unit * latent_gain_wide).astype(jnp.bfloat16)
    keyval = (
        jnp.dot(latent_normed, keyval_weight, preferred_element_type=jnp.float32)
        .astype(jnp.bfloat16)
        .reshape(tokens, heads, NOPE + VD)
    )
    key_nope = keyval[..., :NOPE]
    values = keyval[..., NOPE:]
    scores = attention_scores(query_rows, key_nope, key_rope, allowed, scale)
    row_max = jnp.max(scores, axis=-1, keepdims=True)
    log_total = row_max + jnp.log(jnp.sum(jnp.exp(scores - row_max), axis=-1, keepdims=True))
    weights_low = jnp.exp(scores - log_total).astype(jnp.bfloat16)
    attended = (
        jnp.einsum("hij,jhd->ihd", weights_low, values, preferred_element_type=jnp.float32)
        .astype(jnp.bfloat16)
        .reshape(tokens, heads * VD)
    )
    attn_part = jnp.dot(attended, output_weight, preferred_element_type=jnp.float32)
    mixed = inputs + lax.psum(attn_part, "tensor")
    second_scale = rms_scale(mixed)
    second_unit = mixed * second_scale
    second_normed = (second_unit * ffn_gain_wide).astype(jnp.bfloat16)
    logits = jnp.dot(second_normed, router_weight, preferred_element_type=jnp.float32)
    probabilities = jax.nn.softmax(logits, axis=-1)
    gate_values = jnp.take_along_axis(probabilities, routes, axis=1)
    shared_pre = jnp.einsum(
        "td,gdf->tgf", second_normed, shared_in, preferred_element_type=jnp.float32
    )
    shared_hidden = (jax.nn.silu(shared_pre[:, 0]) * shared_pre[:, 1]).astype(jnp.bfloat16)
    shared_part = jnp.dot(shared_hidden, shared_out, preferred_element_type=jnp.float32)
    slot_index, target, owner = slot_layout(routes, experts, capacity)
    owner_grid = owner.reshape(experts, capacity)
    padded_rows = jnp.concatenate([second_normed, jnp.zeros((1, D), jnp.bfloat16)], axis=0)
    outgoing = padded_rows[owner_grid]
    arrived = lax.all_to_all(outgoing, "dp", split_axis=0, concat_axis=0, tiled=True)
    expert_rows = to_expert_major(arrived, dp_size, local_experts)
    expert_pre = jnp.einsum(
        "erd,egdf->ergf", expert_rows, expert_gate_up, preferred_element_type=jnp.float32
    )
    expert_hidden = (jax.nn.silu(expert_pre[:, :, 0]) * expert_pre[:, :, 1]).astype(jnp.bfloat16)
    expert_result = jnp.einsum(
        "erf,efd->erd", expert_hidden, expert_down, preferred_element_type=jnp.float32
    )
    returning = from_expert_major(expert_result, dp_size)
    returned = lax.all_to_all(
        returning.astype(jnp.bfloat16), "dp", split_axis=0, concat_axis=0, tiled=True
    ).astype(returning.dtype)
    padded_back = jnp.concatenate([returned.reshape(-1, D), jnp.zeros((1, D), jnp.float32)], axis=0)
    picked = padded_back[target].reshape(tokens, TOP, D)
    routed_part = jnp.sum(gate_values[:, :, None] * picked, axis=1)
    branch_sum = lax.psum_scatter(
        (shared_part + routed_part).astype(jnp.bfloat16), "tensor", scatter_dimension=0, tiled=True
    ).astype(jnp.float32)
    block_output = lax.dynamic_slice_in_dim(mixed, start, local_rows, 0) + branch_sum
    grad_rows = lax.all_gather(cotangent, "tensor", axis=0, tiled=True)
    grad_out = grad_rows.astype(jnp.float32)
    grad_shared_hidden = jnp.dot(grad_rows, shared_out.T, preferred_element_type=jnp.float32)
    grad_shared_out = jnp.dot(shared_hidden.T, grad_rows, preferred_element_type=jnp.float32)
    grad_shared_pre = swiglu_back(shared_pre[:, 0], shared_pre[:, 1], grad_shared_hidden, 1).astype(
        jnp.bfloat16
    )
    grad_shared_in = jnp.einsum(
        "td,tgf->gdf", second_normed, grad_shared_pre, preferred_element_type=jnp.float32
    )
    grad_second = jnp.einsum(
        "tgf,gdf->td", grad_shared_pre, shared_in, preferred_element_type=jnp.float32
    )
    gate_by_slot = (
        jnp.zeros((experts * capacity + 1,), jnp.float32).at[target].set(gate_values.reshape(-1))
    )
    slot_ids = jnp.arange(experts * capacity, dtype=jnp.int32).reshape(experts, capacity)
    padded_grad = jnp.concatenate([grad_out, jnp.zeros((1, D), jnp.float32)], axis=0)
    grad_outgoing = (gate_by_slot[slot_ids][..., None] * padded_grad[owner_grid]).astype(
        jnp.bfloat16
    )
    grad_arrived = lax.all_to_all(grad_outgoing, "dp", split_axis=0, concat_axis=0, tiled=True)
    grad_expert_rows = to_expert_major(grad_arrived, dp_size, local_experts)
    grad_expert_hidden = jnp.einsum(
        "erd,efd->erf", grad_expert_rows, expert_down, preferred_element_type=jnp.float32
    )
    grad_expert_down = jnp.einsum(
        "erf,erd->efd", expert_hidden, grad_expert_rows, preferred_element_type=jnp.float32
    )
    grad_expert_pre = swiglu_back(
        expert_pre[:, :, 0], expert_pre[:, :, 1], grad_expert_hidden, 2
    ).astype(jnp.bfloat16)
    grad_expert_gate_up = jnp.einsum(
        "erd,ergf->egdf", expert_rows, grad_expert_pre, preferred_element_type=jnp.float32
    )
    grad_expert_input = jnp.einsum(
        "ergf,egdf->erd", grad_expert_pre, expert_gate_up, preferred_element_type=jnp.float32
    )
    grad_returning = from_expert_major(grad_expert_input, dp_size)
    grad_returned = lax.all_to_all(
        grad_returning.astype(jnp.bfloat16), "dp", split_axis=0, concat_axis=0, tiled=True
    ).astype(grad_returning.dtype)
    padded_grad_back = jnp.concatenate(
        [grad_returned.reshape(-1, D), jnp.zeros((1, D), jnp.float32)], axis=0
    )
    grad_second = grad_second + jnp.sum(padded_grad_back[target].reshape(tokens, TOP, D), axis=1)
    grad_gates = jnp.sum(grad_out[:, None, :] * picked, axis=-1)
    grad_second, grad_gates = (
        lax.psum(grad_second.astype(jnp.bfloat16), "tensor").astype(jnp.float32),
        lax.psum(grad_gates.astype(jnp.bfloat16), "tensor").astype(jnp.float32),
    )
    chosen = (routes[:, :, None] == jnp.arange(experts, dtype=jnp.int32)[None, None, :]).astype(
        jnp.float32
    )
    grad_probabilities = jnp.sum(chosen * grad_gates[:, :, None], axis=1)
    grad_logits = probabilities * (
        grad_probabilities - jnp.sum(probabilities * grad_probabilities, axis=-1, keepdims=True)
    )
    grad_logits_low = grad_logits.astype(jnp.bfloat16)
    grad_router = jnp.dot(second_normed.T, grad_logits_low, preferred_element_type=jnp.float32)
    grad_second = grad_second + jnp.dot(
        grad_logits_low, router_weight.T, preferred_element_type=jnp.float32
    )
    gain_ffn_grad = jnp.sum(grad_second * second_unit, axis=0)
    grad_mixed = grad_out + rms_back(grad_second * ffn_gain_wide, second_unit, second_scale)
    grad_attn_low = grad_mixed.astype(jnp.bfloat16)
    grad_output_weight = jnp.dot(attended.T, grad_attn_low, preferred_element_type=jnp.float32)
    grad_attended = (
        jnp.dot(grad_attn_low, output_weight.T, preferred_element_type=jnp.float32)
        .astype(jnp.bfloat16)
        .reshape(tokens, heads, VD)
    )
    scores = attention_scores(query_rows, key_nope, key_rope, allowed, scale)
    weights = jnp.exp(scores - log_total)
    weights_low = weights.astype(jnp.bfloat16)
    grad_weights = jnp.einsum(
        "ihd,jhd->hij", grad_attended, values, preferred_element_type=jnp.float32
    )
    grad_values = jnp.einsum(
        "hij,ihd->jhd", weights_low, grad_attended, preferred_element_type=jnp.float32
    )
    grad_scores = (
        weights * (grad_weights - jnp.sum(weights * grad_weights, axis=-1, keepdims=True))
    ).astype(jnp.bfloat16)
    grad_query_nope = (
        jnp.einsum("hij,jhd->ihd", grad_scores, key_nope, preferred_element_type=jnp.float32)
        * scale
    )
    grad_query_rope = (
        jnp.einsum("hij,jd->ihd", grad_scores, key_rope, preferred_element_type=jnp.float32) * scale
    )
    grad_key_nope = (
        jnp.einsum(
            "hij,ihd->jhd", grad_scores, query_rows[..., :NOPE], preferred_element_type=jnp.float32
        )
        * scale
    )
    grad_key_rope = (
        jnp.einsum(
            "hij,ihd->jd", grad_scores, query_rows[..., NOPE:], preferred_element_type=jnp.float32
        )
        * scale
    )
    grad_query = (
        jnp.concatenate(
            [grad_query_nope, rotate_back(grad_query_rope, cosine[:, None, :], sine[:, None, :])],
            axis=-1,
        )
        .astype(jnp.bfloat16)
        .reshape(tokens, heads * (NOPE + ROPE))
    )
    grad_query_weight = jnp.dot(first_normed.T, grad_query, preferred_element_type=jnp.float32)
    grad_first = jnp.dot(grad_query, query_weight.T, preferred_element_type=jnp.float32)
    grad_keyval = (
        jnp.concatenate([grad_key_nope, grad_values], axis=-1)
        .astype(jnp.bfloat16)
        .reshape(tokens, heads * (NOPE + VD))
    )
    grad_keyval_weight = jnp.dot(latent_normed.T, grad_keyval, preferred_element_type=jnp.float32)
    grad_latent_normed = jnp.dot(grad_keyval, keyval_weight.T, preferred_element_type=jnp.float32)
    gain_latent_part = jnp.sum(grad_latent_normed * latent_unit, axis=0)
    grad_latent = rms_back(grad_latent_normed * latent_gain_wide, latent_unit, latent_scale)
    grad_latent_all = jnp.concatenate(
        [grad_latent, rotate_back(grad_key_rope, cosine, sine)], axis=-1
    )
    grad_first, grad_latent_all, gain_latent_grad = (
        lax.psum(grad_first.astype(jnp.bfloat16), "tensor").astype(jnp.float32),
        lax.psum(grad_latent_all.astype(jnp.bfloat16), "tensor").astype(jnp.float32),
        lax.psum(gain_latent_part.astype(jnp.bfloat16), "tensor").astype(jnp.float32),
    )
    grad_latent_low = grad_latent_all.astype(jnp.bfloat16)
    grad_latent_weight = jnp.dot(
        first_normed.T, grad_latent_low, preferred_element_type=jnp.float32
    )
    grad_first = grad_first + jnp.dot(
        grad_latent_low, latent_weight.T, preferred_element_type=jnp.float32
    )
    gain_attn_grad = jnp.sum(grad_first * first_unit, axis=0)
    grad_inputs = grad_mixed + rms_back(grad_first * attn_gain_wide, first_unit, first_scale)
    grad_local = lax.dynamic_slice_in_dim(grad_inputs, start, local_rows, 0)
    summed = (
        lax.psum_scatter(gain_attn_grad, "dp", scatter_dimension=0, tiled=True),
        lax.psum_scatter(grad_query_weight, "dp", scatter_dimension=0, tiled=True),
        lax.psum_scatter(grad_latent_weight, "dp", scatter_dimension=0, tiled=True),
        lax.psum_scatter(gain_latent_grad, "dp", scatter_dimension=0, tiled=True),
        lax.psum_scatter(grad_keyval_weight, "dp", scatter_dimension=0, tiled=True),
        lax.psum_scatter(grad_output_weight, "dp", scatter_dimension=1, tiled=True),
        lax.psum_scatter(gain_ffn_grad, "dp", scatter_dimension=0, tiled=True),
        lax.psum_scatter(grad_router, "dp", scatter_dimension=0, tiled=True),
        lax.psum_scatter(grad_shared_in, "dp", scatter_dimension=1, tiled=True),
        lax.psum_scatter(grad_shared_out, "dp", scatter_dimension=1, tiled=True),
    )
    return (
        block_output,
        grad_local,
        summed[0],
        summed[1],
        summed[2],
        summed[3],
        summed[4],
        summed[5],
        summed[6],
        summed[7],
        summed[8],
        summed[9],
        grad_expert_gate_up,
        grad_expert_down,
    )


RINGS = 4


def ring_step(values):
    return lax.ppermute(values, "dp", [(i, (i + RINGS) % 16) for i in range(16)])


def other_y(values):
    return lax.ppermute(values, "dp", [(i, i ^ 2) for i in range(16)])


def other_core(values):
    return lax.ppermute(values, "dp", [(i, i ^ 1) for i in range(16)])


def other_x(values):
    return lax.ppermute(values, "tensor", [(0, 1), (1, 0)])


def fence_kernel(*refs):
    pass


def after(values, *others):
    anywhere = pl.BlockSpec(memory_space=pl.ANY)
    return pl.pallas_call(
        fence_kernel,
        out_shape=jax.ShapeDtypeStruct(values.shape, values.dtype),
        in_specs=[anywhere] * (1 + len(others)),
        out_specs=anywhere,
        input_output_aliases={0: 0},
    )(values, *others)


def gather_rows(rows, corners, eager=False):
    planes = []
    current = rows
    for distance in range(RINGS):
        if distance > 1 and eager:
            current = after(current, *planes[distance - 2][1:3])
        if distance:
            current = ring_step(current)
        beside = other_y(current)
        across = other_x(current)
        corner = other_x(beside) if corners[distance] == "x" else other_y(across)
        planes.append((current, beside, across, corner))
    return planes


def add_low(first, second):
    return (first.astype(jnp.float32) + second.astype(jnp.float32)).astype(jnp.bfloat16)


def turn_corner(plane, direction):
    own, beside, across, corner = plane
    if direction == "x":
        return own, add_low(beside, other_x(corner)), across
    return own, beside, add_low(across, other_y(corner))


def close_plane(turned):
    own, beside, across = turned
    return own, other_y(beside), other_x(across)


def wide_sum(*values):
    total = values[0].astype(jnp.float32)
    for value in values[1:]:
        total = total + value.astype(jnp.float32)
    return total


def ring_sum(parts, low):
    moving = parts[1]
    for distance in (2, 3, 0):
        moving = ring_step(moving.astype(low)).astype(jnp.float32) + parts[distance].astype(
            jnp.float32
        )
    return moving


def ring_shards(shard):
    held = [shard]
    for _ in range(RINGS - 1):
        held.append(ring_step(held[-1]))
    return held


def gather_weight(held, early):
    chunks = []
    beside = None
    for distance, current in enumerate(held):
        if distance:
            current_after = after(current, beside, *(early if distance == 2 else ()))
        beside = other_y(current_after if distance else current)
        for flip_y, chunk in ((0, current), (1, beside)):
            for flip_core, piece in ((0, chunk), (1, other_core(chunk))):
                chunks.append(((distance, flip_y, flip_core), piece))
    return chunks


def place_of(coords, key):
    z, y, core = coords
    distance, flip_y, flip_core = key
    return (
        lax.rem(z + RINGS - distance, RINGS) * 4
        + (1 - y if flip_y else y) * 2
        + (1 - core if flip_core else core)
    )


def weight_keys():
    return [
        (distance, flip_y, flip_core)
        for flip_core in (0, 1)
        for flip_y in (0, 1)
        for distance in range(RINGS)
    ]


def scatter_blocks(grads, low):
    half = grads.shape[0] // 2
    total = grads[:half].astype(jnp.float32) + other_core(grads[half:].astype(low)).astype(
        jnp.float32
    )
    quarter = half // 2
    total = total[:quarter] + other_y(total[quarter:].astype(low)).astype(jnp.float32)
    size = quarter // RINGS
    return ring_sum([total[r * size : (r + 1) * size] for r in range(RINGS)], low)


def pick_blocks(values, order):
    chosen = order[:, None] == jnp.arange(values.shape[0], dtype=jnp.int32)[None, :]
    chosen = chosen.reshape(chosen.shape + (1,) * (values.ndim - 1))
    return jnp.sum(jnp.where(chosen, values[None], 0.0), axis=1)


def wide_dot(left, right):
    return jnp.dot(left, right, preferred_element_type=jnp.float32)


def dot_turned(left, right):
    return lax.dot_general(left, right, (((1,), (1,)), ((), ())), preferred_element_type=jnp.float32)


def dot_rows(left, right):
    return lax.dot_general(left, right, (((0,), (0,)), ((), ())), preferred_element_type=jnp.float32)


TILE = 256


def whole(array):
    return pl.BlockSpec(array.shape, lambda *i: (0,) * array.ndim)


def in_vmem(count):
    return [pl.BlockSpec(memory_space=pltpu.VMEM)] * count


def in_place(count):
    return [pl.BlockSpec(memory_space=pl.ANY)] * count


def head_scores(heads, h, nope_ref, turned_ref, keyval_ref, key_ref, masks):
    span = ROPE // 2 * heads
    column = pl.ds(pl.multiple_of(h * NOPE, NOPE), NOPE)
    key_column = pl.ds(pl.multiple_of(h * (NOPE + VD), NOPE), NOPE)
    scores = dot_turned(nope_ref[:, column], keyval_ref[:, key_column])
    for k in (0, 1):
        part = turned_ref[:, k * span : (k + 1) * span]
        part = jnp.where(masks, part, jnp.zeros_like(part))
        scores += dot_turned(part, key_ref[:, k * span : (k + 1) * span])
    return scores * (NOPE + ROPE) ** (-0.5)


def head_lanes(heads, h):
    span = ROPE // 2 * heads
    lane = lax.broadcasted_iota(jnp.int32, (1, span), 1)
    return (lane >= h * (ROPE // 2)) & (lane < (h + 1) * (ROPE // 2))


def allowed_rows(count, segment_row, segment_column):
    tokens = segment_row.shape[1]
    column = lax.broadcasted_iota(jnp.int32, (tokens, tokens), 0)
    row = lax.broadcasted_iota(jnp.int32, (tokens, tokens), 1)
    live = (column < count) & (row < count) & (row <= column)
    return (segment_row == segment_column) & live | (column == row)


def attend_kernel(
    keys,
    extra,
    heads,
    sizes,
    place_ref,
    segment_row_ref,
    segment_column_ref,
    cosine_ref,
    sine_ref,
    own_ref,
    other_ref,
    *refs,
):
    depth, query_width, used, latent_depth, keyval_part, first_width = sizes
    chunks = refs[: len(keys)]
    (
        own_out,
        sent_out,
        first_ref,
        keyval_weight_ref,
        output_ref,
        normed_ref,
        nope_ref,
        turned_ref,
        latent_ref,
        key_ref,
        keyval_ref,
        total_ref,
        attended_ref,
        gains_ref,
        latent_gain_ref,
        semaphores,
    ) = refs[len(keys) + extra :]
    f32, bf16 = jnp.float32, jnp.bfloat16
    local_rows = own_ref.shape[0]
    tokens = 2 * local_rows
    coords = (place_ref[0], place_ref[1], place_ref[2])
    x = place_ref[3]
    copies = []
    parts = depth // latent_depth
    for key, chunk in zip(keys, chunks):
        block = place_of(coords, key)
        rows = pl.ds(pl.multiple_of(block * depth, depth), depth)
        small_rows = pl.ds(pl.multiple_of(block * latent_depth, latent_depth), latent_depth)
        moves = [(chunk.at[:, pl.ds(0, first_width)], first_ref.at[rows])]
        for k in range(parts):
            moves.append(
                (
                    chunk.at[
                        pl.ds(k * latent_depth, latent_depth), pl.ds(first_width, keyval_part)
                    ],
                    keyval_weight_ref.at[small_rows, pl.ds(k * keyval_part, keyval_part)],
                )
            )
        moves.append(
            (
                chunk.at[:, pl.ds(first_width + keyval_part, heads * VD)],
                output_ref.at[rows],
            )
        )
        for source, target in moves:
            copies.append(pltpu.make_async_copy(source, target, semaphores.at[len(copies)]))
    for copy in copies:
        copy.start()
    for copy in copies:
        copy.wait()

    edge = query_width + KVR
    spread = jnp.transpose(first_ref[:, edge:].astype(f32))[used - edge : used - edge + 8]
    gains_ref[...] = spread
    gain = spread[0:1]
    source = lax.broadcasted_iota(jnp.int32, (D, KVR), 0)
    target = lax.broadcasted_iota(jnp.int32, (D, KVR), 1)
    wanted = target // latent_depth * depth + target % latent_depth
    chosen = jnp.where(source == wanted, 1.0, 0.0).astype(bf16)
    latent_gain = wide_dot(spread.astype(bf16), chosen)[2:3]
    latent_gain_ref[...] = latent_gain
    for ref, start in ((own_ref, x * local_rows), (other_ref, (1 - x) * local_rows)):
        rows = ref[...].astype(f32)
        unit = rows * lax.rsqrt(jnp.mean(rows * rows, axis=1, keepdims=True) + EPSILON)
        normed_ref[pl.ds(pl.multiple_of(start, local_rows), local_rows), :] = (unit * gain).astype(
            bf16
        )
    nope_width = heads * NOPE
    span = heads * (ROPE // 2)
    half = nope_width // 2
    for k in (0, 1):
        nope_ref[:, k * half : (k + 1) * half] = wide_dot(
            normed_ref[...], first_ref[:, k * half : (k + 1) * half]
        ).astype(bf16)
    turning = wide_dot(normed_ref[...], first_ref[:, nope_width : nope_width + 2 * span])
    cosine, sine = cosine_ref[...], sine_ref[...]
    first, second = turning[:, :span], turning[:, span:]
    turned_ref[:, :span] = (first * cosine - second * sine).astype(bf16)
    turned_ref[:, span:] = (second * cosine + first * sine).astype(bf16)
    latent = wide_dot(normed_ref[...], first_ref[:, query_width : query_width + KVR])
    latent_ref[...] = latent
    tail = wide_dot(normed_ref[...], first_ref[:, query_width + KVR :])
    lane = lax.broadcasted_iota(jnp.int32, (1, tail.shape[1]), 1)
    swapped = jnp.where(
        lane < ROPE // 2,
        -pltpu.roll(tail, tail.shape[1] - ROPE // 2, 1),
        pltpu.roll(tail, ROPE // 2, 1),
    )
    width = tail.shape[1]
    turned_key = tail * cosine[:, :width] + swapped * sine[:, :width]
    turned_key = jnp.where(lane < ROPE, turned_key, 0.0).astype(bf16)
    source = lax.broadcasted_iota(jnp.int32, (width, 2 * span), 0)
    target = lax.broadcasted_iota(jnp.int32, (width, 2 * span), 1)
    wanted = target % (ROPE // 2) + jnp.where(target < span, 0, ROPE // 2)
    key_ref[...] = wide_dot(turned_key, (source == wanted).astype(bf16)).astype(bf16)
    unit = latent * lax.rsqrt(jnp.mean(latent * latent, axis=1, keepdims=True) + EPSILON)
    latent_normed = (unit * latent_gain).astype(bf16)
    half = keyval_ref.shape[1] // 4
    for k in range(4):
        keyval_ref[:, k * half : (k + 1) * half] = wide_dot(
            latent_normed, keyval_weight_ref[:, k * half : (k + 1) * half]
        ).astype(bf16)
    allowed = allowed_rows(place_ref[4], segment_row_ref[...], segment_column_ref[...])
    total_lane = lax.broadcasted_iota(jnp.int32, total_ref.shape, 1)
    total_ref[...] = jnp.zeros_like(total_ref)

    def one_head(h, _):
        scores = head_scores(
            heads, h, nope_ref, turned_ref, keyval_ref, key_ref, head_lanes(heads, h)
        )
        scores = jnp.where(allowed, scores, -1e30)
        most = jnp.max(scores, axis=1, keepdims=True)
        total = most + jnp.log(jnp.sum(jnp.exp(scores - most), axis=1, keepdims=True))
        weights = jnp.exp(scores - total).astype(bf16)
        total_ref[...] += jnp.where(total_lane == h, total, 0.0)
        value_column = pl.ds(pl.multiple_of(h * (NOPE + VD) + NOPE, NOPE), VD)
        attended_ref[:, pl.ds(pl.multiple_of(h * VD, VD), VD)] = wide_dot(
            weights, keyval_ref[:, value_column]
        ).astype(bf16)
        return 0

    lax.fori_loop(0, heads, one_head, 0)
    own = pl.ds(pl.multiple_of(x * local_rows, local_rows), local_rows)
    other = pl.ds(pl.multiple_of((1 - x) * local_rows, local_rows), local_rows)
    pieces = 4
    size = output_ref.shape[0] // pieces
    for k in range(pieces):
        columns = slice(k * size, (k + 1) * size)
        own_out[:, columns] = dot_turned(attended_ref[own, :], output_ref[columns, :])
        sent_out[:, columns] = dot_turned(attended_ref[other, :], output_ref[columns, :]).astype(
            bf16
        )


def attend_forward(place, segments, cosine, sine, own, other, chunks, heads, sizes, others):
    depth, query_width, used, latent_depth, keyval_part, first_width = sizes
    f32, bf16 = jnp.float32, jnp.bfloat16
    keys = [key for key, _ in chunks]
    local_rows = own.shape[0]
    tokens = 2 * local_rows
    span = heads * (ROPE // 2)
    shapes = [
        ((local_rows, D), f32),
        ((local_rows, D), bf16),
        ((D, first_width), bf16),
        ((KVR, heads * (NOPE + VD)), bf16),
        ((D, heads * VD), bf16),
        ((tokens, D), bf16),
        ((tokens, heads * NOPE), bf16),
        ((tokens, 2 * span), bf16),
        ((tokens, KVR), f32),
        ((tokens, 2 * span), bf16),
        ((tokens, heads * (NOPE + VD)), bf16),
        ((tokens, 128), f32),
        ((tokens, heads * VD), bf16),
        ((8, D), f32),
        ((1, KVR), f32),
    ]
    return pl.pallas_call(
        functools.partial(attend_kernel, keys, len(others), heads, sizes),
        out_shape=[jax.ShapeDtypeStruct(*shape) for shape in shapes],
        in_specs=[pl.BlockSpec(memory_space=pltpu.SMEM)]
        + in_vmem(6)
        + in_place(len(chunks) + len(others)),
        out_specs=in_vmem(len(shapes)),
        scratch_shapes=[
            pltpu.SemaphoreType.DMA((len(chunks) * (2 + depth // latent_depth),))
        ],
        compiler_params=pltpu.CompilerParams(vmem_limit_bytes=48 * 1024 * 1024),
        cost_estimate=pl.CostEstimate(
            flops=2 * tokens * D * (first_width + heads * VD + 1024),
            bytes_accessed=4 * D * (first_width + 1536),
            transcendentals=2 * heads * tokens * tokens,
        ),
    )(
        place,
        segments,
        segments.T,
        cosine,
        sine,
        own,
        other,
        *[piece for _, piece in chunks],
        *others,
    )


def attend_back_kernel(
    heads,
    place_ref,
    segment_row_ref,
    segment_column_ref,
    cosine_ref,
    sine_ref,
    own_ref,
    other_ref,
    keyval_weight_ref,
    output_ref,
    nope_ref,
    turned_ref,
    latent_ref,
    key_ref,
    keyval_ref,
    total_ref,
    latent_gain_ref,
    projected_ref,
    keyval_grad_ref,
    latent_out,
    gain_ref,
    grad_ref,
    turn_ref,
    back_ref,
):
    f32, bf16 = jnp.float32, jnp.bfloat16
    local_rows = own_ref.shape[0]
    x = place_ref[3]
    span = heads * (ROPE // 2)
    nope_width = heads * NOPE
    query_width = nope_width + 2 * span
    scale = (NOPE + ROPE) ** (-0.5)
    for ref, start in ((own_ref, x * local_rows), (other_ref, (1 - x) * local_rows)):
        rows = pl.ds(pl.multiple_of(start, local_rows), local_rows)
        for k in (0, 1):
            half = slice(k * nope_width // 2, (k + 1) * nope_width // 2)
            grad_ref[rows, half] = wide_dot(ref[...], output_ref[:, half]).astype(bf16)
    allowed = allowed_rows(place_ref[4], segment_row_ref[...], segment_column_ref[...])
    total_lane = lax.broadcasted_iota(jnp.int32, total_ref.shape, 1)
    turn_ref[...] = jnp.zeros_like(turn_ref)
    back_ref[...] = jnp.zeros_like(back_ref)

    def one_head(h, _):
        mask = head_lanes(heads, h)
        scores = head_scores(heads, h, nope_ref, turned_ref, keyval_ref, key_ref, mask)
        total = jnp.sum(jnp.where(total_lane == h, total_ref[...], 0.0), axis=1, keepdims=True)
        weights = jnp.exp(jnp.where(allowed, scores, -1e30) - total)
        weights_low = weights.astype(bf16)
        column = pl.ds(pl.multiple_of(h * NOPE, NOPE), NOPE)
        key_column = pl.ds(pl.multiple_of(h * (NOPE + VD), NOPE), NOPE)
        value_column = pl.ds(pl.multiple_of(h * (NOPE + VD) + NOPE, NOPE), VD)
        grads = grad_ref[:, column]
        grad_weights = dot_turned(grads, keyval_ref[:, value_column])
        keyval_grad_ref[:, value_column] = dot_rows(weights_low, grads).astype(bf16)
        grad_scores = (
            weights * (grad_weights - jnp.sum(weights * grad_weights, axis=1, keepdims=True))
        ).astype(bf16)
        projected_ref[:, column] = (
            scale * wide_dot(grad_scores, keyval_ref[:, key_column])
        ).astype(bf16)
        keyval_grad_ref[:, key_column] = (
            scale * dot_rows(grad_scores, nope_ref[:, column])
        ).astype(bf16)
        for k in (0, 1):
            part = slice(k * span, (k + 1) * span)
            turn = wide_dot(grad_scores, key_ref[:, part])
            turn_ref[:, part] += jnp.where(mask, turn, 0.0)
            own = turned_ref[:, part]
            own = jnp.where(mask, own, jnp.zeros_like(own))
            back_ref[:, part] += dot_rows(grad_scores, own)
        return 0

    lax.fori_loop(0, heads, one_head, 0)
    cosine, sine = cosine_ref[...], sine_ref[...]
    first, second = scale * turn_ref[:, :span], scale * turn_ref[:, span:]
    projected_ref[:, nope_width : nope_width + span] = (first * cosine + second * sine).astype(bf16)
    projected_ref[:, nope_width + span : query_width] = (second * cosine - first * sine).astype(
        bf16
    )
    folded = []
    for k in (0, 1):
        part = scale * back_ref[:, k * span : (k + 1) * span]
        shift = span // 2
        while shift >= ROPE // 2:
            part = part + pltpu.roll(part, shift, 1)
            shift //= 2
        folded.append(part)
    width = projected_ref.shape[1] - query_width - KVR
    lane = lax.broadcasted_iota(jnp.int32, (1, width), 1)
    first = (folded[0] * cosine + folded[1] * sine)[:, :width]
    second = (folded[1] * cosine - folded[0] * sine)[:, :width]
    projected_ref[:, query_width + KVR :] = jnp.where(
        lane < ROPE // 2, first, jnp.where(lane < ROPE, second, 0.0)
    ).astype(bf16)
    gain = latent_gain_ref[...]
    latent = latent_ref[...]
    row_scale = lax.rsqrt(jnp.mean(latent * latent, axis=1, keepdims=True) + EPSILON)
    unit = latent * row_scale
    latent_out[...] = (unit * gain).astype(bf16)
    grad_normed = dot_turned(keyval_grad_ref[...], keyval_weight_ref[...])
    gain_ref[...] = jnp.sum(grad_normed * unit, axis=0, keepdims=True)
    grad_unit = grad_normed * gain
    projected_ref[:, query_width : query_width + KVR] = (
        row_scale * (grad_unit - unit * jnp.mean(grad_unit * unit, axis=1, keepdims=True))
    ).astype(bf16)


def attend_back(place, segments, cosine, sine, own, other, saved, heads, first_width, others):
    f32, bf16 = jnp.float32, jnp.bfloat16
    keyval = saved[6]
    tokens = 2 * own.shape[0]
    span = heads * (ROPE // 2)
    return pl.pallas_call(
        lambda *refs: attend_back_kernel(heads, *refs[:16], *refs[16 + len(others) :]),
        out_shape=[
            jax.ShapeDtypeStruct((tokens, first_width), bf16),
            jax.ShapeDtypeStruct((tokens, keyval.shape[1]), bf16),
            jax.ShapeDtypeStruct((tokens, KVR), bf16),
            jax.ShapeDtypeStruct((1, KVR), f32),
        ],
        in_specs=[pl.BlockSpec(memory_space=pltpu.SMEM)] + in_vmem(15) + in_place(len(others)),
        out_specs=in_vmem(4),
        scratch_shapes=[
            pltpu.VMEM((tokens, heads * NOPE), bf16),
            pltpu.VMEM((tokens, 2 * span), f32),
            pltpu.VMEM((tokens, 2 * span), f32),
        ],
        compiler_params=pltpu.CompilerParams(vmem_limit_bytes=48 * 1024 * 1024),
        cost_estimate=pl.CostEstimate(
            flops=2 * tokens * D * 3000,
            bytes_accessed=2 * D * 1536,
            transcendentals=heads * tokens * tokens,
        ),
    )(
        place,
        segments,
        segments.T,
        cosine,
        sine,
        own,
        other,
        *saved,
        *others,
    )


def first_grads_kernel(extra, places_ref, left_ref, right_ref, small_ref, *refs):
    out_ref = refs[-1]
    size = left_ref.shape[1]
    edge = right_ref.shape[1] - small_ref.shape[0]
    result = dot_rows(left_ref[...], right_ref[...])
    for value, some in (
        (result[:, :edge], slice(0, edge)),
        (result[:, edge:] + jnp.transpose(small_ref[...]), slice(edge, right_ref.shape[1])),
    ):
        if extra:
            value = value + refs[0][:, some].astype(jnp.float32)
        out_ref[:, some] = value.astype(jnp.bfloat16)


def other_grads_kernel(first, extra, places_ref, latent_ref, keyval_ref, grad_ref, attended_ref, *refs):
    out_ref, keyval_all = refs[-2:]
    step = pl.program_id(0)
    size = grad_ref.shape[1]
    latent_size = latent_ref.shape[1] // places_ref.shape[0]
    parts = size // latent_size
    columns = keyval_ref.shape[1] // parts

    @pl.when(step == 0)
    def _():
        for k in range(parts):
            some = slice(k * columns, (k + 1) * columns)
            keyval_all[:, some] = dot_rows(latent_ref[...], keyval_ref[:, some])

    start = pl.multiple_of(places_ref[first + step] * latent_size, latent_size)
    strip = keyval_all[pl.ds(start, latent_size), :]
    keyval = jnp.concatenate([strip[:, k * columns : (k + 1) * columns] for k in range(parts)], axis=0)
    output = dot_rows(grad_ref[...], attended_ref[...])
    for value, some in (
        (keyval, slice(0, columns)),
        (output, slice(columns, columns + output.shape[1])),
    ):
        if extra:
            value = value + refs[0][:, some].astype(jnp.float32)
        out_ref[:, some] = value.astype(jnp.bfloat16)


def still(array):
    return pl.BlockSpec(array.shape, lambda i, where: (0, 0))


def grads_call(kernel, specs, operands, scratch, size, width, places, first, count, arrived):
    extra = [] if arrived is None else [arrived]
    return pl.pallas_call(
        functools.partial(kernel, len(extra)),
        grid_spec=pltpu.PrefetchScalarGridSpec(
            num_scalar_prefetch=1,
            grid=(count,),
            in_specs=specs
            + [pl.BlockSpec((size, width), lambda i, where: (first + i, 0))] * len(extra),
            out_specs=pl.BlockSpec((size, width), lambda i, where: (i, 0)),
            scratch_shapes=scratch,
        ),
        out_shape=jax.ShapeDtypeStruct((count * size, width), jnp.bfloat16),
        compiler_params=pltpu.CompilerParams(vmem_limit_bytes=32 * 1024 * 1024),
        cost_estimate=pl.CostEstimate(
            flops=1024 * count * size * width,
            bytes_accessed=4 * count * size * width,
            transcendentals=0,
        ),
    )(places, *operands, *extra)


def first_grads(left, right, small, places, first, count, arrived=None):
    rows, width = right.shape
    size = left.shape[1] // places.shape[0]
    specs = [
        pl.BlockSpec((rows, size), lambda i, where: (0, where[first + i])),
        still(right),
        pl.BlockSpec((small.shape[0], size), lambda i, where: (0, where[first + i])),
    ]
    return grads_call(
        first_grads_kernel, specs, (left, right, small), [], size, width, places, first, count, arrived
    )


def other_grads(latent, keyval, grad, attended, places, first, count, arrived=None):
    rows = grad.shape[0]
    blocks = places.shape[0]
    size = grad.shape[1] // blocks
    parts = size // (latent.shape[1] // blocks)
    width = keyval.shape[1] // parts + attended.shape[1]
    specs = [
        still(latent),
        still(keyval),
        pl.BlockSpec((rows, size), lambda i, where: (0, where[first + i])),
        still(attended),
    ]
    scratch = [pltpu.VMEM((latent.shape[1], keyval.shape[1]), jnp.float32)]
    return grads_call(
        functools.partial(other_grads_kernel, first),
        specs,
        (latent, keyval, grad, attended),
        scratch,
        size,
        width,
        places,
        first,
        count,
        arrived,
    )


def first_back_kernel(place_ref, own_ref, other_ref, grad_ref, weight_ref, own_out, sent_out, gain_ref):
    local_rows = own_ref.shape[0]
    x = place_ref[3]
    size = weight_ref.shape[0] // 4
    for ref, start, out in (
        (own_ref, x * local_rows, own_out),
        (other_ref, (1 - x) * local_rows, sent_out),
    ):
        rows = ref[...].astype(jnp.float32)
        unit = rows * lax.rsqrt(jnp.mean(rows * rows, axis=1, keepdims=True) + EPSILON)
        grads = grad_ref[pl.ds(pl.multiple_of(start, local_rows), local_rows), :]
        for k in range(4):
            some = slice(k * size, (k + 1) * size)
            part = dot_turned(grads, weight_ref[some, :])
            out[:, some] = part.astype(out.dtype)
            gain = jnp.sum(part * unit[:, some], axis=0, keepdims=True)
            if ref is own_ref:
                gain_ref[:, some] = gain
            else:
                gain_ref[:, some] += gain


def first_back(place, own, other, grads, weight):
    f32, bf16 = jnp.float32, jnp.bfloat16
    depth = weight.shape[0]
    return pl.pallas_call(
        first_back_kernel,
        out_shape=[
            jax.ShapeDtypeStruct(own.shape, f32),
            jax.ShapeDtypeStruct(own.shape, bf16),
            jax.ShapeDtypeStruct((1, depth), f32),
        ],
        in_specs=[pl.BlockSpec(memory_space=pltpu.SMEM)] + in_vmem(4),
        out_specs=in_vmem(3),
        compiler_params=pltpu.CompilerParams(vmem_limit_bytes=32 * 1024 * 1024),
        cost_estimate=pl.CostEstimate(
            flops=4 * own.shape[0] * weight.shape[0] * weight.shape[1],
            bytes_accessed=2 * weight.shape[0] * weight.shape[1],
            transcendentals=0,
        ),
    )(place, own, other, grads, weight)


def close_ring(near, arrived):
    size = near.shape[0] // RINGS
    total = near.astype(jnp.float32) + arrived.astype(jnp.float32)
    return ring_sum([total[r * size : (r + 1) * size] for r in range(RINGS)], jnp.bfloat16)


def pack_kernel(heads, query_ref, latent_ref, small_ref, keyval_ref, output_ref, out_ref):
    half = ROPE // 2
    head = NOPE + ROPE
    nope_width = heads * NOPE
    for h in range(heads):
        start = h * head
        out_ref[:, h * NOPE : (h + 1) * NOPE] = query_ref[:, start : start + NOPE]
        for k in (0, 1):
            to = nope_width + k * heads * half + h * half
            out_ref[:, to : to + half] = query_ref[
                :, start + NOPE + k * half : start + NOPE + (k + 1) * half
            ]
    at = heads * head
    edge = at + KVR
    out_ref[:, at:edge] = latent_ref[:, :KVR]
    out_ref[:, edge : edge + 128] = jnp.concatenate([latent_ref[:, KVR:], small_ref[...]], axis=1)
    at = edge + 128
    size = keyval_ref.shape[0]
    parts = out_ref.shape[0] // size
    part = keyval_ref.shape[1] // parts
    for k in range(parts):
        out_ref[k * size : (k + 1) * size, at : at + part] = keyval_ref[
            :, k * part : (k + 1) * part
        ]
    out_ref[:, at + part :] = jnp.transpose(output_ref[...].astype(jnp.float32)).astype(
        jnp.bfloat16
    )


def pack_weights(query, latent, small, keyval, output):
    depth, query_width = query.shape
    heads = query_width // (NOPE + ROPE)
    width = query_width + KVR + 128 + keyval.size // depth + output.shape[0]
    return pl.pallas_call(
        functools.partial(pack_kernel, heads),
        out_shape=jax.ShapeDtypeStruct((depth, width), jnp.bfloat16),
        in_specs=in_vmem(5),
        out_specs=pl.BlockSpec(memory_space=pltpu.VMEM),
    )(query, latent, small, keyval, output)


def load_pieces(pieces, target, semaphores):
    size = pieces[0].shape[0]
    copies = [
        pltpu.make_async_copy(piece, target.at[pl.ds(k * size, size)], semaphores.at[k])
        for k, piece in enumerate(pieces)
    ]
    for copy in copies:
        copy.start()
    for copy in copies:
        copy.wait()


def shared_stride(shared):
    return -(-shared // 32) * 32


def pack_shared_kernel(blocks, shared, in_ref, down_ref, out_ref):
    stride = shared_stride(shared)
    out_ref[...] = jnp.zeros_like(out_ref)
    for k in range(3):
        if k < 2:
            units = jnp.transpose(in_ref[k].astype(jnp.float32)).astype(jnp.bfloat16)
        else:
            units = down_ref[...]
        for b in range(blocks):
            out_ref[b, k * stride : k * stride + shared] = units[b * shared : (b + 1) * shared]


def pack_shared(shared_in, shared_down, blocks, others):
    depth = shared_in.shape[1]
    shared = shared_down.shape[0] // blocks
    return pl.pallas_call(
        lambda in_ref, down_ref, *refs: pack_shared_kernel(
            blocks, shared, in_ref, down_ref, refs[-1]
        ),
        out_shape=jax.ShapeDtypeStruct((blocks, 3 * shared_stride(shared), depth), jnp.bfloat16),
        in_specs=in_vmem(2) + in_place(len(others)),
        out_specs=pl.BlockSpec(memory_space=pltpu.VMEM),
    )(shared_in, shared_down, *others)


def unpack_shared_kernel(shared, packed_ref, in_ref, down_ref, units_ref):
    stride = shared_stride(shared)
    blocks = packed_ref.shape[0]
    for k in range(3):
        target = down_ref if k == 2 else units_ref
        for b in range(blocks):
            target[b * shared : (b + 1) * shared, :] = packed_ref[
                b, k * stride : k * stride + shared
            ].astype(jnp.float32)
        if k < 2:
            in_ref[k] = jnp.transpose(units_ref[...])


def unpack_shared(packed, shared, others):
    blocks, _, depth = packed.shape
    return pl.pallas_call(
        lambda packed_ref, *refs: unpack_shared_kernel(shared, packed_ref, *refs[len(others) :]),
        out_shape=[
            jax.ShapeDtypeStruct((2, depth, blocks * shared), jnp.float32),
            jax.ShapeDtypeStruct((blocks * shared, depth), jnp.float32),
        ],
        in_specs=in_vmem(1) + in_place(len(others)),
        out_specs=in_vmem(2),
        scratch_shapes=[pltpu.VMEM((blocks * shared, depth), jnp.float32)],
    )(packed, *others)


def pack_units_kernel(units, shared, own_in, other_in, own_down, other_down, near, far, *refs):
    outs = refs[-3:]
    hole = -(-units // TILE) * TILE
    stride = shared_stride(shared)
    columns = outs[0].shape[1]
    size = near.shape[2]
    for k, out in enumerate(outs):
        first = own_in[0, k] if k < 2 else own_down[0]
        second = other_in[0, k] if k < 2 else other_down[0]
        out[:units] = first
        out[units:hole] = jnp.zeros((hole - units, columns), jnp.bfloat16)
        out[hole : hole + units] = second
        out[hole + units : 2 * hole] = jnp.zeros((hole - units, columns), jnp.bfloat16)
        out[2 * hole :] = jnp.zeros((TILE, columns), jnp.bfloat16)
        for b in range(columns // size):
            part = slice(b * size, (b + 1) * size)
            for at, ref in ((2 * hole, near), (2 * hole + stride, far)):
                out[at : at + shared, part] = ref[b, k * stride : k * stride + shared]


def pack_units(own_in, other_in, own_down, other_down, near, far, shared, others):
    units, depth = own_down.shape[1:]
    size = near.shape[2]
    height = 2 * (-(-units // TILE) * TILE) + TILE
    columns = 2 * size
    in_spec = pl.BlockSpec((1, 2, units, columns), lambda i: (0, 0, 0, i))
    down_spec = pl.BlockSpec((1, units, columns), lambda i: (0, 0, i))
    narrow = pl.BlockSpec((2,) + near.shape[1:], lambda i: (i, 0, 0))
    return pl.pallas_call(
        functools.partial(pack_units_kernel, units, shared),
        grid=(depth // columns,),
        in_specs=[in_spec, in_spec, down_spec, down_spec, narrow, narrow]
        + in_place(len(others)),
        out_specs=[pl.BlockSpec((height, columns), lambda i: (0, i))] * 3,
        out_shape=[jax.ShapeDtypeStruct((height, depth), jnp.bfloat16)] * 3,
        compiler_params=pltpu.CompilerParams(vmem_limit_bytes=32 * 1024 * 1024),
        cost_estimate=pl.CostEstimate(
            flops=0, bytes_accessed=12 * height * depth, transcendentals=0
        ),
    )(own_in, other_in, own_down, other_down, near, far, *others)


def expert_grads_kernel(units, count, extra, right_ref, *refs):
    out = refs[-1]
    for k in range(count):

        @pl.when(pl.program_id(0) == k)
        def _():
            result = dot_rows(refs[k][...], right_ref[...])[:units]
            if extra:
                result += refs[count][0, 0].astype(jnp.float32)
            out[0, 0] = result.astype(out.dtype)


def expert_grads(lefts, right, units, column, arrived, kind, others=()):
    total, depth = right.shape
    wide = -(-units // TILE) * TILE
    extra = [] if arrived is None else [arrived]
    out = pl.BlockSpec((1, 1, units, 2 * TILE), lambda k, i: (0, k, 0, i))
    side = pl.BlockSpec((total, wide), lambda k, i: (0, column))
    return pl.pallas_call(
        functools.partial(expert_grads_kernel, units, len(lefts), len(extra)),
        grid=(len(lefts), depth // (2 * TILE)),
        in_specs=[pl.BlockSpec((total, 2 * TILE), lambda k, i: (0, i))]
        + [side] * len(lefts)
        + [out] * len(extra)
        + in_place(len(others)),
        out_specs=out,
        out_shape=jax.ShapeDtypeStruct((1, len(lefts), units, depth), kind),
        compiler_params=pltpu.CompilerParams(vmem_limit_bytes=48 * 1024 * 1024),
        cost_estimate=pl.CostEstimate(
            flops=2 * len(lefts) * total * depth * wide,
            bytes_accessed=2 * len(lefts) * total * (depth + wide) + 8 * depth * units,
            transcendentals=0,
        ),
    )(right, *lefts, *extra, *others)


def side_grads_kernel(shared, rows_ref, cots_ref, gate_ref, up_ref, hidden_ref, logit_ref, *outs):
    kept_ref, sent_ref, router_ref = outs
    stride = shared_stride(shared)
    size = kept_ref.shape[2]
    for k, (left, right) in enumerate(
        ((gate_ref, rows_ref), (up_ref, rows_ref), (hidden_ref, cots_ref))
    ):
        result = dot_rows(left[...], right[...])
        for b in range(kept_ref.shape[0]):
            part = slice(b * size, (b + 1) * size)
            kept_ref[b, k * stride : (k + 1) * stride] = result[:stride, part]
            sent_ref[b, k * stride : (k + 1) * stride] = result[
                stride : 2 * stride, part
            ].astype(jnp.bfloat16)
    router_ref[...] = dot_rows(logit_ref[...], rows_ref[...])


def side_grads(rows, cots, gate, up, hidden, logits, shared, blocks):
    total, depth = rows.shape
    column = gate.shape[1] // TILE - 1
    size = depth // blocks
    stride = shared_stride(shared)
    wide = pl.BlockSpec((total, 2 * TILE), lambda i: (0, i))
    side = pl.BlockSpec((total, TILE), lambda i: (0, column))
    packed = pl.BlockSpec((2 * TILE // size, 3 * stride, size), lambda i: (i, 0, 0))
    return pl.pallas_call(
        functools.partial(side_grads_kernel, shared),
        grid=(depth // (2 * TILE),),
        in_specs=[wide, wide, side, side, side, whole(logits)],
        out_specs=[packed, packed, pl.BlockSpec((logits.shape[1], 2 * TILE), lambda i: (0, i))],
        out_shape=[
            jax.ShapeDtypeStruct((blocks, 3 * stride, size), jnp.float32),
            jax.ShapeDtypeStruct((blocks, 3 * stride, size), jnp.bfloat16),
            jax.ShapeDtypeStruct((logits.shape[1], depth), jnp.float32),
        ],
        compiler_params=pltpu.CompilerParams(vmem_limit_bytes=48 * 1024 * 1024),
        cost_estimate=pl.CostEstimate(
            flops=8 * total * depth * TILE,
            bytes_accessed=4 * total * depth,
            transcendentals=0,
        ),
    )(rows, cots, gate, up, hidden, logits)


def down_kernel(count, *refs):
    pieces, weight_ref = refs[:count], refs[count]
    grads_ref, rows_ref, semaphores = refs[-3:]

    @pl.when(pl.program_id(0) == 0)
    def _():
        load_pieces(pieces, rows_ref, semaphores)

    size = rows_ref.shape[0] // 2
    for k in range(2):
        part = slice(k * size, (k + 1) * size)
        grads_ref[part, :] = dot_turned(rows_ref[part, :], weight_ref[...]).astype(jnp.bfloat16)


def down_grads(part, pieces, down, kept, others):
    count = len(pieces)
    size, depth = pieces[0].shape
    width = down.shape[0]
    rows = count * size
    return pl.pallas_call(
        functools.partial(down_kernel, count),
        grid=(width // TILE,),
        in_specs=in_place(count)
        + [pl.BlockSpec((TILE, depth), lambda i: (i, 0))]
        + in_place(len(kept) + len(others)),
        out_specs=[
            pl.BlockSpec((rows, TILE), lambda i: (part, i)),
            pl.BlockSpec((rows, depth), lambda i: (part, 0)),
        ],
        out_shape=[
            jax.ShapeDtypeStruct((2 * rows, width), jnp.bfloat16),
            jax.ShapeDtypeStruct((2 * rows, depth), jnp.bfloat16),
        ],
        scratch_shapes=[pltpu.SemaphoreType.DMA((count,))],
        input_output_aliases={count + 1 + k: k for k in range(len(kept))},
        compiler_params=pltpu.CompilerParams(vmem_limit_bytes=48 * 1024 * 1024),
        cost_estimate=pl.CostEstimate(
            flops=2 * rows * depth * width,
            bytes_accessed=2 * (2 * rows * depth + depth * width + rows * width),
            transcendentals=0,
        ),
    )(*pieces, down, *kept, *others)


def out_kernel(pieces, *refs):
    hidden_ref, weight_ref = refs[:2]
    outs = refs[2 : 2 + pieces]
    size = hidden_ref.shape[0] // (RINGS * pieces)
    for r in range(RINGS):
        part = hidden_ref[r * pieces * size : (r + 1) * pieces * size, :]
        result = wide_dot(part, weight_ref[...]).astype(jnp.bfloat16)
        for k in range(pieces):
            outs[k][r * size : (r + 1) * size, :] = result[k * size : (k + 1) * size]


def out_rows(pieces, hidden, down):
    rows, width = hidden.shape
    depth = down.shape[1]
    return pl.pallas_call(
        functools.partial(out_kernel, pieces),
        grid=(depth // TILE,),
        in_specs=[whole(hidden), pl.BlockSpec((width, TILE), lambda i: (0, i))],
        out_specs=[pl.BlockSpec((rows // pieces, TILE), lambda i: (0, i))] * pieces,
        out_shape=[jax.ShapeDtypeStruct((rows // pieces, depth), jnp.bfloat16)] * pieces,
        compiler_params=pltpu.CompilerParams(vmem_limit_bytes=48 * 1024 * 1024),
        cost_estimate=pl.CostEstimate(
            flops=2 * rows * depth * width,
            bytes_accessed=2 * (rows * depth + depth * width + rows * width),
            transcendentals=0,
        ),
    )(hidden, down)


def mlp_kernel(tiles, pieces, others, experts_ref, routed_ref, *refs):
    row_refs = refs[:pieces]
    router_ref, gate_col, up_col, down_grad, gate_row, up_row = refs[pieces : pieces + 6]
    outs = refs[pieces + 6 + others :]
    grad_refs = outs[:pieces]
    rows_out, hidden_out, gate_out, up_out, logit_out = outs[pieces : pieces + 5]
    gate_all, up_all, prob_ref, scale_ref, sum_ref, semaphores = outs[pieces + 5 :]
    step = pl.program_id(0)
    third = tiles // 2
    total = rows_out.shape[0]
    size = total // pieces
    lane = lax.broadcasted_iota(jnp.int32, (1, router_ref.shape[1]), 1) - experts_ref[3]

    @pl.when(step == 0)
    def _():
        load_pieces(row_refs, rows_out, semaphores)
        logits = wide_dot(rows_out[...], router_ref[...])
        logits = jnp.where((lane >= 0) & (lane < experts_ref[2]), logits, -1e30)
        raised = jnp.exp(logits - jnp.max(logits, axis=1, keepdims=True))
        chances = raised / jnp.sum(raised, axis=1, keepdims=True)
        prob_ref[...] = chances
        for k in (0, 1):
            chance = jnp.sum(jnp.where(lane == experts_ref[k], chances, 0.0), axis=1, keepdims=True)
            scale_ref[k] = routed_ref[:, k : k + 1] * chance
        scale_ref[2] = jnp.ones_like(scale_ref[2])
        sum_ref[...] = jnp.zeros_like(sum_ref)

    @pl.when(step < tiles)
    def _():
        columns = pl.ds(pl.multiple_of(step * TILE, TILE), TILE)
        kind = step // third
        half = total // 2
        for k in (0, 1):
            part = slice(k * half, (k + 1) * half)
            pre_gate = dot_turned(rows_out[part, :], gate_col[...])
            pre_up = dot_turned(rows_out[part, :], up_col[...])
            grads = down_grad[part, :].astype(jnp.float32)
            scale = scale_ref[kind, part, :]
            sigmoid = 1.0 / (1.0 + jnp.exp(-pre_gate))
            silu = pre_gate * sigmoid
            hidden = (silu * pre_up).astype(jnp.bfloat16).astype(jnp.float32)
            sum_ref[kind, part, :] += jnp.sum(hidden * grads, axis=1, keepdims=True)
            grad_hidden = scale * grads
            low_gate = (grad_hidden * pre_up * (sigmoid + silu * (1.0 - sigmoid))).astype(
                jnp.bfloat16
            )
            low_up = (grad_hidden * silu).astype(jnp.bfloat16)
            gate_all[part, columns] = low_gate
            up_all[part, columns] = low_up
            hidden_out[part, :] = (scale * hidden).astype(jnp.bfloat16)
            gate_out[part, :] = low_gate
            up_out[part, :] = low_up

    @pl.when(step == tiles - 1)
    def _():
        grad_logits = jnp.zeros_like(prob_ref)
        for k in (0, 1):
            own = jnp.where(lane == experts_ref[k], 1.0, 0.0)
            grad_logits += scale_ref[k] * sum_ref[k] * (own - prob_ref[...])
        logit_out[...] = grad_logits.astype(jnp.bfloat16)

    @pl.when(step >= tiles)
    def _():
        some = pl.ds(pl.multiple_of((step - tiles) * 2 * TILE, TILE), 2 * TILE)
        grads = wide_dot(gate_all[...], gate_row[...]) + wide_dot(up_all[...], up_row[...])
        grads += dot_turned(logit_out[...], router_ref[some, :])
        grads = grads.astype(jnp.bfloat16)
        for k in range(pieces):
            grad_refs[k][...] = grads[k * size : (k + 1) * size]


def mlp_plane(distance, experts, routed, rows, down_grad, router, weights, kept, others):
    gate, up = weights
    pieces = len(rows)
    size, depth = rows[0].shape
    width = gate.shape[0]
    tiles, columns = width // TILE, depth // (2 * TILE)
    total = pieces * size
    low = jnp.bfloat16

    def early(i):
        return jnp.minimum(i, tiles - 1)

    def late(i):
        return jnp.maximum(i - tiles, 0)

    tile_spec = pl.BlockSpec((total, TILE), lambda i: (distance, early(i)))
    anywhere = pl.BlockSpec(memory_space=pl.ANY)
    first_kept = 2 + pieces + 6
    results = pl.pallas_call(
        functools.partial(mlp_kernel, tiles, pieces, len(kept) + len(others)),
        grid=(tiles + columns,),
        in_specs=[pl.BlockSpec(memory_space=pltpu.SMEM), whole(routed)]
        + [anywhere] * pieces
        + [
            pl.BlockSpec((depth, 128), lambda i: (0, router.shape[1] // 128 - 1)),
            pl.BlockSpec((TILE, depth), lambda i: (early(i), 0)),
            pl.BlockSpec((TILE, depth), lambda i: (early(i), 0)),
            tile_spec,
            pl.BlockSpec((width, 2 * TILE), lambda i: (0, late(i))),
            pl.BlockSpec((width, 2 * TILE), lambda i: (0, late(i))),
        ]
        + [anywhere] * (len(kept) + len(others)),
        out_specs=[pl.BlockSpec((size, 2 * TILE), lambda i: (0, late(i)))] * pieces
        + [
            pl.BlockSpec((total, depth), lambda i: (distance, 0)),
            tile_spec,
            tile_spec,
            tile_spec,
            pl.BlockSpec((total, 128), lambda i: (distance, 0)),
        ],
        out_shape=[jax.ShapeDtypeStruct((size, depth), low)] * pieces
        + [
            jax.ShapeDtypeStruct((RINGS * total, many), low)
            for many in (depth, width, width, width, 128)
        ],
        scratch_shapes=[pltpu.VMEM((total, width), low)] * 2
        + [
            pltpu.VMEM((total, 128), jnp.float32),
            pltpu.VMEM((3, total, 1), jnp.float32),
            pltpu.VMEM((3, total, 1), jnp.float32),
            pltpu.SemaphoreType.DMA((pieces,)),
        ],
        input_output_aliases={first_kept + k: pieces + k for k in range(len(kept))},
        compiler_params=pltpu.CompilerParams(vmem_limit_bytes=48 * 1024 * 1024),
        cost_estimate=pl.CostEstimate(
            flops=2 * total * depth * width * 4,
            bytes_accessed=2 * (4 * depth * width + 3 * total * depth + 4 * total * width),
            transcendentals=total * width,
        ),
    )(experts, routed, *rows, router, gate, up, down_grad, gate, up, *kept, *others)
    return results[:pieces], results[pieces:]


def gather_body(
    block_input,
    segments,
    counts,
    routes,
    attn_gain,
    w_query,
    w_latent,
    latent_gain,
    w_keyval,
    w_output,
    ffn_gain,
    w_router,
    shared_gate_up,
    shared_down,
    expert_gate_up,
    expert_down,
    cotangent,
):
    f32 = jnp.float32
    bf16 = jnp.bfloat16
    blocks = 16
    index = lax.axis_index("dp")
    x = lax.axis_index("tensor")
    coords = jnp.stack([index // 4, (index // 2) % 2, index % 2]).astype(jnp.int32)
    core = coords[2]
    place = jnp.concatenate([coords, x.astype(jnp.int32)[None], counts])
    local_rows = block_input.shape[0]
    tokens = 2 * local_rows
    depth = w_query.shape[0]
    query_width = w_query.shape[1]
    heads = query_width // (NOPE + ROPE)
    experts = w_router.shape[1]
    units = expert_gate_up.shape[3]
    shared = shared_gate_up.shape[2] // blocks
    latent_depth = w_keyval.shape[0]

    used = query_width + KVR + ROPE
    small = jnp.concatenate(
        [
            attn_gain[:, None],
            ffn_gain[:, None],
            jnp.pad(latent_gain, (0, depth - latent_depth))[:, None],
            w_router,
            routes.reshape(depth, -1).astype(bf16),
            jnp.zeros((depth, 128 - ROPE - 3 - experts - 2 * TOP), bf16),
        ],
        axis=1,
    )
    first_width = query_width + KVR + 128
    shards = pack_weights(w_query, w_latent, small, w_keyval, w_output)
    held = ring_shards(shards)
    other_input = other_x(block_input)
    expert_in = expert_gate_up.swapaxes(2, 3)
    expert_in_other = other_core(expert_in)
    expert_down_other = other_core(expert_down)
    shared_near = lax.all_to_all(
        pack_shared(shared_gate_up, shared_down, blocks, ()),
        "dp",
        split_axis=0,
        concat_axis=0,
        tiled=True,
    )
    shared_far = other_core(shared_near)

    chunks = gather_weight(held, (shared_near,))
    grad_planes = gather_rows(after(cotangent, held[3]), "xyxy")

    cosine, sine = rotary_tables(segments[0], ROPE)
    cosine = jnp.tile(cosine, (1, heads))
    sine = jnp.tile(sine, (1, heads))
    sizes = (depth, query_width, used, latent_depth, w_keyval.shape[1] * latent_depth // depth, first_width)
    (
        own_part,
        sent_part,
        first_weight,
        keyval_weight,
        output_turned,
        first_normed,
        nope,
        turned_query,
        latent,
        key,
        keyval,
        total,
        attended,
        gains,
        latent_gain_row,
    ) = attend_forward(
        place,
        segments,
        cosine,
        sine,
        block_input,
        other_input,
        chunks,
        heads,
        sizes,
        (
            grad_planes[3][0],
            grad_planes[0][1],
            grad_planes[0][2],
            grad_planes[1][2],
            grad_planes[2][2],
        ),
    )
    attn_gain_wide, ffn_gain_wide = gains[0], gains[1]
    mixed = block_input.astype(f32) + own_part + other_x(sent_part).astype(f32)
    second_scale = rms_scale(mixed)
    second_unit = mixed * second_scale
    second_normed = (second_unit * ffn_gain_wide).astype(bf16)

    routes_at = used + 3 + experts
    routes_all = first_weight[:, routes_at : routes_at + 2 * TOP].reshape(blocks * tokens, TOP)
    chip_experts = jnp.stack([index, index + 1 - 2 * core]).astype(jnp.int32)
    routed_all = jnp.any(
        routes_all[None] == chip_experts[:, None, None].astype(bf16), axis=2
    ).astype(f32)
    order = jnp.stack(
        [
            place_of(coords, (distance, flip_y, 0)) * 2 + (1 - x if flip_x else x)
            for distance in range(RINGS)
            for flip_x, flip_y in ((0, 0), (0, 1), (1, 0), (1, 1))
        ]
    )
    routed = jnp.stack(
        [
            pick_blocks(one.reshape(blocks * 2, local_rows), order).reshape(RINGS, -1)
            for one in routed_all
        ],
        axis=2,
    )

    corners = "yxyx"
    row_planes = gather_rows(second_normed, corners, True)

    gate_weight, up_weight, down_weight = pack_units(
        expert_in,
        expert_in_other,
        expert_down,
        expert_down_other,
        shared_near,
        shared_far,
        shared,
        (second_normed,),
    )
    half_kept = down_grads(
        0,
        [piece for plane in grad_planes[:2] for piece in plane],
        down_weight,
        (),
        (row_planes[1][0],),
    )
    down_grad, every_grad = down_grads(
        1,
        [piece for plane in grad_planes[2:] for piece in plane],
        down_weight,
        half_kept,
        (row_planes[2][0],),
    )
    expert_ids = jnp.concatenate(
        [chip_experts, jnp.array([experts, used + 3 - query_width - KVR], jnp.int32)]
    )
    kept = []
    turned, closed = [], []
    for distance in range(RINGS):
        others = [row_planes[3][0]] if distance == 0 else [row_planes[2][3]]
        if distance == 2:
            others = list(turned[0][1:]) + [row_planes[3][3]]
        elif distance == 3:
            others = list(turned[1][1:]) + list(closed[0][1:])
        grads, kept = mlp_plane(
            distance,
            expert_ids,
            routed[distance],
            row_planes[distance],
            down_grad,
            first_weight,
            (gate_weight, up_weight),
            kept,
            others,
        )
        turned.append(turn_corner(grads, corners[distance]))
        if distance < RINGS - 1:
            closed.append(close_plane(turned[distance]))
    every_row, every_hidden, every_gate_grad, every_up_grad, logit_grads = kept
    shared_kept, shared_sent, logit_rows = side_grads(
        every_row,
        every_grad,
        every_gate_grad,
        every_up_grad,
        every_hidden,
        logit_grads,
        shared,
        blocks,
    )
    sent_in = expert_grads((every_gate_grad, every_up_grad), every_row, units, 1, None, bf16)
    sent_down = expert_grads((every_hidden,), every_grad, units, 1, None, bf16)
    moving = ring_step(wide_sum(*closed[1]).astype(bf16))
    moving = ring_step(wide_sum(moving, *closed[2]).astype(bf16))
    own, beside, across = turned[3]
    own = after(own, sent_down)
    grad_close = close_plane((own, after(beside, shared_sent), across))
    grad_second = wide_sum(
        ring_step(wide_sum(moving, *grad_close).astype(bf16)),
        after(closed[0][0], sent_in),
        *closed[0][1:],
    )
    arrived_in = other_core(sent_in)
    arrived_down = other_core(sent_down)
    router_at = used + 3 - query_width - KVR
    grad_router = logit_rows[router_at : router_at + experts]
    shared_grads = lax.all_to_all(
        add_low(shared_kept, other_core(shared_sent)), "dp", split_axis=0, concat_axis=0, tiled=True
    )

    gain_ffn_part = jnp.sum(grad_second * second_unit, axis=0)
    grad_mixed = cotangent.astype(f32) + rms_back(
        grad_second * ffn_gain_wide, second_unit, second_scale
    )
    grad_mixed_low = grad_mixed.astype(bf16)
    other_grad = other_x(grad_mixed_low)
    outs = list(out_rows(4, every_hidden, down_weight))
    outs[3] = after(outs[3], grad_close[2])
    outs[2] = after(outs[2], other_grad)
    out_own, out_beside, out_across = close_plane(turn_corner(outs, "x"))


    places = jnp.stack([place_of(coords, key_of) for key_of in weight_keys()]).astype(jnp.int32)
    projected_grad, keyval_grad, latent_normed, gain_latent_part = attend_back(
        place,
        segments,
        cosine,
        sine,
        grad_mixed_low,
        other_grad,
        (keyval_weight, output_turned, nope, turned_query, latent, key, keyval, total, latent_gain_row),
        heads,
        first_width,
        (shared_grads,),
    )
    grad_attn = jnp.concatenate(
        [
            jnp.where(x == 0, grad_mixed_low, other_grad),
            jnp.where(x == 0, other_grad, grad_mixed_low),
        ],
        axis=0,
    )
    ring_places = places.reshape(2, 2, RINGS).swapaxes(1, 2).reshape(-1)
    other_parts = (latent_normed, keyval_grad, grad_attn, attended, ring_places)
    other_arrived = other_core(other_grads(*other_parts, 8, 8))
    own_first, sent_first, gain_attn_part = first_back(
        place, block_input, other_input, projected_grad, first_weight
    )
    grad_first = own_first + other_x(sent_first).astype(f32)
    small_rows = jnp.concatenate(
        [
            jnp.zeros((ROPE, D), f32),
            gain_attn_part,
            gain_ffn_part[None],
            jnp.pad(
                gain_latent_part.reshape(blocks, latent_depth),
                ((0, 0), (0, depth - latent_depth)),
            ).reshape(1, D),
            grad_router,
            jnp.zeros((128 - ROPE - 3 - experts, D), f32),
        ],
        axis=0,
    )
    first_parts = (first_normed, projected_grad, small_rows, places)
    first_arrived = other_core(first_grads(*first_parts, 8, 8))
    other_kept = other_grads(*other_parts, 0, 8, other_arrived)
    far = first_grads(*first_parts, 4, 4, first_arrived)
    from_y = other_y(far)
    out_total = wide_sum(after(out_own, far), out_beside, out_across)
    block_output = mixed + ring_sum(
        [out_total[r * local_rows : (r + 1) * local_rows] for r in range(RINGS)], bf16
    )
    near = first_grads(*first_parts, 0, 4, first_arrived)
    other_summed = ring_sum(
        [other_kept[2 * r * depth : 2 * (r + 1) * depth] for r in range(RINGS)], bf16
    )
    other_closed = other_summed[:depth] + other_y(other_summed[depth:].astype(bf16)).astype(f32)
    grad_expert_down = expert_grads(
        (every_hidden,), every_grad, units, 0, arrived_down, f32, (from_y,)
    )
    first_closed = close_ring(near, from_y)
    grad_expert_in = expert_grads(
        (every_gate_grad, every_up_grad), every_row, units, 0, arrived_in, f32, (near,)
    )
    grad_shared_in, grad_shared_down = unpack_shared(shared_grads, shared, (from_y,))
    grad_expert_gate_up = grad_expert_in.swapaxes(2, 3)
    grad_expert_down = grad_expert_down[0]
    nope_width = heads * NOPE
    span = heads * (ROPE // 2)
    grad_query_weight = jnp.concatenate(
        [
            first_closed[:, :nope_width].reshape(depth, heads, NOPE),
            first_closed[:, nope_width : nope_width + span].reshape(depth, heads, -1),
            first_closed[:, nope_width + span : query_width].reshape(depth, heads, -1),
        ],
        axis=2,
    ).reshape(depth, query_width)
    both = first_closed[:, query_width:]
    both = both + other_x(both)
    grad_latent_weight = both[:, : KVR + ROPE]
    small_grads = both[:, KVR + ROPE :].T
    keyval_columns = w_keyval.shape[1] * latent_depth // depth
    grad_keyval_weight = (
        other_closed[:, :keyval_columns]
        .reshape(-1, latent_depth, keyval_columns)
        .transpose(1, 0, 2)
        .reshape(latent_depth, -1)
    )
    grad_output_weight = other_closed[:, keyval_columns:].T
    own_inputs = block_input.astype(f32)
    own_scale = rms_scale(own_inputs)
    own_unit = own_inputs * own_scale
    grad_input = grad_mixed + rms_back(grad_first * attn_gain_wide, own_unit, own_scale)
    return (
        block_output,
        grad_input,
        small_grads[0],
        grad_query_weight,
        grad_latent_weight,
        small_grads[2, :latent_depth],
        grad_keyval_weight,
        grad_output_weight,
        small_grads[1],
        small_grads[3 : 3 + experts].T,
        grad_shared_in,
        grad_shared_down,
        grad_expert_gate_up,
        grad_expert_down,
    )


def solution(mesh):
    in_specs = (
        P(("dp", "tensor"), None),
        P("dp", None),
        P("dp"),
        P("dp", None),
        P("dp"),
        P("dp", "tensor"),
        P("dp", None),
        P("dp"),
        P("dp", "tensor"),
        P("tensor", "dp"),
        P("dp"),
        P("dp", None),
        P(None, "dp", "tensor"),
        P("tensor", "dp"),
        P("dp", None, None, "tensor"),
        P("dp", "tensor", None),
        P(("dp", "tensor"), None),
    )
    out_specs = (
        P(("dp", "tensor"), None),
        P(("dp", "tensor"), None),
        P("dp"),
        P("dp", "tensor"),
        P("dp", None),
        P("dp"),
        P("dp", "tensor"),
        P("tensor", "dp"),
        P("dp"),
        P("dp", None),
        P(None, "dp", "tensor"),
        P("tensor", "dp"),
        P("dp", None, None, "tensor"),
        P("dp", "tensor", None),
    )
    body = gather_body if mesh.shape["dp"] == 16 else exchange_body
    return jax.shard_map(body, mesh=mesh, in_specs=in_specs, out_specs=out_specs, check_vma=False)
```

```python
import functools
import math

import jax
import jax.numpy as jnp
from jax import lax
from jax.experimental import pallas as pl
from jax.experimental.pallas import tpu as pltpu
from jax.sharding import PartitionSpec as P

D = 2048
NOPE = 128
ROPE = 64
VD = 128
KVR = 512
TOP = 6


EPSILON = 1e-06


def rms_scale(values):
    return lax.rsqrt(jnp.mean(values * values, axis=-1, keepdims=True) + EPSILON)


def rms_back(grad_unit, unit_rows, row_scale):
    return row_scale * (
        grad_unit - unit_rows * jnp.mean(grad_unit * unit_rows, axis=-1, keepdims=True)
    )


def rotary_tables(segment_row, width):
    count = segment_row.shape[0]
    position = jnp.arange(count, dtype=jnp.int32)
    same = segment_row[:, None] == segment_row[None, :]
    start = jnp.min(jnp.where(same, position[None, :], count), axis=1)
    offset = (position - start).astype(jnp.float32)
    freq = jnp.exp(jnp.arange(width // 2, dtype=jnp.float32) * (-2.0 * math.log(10000.0) / width))
    angle = offset[:, None] * freq[None, :]
    return (jnp.cos(angle), jnp.sin(angle))


def rotate(values, cosine, sine):
    half = values.shape[-1] // 2
    first = values[..., :half]
    second = values[..., half:]
    return jnp.concatenate(
        [first * cosine - second * sine, second * cosine + first * sine], axis=-1
    )


def rotate_back(grads, cosine, sine):
    half = grads.shape[-1] // 2
    first = grads[..., :half]
    second = grads[..., half:]
    return jnp.concatenate(
        [first * cosine + second * sine, second * cosine - first * sine], axis=-1
    )


def allowed_pairs(segment_row, count):
    position = jnp.arange(segment_row.shape[0], dtype=jnp.int32)
    live = position < count
    same = segment_row[:, None] == segment_row[None, :]
    causal = position[None, :] <= position[:, None]
    return same & causal & live[:, None] & live[None, :] | (position[:, None] == position[None, :])


def attention_scores(query_rows, key_nope, key_rope, allowed, scale):
    scores = jnp.einsum(
        "ihd,jhd->hij", query_rows[..., :NOPE], key_nope, preferred_element_type=jnp.float32
    )
    scores = scores + jnp.einsum(
        "ihd,jd->hij", query_rows[..., NOPE:], key_rope, preferred_element_type=jnp.float32
    )
    return jnp.where(allowed[None], scores * scale, -1e30)


def swiglu_back(gate, upper, grad_hidden, axis):
    sigmoid = jax.nn.sigmoid(gate)
    grad_gate = grad_hidden * upper * sigmoid * (1.0 + gate * (1.0 - sigmoid))
    grad_upper = grad_hidden * gate * sigmoid
    return jnp.stack([grad_gate, grad_upper], axis=axis)


def slot_layout(routes, experts, capacity):
    tokens = routes.shape[0]
    flat = routes.reshape(-1)
    onehot = (flat[:, None] == jnp.arange(experts, dtype=jnp.int32)[None, :]).astype(jnp.int32)
    rank = jnp.arange(flat.shape[0], dtype=jnp.int32)
    earlier = (rank[None, :] < rank[:, None]).astype(jnp.bfloat16)
    before = jnp.dot(
        earlier, onehot.astype(jnp.bfloat16), preferred_element_type=jnp.float32
    ).astype(jnp.int32)
    slot_index = jnp.sum(before * onehot, axis=1)
    target = flat * capacity + slot_index
    token_ids = jnp.arange(flat.shape[0], dtype=jnp.int32) // routes.shape[1]
    owner = jnp.full((experts * capacity,), tokens, jnp.int32).at[target].set(token_ids)
    return (slot_index, target, owner)


def to_expert_major(arrived, groups, local_experts):
    capacity = arrived.shape[1]
    width = arrived.shape[2]
    return (
        arrived.reshape(groups, local_experts, capacity, width)
        .transpose(1, 0, 2, 3)
        .reshape(local_experts, groups * capacity, width)
    )


def from_expert_major(results, groups):
    local_experts = results.shape[0]
    width = results.shape[2]
    capacity = results.shape[1] // groups
    return (
        results.reshape(local_experts, groups, capacity, width)
        .transpose(1, 0, 2, 3)
        .reshape(groups * local_experts, capacity, width)
    )


def exchange_body(
    block_input,
    segments,
    counts,
    routes,
    attn_gain,
    w_query,
    w_latent,
    latent_gain,
    w_keyval,
    w_output,
    ffn_gain,
    w_router,
    shared_gate_up,
    shared_down,
    expert_gate_up,
    expert_down,
    cotangent,
):
    gathered = (
        lax.all_gather(attn_gain, "dp", axis=0, tiled=True),
        lax.all_gather(w_query, "dp", axis=0, tiled=True),
        lax.all_gather(w_latent, "dp", axis=0, tiled=True),
        lax.all_gather(latent_gain, "dp", axis=0, tiled=True),
        lax.all_gather(w_keyval, "dp", axis=0, tiled=True),
        lax.all_gather(w_output, "dp", axis=1, tiled=True),
        lax.all_gather(ffn_gain, "dp", axis=0, tiled=True),
        lax.all_gather(w_router, "dp", axis=0, tiled=True),
        lax.all_gather(shared_gate_up, "dp", axis=1, tiled=True),
        lax.all_gather(shared_down, "dp", axis=1, tiled=True),
    )
    (
        full_attn_gain,
        query_weight,
        latent_weight,
        full_latent_gain,
        keyval_weight,
        output_weight,
        full_ffn_gain,
        router_weight,
        shared_in,
        shared_out,
    ) = gathered
    tensor_rank = lax.axis_index("tensor")
    dp_size = lax.axis_size("dp")
    rows_all = lax.all_gather(block_input, "tensor", axis=0, tiled=True)
    tokens = rows_all.shape[0]
    local_rows = block_input.shape[0]
    heads = query_weight.shape[1] // (NOPE + ROPE)
    experts = router_weight.shape[1]
    local_experts = expert_gate_up.shape[0]
    capacity = 2 * tokens * TOP // experts
    scale = (NOPE + ROPE) ** (-0.5)
    start = tensor_rank * local_rows
    cosine, sine = rotary_tables(segments[0], ROPE)
    allowed = allowed_pairs(segments[0], counts[0])
    attn_gain_wide = full_attn_gain.astype(jnp.float32)
    latent_gain_wide = full_latent_gain.astype(jnp.float32)
    ffn_gain_wide = full_ffn_gain.astype(jnp.float32)
    inputs = rows_all.astype(jnp.float32)
    first_scale = rms_scale(inputs)
    first_unit = inputs * first_scale
    first_normed = (first_unit * attn_gain_wide).astype(jnp.bfloat16)
    query = jnp.dot(first_normed, query_weight, preferred_element_type=jnp.float32).reshape(
        tokens, heads, NOPE + ROPE
    )
    query_rows = jnp.concatenate(
        [query[..., :NOPE], rotate(query[..., NOPE:], cosine[:, None, :], sine[:, None, :])],
        axis=-1,
    ).astype(jnp.bfloat16)
    latent_all = jnp.dot(first_normed, latent_weight, preferred_element_type=jnp.float32)
    latent = latent_all[:, :KVR]
    key_rope = rotate(latent_all[:, KVR:], cosine, sine).astype(jnp.bfloat16)
    latent_scale = rms_scale(latent)
    latent_unit = latent * latent_scale
    latent_normed = (latent_unit * latent_gain_wide).astype(jnp.bfloat16)
    keyval = (
        jnp.dot(latent_normed, keyval_weight, preferred_element_type=jnp.float32)
        .astype(jnp.bfloat16)
        .reshape(tokens, heads, NOPE + VD)
    )
    key_nope = keyval[..., :NOPE]
    values = keyval[..., NOPE:]
    scores = attention_scores(query_rows, key_nope, key_rope, allowed, scale)
    row_max = jnp.max(scores, axis=-1, keepdims=True)
    log_total = row_max + jnp.log(jnp.sum(jnp.exp(scores - row_max), axis=-1, keepdims=True))
    weights_low = jnp.exp(scores - log_total).astype(jnp.bfloat16)
    attended = (
        jnp.einsum("hij,jhd->ihd", weights_low, values, preferred_element_type=jnp.float32)
        .astype(jnp.bfloat16)
        .reshape(tokens, heads * VD)
    )
    attn_part = jnp.dot(attended, output_weight, preferred_element_type=jnp.float32)
    mixed = inputs + lax.psum(attn_part, "tensor")
    second_scale = rms_scale(mixed)
    second_unit = mixed * second_scale
    second_normed = (second_unit * ffn_gain_wide).astype(jnp.bfloat16)
    logits = jnp.dot(second_normed, router_weight, preferred_element_type=jnp.float32)
    probabilities = jax.nn.softmax(logits, axis=-1)
    gate_values = jnp.take_along_axis(probabilities, routes, axis=1)
    shared_pre = jnp.einsum(
        "td,gdf->tgf", second_normed, shared_in, preferred_element_type=jnp.float32
    )
    shared_hidden = (jax.nn.silu(shared_pre[:, 0]) * shared_pre[:, 1]).astype(jnp.bfloat16)
    shared_part = jnp.dot(shared_hidden, shared_out, preferred_element_type=jnp.float32)
    slot_index, target, owner = slot_layout(routes, experts, capacity)
    owner_grid = owner.reshape(experts, capacity)
    padded_rows = jnp.concatenate([second_normed, jnp.zeros((1, D), jnp.bfloat16)], axis=0)
    outgoing = padded_rows[owner_grid]
    arrived = lax.all_to_all(outgoing, "dp", split_axis=0, concat_axis=0, tiled=True)
    expert_rows = to_expert_major(arrived, dp_size, local_experts)
    expert_pre = jnp.einsum(
        "erd,egdf->ergf", expert_rows, expert_gate_up, preferred_element_type=jnp.float32
    )
    expert_hidden = (jax.nn.silu(expert_pre[:, :, 0]) * expert_pre[:, :, 1]).astype(jnp.bfloat16)
    expert_result = jnp.einsum(
        "erf,efd->erd", expert_hidden, expert_down, preferred_element_type=jnp.float32
    )
    returning = from_expert_major(expert_result, dp_size)
    returned = lax.all_to_all(
        returning.astype(jnp.bfloat16), "dp", split_axis=0, concat_axis=0, tiled=True
    ).astype(returning.dtype)
    padded_back = jnp.concatenate([returned.reshape(-1, D), jnp.zeros((1, D), jnp.float32)], axis=0)
    picked = padded_back[target].reshape(tokens, TOP, D)
    routed_part = jnp.sum(gate_values[:, :, None] * picked, axis=1)
    branch_sum = lax.psum_scatter(
        (shared_part + routed_part).astype(jnp.bfloat16), "tensor", scatter_dimension=0, tiled=True
    ).astype(jnp.float32)
    block_output = lax.dynamic_slice_in_dim(mixed, start, local_rows, 0) + branch_sum
    grad_rows = lax.all_gather(cotangent, "tensor", axis=0, tiled=True)
    grad_out = grad_rows.astype(jnp.float32)
    grad_shared_hidden = jnp.dot(grad_rows, shared_out.T, preferred_element_type=jnp.float32)
    grad_shared_out = jnp.dot(shared_hidden.T, grad_rows, preferred_element_type=jnp.float32)
    grad_shared_pre = swiglu_back(shared_pre[:, 0], shared_pre[:, 1], grad_shared_hidden, 1).astype(
        jnp.bfloat16
    )
    grad_shared_in = jnp.einsum(
        "td,tgf->gdf", second_normed, grad_shared_pre, preferred_element_type=jnp.float32
    )
    grad_second = jnp.einsum(
        "tgf,gdf->td", grad_shared_pre, shared_in, preferred_element_type=jnp.float32
    )
    gate_by_slot = (
        jnp.zeros((experts * capacity + 1,), jnp.float32).at[target].set(gate_values.reshape(-1))
    )
    slot_ids = jnp.arange(experts * capacity, dtype=jnp.int32).reshape(experts, capacity)
    padded_grad = jnp.concatenate([grad_out, jnp.zeros((1, D), jnp.float32)], axis=0)
    grad_outgoing = (gate_by_slot[slot_ids][..., None] * padded_grad[owner_grid]).astype(
        jnp.bfloat16
    )
    grad_arrived = lax.all_to_all(grad_outgoing, "dp", split_axis=0, concat_axis=0, tiled=True)
    grad_expert_rows = to_expert_major(grad_arrived, dp_size, local_experts)
    grad_expert_hidden = jnp.einsum(
        "erd,efd->erf", grad_expert_rows, expert_down, preferred_element_type=jnp.float32
    )
    grad_expert_down = jnp.einsum(
        "erf,erd->efd", expert_hidden, grad_expert_rows, preferred_element_type=jnp.float32
    )
    grad_expert_pre = swiglu_back(
        expert_pre[:, :, 0], expert_pre[:, :, 1], grad_expert_hidden, 2
    ).astype(jnp.bfloat16)
    grad_expert_gate_up = jnp.einsum(
        "erd,ergf->egdf", expert_rows, grad_expert_pre, preferred_element_type=jnp.float32
    )
    grad_expert_input = jnp.einsum(
        "ergf,egdf->erd", grad_expert_pre, expert_gate_up, preferred_element_type=jnp.float32
    )
    grad_returning = from_expert_major(grad_expert_input, dp_size)
    grad_returned = lax.all_to_all(
        grad_returning.astype(jnp.bfloat16), "dp", split_axis=0, concat_axis=0, tiled=True
    ).astype(grad_returning.dtype)
    padded_grad_back = jnp.concatenate(
        [grad_returned.reshape(-1, D), jnp.zeros((1, D), jnp.float32)], axis=0
    )
    grad_second = grad_second + jnp.sum(padded_grad_back[target].reshape(tokens, TOP, D), axis=1)
    grad_gates = jnp.sum(grad_out[:, None, :] * picked, axis=-1)
    grad_second, grad_gates = (
        lax.psum(grad_second.astype(jnp.bfloat16), "tensor").astype(jnp.float32),
        lax.psum(grad_gates.astype(jnp.bfloat16), "tensor").astype(jnp.float32),
    )
    chosen = (routes[:, :, None] == jnp.arange(experts, dtype=jnp.int32)[None, None, :]).astype(
        jnp.float32
    )
    grad_probabilities = jnp.sum(chosen * grad_gates[:, :, None], axis=1)
    grad_logits = probabilities * (
        grad_probabilities - jnp.sum(probabilities * grad_probabilities, axis=-1, keepdims=True)
    )
    grad_logits_low = grad_logits.astype(jnp.bfloat16)
    grad_router = jnp.dot(second_normed.T, grad_logits_low, preferred_element_type=jnp.float32)
    grad_second = grad_second + jnp.dot(
        grad_logits_low, router_weight.T, preferred_element_type=jnp.float32
    )
    gain_ffn_grad = jnp.sum(grad_second * second_unit, axis=0)
    grad_mixed = grad_out + rms_back(grad_second * ffn_gain_wide, second_unit, second_scale)
    grad_attn_low = grad_mixed.astype(jnp.bfloat16)
    grad_output_weight = jnp.dot(attended.T, grad_attn_low, preferred_element_type=jnp.float32)
    grad_attended = (
        jnp.dot(grad_attn_low, output_weight.T, preferred_element_type=jnp.float32)
        .astype(jnp.bfloat16)
        .reshape(tokens, heads, VD)
    )
    scores = attention_scores(query_rows, key_nope, key_rope, allowed, scale)
    weights = jnp.exp(scores - log_total)
    weights_low = weights.astype(jnp.bfloat16)
    grad_weights = jnp.einsum(
        "ihd,jhd->hij", grad_attended, values, preferred_element_type=jnp.float32
    )
    grad_values = jnp.einsum(
        "hij,ihd->jhd", weights_low, grad_attended, preferred_element_type=jnp.float32
    )
    grad_scores = (
        weights * (grad_weights - jnp.sum(weights * grad_weights, axis=-1, keepdims=True))
    ).astype(jnp.bfloat16)
    grad_query_nope = (
        jnp.einsum("hij,jhd->ihd", grad_scores, key_nope, preferred_element_type=jnp.float32)
        * scale
    )
    grad_query_rope = (
        jnp.einsum("hij,jd->ihd", grad_scores, key_rope, preferred_element_type=jnp.float32) * scale
    )
    grad_key_nope = (
        jnp.einsum(
            "hij,ihd->jhd", grad_scores, query_rows[..., :NOPE], preferred_element_type=jnp.float32
        )
        * scale
    )
    grad_key_rope = (
        jnp.einsum(
            "hij,ihd->jd", grad_scores, query_rows[..., NOPE:], preferred_element_type=jnp.float32
        )
        * scale
    )
    grad_query = (
        jnp.concatenate(
            [grad_query_nope, rotate_back(grad_query_rope, cosine[:, None, :], sine[:, None, :])],
            axis=-1,
        )
        .astype(jnp.bfloat16)
        .reshape(tokens, heads * (NOPE + ROPE))
    )
    grad_query_weight = jnp.dot(first_normed.T, grad_query, preferred_element_type=jnp.float32)
    grad_first = jnp.dot(grad_query, query_weight.T, preferred_element_type=jnp.float32)
    grad_keyval = (
        jnp.concatenate([grad_key_nope, grad_values], axis=-1)
        .astype(jnp.bfloat16)
        .reshape(tokens, heads * (NOPE + VD))
    )
    grad_keyval_weight = jnp.dot(latent_normed.T, grad_keyval, preferred_element_type=jnp.float32)
    grad_latent_normed = jnp.dot(grad_keyval, keyval_weight.T, preferred_element_type=jnp.float32)
    gain_latent_part = jnp.sum(grad_latent_normed * latent_unit, axis=0)
    grad_latent = rms_back(grad_latent_normed * latent_gain_wide, latent_unit, latent_scale)
    grad_latent_all = jnp.concatenate(
        [grad_latent, rotate_back(grad_key_rope, cosine, sine)], axis=-1
    )
    grad_first, grad_latent_all, gain_latent_grad = (
        lax.psum(grad_first.astype(jnp.bfloat16), "tensor").astype(jnp.float32),
        lax.psum(grad_latent_all.astype(jnp.bfloat16), "tensor").astype(jnp.float32),
        lax.psum(gain_latent_part.astype(jnp.bfloat16), "tensor").astype(jnp.float32),
    )
    grad_latent_low = grad_latent_all.astype(jnp.bfloat16)
    grad_latent_weight = jnp.dot(
        first_normed.T, grad_latent_low, preferred_element_type=jnp.float32
    )
    grad_first = grad_first + jnp.dot(
        grad_latent_low, latent_weight.T, preferred_element_type=jnp.float32
    )
    gain_attn_grad = jnp.sum(grad_first * first_unit, axis=0)
    grad_inputs = grad_mixed + rms_back(grad_first * attn_gain_wide, first_unit, first_scale)
    grad_local = lax.dynamic_slice_in_dim(grad_inputs, start, local_rows, 0)
    summed = (
        lax.psum_scatter(gain_attn_grad, "dp", scatter_dimension=0, tiled=True),
        lax.psum_scatter(grad_query_weight, "dp", scatter_dimension=0, tiled=True),
        lax.psum_scatter(grad_latent_weight, "dp", scatter_dimension=0, tiled=True),
        lax.psum_scatter(gain_latent_grad, "dp", scatter_dimension=0, tiled=True),
        lax.psum_scatter(grad_keyval_weight, "dp", scatter_dimension=0, tiled=True),
        lax.psum_scatter(grad_output_weight, "dp", scatter_dimension=1, tiled=True),
        lax.psum_scatter(gain_ffn_grad, "dp", scatter_dimension=0, tiled=True),
        lax.psum_scatter(grad_router, "dp", scatter_dimension=0, tiled=True),
        lax.psum_scatter(grad_shared_in, "dp", scatter_dimension=1, tiled=True),
        lax.psum_scatter(grad_shared_out, "dp", scatter_dimension=1, tiled=True),
    )
    return (
        block_output,
        grad_local,
        summed[0],
        summed[1],
        summed[2],
        summed[3],
        summed[4],
        summed[5],
        summed[6],
        summed[7],
        summed[8],
        summed[9],
        grad_expert_gate_up,
        grad_expert_down,
    )


RINGS = 4


def cost(flops, bytes_accessed, transcendentals):
    return pl.CostEstimate(
        flops=flops // 16,
        bytes_accessed=bytes_accessed // 16,
        transcendentals=transcendentals // 16,
    )


def ring_step(values):
    return lax.ppermute(values, "dp", [(i, (i + RINGS) % 16) for i in range(16)])


def other_y(values):
    return lax.ppermute(values, "dp", [(i, i ^ 2) for i in range(16)])


def other_core(values):
    return lax.ppermute(values, "dp", [(i, i ^ 1) for i in range(16)])


def other_x(values):
    return lax.ppermute(values, "tensor", [(0, 1), (1, 0)])


def fence_kernel(*refs):
    pass


def after(values, *others):
    anywhere = pl.BlockSpec(memory_space=pl.ANY)
    return pl.pallas_call(
        fence_kernel,
        out_shape=jax.ShapeDtypeStruct(values.shape, values.dtype),
        in_specs=[anywhere] * (1 + len(others)),
        out_specs=anywhere,
        input_output_aliases={0: 0},
    )(values, *others)


def gather_whole(rows, early):
    ring = [rows, ring_step(rows)]
    ring.append(ring_step(ring[1]))
    ring.append(ring_step(after(ring[2], early)))
    over_x = [other_x(part) for part in ring]
    groups = []
    for k in (0, 2):
        held = jnp.concatenate(ring[k : k + 2], axis=0)
        across = jnp.concatenate(over_x[k : k + 2], axis=0)
        beside = other_y(held)
        groups.append((held, beside, across, other_x(beside) if k else other_y(across)))
    return groups, ring, over_x


def gather_rows(rows, corners):
    held = [rows, ring_step(rows)]
    first = (other_y(rows), other_x(rows))
    held.append(ring_step(after(held[1], *first)))
    held.append(ring_step(held[2]))
    groups = []
    for k, current in enumerate((held[0], held[1], jnp.concatenate(held[2:], axis=0))):
        beside, across = (other_y(current), other_x(current)) if k else first
        corner = other_x(beside) if corners[k] == "x" else other_y(across)
        groups.append((current, beside, across, corner))
    return held, groups


def add_low(first, second):
    return (first.astype(jnp.float32) + second.astype(jnp.float32)).astype(jnp.bfloat16)


def turn_corner(plane, direction):
    own, beside, across, corner = plane
    if direction == "x":
        return own, add_low(beside, other_x(corner)), across
    return own, beside, add_low(across, other_y(corner))


def close_plane(turned):
    own, beside, across = turned
    return own, other_y(beside), other_x(across)


def wide_sum(*values):
    total = values[0].astype(jnp.float32)
    for value in values[1:]:
        total = total + value.astype(jnp.float32)
    return total


def ring_sum(parts, low):
    moving = parts[1]
    for distance in (2, 3, 0):
        moving = ring_step(moving.astype(low)).astype(jnp.float32) + parts[distance].astype(
            jnp.float32
        )
    return moving


def ring_shards(shard):
    held = [shard]
    for _ in range(RINGS - 1):
        held.append(ring_step(held[-1]))
    return held


def gather_weight(shard, early):
    held, besides = [shard], []
    for distance in range(RINGS):
        beside = other_y(after(held[1], *early) if distance == 1 else held[distance])
        besides.append(beside)
        if distance < RINGS - 1:
            source = after(held[distance], besides[distance - 1]) if distance else shard
            held.append(ring_step(source))
    chunks = []
    for distance, (current, beside) in enumerate(zip(held, besides)):
        for flip_y, chunk in ((0, current), (1, beside)):
            for flip_core, piece in ((0, chunk), (1, other_core(chunk))):
                chunks.append(((distance, flip_y, flip_core), piece))
    return chunks, held, besides


def place_of(coords, key):
    z, y, core = coords
    distance, flip_y, flip_core = key
    return (
        lax.rem(z + RINGS - distance, RINGS) * 4
        + (1 - y if flip_y else y) * 2
        + (1 - core if flip_core else core)
    )


def weight_keys():
    return [
        (distance, flip_y, flip_core)
        for flip_core in (0, 1)
        for flip_y in (0, 1)
        for distance in range(RINGS)
    ]


def scatter_blocks(grads, low):
    half = grads.shape[0] // 2
    total = grads[:half].astype(jnp.float32) + other_core(grads[half:].astype(low)).astype(
        jnp.float32
    )
    quarter = half // 2
    total = total[:quarter] + other_y(total[quarter:].astype(low)).astype(jnp.float32)
    size = quarter // RINGS
    return ring_sum([total[r * size : (r + 1) * size] for r in range(RINGS)], low)


def pick_blocks(values, order):
    chosen = order[:, None] == jnp.arange(values.shape[0], dtype=jnp.int32)[None, :]
    chosen = chosen.reshape(chosen.shape + (1,) * (values.ndim - 1))
    return jnp.sum(jnp.where(chosen, values[None], 0.0), axis=1)


def wide_dot(left, right):
    return jnp.dot(left, right, preferred_element_type=jnp.float32)


def dot_turned(left, right):
    return lax.dot_general(left, right, (((1,), (1,)), ((), ())), preferred_element_type=jnp.float32)


def dot_rows(left, right):
    return lax.dot_general(left, right, (((0,), (0,)), ((), ())), preferred_element_type=jnp.float32)


TILE = 256


def whole(array):
    return pl.BlockSpec(array.shape, lambda *i: (0,) * array.ndim)


def in_vmem(count):
    return [pl.BlockSpec(memory_space=pltpu.VMEM)] * count


def in_place(count):
    return [pl.BlockSpec(memory_space=pl.ANY)] * count


def head_scores(heads, h, nope_ref, turned_ref, keyval_ref, key_ref, masks):
    span = ROPE // 2 * heads
    column = pl.ds(pl.multiple_of(h * NOPE, NOPE), NOPE)
    key_column = pl.ds(pl.multiple_of(h * (NOPE + VD), NOPE), NOPE)
    scores = dot_turned(nope_ref[:, column], keyval_ref[:, key_column])
    for k in (0, 1):
        part = turned_ref[:, k * span : (k + 1) * span]
        part = jnp.where(masks, part, jnp.zeros_like(part))
        scores += dot_turned(part, key_ref[:, k * span : (k + 1) * span])
    return scores * (NOPE + ROPE) ** (-0.5)


def head_lanes(heads, h):
    span = ROPE // 2 * heads
    lane = lax.broadcasted_iota(jnp.int32, (1, span), 1)
    return (lane >= h * (ROPE // 2)) & (lane < (h + 1) * (ROPE // 2))


def allowed_rows(count, segment_row, segment_column):
    tokens = segment_row.shape[1]
    column = lax.broadcasted_iota(jnp.int32, (tokens, tokens), 0)
    row = lax.broadcasted_iota(jnp.int32, (tokens, tokens), 1)
    live = (column < count) & (row < count) & (row <= column)
    return (segment_row == segment_column) & live | (column == row)


def attend_kernel(
    keys,
    extra,
    heads,
    sizes,
    place_ref,
    segment_row_ref,
    segment_column_ref,
    cosine_ref,
    sine_ref,
    own_ref,
    other_ref,
    *refs,
):
    depth, query_width, used, latent_depth, keyval_part, first_width = sizes
    chunks = refs[: len(keys)]
    (
        own_out,
        sent_out,
        first_ref,
        keyval_weight_ref,
        output_ref,
        normed_ref,
        nope_ref,
        turned_ref,
        latent_ref,
        key_ref,
        keyval_ref,
        total_ref,
        attended_ref,
        gains_ref,
        latent_gain_ref,
        semaphores,
    ) = refs[len(keys) + extra :]
    f32, bf16 = jnp.float32, jnp.bfloat16
    local_rows = own_ref.shape[0]
    tokens = 2 * local_rows
    coords = (place_ref[0], place_ref[1], place_ref[2])
    x = place_ref[3]
    copies = []
    parts = depth // latent_depth
    for key, chunk in zip(keys, chunks):
        block = place_of(coords, key)
        rows = pl.ds(pl.multiple_of(block * depth, depth), depth)
        small_rows = pl.ds(pl.multiple_of(block * latent_depth, latent_depth), latent_depth)
        moves = [(chunk.at[:, pl.ds(0, first_width)], first_ref.at[rows])]
        for k in range(parts):
            moves.append(
                (
                    chunk.at[
                        pl.ds(k * latent_depth, latent_depth), pl.ds(first_width, keyval_part)
                    ],
                    keyval_weight_ref.at[small_rows, pl.ds(k * keyval_part, keyval_part)],
                )
            )
        moves.append(
            (
                chunk.at[:, pl.ds(first_width + keyval_part, heads * VD)],
                output_ref.at[rows],
            )
        )
        for source, target in moves:
            copies.append(pltpu.make_async_copy(source, target, semaphores.at[len(copies)]))
    for copy in copies:
        copy.start()
    for copy in copies:
        copy.wait()

    edge = query_width + KVR
    spread = jnp.transpose(first_ref[:, edge:].astype(f32))[used - edge : used - edge + 8]
    gains_ref[...] = spread
    gain = spread[0:1]
    source = lax.broadcasted_iota(jnp.int32, (D, KVR), 0)
    target = lax.broadcasted_iota(jnp.int32, (D, KVR), 1)
    wanted = target // latent_depth * depth + target % latent_depth
    chosen = jnp.where(source == wanted, 1.0, 0.0).astype(bf16)
    latent_gain = wide_dot(spread.astype(bf16), chosen)[2:3]
    latent_gain_ref[...] = latent_gain
    for ref, start in ((own_ref, x * local_rows), (other_ref, (1 - x) * local_rows)):
        rows = ref[...].astype(f32)
        unit = rows * lax.rsqrt(jnp.mean(rows * rows, axis=1, keepdims=True) + EPSILON)
        normed_ref[pl.ds(pl.multiple_of(start, local_rows), local_rows), :] = (unit * gain).astype(
            bf16
        )
    nope_width = heads * NOPE
    span = heads * (ROPE // 2)
    half = nope_width // 2
    for k in (0, 1):
        nope_ref[:, k * half : (k + 1) * half] = wide_dot(
            normed_ref[...], first_ref[:, k * half : (k + 1) * half]
        ).astype(bf16)
    turning = wide_dot(normed_ref[...], first_ref[:, nope_width : nope_width + 2 * span])
    cosine, sine = cosine_ref[...], sine_ref[...]
    first, second = turning[:, :span], turning[:, span:]
    turned_ref[:, :span] = (first * cosine - second * sine).astype(bf16)
    turned_ref[:, span:] = (second * cosine + first * sine).astype(bf16)
    latent = wide_dot(normed_ref[...], first_ref[:, query_width : query_width + KVR])
    latent_ref[...] = latent
    tail = wide_dot(normed_ref[...], first_ref[:, query_width + KVR :])
    lane = lax.broadcasted_iota(jnp.int32, (1, tail.shape[1]), 1)
    swapped = jnp.where(
        lane < ROPE // 2,
        -pltpu.roll(tail, tail.shape[1] - ROPE // 2, 1),
        pltpu.roll(tail, ROPE // 2, 1),
    )
    width = tail.shape[1]
    turned_key = tail * cosine[:, :width] + swapped * sine[:, :width]
    turned_key = jnp.where(lane < ROPE, turned_key, 0.0).astype(bf16)
    source = lax.broadcasted_iota(jnp.int32, (width, 2 * span), 0)
    target = lax.broadcasted_iota(jnp.int32, (width, 2 * span), 1)
    wanted = target % (ROPE // 2) + jnp.where(target < span, 0, ROPE // 2)
    key_ref[...] = wide_dot(turned_key, (source == wanted).astype(bf16)).astype(bf16)
    unit = latent * lax.rsqrt(jnp.mean(latent * latent, axis=1, keepdims=True) + EPSILON)
    latent_normed = (unit * latent_gain).astype(bf16)
    half = keyval_ref.shape[1] // 4
    for k in range(4):
        keyval_ref[:, k * half : (k + 1) * half] = wide_dot(
            latent_normed, keyval_weight_ref[:, k * half : (k + 1) * half]
        ).astype(bf16)
    allowed = allowed_rows(place_ref[4], segment_row_ref[...], segment_column_ref[...])
    total_lane = lax.broadcasted_iota(jnp.int32, total_ref.shape, 1)
    total_ref[...] = jnp.zeros_like(total_ref)

    def one_head(h, _):
        scores = head_scores(
            heads, h, nope_ref, turned_ref, keyval_ref, key_ref, head_lanes(heads, h)
        )
        scores = jnp.where(allowed, scores, -1e30)
        most = jnp.max(scores, axis=1, keepdims=True)
        total = most + jnp.log(jnp.sum(jnp.exp(scores - most), axis=1, keepdims=True))
        weights = jnp.exp(scores - total).astype(bf16)
        total_ref[...] += jnp.where(total_lane == h, total, 0.0)
        value_column = pl.ds(pl.multiple_of(h * (NOPE + VD) + NOPE, NOPE), VD)
        attended_ref[:, pl.ds(pl.multiple_of(h * VD, VD), VD)] = wide_dot(
            weights, keyval_ref[:, value_column]
        ).astype(bf16)
        return 0

    lax.fori_loop(0, heads, one_head, 0)
    own = pl.ds(pl.multiple_of(x * local_rows, local_rows), local_rows)
    other = pl.ds(pl.multiple_of((1 - x) * local_rows, local_rows), local_rows)
    pieces = 4
    size = output_ref.shape[0] // pieces
    for k in range(pieces):
        columns = slice(k * size, (k + 1) * size)
        own_out[:, columns] = dot_turned(attended_ref[own, :], output_ref[columns, :])
        sent_out[:, columns] = dot_turned(attended_ref[other, :], output_ref[columns, :]).astype(
            bf16
        )


def attend_forward(place, segments, cosine, sine, own, other, chunks, heads, sizes, others):
    depth, query_width, used, latent_depth, keyval_part, first_width = sizes
    f32, bf16 = jnp.float32, jnp.bfloat16
    keys = [key for key, _ in chunks]
    local_rows = own.shape[0]
    tokens = 2 * local_rows
    span = heads * (ROPE // 2)
    shapes = [
        ((local_rows, D), f32),
        ((local_rows, D), bf16),
        ((D, first_width), bf16),
        ((KVR, heads * (NOPE + VD)), bf16),
        ((D, heads * VD), bf16),
        ((tokens, D), bf16),
        ((tokens, heads * NOPE), bf16),
        ((tokens, 2 * span), bf16),
        ((tokens, KVR), f32),
        ((tokens, 2 * span), bf16),
        ((tokens, heads * (NOPE + VD)), bf16),
        ((tokens, 128), f32),
        ((tokens, heads * VD), bf16),
        ((8, D), f32),
        ((1, KVR), f32),
    ]
    return pl.pallas_call(
        functools.partial(attend_kernel, keys, len(others), heads, sizes),
        out_shape=[jax.ShapeDtypeStruct(*shape) for shape in shapes],
        in_specs=[pl.BlockSpec(memory_space=pltpu.SMEM)]
        + in_vmem(6)
        + in_place(len(chunks) + len(others)),
        out_specs=in_vmem(len(shapes)),
        scratch_shapes=[
            pltpu.SemaphoreType.DMA((len(chunks) * (2 + depth // latent_depth),))
        ],
        compiler_params=pltpu.CompilerParams(vmem_limit_bytes=48 * 1024 * 1024),
        cost_estimate=cost(
            flops=2 * tokens * D * (first_width + heads * VD + 1024),
            bytes_accessed=4 * D * (first_width + 1536),
            transcendentals=2 * heads * tokens * tokens,
        ),
    )(
        place,
        segments,
        segments.T,
        cosine,
        sine,
        own,
        other,
        *[piece for _, piece in chunks],
        *others,
    )


def attend_back_kernel(
    heads,
    place_ref,
    segment_row_ref,
    segment_column_ref,
    cosine_ref,
    sine_ref,
    own_ref,
    other_ref,
    keyval_weight_ref,
    output_ref,
    nope_ref,
    turned_ref,
    latent_ref,
    key_ref,
    keyval_ref,
    total_ref,
    latent_gain_ref,
    projected_ref,
    keyval_grad_ref,
    latent_out,
    gain_ref,
    grad_ref,
    turn_ref,
    back_ref,
):
    f32, bf16 = jnp.float32, jnp.bfloat16
    local_rows = own_ref.shape[0]
    x = place_ref[3]
    span = heads * (ROPE // 2)
    nope_width = heads * NOPE
    query_width = nope_width + 2 * span
    scale = (NOPE + ROPE) ** (-0.5)
    for ref, start in ((own_ref, x * local_rows), (other_ref, (1 - x) * local_rows)):
        rows = pl.ds(pl.multiple_of(start, local_rows), local_rows)
        for k in (0, 1):
            half = slice(k * nope_width // 2, (k + 1) * nope_width // 2)
            grad_ref[rows, half] = wide_dot(ref[...], output_ref[:, half]).astype(bf16)
    allowed = allowed_rows(place_ref[4], segment_row_ref[...], segment_column_ref[...])
    total_lane = lax.broadcasted_iota(jnp.int32, total_ref.shape, 1)
    turn_ref[...] = jnp.zeros_like(turn_ref)
    back_ref[...] = jnp.zeros_like(back_ref)

    def one_head(h, _):
        mask = head_lanes(heads, h)
        scores = head_scores(heads, h, nope_ref, turned_ref, keyval_ref, key_ref, mask)
        total = jnp.sum(jnp.where(total_lane == h, total_ref[...], 0.0), axis=1, keepdims=True)
        weights = jnp.exp(jnp.where(allowed, scores, -1e30) - total)
        weights_low = weights.astype(bf16)
        column = pl.ds(pl.multiple_of(h * NOPE, NOPE), NOPE)
        key_column = pl.ds(pl.multiple_of(h * (NOPE + VD), NOPE), NOPE)
        value_column = pl.ds(pl.multiple_of(h * (NOPE + VD) + NOPE, NOPE), VD)
        grads = grad_ref[:, column]
        grad_weights = dot_turned(grads, keyval_ref[:, value_column])
        keyval_grad_ref[:, value_column] = dot_rows(weights_low, grads).astype(bf16)
        grad_scores = (
            weights * (grad_weights - jnp.sum(weights * grad_weights, axis=1, keepdims=True))
        ).astype(bf16)
        projected_ref[:, column] = (
            scale * wide_dot(grad_scores, keyval_ref[:, key_column])
        ).astype(bf16)
        keyval_grad_ref[:, key_column] = (
            scale * dot_rows(grad_scores, nope_ref[:, column])
        ).astype(bf16)
        for k in (0, 1):
            part = slice(k * span, (k + 1) * span)
            turn = wide_dot(grad_scores, key_ref[:, part])
            turn_ref[:, part] += jnp.where(mask, turn, 0.0)
            own = turned_ref[:, part]
            own = jnp.where(mask, own, jnp.zeros_like(own))
            back_ref[:, part] += dot_rows(grad_scores, own)
        return 0

    lax.fori_loop(0, heads, one_head, 0)
    cosine, sine = cosine_ref[...], sine_ref[...]
    first, second = scale * turn_ref[:, :span], scale * turn_ref[:, span:]
    projected_ref[:, nope_width : nope_width + span] = (first * cosine + second * sine).astype(bf16)
    projected_ref[:, nope_width + span : query_width] = (second * cosine - first * sine).astype(
        bf16
    )
    folded = []
    for k in (0, 1):
        part = scale * back_ref[:, k * span : (k + 1) * span]
        shift = span // 2
        while shift >= ROPE // 2:
            part = part + pltpu.roll(part, shift, 1)
            shift //= 2
        folded.append(part)
    width = projected_ref.shape[1] - query_width - KVR
    lane = lax.broadcasted_iota(jnp.int32, (1, width), 1)
    first = (folded[0] * cosine + folded[1] * sine)[:, :width]
    second = (folded[1] * cosine - folded[0] * sine)[:, :width]
    projected_ref[:, query_width + KVR :] = jnp.where(
        lane < ROPE // 2, first, jnp.where(lane < ROPE, second, 0.0)
    ).astype(bf16)
    gain = latent_gain_ref[...]
    latent = latent_ref[...]
    row_scale = lax.rsqrt(jnp.mean(latent * latent, axis=1, keepdims=True) + EPSILON)
    unit = latent * row_scale
    latent_out[...] = (unit * gain).astype(bf16)
    grad_normed = dot_turned(keyval_grad_ref[...], keyval_weight_ref[...])
    gain_ref[...] = jnp.sum(grad_normed * unit, axis=0, keepdims=True)
    grad_unit = grad_normed * gain
    projected_ref[:, query_width : query_width + KVR] = (
        row_scale * (grad_unit - unit * jnp.mean(grad_unit * unit, axis=1, keepdims=True))
    ).astype(bf16)


def attend_back(place, segments, cosine, sine, own, other, saved, heads, first_width, others):
    f32, bf16 = jnp.float32, jnp.bfloat16
    keyval = saved[6]
    tokens = 2 * own.shape[0]
    span = heads * (ROPE // 2)
    return pl.pallas_call(
        lambda *refs: attend_back_kernel(heads, *refs[:16], *refs[16 + len(others) :]),
        out_shape=[
            jax.ShapeDtypeStruct((tokens, first_width), bf16),
            jax.ShapeDtypeStruct((tokens, keyval.shape[1]), bf16),
            jax.ShapeDtypeStruct((tokens, KVR), bf16),
            jax.ShapeDtypeStruct((1, KVR), f32),
        ],
        in_specs=[pl.BlockSpec(memory_space=pltpu.SMEM)] + in_vmem(15) + in_place(len(others)),
        out_specs=in_vmem(4),
        scratch_shapes=[
            pltpu.VMEM((tokens, heads * NOPE), bf16),
            pltpu.VMEM((tokens, 2 * span), f32),
            pltpu.VMEM((tokens, 2 * span), f32),
        ],
        compiler_params=pltpu.CompilerParams(vmem_limit_bytes=48 * 1024 * 1024),
        cost_estimate=cost(
            flops=2 * tokens * D * 3000,
            bytes_accessed=2 * D * 1536,
            transcendentals=heads * tokens * tokens,
        ),
    )(
        place,
        segments,
        segments.T,
        cosine,
        sine,
        own,
        other,
        *saved,
        *others,
    )


def first_grads_kernel(extra, places_ref, left_ref, right_ref, small_ref, *refs):
    out_ref = refs[-1]
    size = left_ref.shape[1]
    edge = right_ref.shape[1] - small_ref.shape[0]
    result = dot_rows(left_ref[...], right_ref[...])
    for value, some in (
        (result[:, :edge], slice(0, edge)),
        (result[:, edge:] + jnp.transpose(small_ref[...]), slice(edge, right_ref.shape[1])),
    ):
        if extra:
            value = value + refs[0][:, some].astype(jnp.float32)
        out_ref[:, some] = value.astype(jnp.bfloat16)


def other_grads_kernel(first, extra, places_ref, latent_ref, keyval_ref, grad_ref, attended_ref, *refs):
    out_ref, keyval_all = refs[-2:]
    step = pl.program_id(0)
    size = grad_ref.shape[1]
    latent_size = latent_ref.shape[1] // places_ref.shape[0]
    parts = size // latent_size
    columns = keyval_ref.shape[1] // parts

    @pl.when(step == 0)
    def _():
        for k in range(parts):
            some = slice(k * columns, (k + 1) * columns)
            keyval_all[:, some] = dot_rows(latent_ref[...], keyval_ref[:, some])

    start = pl.multiple_of(places_ref[first + step] * latent_size, latent_size)
    strip = keyval_all[pl.ds(start, latent_size), :]
    keyval = jnp.concatenate([strip[:, k * columns : (k + 1) * columns] for k in range(parts)], axis=0)
    output = dot_rows(grad_ref[...], attended_ref[...])
    for value, some in (
        (keyval, slice(0, columns)),
        (output, slice(columns, columns + output.shape[1])),
    ):
        if extra:
            value = value + refs[0][:, some].astype(jnp.float32)
        out_ref[:, some] = value.astype(jnp.bfloat16)


def still(array):
    return pl.BlockSpec(array.shape, lambda i, where: (0, 0))


def grads_call(kernel, specs, operands, scratch, size, width, places, first, count, arrived):
    extra = [] if arrived is None else [arrived]
    return pl.pallas_call(
        functools.partial(kernel, len(extra)),
        grid_spec=pltpu.PrefetchScalarGridSpec(
            num_scalar_prefetch=1,
            grid=(count,),
            in_specs=specs
            + [pl.BlockSpec((size, width), lambda i, where: (first + i, 0))] * len(extra),
            out_specs=pl.BlockSpec((size, width), lambda i, where: (i, 0)),
            scratch_shapes=scratch,
        ),
        out_shape=jax.ShapeDtypeStruct((count * size, width), jnp.bfloat16),
        compiler_params=pltpu.CompilerParams(vmem_limit_bytes=32 * 1024 * 1024),
        cost_estimate=cost(
            flops=1024 * count * size * width,
            bytes_accessed=4 * count * size * width,
            transcendentals=0,
        ),
    )(places, *operands, *extra)


def first_grads(left, right, small, places, first, count, arrived=None):
    rows, width = right.shape
    size = left.shape[1] // places.shape[0]
    specs = [
        pl.BlockSpec((rows, size), lambda i, where: (0, where[first + i])),
        still(right),
        pl.BlockSpec((small.shape[0], size), lambda i, where: (0, where[first + i])),
    ]
    return grads_call(
        first_grads_kernel, specs, (left, right, small), [], size, width, places, first, count, arrived
    )


def other_grads(latent, keyval, grad, attended, places, first, count, arrived=None):
    rows = grad.shape[0]
    blocks = places.shape[0]
    size = grad.shape[1] // blocks
    parts = size // (latent.shape[1] // blocks)
    width = keyval.shape[1] // parts + attended.shape[1]
    specs = [
        still(latent),
        still(keyval),
        pl.BlockSpec((rows, size), lambda i, where: (0, where[first + i])),
        still(attended),
    ]
    scratch = [pltpu.VMEM((latent.shape[1], keyval.shape[1]), jnp.float32)]
    return grads_call(
        functools.partial(other_grads_kernel, first),
        specs,
        (latent, keyval, grad, attended),
        scratch,
        size,
        width,
        places,
        first,
        count,
        arrived,
    )


def first_back_kernel(place_ref, own_ref, other_ref, grad_ref, weight_ref, own_out, sent_out, gain_ref):
    local_rows = own_ref.shape[0]
    x = place_ref[3]
    size = weight_ref.shape[0] // 4
    for ref, start, out in (
        (own_ref, x * local_rows, own_out),
        (other_ref, (1 - x) * local_rows, sent_out),
    ):
        rows = ref[...].astype(jnp.float32)
        unit = rows * lax.rsqrt(jnp.mean(rows * rows, axis=1, keepdims=True) + EPSILON)
        grads = grad_ref[pl.ds(pl.multiple_of(start, local_rows), local_rows), :]
        for k in range(4):
            some = slice(k * size, (k + 1) * size)
            part = dot_turned(grads, weight_ref[some, :])
            out[:, some] = part.astype(out.dtype)
            gain = jnp.sum(part * unit[:, some], axis=0, keepdims=True)
            if ref is own_ref:
                gain_ref[:, some] = gain
            else:
                gain_ref[:, some] += gain


def first_back(place, own, other, grads, weight):
    f32, bf16 = jnp.float32, jnp.bfloat16
    depth = weight.shape[0]
    return pl.pallas_call(
        first_back_kernel,
        out_shape=[
            jax.ShapeDtypeStruct(own.shape, f32),
            jax.ShapeDtypeStruct(own.shape, bf16),
            jax.ShapeDtypeStruct((1, depth), f32),
        ],
        in_specs=[pl.BlockSpec(memory_space=pltpu.SMEM)] + in_vmem(4),
        out_specs=in_vmem(3),
        compiler_params=pltpu.CompilerParams(vmem_limit_bytes=32 * 1024 * 1024),
        cost_estimate=cost(
            flops=4 * own.shape[0] * weight.shape[0] * weight.shape[1],
            bytes_accessed=2 * weight.shape[0] * weight.shape[1],
            transcendentals=0,
        ),
    )(place, own, other, grads, weight)


def close_ring(near, arrived):
    size = near.shape[0] // RINGS
    total = near.astype(jnp.float32) + arrived.astype(jnp.float32)
    return ring_sum([total[r * size : (r + 1) * size] for r in range(RINGS)], jnp.bfloat16)


def pack_kernel(heads, query_ref, latent_ref, small_ref, keyval_ref, output_ref, out_ref):
    half = ROPE // 2
    head = NOPE + ROPE
    nope_width = heads * NOPE
    for h in range(heads):
        start = h * head
        out_ref[:, h * NOPE : (h + 1) * NOPE] = query_ref[:, start : start + NOPE]
        for k in (0, 1):
            to = nope_width + k * heads * half + h * half
            out_ref[:, to : to + half] = query_ref[
                :, start + NOPE + k * half : start + NOPE + (k + 1) * half
            ]
    at = heads * head
    edge = at + KVR
    out_ref[:, at:edge] = latent_ref[:, :KVR]
    out_ref[:, edge : edge + 128] = jnp.concatenate([latent_ref[:, KVR:], small_ref[...]], axis=1)
    at = edge + 128
    size = keyval_ref.shape[0]
    parts = out_ref.shape[0] // size
    part = keyval_ref.shape[1] // parts
    for k in range(parts):
        out_ref[k * size : (k + 1) * size, at : at + part] = keyval_ref[
            :, k * part : (k + 1) * part
        ]
    out_ref[:, at + part :] = jnp.transpose(output_ref[...].astype(jnp.float32)).astype(
        jnp.bfloat16
    )


def pack_weights(query, latent, small, keyval, output):
    depth, query_width = query.shape
    heads = query_width // (NOPE + ROPE)
    width = query_width + KVR + 128 + keyval.size // depth + output.shape[0]
    return pl.pallas_call(
        functools.partial(pack_kernel, heads),
        out_shape=jax.ShapeDtypeStruct((depth, width), jnp.bfloat16),
        in_specs=in_vmem(5),
        out_specs=pl.BlockSpec(memory_space=pltpu.VMEM),
    )(query, latent, small, keyval, output)


def load_pieces(pieces, starts, target, semaphores):
    size = target.shape[0] // len(pieces)
    copies = [
        pltpu.make_async_copy(
            piece.at[pl.ds(start, size)], target.at[pl.ds(k * size, size)], semaphores.at[k]
        )
        for k, (piece, start) in enumerate(zip(pieces, starts))
    ]
    for copy in copies:
        copy.start()
    for copy in copies:
        copy.wait()


def shared_stride(shared):
    return -(-shared // 32) * 32


def pack_shared_kernel(blocks, shared, in_ref, down_ref, out_ref):
    stride = shared_stride(shared)
    out_ref[...] = jnp.zeros_like(out_ref)
    for k in range(3):
        if k < 2:
            units = jnp.transpose(in_ref[k].astype(jnp.float32)).astype(jnp.bfloat16)
        else:
            units = down_ref[...]
        for b in range(blocks):
            out_ref[b, k * stride : k * stride + shared] = units[b * shared : (b + 1) * shared]


def pack_shared(shared_in, shared_down, blocks, others):
    depth = shared_in.shape[1]
    shared = shared_down.shape[0] // blocks
    return pl.pallas_call(
        lambda in_ref, down_ref, *refs: pack_shared_kernel(
            blocks, shared, in_ref, down_ref, refs[-1]
        ),
        out_shape=jax.ShapeDtypeStruct((blocks, 3 * shared_stride(shared), depth), jnp.bfloat16),
        in_specs=in_vmem(2) + in_place(len(others)),
        out_specs=pl.BlockSpec(memory_space=pltpu.VMEM),
    )(shared_in, shared_down, *others)


def unpack_shared_kernel(shared, packed_ref, in_ref, down_ref, units_ref):
    stride = shared_stride(shared)
    blocks = packed_ref.shape[0]
    for k in range(3):
        target = down_ref if k == 2 else units_ref
        for b in range(blocks):
            target[b * shared : (b + 1) * shared, :] = packed_ref[
                b, k * stride : k * stride + shared
            ].astype(jnp.float32)
        if k < 2:
            in_ref[k] = jnp.transpose(units_ref[...])


def unpack_shared(packed, shared, others):
    blocks, _, depth = packed.shape
    return pl.pallas_call(
        lambda packed_ref, *refs: unpack_shared_kernel(shared, packed_ref, *refs[len(others) :]),
        out_shape=[
            jax.ShapeDtypeStruct((2, depth, blocks * shared), jnp.float32),
            jax.ShapeDtypeStruct((blocks * shared, depth), jnp.float32),
        ],
        in_specs=in_vmem(1) + in_place(len(others)),
        out_specs=in_vmem(2),
        scratch_shapes=[pltpu.VMEM((blocks * shared, depth), jnp.float32)],
    )(packed, *others)


def pack_units_kernel(units, shared, own_in, other_in, own_down, other_down, near, far, *refs):
    outs = refs[-3:]
    hole = -(-units // TILE) * TILE
    stride = shared_stride(shared)
    columns = outs[0].shape[1]
    size = near.shape[2]
    for k, out in enumerate(outs):
        first = own_in[0, k] if k < 2 else own_down[0]
        second = other_in[0, k] if k < 2 else other_down[0]
        out[:units] = first
        out[units:hole] = jnp.zeros((hole - units, columns), jnp.bfloat16)
        out[hole : hole + units] = second
        out[hole + units : 2 * hole] = jnp.zeros((hole - units, columns), jnp.bfloat16)
        out[2 * hole :] = jnp.zeros((TILE, columns), jnp.bfloat16)
        for b in range(columns // size):
            part = slice(b * size, (b + 1) * size)
            for at, ref in ((2 * hole, near), (2 * hole + stride, far)):
                out[at : at + shared, part] = ref[b, k * stride : k * stride + shared]


def pack_units(own_in, other_in, own_down, other_down, near, far, shared, others):
    units, depth = own_down.shape[1:]
    size = near.shape[2]
    height = 2 * (-(-units // TILE) * TILE) + TILE
    columns = 2 * size
    in_spec = pl.BlockSpec((1, 2, units, columns), lambda i: (0, 0, 0, i))
    down_spec = pl.BlockSpec((1, units, columns), lambda i: (0, 0, i))
    narrow = pl.BlockSpec((2,) + near.shape[1:], lambda i: (i, 0, 0))
    return pl.pallas_call(
        functools.partial(pack_units_kernel, units, shared),
        grid=(depth // columns,),
        in_specs=[in_spec, in_spec, down_spec, down_spec, narrow, narrow]
        + in_place(len(others)),
        out_specs=[pl.BlockSpec((height, columns), lambda i: (0, i))] * 3,
        out_shape=[jax.ShapeDtypeStruct((height, depth), jnp.bfloat16)] * 3,
        compiler_params=pltpu.CompilerParams(vmem_limit_bytes=32 * 1024 * 1024),
        cost_estimate=cost(
            flops=0, bytes_accessed=12 * height * depth, transcendentals=0
        ),
    )(own_in, other_in, own_down, other_down, near, far, *others)


def expert_grads_kernel(units, count, extra, right_ref, *refs):
    out = refs[-1]
    for k in range(count):

        @pl.when(pl.program_id(0) == k)
        def _():
            result = dot_rows(refs[k][...], right_ref[...])[:units]
            if extra:
                result += refs[count][0, 0].astype(jnp.float32)
            out[0, 0] = result.astype(out.dtype)


def expert_grads(lefts, right, units, column, arrived, kind, others=()):
    total, depth = right.shape
    wide = -(-units // TILE) * TILE
    extra = [] if arrived is None else [arrived]
    out = pl.BlockSpec((1, 1, units, 2 * TILE), lambda k, i: (0, k, 0, i))
    side = pl.BlockSpec((total, wide), lambda k, i: (0, column))
    return pl.pallas_call(
        functools.partial(expert_grads_kernel, units, len(lefts), len(extra)),
        grid=(len(lefts), depth // (2 * TILE)),
        in_specs=[pl.BlockSpec((total, 2 * TILE), lambda k, i: (0, i))]
        + [side] * len(lefts)
        + [out] * len(extra)
        + in_place(len(others)),
        out_specs=out,
        out_shape=jax.ShapeDtypeStruct((1, len(lefts), units, depth), kind),
        compiler_params=pltpu.CompilerParams(vmem_limit_bytes=48 * 1024 * 1024),
        cost_estimate=cost(
            flops=2 * len(lefts) * total * depth * wide,
            bytes_accessed=2 * len(lefts) * total * (depth + wide) + 8 * depth * units,
            transcendentals=0,
        ),
    )(right, *lefts, *extra, *others)


def side_grads_kernel(shared, rows_ref, cots_ref, gate_ref, up_ref, hidden_ref, logit_ref, *outs):
    kept_ref, sent_ref, router_ref = outs
    stride = shared_stride(shared)
    size = kept_ref.shape[2]
    for k, (left, right) in enumerate(
        ((gate_ref, rows_ref), (up_ref, rows_ref), (hidden_ref, cots_ref))
    ):
        result = dot_rows(left[...], right[...])
        for b in range(kept_ref.shape[0]):
            part = slice(b * size, (b + 1) * size)
            kept_ref[b, k * stride : (k + 1) * stride] = result[:stride, part]
            sent_ref[b, k * stride : (k + 1) * stride] = result[
                stride : 2 * stride, part
            ].astype(jnp.bfloat16)
    router_ref[...] = dot_rows(logit_ref[...], rows_ref[...])


def side_grads(rows, cots, gate, up, hidden, logits, shared, blocks):
    total, depth = rows.shape
    column = gate.shape[1] // TILE - 1
    size = depth // blocks
    stride = shared_stride(shared)
    wide = pl.BlockSpec((total, 2 * TILE), lambda i: (0, i))
    side = pl.BlockSpec((total, TILE), lambda i: (0, column))
    packed = pl.BlockSpec((2 * TILE // size, 3 * stride, size), lambda i: (i, 0, 0))
    return pl.pallas_call(
        functools.partial(side_grads_kernel, shared),
        grid=(depth // (2 * TILE),),
        in_specs=[wide, wide, side, side, side, whole(logits)],
        out_specs=[packed, packed, pl.BlockSpec((logits.shape[1], 2 * TILE), lambda i: (0, i))],
        out_shape=[
            jax.ShapeDtypeStruct((blocks, 3 * stride, size), jnp.float32),
            jax.ShapeDtypeStruct((blocks, 3 * stride, size), jnp.bfloat16),
            jax.ShapeDtypeStruct((logits.shape[1], depth), jnp.float32),
        ],
        compiler_params=pltpu.CompilerParams(vmem_limit_bytes=48 * 1024 * 1024),
        cost_estimate=cost(
            flops=8 * total * depth * TILE,
            bytes_accessed=4 * total * depth,
            transcendentals=0,
        ),
    )(rows, cots, gate, up, hidden, logits)


def down_kernel(starts, *refs):
    count = len(starts)
    pieces, weight_ref = refs[:count], refs[count]
    grads_ref, rows_ref, semaphores = refs[-3:]

    @pl.when(pl.program_id(0) == 0)
    def _():
        load_pieces(pieces, starts, rows_ref, semaphores)

    size = rows_ref.shape[0] // 2
    for k in range(2):
        part = slice(k * size, (k + 1) * size)
        grads_ref[part, :] = dot_turned(rows_ref[part, :], weight_ref[...]).astype(jnp.bfloat16)


def down_grads(part, pieces, size, down, kept, others):
    count = len(pieces)
    depth = down.shape[1]
    width = down.shape[0]
    rows = count * size
    return pl.pallas_call(
        functools.partial(down_kernel, tuple(start for _, start in pieces)),
        grid=(width // TILE,),
        in_specs=in_place(count)
        + [pl.BlockSpec((TILE, depth), lambda i: (i, 0))]
        + in_place(len(kept) + len(others)),
        out_specs=[
            pl.BlockSpec((rows, TILE), lambda i: (part, i)),
            pl.BlockSpec((rows, depth), lambda i: (part, 0)),
        ],
        out_shape=[
            jax.ShapeDtypeStruct((2 * rows, width), jnp.bfloat16),
            jax.ShapeDtypeStruct((2 * rows, depth), jnp.bfloat16),
        ],
        scratch_shapes=[pltpu.SemaphoreType.DMA((count,))],
        input_output_aliases={count + 1 + k: k for k in range(len(kept))},
        compiler_params=pltpu.CompilerParams(vmem_limit_bytes=48 * 1024 * 1024),
        cost_estimate=cost(
            flops=2 * rows * depth * width,
            bytes_accessed=2 * (2 * rows * depth + depth * width + rows * width),
            transcendentals=0,
        ),
    )(*[array for array, _ in pieces], down, *kept, *others)


def out_kernel(pieces, *refs):
    hidden_ref, weight_ref = refs[:2]
    outs = refs[2 : 2 + pieces]
    size = hidden_ref.shape[0] // (RINGS * pieces)
    for r in range(RINGS):
        part = hidden_ref[r * pieces * size : (r + 1) * pieces * size, :]
        result = wide_dot(part, weight_ref[...]).astype(jnp.bfloat16)
        for k in range(pieces):
            outs[k][r * size : (r + 1) * size, :] = result[k * size : (k + 1) * size]


def out_rows(pieces, hidden, down):
    rows, width = hidden.shape
    depth = down.shape[1]
    return pl.pallas_call(
        functools.partial(out_kernel, pieces),
        grid=(depth // TILE,),
        in_specs=[whole(hidden), pl.BlockSpec((width, TILE), lambda i: (0, i))],
        out_specs=[pl.BlockSpec((rows // pieces, TILE), lambda i: (0, i))] * pieces,
        out_shape=[jax.ShapeDtypeStruct((rows // pieces, depth), jnp.bfloat16)] * pieces,
        compiler_params=pltpu.CompilerParams(vmem_limit_bytes=48 * 1024 * 1024),
        cost_estimate=cost(
            flops=2 * rows * depth * width,
            bytes_accessed=2 * (rows * depth + depth * width + rows * width),
            transcendentals=0,
        ),
    )(hidden, down)


def mlp_kernel(tiles, starts, others, experts_ref, routed_ref, *refs):
    pieces = len(starts)
    row_refs = refs[:pieces]
    router_ref, gate_col, up_col, down_grad, gate_row, up_row = refs[pieces : pieces + 6]
    outs = refs[pieces + 6 + others :]
    grad_refs = outs[:pieces]
    rows_out, hidden_out, gate_out, up_out, logit_out = outs[pieces : pieces + 5]
    gate_all, up_all, prob_ref, scale_ref, sum_ref, semaphores = outs[pieces + 5 :]
    step = pl.program_id(0)
    third = tiles // 2
    total = rows_out.shape[0]
    size = total // pieces
    lane = lax.broadcasted_iota(jnp.int32, (1, router_ref.shape[1]), 1) - experts_ref[3]

    @pl.when(step == 0)
    def _():
        load_pieces(row_refs, starts, rows_out, semaphores)
        logits = wide_dot(rows_out[...], router_ref[...])
        logits = jnp.where((lane >= 0) & (lane < experts_ref[2]), logits, -1e30)
        raised = jnp.exp(logits - jnp.max(logits, axis=1, keepdims=True))
        chances = raised / jnp.sum(raised, axis=1, keepdims=True)
        prob_ref[...] = chances
        for k in (0, 1):
            chance = jnp.sum(jnp.where(lane == experts_ref[k], chances, 0.0), axis=1, keepdims=True)
            scale_ref[k] = routed_ref[:, k : k + 1] * chance
        scale_ref[2] = jnp.ones_like(scale_ref[2])
        sum_ref[...] = jnp.zeros_like(sum_ref)

    @pl.when(step < tiles)
    def _():
        columns = pl.ds(pl.multiple_of(step * TILE, TILE), TILE)
        kind = step // third
        half = total // 2
        for k in (0, 1):
            part = slice(k * half, (k + 1) * half)
            pre_gate = dot_turned(rows_out[part, :], gate_col[...])
            pre_up = dot_turned(rows_out[part, :], up_col[...])
            grads = down_grad[part, :].astype(jnp.float32)
            scale = scale_ref[kind, part, :]
            sigmoid = 1.0 / (1.0 + jnp.exp(-pre_gate))
            silu = pre_gate * sigmoid
            hidden = (silu * pre_up).astype(jnp.bfloat16).astype(jnp.float32)
            sum_ref[kind, part, :] += jnp.sum(hidden * grads, axis=1, keepdims=True)
            grad_hidden = scale * grads
            low_gate = (grad_hidden * pre_up * (sigmoid + silu * (1.0 - sigmoid))).astype(
                jnp.bfloat16
            )
            low_up = (grad_hidden * silu).astype(jnp.bfloat16)
            gate_all[part, columns] = low_gate
            up_all[part, columns] = low_up
            hidden_out[part, :] = (scale * hidden).astype(jnp.bfloat16)
            gate_out[part, :] = low_gate
            up_out[part, :] = low_up

    @pl.when(step == tiles - 1)
    def _():
        grad_logits = jnp.zeros_like(prob_ref)
        for k in (0, 1):
            own = jnp.where(lane == experts_ref[k], 1.0, 0.0)
            grad_logits += scale_ref[k] * sum_ref[k] * (own - prob_ref[...])
        logit_out[...] = grad_logits.astype(jnp.bfloat16)

    @pl.when(step >= tiles)
    def _():
        some = pl.ds(pl.multiple_of((step - tiles) * 2 * TILE, TILE), 2 * TILE)
        grads = wide_dot(gate_all[...], gate_row[...]) + wide_dot(up_all[...], up_row[...])
        grads += dot_turned(logit_out[...], router_ref[some, :])
        grads = grads.astype(jnp.bfloat16)
        for k in range(pieces):
            grad_refs[k][...] = grads[k * size : (k + 1) * size]


def mlp_plane(distance, experts, routed, rows, down_grad, router, weights, kept, others):
    gate, up = weights
    pieces = len(rows)
    width, depth = gate.shape
    size = routed.shape[0] // pieces
    tiles, columns = width // TILE, depth // (2 * TILE)
    total = pieces * size
    low = jnp.bfloat16

    def early(i):
        return jnp.minimum(i, tiles - 1)

    def late(i):
        return jnp.maximum(i - tiles, 0)

    tile_spec = pl.BlockSpec((total, TILE), lambda i: (distance, early(i)))
    anywhere = pl.BlockSpec(memory_space=pl.ANY)
    first_kept = 2 + pieces + 6
    results = pl.pallas_call(
        functools.partial(
            mlp_kernel, tiles, tuple(start for _, start in rows), len(kept) + len(others)
        ),
        grid=(tiles + columns,),
        in_specs=[pl.BlockSpec(memory_space=pltpu.SMEM), whole(routed)]
        + [anywhere] * pieces
        + [
            pl.BlockSpec((depth, 128), lambda i: (0, router.shape[1] // 128 - 1)),
            pl.BlockSpec((TILE, depth), lambda i: (early(i), 0)),
            pl.BlockSpec((TILE, depth), lambda i: (early(i), 0)),
            tile_spec,
            pl.BlockSpec((width, 2 * TILE), lambda i: (0, late(i))),
            pl.BlockSpec((width, 2 * TILE), lambda i: (0, late(i))),
        ]
        + [anywhere] * (len(kept) + len(others)),
        out_specs=[pl.BlockSpec((size, 2 * TILE), lambda i: (0, late(i)))] * pieces
        + [
            pl.BlockSpec((total, depth), lambda i: (distance, 0)),
            tile_spec,
            tile_spec,
            tile_spec,
            pl.BlockSpec((total, 128), lambda i: (distance, 0)),
        ],
        out_shape=[jax.ShapeDtypeStruct((size, depth), low)] * pieces
        + [
            jax.ShapeDtypeStruct((RINGS * total, many), low)
            for many in (depth, width, width, width, 128)
        ],
        scratch_shapes=[pltpu.VMEM((total, width), low)] * 2
        + [
            pltpu.VMEM((total, 128), jnp.float32),
            pltpu.VMEM((3, total, 1), jnp.float32),
            pltpu.VMEM((3, total, 1), jnp.float32),
            pltpu.SemaphoreType.DMA((pieces,)),
        ],
        input_output_aliases={first_kept + k: pieces + k for k in range(len(kept))},
        compiler_params=pltpu.CompilerParams(vmem_limit_bytes=48 * 1024 * 1024),
        cost_estimate=cost(
            flops=2 * total * depth * width * 4,
            bytes_accessed=2 * (4 * depth * width + 3 * total * depth + 4 * total * width),
            transcendentals=total * width,
        ),
    )(experts, routed, *[array for array, _ in rows], router, gate, up, down_grad, gate, up, *kept, *others)
    return results[:pieces], results[pieces:]


def gather_body(
    block_input,
    segments,
    counts,
    routes,
    attn_gain,
    w_query,
    w_latent,
    latent_gain,
    w_keyval,
    w_output,
    ffn_gain,
    w_router,
    shared_gate_up,
    shared_down,
    expert_gate_up,
    expert_down,
    cotangent,
):
    f32 = jnp.float32
    bf16 = jnp.bfloat16
    blocks = 16
    index = lax.axis_index("dp")
    x = lax.axis_index("tensor")
    coords = jnp.stack([index // 4, (index // 2) % 2, index % 2]).astype(jnp.int32)
    core = coords[2]
    place = jnp.concatenate([coords, x.astype(jnp.int32)[None], counts])
    local_rows = block_input.shape[0]
    tokens = 2 * local_rows
    depth = w_query.shape[0]
    query_width = w_query.shape[1]
    heads = query_width // (NOPE + ROPE)
    experts = w_router.shape[1]
    units = expert_gate_up.shape[3]
    shared = shared_gate_up.shape[2] // blocks
    latent_depth = w_keyval.shape[0]

    used = query_width + KVR + ROPE
    small = jnp.concatenate(
        [
            attn_gain[:, None],
            ffn_gain[:, None],
            jnp.pad(latent_gain, (0, depth - latent_depth))[:, None],
            w_router,
            routes.reshape(depth, -1).astype(bf16),
            jnp.zeros((depth, 128 - ROPE - 3 - experts - 2 * TOP), bf16),
        ],
        axis=1,
    )
    first_width = query_width + KVR + 128
    shards = pack_weights(w_query, w_latent, small, w_keyval, w_output)
    other_input = other_x(block_input)
    expert_in = expert_gate_up.swapaxes(2, 3)
    expert_in_other = other_core(expert_in)
    expert_down_other = other_core(expert_down)
    chunks, held, besides = gather_weight(
        shards, (expert_in_other, expert_down_other, other_input)
    )
    grad_groups, grad_ring, grad_across = gather_whole(
        after(cotangent, held[3], besides[2]), besides[3]
    )

    cosine, sine = rotary_tables(segments[0], ROPE)
    cosine = jnp.tile(cosine, (1, heads))
    sine = jnp.tile(sine, (1, heads))
    sizes = (depth, query_width, used, latent_depth, w_keyval.shape[1] * latent_depth // depth, first_width)
    (
        own_part,
        sent_part,
        first_weight,
        keyval_weight,
        output_turned,
        first_normed,
        nope,
        turned_query,
        latent,
        key,
        keyval,
        total,
        attended,
        gains,
        latent_gain_row,
    ) = attend_forward(
        place,
        segments,
        cosine,
        sine,
        block_input,
        other_input,
        chunks,
        heads,
        sizes,
        (grad_ring[3], grad_across[2], grad_groups[0][1]),
    )
    attn_gain_wide, ffn_gain_wide = gains[0], gains[1]
    mixed = block_input.astype(f32) + own_part + other_x(sent_part).astype(f32)
    second_scale = rms_scale(mixed)
    second_unit = mixed * second_scale
    second_normed = (second_unit * ffn_gain_wide).astype(bf16)

    routes_at = used + 3 + experts
    routes_all = first_weight[:, routes_at : routes_at + 2 * TOP].reshape(blocks * tokens, TOP)
    chip_experts = jnp.stack([index, index + 1 - 2 * core]).astype(jnp.int32)
    routed_all = jnp.any(
        routes_all[None] == chip_experts[:, None, None].astype(bf16), axis=2
    ).astype(f32)
    order = jnp.stack(
        [
            place_of(coords, (distance, flip_y, 0)) * 2 + (1 - x if flip_x else x)
            for distance in range(RINGS)
            for flip_x, flip_y in ((0, 0), (0, 1), (1, 0), (1, 1))
        ]
    )
    routed = jnp.stack(
        [
            pick_blocks(one.reshape(blocks * 2, local_rows), order).reshape(RINGS, -1)
            for one in routed_all
        ],
        axis=2,
    )

    corners = "yxyx"
    row_ring, row_groups = gather_rows(second_normed, "yyx")
    row_planes = [
        [(array, 0) for array in row_groups[0]],
        [(array, 0) for array in row_groups[1]],
        [(array, 0) for array in row_groups[2]],
        [(array, local_rows) for array in row_groups[2]],
    ]

    shared_near = lax.all_to_all(
        after(pack_shared(shared_gate_up, shared_down, blocks, (held[1],)), sent_part),
        "dp",
        split_axis=0,
        concat_axis=0,
        tiled=True,
    )
    shared_far = other_core(shared_near)

    gate_weight, up_weight, down_weight = pack_units(
        expert_in,
        expert_in_other,
        expert_down,
        expert_down_other,
        shared_near,
        shared_far,
        shared,
        (second_normed,),
    )
    half_kept = down_grads(
        0,
        [(array, r * local_rows) for r in (0, 1) for array in grad_groups[0]],
        local_rows,
        down_weight,
        (),
        (row_ring[1],),
    )
    down_grad, every_grad = down_grads(
        1,
        [(array, r * local_rows) for r in (0, 1) for array in grad_groups[1]],
        local_rows,
        down_weight,
        half_kept,
        (row_ring[2],),
    )
    expert_ids = jnp.concatenate(
        [chip_experts, jnp.array([experts, used + 3 - query_width - KVR], jnp.int32)]
    )
    kept = []
    turned, closed = [], []
    for distance in range(RINGS):
        others = [row_ring[3]] if distance == 0 else list(row_groups[2][1:3])
        if distance == 2:
            others = list(turned[0][1:])
        elif distance == 3:
            others = list(turned[1][1:]) + list(closed[0][1:])
        grads, kept = mlp_plane(
            distance,
            expert_ids,
            routed[distance],
            row_planes[distance],
            down_grad,
            first_weight,
            (gate_weight, up_weight),
            kept,
            others,
        )
        turned.append(turn_corner(grads, corners[distance]))
        if distance < RINGS - 1:
            closed.append(close_plane(turned[distance]))
    every_row, every_hidden, every_gate_grad, every_up_grad, logit_grads = kept
    shared_kept, shared_sent, logit_rows = side_grads(
        every_row,
        every_grad,
        every_gate_grad,
        every_up_grad,
        every_hidden,
        logit_grads,
        shared,
        blocks,
    )
    outs = list(out_rows(4, every_hidden, down_weight))
    sent_down = expert_grads((every_hidden,), every_grad, units, 1, None, bf16)
    moving = ring_step(wide_sum(*closed[1]).astype(bf16))
    moving = ring_step(wide_sum(moving, *closed[2]).astype(bf16))
    own, beside, across = turned[3]
    own = after(own, sent_down)
    grad_close = close_plane((own, after(beside, shared_sent), across))
    grad_second = wide_sum(
        ring_step(wide_sum(moving, *grad_close).astype(bf16)),
        after(closed[0][0], outs[0]),
        *closed[0][1:],
    )
    arrived_down = other_core(sent_down)
    router_at = used + 3 - query_width - KVR
    grad_router = logit_rows[router_at : router_at + experts]
    shared_grads = lax.all_to_all(
        add_low(shared_kept, other_core(shared_sent)), "dp", split_axis=0, concat_axis=0, tiled=True
    )

    gain_ffn_part = jnp.sum(grad_second * second_unit, axis=0)
    grad_mixed = cotangent.astype(f32) + rms_back(
        grad_second * ffn_gain_wide, second_unit, second_scale
    )
    grad_mixed_low = grad_mixed.astype(bf16)
    other_grad = other_x(grad_mixed_low)
    outs[3] = after(outs[3], grad_close[2])
    outs[2] = after(outs[2], other_grad)
    out_own, out_beside, out_across = close_plane(turn_corner(outs, "x"))


    places = jnp.stack([place_of(coords, key_of) for key_of in weight_keys()]).astype(jnp.int32)
    projected_grad, keyval_grad, latent_normed, gain_latent_part = attend_back(
        place,
        segments,
        cosine,
        sine,
        grad_mixed_low,
        other_grad,
        (keyval_weight, output_turned, nope, turned_query, latent, key, keyval, total, latent_gain_row),
        heads,
        first_width,
        (shared_grads, arrived_down),
    )
    grad_attn = jnp.concatenate(
        [
            jnp.where(x == 0, grad_mixed_low, other_grad),
            jnp.where(x == 0, other_grad, grad_mixed_low),
        ],
        axis=0,
    )
    ring_places = places.reshape(2, 2, RINGS).swapaxes(1, 2).reshape(-1)
    other_parts = (latent_normed, keyval_grad, grad_attn, attended, ring_places)
    other_arrived = other_core(other_grads(*other_parts, 8, 8))
    own_first, sent_first, gain_attn_part = first_back(
        place, block_input, other_input, projected_grad, first_weight
    )
    grad_first = own_first + other_x(sent_first).astype(f32)
    small_rows = jnp.concatenate(
        [
            jnp.zeros((ROPE, D), f32),
            gain_attn_part,
            gain_ffn_part[None],
            jnp.pad(
                gain_latent_part.reshape(blocks, latent_depth),
                ((0, 0), (0, depth - latent_depth)),
            ).reshape(1, D),
            grad_router,
            jnp.zeros((128 - ROPE - 3 - experts, D), f32),
        ],
        axis=0,
    )
    first_parts = (first_normed, projected_grad, small_rows, places)
    first_arrived = other_core(first_grads(*first_parts, 8, 8))
    other_kept = other_grads(*other_parts, 0, 8, other_arrived)
    far = first_grads(*first_parts, 4, 4, first_arrived)
    from_y = other_y(far)
    arrived_in = other_core(
        expert_grads((every_gate_grad, every_up_grad), every_row, units, 1, None, bf16, (far,))
    )
    out_total = wide_sum(after(out_own, far), out_beside, out_across)
    block_output = mixed + ring_sum(
        [out_total[r * local_rows : (r + 1) * local_rows] for r in range(RINGS)], bf16
    )
    near = first_grads(*first_parts, 0, 4, first_arrived)
    other_summed = ring_sum(
        [other_kept[2 * r * depth : 2 * (r + 1) * depth] for r in range(RINGS)], bf16
    )
    other_closed = other_summed[:depth] + other_y(other_summed[depth:].astype(bf16)).astype(f32)
    grad_expert_down = expert_grads(
        (every_hidden,), every_grad, units, 0, arrived_down, f32, (from_y,)
    )
    grad_expert_in = expert_grads(
        (every_gate_grad, every_up_grad), every_row, units, 0, arrived_in, f32, (near,)
    )
    first_closed = close_ring(after(near, grad_expert_in), from_y)
    grad_shared_in, grad_shared_down = unpack_shared(shared_grads, shared, (from_y,))
    grad_expert_gate_up = grad_expert_in.swapaxes(2, 3)
    grad_expert_down = grad_expert_down[0]
    nope_width = heads * NOPE
    span = heads * (ROPE // 2)
    grad_query_weight = jnp.concatenate(
        [
            first_closed[:, :nope_width].reshape(depth, heads, NOPE),
            first_closed[:, nope_width : nope_width + span].reshape(depth, heads, -1),
            first_closed[:, nope_width + span : query_width].reshape(depth, heads, -1),
        ],
        axis=2,
    ).reshape(depth, query_width)
    both = first_closed[:, query_width:]
    both = both + other_x(both)
    grad_latent_weight = both[:, : KVR + ROPE]
    small_grads = both[:, KVR + ROPE :].T
    keyval_columns = w_keyval.shape[1] * latent_depth // depth
    grad_keyval_weight = (
        other_closed[:, :keyval_columns]
        .reshape(-1, latent_depth, keyval_columns)
        .transpose(1, 0, 2)
        .reshape(latent_depth, -1)
    )
    grad_output_weight = other_closed[:, keyval_columns:].T
    own_inputs = block_input.astype(f32)
    own_scale = rms_scale(own_inputs)
    own_unit = own_inputs * own_scale
    grad_input = grad_mixed + rms_back(grad_first * attn_gain_wide, own_unit, own_scale)
    return (
        block_output,
        grad_input,
        small_grads[0],
        grad_query_weight,
        grad_latent_weight,
        small_grads[2, :latent_depth],
        grad_keyval_weight,
        grad_output_weight,
        small_grads[1],
        small_grads[3 : 3 + experts].T,
        grad_shared_in,
        grad_shared_down,
        grad_expert_gate_up,
        grad_expert_down,
    )


def solution(mesh):
    in_specs = (
        P(("dp", "tensor"), None),
        P("dp", None),
        P("dp"),
        P("dp", None),
        P("dp"),
        P("dp", "tensor"),
        P("dp", None),
        P("dp"),
        P("dp", "tensor"),
        P("tensor", "dp"),
        P("dp"),
        P("dp", None),
        P(None, "dp", "tensor"),
        P("tensor", "dp"),
        P("dp", None, None, "tensor"),
        P("dp", "tensor", None),
        P(("dp", "tensor"), None),
    )
    out_specs = (
        P(("dp", "tensor"), None),
        P(("dp", "tensor"), None),
        P("dp"),
        P("dp", "tensor"),
        P("dp", None),
        P("dp"),
        P("dp", "tensor"),
        P("tensor", "dp"),
        P("dp"),
        P("dp", None),
        P(None, "dp", "tensor"),
        P("tensor", "dp"),
        P("dp", None, None, "tensor"),
        P("dp", "tensor", None),
    )
    body = gather_body if mesh.shape["dp"] == 16 else exchange_body
    return jax.shard_map(body, mesh=mesh, in_specs=in_specs, out_specs=out_specs, check_vma=False)
```

```python
import functools
import math

import jax
import jax.numpy as jnp
from jax import lax
from jax.experimental import pallas as pl
from jax.experimental.pallas import tpu as pltpu
from jax.sharding import PartitionSpec as P

D = 2048
NOPE = 128
ROPE = 64
VD = 128
KVR = 512
TOP = 6


EPSILON = 1e-06


def rms_scale(values):
    return lax.rsqrt(jnp.mean(values * values, axis=-1, keepdims=True) + EPSILON)


def rms_back(grad_unit, unit_rows, row_scale):
    return row_scale * (
        grad_unit - unit_rows * jnp.mean(grad_unit * unit_rows, axis=-1, keepdims=True)
    )


def rotary_tables(segment_row, width):
    count = segment_row.shape[0]
    position = jnp.arange(count, dtype=jnp.int32)
    same = segment_row[:, None] == segment_row[None, :]
    start = jnp.min(jnp.where(same, position[None, :], count), axis=1)
    offset = (position - start).astype(jnp.float32)
    freq = jnp.exp(jnp.arange(width // 2, dtype=jnp.float32) * (-2.0 * math.log(10000.0) / width))
    angle = offset[:, None] * freq[None, :]
    return (jnp.cos(angle), jnp.sin(angle))


def rotate(values, cosine, sine):
    half = values.shape[-1] // 2
    first = values[..., :half]
    second = values[..., half:]
    return jnp.concatenate(
        [first * cosine - second * sine, second * cosine + first * sine], axis=-1
    )


def rotate_back(grads, cosine, sine):
    half = grads.shape[-1] // 2
    first = grads[..., :half]
    second = grads[..., half:]
    return jnp.concatenate(
        [first * cosine + second * sine, second * cosine - first * sine], axis=-1
    )


def allowed_pairs(segment_row, count):
    position = jnp.arange(segment_row.shape[0], dtype=jnp.int32)
    live = position < count
    same = segment_row[:, None] == segment_row[None, :]
    causal = position[None, :] <= position[:, None]
    return same & causal & live[:, None] & live[None, :] | (position[:, None] == position[None, :])


def attention_scores(query_rows, key_nope, key_rope, allowed, scale):
    scores = jnp.einsum(
        "ihd,jhd->hij", query_rows[..., :NOPE], key_nope, preferred_element_type=jnp.float32
    )
    scores = scores + jnp.einsum(
        "ihd,jd->hij", query_rows[..., NOPE:], key_rope, preferred_element_type=jnp.float32
    )
    return jnp.where(allowed[None], scores * scale, -1e30)


def swiglu_back(gate, upper, grad_hidden, axis):
    sigmoid = jax.nn.sigmoid(gate)
    grad_gate = grad_hidden * upper * sigmoid * (1.0 + gate * (1.0 - sigmoid))
    grad_upper = grad_hidden * gate * sigmoid
    return jnp.stack([grad_gate, grad_upper], axis=axis)


def slot_layout(routes, experts, capacity):
    tokens = routes.shape[0]
    flat = routes.reshape(-1)
    onehot = (flat[:, None] == jnp.arange(experts, dtype=jnp.int32)[None, :]).astype(jnp.int32)
    rank = jnp.arange(flat.shape[0], dtype=jnp.int32)
    earlier = (rank[None, :] < rank[:, None]).astype(jnp.bfloat16)
    before = jnp.dot(
        earlier, onehot.astype(jnp.bfloat16), preferred_element_type=jnp.float32
    ).astype(jnp.int32)
    slot_index = jnp.sum(before * onehot, axis=1)
    target = flat * capacity + slot_index
    token_ids = jnp.arange(flat.shape[0], dtype=jnp.int32) // routes.shape[1]
    owner = jnp.full((experts * capacity,), tokens, jnp.int32).at[target].set(token_ids)
    return (slot_index, target, owner)


def to_expert_major(arrived, groups, local_experts):
    capacity = arrived.shape[1]
    width = arrived.shape[2]
    return (
        arrived.reshape(groups, local_experts, capacity, width)
        .transpose(1, 0, 2, 3)
        .reshape(local_experts, groups * capacity, width)
    )


def from_expert_major(results, groups):
    local_experts = results.shape[0]
    width = results.shape[2]
    capacity = results.shape[1] // groups
    return (
        results.reshape(local_experts, groups, capacity, width)
        .transpose(1, 0, 2, 3)
        .reshape(groups * local_experts, capacity, width)
    )


def exchange_body(
    block_input,
    segments,
    counts,
    routes,
    attn_gain,
    w_query,
    w_latent,
    latent_gain,
    w_keyval,
    w_output,
    ffn_gain,
    w_router,
    shared_gate_up,
    shared_down,
    expert_gate_up,
    expert_down,
    cotangent,
):
    gathered = (
        lax.all_gather(attn_gain, "dp", axis=0, tiled=True),
        lax.all_gather(w_query, "dp", axis=0, tiled=True),
        lax.all_gather(w_latent, "dp", axis=0, tiled=True),
        lax.all_gather(latent_gain, "dp", axis=0, tiled=True),
        lax.all_gather(w_keyval, "dp", axis=0, tiled=True),
        lax.all_gather(w_output, "dp", axis=1, tiled=True),
        lax.all_gather(ffn_gain, "dp", axis=0, tiled=True),
        lax.all_gather(w_router, "dp", axis=0, tiled=True),
        lax.all_gather(shared_gate_up, "dp", axis=1, tiled=True),
        lax.all_gather(shared_down, "dp", axis=1, tiled=True),
    )
    (
        full_attn_gain,
        query_weight,
        latent_weight,
        full_latent_gain,
        keyval_weight,
        output_weight,
        full_ffn_gain,
        router_weight,
        shared_in,
        shared_out,
    ) = gathered
    tensor_rank = lax.axis_index("tensor")
    dp_size = lax.axis_size("dp")
    rows_all = lax.all_gather(block_input, "tensor", axis=0, tiled=True)
    tokens = rows_all.shape[0]
    local_rows = block_input.shape[0]
    heads = query_weight.shape[1] // (NOPE + ROPE)
    experts = router_weight.shape[1]
    local_experts = expert_gate_up.shape[0]
    capacity = 2 * tokens * TOP // experts
    scale = (NOPE + ROPE) ** (-0.5)
    start = tensor_rank * local_rows
    cosine, sine = rotary_tables(segments[0], ROPE)
    allowed = allowed_pairs(segments[0], counts[0])
    attn_gain_wide = full_attn_gain.astype(jnp.float32)
    latent_gain_wide = full_latent_gain.astype(jnp.float32)
    ffn_gain_wide = full_ffn_gain.astype(jnp.float32)
    inputs = rows_all.astype(jnp.float32)
    first_scale = rms_scale(inputs)
    first_unit = inputs * first_scale
    first_normed = (first_unit * attn_gain_wide).astype(jnp.bfloat16)
    query = jnp.dot(first_normed, query_weight, preferred_element_type=jnp.float32).reshape(
        tokens, heads, NOPE + ROPE
    )
    query_rows = jnp.concatenate(
        [query[..., :NOPE], rotate(query[..., NOPE:], cosine[:, None, :], sine[:, None, :])],
        axis=-1,
    ).astype(jnp.bfloat16)
    latent_all = jnp.dot(first_normed, latent_weight, preferred_element_type=jnp.float32)
    latent = latent_all[:, :KVR]
    key_rope = rotate(latent_all[:, KVR:], cosine, sine).astype(jnp.bfloat16)
    latent_scale = rms_scale(latent)
    latent_unit = latent * latent_scale
    latent_normed = (latent_unit * latent_gain_wide).astype(jnp.bfloat16)
    keyval = (
        jnp.dot(latent_normed, keyval_weight, preferred_element_type=jnp.float32)
        .astype(jnp.bfloat16)
        .reshape(tokens, heads, NOPE + VD)
    )
    key_nope = keyval[..., :NOPE]
    values = keyval[..., NOPE:]
    scores = attention_scores(query_rows, key_nope, key_rope, allowed, scale)
    row_max = jnp.max(scores, axis=-1, keepdims=True)
    log_total = row_max + jnp.log(jnp.sum(jnp.exp(scores - row_max), axis=-1, keepdims=True))
    weights_low = jnp.exp(scores - log_total).astype(jnp.bfloat16)
    attended = (
        jnp.einsum("hij,jhd->ihd", weights_low, values, preferred_element_type=jnp.float32)
        .astype(jnp.bfloat16)
        .reshape(tokens, heads * VD)
    )
    attn_part = jnp.dot(attended, output_weight, preferred_element_type=jnp.float32)
    mixed = inputs + lax.psum(attn_part, "tensor")
    second_scale = rms_scale(mixed)
    second_unit = mixed * second_scale
    second_normed = (second_unit * ffn_gain_wide).astype(jnp.bfloat16)
    logits = jnp.dot(second_normed, router_weight, preferred_element_type=jnp.float32)
    probabilities = jax.nn.softmax(logits, axis=-1)
    gate_values = jnp.take_along_axis(probabilities, routes, axis=1)
    shared_pre = jnp.einsum(
        "td,gdf->tgf", second_normed, shared_in, preferred_element_type=jnp.float32
    )
    shared_hidden = (jax.nn.silu(shared_pre[:, 0]) * shared_pre[:, 1]).astype(jnp.bfloat16)
    shared_part = jnp.dot(shared_hidden, shared_out, preferred_element_type=jnp.float32)
    slot_index, target, owner = slot_layout(routes, experts, capacity)
    owner_grid = owner.reshape(experts, capacity)
    padded_rows = jnp.concatenate([second_normed, jnp.zeros((1, D), jnp.bfloat16)], axis=0)
    outgoing = padded_rows[owner_grid]
    arrived = lax.all_to_all(outgoing, "dp", split_axis=0, concat_axis=0, tiled=True)
    expert_rows = to_expert_major(arrived, dp_size, local_experts)
    expert_pre = jnp.einsum(
        "erd,egdf->ergf", expert_rows, expert_gate_up, preferred_element_type=jnp.float32
    )
    expert_hidden = (jax.nn.silu(expert_pre[:, :, 0]) * expert_pre[:, :, 1]).astype(jnp.bfloat16)
    expert_result = jnp.einsum(
        "erf,efd->erd", expert_hidden, expert_down, preferred_element_type=jnp.float32
    )
    returning = from_expert_major(expert_result, dp_size)
    returned = lax.all_to_all(
        returning.astype(jnp.bfloat16), "dp", split_axis=0, concat_axis=0, tiled=True
    ).astype(returning.dtype)
    padded_back = jnp.concatenate([returned.reshape(-1, D), jnp.zeros((1, D), jnp.float32)], axis=0)
    picked = padded_back[target].reshape(tokens, TOP, D)
    routed_part = jnp.sum(gate_values[:, :, None] * picked, axis=1)
    branch_sum = lax.psum_scatter(
        (shared_part + routed_part).astype(jnp.bfloat16), "tensor", scatter_dimension=0, tiled=True
    ).astype(jnp.float32)
    block_output = lax.dynamic_slice_in_dim(mixed, start, local_rows, 0) + branch_sum
    grad_rows = lax.all_gather(cotangent, "tensor", axis=0, tiled=True)
    grad_out = grad_rows.astype(jnp.float32)
    grad_shared_hidden = jnp.dot(grad_rows, shared_out.T, preferred_element_type=jnp.float32)
    grad_shared_out = jnp.dot(shared_hidden.T, grad_rows, preferred_element_type=jnp.float32)
    grad_shared_pre = swiglu_back(shared_pre[:, 0], shared_pre[:, 1], grad_shared_hidden, 1).astype(
        jnp.bfloat16
    )
    grad_shared_in = jnp.einsum(
        "td,tgf->gdf", second_normed, grad_shared_pre, preferred_element_type=jnp.float32
    )
    grad_second = jnp.einsum(
        "tgf,gdf->td", grad_shared_pre, shared_in, preferred_element_type=jnp.float32
    )
    gate_by_slot = (
        jnp.zeros((experts * capacity + 1,), jnp.float32).at[target].set(gate_values.reshape(-1))
    )
    slot_ids = jnp.arange(experts * capacity, dtype=jnp.int32).reshape(experts, capacity)
    padded_grad = jnp.concatenate([grad_out, jnp.zeros((1, D), jnp.float32)], axis=0)
    grad_outgoing = (gate_by_slot[slot_ids][..., None] * padded_grad[owner_grid]).astype(
        jnp.bfloat16
    )
    grad_arrived = lax.all_to_all(grad_outgoing, "dp", split_axis=0, concat_axis=0, tiled=True)
    grad_expert_rows = to_expert_major(grad_arrived, dp_size, local_experts)
    grad_expert_hidden = jnp.einsum(
        "erd,efd->erf", grad_expert_rows, expert_down, preferred_element_type=jnp.float32
    )
    grad_expert_down = jnp.einsum(
        "erf,erd->efd", expert_hidden, grad_expert_rows, preferred_element_type=jnp.float32
    )
    grad_expert_pre = swiglu_back(
        expert_pre[:, :, 0], expert_pre[:, :, 1], grad_expert_hidden, 2
    ).astype(jnp.bfloat16)
    grad_expert_gate_up = jnp.einsum(
        "erd,ergf->egdf", expert_rows, grad_expert_pre, preferred_element_type=jnp.float32
    )
    grad_expert_input = jnp.einsum(
        "ergf,egdf->erd", grad_expert_pre, expert_gate_up, preferred_element_type=jnp.float32
    )
    grad_returning = from_expert_major(grad_expert_input, dp_size)
    grad_returned = lax.all_to_all(
        grad_returning.astype(jnp.bfloat16), "dp", split_axis=0, concat_axis=0, tiled=True
    ).astype(grad_returning.dtype)
    padded_grad_back = jnp.concatenate(
        [grad_returned.reshape(-1, D), jnp.zeros((1, D), jnp.float32)], axis=0
    )
    grad_second = grad_second + jnp.sum(padded_grad_back[target].reshape(tokens, TOP, D), axis=1)
    grad_gates = jnp.sum(grad_out[:, None, :] * picked, axis=-1)
    grad_second, grad_gates = (
        lax.psum(grad_second.astype(jnp.bfloat16), "tensor").astype(jnp.float32),
        lax.psum(grad_gates.astype(jnp.bfloat16), "tensor").astype(jnp.float32),
    )
    chosen = (routes[:, :, None] == jnp.arange(experts, dtype=jnp.int32)[None, None, :]).astype(
        jnp.float32
    )
    grad_probabilities = jnp.sum(chosen * grad_gates[:, :, None], axis=1)
    grad_logits = probabilities * (
        grad_probabilities - jnp.sum(probabilities * grad_probabilities, axis=-1, keepdims=True)
    )
    grad_logits_low = grad_logits.astype(jnp.bfloat16)
    grad_router = jnp.dot(second_normed.T, grad_logits_low, preferred_element_type=jnp.float32)
    grad_second = grad_second + jnp.dot(
        grad_logits_low, router_weight.T, preferred_element_type=jnp.float32
    )
    gain_ffn_grad = jnp.sum(grad_second * second_unit, axis=0)
    grad_mixed = grad_out + rms_back(grad_second * ffn_gain_wide, second_unit, second_scale)
    grad_attn_low = grad_mixed.astype(jnp.bfloat16)
    grad_output_weight = jnp.dot(attended.T, grad_attn_low, preferred_element_type=jnp.float32)
    grad_attended = (
        jnp.dot(grad_attn_low, output_weight.T, preferred_element_type=jnp.float32)
        .astype(jnp.bfloat16)
        .reshape(tokens, heads, VD)
    )
    scores = attention_scores(query_rows, key_nope, key_rope, allowed, scale)
    weights = jnp.exp(scores - log_total)
    weights_low = weights.astype(jnp.bfloat16)
    grad_weights = jnp.einsum(
        "ihd,jhd->hij", grad_attended, values, preferred_element_type=jnp.float32
    )
    grad_values = jnp.einsum(
        "hij,ihd->jhd", weights_low, grad_attended, preferred_element_type=jnp.float32
    )
    grad_scores = (
        weights * (grad_weights - jnp.sum(weights * grad_weights, axis=-1, keepdims=True))
    ).astype(jnp.bfloat16)
    grad_query_nope = (
        jnp.einsum("hij,jhd->ihd", grad_scores, key_nope, preferred_element_type=jnp.float32)
        * scale
    )
    grad_query_rope = (
        jnp.einsum("hij,jd->ihd", grad_scores, key_rope, preferred_element_type=jnp.float32) * scale
    )
    grad_key_nope = (
        jnp.einsum(
            "hij,ihd->jhd", grad_scores, query_rows[..., :NOPE], preferred_element_type=jnp.float32
        )
        * scale
    )
    grad_key_rope = (
        jnp.einsum(
            "hij,ihd->jd", grad_scores, query_rows[..., NOPE:], preferred_element_type=jnp.float32
        )
        * scale
    )
    grad_query = (
        jnp.concatenate(
            [grad_query_nope, rotate_back(grad_query_rope, cosine[:, None, :], sine[:, None, :])],
            axis=-1,
        )
        .astype(jnp.bfloat16)
        .reshape(tokens, heads * (NOPE + ROPE))
    )
    grad_query_weight = jnp.dot(first_normed.T, grad_query, preferred_element_type=jnp.float32)
    grad_first = jnp.dot(grad_query, query_weight.T, preferred_element_type=jnp.float32)
    grad_keyval = (
        jnp.concatenate([grad_key_nope, grad_values], axis=-1)
        .astype(jnp.bfloat16)
        .reshape(tokens, heads * (NOPE + VD))
    )
    grad_keyval_weight = jnp.dot(latent_normed.T, grad_keyval, preferred_element_type=jnp.float32)
    grad_latent_normed = jnp.dot(grad_keyval, keyval_weight.T, preferred_element_type=jnp.float32)
    gain_latent_part = jnp.sum(grad_latent_normed * latent_unit, axis=0)
    grad_latent = rms_back(grad_latent_normed * latent_gain_wide, latent_unit, latent_scale)
    grad_latent_all = jnp.concatenate(
        [grad_latent, rotate_back(grad_key_rope, cosine, sine)], axis=-1
    )
    grad_first, grad_latent_all, gain_latent_grad = (
        lax.psum(grad_first.astype(jnp.bfloat16), "tensor").astype(jnp.float32),
        lax.psum(grad_latent_all.astype(jnp.bfloat16), "tensor").astype(jnp.float32),
        lax.psum(gain_latent_part.astype(jnp.bfloat16), "tensor").astype(jnp.float32),
    )
    grad_latent_low = grad_latent_all.astype(jnp.bfloat16)
    grad_latent_weight = jnp.dot(
        first_normed.T, grad_latent_low, preferred_element_type=jnp.float32
    )
    grad_first = grad_first + jnp.dot(
        grad_latent_low, latent_weight.T, preferred_element_type=jnp.float32
    )
    gain_attn_grad = jnp.sum(grad_first * first_unit, axis=0)
    grad_inputs = grad_mixed + rms_back(grad_first * attn_gain_wide, first_unit, first_scale)
    grad_local = lax.dynamic_slice_in_dim(grad_inputs, start, local_rows, 0)
    summed = (
        lax.psum_scatter(gain_attn_grad, "dp", scatter_dimension=0, tiled=True),
        lax.psum_scatter(grad_query_weight, "dp", scatter_dimension=0, tiled=True),
        lax.psum_scatter(grad_latent_weight, "dp", scatter_dimension=0, tiled=True),
        lax.psum_scatter(gain_latent_grad, "dp", scatter_dimension=0, tiled=True),
        lax.psum_scatter(grad_keyval_weight, "dp", scatter_dimension=0, tiled=True),
        lax.psum_scatter(grad_output_weight, "dp", scatter_dimension=1, tiled=True),
        lax.psum_scatter(gain_ffn_grad, "dp", scatter_dimension=0, tiled=True),
        lax.psum_scatter(grad_router, "dp", scatter_dimension=0, tiled=True),
        lax.psum_scatter(grad_shared_in, "dp", scatter_dimension=1, tiled=True),
        lax.psum_scatter(grad_shared_out, "dp", scatter_dimension=1, tiled=True),
    )
    return (
        block_output,
        grad_local,
        summed[0],
        summed[1],
        summed[2],
        summed[3],
        summed[4],
        summed[5],
        summed[6],
        summed[7],
        summed[8],
        summed[9],
        grad_expert_gate_up,
        grad_expert_down,
    )


RINGS = 4


def ring_step(values):
    return lax.ppermute(values, "dp", [(i, (i + RINGS) % 16) for i in range(16)])


def other_y(values):
    return lax.ppermute(values, "dp", [(i, i ^ 2) for i in range(16)])


def other_core(values):
    return lax.ppermute(values, "dp", [(i, i ^ 1) for i in range(16)])


def other_x(values):
    return lax.ppermute(values, "tensor", [(0, 1), (1, 0)])


def fence_kernel(*refs):
    pass


def after(values, *others):
    anywhere = pl.BlockSpec(memory_space=pl.ANY)
    return pl.pallas_call(
        fence_kernel,
        out_shape=jax.ShapeDtypeStruct(values.shape, values.dtype),
        in_specs=[anywhere] * (1 + len(others)),
        out_specs=anywhere,
        input_output_aliases={0: 0},
    )(values, *others)


def gather_whole(rows, early):
    ring = [rows, ring_step(rows)]
    ring.append(ring_step(ring[1]))
    ring.append(ring_step(after(ring[2], early)))
    over_x = [other_x(part) for part in ring]
    groups = []
    for k in (0, 2):
        held = jnp.concatenate(ring[k : k + 2], axis=0)
        across = jnp.concatenate(over_x[k : k + 2], axis=0)
        beside = other_y(held)
        groups.append((held, beside, across, other_y(across) if k else other_x(beside)))
    return groups, ring, over_x


def gather_rows(rows, corners):
    held = [rows, ring_step(rows)]
    first = (other_y(rows), other_x(rows))
    held.append(ring_step(after(held[1], *first)))
    held.append(ring_step(held[2]))
    groups = []
    for k, current in enumerate((held[0], held[1], jnp.concatenate(held[2:], axis=0))):
        beside, across = (other_y(current), other_x(current)) if k else first
        corner = other_x(beside) if corners[k] == "x" else other_y(across)
        groups.append((current, beside, across, corner))
    return held, groups


def add_low(first, second):
    return (first.astype(jnp.float32) + second.astype(jnp.float32)).astype(jnp.bfloat16)


def turn_corner(plane, direction):
    own, beside, across, corner = plane
    if direction == "x":
        return own, add_low(beside, other_x(corner)), across
    return own, beside, add_low(across, other_y(corner))


def close_plane(turned):
    own, beside, across = turned
    return own, other_y(beside), other_x(across)


def wide_sum(*values):
    total = values[0].astype(jnp.float32)
    for value in values[1:]:
        total = total + value.astype(jnp.float32)
    return total


def ring_sum(parts, low):
    moving = parts[1]
    for distance in (2, 3, 0):
        moving = ring_step(moving.astype(low)).astype(jnp.float32) + parts[distance].astype(
            jnp.float32
        )
    return moving


def ring_shards(shard):
    held = [shard]
    for _ in range(RINGS - 1):
        held.append(ring_step(held[-1]))
    return held


def gather_weight(shard, early):
    held, besides = [shard], []
    for distance in range(RINGS):
        beside = other_y(after(held[1], *early) if distance == 1 else held[distance])
        besides.append(beside)
        if distance < RINGS - 1:
            source = after(held[distance], besides[distance - 1]) if distance else shard
            held.append(ring_step(source))
    chunks = []
    for distance, (current, beside) in enumerate(zip(held, besides)):
        for flip_y, chunk in ((0, current), (1, beside)):
            for flip_core, piece in ((0, chunk), (1, other_core(chunk))):
                chunks.append(((distance, flip_y, flip_core), piece))
    return chunks, held, besides


def place_of(coords, key):
    z, y, core = coords
    distance, flip_y, flip_core = key
    return (
        lax.rem(z + RINGS - distance, RINGS) * 4
        + (1 - y if flip_y else y) * 2
        + (1 - core if flip_core else core)
    )


def weight_keys():
    return [
        (distance, flip_y, flip_core)
        for flip_core in (0, 1)
        for flip_y in (0, 1)
        for distance in range(RINGS)
    ]


def scatter_blocks(grads, low):
    half = grads.shape[0] // 2
    total = grads[:half].astype(jnp.float32) + other_core(grads[half:].astype(low)).astype(
        jnp.float32
    )
    quarter = half // 2
    total = total[:quarter] + other_y(total[quarter:].astype(low)).astype(jnp.float32)
    size = quarter // RINGS
    return ring_sum([total[r * size : (r + 1) * size] for r in range(RINGS)], low)


def pick_blocks(values, order):
    chosen = order[:, None] == jnp.arange(values.shape[0], dtype=jnp.int32)[None, :]
    chosen = chosen.reshape(chosen.shape + (1,) * (values.ndim - 1))
    return jnp.sum(jnp.where(chosen, values[None], 0.0), axis=1)


def wide_dot(left, right):
    return jnp.dot(left, right, preferred_element_type=jnp.float32)


def dot_turned(left, right):
    return lax.dot_general(left, right, (((1,), (1,)), ((), ())), preferred_element_type=jnp.float32)


def dot_rows(left, right):
    return lax.dot_general(left, right, (((0,), (0,)), ((), ())), preferred_element_type=jnp.float32)


TILE = 256


def whole(array):
    return pl.BlockSpec(array.shape, lambda *i: (0,) * array.ndim)


def in_vmem(count):
    return [pl.BlockSpec(memory_space=pltpu.VMEM)] * count


def in_place(count):
    return [pl.BlockSpec(memory_space=pl.ANY)] * count


def head_scores(heads, h, nope_ref, turned_ref, keyval_ref, key_ref, masks):
    span = ROPE // 2 * heads
    column = pl.ds(pl.multiple_of(h * NOPE, NOPE), NOPE)
    key_column = pl.ds(pl.multiple_of(h * (NOPE + VD), NOPE), NOPE)
    scores = dot_turned(nope_ref[:, column], keyval_ref[:, key_column])
    for k in (0, 1):
        part = turned_ref[:, k * span : (k + 1) * span]
        part = jnp.where(masks, part, jnp.zeros_like(part))
        scores += dot_turned(part, key_ref[:, k * span : (k + 1) * span])
    return scores * (NOPE + ROPE) ** (-0.5)


def head_lanes(heads, h):
    span = ROPE // 2 * heads
    lane = lax.broadcasted_iota(jnp.int32, (1, span), 1)
    return (lane >= h * (ROPE // 2)) & (lane < (h + 1) * (ROPE // 2))


def allowed_rows(count, segment_row, segment_column):
    tokens = segment_row.shape[1]
    column = lax.broadcasted_iota(jnp.int32, (tokens, tokens), 0)
    row = lax.broadcasted_iota(jnp.int32, (tokens, tokens), 1)
    live = (column < count) & (row < count) & (row <= column)
    return (segment_row == segment_column) & live | (column == row)


def attend_kernel(
    keys,
    extra,
    heads,
    sizes,
    place_ref,
    segment_row_ref,
    segment_column_ref,
    cosine_ref,
    sine_ref,
    own_ref,
    other_ref,
    *refs,
):
    depth, query_width, used, latent_depth, keyval_part, first_width = sizes
    chunks = refs[: len(keys)]
    (
        own_out,
        sent_out,
        first_ref,
        keyval_weight_ref,
        output_ref,
        normed_ref,
        nope_ref,
        turned_ref,
        latent_ref,
        key_ref,
        keyval_ref,
        total_ref,
        attended_ref,
        gains_ref,
        latent_gain_ref,
        semaphores,
    ) = refs[len(keys) + extra :]
    f32, bf16 = jnp.float32, jnp.bfloat16
    local_rows = own_ref.shape[0]
    tokens = 2 * local_rows
    coords = (place_ref[0], place_ref[1], place_ref[2])
    x = place_ref[3]
    copies = []
    parts = depth // latent_depth
    for key, chunk in zip(keys, chunks):
        block = place_of(coords, key)
        rows = pl.ds(pl.multiple_of(block * depth, depth), depth)
        small_rows = pl.ds(pl.multiple_of(block * latent_depth, latent_depth), latent_depth)
        moves = [(chunk.at[:, pl.ds(0, first_width)], first_ref.at[rows])]
        for k in range(parts):
            moves.append(
                (
                    chunk.at[
                        pl.ds(k * latent_depth, latent_depth), pl.ds(first_width, keyval_part)
                    ],
                    keyval_weight_ref.at[small_rows, pl.ds(k * keyval_part, keyval_part)],
                )
            )
        moves.append(
            (
                chunk.at[:, pl.ds(first_width + keyval_part, heads * VD)],
                output_ref.at[rows],
            )
        )
        for source, target in moves:
            copies.append(pltpu.make_async_copy(source, target, semaphores.at[len(copies)]))
    for copy in copies:
        copy.start()
    for copy in copies:
        copy.wait()

    edge = query_width + KVR
    spread = jnp.transpose(first_ref[:, edge:].astype(f32))[used - edge : used - edge + 8]
    gains_ref[...] = spread
    gain = spread[0:1]
    source = lax.broadcasted_iota(jnp.int32, (D, KVR), 0)
    target = lax.broadcasted_iota(jnp.int32, (D, KVR), 1)
    wanted = target // latent_depth * depth + target % latent_depth
    chosen = jnp.where(source == wanted, 1.0, 0.0).astype(bf16)
    latent_gain = wide_dot(spread.astype(bf16), chosen)[2:3]
    latent_gain_ref[...] = latent_gain
    for ref, start in ((own_ref, x * local_rows), (other_ref, (1 - x) * local_rows)):
        rows = ref[...].astype(f32)
        unit = rows * lax.rsqrt(jnp.mean(rows * rows, axis=1, keepdims=True) + EPSILON)
        normed_ref[pl.ds(pl.multiple_of(start, local_rows), local_rows), :] = (unit * gain).astype(
            bf16
        )
    nope_width = heads * NOPE
    span = heads * (ROPE // 2)
    half = nope_width // 2
    for k in (0, 1):
        nope_ref[:, k * half : (k + 1) * half] = wide_dot(
            normed_ref[...], first_ref[:, k * half : (k + 1) * half]
        ).astype(bf16)
    turning = wide_dot(normed_ref[...], first_ref[:, nope_width : nope_width + 2 * span])
    cosine, sine = cosine_ref[...], sine_ref[...]
    first, second = turning[:, :span], turning[:, span:]
    turned_ref[:, :span] = (first * cosine - second * sine).astype(bf16)
    turned_ref[:, span:] = (second * cosine + first * sine).astype(bf16)
    latent = wide_dot(normed_ref[...], first_ref[:, query_width : query_width + KVR])
    latent_ref[...] = latent
    tail = wide_dot(normed_ref[...], first_ref[:, query_width + KVR :])
    lane = lax.broadcasted_iota(jnp.int32, (1, tail.shape[1]), 1)
    swapped = jnp.where(
        lane < ROPE // 2,
        -pltpu.roll(tail, tail.shape[1] - ROPE // 2, 1),
        pltpu.roll(tail, ROPE // 2, 1),
    )
    width = tail.shape[1]
    turned_key = tail * cosine[:, :width] + swapped * sine[:, :width]
    turned_key = jnp.where(lane < ROPE, turned_key, 0.0).astype(bf16)
    source = lax.broadcasted_iota(jnp.int32, (width, 2 * span), 0)
    target = lax.broadcasted_iota(jnp.int32, (width, 2 * span), 1)
    wanted = target % (ROPE // 2) + jnp.where(target < span, 0, ROPE // 2)
    key_ref[...] = wide_dot(turned_key, (source == wanted).astype(bf16)).astype(bf16)
    unit = latent * lax.rsqrt(jnp.mean(latent * latent, axis=1, keepdims=True) + EPSILON)
    latent_normed = (unit * latent_gain).astype(bf16)
    half = keyval_ref.shape[1] // 4
    for k in range(4):
        keyval_ref[:, k * half : (k + 1) * half] = wide_dot(
            latent_normed, keyval_weight_ref[:, k * half : (k + 1) * half]
        ).astype(bf16)
    allowed = allowed_rows(place_ref[4], segment_row_ref[...], segment_column_ref[...])
    total_lane = lax.broadcasted_iota(jnp.int32, total_ref.shape, 1)
    total_ref[...] = jnp.zeros_like(total_ref)

    def one_head(h, _):
        scores = head_scores(
            heads, h, nope_ref, turned_ref, keyval_ref, key_ref, head_lanes(heads, h)
        )
        scores = jnp.where(allowed, scores, -1e30)
        most = jnp.max(scores, axis=1, keepdims=True)
        total = most + jnp.log(jnp.sum(jnp.exp(scores - most), axis=1, keepdims=True))
        weights = jnp.exp(scores - total).astype(bf16)
        total_ref[...] += jnp.where(total_lane == h, total, 0.0)
        value_column = pl.ds(pl.multiple_of(h * (NOPE + VD) + NOPE, NOPE), VD)
        attended_ref[:, pl.ds(pl.multiple_of(h * VD, VD), VD)] = wide_dot(
            weights, keyval_ref[:, value_column]
        ).astype(bf16)
        return 0

    lax.fori_loop(0, heads, one_head, 0)
    own = pl.ds(pl.multiple_of(x * local_rows, local_rows), local_rows)
    other = pl.ds(pl.multiple_of((1 - x) * local_rows, local_rows), local_rows)
    pieces = 4
    size = output_ref.shape[0] // pieces
    for k in range(pieces):
        columns = slice(k * size, (k + 1) * size)
        own_out[:, columns] = dot_turned(attended_ref[own, :], output_ref[columns, :])
        sent_out[:, columns] = dot_turned(attended_ref[other, :], output_ref[columns, :]).astype(
            bf16
        )


def attend_forward(place, segments, cosine, sine, own, other, chunks, heads, sizes, others):
    depth, query_width, used, latent_depth, keyval_part, first_width = sizes
    f32, bf16 = jnp.float32, jnp.bfloat16
    keys = [key for key, _ in chunks]
    local_rows = own.shape[0]
    tokens = 2 * local_rows
    span = heads * (ROPE // 2)
    shapes = [
        ((local_rows, D), f32),
        ((local_rows, D), bf16),
        ((D, first_width), bf16),
        ((KVR, heads * (NOPE + VD)), bf16),
        ((D, heads * VD), bf16),
        ((tokens, D), bf16),
        ((tokens, heads * NOPE), bf16),
        ((tokens, 2 * span), bf16),
        ((tokens, KVR), f32),
        ((tokens, 2 * span), bf16),
        ((tokens, heads * (NOPE + VD)), bf16),
        ((tokens, 128), f32),
        ((tokens, heads * VD), bf16),
        ((8, D), f32),
        ((1, KVR), f32),
    ]
    return pl.pallas_call(
        functools.partial(attend_kernel, keys, len(others), heads, sizes),
        out_shape=[jax.ShapeDtypeStruct(*shape) for shape in shapes],
        in_specs=[pl.BlockSpec(memory_space=pltpu.SMEM)]
        + in_vmem(6)
        + in_place(len(chunks) + len(others)),
        out_specs=in_vmem(len(shapes)),
        scratch_shapes=[
            pltpu.SemaphoreType.DMA((len(chunks) * (2 + depth // latent_depth),))
        ],
        compiler_params=pltpu.CompilerParams(vmem_limit_bytes=48 * 1024 * 1024),
        cost_estimate=pl.CostEstimate(
            flops=2 * tokens * D * (first_width + heads * VD + 1024),
            bytes_accessed=4 * D * (first_width + 1536),
            transcendentals=2 * heads * tokens * tokens,
        ),
    )(
        place,
        segments,
        segments.T,
        cosine,
        sine,
        own,
        other,
        *[piece for _, piece in chunks],
        *others,
    )


def attend_back_kernel(
    heads,
    place_ref,
    segment_row_ref,
    segment_column_ref,
    cosine_ref,
    sine_ref,
    own_ref,
    other_ref,
    keyval_weight_ref,
    output_ref,
    nope_ref,
    turned_ref,
    latent_ref,
    key_ref,
    keyval_ref,
    total_ref,
    latent_gain_ref,
    projected_ref,
    keyval_grad_ref,
    latent_out,
    gain_ref,
    grad_ref,
    turn_ref,
    back_ref,
):
    f32, bf16 = jnp.float32, jnp.bfloat16
    local_rows = own_ref.shape[0]
    x = place_ref[3]
    span = heads * (ROPE // 2)
    nope_width = heads * NOPE
    query_width = nope_width + 2 * span
    scale = (NOPE + ROPE) ** (-0.5)
    for ref, start in ((own_ref, x * local_rows), (other_ref, (1 - x) * local_rows)):
        rows = pl.ds(pl.multiple_of(start, local_rows), local_rows)
        for k in (0, 1):
            half = slice(k * nope_width // 2, (k + 1) * nope_width // 2)
            grad_ref[rows, half] = wide_dot(ref[...], output_ref[:, half]).astype(bf16)
    allowed = allowed_rows(place_ref[4], segment_row_ref[...], segment_column_ref[...])
    total_lane = lax.broadcasted_iota(jnp.int32, total_ref.shape, 1)
    turn_ref[...] = jnp.zeros_like(turn_ref)
    back_ref[...] = jnp.zeros_like(back_ref)

    def one_head(h, _):
        mask = head_lanes(heads, h)
        scores = head_scores(heads, h, nope_ref, turned_ref, keyval_ref, key_ref, mask)
        total = jnp.sum(jnp.where(total_lane == h, total_ref[...], 0.0), axis=1, keepdims=True)
        weights = jnp.exp(jnp.where(allowed, scores, -1e30) - total)
        weights_low = weights.astype(bf16)
        column = pl.ds(pl.multiple_of(h * NOPE, NOPE), NOPE)
        key_column = pl.ds(pl.multiple_of(h * (NOPE + VD), NOPE), NOPE)
        value_column = pl.ds(pl.multiple_of(h * (NOPE + VD) + NOPE, NOPE), VD)
        grads = grad_ref[:, column]
        grad_weights = dot_turned(grads, keyval_ref[:, value_column])
        keyval_grad_ref[:, value_column] = dot_rows(weights_low, grads).astype(bf16)
        grad_scores = (
            weights * (grad_weights - jnp.sum(weights * grad_weights, axis=1, keepdims=True))
        ).astype(bf16)
        projected_ref[:, column] = (
            scale * wide_dot(grad_scores, keyval_ref[:, key_column])
        ).astype(bf16)
        keyval_grad_ref[:, key_column] = (
            scale * dot_rows(grad_scores, nope_ref[:, column])
        ).astype(bf16)
        for k in (0, 1):
            part = slice(k * span, (k + 1) * span)
            turn = wide_dot(grad_scores, key_ref[:, part])
            turn_ref[:, part] += jnp.where(mask, turn, 0.0)
            own = turned_ref[:, part]
            own = jnp.where(mask, own, jnp.zeros_like(own))
            back_ref[:, part] += dot_rows(grad_scores, own)
        return 0

    lax.fori_loop(0, heads, one_head, 0)
    cosine, sine = cosine_ref[...], sine_ref[...]
    first, second = scale * turn_ref[:, :span], scale * turn_ref[:, span:]
    projected_ref[:, nope_width : nope_width + span] = (first * cosine + second * sine).astype(bf16)
    projected_ref[:, nope_width + span : query_width] = (second * cosine - first * sine).astype(
        bf16
    )
    folded = []
    for k in (0, 1):
        part = scale * back_ref[:, k * span : (k + 1) * span]
        shift = span // 2
        while shift >= ROPE // 2:
            part = part + pltpu.roll(part, shift, 1)
            shift //= 2
        folded.append(part)
    width = projected_ref.shape[1] - query_width - KVR
    lane = lax.broadcasted_iota(jnp.int32, (1, width), 1)
    first = (folded[0] * cosine + folded[1] * sine)[:, :width]
    second = (folded[1] * cosine - folded[0] * sine)[:, :width]
    projected_ref[:, query_width + KVR :] = jnp.where(
        lane < ROPE // 2, first, jnp.where(lane < ROPE, second, 0.0)
    ).astype(bf16)
    gain = latent_gain_ref[...]
    latent = latent_ref[...]
    row_scale = lax.rsqrt(jnp.mean(latent * latent, axis=1, keepdims=True) + EPSILON)
    unit = latent * row_scale
    latent_out[...] = (unit * gain).astype(bf16)
    grad_normed = dot_turned(keyval_grad_ref[...], keyval_weight_ref[...])
    gain_ref[...] = jnp.sum(grad_normed * unit, axis=0, keepdims=True)
    grad_unit = grad_normed * gain
    projected_ref[:, query_width : query_width + KVR] = (
        row_scale * (grad_unit - unit * jnp.mean(grad_unit * unit, axis=1, keepdims=True))
    ).astype(bf16)


def attend_back(place, segments, cosine, sine, own, other, saved, heads, first_width, others):
    f32, bf16 = jnp.float32, jnp.bfloat16
    keyval = saved[6]
    tokens = 2 * own.shape[0]
    span = heads * (ROPE // 2)
    return pl.pallas_call(
        lambda *refs: attend_back_kernel(heads, *refs[:16], *refs[16 + len(others) :]),
        out_shape=[
            jax.ShapeDtypeStruct((tokens, first_width), bf16),
            jax.ShapeDtypeStruct((tokens, keyval.shape[1]), bf16),
            jax.ShapeDtypeStruct((tokens, KVR), bf16),
            jax.ShapeDtypeStruct((1, KVR), f32),
        ],
        in_specs=[pl.BlockSpec(memory_space=pltpu.SMEM)] + in_vmem(15) + in_place(len(others)),
        out_specs=in_vmem(4),
        scratch_shapes=[
            pltpu.VMEM((tokens, heads * NOPE), bf16),
            pltpu.VMEM((tokens, 2 * span), f32),
            pltpu.VMEM((tokens, 2 * span), f32),
        ],
        compiler_params=pltpu.CompilerParams(vmem_limit_bytes=48 * 1024 * 1024),
        cost_estimate=pl.CostEstimate(
            flops=2 * tokens * D * 3000,
            bytes_accessed=2 * D * 1536,
            transcendentals=heads * tokens * tokens,
        ),
    )(
        place,
        segments,
        segments.T,
        cosine,
        sine,
        own,
        other,
        *saved,
        *others,
    )


def first_grads_kernel(extra, places_ref, left_ref, right_ref, small_ref, *refs):
    out_ref = refs[-1]
    size = left_ref.shape[1]
    edge = right_ref.shape[1] - small_ref.shape[0]
    result = dot_rows(left_ref[...], right_ref[...])
    for value, some in (
        (result[:, :edge], slice(0, edge)),
        (result[:, edge:] + jnp.transpose(small_ref[...]), slice(edge, right_ref.shape[1])),
    ):
        if extra:
            value = value + refs[0][:, some].astype(jnp.float32)
        out_ref[:, some] = value.astype(jnp.bfloat16)


def other_grads_kernel(first, extra, places_ref, latent_ref, keyval_ref, grad_ref, attended_ref, *refs):
    out_ref, keyval_all = refs[-2:]
    step = pl.program_id(0)
    size = grad_ref.shape[1]
    latent_size = latent_ref.shape[1] // places_ref.shape[0]
    parts = size // latent_size
    columns = keyval_ref.shape[1] // parts

    @pl.when(step == 0)
    def _():
        for k in range(parts):
            some = slice(k * columns, (k + 1) * columns)
            keyval_all[:, some] = dot_rows(latent_ref[...], keyval_ref[:, some])

    start = pl.multiple_of(places_ref[first + step] * latent_size, latent_size)
    strip = keyval_all[pl.ds(start, latent_size), :]
    keyval = jnp.concatenate([strip[:, k * columns : (k + 1) * columns] for k in range(parts)], axis=0)
    output = dot_rows(grad_ref[...], attended_ref[...])
    for value, some in (
        (keyval, slice(0, columns)),
        (output, slice(columns, columns + output.shape[1])),
    ):
        if extra:
            value = value + refs[0][:, some].astype(jnp.float32)
        out_ref[:, some] = value.astype(jnp.bfloat16)


def still(array):
    return pl.BlockSpec(array.shape, lambda i, where: (0, 0))


def grads_call(kernel, specs, operands, scratch, size, width, places, first, count, arrived):
    extra = [] if arrived is None else [arrived]
    return pl.pallas_call(
        functools.partial(kernel, len(extra)),
        grid_spec=pltpu.PrefetchScalarGridSpec(
            num_scalar_prefetch=1,
            grid=(count,),
            in_specs=specs
            + [pl.BlockSpec((size, width), lambda i, where: (first + i, 0))] * len(extra),
            out_specs=pl.BlockSpec((size, width), lambda i, where: (i, 0)),
            scratch_shapes=scratch,
        ),
        out_shape=jax.ShapeDtypeStruct((count * size, width), jnp.bfloat16),
        compiler_params=pltpu.CompilerParams(vmem_limit_bytes=32 * 1024 * 1024),
        cost_estimate=pl.CostEstimate(
            flops=1024 * count * size * width,
            bytes_accessed=4 * count * size * width,
            transcendentals=0,
        ),
    )(places, *operands, *extra)


def first_grads(left, right, small, places, first, count, arrived=None):
    rows, width = right.shape
    size = left.shape[1] // places.shape[0]
    specs = [
        pl.BlockSpec((rows, size), lambda i, where: (0, where[first + i])),
        still(right),
        pl.BlockSpec((small.shape[0], size), lambda i, where: (0, where[first + i])),
    ]
    return grads_call(
        first_grads_kernel, specs, (left, right, small), [], size, width, places, first, count, arrived
    )


def other_grads(latent, keyval, grad, attended, places, first, count, arrived=None):
    rows = grad.shape[0]
    blocks = places.shape[0]
    size = grad.shape[1] // blocks
    parts = size // (latent.shape[1] // blocks)
    width = keyval.shape[1] // parts + attended.shape[1]
    specs = [
        still(latent),
        still(keyval),
        pl.BlockSpec((rows, size), lambda i, where: (0, where[first + i])),
        still(attended),
    ]
    scratch = [pltpu.VMEM((latent.shape[1], keyval.shape[1]), jnp.float32)]
    return grads_call(
        functools.partial(other_grads_kernel, first),
        specs,
        (latent, keyval, grad, attended),
        scratch,
        size,
        width,
        places,
        first,
        count,
        arrived,
    )


def first_back_kernel(place_ref, own_ref, other_ref, grad_ref, weight_ref, own_out, sent_out, gain_ref):
    local_rows = own_ref.shape[0]
    x = place_ref[3]
    size = weight_ref.shape[0] // 4
    for ref, start, out in (
        (own_ref, x * local_rows, own_out),
        (other_ref, (1 - x) * local_rows, sent_out),
    ):
        rows = ref[...].astype(jnp.float32)
        unit = rows * lax.rsqrt(jnp.mean(rows * rows, axis=1, keepdims=True) + EPSILON)
        grads = grad_ref[pl.ds(pl.multiple_of(start, local_rows), local_rows), :]
        for k in range(4):
            some = slice(k * size, (k + 1) * size)
            part = dot_turned(grads, weight_ref[some, :])
            out[:, some] = part.astype(out.dtype)
            gain = jnp.sum(part * unit[:, some], axis=0, keepdims=True)
            if ref is own_ref:
                gain_ref[:, some] = gain
            else:
                gain_ref[:, some] += gain


def first_back(place, own, other, grads, weight):
    f32, bf16 = jnp.float32, jnp.bfloat16
    depth = weight.shape[0]
    return pl.pallas_call(
        first_back_kernel,
        out_shape=[
            jax.ShapeDtypeStruct(own.shape, f32),
            jax.ShapeDtypeStruct(own.shape, bf16),
            jax.ShapeDtypeStruct((1, depth), f32),
        ],
        in_specs=[pl.BlockSpec(memory_space=pltpu.SMEM)] + in_vmem(4),
        out_specs=in_vmem(3),
        compiler_params=pltpu.CompilerParams(vmem_limit_bytes=32 * 1024 * 1024),
        cost_estimate=pl.CostEstimate(
            flops=4 * own.shape[0] * weight.shape[0] * weight.shape[1],
            bytes_accessed=2 * weight.shape[0] * weight.shape[1],
            transcendentals=0,
        ),
    )(place, own, other, grads, weight)


def close_ring(near, arrived):
    size = near.shape[0] // RINGS
    total = near.astype(jnp.float32) + arrived.astype(jnp.float32)
    return ring_sum([total[r * size : (r + 1) * size] for r in range(RINGS)], jnp.bfloat16)


def pack_kernel(heads, query_ref, latent_ref, small_ref, keyval_ref, output_ref, out_ref):
    half = ROPE // 2
    head = NOPE + ROPE
    nope_width = heads * NOPE
    for h in range(heads):
        start = h * head
        out_ref[:, h * NOPE : (h + 1) * NOPE] = query_ref[:, start : start + NOPE]
        for k in (0, 1):
            to = nope_width + k * heads * half + h * half
            out_ref[:, to : to + half] = query_ref[
                :, start + NOPE + k * half : start + NOPE + (k + 1) * half
            ]
    at = heads * head
    edge = at + KVR
    out_ref[:, at:edge] = latent_ref[:, :KVR]
    out_ref[:, edge : edge + 128] = jnp.concatenate([latent_ref[:, KVR:], small_ref[...]], axis=1)
    at = edge + 128
    size = keyval_ref.shape[0]
    parts = out_ref.shape[0] // size
    part = keyval_ref.shape[1] // parts
    for k in range(parts):
        out_ref[k * size : (k + 1) * size, at : at + part] = keyval_ref[
            :, k * part : (k + 1) * part
        ]
    out_ref[:, at + part :] = jnp.transpose(output_ref[...].astype(jnp.float32)).astype(
        jnp.bfloat16
    )


def pack_weights(query, latent, small, keyval, output):
    depth, query_width = query.shape
    heads = query_width // (NOPE + ROPE)
    width = query_width + KVR + 128 + keyval.size // depth + output.shape[0]
    return pl.pallas_call(
        functools.partial(pack_kernel, heads),
        out_shape=jax.ShapeDtypeStruct((depth, width), jnp.bfloat16),
        in_specs=in_vmem(5),
        out_specs=pl.BlockSpec(memory_space=pltpu.VMEM),
    )(query, latent, small, keyval, output)


def load_pieces(pieces, starts, target, semaphores):
    size = target.shape[0] // len(pieces)
    copies = [
        pltpu.make_async_copy(
            piece.at[pl.ds(start, size)], target.at[pl.ds(k * size, size)], semaphores.at[k]
        )
        for k, (piece, start) in enumerate(zip(pieces, starts))
    ]
    for copy in copies:
        copy.start()
    for copy in copies:
        copy.wait()


def shared_stride(shared):
    return -(-shared // 32) * 32


def pack_shared_kernel(blocks, shared, in_ref, down_ref, out_ref):
    stride = shared_stride(shared)
    out_ref[...] = jnp.zeros_like(out_ref)
    for k in range(3):
        if k < 2:
            units = jnp.transpose(in_ref[k].astype(jnp.float32)).astype(jnp.bfloat16)
        else:
            units = down_ref[...]
        for b in range(blocks):
            out_ref[b, k * stride : k * stride + shared] = units[b * shared : (b + 1) * shared]


def pack_shared(shared_in, shared_down, blocks, others):
    depth = shared_in.shape[1]
    shared = shared_down.shape[0] // blocks
    return pl.pallas_call(
        lambda in_ref, down_ref, *refs: pack_shared_kernel(
            blocks, shared, in_ref, down_ref, refs[-1]
        ),
        out_shape=jax.ShapeDtypeStruct((blocks, 3 * shared_stride(shared), depth), jnp.bfloat16),
        in_specs=in_vmem(2) + in_place(len(others)),
        out_specs=pl.BlockSpec(memory_space=pltpu.VMEM),
    )(shared_in, shared_down, *others)


def unpack_shared_kernel(shared, packed_ref, in_ref, down_ref, units_ref):
    stride = shared_stride(shared)
    blocks = packed_ref.shape[0]
    for k in range(3):
        target = down_ref if k == 2 else units_ref
        for b in range(blocks):
            target[b * shared : (b + 1) * shared, :] = packed_ref[
                b, k * stride : k * stride + shared
            ].astype(jnp.float32)
        if k < 2:
            in_ref[k] = jnp.transpose(units_ref[...])


def unpack_shared(packed, shared, others):
    blocks, _, depth = packed.shape
    return pl.pallas_call(
        lambda packed_ref, *refs: unpack_shared_kernel(shared, packed_ref, *refs[len(others) :]),
        out_shape=[
            jax.ShapeDtypeStruct((2, depth, blocks * shared), jnp.float32),
            jax.ShapeDtypeStruct((blocks * shared, depth), jnp.float32),
        ],
        in_specs=in_vmem(1) + in_place(len(others)),
        out_specs=in_vmem(2),
        scratch_shapes=[pltpu.VMEM((blocks * shared, depth), jnp.float32)],
    )(packed, *others)


def pack_units_kernel(units, shared, own_in, other_in, own_down, other_down, near, far, *refs):
    outs = refs[-3:]
    hole = -(-units // TILE) * TILE
    stride = shared_stride(shared)
    columns = outs[0].shape[1]
    size = near.shape[2]
    for k, out in enumerate(outs):
        first = own_in[0, k] if k < 2 else own_down[0]
        second = other_in[0, k] if k < 2 else other_down[0]
        out[:units] = first
        out[units:hole] = jnp.zeros((hole - units, columns), jnp.bfloat16)
        out[hole : hole + units] = second
        out[hole + units : 2 * hole] = jnp.zeros((hole - units, columns), jnp.bfloat16)
        out[2 * hole :] = jnp.zeros((TILE, columns), jnp.bfloat16)
        for b in range(columns // size):
            part = slice(b * size, (b + 1) * size)
            for at, ref in ((2 * hole, near), (2 * hole + stride, far)):
                out[at : at + shared, part] = ref[b, k * stride : k * stride + shared]


def pack_units(own_in, other_in, own_down, other_down, near, far, shared, others):
    units, depth = own_down.shape[1:]
    size = near.shape[2]
    height = 2 * (-(-units // TILE) * TILE) + TILE
    columns = 2 * size
    in_spec = pl.BlockSpec((1, 2, units, columns), lambda i: (0, 0, 0, i))
    down_spec = pl.BlockSpec((1, units, columns), lambda i: (0, 0, i))
    narrow = pl.BlockSpec((2,) + near.shape[1:], lambda i: (i, 0, 0))
    return pl.pallas_call(
        functools.partial(pack_units_kernel, units, shared),
        grid=(depth // columns,),
        in_specs=[in_spec, in_spec, down_spec, down_spec, narrow, narrow]
        + in_place(len(others)),
        out_specs=[pl.BlockSpec((height, columns), lambda i: (0, i))] * 3,
        out_shape=[jax.ShapeDtypeStruct((height, depth), jnp.bfloat16)] * 3,
        compiler_params=pltpu.CompilerParams(vmem_limit_bytes=32 * 1024 * 1024),
        cost_estimate=pl.CostEstimate(
            flops=0, bytes_accessed=12 * height * depth, transcendentals=0
        ),
    )(own_in, other_in, own_down, other_down, near, far, *others)


def expert_grads_kernel(units, count, extra, right_ref, *refs):
    out = refs[-1]
    for k in range(count):

        @pl.when(pl.program_id(0) == k)
        def _():
            result = dot_rows(refs[k][...], right_ref[...])[:units]
            if extra:
                result += refs[count][0, 0].astype(jnp.float32)
            out[0, 0] = result.astype(out.dtype)


def expert_grads(lefts, right, units, column, arrived, kind, others=()):
    total, depth = right.shape
    wide = -(-units // TILE) * TILE
    extra = [] if arrived is None else [arrived]
    out = pl.BlockSpec((1, 1, units, 2 * TILE), lambda k, i: (0, k, 0, i))
    side = pl.BlockSpec((total, wide), lambda k, i: (0, column))
    return pl.pallas_call(
        functools.partial(expert_grads_kernel, units, len(lefts), len(extra)),
        grid=(len(lefts), depth // (2 * TILE)),
        in_specs=[pl.BlockSpec((total, 2 * TILE), lambda k, i: (0, i))]
        + [side] * len(lefts)
        + [out] * len(extra)
        + in_place(len(others)),
        out_specs=out,
        out_shape=jax.ShapeDtypeStruct((1, len(lefts), units, depth), kind),
        compiler_params=pltpu.CompilerParams(vmem_limit_bytes=48 * 1024 * 1024),
        cost_estimate=pl.CostEstimate(
            flops=2 * len(lefts) * total * depth * wide,
            bytes_accessed=2 * len(lefts) * total * (depth + wide) + 8 * depth * units,
            transcendentals=0,
        ),
    )(right, *lefts, *extra, *others)


def side_grads_kernel(shared, rows_ref, cots_ref, gate_ref, up_ref, hidden_ref, logit_ref, *outs):
    kept_ref, sent_ref, router_ref = outs
    stride = shared_stride(shared)
    size = kept_ref.shape[2]
    for k, (left, right) in enumerate(
        ((gate_ref, rows_ref), (up_ref, rows_ref), (hidden_ref, cots_ref))
    ):
        result = dot_rows(left[...], right[...])
        for b in range(kept_ref.shape[0]):
            part = slice(b * size, (b + 1) * size)
            kept_ref[b, k * stride : (k + 1) * stride] = result[:stride, part]
            sent_ref[b, k * stride : (k + 1) * stride] = result[
                stride : 2 * stride, part
            ].astype(jnp.bfloat16)
    router_ref[...] = dot_rows(logit_ref[...], rows_ref[...])


def side_grads(rows, cots, gate, up, hidden, logits, shared, blocks):
    total, depth = rows.shape
    column = gate.shape[1] // TILE - 1
    size = depth // blocks
    stride = shared_stride(shared)
    wide = pl.BlockSpec((total, 2 * TILE), lambda i: (0, i))
    side = pl.BlockSpec((total, TILE), lambda i: (0, column))
    packed = pl.BlockSpec((2 * TILE // size, 3 * stride, size), lambda i: (i, 0, 0))
    return pl.pallas_call(
        functools.partial(side_grads_kernel, shared),
        grid=(depth // (2 * TILE),),
        in_specs=[wide, wide, side, side, side, whole(logits)],
        out_specs=[packed, packed, pl.BlockSpec((logits.shape[1], 2 * TILE), lambda i: (0, i))],
        out_shape=[
            jax.ShapeDtypeStruct((blocks, 3 * stride, size), jnp.float32),
            jax.ShapeDtypeStruct((blocks, 3 * stride, size), jnp.bfloat16),
            jax.ShapeDtypeStruct((logits.shape[1], depth), jnp.float32),
        ],
        compiler_params=pltpu.CompilerParams(vmem_limit_bytes=48 * 1024 * 1024),
        cost_estimate=pl.CostEstimate(
            flops=8 * total * depth * TILE,
            bytes_accessed=4 * total * depth,
            transcendentals=0,
        ),
    )(rows, cots, gate, up, hidden, logits)


def down_kernel(starts, *refs):
    count = len(starts)
    pieces, weight_ref = refs[:count], refs[count]
    grads_ref, rows_ref, semaphores = refs[-3:]

    @pl.when(pl.program_id(0) == 0)
    def _():
        load_pieces(pieces, starts, rows_ref, semaphores)

    size = rows_ref.shape[0] // 2
    for k in range(2):
        part = slice(k * size, (k + 1) * size)
        grads_ref[part, :] = dot_turned(rows_ref[part, :], weight_ref[...]).astype(jnp.bfloat16)


def down_grads(part, pieces, size, down, kept, others):
    count = len(pieces)
    depth = down.shape[1]
    width = down.shape[0]
    rows = count * size
    return pl.pallas_call(
        functools.partial(down_kernel, tuple(start for _, start in pieces)),
        grid=(width // TILE,),
        in_specs=in_place(count)
        + [pl.BlockSpec((TILE, depth), lambda i: (i, 0))]
        + in_place(len(kept) + len(others)),
        out_specs=[
            pl.BlockSpec((rows, TILE), lambda i: (part, i)),
            pl.BlockSpec((rows, depth), lambda i: (part, 0)),
        ],
        out_shape=[
            jax.ShapeDtypeStruct((2 * rows, width), jnp.bfloat16),
            jax.ShapeDtypeStruct((2 * rows, depth), jnp.bfloat16),
        ],
        scratch_shapes=[pltpu.SemaphoreType.DMA((count,))],
        input_output_aliases={count + 1 + k: k for k in range(len(kept))},
        compiler_params=pltpu.CompilerParams(vmem_limit_bytes=48 * 1024 * 1024),
        cost_estimate=pl.CostEstimate(
            flops=2 * rows * depth * width,
            bytes_accessed=2 * (2 * rows * depth + depth * width + rows * width),
            transcendentals=0,
        ),
    )(*[array for array, _ in pieces], down, *kept, *others)


def out_kernel(pieces, *refs):
    hidden_ref, weight_ref = refs[:2]
    outs = refs[2 : 2 + pieces]
    size = hidden_ref.shape[0] // (RINGS * pieces)
    for r in range(RINGS):
        part = hidden_ref[r * pieces * size : (r + 1) * pieces * size, :]
        result = wide_dot(part, weight_ref[...]).astype(jnp.bfloat16)
        for k in range(pieces):
            outs[k][r * size : (r + 1) * size, :] = result[k * size : (k + 1) * size]


def out_rows(pieces, hidden, down):
    rows, width = hidden.shape
    depth = down.shape[1]
    return pl.pallas_call(
        functools.partial(out_kernel, pieces),
        grid=(depth // TILE,),
        in_specs=[whole(hidden), pl.BlockSpec((width, TILE), lambda i: (0, i))],
        out_specs=[pl.BlockSpec((rows // pieces, TILE), lambda i: (0, i))] * pieces,
        out_shape=[jax.ShapeDtypeStruct((rows // pieces, depth), jnp.bfloat16)] * pieces,
        compiler_params=pltpu.CompilerParams(vmem_limit_bytes=48 * 1024 * 1024),
        cost_estimate=pl.CostEstimate(
            flops=2 * rows * depth * width,
            bytes_accessed=2 * (rows * depth + depth * width + rows * width),
            transcendentals=0,
        ),
    )(hidden, down)


def mlp_kernel(tiles, starts, others, experts_ref, routed_ref, *refs):
    pieces = len(starts)
    row_refs = refs[:pieces]
    router_ref, gate_col, up_col, down_grad, gate_row, up_row = refs[pieces : pieces + 6]
    outs = refs[pieces + 6 + others :]
    grad_refs = outs[:pieces]
    rows_out, hidden_out, gate_out, up_out, logit_out = outs[pieces : pieces + 5]
    gate_all, up_all, prob_ref, scale_ref, sum_ref, semaphores = outs[pieces + 5 :]
    step = pl.program_id(0)
    third = tiles // 2
    total = rows_out.shape[0]
    size = total // pieces
    lane = lax.broadcasted_iota(jnp.int32, (1, router_ref.shape[1]), 1) - experts_ref[3]

    @pl.when(step == 0)
    def _():
        load_pieces(row_refs, starts, rows_out, semaphores)
        logits = wide_dot(rows_out[...], router_ref[...])
        logits = jnp.where((lane >= 0) & (lane < experts_ref[2]), logits, -1e30)
        raised = jnp.exp(logits - jnp.max(logits, axis=1, keepdims=True))
        chances = raised / jnp.sum(raised, axis=1, keepdims=True)
        prob_ref[...] = chances
        for k in (0, 1):
            chance = jnp.sum(jnp.where(lane == experts_ref[k], chances, 0.0), axis=1, keepdims=True)
            scale_ref[k] = routed_ref[:, k : k + 1] * chance
        scale_ref[2] = jnp.ones_like(scale_ref[2])
        sum_ref[...] = jnp.zeros_like(sum_ref)

    @pl.when(step < tiles)
    def _():
        columns = pl.ds(pl.multiple_of(step * TILE, TILE), TILE)
        kind = step // third
        half = total // 2
        for k in (0, 1):
            part = slice(k * half, (k + 1) * half)
            pre_gate = dot_turned(rows_out[part, :], gate_col[...])
            pre_up = dot_turned(rows_out[part, :], up_col[...])
            grads = down_grad[part, :].astype(jnp.float32)
            scale = scale_ref[kind, part, :]
            sigmoid = 1.0 / (1.0 + jnp.exp(-pre_gate))
            silu = pre_gate * sigmoid
            hidden = (silu * pre_up).astype(jnp.bfloat16).astype(jnp.float32)
            sum_ref[kind, part, :] += jnp.sum(hidden * grads, axis=1, keepdims=True)
            grad_hidden = scale * grads
            low_gate = (grad_hidden * pre_up * (sigmoid + silu * (1.0 - sigmoid))).astype(
                jnp.bfloat16
            )
            low_up = (grad_hidden * silu).astype(jnp.bfloat16)
            gate_all[part, columns] = low_gate
            up_all[part, columns] = low_up
            hidden_out[part, :] = (scale * hidden).astype(jnp.bfloat16)
            gate_out[part, :] = low_gate
            up_out[part, :] = low_up

    @pl.when(step == tiles - 1)
    def _():
        grad_logits = jnp.zeros_like(prob_ref)
        for k in (0, 1):
            own = jnp.where(lane == experts_ref[k], 1.0, 0.0)
            grad_logits += scale_ref[k] * sum_ref[k] * (own - prob_ref[...])
        logit_out[...] = grad_logits.astype(jnp.bfloat16)

    @pl.when(step >= tiles)
    def _():
        some = pl.ds(pl.multiple_of((step - tiles) * 2 * TILE, TILE), 2 * TILE)
        grads = wide_dot(gate_all[...], gate_row[...]) + wide_dot(up_all[...], up_row[...])
        grads += dot_turned(logit_out[...], router_ref[some, :])
        grads = grads.astype(jnp.bfloat16)
        for k in range(pieces):
            grad_refs[k][...] = grads[k * size : (k + 1) * size]


def mlp_plane(distance, experts, routed, rows, down_grad, router, weights, kept, others):
    gate, up = weights
    pieces = len(rows)
    width, depth = gate.shape
    size = routed.shape[0] // pieces
    tiles, columns = width // TILE, depth // (2 * TILE)
    total = pieces * size
    low = jnp.bfloat16

    def early(i):
        return jnp.minimum(i, tiles - 1)

    def late(i):
        return jnp.maximum(i - tiles, 0)

    tile_spec = pl.BlockSpec((total, TILE), lambda i: (distance, early(i)))
    anywhere = pl.BlockSpec(memory_space=pl.ANY)
    first_kept = 2 + pieces + 6
    results = pl.pallas_call(
        functools.partial(
            mlp_kernel, tiles, tuple(start for _, start in rows), len(kept) + len(others)
        ),
        grid=(tiles + columns,),
        in_specs=[pl.BlockSpec(memory_space=pltpu.SMEM), whole(routed)]
        + [anywhere] * pieces
        + [
            pl.BlockSpec((depth, 128), lambda i: (0, router.shape[1] // 128 - 1)),
            pl.BlockSpec((TILE, depth), lambda i: (early(i), 0)),
            pl.BlockSpec((TILE, depth), lambda i: (early(i), 0)),
            tile_spec,
            pl.BlockSpec((width, 2 * TILE), lambda i: (0, late(i))),
            pl.BlockSpec((width, 2 * TILE), lambda i: (0, late(i))),
        ]
        + [anywhere] * (len(kept) + len(others)),
        out_specs=[pl.BlockSpec((size, 2 * TILE), lambda i: (0, late(i)))] * pieces
        + [
            pl.BlockSpec((total, depth), lambda i: (distance, 0)),
            tile_spec,
            tile_spec,
            tile_spec,
            pl.BlockSpec((total, 128), lambda i: (distance, 0)),
        ],
        out_shape=[jax.ShapeDtypeStruct((size, depth), low)] * pieces
        + [
            jax.ShapeDtypeStruct((RINGS * total, many), low)
            for many in (depth, width, width, width, 128)
        ],
        scratch_shapes=[pltpu.VMEM((total, width), low)] * 2
        + [
            pltpu.VMEM((total, 128), jnp.float32),
            pltpu.VMEM((3, total, 1), jnp.float32),
            pltpu.VMEM((3, total, 1), jnp.float32),
            pltpu.SemaphoreType.DMA((pieces,)),
        ],
        input_output_aliases={first_kept + k: pieces + k for k in range(len(kept))},
        compiler_params=pltpu.CompilerParams(vmem_limit_bytes=48 * 1024 * 1024),
        cost_estimate=pl.CostEstimate(
            flops=2 * total * depth * width * 4,
            bytes_accessed=2 * (4 * depth * width + 3 * total * depth + 4 * total * width),
            transcendentals=total * width,
        ),
    )(experts, routed, *[array for array, _ in rows], router, gate, up, down_grad, gate, up, *kept, *others)
    return results[:pieces], results[pieces:]


def gather_body(
    block_input,
    segments,
    counts,
    routes,
    attn_gain,
    w_query,
    w_latent,
    latent_gain,
    w_keyval,
    w_output,
    ffn_gain,
    w_router,
    shared_gate_up,
    shared_down,
    expert_gate_up,
    expert_down,
    cotangent,
):
    f32 = jnp.float32
    bf16 = jnp.bfloat16
    blocks = 16
    index = lax.axis_index("dp")
    x = lax.axis_index("tensor")
    coords = jnp.stack([index // 4, (index // 2) % 2, index % 2]).astype(jnp.int32)
    core = coords[2]
    place = jnp.concatenate([coords, x.astype(jnp.int32)[None], counts])
    local_rows = block_input.shape[0]
    tokens = 2 * local_rows
    depth = w_query.shape[0]
    query_width = w_query.shape[1]
    heads = query_width // (NOPE + ROPE)
    experts = w_router.shape[1]
    units = expert_gate_up.shape[3]
    shared = shared_gate_up.shape[2] // blocks
    latent_depth = w_keyval.shape[0]

    used = query_width + KVR + ROPE
    small = jnp.concatenate(
        [
            attn_gain[:, None],
            ffn_gain[:, None],
            jnp.pad(latent_gain, (0, depth - latent_depth))[:, None],
            w_router,
            routes.reshape(depth, -1).astype(bf16),
            jnp.zeros((depth, 128 - ROPE - 3 - experts - 2 * TOP), bf16),
        ],
        axis=1,
    )
    first_width = query_width + KVR + 128
    shards = pack_weights(w_query, w_latent, small, w_keyval, w_output)
    other_input = other_x(block_input)
    expert_in = expert_gate_up.swapaxes(2, 3)
    expert_in_other = other_core(expert_in)
    expert_down_other = other_core(expert_down)
    chunks, held, besides = gather_weight(
        shards, (expert_in_other, expert_down_other, other_input)
    )
    shared_near = lax.all_to_all(
        pack_shared(shared_gate_up, shared_down, blocks, (held[3],)),
        "dp",
        split_axis=0,
        concat_axis=0,
        tiled=True,
    )
    shared_far = other_core(shared_near)

    grad_groups, grad_ring, grad_across = gather_whole(
        after(cotangent, held[3], besides[2]), besides[3]
    )

    cosine, sine = rotary_tables(segments[0], ROPE)
    cosine = jnp.tile(cosine, (1, heads))
    sine = jnp.tile(sine, (1, heads))
    sizes = (depth, query_width, used, latent_depth, w_keyval.shape[1] * latent_depth // depth, first_width)
    (
        own_part,
        sent_part,
        first_weight,
        keyval_weight,
        output_turned,
        first_normed,
        nope,
        turned_query,
        latent,
        key,
        keyval,
        total,
        attended,
        gains,
        latent_gain_row,
    ) = attend_forward(
        place,
        segments,
        cosine,
        sine,
        block_input,
        other_input,
        chunks,
        heads,
        sizes,
        (grad_ring[3], grad_across[1], grad_across[2], grad_groups[0][1]),
    )
    attn_gain_wide, ffn_gain_wide = gains[0], gains[1]
    mixed = block_input.astype(f32) + own_part + other_x(sent_part).astype(f32)
    second_scale = rms_scale(mixed)
    second_unit = mixed * second_scale
    second_normed = (second_unit * ffn_gain_wide).astype(bf16)

    routes_at = used + 3 + experts
    routes_all = first_weight[:, routes_at : routes_at + 2 * TOP].reshape(blocks * tokens, TOP)
    chip_experts = jnp.stack([index, index + 1 - 2 * core]).astype(jnp.int32)
    routed_all = jnp.any(
        routes_all[None] == chip_experts[:, None, None].astype(bf16), axis=2
    ).astype(f32)
    order = jnp.stack(
        [
            place_of(coords, (distance, flip_y, 0)) * 2 + (1 - x if flip_x else x)
            for distance in range(RINGS)
            for flip_x, flip_y in ((0, 0), (0, 1), (1, 0), (1, 1))
        ]
    )
    routed = jnp.stack(
        [
            pick_blocks(one.reshape(blocks * 2, local_rows), order).reshape(RINGS, -1)
            for one in routed_all
        ],
        axis=2,
    )

    corners = "yxyx"
    row_ring, row_groups = gather_rows(second_normed, "yyx")
    row_planes = [
        [(array, 0) for array in row_groups[0]],
        [(array, 0) for array in row_groups[1]],
        [(array, 0) for array in row_groups[2]],
        [(array, local_rows) for array in row_groups[2]],
    ]

    gate_weight, up_weight, down_weight = pack_units(
        expert_in,
        expert_in_other,
        expert_down,
        expert_down_other,
        shared_near,
        shared_far,
        shared,
        (second_normed,),
    )
    half_kept = down_grads(
        0,
        [(array, r * local_rows) for r in (0, 1) for array in grad_groups[0]],
        local_rows,
        down_weight,
        (),
        (row_ring[1],),
    )
    down_grad, every_grad = down_grads(
        1,
        [(array, r * local_rows) for r in (0, 1) for array in grad_groups[1]],
        local_rows,
        down_weight,
        half_kept,
        (row_ring[2],),
    )
    expert_ids = jnp.concatenate(
        [chip_experts, jnp.array([experts, used + 3 - query_width - KVR], jnp.int32)]
    )
    kept = []
    planes = []
    turned, closed = [None] * RINGS, [None] * RINGS
    for distance in range(RINGS):
        others = [row_ring[3]] if distance == 0 else []
        if distance == 1:
            others = list(row_groups[2][1:3])
        elif distance == 3:
            others = list(turned[0][1:])
        grads, kept = mlp_plane(
            distance,
            expert_ids,
            routed[distance],
            row_planes[distance],
            down_grad,
            first_weight,
            (gate_weight, up_weight),
            kept,
            others,
        )
        planes.append(list(grads))
        if distance:
            before = planes[distance - 1]
            k = 1 if corners[distance - 1] == "x" else 2
            before[k] = after(before[k], grads[3])
            turned[distance - 1] = turn_corner(before, corners[distance - 1])
            closed[distance - 1] = close_plane(turned[distance - 1])
    turned[3] = turn_corner(planes[3], corners[3])
    first_part = closed[1]
    closed[1] = (after(first_part[0], planes[3][3]),) + tuple(first_part[1:])
    every_row, every_hidden, every_gate_grad, every_up_grad, logit_grads = kept
    shared_kept, shared_sent, logit_rows = side_grads(
        every_row,
        every_grad,
        every_gate_grad,
        every_up_grad,
        every_hidden,
        logit_grads,
        shared,
        blocks,
    )
    first_total = wide_sum(*closed[1]).astype(bf16)
    sent_in = expert_grads(
        (every_gate_grad, every_up_grad), every_row, units, 1, None, bf16, (first_total,)
    )
    sent_down = expert_grads((every_hidden,), every_grad, units, 1, None, bf16)
    moving = ring_step(first_total)
    moving = ring_step(wide_sum(moving, *closed[2]).astype(bf16))
    own, beside, across = turned[3]
    own = after(own, sent_down)
    grad_close = close_plane((own, after(beside, shared_sent), across))
    grad_second = wide_sum(
        ring_step(wide_sum(moving, *grad_close).astype(bf16)),
        after(closed[0][0], sent_in),
        *closed[0][1:],
    )
    arrived_in = other_core(sent_in)
    arrived_down = other_core(sent_down)
    router_at = used + 3 - query_width - KVR
    grad_router = logit_rows[router_at : router_at + experts]
    shared_grads = lax.all_to_all(
        add_low(shared_kept, other_core(shared_sent)), "dp", split_axis=0, concat_axis=0, tiled=True
    )

    gain_ffn_part = jnp.sum(grad_second * second_unit, axis=0)
    grad_mixed = cotangent.astype(f32) + rms_back(
        grad_second * ffn_gain_wide, second_unit, second_scale
    )
    grad_mixed_low = grad_mixed.astype(bf16)
    other_grad = other_x(grad_mixed_low)
    outs = list(out_rows(4, every_hidden, down_weight))
    outs[3] = after(outs[3], grad_close[2])
    outs[2] = after(outs[2], other_grad)
    out_own, out_beside, out_across = close_plane(turn_corner(outs, "x"))


    places = jnp.stack([place_of(coords, key_of) for key_of in weight_keys()]).astype(jnp.int32)
    projected_grad, keyval_grad, latent_normed, gain_latent_part = attend_back(
        place,
        segments,
        cosine,
        sine,
        grad_mixed_low,
        other_grad,
        (keyval_weight, output_turned, nope, turned_query, latent, key, keyval, total, latent_gain_row),
        heads,
        first_width,
        (shared_grads, arrived_in, arrived_down),
    )
    grad_attn = jnp.concatenate(
        [
            jnp.where(x == 0, grad_mixed_low, other_grad),
            jnp.where(x == 0, other_grad, grad_mixed_low),
        ],
        axis=0,
    )
    ring_places = places.reshape(2, 2, RINGS).swapaxes(1, 2).reshape(-1)
    other_parts = (latent_normed, keyval_grad, grad_attn, attended, ring_places)
    other_arrived = other_core(other_grads(*other_parts, 8, 8))
    own_first, sent_first, gain_attn_part = first_back(
        place, block_input, other_input, projected_grad, first_weight
    )
    grad_first = own_first + other_x(sent_first).astype(f32)
    small_rows = jnp.concatenate(
        [
            jnp.zeros((ROPE, D), f32),
            gain_attn_part,
            gain_ffn_part[None],
            jnp.pad(
                gain_latent_part.reshape(blocks, latent_depth),
                ((0, 0), (0, depth - latent_depth)),
            ).reshape(1, D),
            grad_router,
            jnp.zeros((128 - ROPE - 3 - experts, D), f32),
        ],
        axis=0,
    )
    first_parts = (first_normed, projected_grad, small_rows, places)
    first_arrived = other_core(first_grads(*first_parts, 8, 8))
    other_kept = other_grads(*other_parts, 0, 8, other_arrived)
    far = first_grads(*first_parts, 4, 4, first_arrived)
    from_y = other_y(far)
    out_total = wide_sum(after(out_own, far), out_beside, out_across)
    block_output = mixed + ring_sum(
        [out_total[r * local_rows : (r + 1) * local_rows] for r in range(RINGS)], bf16
    )
    near = first_grads(*first_parts, 0, 4, first_arrived)
    other_summed = ring_sum(
        [other_kept[2 * r * depth : 2 * (r + 1) * depth] for r in range(RINGS)], bf16
    )
    other_closed = other_summed[:depth] + other_y(other_summed[depth:].astype(bf16)).astype(f32)
    grad_expert_down = expert_grads(
        (every_hidden,), every_grad, units, 0, arrived_down, f32, (from_y,)
    )
    first_closed = close_ring(near, from_y)
    grad_expert_in = expert_grads(
        (every_gate_grad, every_up_grad), every_row, units, 0, arrived_in, f32, (near,)
    )
    grad_shared_in, grad_shared_down = unpack_shared(shared_grads, shared, (from_y,))
    grad_expert_gate_up = grad_expert_in.swapaxes(2, 3)
    grad_expert_down = grad_expert_down[0]
    nope_width = heads * NOPE
    span = heads * (ROPE // 2)
    grad_query_weight = jnp.concatenate(
        [
            first_closed[:, :nope_width].reshape(depth, heads, NOPE),
            first_closed[:, nope_width : nope_width + span].reshape(depth, heads, -1),
            first_closed[:, nope_width + span : query_width].reshape(depth, heads, -1),
        ],
        axis=2,
    ).reshape(depth, query_width)
    both = first_closed[:, query_width:]
    both = both + other_x(both)
    grad_latent_weight = both[:, : KVR + ROPE]
    small_grads = both[:, KVR + ROPE :].T
    keyval_columns = w_keyval.shape[1] * latent_depth // depth
    grad_keyval_weight = (
        other_closed[:, :keyval_columns]
        .reshape(-1, latent_depth, keyval_columns)
        .transpose(1, 0, 2)
        .reshape(latent_depth, -1)
    )
    grad_output_weight = other_closed[:, keyval_columns:].T
    own_inputs = block_input.astype(f32)
    own_scale = rms_scale(own_inputs)
    own_unit = own_inputs * own_scale
    grad_input = grad_mixed + rms_back(grad_first * attn_gain_wide, own_unit, own_scale)
    return (
        block_output,
        grad_input,
        small_grads[0],
        grad_query_weight,
        grad_latent_weight,
        small_grads[2, :latent_depth],
        grad_keyval_weight,
        grad_output_weight,
        small_grads[1],
        small_grads[3 : 3 + experts].T,
        grad_shared_in,
        grad_shared_down,
        grad_expert_gate_up,
        grad_expert_down,
    )


def solution(mesh):
    in_specs = (
        P(("dp", "tensor"), None),
        P("dp", None),
        P("dp"),
        P("dp", None),
        P("dp"),
        P("dp", "tensor"),
        P("dp", None),
        P("dp"),
        P("dp", "tensor"),
        P("tensor", "dp"),
        P("dp"),
        P("dp", None),
        P(None, "dp", "tensor"),
        P("tensor", "dp"),
        P("dp", None, None, "tensor"),
        P("dp", "tensor", None),
        P(("dp", "tensor"), None),
    )
    out_specs = (
        P(("dp", "tensor"), None),
        P(("dp", "tensor"), None),
        P("dp"),
        P("dp", "tensor"),
        P("dp", None),
        P("dp"),
        P("dp", "tensor"),
        P("tensor", "dp"),
        P("dp"),
        P("dp", None),
        P(None, "dp", "tensor"),
        P("tensor", "dp"),
        P("dp", None, None, "tensor"),
        P("dp", "tensor", None),
    )
    body = gather_body if mesh.shape["dp"] == 16 else exchange_body
    return jax.shard_map(body, mesh=mesh, in_specs=in_specs, out_specs=out_specs, check_vma=False)
```

```python
import functools
import math

import jax
import jax.numpy as jnp
from jax import lax
from jax.experimental import pallas as pl
from jax.experimental.pallas import tpu as pltpu
from jax.sharding import PartitionSpec as P

D = 2048
NOPE = 128
ROPE = 64
VD = 128
KVR = 512
TOP = 6


EPSILON = 1e-06


def rms_scale(values):
    return lax.rsqrt(jnp.mean(values * values, axis=-1, keepdims=True) + EPSILON)


def rms_back(grad_unit, unit_rows, row_scale):
    return row_scale * (
        grad_unit - unit_rows * jnp.mean(grad_unit * unit_rows, axis=-1, keepdims=True)
    )


def rotary_tables(segment_row, width):
    count = segment_row.shape[0]
    position = jnp.arange(count, dtype=jnp.int32)
    same = segment_row[:, None] == segment_row[None, :]
    start = jnp.min(jnp.where(same, position[None, :], count), axis=1)
    offset = (position - start).astype(jnp.float32)
    freq = jnp.exp(jnp.arange(width // 2, dtype=jnp.float32) * (-2.0 * math.log(10000.0) / width))
    angle = offset[:, None] * freq[None, :]
    return (jnp.cos(angle), jnp.sin(angle))


def rotate(values, cosine, sine):
    half = values.shape[-1] // 2
    first = values[..., :half]
    second = values[..., half:]
    return jnp.concatenate(
        [first * cosine - second * sine, second * cosine + first * sine], axis=-1
    )


def rotate_back(grads, cosine, sine):
    half = grads.shape[-1] // 2
    first = grads[..., :half]
    second = grads[..., half:]
    return jnp.concatenate(
        [first * cosine + second * sine, second * cosine - first * sine], axis=-1
    )


def allowed_pairs(segment_row, count):
    position = jnp.arange(segment_row.shape[0], dtype=jnp.int32)
    live = position < count
    same = segment_row[:, None] == segment_row[None, :]
    causal = position[None, :] <= position[:, None]
    return same & causal & live[:, None] & live[None, :] | (position[:, None] == position[None, :])


def attention_scores(query_rows, key_nope, key_rope, allowed, scale):
    scores = jnp.einsum(
        "ihd,jhd->hij", query_rows[..., :NOPE], key_nope, preferred_element_type=jnp.float32
    )
    scores = scores + jnp.einsum(
        "ihd,jd->hij", query_rows[..., NOPE:], key_rope, preferred_element_type=jnp.float32
    )
    return jnp.where(allowed[None], scores * scale, -1e30)


def swiglu_back(gate, upper, grad_hidden, axis):
    sigmoid = jax.nn.sigmoid(gate)
    grad_gate = grad_hidden * upper * sigmoid * (1.0 + gate * (1.0 - sigmoid))
    grad_upper = grad_hidden * gate * sigmoid
    return jnp.stack([grad_gate, grad_upper], axis=axis)


def slot_layout(routes, experts, capacity):
    tokens = routes.shape[0]
    flat = routes.reshape(-1)
    onehot = (flat[:, None] == jnp.arange(experts, dtype=jnp.int32)[None, :]).astype(jnp.int32)
    rank = jnp.arange(flat.shape[0], dtype=jnp.int32)
    earlier = (rank[None, :] < rank[:, None]).astype(jnp.bfloat16)
    before = jnp.dot(
        earlier, onehot.astype(jnp.bfloat16), preferred_element_type=jnp.float32
    ).astype(jnp.int32)
    slot_index = jnp.sum(before * onehot, axis=1)
    target = flat * capacity + slot_index
    token_ids = jnp.arange(flat.shape[0], dtype=jnp.int32) // routes.shape[1]
    owner = jnp.full((experts * capacity,), tokens, jnp.int32).at[target].set(token_ids)
    return (slot_index, target, owner)


def to_expert_major(arrived, groups, local_experts):
    capacity = arrived.shape[1]
    width = arrived.shape[2]
    return (
        arrived.reshape(groups, local_experts, capacity, width)
        .transpose(1, 0, 2, 3)
        .reshape(local_experts, groups * capacity, width)
    )


def from_expert_major(results, groups):
    local_experts = results.shape[0]
    width = results.shape[2]
    capacity = results.shape[1] // groups
    return (
        results.reshape(local_experts, groups, capacity, width)
        .transpose(1, 0, 2, 3)
        .reshape(groups * local_experts, capacity, width)
    )


def exchange_body(
    block_input,
    segments,
    counts,
    routes,
    attn_gain,
    w_query,
    w_latent,
    latent_gain,
    w_keyval,
    w_output,
    ffn_gain,
    w_router,
    shared_gate_up,
    shared_down,
    expert_gate_up,
    expert_down,
    cotangent,
):
    gathered = (
        lax.all_gather(attn_gain, "dp", axis=0, tiled=True),
        lax.all_gather(w_query, "dp", axis=0, tiled=True),
        lax.all_gather(w_latent, "dp", axis=0, tiled=True),
        lax.all_gather(latent_gain, "dp", axis=0, tiled=True),
        lax.all_gather(w_keyval, "dp", axis=0, tiled=True),
        lax.all_gather(w_output, "dp", axis=1, tiled=True),
        lax.all_gather(ffn_gain, "dp", axis=0, tiled=True),
        lax.all_gather(w_router, "dp", axis=0, tiled=True),
        lax.all_gather(shared_gate_up, "dp", axis=1, tiled=True),
        lax.all_gather(shared_down, "dp", axis=1, tiled=True),
    )
    (
        full_attn_gain,
        query_weight,
        latent_weight,
        full_latent_gain,
        keyval_weight,
        output_weight,
        full_ffn_gain,
        router_weight,
        shared_in,
        shared_out,
    ) = gathered
    tensor_rank = lax.axis_index("tensor")
    dp_size = lax.axis_size("dp")
    rows_all = lax.all_gather(block_input, "tensor", axis=0, tiled=True)
    tokens = rows_all.shape[0]
    local_rows = block_input.shape[0]
    heads = query_weight.shape[1] // (NOPE + ROPE)
    experts = router_weight.shape[1]
    local_experts = expert_gate_up.shape[0]
    capacity = 2 * tokens * TOP // experts
    scale = (NOPE + ROPE) ** (-0.5)
    start = tensor_rank * local_rows
    cosine, sine = rotary_tables(segments[0], ROPE)
    allowed = allowed_pairs(segments[0], counts[0])
    attn_gain_wide = full_attn_gain.astype(jnp.float32)
    latent_gain_wide = full_latent_gain.astype(jnp.float32)
    ffn_gain_wide = full_ffn_gain.astype(jnp.float32)
    inputs = rows_all.astype(jnp.float32)
    first_scale = rms_scale(inputs)
    first_unit = inputs * first_scale
    first_normed = (first_unit * attn_gain_wide).astype(jnp.bfloat16)
    query = jnp.dot(first_normed, query_weight, preferred_element_type=jnp.float32).reshape(
        tokens, heads, NOPE + ROPE
    )
    query_rows = jnp.concatenate(
        [query[..., :NOPE], rotate(query[..., NOPE:], cosine[:, None, :], sine[:, None, :])],
        axis=-1,
    ).astype(jnp.bfloat16)
    latent_all = jnp.dot(first_normed, latent_weight, preferred_element_type=jnp.float32)
    latent = latent_all[:, :KVR]
    key_rope = rotate(latent_all[:, KVR:], cosine, sine).astype(jnp.bfloat16)
    latent_scale = rms_scale(latent)
    latent_unit = latent * latent_scale
    latent_normed = (latent_unit * latent_gain_wide).astype(jnp.bfloat16)
    keyval = (
        jnp.dot(latent_normed, keyval_weight, preferred_element_type=jnp.float32)
        .astype(jnp.bfloat16)
        .reshape(tokens, heads, NOPE + VD)
    )
    key_nope = keyval[..., :NOPE]
    values = keyval[..., NOPE:]
    scores = attention_scores(query_rows, key_nope, key_rope, allowed, scale)
    row_max = jnp.max(scores, axis=-1, keepdims=True)
    log_total = row_max + jnp.log(jnp.sum(jnp.exp(scores - row_max), axis=-1, keepdims=True))
    weights_low = jnp.exp(scores - log_total).astype(jnp.bfloat16)
    attended = (
        jnp.einsum("hij,jhd->ihd", weights_low, values, preferred_element_type=jnp.float32)
        .astype(jnp.bfloat16)
        .reshape(tokens, heads * VD)
    )
    attn_part = jnp.dot(attended, output_weight, preferred_element_type=jnp.float32)
    mixed = inputs + lax.psum(attn_part, "tensor")
    second_scale = rms_scale(mixed)
    second_unit = mixed * second_scale
    second_normed = (second_unit * ffn_gain_wide).astype(jnp.bfloat16)
    logits = jnp.dot(second_normed, router_weight, preferred_element_type=jnp.float32)
    probabilities = jax.nn.softmax(logits, axis=-1)
    gate_values = jnp.take_along_axis(probabilities, routes, axis=1)
    shared_pre = jnp.einsum(
        "td,gdf->tgf", second_normed, shared_in, preferred_element_type=jnp.float32
    )
    shared_hidden = (jax.nn.silu(shared_pre[:, 0]) * shared_pre[:, 1]).astype(jnp.bfloat16)
    shared_part = jnp.dot(shared_hidden, shared_out, preferred_element_type=jnp.float32)
    slot_index, target, owner = slot_layout(routes, experts, capacity)
    owner_grid = owner.reshape(experts, capacity)
    padded_rows = jnp.concatenate([second_normed, jnp.zeros((1, D), jnp.bfloat16)], axis=0)
    outgoing = padded_rows[owner_grid]
    arrived = lax.all_to_all(outgoing, "dp", split_axis=0, concat_axis=0, tiled=True)
    expert_rows = to_expert_major(arrived, dp_size, local_experts)
    expert_pre = jnp.einsum(
        "erd,egdf->ergf", expert_rows, expert_gate_up, preferred_element_type=jnp.float32
    )
    expert_hidden = (jax.nn.silu(expert_pre[:, :, 0]) * expert_pre[:, :, 1]).astype(jnp.bfloat16)
    expert_result = jnp.einsum(
        "erf,efd->erd", expert_hidden, expert_down, preferred_element_type=jnp.float32
    )
    returning = from_expert_major(expert_result, dp_size)
    returned = lax.all_to_all(
        returning.astype(jnp.bfloat16), "dp", split_axis=0, concat_axis=0, tiled=True
    ).astype(returning.dtype)
    padded_back = jnp.concatenate([returned.reshape(-1, D), jnp.zeros((1, D), jnp.float32)], axis=0)
    picked = padded_back[target].reshape(tokens, TOP, D)
    routed_part = jnp.sum(gate_values[:, :, None] * picked, axis=1)
    branch_sum = lax.psum_scatter(
        (shared_part + routed_part).astype(jnp.bfloat16), "tensor", scatter_dimension=0, tiled=True
    ).astype(jnp.float32)
    block_output = lax.dynamic_slice_in_dim(mixed, start, local_rows, 0) + branch_sum
    grad_rows = lax.all_gather(cotangent, "tensor", axis=0, tiled=True)
    grad_out = grad_rows.astype(jnp.float32)
    grad_shared_hidden = jnp.dot(grad_rows, shared_out.T, preferred_element_type=jnp.float32)
    grad_shared_out = jnp.dot(shared_hidden.T, grad_rows, preferred_element_type=jnp.float32)
    grad_shared_pre = swiglu_back(shared_pre[:, 0], shared_pre[:, 1], grad_shared_hidden, 1).astype(
        jnp.bfloat16
    )
    grad_shared_in = jnp.einsum(
        "td,tgf->gdf", second_normed, grad_shared_pre, preferred_element_type=jnp.float32
    )
    grad_second = jnp.einsum(
        "tgf,gdf->td", grad_shared_pre, shared_in, preferred_element_type=jnp.float32
    )
    gate_by_slot = (
        jnp.zeros((experts * capacity + 1,), jnp.float32).at[target].set(gate_values.reshape(-1))
    )
    slot_ids = jnp.arange(experts * capacity, dtype=jnp.int32).reshape(experts, capacity)
    padded_grad = jnp.concatenate([grad_out, jnp.zeros((1, D), jnp.float32)], axis=0)
    grad_outgoing = (gate_by_slot[slot_ids][..., None] * padded_grad[owner_grid]).astype(
        jnp.bfloat16
    )
    grad_arrived = lax.all_to_all(grad_outgoing, "dp", split_axis=0, concat_axis=0, tiled=True)
    grad_expert_rows = to_expert_major(grad_arrived, dp_size, local_experts)
    grad_expert_hidden = jnp.einsum(
        "erd,efd->erf", grad_expert_rows, expert_down, preferred_element_type=jnp.float32
    )
    grad_expert_down = jnp.einsum(
        "erf,erd->efd", expert_hidden, grad_expert_rows, preferred_element_type=jnp.float32
    )
    grad_expert_pre = swiglu_back(
        expert_pre[:, :, 0], expert_pre[:, :, 1], grad_expert_hidden, 2
    ).astype(jnp.bfloat16)
    grad_expert_gate_up = jnp.einsum(
        "erd,ergf->egdf", expert_rows, grad_expert_pre, preferred_element_type=jnp.float32
    )
    grad_expert_input = jnp.einsum(
        "ergf,egdf->erd", grad_expert_pre, expert_gate_up, preferred_element_type=jnp.float32
    )
    grad_returning = from_expert_major(grad_expert_input, dp_size)
    grad_returned = lax.all_to_all(
        grad_returning.astype(jnp.bfloat16), "dp", split_axis=0, concat_axis=0, tiled=True
    ).astype(grad_returning.dtype)
    padded_grad_back = jnp.concatenate(
        [grad_returned.reshape(-1, D), jnp.zeros((1, D), jnp.float32)], axis=0
    )
    grad_second = grad_second + jnp.sum(padded_grad_back[target].reshape(tokens, TOP, D), axis=1)
    grad_gates = jnp.sum(grad_out[:, None, :] * picked, axis=-1)
    grad_second, grad_gates = (
        lax.psum(grad_second.astype(jnp.bfloat16), "tensor").astype(jnp.float32),
        lax.psum(grad_gates.astype(jnp.bfloat16), "tensor").astype(jnp.float32),
    )
    chosen = (routes[:, :, None] == jnp.arange(experts, dtype=jnp.int32)[None, None, :]).astype(
        jnp.float32
    )
    grad_probabilities = jnp.sum(chosen * grad_gates[:, :, None], axis=1)
    grad_logits = probabilities * (
        grad_probabilities - jnp.sum(probabilities * grad_probabilities, axis=-1, keepdims=True)
    )
    grad_logits_low = grad_logits.astype(jnp.bfloat16)
    grad_router = jnp.dot(second_normed.T, grad_logits_low, preferred_element_type=jnp.float32)
    grad_second = grad_second + jnp.dot(
        grad_logits_low, router_weight.T, preferred_element_type=jnp.float32
    )
    gain_ffn_grad = jnp.sum(grad_second * second_unit, axis=0)
    grad_mixed = grad_out + rms_back(grad_second * ffn_gain_wide, second_unit, second_scale)
    grad_attn_low = grad_mixed.astype(jnp.bfloat16)
    grad_output_weight = jnp.dot(attended.T, grad_attn_low, preferred_element_type=jnp.float32)
    grad_attended = (
        jnp.dot(grad_attn_low, output_weight.T, preferred_element_type=jnp.float32)
        .astype(jnp.bfloat16)
        .reshape(tokens, heads, VD)
    )
    scores = attention_scores(query_rows, key_nope, key_rope, allowed, scale)
    weights = jnp.exp(scores - log_total)
    weights_low = weights.astype(jnp.bfloat16)
    grad_weights = jnp.einsum(
        "ihd,jhd->hij", grad_attended, values, preferred_element_type=jnp.float32
    )
    grad_values = jnp.einsum(
        "hij,ihd->jhd", weights_low, grad_attended, preferred_element_type=jnp.float32
    )
    grad_scores = (
        weights * (grad_weights - jnp.sum(weights * grad_weights, axis=-1, keepdims=True))
    ).astype(jnp.bfloat16)
    grad_query_nope = (
        jnp.einsum("hij,jhd->ihd", grad_scores, key_nope, preferred_element_type=jnp.float32)
        * scale
    )
    grad_query_rope = (
        jnp.einsum("hij,jd->ihd", grad_scores, key_rope, preferred_element_type=jnp.float32) * scale
    )
    grad_key_nope = (
        jnp.einsum(
            "hij,ihd->jhd", grad_scores, query_rows[..., :NOPE], preferred_element_type=jnp.float32
        )
        * scale
    )
    grad_key_rope = (
        jnp.einsum(
            "hij,ihd->jd", grad_scores, query_rows[..., NOPE:], preferred_element_type=jnp.float32
        )
        * scale
    )
    grad_query = (
        jnp.concatenate(
            [grad_query_nope, rotate_back(grad_query_rope, cosine[:, None, :], sine[:, None, :])],
            axis=-1,
        )
        .astype(jnp.bfloat16)
        .reshape(tokens, heads * (NOPE + ROPE))
    )
    grad_query_weight = jnp.dot(first_normed.T, grad_query, preferred_element_type=jnp.float32)
    grad_first = jnp.dot(grad_query, query_weight.T, preferred_element_type=jnp.float32)
    grad_keyval = (
        jnp.concatenate([grad_key_nope, grad_values], axis=-1)
        .astype(jnp.bfloat16)
        .reshape(tokens, heads * (NOPE + VD))
    )
    grad_keyval_weight = jnp.dot(latent_normed.T, grad_keyval, preferred_element_type=jnp.float32)
    grad_latent_normed = jnp.dot(grad_keyval, keyval_weight.T, preferred_element_type=jnp.float32)
    gain_latent_part = jnp.sum(grad_latent_normed * latent_unit, axis=0)
    grad_latent = rms_back(grad_latent_normed * latent_gain_wide, latent_unit, latent_scale)
    grad_latent_all = jnp.concatenate(
        [grad_latent, rotate_back(grad_key_rope, cosine, sine)], axis=-1
    )
    grad_first, grad_latent_all, gain_latent_grad = (
        lax.psum(grad_first.astype(jnp.bfloat16), "tensor").astype(jnp.float32),
        lax.psum(grad_latent_all.astype(jnp.bfloat16), "tensor").astype(jnp.float32),
        lax.psum(gain_latent_part.astype(jnp.bfloat16), "tensor").astype(jnp.float32),
    )
    grad_latent_low = grad_latent_all.astype(jnp.bfloat16)
    grad_latent_weight = jnp.dot(
        first_normed.T, grad_latent_low, preferred_element_type=jnp.float32
    )
    grad_first = grad_first + jnp.dot(
        grad_latent_low, latent_weight.T, preferred_element_type=jnp.float32
    )
    gain_attn_grad = jnp.sum(grad_first * first_unit, axis=0)
    grad_inputs = grad_mixed + rms_back(grad_first * attn_gain_wide, first_unit, first_scale)
    grad_local = lax.dynamic_slice_in_dim(grad_inputs, start, local_rows, 0)
    summed = (
        lax.psum_scatter(gain_attn_grad, "dp", scatter_dimension=0, tiled=True),
        lax.psum_scatter(grad_query_weight, "dp", scatter_dimension=0, tiled=True),
        lax.psum_scatter(grad_latent_weight, "dp", scatter_dimension=0, tiled=True),
        lax.psum_scatter(gain_latent_grad, "dp", scatter_dimension=0, tiled=True),
        lax.psum_scatter(grad_keyval_weight, "dp", scatter_dimension=0, tiled=True),
        lax.psum_scatter(grad_output_weight, "dp", scatter_dimension=1, tiled=True),
        lax.psum_scatter(gain_ffn_grad, "dp", scatter_dimension=0, tiled=True),
        lax.psum_scatter(grad_router, "dp", scatter_dimension=0, tiled=True),
        lax.psum_scatter(grad_shared_in, "dp", scatter_dimension=1, tiled=True),
        lax.psum_scatter(grad_shared_out, "dp", scatter_dimension=1, tiled=True),
    )
    return (
        block_output,
        grad_local,
        summed[0],
        summed[1],
        summed[2],
        summed[3],
        summed[4],
        summed[5],
        summed[6],
        summed[7],
        summed[8],
        summed[9],
        grad_expert_gate_up,
        grad_expert_down,
    )


RINGS = 4


def ring_step(values):
    return lax.ppermute(values, "dp", [(i, (i + RINGS) % 16) for i in range(16)])


def other_y(values):
    return lax.ppermute(values, "dp", [(i, i ^ 2) for i in range(16)])


def other_core(values):
    return lax.ppermute(values, "dp", [(i, i ^ 1) for i in range(16)])


def other_x(values):
    return lax.ppermute(values, "tensor", [(0, 1), (1, 0)])


def fence_kernel(*refs):
    pass


def after(values, *others):
    anywhere = pl.BlockSpec(memory_space=pl.ANY)
    return pl.pallas_call(
        fence_kernel,
        out_shape=jax.ShapeDtypeStruct(values.shape, values.dtype),
        in_specs=[anywhere] * (1 + len(others)),
        out_specs=anywhere,
        input_output_aliases={0: 0},
    )(values, *others)


def gather_whole(rows, early):
    ring = [rows, ring_step(rows)]
    ring.append(ring_step(ring[1]))
    ring.append(ring_step(after(ring[2], early)))
    over_x = [other_x(part) for part in ring]
    groups = []
    for k in (0, 2):
        held = jnp.concatenate(ring[k : k + 2], axis=0)
        across = jnp.concatenate(over_x[k : k + 2], axis=0)
        beside = other_y(held)
        groups.append((held, beside, across, other_y(across) if k else other_x(beside)))
    return groups, ring, over_x


def gather_rows(rows, corners):
    held = [rows, ring_step(rows)]
    first = (other_y(rows), other_x(rows))
    held.append(ring_step(after(held[1], *first)))
    held.append(ring_step(held[2]))
    groups = []
    for k, current in enumerate((held[0], held[1], jnp.concatenate(held[2:], axis=0))):
        beside, across = (other_y(current), other_x(current)) if k else first
        corner = other_x(beside) if corners[k] == "x" else other_y(across)
        groups.append((current, beside, across, corner))
    return held, groups


def add_low(first, second):
    return (first.astype(jnp.float32) + second.astype(jnp.float32)).astype(jnp.bfloat16)


def turn_corner(plane, direction):
    own, beside, across, corner = plane
    if direction == "x":
        return own, add_low(beside, other_x(corner)), across
    return own, beside, add_low(across, other_y(corner))


def close_plane(turned):
    own, beside, across = turned
    return own, other_y(beside), other_x(across)


def wide_sum(*values):
    total = values[0].astype(jnp.float32)
    for value in values[1:]:
        total = total + value.astype(jnp.float32)
    return total


def ring_sum(parts, low):
    moving = parts[1]
    for distance in (2, 3, 0):
        moving = ring_step(moving.astype(low)).astype(jnp.float32) + parts[distance].astype(
            jnp.float32
        )
    return moving


def ring_shards(shard):
    held = [shard]
    for _ in range(RINGS - 1):
        held.append(ring_step(held[-1]))
    return held


def gather_weight(shard, early):
    held, besides = [shard], []
    for distance in range(RINGS):
        beside = other_y(after(held[1], *early) if distance == 1 else held[distance])
        besides.append(beside)
        if distance < RINGS - 1:
            source = after(held[distance], besides[distance - 1]) if distance else shard
            held.append(ring_step(source))
    chunks = []
    for distance, (current, beside) in enumerate(zip(held, besides)):
        for flip_y, chunk in ((0, current), (1, beside)):
            for flip_core, piece in ((0, chunk), (1, other_core(chunk))):
                chunks.append(((distance, flip_y, flip_core), piece))
    return chunks, held, besides


def place_of(coords, key):
    z, y, core = coords
    distance, flip_y, flip_core = key
    return (
        lax.rem(z + RINGS - distance, RINGS) * 4
        + (1 - y if flip_y else y) * 2
        + (1 - core if flip_core else core)
    )


def weight_keys():
    return [
        (distance, flip_y, flip_core)
        for flip_core in (0, 1)
        for flip_y in (0, 1)
        for distance in range(RINGS)
    ]


def scatter_blocks(grads, low):
    half = grads.shape[0] // 2
    total = grads[:half].astype(jnp.float32) + other_core(grads[half:].astype(low)).astype(
        jnp.float32
    )
    quarter = half // 2
    total = total[:quarter] + other_y(total[quarter:].astype(low)).astype(jnp.float32)
    size = quarter // RINGS
    return ring_sum([total[r * size : (r + 1) * size] for r in range(RINGS)], low)


def pick_blocks(values, order):
    chosen = order[:, None] == jnp.arange(values.shape[0], dtype=jnp.int32)[None, :]
    chosen = chosen.reshape(chosen.shape + (1,) * (values.ndim - 1))
    return jnp.sum(jnp.where(chosen, values[None], 0.0), axis=1)


def wide_dot(left, right):
    return jnp.dot(left, right, preferred_element_type=jnp.float32)


def dot_turned(left, right):
    return lax.dot_general(left, right, (((1,), (1,)), ((), ())), preferred_element_type=jnp.float32)


def dot_rows(left, right):
    return lax.dot_general(left, right, (((0,), (0,)), ((), ())), preferred_element_type=jnp.float32)


TILE = 256


def whole(array):
    return pl.BlockSpec(array.shape, lambda *i: (0,) * array.ndim)


def in_vmem(count):
    return [pl.BlockSpec(memory_space=pltpu.VMEM)] * count


def in_place(count):
    return [pl.BlockSpec(memory_space=pl.ANY)] * count


def head_scores(heads, h, nope_ref, turned_ref, keyval_ref, key_ref, masks):
    span = ROPE // 2 * heads
    column = pl.ds(pl.multiple_of(h * NOPE, NOPE), NOPE)
    key_column = pl.ds(pl.multiple_of(h * (NOPE + VD), NOPE), NOPE)
    scores = dot_turned(nope_ref[:, column], keyval_ref[:, key_column])
    for k in (0, 1):
        part = turned_ref[:, k * span : (k + 1) * span]
        part = jnp.where(masks, part, jnp.zeros_like(part))
        scores += dot_turned(part, key_ref[:, k * span : (k + 1) * span])
    return scores * (NOPE + ROPE) ** (-0.5)


def head_lanes(heads, h):
    span = ROPE // 2 * heads
    lane = lax.broadcasted_iota(jnp.int32, (1, span), 1)
    return (lane >= h * (ROPE // 2)) & (lane < (h + 1) * (ROPE // 2))


def allowed_rows(count, segment_row, segment_column):
    tokens = segment_row.shape[1]
    column = lax.broadcasted_iota(jnp.int32, (tokens, tokens), 0)
    row = lax.broadcasted_iota(jnp.int32, (tokens, tokens), 1)
    live = (column < count) & (row < count) & (row <= column)
    return (segment_row == segment_column) & live | (column == row)


def attend_kernel(
    keys,
    extra,
    heads,
    sizes,
    place_ref,
    segment_row_ref,
    segment_column_ref,
    cosine_ref,
    sine_ref,
    own_ref,
    other_ref,
    *refs,
):
    depth, query_width, used, latent_depth, keyval_part, first_width = sizes
    chunks = refs[: len(keys)]
    (
        own_out,
        sent_out,
        first_ref,
        keyval_weight_ref,
        output_ref,
        normed_ref,
        nope_ref,
        turned_ref,
        latent_ref,
        key_ref,
        keyval_ref,
        total_ref,
        attended_ref,
        gains_ref,
        latent_gain_ref,
        semaphores,
    ) = refs[len(keys) + extra :]
    f32, bf16 = jnp.float32, jnp.bfloat16
    local_rows = own_ref.shape[0]
    tokens = 2 * local_rows
    coords = (place_ref[0], place_ref[1], place_ref[2])
    x = place_ref[3]
    copies = []
    parts = depth // latent_depth
    for key, chunk in zip(keys, chunks):
        block = place_of(coords, key)
        rows = pl.ds(pl.multiple_of(block * depth, depth), depth)
        small_rows = pl.ds(pl.multiple_of(block * latent_depth, latent_depth), latent_depth)
        moves = [(chunk.at[:, pl.ds(0, first_width)], first_ref.at[rows])]
        for k in range(parts):
            moves.append(
                (
                    chunk.at[
                        pl.ds(k * latent_depth, latent_depth), pl.ds(first_width, keyval_part)
                    ],
                    keyval_weight_ref.at[small_rows, pl.ds(k * keyval_part, keyval_part)],
                )
            )
        moves.append(
            (
                chunk.at[:, pl.ds(first_width + keyval_part, heads * VD)],
                output_ref.at[rows],
            )
        )
        for source, target in moves:
            copies.append(pltpu.make_async_copy(source, target, semaphores.at[len(copies)]))
    for copy in copies:
        copy.start()
    for copy in copies:
        copy.wait()

    edge = query_width + KVR
    spread = jnp.transpose(first_ref[:, edge:].astype(f32))[used - edge : used - edge + 8]
    gains_ref[...] = spread
    gain = spread[0:1]
    source = lax.broadcasted_iota(jnp.int32, (D, KVR), 0)
    target = lax.broadcasted_iota(jnp.int32, (D, KVR), 1)
    wanted = target // latent_depth * depth + target % latent_depth
    chosen = jnp.where(source == wanted, 1.0, 0.0).astype(bf16)
    latent_gain = wide_dot(spread.astype(bf16), chosen)[2:3]
    latent_gain_ref[...] = latent_gain
    for ref, start in ((own_ref, x * local_rows), (other_ref, (1 - x) * local_rows)):
        rows = ref[...].astype(f32)
        unit = rows * lax.rsqrt(jnp.mean(rows * rows, axis=1, keepdims=True) + EPSILON)
        normed_ref[pl.ds(pl.multiple_of(start, local_rows), local_rows), :] = (unit * gain).astype(
            bf16
        )
    nope_width = heads * NOPE
    span = heads * (ROPE // 2)
    half = nope_width // 2
    for k in (0, 1):
        nope_ref[:, k * half : (k + 1) * half] = wide_dot(
            normed_ref[...], first_ref[:, k * half : (k + 1) * half]
        ).astype(bf16)
    turning = wide_dot(normed_ref[...], first_ref[:, nope_width : nope_width + 2 * span])
    cosine, sine = cosine_ref[...], sine_ref[...]
    first, second = turning[:, :span], turning[:, span:]
    turned_ref[:, :span] = (first * cosine - second * sine).astype(bf16)
    turned_ref[:, span:] = (second * cosine + first * sine).astype(bf16)
    latent = wide_dot(normed_ref[...], first_ref[:, query_width : query_width + KVR])
    latent_ref[...] = latent
    tail = wide_dot(normed_ref[...], first_ref[:, query_width + KVR :])
    lane = lax.broadcasted_iota(jnp.int32, (1, tail.shape[1]), 1)
    swapped = jnp.where(
        lane < ROPE // 2,
        -pltpu.roll(tail, tail.shape[1] - ROPE // 2, 1),
        pltpu.roll(tail, ROPE // 2, 1),
    )
    width = tail.shape[1]
    turned_key = tail * cosine[:, :width] + swapped * sine[:, :width]
    turned_key = jnp.where(lane < ROPE, turned_key, 0.0).astype(bf16)
    source = lax.broadcasted_iota(jnp.int32, (width, 2 * span), 0)
    target = lax.broadcasted_iota(jnp.int32, (width, 2 * span), 1)
    wanted = target % (ROPE // 2) + jnp.where(target < span, 0, ROPE // 2)
    key_ref[...] = wide_dot(turned_key, (source == wanted).astype(bf16)).astype(bf16)
    unit = latent * lax.rsqrt(jnp.mean(latent * latent, axis=1, keepdims=True) + EPSILON)
    latent_normed = (unit * latent_gain).astype(bf16)
    half = keyval_ref.shape[1] // 4
    for k in range(4):
        keyval_ref[:, k * half : (k + 1) * half] = wide_dot(
            latent_normed, keyval_weight_ref[:, k * half : (k + 1) * half]
        ).astype(bf16)
    allowed = allowed_rows(place_ref[4], segment_row_ref[...], segment_column_ref[...])
    total_lane = lax.broadcasted_iota(jnp.int32, total_ref.shape, 1)
    total_ref[...] = jnp.zeros_like(total_ref)

    def one_head(h, _):
        scores = head_scores(
            heads, h, nope_ref, turned_ref, keyval_ref, key_ref, head_lanes(heads, h)
        )
        scores = jnp.where(allowed, scores, -1e30)
        most = jnp.max(scores, axis=1, keepdims=True)
        total = most + jnp.log(jnp.sum(jnp.exp(scores - most), axis=1, keepdims=True))
        weights = jnp.exp(scores - total).astype(bf16)
        total_ref[...] += jnp.where(total_lane == h, total, 0.0)
        value_column = pl.ds(pl.multiple_of(h * (NOPE + VD) + NOPE, NOPE), VD)
        attended_ref[:, pl.ds(pl.multiple_of(h * VD, VD), VD)] = wide_dot(
            weights, keyval_ref[:, value_column]
        ).astype(bf16)
        return 0

    lax.fori_loop(0, heads, one_head, 0)
    own = pl.ds(pl.multiple_of(x * local_rows, local_rows), local_rows)
    other = pl.ds(pl.multiple_of((1 - x) * local_rows, local_rows), local_rows)
    pieces = 4
    size = output_ref.shape[0] // pieces
    for k in range(pieces):
        columns = slice(k * size, (k + 1) * size)
        own_out[:, columns] = dot_turned(attended_ref[own, :], output_ref[columns, :])
        sent_out[:, columns] = dot_turned(attended_ref[other, :], output_ref[columns, :]).astype(
            bf16
        )


def attend_forward(place, segments, cosine, sine, own, other, chunks, heads, sizes, others):
    depth, query_width, used, latent_depth, keyval_part, first_width = sizes
    f32, bf16 = jnp.float32, jnp.bfloat16
    keys = [key for key, _ in chunks]
    local_rows = own.shape[0]
    tokens = 2 * local_rows
    span = heads * (ROPE // 2)
    shapes = [
        ((local_rows, D), f32),
        ((local_rows, D), bf16),
        ((D, first_width), bf16),
        ((KVR, heads * (NOPE + VD)), bf16),
        ((D, heads * VD), bf16),
        ((tokens, D), bf16),
        ((tokens, heads * NOPE), bf16),
        ((tokens, 2 * span), bf16),
        ((tokens, KVR), f32),
        ((tokens, 2 * span), bf16),
        ((tokens, heads * (NOPE + VD)), bf16),
        ((tokens, 128), f32),
        ((tokens, heads * VD), bf16),
        ((8, D), f32),
        ((1, KVR), f32),
    ]
    return pl.pallas_call(
        functools.partial(attend_kernel, keys, len(others), heads, sizes),
        out_shape=[jax.ShapeDtypeStruct(*shape) for shape in shapes],
        in_specs=[pl.BlockSpec(memory_space=pltpu.SMEM)]
        + in_vmem(6)
        + in_place(len(chunks) + len(others)),
        out_specs=in_vmem(len(shapes)),
        scratch_shapes=[
            pltpu.SemaphoreType.DMA((len(chunks) * (2 + depth // latent_depth),))
        ],
        compiler_params=pltpu.CompilerParams(vmem_limit_bytes=48 * 1024 * 1024),
        cost_estimate=pl.CostEstimate(
            flops=2 * tokens * D * (first_width + heads * VD + 1024),
            bytes_accessed=4 * D * (first_width + 1536),
            transcendentals=2 * heads * tokens * tokens,
        ),
    )(
        place,
        segments,
        segments.T,
        cosine,
        sine,
        own,
        other,
        *[piece for _, piece in chunks],
        *others,
    )


def attend_back_kernel(
    heads,
    place_ref,
    segment_row_ref,
    segment_column_ref,
    cosine_ref,
    sine_ref,
    own_ref,
    other_ref,
    keyval_weight_ref,
    output_ref,
    nope_ref,
    turned_ref,
    latent_ref,
    key_ref,
    keyval_ref,
    total_ref,
    latent_gain_ref,
    projected_ref,
    keyval_grad_ref,
    latent_out,
    gain_ref,
    grad_ref,
    turn_ref,
    back_ref,
):
    f32, bf16 = jnp.float32, jnp.bfloat16
    local_rows = own_ref.shape[0]
    x = place_ref[3]
    span = heads * (ROPE // 2)
    nope_width = heads * NOPE
    query_width = nope_width + 2 * span
    scale = (NOPE + ROPE) ** (-0.5)
    for ref, start in ((own_ref, x * local_rows), (other_ref, (1 - x) * local_rows)):
        rows = pl.ds(pl.multiple_of(start, local_rows), local_rows)
        for k in (0, 1):
            half = slice(k * nope_width // 2, (k + 1) * nope_width // 2)
            grad_ref[rows, half] = wide_dot(ref[...], output_ref[:, half]).astype(bf16)
    allowed = allowed_rows(place_ref[4], segment_row_ref[...], segment_column_ref[...])
    total_lane = lax.broadcasted_iota(jnp.int32, total_ref.shape, 1)
    turn_ref[...] = jnp.zeros_like(turn_ref)
    back_ref[...] = jnp.zeros_like(back_ref)

    def one_head(h, _):
        mask = head_lanes(heads, h)
        scores = head_scores(heads, h, nope_ref, turned_ref, keyval_ref, key_ref, mask)
        total = jnp.sum(jnp.where(total_lane == h, total_ref[...], 0.0), axis=1, keepdims=True)
        weights = jnp.exp(jnp.where(allowed, scores, -1e30) - total)
        weights_low = weights.astype(bf16)
        column = pl.ds(pl.multiple_of(h * NOPE, NOPE), NOPE)
        key_column = pl.ds(pl.multiple_of(h * (NOPE + VD), NOPE), NOPE)
        value_column = pl.ds(pl.multiple_of(h * (NOPE + VD) + NOPE, NOPE), VD)
        grads = grad_ref[:, column]
        grad_weights = dot_turned(grads, keyval_ref[:, value_column])
        keyval_grad_ref[:, value_column] = dot_rows(weights_low, grads).astype(bf16)
        grad_scores = (
            weights * (grad_weights - jnp.sum(weights * grad_weights, axis=1, keepdims=True))
        ).astype(bf16)
        projected_ref[:, column] = (
            scale * wide_dot(grad_scores, keyval_ref[:, key_column])
        ).astype(bf16)
        keyval_grad_ref[:, key_column] = (
            scale * dot_rows(grad_scores, nope_ref[:, column])
        ).astype(bf16)
        for k in (0, 1):
            part = slice(k * span, (k + 1) * span)
            turn = wide_dot(grad_scores, key_ref[:, part])
            turn_ref[:, part] += jnp.where(mask, turn, 0.0)
            own = turned_ref[:, part]
            own = jnp.where(mask, own, jnp.zeros_like(own))
            back_ref[:, part] += dot_rows(grad_scores, own)
        return 0

    lax.fori_loop(0, heads, one_head, 0)
    cosine, sine = cosine_ref[...], sine_ref[...]
    first, second = scale * turn_ref[:, :span], scale * turn_ref[:, span:]
    projected_ref[:, nope_width : nope_width + span] = (first * cosine + second * sine).astype(bf16)
    projected_ref[:, nope_width + span : query_width] = (second * cosine - first * sine).astype(
        bf16
    )
    folded = []
    for k in (0, 1):
        part = scale * back_ref[:, k * span : (k + 1) * span]
        shift = span // 2
        while shift >= ROPE // 2:
            part = part + pltpu.roll(part, shift, 1)
            shift //= 2
        folded.append(part)
    width = projected_ref.shape[1] - query_width - KVR
    lane = lax.broadcasted_iota(jnp.int32, (1, width), 1)
    first = (folded[0] * cosine + folded[1] * sine)[:, :width]
    second = (folded[1] * cosine - folded[0] * sine)[:, :width]
    projected_ref[:, query_width + KVR :] = jnp.where(
        lane < ROPE // 2, first, jnp.where(lane < ROPE, second, 0.0)
    ).astype(bf16)
    gain = latent_gain_ref[...]
    latent = latent_ref[...]
    row_scale = lax.rsqrt(jnp.mean(latent * latent, axis=1, keepdims=True) + EPSILON)
    unit = latent * row_scale
    latent_out[...] = (unit * gain).astype(bf16)
    grad_normed = dot_turned(keyval_grad_ref[...], keyval_weight_ref[...])
    gain_ref[...] = jnp.sum(grad_normed * unit, axis=0, keepdims=True)
    grad_unit = grad_normed * gain
    projected_ref[:, query_width : query_width + KVR] = (
        row_scale * (grad_unit - unit * jnp.mean(grad_unit * unit, axis=1, keepdims=True))
    ).astype(bf16)


def attend_back(place, segments, cosine, sine, own, other, saved, heads, first_width, others):
    f32, bf16 = jnp.float32, jnp.bfloat16
    keyval = saved[6]
    tokens = 2 * own.shape[0]
    span = heads * (ROPE // 2)
    return pl.pallas_call(
        lambda *refs: attend_back_kernel(heads, *refs[:16], *refs[16 + len(others) :]),
        out_shape=[
            jax.ShapeDtypeStruct((tokens, first_width), bf16),
            jax.ShapeDtypeStruct((tokens, keyval.shape[1]), bf16),
            jax.ShapeDtypeStruct((tokens, KVR), bf16),
            jax.ShapeDtypeStruct((1, KVR), f32),
        ],
        in_specs=[pl.BlockSpec(memory_space=pltpu.SMEM)] + in_vmem(15) + in_place(len(others)),
        out_specs=in_vmem(4),
        scratch_shapes=[
            pltpu.VMEM((tokens, heads * NOPE), bf16),
            pltpu.VMEM((tokens, 2 * span), f32),
            pltpu.VMEM((tokens, 2 * span), f32),
        ],
        compiler_params=pltpu.CompilerParams(vmem_limit_bytes=48 * 1024 * 1024),
        cost_estimate=pl.CostEstimate(
            flops=2 * tokens * D * 3000,
            bytes_accessed=2 * D * 1536,
            transcendentals=heads * tokens * tokens,
        ),
    )(
        place,
        segments,
        segments.T,
        cosine,
        sine,
        own,
        other,
        *saved,
        *others,
    )


def first_grads_kernel(extra, places_ref, left_ref, right_ref, small_ref, *refs):
    out_ref = refs[-1]
    size = left_ref.shape[1]
    edge = right_ref.shape[1] - small_ref.shape[0]
    result = dot_rows(left_ref[...], right_ref[...])
    for value, some in (
        (result[:, :edge], slice(0, edge)),
        (result[:, edge:] + jnp.transpose(small_ref[...]), slice(edge, right_ref.shape[1])),
    ):
        if extra:
            value = value + refs[0][:, some].astype(jnp.float32)
        out_ref[:, some] = value.astype(jnp.bfloat16)


def other_grads_kernel(first, extra, places_ref, latent_ref, keyval_ref, grad_ref, attended_ref, *refs):
    out_ref, keyval_all = refs[-2:]
    step = pl.program_id(0)
    size = grad_ref.shape[1]
    latent_size = latent_ref.shape[1] // places_ref.shape[0]
    parts = size // latent_size
    columns = keyval_ref.shape[1] // parts

    @pl.when(step == 0)
    def _():
        for k in range(parts):
            some = slice(k * columns, (k + 1) * columns)
            keyval_all[:, some] = dot_rows(latent_ref[...], keyval_ref[:, some])

    start = pl.multiple_of(places_ref[first + step] * latent_size, latent_size)
    strip = keyval_all[pl.ds(start, latent_size), :]
    keyval = jnp.concatenate([strip[:, k * columns : (k + 1) * columns] for k in range(parts)], axis=0)
    output = dot_rows(grad_ref[...], attended_ref[...])
    for value, some in (
        (keyval, slice(0, columns)),
        (output, slice(columns, columns + output.shape[1])),
    ):
        if extra:
            value = value + refs[0][:, some].astype(jnp.float32)
        out_ref[:, some] = value.astype(jnp.bfloat16)


def still(array):
    return pl.BlockSpec(array.shape, lambda i, where: (0, 0))


def grads_call(
    kernel, specs, operands, scratch, size, width, places, first, count, arrived, others
):
    extra = [] if arrived is None else [arrived]
    return pl.pallas_call(
        lambda *refs: kernel(
            len(extra),
            *refs[: 1 + len(operands) + len(extra)],
            *refs[1 + len(operands) + len(extra) + len(others) :],
        ),
        grid_spec=pltpu.PrefetchScalarGridSpec(
            num_scalar_prefetch=1,
            grid=(count,),
            in_specs=specs
            + [pl.BlockSpec((size, width), lambda i, where: (first + i, 0))] * len(extra)
            + in_place(len(others)),
            out_specs=pl.BlockSpec((size, width), lambda i, where: (i, 0)),
            scratch_shapes=scratch,
        ),
        out_shape=jax.ShapeDtypeStruct((count * size, width), jnp.bfloat16),
        compiler_params=pltpu.CompilerParams(vmem_limit_bytes=32 * 1024 * 1024),
        cost_estimate=pl.CostEstimate(
            flops=1024 * count * size * width,
            bytes_accessed=4 * count * size * width,
            transcendentals=0,
        ),
    )(places, *operands, *extra, *others)


def first_grads(left, right, small, places, first, count, arrived=None, others=()):
    rows, width = right.shape
    size = left.shape[1] // places.shape[0]
    specs = [
        pl.BlockSpec((rows, size), lambda i, where: (0, where[first + i])),
        still(right),
        pl.BlockSpec((small.shape[0], size), lambda i, where: (0, where[first + i])),
    ]
    return grads_call(
        first_grads_kernel,
        specs,
        (left, right, small),
        [],
        size,
        width,
        places,
        first,
        count,
        arrived,
        others,
    )


def other_grads(latent, keyval, grad, attended, places, first, count, arrived=None, others=()):
    rows = grad.shape[0]
    blocks = places.shape[0]
    size = grad.shape[1] // blocks
    parts = size // (latent.shape[1] // blocks)
    width = keyval.shape[1] // parts + attended.shape[1]
    specs = [
        still(latent),
        still(keyval),
        pl.BlockSpec((rows, size), lambda i, where: (0, where[first + i])),
        still(attended),
    ]
    scratch = [pltpu.VMEM((latent.shape[1], keyval.shape[1]), jnp.float32)]
    return grads_call(
        functools.partial(other_grads_kernel, first),
        specs,
        (latent, keyval, grad, attended),
        scratch,
        size,
        width,
        places,
        first,
        count,
        arrived,
        others,
    )


def first_back_kernel(place_ref, own_ref, other_ref, grad_ref, weight_ref, own_out, sent_out, gain_ref):
    local_rows = own_ref.shape[0]
    x = place_ref[3]
    size = weight_ref.shape[0] // 4
    for ref, start, out in (
        (own_ref, x * local_rows, own_out),
        (other_ref, (1 - x) * local_rows, sent_out),
    ):
        rows = ref[...].astype(jnp.float32)
        unit = rows * lax.rsqrt(jnp.mean(rows * rows, axis=1, keepdims=True) + EPSILON)
        grads = grad_ref[pl.ds(pl.multiple_of(start, local_rows), local_rows), :]
        for k in range(4):
            some = slice(k * size, (k + 1) * size)
            part = dot_turned(grads, weight_ref[some, :])
            out[:, some] = part.astype(out.dtype)
            gain = jnp.sum(part * unit[:, some], axis=0, keepdims=True)
            if ref is own_ref:
                gain_ref[:, some] = gain
            else:
                gain_ref[:, some] += gain


def first_back(place, own, other, grads, weight):
    f32, bf16 = jnp.float32, jnp.bfloat16
    depth = weight.shape[0]
    return pl.pallas_call(
        first_back_kernel,
        out_shape=[
            jax.ShapeDtypeStruct(own.shape, f32),
            jax.ShapeDtypeStruct(own.shape, bf16),
            jax.ShapeDtypeStruct((1, depth), f32),
        ],
        in_specs=[pl.BlockSpec(memory_space=pltpu.SMEM)] + in_vmem(4),
        out_specs=in_vmem(3),
        compiler_params=pltpu.CompilerParams(vmem_limit_bytes=32 * 1024 * 1024),
        cost_estimate=pl.CostEstimate(
            flops=4 * own.shape[0] * weight.shape[0] * weight.shape[1],
            bytes_accessed=2 * weight.shape[0] * weight.shape[1],
            transcendentals=0,
        ),
    )(place, own, other, grads, weight)


def close_ring(near, arrived):
    size = near.shape[0] // RINGS
    total = near.astype(jnp.float32) + arrived.astype(jnp.float32)
    return ring_sum([total[r * size : (r + 1) * size] for r in range(RINGS)], jnp.bfloat16)


def pack_kernel(heads, query_ref, latent_ref, small_ref, keyval_ref, output_ref, out_ref):
    half = ROPE // 2
    head = NOPE + ROPE
    nope_width = heads * NOPE
    for h in range(heads):
        start = h * head
        out_ref[:, h * NOPE : (h + 1) * NOPE] = query_ref[:, start : start + NOPE]
        for k in (0, 1):
            to = nope_width + k * heads * half + h * half
            out_ref[:, to : to + half] = query_ref[
                :, start + NOPE + k * half : start + NOPE + (k + 1) * half
            ]
    at = heads * head
    edge = at + KVR
    out_ref[:, at:edge] = latent_ref[:, :KVR]
    out_ref[:, edge : edge + 128] = jnp.concatenate([latent_ref[:, KVR:], small_ref[...]], axis=1)
    at = edge + 128
    size = keyval_ref.shape[0]
    parts = out_ref.shape[0] // size
    part = keyval_ref.shape[1] // parts
    for k in range(parts):
        out_ref[k * size : (k + 1) * size, at : at + part] = keyval_ref[
            :, k * part : (k + 1) * part
        ]
    out_ref[:, at + part :] = jnp.transpose(output_ref[...].astype(jnp.float32)).astype(
        jnp.bfloat16
    )


def pack_weights(query, latent, small, keyval, output):
    depth, query_width = query.shape
    heads = query_width // (NOPE + ROPE)
    width = query_width + KVR + 128 + keyval.size // depth + output.shape[0]
    return pl.pallas_call(
        functools.partial(pack_kernel, heads),
        out_shape=jax.ShapeDtypeStruct((depth, width), jnp.bfloat16),
        in_specs=in_vmem(5),
        out_specs=pl.BlockSpec(memory_space=pltpu.VMEM),
    )(query, latent, small, keyval, output)


def load_pieces(pieces, starts, target, semaphores):
    size = target.shape[0] // len(pieces)
    copies = [
        pltpu.make_async_copy(
            piece.at[pl.ds(start, size)], target.at[pl.ds(k * size, size)], semaphores.at[k]
        )
        for k, (piece, start) in enumerate(zip(pieces, starts))
    ]
    for copy in copies:
        copy.start()
    for copy in copies:
        copy.wait()


def shared_stride(shared):
    return -(-shared // 32) * 32


def pack_shared_kernel(blocks, shared, in_ref, down_ref, out_ref):
    stride = shared_stride(shared)
    out_ref[...] = jnp.zeros_like(out_ref)
    for k in range(3):
        if k < 2:
            units = jnp.transpose(in_ref[k].astype(jnp.float32)).astype(jnp.bfloat16)
        else:
            units = down_ref[...]
        for b in range(blocks):
            out_ref[b, k * stride : k * stride + shared] = units[b * shared : (b + 1) * shared]


def pack_shared(shared_in, shared_down, blocks, others):
    depth = shared_in.shape[1]
    shared = shared_down.shape[0] // blocks
    return pl.pallas_call(
        lambda in_ref, down_ref, *refs: pack_shared_kernel(
            blocks, shared, in_ref, down_ref, refs[-1]
        ),
        out_shape=jax.ShapeDtypeStruct((blocks, 3 * shared_stride(shared), depth), jnp.bfloat16),
        in_specs=in_vmem(2) + in_place(len(others)),
        out_specs=pl.BlockSpec(memory_space=pltpu.VMEM),
    )(shared_in, shared_down, *others)


def unpack_shared_kernel(shared, packed_ref, in_ref, down_ref, units_ref):
    stride = shared_stride(shared)
    blocks = packed_ref.shape[0]
    for k in range(3):
        target = down_ref if k == 2 else units_ref
        for b in range(blocks):
            target[b * shared : (b + 1) * shared, :] = packed_ref[
                b, k * stride : k * stride + shared
            ].astype(jnp.float32)
        if k < 2:
            in_ref[k] = jnp.transpose(units_ref[...])


def unpack_shared(packed, shared, others):
    blocks, _, depth = packed.shape
    return pl.pallas_call(
        lambda packed_ref, *refs: unpack_shared_kernel(shared, packed_ref, *refs[len(others) :]),
        out_shape=[
            jax.ShapeDtypeStruct((2, depth, blocks * shared), jnp.float32),
            jax.ShapeDtypeStruct((blocks * shared, depth), jnp.float32),
        ],
        in_specs=in_vmem(1) + in_place(len(others)),
        out_specs=in_vmem(2),
        scratch_shapes=[pltpu.VMEM((blocks * shared, depth), jnp.float32)],
    )(packed, *others)


def pack_units_kernel(units, shared, own_in, other_in, own_down, other_down, near, far, *refs):
    outs = refs[-3:]
    hole = -(-units // TILE) * TILE
    stride = shared_stride(shared)
    columns = outs[0].shape[1]
    size = near.shape[2]
    for k, out in enumerate(outs):
        first = own_in[0, k] if k < 2 else own_down[0]
        second = other_in[0, k] if k < 2 else other_down[0]
        out[:units] = first
        out[units:hole] = jnp.zeros((hole - units, columns), jnp.bfloat16)
        out[hole : hole + units] = second
        out[hole + units : 2 * hole] = jnp.zeros((hole - units, columns), jnp.bfloat16)
        out[2 * hole :] = jnp.zeros((TILE, columns), jnp.bfloat16)
        for b in range(columns // size):
            part = slice(b * size, (b + 1) * size)
            for at, ref in ((2 * hole, near), (2 * hole + stride, far)):
                out[at : at + shared, part] = ref[b, k * stride : k * stride + shared]


def pack_units(own_in, other_in, own_down, other_down, near, far, shared, others):
    units, depth = own_down.shape[1:]
    size = near.shape[2]
    height = 2 * (-(-units // TILE) * TILE) + TILE
    columns = 2 * size
    in_spec = pl.BlockSpec((1, 2, units, columns), lambda i: (0, 0, 0, i))
    down_spec = pl.BlockSpec((1, units, columns), lambda i: (0, 0, i))
    narrow = pl.BlockSpec((2,) + near.shape[1:], lambda i: (i, 0, 0))
    return pl.pallas_call(
        functools.partial(pack_units_kernel, units, shared),
        grid=(depth // columns,),
        in_specs=[in_spec, in_spec, down_spec, down_spec, narrow, narrow]
        + in_place(len(others)),
        out_specs=[pl.BlockSpec((height, columns), lambda i: (0, i))] * 3,
        out_shape=[jax.ShapeDtypeStruct((height, depth), jnp.bfloat16)] * 3,
        compiler_params=pltpu.CompilerParams(vmem_limit_bytes=32 * 1024 * 1024),
        cost_estimate=pl.CostEstimate(
            flops=0, bytes_accessed=12 * height * depth, transcendentals=0
        ),
    )(own_in, other_in, own_down, other_down, near, far, *others)


def expert_grads_kernel(units, count, extra, right_ref, *refs):
    out = refs[-1]
    for k in range(count):

        @pl.when(pl.program_id(0) == k)
        def _():
            result = dot_rows(refs[k][...], right_ref[...])[:units]
            if extra:
                result += refs[count][0, 0].astype(jnp.float32)
            out[0, 0] = result.astype(out.dtype)


def expert_grads(lefts, right, units, column, arrived, kind, others=()):
    total, depth = right.shape
    wide = -(-units // TILE) * TILE
    extra = [] if arrived is None else [arrived]
    out = pl.BlockSpec((1, 1, units, 2 * TILE), lambda k, i: (0, k, 0, i))
    side = pl.BlockSpec((total, wide), lambda k, i: (0, column))
    return pl.pallas_call(
        functools.partial(expert_grads_kernel, units, len(lefts), len(extra)),
        grid=(len(lefts), depth // (2 * TILE)),
        in_specs=[pl.BlockSpec((total, 2 * TILE), lambda k, i: (0, i))]
        + [side] * len(lefts)
        + [out] * len(extra)
        + in_place(len(others)),
        out_specs=out,
        out_shape=jax.ShapeDtypeStruct((1, len(lefts), units, depth), kind),
        compiler_params=pltpu.CompilerParams(vmem_limit_bytes=48 * 1024 * 1024),
        cost_estimate=pl.CostEstimate(
            flops=2 * len(lefts) * total * depth * wide,
            bytes_accessed=2 * len(lefts) * total * (depth + wide) + 8 * depth * units,
            transcendentals=0,
        ),
    )(right, *lefts, *extra, *others)


def side_grads_kernel(shared, rows_ref, cots_ref, gate_ref, up_ref, hidden_ref, logit_ref, *outs):
    kept_ref, sent_ref, router_ref = outs
    stride = shared_stride(shared)
    size = kept_ref.shape[2]
    for k, (left, right) in enumerate(
        ((gate_ref, rows_ref), (up_ref, rows_ref), (hidden_ref, cots_ref))
    ):
        result = dot_rows(left[...], right[...])
        for b in range(kept_ref.shape[0]):
            part = slice(b * size, (b + 1) * size)
            kept_ref[b, k * stride : (k + 1) * stride] = result[:stride, part]
            sent_ref[b, k * stride : (k + 1) * stride] = result[
                stride : 2 * stride, part
            ].astype(jnp.bfloat16)
    router_ref[...] = dot_rows(logit_ref[...], rows_ref[...])


def side_grads(rows, cots, gate, up, hidden, logits, shared, blocks, others):
    total, depth = rows.shape
    column = gate.shape[1] // TILE - 1
    size = depth // blocks
    stride = shared_stride(shared)
    wide = pl.BlockSpec((total, 2 * TILE), lambda i: (0, i))
    side = pl.BlockSpec((total, TILE), lambda i: (0, column))
    packed = pl.BlockSpec((2 * TILE // size, 3 * stride, size), lambda i: (i, 0, 0))
    return pl.pallas_call(
        lambda *refs: side_grads_kernel(shared, *refs[:6], *refs[6 + len(others) :]),
        grid=(depth // (2 * TILE),),
        in_specs=[wide, wide, side, side, side, whole(logits)] + in_place(len(others)),
        out_specs=[packed, packed, pl.BlockSpec((logits.shape[1], 2 * TILE), lambda i: (0, i))],
        out_shape=[
            jax.ShapeDtypeStruct((blocks, 3 * stride, size), jnp.float32),
            jax.ShapeDtypeStruct((blocks, 3 * stride, size), jnp.bfloat16),
            jax.ShapeDtypeStruct((logits.shape[1], depth), jnp.float32),
        ],
        compiler_params=pltpu.CompilerParams(vmem_limit_bytes=48 * 1024 * 1024),
        cost_estimate=pl.CostEstimate(
            flops=8 * total * depth * TILE,
            bytes_accessed=4 * total * depth,
            transcendentals=0,
        ),
    )(rows, cots, gate, up, hidden, logits, *others)


def down_kernel(starts, *refs):
    count = len(starts)
    pieces, weight_ref = refs[:count], refs[count]
    grads_ref, rows_ref, semaphores = refs[-3:]

    @pl.when(pl.program_id(0) == 0)
    def _():
        load_pieces(pieces, starts, rows_ref, semaphores)

    size = rows_ref.shape[0] // 2
    for k in range(2):
        part = slice(k * size, (k + 1) * size)
        grads_ref[part, :] = dot_turned(rows_ref[part, :], weight_ref[...]).astype(jnp.bfloat16)


def down_grads(part, pieces, size, down, kept, others):
    count = len(pieces)
    depth = down.shape[1]
    width = down.shape[0]
    rows = count * size
    return pl.pallas_call(
        functools.partial(down_kernel, tuple(start for _, start in pieces)),
        grid=(width // TILE,),
        in_specs=in_place(count)
        + [pl.BlockSpec((TILE, depth), lambda i: (i, 0))]
        + in_place(len(kept) + len(others)),
        out_specs=[
            pl.BlockSpec((rows, TILE), lambda i: (part, i)),
            pl.BlockSpec((rows, depth), lambda i: (part, 0)),
        ],
        out_shape=[
            jax.ShapeDtypeStruct((2 * rows, width), jnp.bfloat16),
            jax.ShapeDtypeStruct((2 * rows, depth), jnp.bfloat16),
        ],
        scratch_shapes=[pltpu.SemaphoreType.DMA((count,))],
        input_output_aliases={count + 1 + k: k for k in range(len(kept))},
        compiler_params=pltpu.CompilerParams(vmem_limit_bytes=48 * 1024 * 1024),
        cost_estimate=pl.CostEstimate(
            flops=2 * rows * depth * width,
            bytes_accessed=2 * (2 * rows * depth + depth * width + rows * width),
            transcendentals=0,
        ),
    )(*[array for array, _ in pieces], down, *kept, *others)


def out_kernel(pieces, hidden_ref, weight_ref, *refs):
    outs, done_ref = refs[-1 - pieces : -1], refs[-1]
    size = hidden_ref.shape[0] // (RINGS * pieces)
    done_ref[...] = jnp.zeros_like(done_ref)
    for r in range(RINGS):
        part = hidden_ref[r * pieces * size : (r + 1) * pieces * size, :]
        result = wide_dot(part, weight_ref[...]).astype(jnp.bfloat16)
        for k in range(pieces):
            outs[k][r * size : (r + 1) * size, :] = result[k * size : (k + 1) * size]


def out_rows(pieces, half, hidden, down, kept, others):
    rows, width = hidden.shape
    depth = down.shape[1]
    steps = depth // (2 * TILE)
    results = pl.pallas_call(
        functools.partial(out_kernel, pieces),
        grid=(steps,),
        in_specs=[whole(hidden), pl.BlockSpec((width, TILE), lambda i: (0, half * steps + i))]
        + in_place(len(kept) + len(others)),
        out_specs=[pl.BlockSpec((rows // pieces, TILE), lambda i: (0, half * steps + i))] * pieces
        + [pl.BlockSpec((8, 128), lambda i: (0, 0))],
        out_shape=[jax.ShapeDtypeStruct((rows // pieces, depth), jnp.bfloat16)] * pieces
        + [jax.ShapeDtypeStruct((8, 128), jnp.float32)],
        input_output_aliases={2 + k: k for k in range(len(kept))},
        compiler_params=pltpu.CompilerParams(vmem_limit_bytes=48 * 1024 * 1024),
        cost_estimate=pl.CostEstimate(
            flops=rows * depth * width,
            bytes_accessed=rows * depth + depth * width + 2 * rows * width,
            transcendentals=0,
        ),
    )(hidden, down, *kept, *others)
    return results[:-1], results[-1]


def mlp_kernel(tiles, starts, others, experts_ref, routed_ref, *refs):
    pieces = len(starts)
    row_refs = refs[:pieces]
    router_ref, gate_col, up_col, down_grad, gate_row, up_row = refs[pieces : pieces + 6]
    outs = refs[pieces + 6 + others :]
    grad_refs = outs[:pieces]
    rows_out, hidden_out, gate_out, up_out, logit_out = outs[pieces : pieces + 5]
    gate_all, up_all, prob_ref, scale_ref, sum_ref, semaphores = outs[pieces + 5 :]
    step = pl.program_id(0)
    third = tiles // 2
    total = rows_out.shape[0]
    size = total // pieces
    lane = lax.broadcasted_iota(jnp.int32, (1, router_ref.shape[1]), 1) - experts_ref[3]

    @pl.when(step == 0)
    def _():
        load_pieces(row_refs, starts, rows_out, semaphores)
        logits = wide_dot(rows_out[...], router_ref[...])
        logits = jnp.where((lane >= 0) & (lane < experts_ref[2]), logits, -1e30)
        raised = jnp.exp(logits - jnp.max(logits, axis=1, keepdims=True))
        chances = raised / jnp.sum(raised, axis=1, keepdims=True)
        prob_ref[...] = chances
        for k in (0, 1):
            chance = jnp.sum(jnp.where(lane == experts_ref[k], chances, 0.0), axis=1, keepdims=True)
            scale_ref[k] = routed_ref[:, k : k + 1] * chance
        scale_ref[2] = jnp.ones_like(scale_ref[2])
        sum_ref[...] = jnp.zeros_like(sum_ref)

    @pl.when(step < tiles)
    def _():
        columns = pl.ds(pl.multiple_of(step * TILE, TILE), TILE)
        kind = step // third
        half = total // 2
        for k in (0, 1):
            part = slice(k * half, (k + 1) * half)
            pre_gate = dot_turned(rows_out[part, :], gate_col[...])
            pre_up = dot_turned(rows_out[part, :], up_col[...])
            grads = down_grad[part, :].astype(jnp.float32)
            scale = scale_ref[kind, part, :]
            sigmoid = 1.0 / (1.0 + jnp.exp(-pre_gate))
            silu = pre_gate * sigmoid
            hidden = (silu * pre_up).astype(jnp.bfloat16).astype(jnp.float32)
            sum_ref[kind, part, :] += jnp.sum(hidden * grads, axis=1, keepdims=True)
            grad_hidden = scale * grads
            low_gate = (grad_hidden * pre_up * (sigmoid + silu * (1.0 - sigmoid))).astype(
                jnp.bfloat16
            )
            low_up = (grad_hidden * silu).astype(jnp.bfloat16)
            gate_all[part, columns] = low_gate
            up_all[part, columns] = low_up
            hidden_out[part, :] = (scale * hidden).astype(jnp.bfloat16)
            gate_out[part, :] = low_gate
            up_out[part, :] = low_up

    @pl.when(step == tiles - 1)
    def _():
        grad_logits = jnp.zeros_like(prob_ref)
        for k in (0, 1):
            own = jnp.where(lane == experts_ref[k], 1.0, 0.0)
            grad_logits += scale_ref[k] * sum_ref[k] * (own - prob_ref[...])
        logit_out[...] = grad_logits.astype(jnp.bfloat16)

    @pl.when(step >= tiles)
    def _():
        some = pl.ds(pl.multiple_of((step - tiles) * 2 * TILE, TILE), 2 * TILE)
        grads = wide_dot(gate_all[...], gate_row[...]) + wide_dot(up_all[...], up_row[...])
        grads += dot_turned(logit_out[...], router_ref[some, :])
        grads = grads.astype(jnp.bfloat16)
        for k in range(pieces):
            grad_refs[k][...] = grads[k * size : (k + 1) * size]


def mlp_plane(distance, experts, routed, rows, down_grad, router, weights, kept, others):
    gate, up = weights
    pieces = len(rows)
    width, depth = gate.shape
    size = routed.shape[0] // pieces
    tiles, columns = width // TILE, depth // (2 * TILE)
    total = pieces * size
    low = jnp.bfloat16

    def early(i):
        return jnp.minimum(i, tiles - 1)

    def late(i):
        return jnp.maximum(i - tiles, 0)

    tile_spec = pl.BlockSpec((total, TILE), lambda i: (distance, early(i)))
    anywhere = pl.BlockSpec(memory_space=pl.ANY)
    first_kept = 2 + pieces + 6
    results = pl.pallas_call(
        functools.partial(
            mlp_kernel, tiles, tuple(start for _, start in rows), len(kept) + len(others)
        ),
        grid=(tiles + columns,),
        in_specs=[pl.BlockSpec(memory_space=pltpu.SMEM), whole(routed)]
        + [anywhere] * pieces
        + [
            pl.BlockSpec((depth, 128), lambda i: (0, router.shape[1] // 128 - 1)),
            pl.BlockSpec((TILE, depth), lambda i: (early(i), 0)),
            pl.BlockSpec((TILE, depth), lambda i: (early(i), 0)),
            tile_spec,
            pl.BlockSpec((width, 2 * TILE), lambda i: (0, late(i))),
            pl.BlockSpec((width, 2 * TILE), lambda i: (0, late(i))),
        ]
        + [anywhere] * (len(kept) + len(others)),
        out_specs=[pl.BlockSpec((size, 2 * TILE), lambda i: (0, late(i)))] * pieces
        + [
            pl.BlockSpec((total, depth), lambda i: (distance, 0)),
            tile_spec,
            tile_spec,
            tile_spec,
            pl.BlockSpec((total, 128), lambda i: (distance, 0)),
        ],
        out_shape=[jax.ShapeDtypeStruct((size, depth), low)] * pieces
        + [
            jax.ShapeDtypeStruct((RINGS * total, many), low)
            for many in (depth, width, width, width, 128)
        ],
        scratch_shapes=[pltpu.VMEM((total, width), low)] * 2
        + [
            pltpu.VMEM((total, 128), jnp.float32),
            pltpu.VMEM((3, total, 1), jnp.float32),
            pltpu.VMEM((3, total, 1), jnp.float32),
            pltpu.SemaphoreType.DMA((pieces,)),
        ],
        input_output_aliases={first_kept + k: pieces + k for k in range(len(kept))},
        compiler_params=pltpu.CompilerParams(vmem_limit_bytes=48 * 1024 * 1024),
        cost_estimate=pl.CostEstimate(
            flops=2 * total * depth * width * 4,
            bytes_accessed=2 * (4 * depth * width + 3 * total * depth + 4 * total * width),
            transcendentals=total * width,
        ),
    )(experts, routed, *[array for array, _ in rows], router, gate, up, down_grad, gate, up, *kept, *others)
    return results[:pieces], results[pieces:]


def gather_body(
    block_input,
    segments,
    counts,
    routes,
    attn_gain,
    w_query,
    w_latent,
    latent_gain,
    w_keyval,
    w_output,
    ffn_gain,
    w_router,
    shared_gate_up,
    shared_down,
    expert_gate_up,
    expert_down,
    cotangent,
):
    f32 = jnp.float32
    bf16 = jnp.bfloat16
    blocks = 16
    index = lax.axis_index("dp")
    x = lax.axis_index("tensor")
    coords = jnp.stack([index // 4, (index // 2) % 2, index % 2]).astype(jnp.int32)
    core = coords[2]
    place = jnp.concatenate([coords, x.astype(jnp.int32)[None], counts])
    local_rows = block_input.shape[0]
    tokens = 2 * local_rows
    depth = w_query.shape[0]
    query_width = w_query.shape[1]
    heads = query_width // (NOPE + ROPE)
    experts = w_router.shape[1]
    units = expert_gate_up.shape[3]
    shared = shared_gate_up.shape[2] // blocks
    latent_depth = w_keyval.shape[0]

    used = query_width + KVR + ROPE
    small = jnp.concatenate(
        [
            attn_gain[:, None],
            ffn_gain[:, None],
            jnp.pad(latent_gain, (0, depth - latent_depth))[:, None],
            w_router,
            routes.reshape(depth, -1).astype(bf16),
            jnp.zeros((depth, 128 - ROPE - 3 - experts - 2 * TOP), bf16),
        ],
        axis=1,
    )
    first_width = query_width + KVR + 128
    shards = pack_weights(w_query, w_latent, small, w_keyval, w_output)
    other_input = other_x(block_input)
    expert_in = expert_gate_up.swapaxes(2, 3)
    expert_in_other = other_core(expert_in)
    expert_down_other = other_core(expert_down)
    chunks, held, besides = gather_weight(
        shards, (expert_in_other, expert_down_other, other_input)
    )
    shared_near = lax.all_to_all(
        pack_shared(shared_gate_up, shared_down, blocks, (held[3],)),
        "dp",
        split_axis=0,
        concat_axis=0,
        tiled=True,
    )
    shared_far = other_core(shared_near)

    grad_groups, grad_ring, grad_across = gather_whole(
        after(cotangent, held[3], besides[2]), besides[3]
    )

    cosine, sine = rotary_tables(segments[0], ROPE)
    cosine = jnp.tile(cosine, (1, heads))
    sine = jnp.tile(sine, (1, heads))
    sizes = (depth, query_width, used, latent_depth, w_keyval.shape[1] * latent_depth // depth, first_width)
    (
        own_part,
        sent_part,
        first_weight,
        keyval_weight,
        output_turned,
        first_normed,
        nope,
        turned_query,
        latent,
        key,
        keyval,
        total,
        attended,
        gains,
        latent_gain_row,
    ) = attend_forward(
        place,
        segments,
        cosine,
        sine,
        block_input,
        other_input,
        chunks,
        heads,
        sizes,
        (grad_ring[2], grad_across[0], grad_across[1]),
    )
    attn_gain_wide, ffn_gain_wide = gains[0], gains[1]
    mixed = block_input.astype(f32) + own_part + other_x(sent_part).astype(f32)
    second_scale = rms_scale(mixed)
    second_unit = mixed * second_scale
    second_normed = (second_unit * ffn_gain_wide).astype(bf16)

    routes_at = used + 3 + experts
    routes_all = first_weight[:, routes_at : routes_at + 2 * TOP].reshape(blocks * tokens, TOP)
    chip_experts = jnp.stack([index, index + 1 - 2 * core]).astype(jnp.int32)
    routed_all = jnp.any(
        routes_all[None] == chip_experts[:, None, None].astype(bf16), axis=2
    ).astype(f32)
    order = jnp.stack(
        [
            place_of(coords, (distance, flip_y, 0)) * 2 + (1 - x if flip_x else x)
            for distance in range(RINGS)
            for flip_x, flip_y in ((0, 0), (0, 1), (1, 0), (1, 1))
        ]
    )
    routed = jnp.stack(
        [
            pick_blocks(one.reshape(blocks * 2, local_rows), order).reshape(RINGS, -1)
            for one in routed_all
        ],
        axis=2,
    )

    corners = "yxyx"
    row_ring, row_groups = gather_rows(second_normed, "yyx")
    row_planes = [
        [(array, 0) for array in row_groups[0]],
        [(array, 0) for array in row_groups[1]],
        [(array, 0) for array in row_groups[2]],
        [(array, local_rows) for array in row_groups[2]],
    ]

    gate_weight, up_weight, down_weight = pack_units(
        expert_in,
        expert_in_other,
        expert_down,
        expert_down_other,
        shared_near,
        shared_far,
        shared,
        (second_normed,),
    )
    half_kept = down_grads(
        0,
        [(array, r * local_rows) for r in (0, 1) for array in grad_groups[0]],
        local_rows,
        down_weight,
        (),
        (row_ring[1],),
    )
    down_grad, every_grad = down_grads(
        1,
        [(array, r * local_rows) for r in (0, 1) for array in grad_groups[1]],
        local_rows,
        down_weight,
        half_kept,
        (row_ring[2],),
    )
    expert_ids = jnp.concatenate(
        [chip_experts, jnp.array([experts, used + 3 - query_width - KVR], jnp.int32)]
    )
    kept = []
    planes = []
    turned, closed = [None] * RINGS, [None] * RINGS
    for distance in range(RINGS):
        others = [row_ring[3]] if distance == 0 else []
        if distance == 1:
            others = list(row_groups[2][1:3])
        elif distance == 3:
            others = list(turned[0][1:])
        grads, kept = mlp_plane(
            distance,
            expert_ids,
            routed[distance],
            row_planes[distance],
            down_grad,
            first_weight,
            (gate_weight, up_weight),
            kept,
            others,
        )
        planes.append(list(grads))
        if distance:
            before = planes[distance - 1]
            k = 1 if corners[distance - 1] == "x" else 2
            before[k] = after(before[k], grads[3])
            turned[distance - 1] = turn_corner(before, corners[distance - 1])
            closed[distance - 1] = close_plane(turned[distance - 1])
    turned[3] = turn_corner(planes[3], corners[3])
    first_part = closed[1]
    closed[1] = (after(first_part[0], planes[3][3]),) + tuple(first_part[1:])
    every_row, every_hidden, every_gate_grad, every_up_grad, logit_grads = kept
    first_total = wide_sum(*closed[1]).astype(bf16)
    shared_kept, shared_sent, logit_rows = side_grads(
        every_row,
        every_grad,
        every_gate_grad,
        every_up_grad,
        every_hidden,
        logit_grads,
        shared,
        blocks,
        (first_total,),
    )
    sent_down = expert_grads((every_hidden,), every_grad, units, 1, None, bf16, (shared_sent,))
    half_outs, half_done = out_rows(4, 0, every_hidden, down_weight, (), (sent_down,))
    moving = ring_step(first_total)
    moving = ring_step(wide_sum(moving, *closed[2]).astype(bf16))
    own, beside, across = turned[3]
    own = after(own, sent_down)
    grad_close = close_plane((own, after(beside, shared_sent), across))
    grad_second = wide_sum(
        ring_step(wide_sum(moving, *grad_close).astype(bf16)),
        after(closed[0][0], half_done),
        *closed[0][1:],
    )

    arrived_down = other_core(sent_down)
    router_at = used + 3 - query_width - KVR
    grad_router = logit_rows[router_at : router_at + experts]
    shared_came = other_core(shared_sent)

    gain_ffn_part = jnp.sum(grad_second * second_unit, axis=0)
    grad_mixed = cotangent.astype(f32) + rms_back(
        grad_second * ffn_gain_wide, second_unit, second_scale
    )
    grad_mixed_low = grad_mixed.astype(bf16)
    other_grad = other_x(grad_mixed_low)
    outs, outs_done = out_rows(4, 1, every_hidden, down_weight, half_outs, (grad_mixed_low,))
    outs = list(outs)
    outs[2] = after(outs[2], other_grad)
    outs[3] = after(outs[3], other_grad)


    places = jnp.stack([place_of(coords, key_of) for key_of in weight_keys()]).astype(jnp.int32)
    projected_grad, keyval_grad, latent_normed, gain_latent_part = attend_back(
        place,
        segments,
        cosine,
        sine,
        grad_mixed_low,
        other_grad,
        (keyval_weight, output_turned, nope, turned_query, latent, key, keyval, total, latent_gain_row),
        heads,
        first_width,
        (arrived_down, shared_came, outs_done),
    )
    grad_attn = jnp.concatenate(
        [
            jnp.where(x == 0, grad_mixed_low, other_grad),
            jnp.where(x == 0, other_grad, grad_mixed_low),
        ],
        axis=0,
    )
    ring_places = places.reshape(2, 2, RINGS).swapaxes(1, 2).reshape(-1)
    other_parts = (latent_normed, keyval_grad, grad_attn, attended, ring_places)
    own_first, sent_first, gain_attn_part = first_back(
        place, block_input, other_input, projected_grad, first_weight
    )
    grad_first = own_first + other_x(sent_first).astype(f32)
    small_rows = jnp.concatenate(
        [
            jnp.zeros((ROPE, D), f32),
            gain_attn_part,
            gain_ffn_part[None],
            jnp.pad(
                gain_latent_part.reshape(blocks, latent_depth),
                ((0, 0), (0, depth - latent_depth)),
            ).reshape(1, D),
            grad_router,
            jnp.zeros((128 - ROPE - 3 - experts, D), f32),
        ],
        axis=0,
    )
    first_parts = (first_normed, projected_grad, small_rows, places)
    first_sent = first_grads(*first_parts, 8, 8, None)
    first_arrived = other_core(first_sent)
    other_arrived = other_core(other_grads(*other_parts, 8, 8, None, (first_sent,)))
    far = first_grads(*first_parts, 4, 4, first_arrived)
    other_kept = other_grads(*other_parts, 0, 8, other_arrived, (far,))
    shared_grads = lax.all_to_all(
        add_low(after(shared_kept, far), shared_came), "dp", split_axis=0, concat_axis=0, tiled=True
    )
    from_y = other_y(far)
    arrived_in = other_core(
        expert_grads((every_gate_grad, every_up_grad), every_row, units, 1, None, bf16, (far,))
    )
    outs[1] = after(outs[1], from_y)
    out_total = wide_sum(*close_plane(turn_corner(outs, "x")))
    block_output = mixed + ring_sum(
        [out_total[r * local_rows : (r + 1) * local_rows] for r in range(RINGS)], bf16
    )
    near = first_grads(*first_parts, 0, 4, first_arrived)
    other_summed = ring_sum(
        [other_kept[2 * r * depth : 2 * (r + 1) * depth] for r in range(RINGS)], bf16
    )
    grad_expert_down = expert_grads(
        (every_hidden,), every_grad, units, 0, arrived_down, f32, (from_y,)
    )
    first_closed = close_ring(near, from_y)
    grad_expert_in = expert_grads(
        (every_gate_grad, every_up_grad), every_row, units, 0, arrived_in, f32, (near,)
    )
    other_closed = after(other_summed[:depth], grad_expert_in) + other_y(
        other_summed[depth:].astype(bf16)
    ).astype(f32)
    grad_shared_in, grad_shared_down = unpack_shared(shared_grads, shared, (from_y,))
    grad_expert_gate_up = grad_expert_in.swapaxes(2, 3)
    grad_expert_down = grad_expert_down[0]
    nope_width = heads * NOPE
    span = heads * (ROPE // 2)
    grad_query_weight = jnp.concatenate(
        [
            first_closed[:, :nope_width].reshape(depth, heads, NOPE),
            first_closed[:, nope_width : nope_width + span].reshape(depth, heads, -1),
            first_closed[:, nope_width + span : query_width].reshape(depth, heads, -1),
        ],
        axis=2,
    ).reshape(depth, query_width)
    both = first_closed[:, query_width:]
    both = both + other_x(both)
    grad_latent_weight = both[:, : KVR + ROPE]
    small_grads = both[:, KVR + ROPE :].T
    keyval_columns = w_keyval.shape[1] * latent_depth // depth
    grad_keyval_weight = (
        other_closed[:, :keyval_columns]
        .reshape(-1, latent_depth, keyval_columns)
        .transpose(1, 0, 2)
        .reshape(latent_depth, -1)
    )
    grad_output_weight = other_closed[:, keyval_columns:].T
    own_inputs = block_input.astype(f32)
    own_scale = rms_scale(own_inputs)
    own_unit = own_inputs * own_scale
    grad_input = grad_mixed + rms_back(grad_first * attn_gain_wide, own_unit, own_scale)
    return (
        block_output,
        grad_input,
        small_grads[0],
        grad_query_weight,
        grad_latent_weight,
        small_grads[2, :latent_depth],
        grad_keyval_weight,
        grad_output_weight,
        small_grads[1],
        small_grads[3 : 3 + experts].T,
        grad_shared_in,
        grad_shared_down,
        grad_expert_gate_up,
        grad_expert_down,
    )


def solution(mesh):
    in_specs = (
        P(("dp", "tensor"), None),
        P("dp", None),
        P("dp"),
        P("dp", None),
        P("dp"),
        P("dp", "tensor"),
        P("dp", None),
        P("dp"),
        P("dp", "tensor"),
        P("tensor", "dp"),
        P("dp"),
        P("dp", None),
        P(None, "dp", "tensor"),
        P("tensor", "dp"),
        P("dp", None, None, "tensor"),
        P("dp", "tensor", None),
        P(("dp", "tensor"), None),
    )
    out_specs = (
        P(("dp", "tensor"), None),
        P(("dp", "tensor"), None),
        P("dp"),
        P("dp", "tensor"),
        P("dp", None),
        P("dp"),
        P("dp", "tensor"),
        P("tensor", "dp"),
        P("dp"),
        P("dp", None),
        P(None, "dp", "tensor"),
        P("tensor", "dp"),
        P("dp", None, None, "tensor"),
        P("dp", "tensor", None),
    )
    body = gather_body if mesh.shape["dp"] == 16 else exchange_body
    return jax.shard_map(body, mesh=mesh, in_specs=in_specs, out_specs=out_specs, check_vma=False)
```

```python
import functools
import math

import jax
import jax.numpy as jnp
from jax import lax
from jax.experimental import pallas as pl
from jax.experimental.pallas import tpu as pltpu
from jax.sharding import PartitionSpec as P

D = 2048
NOPE = 128
ROPE = 64
VD = 128
KVR = 512
TOP = 6


EPSILON = 1e-06


def rms_scale(values):
    return lax.rsqrt(jnp.mean(values * values, axis=-1, keepdims=True) + EPSILON)


def rms_back(grad_unit, unit_rows, row_scale):
    return row_scale * (
        grad_unit - unit_rows * jnp.mean(grad_unit * unit_rows, axis=-1, keepdims=True)
    )


def rotary_tables(segment_row, width):
    count = segment_row.shape[0]
    position = jnp.arange(count, dtype=jnp.int32)
    same = segment_row[:, None] == segment_row[None, :]
    start = jnp.min(jnp.where(same, position[None, :], count), axis=1)
    offset = (position - start).astype(jnp.float32)
    freq = jnp.exp(jnp.arange(width // 2, dtype=jnp.float32) * (-2.0 * math.log(10000.0) / width))
    angle = offset[:, None] * freq[None, :]
    return (jnp.cos(angle), jnp.sin(angle))


def rotate(values, cosine, sine):
    half = values.shape[-1] // 2
    first = values[..., :half]
    second = values[..., half:]
    return jnp.concatenate(
        [first * cosine - second * sine, second * cosine + first * sine], axis=-1
    )


def rotate_back(grads, cosine, sine):
    half = grads.shape[-1] // 2
    first = grads[..., :half]
    second = grads[..., half:]
    return jnp.concatenate(
        [first * cosine + second * sine, second * cosine - first * sine], axis=-1
    )


def allowed_pairs(segment_row, count):
    position = jnp.arange(segment_row.shape[0], dtype=jnp.int32)
    live = position < count
    same = segment_row[:, None] == segment_row[None, :]
    causal = position[None, :] <= position[:, None]
    return same & causal & live[:, None] & live[None, :] | (position[:, None] == position[None, :])


def attention_scores(query_rows, key_nope, key_rope, allowed, scale):
    scores = jnp.einsum(
        "ihd,jhd->hij", query_rows[..., :NOPE], key_nope, preferred_element_type=jnp.float32
    )
    scores = scores + jnp.einsum(
        "ihd,jd->hij", query_rows[..., NOPE:], key_rope, preferred_element_type=jnp.float32
    )
    return jnp.where(allowed[None], scores * scale, -1e30)


def swiglu_back(gate, upper, grad_hidden, axis):
    sigmoid = jax.nn.sigmoid(gate)
    grad_gate = grad_hidden * upper * sigmoid * (1.0 + gate * (1.0 - sigmoid))
    grad_upper = grad_hidden * gate * sigmoid
    return jnp.stack([grad_gate, grad_upper], axis=axis)


def slot_layout(routes, experts, capacity):
    tokens = routes.shape[0]
    flat = routes.reshape(-1)
    onehot = (flat[:, None] == jnp.arange(experts, dtype=jnp.int32)[None, :]).astype(jnp.int32)
    rank = jnp.arange(flat.shape[0], dtype=jnp.int32)
    earlier = (rank[None, :] < rank[:, None]).astype(jnp.bfloat16)
    before = jnp.dot(
        earlier, onehot.astype(jnp.bfloat16), preferred_element_type=jnp.float32
    ).astype(jnp.int32)
    slot_index = jnp.sum(before * onehot, axis=1)
    target = flat * capacity + slot_index
    token_ids = jnp.arange(flat.shape[0], dtype=jnp.int32) // routes.shape[1]
    owner = jnp.full((experts * capacity,), tokens, jnp.int32).at[target].set(token_ids)
    return (slot_index, target, owner)


def to_expert_major(arrived, groups, local_experts):
    capacity = arrived.shape[1]
    width = arrived.shape[2]
    return (
        arrived.reshape(groups, local_experts, capacity, width)
        .transpose(1, 0, 2, 3)
        .reshape(local_experts, groups * capacity, width)
    )


def from_expert_major(results, groups):
    local_experts = results.shape[0]
    width = results.shape[2]
    capacity = results.shape[1] // groups
    return (
        results.reshape(local_experts, groups, capacity, width)
        .transpose(1, 0, 2, 3)
        .reshape(groups * local_experts, capacity, width)
    )


def exchange_body(
    block_input,
    segments,
    counts,
    routes,
    attn_gain,
    w_query,
    w_latent,
    latent_gain,
    w_keyval,
    w_output,
    ffn_gain,
    w_router,
    shared_gate_up,
    shared_down,
    expert_gate_up,
    expert_down,
    cotangent,
):
    gathered = (
        lax.all_gather(attn_gain, "dp", axis=0, tiled=True),
        lax.all_gather(w_query, "dp", axis=0, tiled=True),
        lax.all_gather(w_latent, "dp", axis=0, tiled=True),
        lax.all_gather(latent_gain, "dp", axis=0, tiled=True),
        lax.all_gather(w_keyval, "dp", axis=0, tiled=True),
        lax.all_gather(w_output, "dp", axis=1, tiled=True),
        lax.all_gather(ffn_gain, "dp", axis=0, tiled=True),
        lax.all_gather(w_router, "dp", axis=0, tiled=True),
        lax.all_gather(shared_gate_up, "dp", axis=1, tiled=True),
        lax.all_gather(shared_down, "dp", axis=1, tiled=True),
    )
    (
        full_attn_gain,
        query_weight,
        latent_weight,
        full_latent_gain,
        keyval_weight,
        output_weight,
        full_ffn_gain,
        router_weight,
        shared_in,
        shared_out,
    ) = gathered
    tensor_rank = lax.axis_index("tensor")
    dp_size = lax.axis_size("dp")
    rows_all = lax.all_gather(block_input, "tensor", axis=0, tiled=True)
    tokens = rows_all.shape[0]
    local_rows = block_input.shape[0]
    heads = query_weight.shape[1] // (NOPE + ROPE)
    experts = router_weight.shape[1]
    local_experts = expert_gate_up.shape[0]
    capacity = 2 * tokens * TOP // experts
    scale = (NOPE + ROPE) ** (-0.5)
    start = tensor_rank * local_rows
    cosine, sine = rotary_tables(segments[0], ROPE)
    allowed = allowed_pairs(segments[0], counts[0])
    attn_gain_wide = full_attn_gain.astype(jnp.float32)
    latent_gain_wide = full_latent_gain.astype(jnp.float32)
    ffn_gain_wide = full_ffn_gain.astype(jnp.float32)
    inputs = rows_all.astype(jnp.float32)
    first_scale = rms_scale(inputs)
    first_unit = inputs * first_scale
    first_normed = (first_unit * attn_gain_wide).astype(jnp.bfloat16)
    query = jnp.dot(first_normed, query_weight, preferred_element_type=jnp.float32).reshape(
        tokens, heads, NOPE + ROPE
    )
    query_rows = jnp.concatenate(
        [query[..., :NOPE], rotate(query[..., NOPE:], cosine[:, None, :], sine[:, None, :])],
        axis=-1,
    ).astype(jnp.bfloat16)
    latent_all = jnp.dot(first_normed, latent_weight, preferred_element_type=jnp.float32)
    latent = latent_all[:, :KVR]
    key_rope = rotate(latent_all[:, KVR:], cosine, sine).astype(jnp.bfloat16)
    latent_scale = rms_scale(latent)
    latent_unit = latent * latent_scale
    latent_normed = (latent_unit * latent_gain_wide).astype(jnp.bfloat16)
    keyval = (
        jnp.dot(latent_normed, keyval_weight, preferred_element_type=jnp.float32)
        .astype(jnp.bfloat16)
        .reshape(tokens, heads, NOPE + VD)
    )
    key_nope = keyval[..., :NOPE]
    values = keyval[..., NOPE:]
    scores = attention_scores(query_rows, key_nope, key_rope, allowed, scale)
    row_max = jnp.max(scores, axis=-1, keepdims=True)
    log_total = row_max + jnp.log(jnp.sum(jnp.exp(scores - row_max), axis=-1, keepdims=True))
    weights_low = jnp.exp(scores - log_total).astype(jnp.bfloat16)
    attended = (
        jnp.einsum("hij,jhd->ihd", weights_low, values, preferred_element_type=jnp.float32)
        .astype(jnp.bfloat16)
        .reshape(tokens, heads * VD)
    )
    attn_part = jnp.dot(attended, output_weight, preferred_element_type=jnp.float32)
    mixed = inputs + lax.psum(attn_part, "tensor")
    second_scale = rms_scale(mixed)
    second_unit = mixed * second_scale
    second_normed = (second_unit * ffn_gain_wide).astype(jnp.bfloat16)
    logits = jnp.dot(second_normed, router_weight, preferred_element_type=jnp.float32)
    probabilities = jax.nn.softmax(logits, axis=-1)
    gate_values = jnp.take_along_axis(probabilities, routes, axis=1)
    shared_pre = jnp.einsum(
        "td,gdf->tgf", second_normed, shared_in, preferred_element_type=jnp.float32
    )
    shared_hidden = (jax.nn.silu(shared_pre[:, 0]) * shared_pre[:, 1]).astype(jnp.bfloat16)
    shared_part = jnp.dot(shared_hidden, shared_out, preferred_element_type=jnp.float32)
    slot_index, target, owner = slot_layout(routes, experts, capacity)
    owner_grid = owner.reshape(experts, capacity)
    padded_rows = jnp.concatenate([second_normed, jnp.zeros((1, D), jnp.bfloat16)], axis=0)
    outgoing = padded_rows[owner_grid]
    arrived = lax.all_to_all(outgoing, "dp", split_axis=0, concat_axis=0, tiled=True)
    expert_rows = to_expert_major(arrived, dp_size, local_experts)
    expert_pre = jnp.einsum(
        "erd,egdf->ergf", expert_rows, expert_gate_up, preferred_element_type=jnp.float32
    )
    expert_hidden = (jax.nn.silu(expert_pre[:, :, 0]) * expert_pre[:, :, 1]).astype(jnp.bfloat16)
    expert_result = jnp.einsum(
        "erf,efd->erd", expert_hidden, expert_down, preferred_element_type=jnp.float32
    )
    returning = from_expert_major(expert_result, dp_size)
    returned = lax.all_to_all(
        returning.astype(jnp.bfloat16), "dp", split_axis=0, concat_axis=0, tiled=True
    ).astype(returning.dtype)
    padded_back = jnp.concatenate([returned.reshape(-1, D), jnp.zeros((1, D), jnp.float32)], axis=0)
    picked = padded_back[target].reshape(tokens, TOP, D)
    routed_part = jnp.sum(gate_values[:, :, None] * picked, axis=1)
    branch_sum = lax.psum_scatter(
        (shared_part + routed_part).astype(jnp.bfloat16), "tensor", scatter_dimension=0, tiled=True
    ).astype(jnp.float32)
    block_output = lax.dynamic_slice_in_dim(mixed, start, local_rows, 0) + branch_sum
    grad_rows = lax.all_gather(cotangent, "tensor", axis=0, tiled=True)
    grad_out = grad_rows.astype(jnp.float32)
    grad_shared_hidden = jnp.dot(grad_rows, shared_out.T, preferred_element_type=jnp.float32)
    grad_shared_out = jnp.dot(shared_hidden.T, grad_rows, preferred_element_type=jnp.float32)
    grad_shared_pre = swiglu_back(shared_pre[:, 0], shared_pre[:, 1], grad_shared_hidden, 1).astype(
        jnp.bfloat16
    )
    grad_shared_in = jnp.einsum(
        "td,tgf->gdf", second_normed, grad_shared_pre, preferred_element_type=jnp.float32
    )
    grad_second = jnp.einsum(
        "tgf,gdf->td", grad_shared_pre, shared_in, preferred_element_type=jnp.float32
    )
    gate_by_slot = (
        jnp.zeros((experts * capacity + 1,), jnp.float32).at[target].set(gate_values.reshape(-1))
    )
    slot_ids = jnp.arange(experts * capacity, dtype=jnp.int32).reshape(experts, capacity)
    padded_grad = jnp.concatenate([grad_out, jnp.zeros((1, D), jnp.float32)], axis=0)
    grad_outgoing = (gate_by_slot[slot_ids][..., None] * padded_grad[owner_grid]).astype(
        jnp.bfloat16
    )
    grad_arrived = lax.all_to_all(grad_outgoing, "dp", split_axis=0, concat_axis=0, tiled=True)
    grad_expert_rows = to_expert_major(grad_arrived, dp_size, local_experts)
    grad_expert_hidden = jnp.einsum(
        "erd,efd->erf", grad_expert_rows, expert_down, preferred_element_type=jnp.float32
    )
    grad_expert_down = jnp.einsum(
        "erf,erd->efd", expert_hidden, grad_expert_rows, preferred_element_type=jnp.float32
    )
    grad_expert_pre = swiglu_back(
        expert_pre[:, :, 0], expert_pre[:, :, 1], grad_expert_hidden, 2
    ).astype(jnp.bfloat16)
    grad_expert_gate_up = jnp.einsum(
        "erd,ergf->egdf", expert_rows, grad_expert_pre, preferred_element_type=jnp.float32
    )
    grad_expert_input = jnp.einsum(
        "ergf,egdf->erd", grad_expert_pre, expert_gate_up, preferred_element_type=jnp.float32
    )
    grad_returning = from_expert_major(grad_expert_input, dp_size)
    grad_returned = lax.all_to_all(
        grad_returning.astype(jnp.bfloat16), "dp", split_axis=0, concat_axis=0, tiled=True
    ).astype(grad_returning.dtype)
    padded_grad_back = jnp.concatenate(
        [grad_returned.reshape(-1, D), jnp.zeros((1, D), jnp.float32)], axis=0
    )
    grad_second = grad_second + jnp.sum(padded_grad_back[target].reshape(tokens, TOP, D), axis=1)
    grad_gates = jnp.sum(grad_out[:, None, :] * picked, axis=-1)
    grad_second, grad_gates = (
        lax.psum(grad_second.astype(jnp.bfloat16), "tensor").astype(jnp.float32),
        lax.psum(grad_gates.astype(jnp.bfloat16), "tensor").astype(jnp.float32),
    )
    chosen = (routes[:, :, None] == jnp.arange(experts, dtype=jnp.int32)[None, None, :]).astype(
        jnp.float32
    )
    grad_probabilities = jnp.sum(chosen * grad_gates[:, :, None], axis=1)
    grad_logits = probabilities * (
        grad_probabilities - jnp.sum(probabilities * grad_probabilities, axis=-1, keepdims=True)
    )
    grad_logits_low = grad_logits.astype(jnp.bfloat16)
    grad_router = jnp.dot(second_normed.T, grad_logits_low, preferred_element_type=jnp.float32)
    grad_second = grad_second + jnp.dot(
        grad_logits_low, router_weight.T, preferred_element_type=jnp.float32
    )
    gain_ffn_grad = jnp.sum(grad_second * second_unit, axis=0)
    grad_mixed = grad_out + rms_back(grad_second * ffn_gain_wide, second_unit, second_scale)
    grad_attn_low = grad_mixed.astype(jnp.bfloat16)
    grad_output_weight = jnp.dot(attended.T, grad_attn_low, preferred_element_type=jnp.float32)
    grad_attended = (
        jnp.dot(grad_attn_low, output_weight.T, preferred_element_type=jnp.float32)
        .astype(jnp.bfloat16)
        .reshape(tokens, heads, VD)
    )
    scores = attention_scores(query_rows, key_nope, key_rope, allowed, scale)
    weights = jnp.exp(scores - log_total)
    weights_low = weights.astype(jnp.bfloat16)
    grad_weights = jnp.einsum(
        "ihd,jhd->hij", grad_attended, values, preferred_element_type=jnp.float32
    )
    grad_values = jnp.einsum(
        "hij,ihd->jhd", weights_low, grad_attended, preferred_element_type=jnp.float32
    )
    grad_scores = (
        weights * (grad_weights - jnp.sum(weights * grad_weights, axis=-1, keepdims=True))
    ).astype(jnp.bfloat16)
    grad_query_nope = (
        jnp.einsum("hij,jhd->ihd", grad_scores, key_nope, preferred_element_type=jnp.float32)
        * scale
    )
    grad_query_rope = (
        jnp.einsum("hij,jd->ihd", grad_scores, key_rope, preferred_element_type=jnp.float32) * scale
    )
    grad_key_nope = (
        jnp.einsum(
            "hij,ihd->jhd", grad_scores, query_rows[..., :NOPE], preferred_element_type=jnp.float32
        )
        * scale
    )
    grad_key_rope = (
        jnp.einsum(
            "hij,ihd->jd", grad_scores, query_rows[..., NOPE:], preferred_element_type=jnp.float32
        )
        * scale
    )
    grad_query = (
        jnp.concatenate(
            [grad_query_nope, rotate_back(grad_query_rope, cosine[:, None, :], sine[:, None, :])],
            axis=-1,
        )
        .astype(jnp.bfloat16)
        .reshape(tokens, heads * (NOPE + ROPE))
    )
    grad_query_weight = jnp.dot(first_normed.T, grad_query, preferred_element_type=jnp.float32)
    grad_first = jnp.dot(grad_query, query_weight.T, preferred_element_type=jnp.float32)
    grad_keyval = (
        jnp.concatenate([grad_key_nope, grad_values], axis=-1)
        .astype(jnp.bfloat16)
        .reshape(tokens, heads * (NOPE + VD))
    )
    grad_keyval_weight = jnp.dot(latent_normed.T, grad_keyval, preferred_element_type=jnp.float32)
    grad_latent_normed = jnp.dot(grad_keyval, keyval_weight.T, preferred_element_type=jnp.float32)
    gain_latent_part = jnp.sum(grad_latent_normed * latent_unit, axis=0)
    grad_latent = rms_back(grad_latent_normed * latent_gain_wide, latent_unit, latent_scale)
    grad_latent_all = jnp.concatenate(
        [grad_latent, rotate_back(grad_key_rope, cosine, sine)], axis=-1
    )
    grad_first, grad_latent_all, gain_latent_grad = (
        lax.psum(grad_first.astype(jnp.bfloat16), "tensor").astype(jnp.float32),
        lax.psum(grad_latent_all.astype(jnp.bfloat16), "tensor").astype(jnp.float32),
        lax.psum(gain_latent_part.astype(jnp.bfloat16), "tensor").astype(jnp.float32),
    )
    grad_latent_low = grad_latent_all.astype(jnp.bfloat16)
    grad_latent_weight = jnp.dot(
        first_normed.T, grad_latent_low, preferred_element_type=jnp.float32
    )
    grad_first = grad_first + jnp.dot(
        grad_latent_low, latent_weight.T, preferred_element_type=jnp.float32
    )
    gain_attn_grad = jnp.sum(grad_first * first_unit, axis=0)
    grad_inputs = grad_mixed + rms_back(grad_first * attn_gain_wide, first_unit, first_scale)
    grad_local = lax.dynamic_slice_in_dim(grad_inputs, start, local_rows, 0)
    summed = (
        lax.psum_scatter(gain_attn_grad, "dp", scatter_dimension=0, tiled=True),
        lax.psum_scatter(grad_query_weight, "dp", scatter_dimension=0, tiled=True),
        lax.psum_scatter(grad_latent_weight, "dp", scatter_dimension=0, tiled=True),
        lax.psum_scatter(gain_latent_grad, "dp", scatter_dimension=0, tiled=True),
        lax.psum_scatter(grad_keyval_weight, "dp", scatter_dimension=0, tiled=True),
        lax.psum_scatter(grad_output_weight, "dp", scatter_dimension=1, tiled=True),
        lax.psum_scatter(gain_ffn_grad, "dp", scatter_dimension=0, tiled=True),
        lax.psum_scatter(grad_router, "dp", scatter_dimension=0, tiled=True),
        lax.psum_scatter(grad_shared_in, "dp", scatter_dimension=1, tiled=True),
        lax.psum_scatter(grad_shared_out, "dp", scatter_dimension=1, tiled=True),
    )
    return (
        block_output,
        grad_local,
        summed[0],
        summed[1],
        summed[2],
        summed[3],
        summed[4],
        summed[5],
        summed[6],
        summed[7],
        summed[8],
        summed[9],
        grad_expert_gate_up,
        grad_expert_down,
    )


RINGS = 4


def ring_step(values):
    return lax.ppermute(values, "dp", [(i, (i + RINGS) % 16) for i in range(16)])


def other_y(values):
    return lax.ppermute(values, "dp", [(i, i ^ 2) for i in range(16)])


def other_core(values):
    return lax.ppermute(values, "dp", [(i, i ^ 1) for i in range(16)])


def other_x(values):
    return lax.ppermute(values, "tensor", [(0, 1), (1, 0)])


def fence_kernel(*refs):
    pass


def after(values, *others):
    anywhere = pl.BlockSpec(memory_space=pl.ANY)
    return pl.pallas_call(
        fence_kernel,
        out_shape=jax.ShapeDtypeStruct(values.shape, values.dtype),
        in_specs=[anywhere] * (1 + len(others)),
        out_specs=anywhere,
        input_output_aliases={0: 0},
    )(values, *others)


def gather_whole(rows, early):
    ring = [rows, ring_step(rows)]
    ring.append(ring_step(ring[1]))
    ring.append(ring_step(after(ring[2], early)))
    over_x = [other_x(part) for part in ring]
    groups = []
    for k in (0, 2):
        held = jnp.concatenate(ring[k : k + 2], axis=0)
        across = jnp.concatenate(over_x[k : k + 2], axis=0)
        beside = other_y(held)
        groups.append((held, beside, across, other_y(across) if k else other_x(beside)))
    return groups, ring, over_x


def gather_rows(rows, corners):
    held = [rows, ring_step(rows)]
    first = (other_y(rows), other_x(rows))
    held.append(ring_step(after(held[1], *first)))
    held.append(ring_step(held[2]))
    groups = []
    for k, current in enumerate((held[0], held[1], jnp.concatenate(held[2:], axis=0))):
        beside, across = (other_y(current), other_x(current)) if k else first
        corner = other_x(beside) if corners[k] == "x" else other_y(across)
        groups.append((current, beside, across, corner))
    return held, groups


def add_low(first, second):
    return (first.astype(jnp.float32) + second.astype(jnp.float32)).astype(jnp.bfloat16)


def turn_corner(plane, direction):
    own, beside, across, corner = plane
    if direction == "x":
        return own, add_low(beside, other_x(corner)), across
    return own, beside, add_low(across, other_y(corner))


def close_plane(turned):
    own, beside, across = turned
    return own, other_y(beside), other_x(across)


def wide_sum(*values):
    total = values[0].astype(jnp.float32)
    for value in values[1:]:
        total = total + value.astype(jnp.float32)
    return total


def ring_sum(parts, low):
    moving = parts[1]
    for distance in (2, 3, 0):
        moving = ring_step(moving.astype(low)).astype(jnp.float32) + parts[distance].astype(
            jnp.float32
        )
    return moving


def ring_shards(shard):
    held = [shard]
    for _ in range(RINGS - 1):
        held.append(ring_step(held[-1]))
    return held


def gather_weight(shard, early):
    held, besides = [shard], []
    for distance in range(RINGS):
        beside = other_y(after(held[1], *early) if distance == 1 else held[distance])
        besides.append(beside)
        if distance < RINGS - 1:
            source = after(held[distance], besides[distance - 1]) if distance else shard
            held.append(ring_step(source))
    chunks = []
    for distance, (current, beside) in enumerate(zip(held, besides)):
        for flip_y, chunk in ((0, current), (1, beside)):
            for flip_core, piece in ((0, chunk), (1, other_core(chunk))):
                chunks.append(((distance, flip_y, flip_core), piece))
    return chunks, held, besides


def place_of(coords, key):
    z, y, core = coords
    distance, flip_y, flip_core = key
    return (
        lax.rem(z + RINGS - distance, RINGS) * 4
        + (1 - y if flip_y else y) * 2
        + (1 - core if flip_core else core)
    )


def weight_keys():
    return [
        (distance, flip_y, flip_core)
        for flip_core in (0, 1)
        for flip_y in (0, 1)
        for distance in range(RINGS)
    ]


def scatter_blocks(grads, low):
    half = grads.shape[0] // 2
    total = grads[:half].astype(jnp.float32) + other_core(grads[half:].astype(low)).astype(
        jnp.float32
    )
    quarter = half // 2
    total = total[:quarter] + other_y(total[quarter:].astype(low)).astype(jnp.float32)
    size = quarter // RINGS
    return ring_sum([total[r * size : (r + 1) * size] for r in range(RINGS)], low)


def pick_blocks(values, order):
    chosen = order[:, None] == jnp.arange(values.shape[0], dtype=jnp.int32)[None, :]
    chosen = chosen.reshape(chosen.shape + (1,) * (values.ndim - 1))
    return jnp.sum(jnp.where(chosen, values[None], 0.0), axis=1)


def wide_dot(left, right):
    return jnp.dot(left, right, preferred_element_type=jnp.float32)


def dot_turned(left, right):
    return lax.dot_general(left, right, (((1,), (1,)), ((), ())), preferred_element_type=jnp.float32)


def dot_rows(left, right):
    return lax.dot_general(left, right, (((0,), (0,)), ((), ())), preferred_element_type=jnp.float32)


TILE = 256


def whole(array):
    return pl.BlockSpec(array.shape, lambda *i: (0,) * array.ndim)


def in_vmem(count):
    return [pl.BlockSpec(memory_space=pltpu.VMEM)] * count


def in_place(count):
    return [pl.BlockSpec(memory_space=pl.ANY)] * count


def head_scores(heads, h, nope_ref, turned_ref, keyval_ref, key_ref, masks):
    span = ROPE // 2 * heads
    column = pl.ds(pl.multiple_of(h * NOPE, NOPE), NOPE)
    key_column = pl.ds(pl.multiple_of(h * (NOPE + VD), NOPE), NOPE)
    scores = dot_turned(nope_ref[:, column], keyval_ref[:, key_column])
    for k in (0, 1):
        part = turned_ref[:, k * span : (k + 1) * span]
        part = jnp.where(masks, part, jnp.zeros_like(part))
        scores += dot_turned(part, key_ref[:, k * span : (k + 1) * span])
    return scores * (NOPE + ROPE) ** (-0.5)


def head_lanes(heads, h):
    span = ROPE // 2 * heads
    lane = lax.broadcasted_iota(jnp.int32, (1, span), 1)
    return (lane >= h * (ROPE // 2)) & (lane < (h + 1) * (ROPE // 2))


def allowed_rows(count, segment_row, segment_column):
    tokens = segment_row.shape[1]
    column = lax.broadcasted_iota(jnp.int32, (tokens, tokens), 0)
    row = lax.broadcasted_iota(jnp.int32, (tokens, tokens), 1)
    live = (column < count) & (row < count) & (row <= column)
    return (segment_row == segment_column) & live | (column == row)


def attend_kernel(
    keys,
    extra,
    heads,
    sizes,
    place_ref,
    segment_row_ref,
    segment_column_ref,
    cosine_ref,
    sine_ref,
    own_ref,
    other_ref,
    *refs,
):
    depth, query_width, used, latent_depth, keyval_part, first_width = sizes
    chunks = refs[: len(keys)]
    (
        own_out,
        sent_out,
        first_ref,
        keyval_weight_ref,
        output_ref,
        normed_ref,
        nope_ref,
        turned_ref,
        latent_ref,
        key_ref,
        keyval_ref,
        total_ref,
        attended_ref,
        gains_ref,
        latent_gain_ref,
        semaphores,
    ) = refs[len(keys) + extra :]
    f32, bf16 = jnp.float32, jnp.bfloat16
    local_rows = own_ref.shape[0]
    tokens = 2 * local_rows
    coords = (place_ref[0], place_ref[1], place_ref[2])
    x = place_ref[3]
    copies = []
    parts = depth // latent_depth
    for key, chunk in zip(keys, chunks):
        block = place_of(coords, key)
        rows = pl.ds(pl.multiple_of(block * depth, depth), depth)
        small_rows = pl.ds(pl.multiple_of(block * latent_depth, latent_depth), latent_depth)
        moves = [(chunk.at[:, pl.ds(0, first_width)], first_ref.at[rows])]
        for k in range(parts):
            moves.append(
                (
                    chunk.at[
                        pl.ds(k * latent_depth, latent_depth), pl.ds(first_width, keyval_part)
                    ],
                    keyval_weight_ref.at[small_rows, pl.ds(k * keyval_part, keyval_part)],
                )
            )
        moves.append(
            (
                chunk.at[:, pl.ds(first_width + keyval_part, heads * VD)],
                output_ref.at[rows],
            )
        )
        for source, target in moves:
            copies.append(pltpu.make_async_copy(source, target, semaphores.at[len(copies)]))
    for copy in copies:
        copy.start()
    for copy in copies:
        copy.wait()

    edge = query_width + KVR
    spread = jnp.transpose(first_ref[:, edge:].astype(f32))[used - edge : used - edge + 8]
    gains_ref[...] = spread
    gain = spread[0:1]
    source = lax.broadcasted_iota(jnp.int32, (D, KVR), 0)
    target = lax.broadcasted_iota(jnp.int32, (D, KVR), 1)
    wanted = target // latent_depth * depth + target % latent_depth
    chosen = jnp.where(source == wanted, 1.0, 0.0).astype(bf16)
    latent_gain = wide_dot(spread.astype(bf16), chosen)[2:3]
    latent_gain_ref[...] = latent_gain
    for ref, start in ((own_ref, x * local_rows), (other_ref, (1 - x) * local_rows)):
        rows = ref[...].astype(f32)
        unit = rows * lax.rsqrt(jnp.mean(rows * rows, axis=1, keepdims=True) + EPSILON)
        normed_ref[pl.ds(pl.multiple_of(start, local_rows), local_rows), :] = (unit * gain).astype(
            bf16
        )
    nope_width = heads * NOPE
    span = heads * (ROPE // 2)
    half = nope_width // 2
    for k in (0, 1):
        nope_ref[:, k * half : (k + 1) * half] = wide_dot(
            normed_ref[...], first_ref[:, k * half : (k + 1) * half]
        ).astype(bf16)
    turning = wide_dot(normed_ref[...], first_ref[:, nope_width : nope_width + 2 * span])
    cosine, sine = cosine_ref[...], sine_ref[...]
    first, second = turning[:, :span], turning[:, span:]
    turned_ref[:, :span] = (first * cosine - second * sine).astype(bf16)
    turned_ref[:, span:] = (second * cosine + first * sine).astype(bf16)
    latent = wide_dot(normed_ref[...], first_ref[:, query_width : query_width + KVR])
    latent_ref[...] = latent
    tail = wide_dot(normed_ref[...], first_ref[:, query_width + KVR :])
    lane = lax.broadcasted_iota(jnp.int32, (1, tail.shape[1]), 1)
    swapped = jnp.where(
        lane < ROPE // 2,
        -pltpu.roll(tail, tail.shape[1] - ROPE // 2, 1),
        pltpu.roll(tail, ROPE // 2, 1),
    )
    width = tail.shape[1]
    turned_key = tail * cosine[:, :width] + swapped * sine[:, :width]
    turned_key = jnp.where(lane < ROPE, turned_key, 0.0).astype(bf16)
    source = lax.broadcasted_iota(jnp.int32, (width, 2 * span), 0)
    target = lax.broadcasted_iota(jnp.int32, (width, 2 * span), 1)
    wanted = target % (ROPE // 2) + jnp.where(target < span, 0, ROPE // 2)
    key_ref[...] = wide_dot(turned_key, (source == wanted).astype(bf16)).astype(bf16)
    unit = latent * lax.rsqrt(jnp.mean(latent * latent, axis=1, keepdims=True) + EPSILON)
    latent_normed = (unit * latent_gain).astype(bf16)
    half = keyval_ref.shape[1] // 4
    for k in range(4):
        keyval_ref[:, k * half : (k + 1) * half] = wide_dot(
            latent_normed, keyval_weight_ref[:, k * half : (k + 1) * half]
        ).astype(bf16)
    allowed = allowed_rows(place_ref[4], segment_row_ref[...], segment_column_ref[...])
    total_lane = lax.broadcasted_iota(jnp.int32, total_ref.shape, 1)
    total_ref[...] = jnp.zeros_like(total_ref)

    def one_head(h, _):
        scores = head_scores(
            heads, h, nope_ref, turned_ref, keyval_ref, key_ref, head_lanes(heads, h)
        )
        scores = jnp.where(allowed, scores, -1e30)
        most = jnp.max(scores, axis=1, keepdims=True)
        total = most + jnp.log(jnp.sum(jnp.exp(scores - most), axis=1, keepdims=True))
        weights = jnp.exp(scores - total).astype(bf16)
        total_ref[...] += jnp.where(total_lane == h, total, 0.0)
        value_column = pl.ds(pl.multiple_of(h * (NOPE + VD) + NOPE, NOPE), VD)
        attended_ref[:, pl.ds(pl.multiple_of(h * VD, VD), VD)] = wide_dot(
            weights, keyval_ref[:, value_column]
        ).astype(bf16)
        return 0

    lax.fori_loop(0, heads, one_head, 0)
    own = pl.ds(pl.multiple_of(x * local_rows, local_rows), local_rows)
    other = pl.ds(pl.multiple_of((1 - x) * local_rows, local_rows), local_rows)
    pieces = 4
    size = output_ref.shape[0] // pieces
    for k in range(pieces):
        columns = slice(k * size, (k + 1) * size)
        own_out[:, columns] = dot_turned(attended_ref[own, :], output_ref[columns, :])
        sent_out[:, columns] = dot_turned(attended_ref[other, :], output_ref[columns, :]).astype(
            bf16
        )


def attend_forward(place, segments, cosine, sine, own, other, chunks, heads, sizes, others):
    depth, query_width, used, latent_depth, keyval_part, first_width = sizes
    f32, bf16 = jnp.float32, jnp.bfloat16
    keys = [key for key, _ in chunks]
    local_rows = own.shape[0]
    tokens = 2 * local_rows
    span = heads * (ROPE // 2)
    shapes = [
        ((local_rows, D), f32),
        ((local_rows, D), bf16),
        ((D, first_width), bf16),
        ((KVR, heads * (NOPE + VD)), bf16),
        ((D, heads * VD), bf16),
        ((tokens, D), bf16),
        ((tokens, heads * NOPE), bf16),
        ((tokens, 2 * span), bf16),
        ((tokens, KVR), f32),
        ((tokens, 2 * span), bf16),
        ((tokens, heads * (NOPE + VD)), bf16),
        ((tokens, 128), f32),
        ((tokens, heads * VD), bf16),
        ((8, D), f32),
        ((1, KVR), f32),
    ]
    return pl.pallas_call(
        functools.partial(attend_kernel, keys, len(others), heads, sizes),
        out_shape=[jax.ShapeDtypeStruct(*shape) for shape in shapes],
        in_specs=[pl.BlockSpec(memory_space=pltpu.SMEM)]
        + in_vmem(6)
        + in_place(len(chunks) + len(others)),
        out_specs=in_vmem(len(shapes)),
        scratch_shapes=[
            pltpu.SemaphoreType.DMA((len(chunks) * (2 + depth // latent_depth),))
        ],
        compiler_params=pltpu.CompilerParams(vmem_limit_bytes=48 * 1024 * 1024),
        cost_estimate=pl.CostEstimate(
            flops=2 * tokens * D * (first_width + heads * VD + 1024),
            bytes_accessed=4 * D * (first_width + 1536),
            transcendentals=2 * heads * tokens * tokens,
        ),
    )(
        place,
        segments,
        segments.T,
        cosine,
        sine,
        own,
        other,
        *[piece for _, piece in chunks],
        *others,
    )


def attend_back_kernel(
    heads,
    place_ref,
    segment_row_ref,
    segment_column_ref,
    cosine_ref,
    sine_ref,
    own_ref,
    other_ref,
    keyval_weight_ref,
    output_ref,
    nope_ref,
    turned_ref,
    latent_ref,
    key_ref,
    keyval_ref,
    total_ref,
    latent_gain_ref,
    projected_ref,
    keyval_grad_ref,
    latent_out,
    gain_ref,
    grad_ref,
    turn_ref,
    back_ref,
):
    f32, bf16 = jnp.float32, jnp.bfloat16
    local_rows = own_ref.shape[0]
    x = place_ref[3]
    span = heads * (ROPE // 2)
    nope_width = heads * NOPE
    query_width = nope_width + 2 * span
    scale = (NOPE + ROPE) ** (-0.5)
    for ref, start in ((own_ref, x * local_rows), (other_ref, (1 - x) * local_rows)):
        rows = pl.ds(pl.multiple_of(start, local_rows), local_rows)
        for k in (0, 1):
            half = slice(k * nope_width // 2, (k + 1) * nope_width // 2)
            grad_ref[rows, half] = wide_dot(ref[...], output_ref[:, half]).astype(bf16)
    allowed = allowed_rows(place_ref[4], segment_row_ref[...], segment_column_ref[...])
    total_lane = lax.broadcasted_iota(jnp.int32, total_ref.shape, 1)
    turn_ref[...] = jnp.zeros_like(turn_ref)
    back_ref[...] = jnp.zeros_like(back_ref)

    def one_head(h, _):
        mask = head_lanes(heads, h)
        scores = head_scores(heads, h, nope_ref, turned_ref, keyval_ref, key_ref, mask)
        total = jnp.sum(jnp.where(total_lane == h, total_ref[...], 0.0), axis=1, keepdims=True)
        weights = jnp.exp(jnp.where(allowed, scores, -1e30) - total)
        weights_low = weights.astype(bf16)
        column = pl.ds(pl.multiple_of(h * NOPE, NOPE), NOPE)
        key_column = pl.ds(pl.multiple_of(h * (NOPE + VD), NOPE), NOPE)
        value_column = pl.ds(pl.multiple_of(h * (NOPE + VD) + NOPE, NOPE), VD)
        grads = grad_ref[:, column]
        grad_weights = dot_turned(grads, keyval_ref[:, value_column])
        keyval_grad_ref[:, value_column] = dot_rows(weights_low, grads).astype(bf16)
        grad_scores = (
            weights * (grad_weights - jnp.sum(weights * grad_weights, axis=1, keepdims=True))
        ).astype(bf16)
        projected_ref[:, column] = (
            scale * wide_dot(grad_scores, keyval_ref[:, key_column])
        ).astype(bf16)
        keyval_grad_ref[:, key_column] = (
            scale * dot_rows(grad_scores, nope_ref[:, column])
        ).astype(bf16)
        for k in (0, 1):
            part = slice(k * span, (k + 1) * span)
            turn = wide_dot(grad_scores, key_ref[:, part])
            turn_ref[:, part] += jnp.where(mask, turn, 0.0)
            own = turned_ref[:, part]
            own = jnp.where(mask, own, jnp.zeros_like(own))
            back_ref[:, part] += dot_rows(grad_scores, own)
        return 0

    lax.fori_loop(0, heads, one_head, 0)
    cosine, sine = cosine_ref[...], sine_ref[...]
    first, second = scale * turn_ref[:, :span], scale * turn_ref[:, span:]
    projected_ref[:, nope_width : nope_width + span] = (first * cosine + second * sine).astype(bf16)
    projected_ref[:, nope_width + span : query_width] = (second * cosine - first * sine).astype(
        bf16
    )
    folded = []
    for k in (0, 1):
        part = scale * back_ref[:, k * span : (k + 1) * span]
        shift = span // 2
        while shift >= ROPE // 2:
            part = part + pltpu.roll(part, shift, 1)
            shift //= 2
        folded.append(part)
    width = projected_ref.shape[1] - query_width - KVR
    lane = lax.broadcasted_iota(jnp.int32, (1, width), 1)
    first = (folded[0] * cosine + folded[1] * sine)[:, :width]
    second = (folded[1] * cosine - folded[0] * sine)[:, :width]
    projected_ref[:, query_width + KVR :] = jnp.where(
        lane < ROPE // 2, first, jnp.where(lane < ROPE, second, 0.0)
    ).astype(bf16)
    gain = latent_gain_ref[...]
    latent = latent_ref[...]
    row_scale = lax.rsqrt(jnp.mean(latent * latent, axis=1, keepdims=True) + EPSILON)
    unit = latent * row_scale
    latent_out[...] = (unit * gain).astype(bf16)
    grad_normed = dot_turned(keyval_grad_ref[...], keyval_weight_ref[...])
    gain_ref[...] = jnp.sum(grad_normed * unit, axis=0, keepdims=True)
    grad_unit = grad_normed * gain
    projected_ref[:, query_width : query_width + KVR] = (
        row_scale * (grad_unit - unit * jnp.mean(grad_unit * unit, axis=1, keepdims=True))
    ).astype(bf16)


def attend_back(place, segments, cosine, sine, own, other, saved, heads, first_width, others):
    f32, bf16 = jnp.float32, jnp.bfloat16
    keyval = saved[6]
    tokens = 2 * own.shape[0]
    span = heads * (ROPE // 2)
    return pl.pallas_call(
        lambda *refs: attend_back_kernel(heads, *refs[:16], *refs[16 + len(others) :]),
        out_shape=[
            jax.ShapeDtypeStruct((tokens, first_width), bf16),
            jax.ShapeDtypeStruct((tokens, keyval.shape[1]), bf16),
            jax.ShapeDtypeStruct((tokens, KVR), bf16),
            jax.ShapeDtypeStruct((1, KVR), f32),
        ],
        in_specs=[pl.BlockSpec(memory_space=pltpu.SMEM)] + in_vmem(15) + in_place(len(others)),
        out_specs=in_vmem(4),
        scratch_shapes=[
            pltpu.VMEM((tokens, heads * NOPE), bf16),
            pltpu.VMEM((tokens, 2 * span), f32),
            pltpu.VMEM((tokens, 2 * span), f32),
        ],
        compiler_params=pltpu.CompilerParams(vmem_limit_bytes=48 * 1024 * 1024),
        cost_estimate=pl.CostEstimate(
            flops=2 * tokens * D * 3000,
            bytes_accessed=2 * D * 1536,
            transcendentals=heads * tokens * tokens,
        ),
    )(
        place,
        segments,
        segments.T,
        cosine,
        sine,
        own,
        other,
        *saved,
        *others,
    )


def first_grads_kernel(extra, places_ref, left_ref, right_ref, small_ref, *refs):
    out_ref = refs[-1]
    size = left_ref.shape[1]
    edge = right_ref.shape[1] - small_ref.shape[0]
    result = dot_rows(left_ref[...], right_ref[...])
    for value, some in (
        (result[:, :edge], slice(0, edge)),
        (result[:, edge:] + jnp.transpose(small_ref[...]), slice(edge, right_ref.shape[1])),
    ):
        if extra:
            value = value + refs[0][:, some].astype(jnp.float32)
        out_ref[:, some] = value.astype(jnp.bfloat16)


def other_grads_kernel(first, extra, places_ref, latent_ref, keyval_ref, grad_ref, attended_ref, *refs):
    out_ref, keyval_all = refs[-2:]
    step = pl.program_id(0)
    size = grad_ref.shape[1]
    latent_size = latent_ref.shape[1] // places_ref.shape[0]
    parts = size // latent_size
    columns = keyval_ref.shape[1] // parts

    @pl.when(step == 0)
    def _():
        for k in range(parts):
            some = slice(k * columns, (k + 1) * columns)
            keyval_all[:, some] = dot_rows(latent_ref[...], keyval_ref[:, some])

    start = pl.multiple_of(places_ref[first + step] * latent_size, latent_size)
    strip = keyval_all[pl.ds(start, latent_size), :]
    keyval = jnp.concatenate([strip[:, k * columns : (k + 1) * columns] for k in range(parts)], axis=0)
    output = dot_rows(grad_ref[...], attended_ref[...])
    for value, some in (
        (keyval, slice(0, columns)),
        (output, slice(columns, columns + output.shape[1])),
    ):
        if extra:
            value = value + refs[0][:, some].astype(jnp.float32)
        out_ref[:, some] = value.astype(jnp.bfloat16)


def still(array):
    return pl.BlockSpec(array.shape, lambda i, where: (0, 0))


def grads_call(
    kernel, specs, operands, scratch, size, width, places, first, count, arrived, others
):
    extra = [] if arrived is None else [arrived]
    return pl.pallas_call(
        lambda *refs: kernel(
            len(extra),
            *refs[: 1 + len(operands) + len(extra)],
            *refs[1 + len(operands) + len(extra) + len(others) :],
        ),
        grid_spec=pltpu.PrefetchScalarGridSpec(
            num_scalar_prefetch=1,
            grid=(count,),
            in_specs=specs
            + [pl.BlockSpec((size, width), lambda i, where: (first + i, 0))] * len(extra)
            + in_place(len(others)),
            out_specs=pl.BlockSpec((size, width), lambda i, where: (i, 0)),
            scratch_shapes=scratch,
        ),
        out_shape=jax.ShapeDtypeStruct((count * size, width), jnp.bfloat16),
        compiler_params=pltpu.CompilerParams(vmem_limit_bytes=32 * 1024 * 1024),
        cost_estimate=pl.CostEstimate(
            flops=1024 * count * size * width,
            bytes_accessed=4 * count * size * width,
            transcendentals=0,
        ),
    )(places, *operands, *extra, *others)


def first_grads(left, right, small, places, first, count, arrived=None, others=()):
    rows, width = right.shape
    size = left.shape[1] // places.shape[0]
    specs = [
        pl.BlockSpec((rows, size), lambda i, where: (0, where[first + i])),
        still(right),
        pl.BlockSpec((small.shape[0], size), lambda i, where: (0, where[first + i])),
    ]
    return grads_call(
        first_grads_kernel,
        specs,
        (left, right, small),
        [],
        size,
        width,
        places,
        first,
        count,
        arrived,
        others,
    )


def other_grads(latent, keyval, grad, attended, places, first, count, arrived=None, others=()):
    rows = grad.shape[0]
    blocks = places.shape[0]
    size = grad.shape[1] // blocks
    parts = size // (latent.shape[1] // blocks)
    width = keyval.shape[1] // parts + attended.shape[1]
    specs = [
        still(latent),
        still(keyval),
        pl.BlockSpec((rows, size), lambda i, where: (0, where[first + i])),
        still(attended),
    ]
    scratch = [pltpu.VMEM((latent.shape[1], keyval.shape[1]), jnp.float32)]
    return grads_call(
        functools.partial(other_grads_kernel, first),
        specs,
        (latent, keyval, grad, attended),
        scratch,
        size,
        width,
        places,
        first,
        count,
        arrived,
        others,
    )


def first_back_kernel(place_ref, own_ref, other_ref, grad_ref, weight_ref, own_out, sent_out, gain_ref):
    local_rows = own_ref.shape[0]
    x = place_ref[3]
    size = weight_ref.shape[0] // 4
    for ref, start, out in (
        (own_ref, x * local_rows, own_out),
        (other_ref, (1 - x) * local_rows, sent_out),
    ):
        rows = ref[...].astype(jnp.float32)
        unit = rows * lax.rsqrt(jnp.mean(rows * rows, axis=1, keepdims=True) + EPSILON)
        grads = grad_ref[pl.ds(pl.multiple_of(start, local_rows), local_rows), :]
        for k in range(4):
            some = slice(k * size, (k + 1) * size)
            part = dot_turned(grads, weight_ref[some, :])
            out[:, some] = part.astype(out.dtype)
            gain = jnp.sum(part * unit[:, some], axis=0, keepdims=True)
            if ref is own_ref:
                gain_ref[:, some] = gain
            else:
                gain_ref[:, some] += gain


def first_back(place, own, other, grads, weight):
    f32, bf16 = jnp.float32, jnp.bfloat16
    depth = weight.shape[0]
    return pl.pallas_call(
        first_back_kernel,
        out_shape=[
            jax.ShapeDtypeStruct(own.shape, f32),
            jax.ShapeDtypeStruct(own.shape, bf16),
            jax.ShapeDtypeStruct((1, depth), f32),
        ],
        in_specs=[pl.BlockSpec(memory_space=pltpu.SMEM)] + in_vmem(4),
        out_specs=in_vmem(3),
        compiler_params=pltpu.CompilerParams(vmem_limit_bytes=32 * 1024 * 1024),
        cost_estimate=pl.CostEstimate(
            flops=4 * own.shape[0] * weight.shape[0] * weight.shape[1],
            bytes_accessed=2 * weight.shape[0] * weight.shape[1],
            transcendentals=0,
        ),
    )(place, own, other, grads, weight)


def close_ring(near, arrived, last):
    size = near.shape[0] // RINGS
    total = near.astype(jnp.float32) + arrived.astype(jnp.float32)
    parts = [total[r * size : (r + 1) * size] for r in range(RINGS)]
    parts[0] = after(parts[0], last)
    return ring_sum(parts, jnp.bfloat16)


def pack_kernel(heads, query_ref, latent_ref, small_ref, keyval_ref, output_ref, out_ref):
    half = ROPE // 2
    head = NOPE + ROPE
    nope_width = heads * NOPE
    for h in range(heads):
        start = h * head
        out_ref[:, h * NOPE : (h + 1) * NOPE] = query_ref[:, start : start + NOPE]
        for k in (0, 1):
            to = nope_width + k * heads * half + h * half
            out_ref[:, to : to + half] = query_ref[
                :, start + NOPE + k * half : start + NOPE + (k + 1) * half
            ]
    at = heads * head
    edge = at + KVR
    out_ref[:, at:edge] = latent_ref[:, :KVR]
    out_ref[:, edge : edge + 128] = jnp.concatenate([latent_ref[:, KVR:], small_ref[...]], axis=1)
    at = edge + 128
    size = keyval_ref.shape[0]
    parts = out_ref.shape[0] // size
    part = keyval_ref.shape[1] // parts
    for k in range(parts):
        out_ref[k * size : (k + 1) * size, at : at + part] = keyval_ref[
            :, k * part : (k + 1) * part
        ]
    out_ref[:, at + part :] = jnp.transpose(output_ref[...].astype(jnp.float32)).astype(
        jnp.bfloat16
    )


def pack_weights(query, latent, small, keyval, output):
    depth, query_width = query.shape
    heads = query_width // (NOPE + ROPE)
    width = query_width + KVR + 128 + keyval.size // depth + output.shape[0]
    return pl.pallas_call(
        functools.partial(pack_kernel, heads),
        out_shape=jax.ShapeDtypeStruct((depth, width), jnp.bfloat16),
        in_specs=in_vmem(5),
        out_specs=pl.BlockSpec(memory_space=pltpu.VMEM),
    )(query, latent, small, keyval, output)


def load_pieces(pieces, starts, target, semaphores):
    size = target.shape[0] // len(pieces)
    copies = [
        pltpu.make_async_copy(
            piece.at[pl.ds(start, size)], target.at[pl.ds(k * size, size)], semaphores.at[k]
        )
        for k, (piece, start) in enumerate(zip(pieces, starts))
    ]
    for copy in copies:
        copy.start()
    for copy in copies:
        copy.wait()


def shared_stride(shared):
    return -(-shared // 32) * 32


def pack_shared_kernel(blocks, shared, in_ref, down_ref, out_ref):
    stride = shared_stride(shared)
    out_ref[...] = jnp.zeros_like(out_ref)
    for k in range(3):
        if k < 2:
            units = jnp.transpose(in_ref[k].astype(jnp.float32)).astype(jnp.bfloat16)
        else:
            units = down_ref[...]
        for b in range(blocks):
            out_ref[b, k * stride : k * stride + shared] = units[b * shared : (b + 1) * shared]


def pack_shared(shared_in, shared_down, blocks, others):
    depth = shared_in.shape[1]
    shared = shared_down.shape[0] // blocks
    return pl.pallas_call(
        lambda in_ref, down_ref, *refs: pack_shared_kernel(
            blocks, shared, in_ref, down_ref, refs[-1]
        ),
        out_shape=jax.ShapeDtypeStruct((blocks, 3 * shared_stride(shared), depth), jnp.bfloat16),
        in_specs=in_vmem(2) + in_place(len(others)),
        out_specs=pl.BlockSpec(memory_space=pltpu.VMEM),
    )(shared_in, shared_down, *others)


def unpack_shared_kernel(shared, packed_ref, in_ref, down_ref, units_ref):
    stride = shared_stride(shared)
    blocks = packed_ref.shape[0]
    for k in range(3):
        target = down_ref if k == 2 else units_ref
        for b in range(blocks):
            target[b * shared : (b + 1) * shared, :] = packed_ref[
                b, k * stride : k * stride + shared
            ].astype(jnp.float32)
        if k < 2:
            in_ref[k] = jnp.transpose(units_ref[...])


def unpack_shared(packed, shared, others):
    blocks, _, depth = packed.shape
    return pl.pallas_call(
        lambda packed_ref, *refs: unpack_shared_kernel(shared, packed_ref, *refs[len(others) :]),
        out_shape=[
            jax.ShapeDtypeStruct((2, depth, blocks * shared), jnp.float32),
            jax.ShapeDtypeStruct((blocks * shared, depth), jnp.float32),
        ],
        in_specs=in_vmem(1) + in_place(len(others)),
        out_specs=in_vmem(2),
        scratch_shapes=[pltpu.VMEM((blocks * shared, depth), jnp.float32)],
    )(packed, *others)


def pack_units_kernel(units, shared, own_in, other_in, own_down, other_down, near, far, *refs):
    outs = refs[-3:]
    hole = -(-units // TILE) * TILE
    stride = shared_stride(shared)
    columns = outs[0].shape[1]
    size = near.shape[2]
    for k, out in enumerate(outs):
        first = own_in[0, k] if k < 2 else own_down[0]
        second = other_in[0, k] if k < 2 else other_down[0]
        out[:units] = first
        out[units:hole] = jnp.zeros((hole - units, columns), jnp.bfloat16)
        out[hole : hole + units] = second
        out[hole + units : 2 * hole] = jnp.zeros((hole - units, columns), jnp.bfloat16)
        out[2 * hole :] = jnp.zeros((TILE, columns), jnp.bfloat16)
        for b in range(columns // size):
            part = slice(b * size, (b + 1) * size)
            for at, ref in ((2 * hole, near), (2 * hole + stride, far)):
                out[at : at + shared, part] = ref[b, k * stride : k * stride + shared]


def pack_units(own_in, other_in, own_down, other_down, near, far, shared, others):
    units, depth = own_down.shape[1:]
    size = near.shape[2]
    height = 2 * (-(-units // TILE) * TILE) + TILE
    columns = 2 * size
    in_spec = pl.BlockSpec((1, 2, units, columns), lambda i: (0, 0, 0, i))
    down_spec = pl.BlockSpec((1, units, columns), lambda i: (0, 0, i))
    narrow = pl.BlockSpec((2,) + near.shape[1:], lambda i: (i, 0, 0))
    return pl.pallas_call(
        functools.partial(pack_units_kernel, units, shared),
        grid=(depth // columns,),
        in_specs=[in_spec, in_spec, down_spec, down_spec, narrow, narrow]
        + in_place(len(others)),
        out_specs=[pl.BlockSpec((height, columns), lambda i: (0, i))] * 3,
        out_shape=[jax.ShapeDtypeStruct((height, depth), jnp.bfloat16)] * 3,
        compiler_params=pltpu.CompilerParams(vmem_limit_bytes=32 * 1024 * 1024),
        cost_estimate=pl.CostEstimate(
            flops=0, bytes_accessed=12 * height * depth, transcendentals=0
        ),
    )(own_in, other_in, own_down, other_down, near, far, *others)


def expert_grads_kernel(units, count, extra, right_ref, *refs):
    out = refs[-1]
    for k in range(count):

        @pl.when(pl.program_id(0) == k)
        def _():
            result = dot_rows(refs[k][...], right_ref[...])[:units]
            if extra:
                result += refs[count][0, 0].astype(jnp.float32)
            out[0, 0] = result.astype(out.dtype)


def expert_grads(lefts, right, units, column, arrived, kind, others=()):
    total, depth = right.shape
    wide = -(-units // TILE) * TILE
    extra = [] if arrived is None else [arrived]
    out = pl.BlockSpec((1, 1, units, 2 * TILE), lambda k, i: (0, k, 0, i))
    side = pl.BlockSpec((total, wide), lambda k, i: (0, column))
    return pl.pallas_call(
        functools.partial(expert_grads_kernel, units, len(lefts), len(extra)),
        grid=(len(lefts), depth // (2 * TILE)),
        in_specs=[pl.BlockSpec((total, 2 * TILE), lambda k, i: (0, i))]
        + [side] * len(lefts)
        + [out] * len(extra)
        + in_place(len(others)),
        out_specs=out,
        out_shape=jax.ShapeDtypeStruct((1, len(lefts), units, depth), kind),
        compiler_params=pltpu.CompilerParams(vmem_limit_bytes=48 * 1024 * 1024),
        cost_estimate=pl.CostEstimate(
            flops=2 * len(lefts) * total * depth * wide,
            bytes_accessed=2 * len(lefts) * total * (depth + wide) + 8 * depth * units,
            transcendentals=0,
        ),
    )(right, *lefts, *extra, *others)


def side_grads_kernel(shared, rows_ref, cots_ref, gate_ref, up_ref, hidden_ref, logit_ref, *outs):
    kept_ref, sent_ref, router_ref = outs
    stride = shared_stride(shared)
    size = kept_ref.shape[2]
    for k, (left, right) in enumerate(
        ((gate_ref, rows_ref), (up_ref, rows_ref), (hidden_ref, cots_ref))
    ):
        result = dot_rows(left[...], right[...])
        for b in range(kept_ref.shape[0]):
            part = slice(b * size, (b + 1) * size)
            kept_ref[b, k * stride : (k + 1) * stride] = result[:stride, part]
            sent_ref[b, k * stride : (k + 1) * stride] = result[
                stride : 2 * stride, part
            ].astype(jnp.bfloat16)
    router_ref[...] = dot_rows(logit_ref[...], rows_ref[...])


def side_grads(rows, cots, gate, up, hidden, logits, shared, blocks, others):
    total, depth = rows.shape
    column = gate.shape[1] // TILE - 1
    size = depth // blocks
    stride = shared_stride(shared)
    wide = pl.BlockSpec((total, 2 * TILE), lambda i: (0, i))
    side = pl.BlockSpec((total, TILE), lambda i: (0, column))
    packed = pl.BlockSpec((2 * TILE // size, 3 * stride, size), lambda i: (i, 0, 0))
    return pl.pallas_call(
        lambda *refs: side_grads_kernel(shared, *refs[:6], *refs[6 + len(others) :]),
        grid=(depth // (2 * TILE),),
        in_specs=[wide, wide, side, side, side, whole(logits)] + in_place(len(others)),
        out_specs=[packed, packed, pl.BlockSpec((logits.shape[1], 2 * TILE), lambda i: (0, i))],
        out_shape=[
            jax.ShapeDtypeStruct((blocks, 3 * stride, size), jnp.float32),
            jax.ShapeDtypeStruct((blocks, 3 * stride, size), jnp.bfloat16),
            jax.ShapeDtypeStruct((logits.shape[1], depth), jnp.float32),
        ],
        compiler_params=pltpu.CompilerParams(vmem_limit_bytes=48 * 1024 * 1024),
        cost_estimate=pl.CostEstimate(
            flops=8 * total * depth * TILE,
            bytes_accessed=4 * total * depth,
            transcendentals=0,
        ),
    )(rows, cots, gate, up, hidden, logits, *others)


def down_kernel(starts, *refs):
    count = len(starts)
    pieces, weight_ref = refs[:count], refs[count]
    grads_ref, rows_ref, semaphores = refs[-3:]

    @pl.when(pl.program_id(0) == 0)
    def _():
        load_pieces(pieces, starts, rows_ref, semaphores)

    size = rows_ref.shape[0] // 2
    for k in range(2):
        part = slice(k * size, (k + 1) * size)
        grads_ref[part, :] = dot_turned(rows_ref[part, :], weight_ref[...]).astype(jnp.bfloat16)


def down_grads(part, pieces, size, down, kept, others):
    count = len(pieces)
    depth = down.shape[1]
    width = down.shape[0]
    rows = count * size
    return pl.pallas_call(
        functools.partial(down_kernel, tuple(start for _, start in pieces)),
        grid=(width // TILE,),
        in_specs=in_place(count)
        + [pl.BlockSpec((TILE, depth), lambda i: (i, 0))]
        + in_place(len(kept) + len(others)),
        out_specs=[
            pl.BlockSpec((rows, TILE), lambda i: (part, i)),
            pl.BlockSpec((rows, depth), lambda i: (part, 0)),
        ],
        out_shape=[
            jax.ShapeDtypeStruct((2 * rows, width), jnp.bfloat16),
            jax.ShapeDtypeStruct((2 * rows, depth), jnp.bfloat16),
        ],
        scratch_shapes=[pltpu.SemaphoreType.DMA((count,))],
        input_output_aliases={count + 1 + k: k for k in range(len(kept))},
        compiler_params=pltpu.CompilerParams(vmem_limit_bytes=48 * 1024 * 1024),
        cost_estimate=pl.CostEstimate(
            flops=2 * rows * depth * width,
            bytes_accessed=2 * (2 * rows * depth + depth * width + rows * width),
            transcendentals=0,
        ),
    )(*[array for array, _ in pieces], down, *kept, *others)


def out_kernel(pieces, hidden_ref, weight_ref, *refs):
    outs, done_ref = refs[-1 - pieces : -1], refs[-1]
    size = hidden_ref.shape[0] // (RINGS * pieces)
    done_ref[...] = jnp.zeros_like(done_ref)
    for r in range(RINGS):
        part = hidden_ref[r * pieces * size : (r + 1) * pieces * size, :]
        result = wide_dot(part, weight_ref[...]).astype(jnp.bfloat16)
        for k in range(pieces):
            outs[k][r * size : (r + 1) * size, :] = result[k * size : (k + 1) * size]


def out_rows(pieces, half, hidden, down, kept, others):
    rows, width = hidden.shape
    depth = down.shape[1]
    steps = depth // (2 * TILE)
    results = pl.pallas_call(
        functools.partial(out_kernel, pieces),
        grid=(steps,),
        in_specs=[whole(hidden), pl.BlockSpec((width, TILE), lambda i: (0, half * steps + i))]
        + in_place(len(kept) + len(others)),
        out_specs=[pl.BlockSpec((rows // pieces, TILE), lambda i: (0, half * steps + i))] * pieces
        + [pl.BlockSpec((8, 128), lambda i: (0, 0))],
        out_shape=[jax.ShapeDtypeStruct((rows // pieces, depth), jnp.bfloat16)] * pieces
        + [jax.ShapeDtypeStruct((8, 128), jnp.float32)],
        input_output_aliases={2 + k: k for k in range(len(kept))},
        compiler_params=pltpu.CompilerParams(vmem_limit_bytes=48 * 1024 * 1024),
        cost_estimate=pl.CostEstimate(
            flops=rows * depth * width,
            bytes_accessed=rows * depth + depth * width + 2 * rows * width,
            transcendentals=0,
        ),
    )(hidden, down, *kept, *others)
    return results[:-1], results[-1]


def mlp_kernel(tiles, starts, others, experts_ref, routed_ref, *refs):
    pieces = len(starts)
    row_refs = refs[:pieces]
    router_ref, gate_col, up_col, down_grad, gate_row, up_row = refs[pieces : pieces + 6]
    outs = refs[pieces + 6 + others :]
    grad_refs = outs[:pieces]
    rows_out, hidden_out, gate_out, up_out, logit_out = outs[pieces : pieces + 5]
    gate_all, up_all, prob_ref, scale_ref, sum_ref, semaphores = outs[pieces + 5 :]
    step = pl.program_id(0)
    third = tiles // 2
    total = rows_out.shape[0]
    size = total // pieces
    lane = lax.broadcasted_iota(jnp.int32, (1, router_ref.shape[1]), 1) - experts_ref[3]

    @pl.when(step == 0)
    def _():
        load_pieces(row_refs, starts, rows_out, semaphores)
        logits = wide_dot(rows_out[...], router_ref[...])
        logits = jnp.where((lane >= 0) & (lane < experts_ref[2]), logits, -1e30)
        raised = jnp.exp(logits - jnp.max(logits, axis=1, keepdims=True))
        chances = raised / jnp.sum(raised, axis=1, keepdims=True)
        prob_ref[...] = chances
        for k in (0, 1):
            chance = jnp.sum(jnp.where(lane == experts_ref[k], chances, 0.0), axis=1, keepdims=True)
            scale_ref[k] = routed_ref[:, k : k + 1] * chance
        scale_ref[2] = jnp.ones_like(scale_ref[2])
        sum_ref[...] = jnp.zeros_like(sum_ref)

    @pl.when(step < tiles)
    def _():
        columns = pl.ds(pl.multiple_of(step * TILE, TILE), TILE)
        kind = step // third
        half = total // 2
        for k in (0, 1):
            part = slice(k * half, (k + 1) * half)
            pre_gate = dot_turned(rows_out[part, :], gate_col[...])
            pre_up = dot_turned(rows_out[part, :], up_col[...])
            grads = down_grad[part, :].astype(jnp.float32)
            scale = scale_ref[kind, part, :]
            sigmoid = 1.0 / (1.0 + jnp.exp(-pre_gate))
            silu = pre_gate * sigmoid
            hidden = (silu * pre_up).astype(jnp.bfloat16).astype(jnp.float32)
            sum_ref[kind, part, :] += jnp.sum(hidden * grads, axis=1, keepdims=True)
            grad_hidden = scale * grads
            low_gate = (grad_hidden * pre_up * (sigmoid + silu * (1.0 - sigmoid))).astype(
                jnp.bfloat16
            )
            low_up = (grad_hidden * silu).astype(jnp.bfloat16)
            gate_all[part, columns] = low_gate
            up_all[part, columns] = low_up
            hidden_out[part, :] = (scale * hidden).astype(jnp.bfloat16)
            gate_out[part, :] = low_gate
            up_out[part, :] = low_up

    @pl.when(step == tiles - 1)
    def _():
        grad_logits = jnp.zeros_like(prob_ref)
        for k in (0, 1):
            own = jnp.where(lane == experts_ref[k], 1.0, 0.0)
            grad_logits += scale_ref[k] * sum_ref[k] * (own - prob_ref[...])
        logit_out[...] = grad_logits.astype(jnp.bfloat16)

    @pl.when(step >= tiles)
    def _():
        some = pl.ds(pl.multiple_of((step - tiles) * 2 * TILE, TILE), 2 * TILE)
        grads = wide_dot(gate_all[...], gate_row[...]) + wide_dot(up_all[...], up_row[...])
        grads += dot_turned(logit_out[...], router_ref[some, :])
        grads = grads.astype(jnp.bfloat16)
        for k in range(pieces):
            grad_refs[k][...] = grads[k * size : (k + 1) * size]


def mlp_plane(distance, experts, routed, rows, down_grad, router, weights, kept, others):
    gate, up = weights
    pieces = len(rows)
    width, depth = gate.shape
    size = routed.shape[0] // pieces
    tiles, columns = width // TILE, depth // (2 * TILE)
    total = pieces * size
    low = jnp.bfloat16

    def early(i):
        return jnp.minimum(i, tiles - 1)

    def late(i):
        return jnp.maximum(i - tiles, 0)

    tile_spec = pl.BlockSpec((total, TILE), lambda i: (distance, early(i)))
    anywhere = pl.BlockSpec(memory_space=pl.ANY)
    first_kept = 2 + pieces + 6
    results = pl.pallas_call(
        functools.partial(
            mlp_kernel, tiles, tuple(start for _, start in rows), len(kept) + len(others)
        ),
        grid=(tiles + columns,),
        in_specs=[pl.BlockSpec(memory_space=pltpu.SMEM), whole(routed)]
        + [anywhere] * pieces
        + [
            pl.BlockSpec((depth, 128), lambda i: (0, router.shape[1] // 128 - 1)),
            pl.BlockSpec((TILE, depth), lambda i: (early(i), 0)),
            pl.BlockSpec((TILE, depth), lambda i: (early(i), 0)),
            tile_spec,
            pl.BlockSpec((width, 2 * TILE), lambda i: (0, late(i))),
            pl.BlockSpec((width, 2 * TILE), lambda i: (0, late(i))),
        ]
        + [anywhere] * (len(kept) + len(others)),
        out_specs=[pl.BlockSpec((size, 2 * TILE), lambda i: (0, late(i)))] * pieces
        + [
            pl.BlockSpec((total, depth), lambda i: (distance, 0)),
            tile_spec,
            tile_spec,
            tile_spec,
            pl.BlockSpec((total, 128), lambda i: (distance, 0)),
        ],
        out_shape=[jax.ShapeDtypeStruct((size, depth), low)] * pieces
        + [
            jax.ShapeDtypeStruct((RINGS * total, many), low)
            for many in (depth, width, width, width, 128)
        ],
        scratch_shapes=[pltpu.VMEM((total, width), low)] * 2
        + [
            pltpu.VMEM((total, 128), jnp.float32),
            pltpu.VMEM((3, total, 1), jnp.float32),
            pltpu.VMEM((3, total, 1), jnp.float32),
            pltpu.SemaphoreType.DMA((pieces,)),
        ],
        input_output_aliases={first_kept + k: pieces + k for k in range(len(kept))},
        compiler_params=pltpu.CompilerParams(vmem_limit_bytes=48 * 1024 * 1024),
        cost_estimate=pl.CostEstimate(
            flops=2 * total * depth * width * 4,
            bytes_accessed=2 * (4 * depth * width + 3 * total * depth + 4 * total * width),
            transcendentals=total * width,
        ),
    )(experts, routed, *[array for array, _ in rows], router, gate, up, down_grad, gate, up, *kept, *others)
    return results[:pieces], results[pieces:]


def gather_body(
    block_input,
    segments,
    counts,
    routes,
    attn_gain,
    w_query,
    w_latent,
    latent_gain,
    w_keyval,
    w_output,
    ffn_gain,
    w_router,
    shared_gate_up,
    shared_down,
    expert_gate_up,
    expert_down,
    cotangent,
):
    f32 = jnp.float32
    bf16 = jnp.bfloat16
    blocks = 16
    index = lax.axis_index("dp")
    x = lax.axis_index("tensor")
    coords = jnp.stack([index // 4, (index // 2) % 2, index % 2]).astype(jnp.int32)
    core = coords[2]
    place = jnp.concatenate([coords, x.astype(jnp.int32)[None], counts])
    local_rows = block_input.shape[0]
    tokens = 2 * local_rows
    depth = w_query.shape[0]
    query_width = w_query.shape[1]
    heads = query_width // (NOPE + ROPE)
    experts = w_router.shape[1]
    units = expert_gate_up.shape[3]
    shared = shared_gate_up.shape[2] // blocks
    latent_depth = w_keyval.shape[0]

    used = query_width + KVR + ROPE
    small = jnp.concatenate(
        [
            attn_gain[:, None],
            ffn_gain[:, None],
            jnp.pad(latent_gain, (0, depth - latent_depth))[:, None],
            w_router,
            routes.reshape(depth, -1).astype(bf16),
            jnp.zeros((depth, 128 - ROPE - 3 - experts - 2 * TOP), bf16),
        ],
        axis=1,
    )
    first_width = query_width + KVR + 128
    shards = pack_weights(w_query, w_latent, small, w_keyval, w_output)
    other_input = other_x(block_input)
    expert_in = expert_gate_up.swapaxes(2, 3)
    expert_in_other = other_core(expert_in)
    expert_down_other = other_core(expert_down)
    chunks, held, besides = gather_weight(
        shards, (expert_in_other, expert_down_other, other_input)
    )
    shared_near = lax.all_to_all(
        pack_shared(shared_gate_up, shared_down, blocks, (held[3],)),
        "dp",
        split_axis=0,
        concat_axis=0,
        tiled=True,
    )
    shared_far = other_core(shared_near)

    grad_groups, grad_ring, grad_across = gather_whole(
        after(cotangent, held[3], besides[2]), besides[3]
    )

    cosine, sine = rotary_tables(segments[0], ROPE)
    cosine = jnp.tile(cosine, (1, heads))
    sine = jnp.tile(sine, (1, heads))
    sizes = (depth, query_width, used, latent_depth, w_keyval.shape[1] * latent_depth // depth, first_width)
    (
        own_part,
        sent_part,
        first_weight,
        keyval_weight,
        output_turned,
        first_normed,
        nope,
        turned_query,
        latent,
        key,
        keyval,
        total,
        attended,
        gains,
        latent_gain_row,
    ) = attend_forward(
        place,
        segments,
        cosine,
        sine,
        block_input,
        other_input,
        chunks,
        heads,
        sizes,
        (grad_ring[2], grad_across[0], grad_across[1]),
    )
    attn_gain_wide, ffn_gain_wide = gains[0], gains[1]
    mixed = block_input.astype(f32) + own_part + other_x(sent_part).astype(f32)
    second_scale = rms_scale(mixed)
    second_unit = mixed * second_scale
    second_normed = (second_unit * ffn_gain_wide).astype(bf16)

    routes_at = used + 3 + experts
    routes_all = first_weight[:, routes_at : routes_at + 2 * TOP].reshape(blocks * tokens, TOP)
    chip_experts = jnp.stack([index, index + 1 - 2 * core]).astype(jnp.int32)
    routed_all = jnp.any(
        routes_all[None] == chip_experts[:, None, None].astype(bf16), axis=2
    ).astype(f32)
    order = jnp.stack(
        [
            place_of(coords, (distance, flip_y, 0)) * 2 + (1 - x if flip_x else x)
            for distance in range(RINGS)
            for flip_x, flip_y in ((0, 0), (0, 1), (1, 0), (1, 1))
        ]
    )
    routed = jnp.stack(
        [
            pick_blocks(one.reshape(blocks * 2, local_rows), order).reshape(RINGS, -1)
            for one in routed_all
        ],
        axis=2,
    )

    corners = "yxyx"
    row_ring, row_groups = gather_rows(second_normed, "yyx")
    row_planes = [
        [(array, 0) for array in row_groups[0]],
        [(array, 0) for array in row_groups[1]],
        [(array, 0) for array in row_groups[2]],
        [(array, local_rows) for array in row_groups[2]],
    ]

    gate_weight, up_weight, down_weight = pack_units(
        expert_in,
        expert_in_other,
        expert_down,
        expert_down_other,
        shared_near,
        shared_far,
        shared,
        (second_normed,),
    )
    half_kept = down_grads(
        0,
        [(array, r * local_rows) for r in (0, 1) for array in grad_groups[0]],
        local_rows,
        down_weight,
        (),
        (row_ring[1],),
    )
    down_grad, every_grad = down_grads(
        1,
        [(array, r * local_rows) for r in (0, 1) for array in grad_groups[1]],
        local_rows,
        down_weight,
        half_kept,
        (row_ring[2],),
    )
    expert_ids = jnp.concatenate(
        [chip_experts, jnp.array([experts, used + 3 - query_width - KVR], jnp.int32)]
    )
    kept = []
    planes = []
    turned, closed = [None] * RINGS, [None] * RINGS
    for distance in range(RINGS):
        others = [row_ring[3]] if distance == 0 else []
        if distance == 1:
            others = list(row_groups[2][1:3])
        elif distance == 3:
            others = list(turned[0][1:])
        grads, kept = mlp_plane(
            distance,
            expert_ids,
            routed[distance],
            row_planes[distance],
            down_grad,
            first_weight,
            (gate_weight, up_weight),
            kept,
            others,
        )
        planes.append(list(grads))
        if distance:
            before = planes[distance - 1]
            k = 1 if corners[distance - 1] == "x" else 2
            before[k] = after(before[k], grads[3])
            turned[distance - 1] = turn_corner(before, corners[distance - 1])
            closed[distance - 1] = close_plane(turned[distance - 1])
    turned[3] = turn_corner(planes[3], corners[3])
    first_part = closed[1]
    closed[1] = (after(first_part[0], planes[3][3]),) + tuple(first_part[1:])
    every_row, every_hidden, every_gate_grad, every_up_grad, logit_grads = kept
    first_total = wide_sum(*closed[1]).astype(bf16)
    half_outs, half_done = out_rows(4, 0, every_hidden, down_weight, (), (first_total,))
    outs, outs_done = out_rows(4, 1, every_hidden, down_weight, half_outs, (half_done,))
    outs = list(outs)
    shared_kept, shared_sent, logit_rows = side_grads(
        every_row,
        every_grad,
        every_gate_grad,
        every_up_grad,
        every_hidden,
        logit_grads,
        shared,
        blocks,
        (outs_done,),
    )
    moving = ring_step(first_total)
    moving = ring_step(wide_sum(moving, *closed[2]).astype(bf16))
    own, beside, across = turned[3]
    grad_close = close_plane((after(own, outs_done), after(beside, half_done), across))
    grad_second = wide_sum(
        ring_step(wide_sum(moving, *grad_close).astype(bf16)),
        after(closed[0][0], shared_sent),
        *closed[0][1:],
    )
    outs[3] = after(outs[3], grad_close[2])

    router_at = used + 3 - query_width - KVR
    grad_router = logit_rows[router_at : router_at + experts]
    shared_came = other_core(shared_sent)

    gain_ffn_part = jnp.sum(grad_second * second_unit, axis=0)
    grad_mixed = cotangent.astype(f32) + rms_back(
        grad_second * ffn_gain_wide, second_unit, second_scale
    )
    grad_mixed_low = grad_mixed.astype(bf16)
    other_grad = other_x(grad_mixed_low)
    outs[2] = after(outs[2], other_grad)
    sent_down = expert_grads(
        (every_hidden,), every_grad, units, 1, None, bf16, (grad_mixed_low,)
    )
    arrived_down = other_core(sent_down)

    places = jnp.stack([place_of(coords, key_of) for key_of in weight_keys()]).astype(jnp.int32)
    projected_grad, keyval_grad, latent_normed, gain_latent_part = attend_back(
        place,
        segments,
        cosine,
        sine,
        grad_mixed_low,
        other_grad,
        (keyval_weight, output_turned, nope, turned_query, latent, key, keyval, total, latent_gain_row),
        heads,
        first_width,
        (sent_down,),
    )
    grad_attn = jnp.concatenate(
        [
            jnp.where(x == 0, grad_mixed_low, other_grad),
            jnp.where(x == 0, other_grad, grad_mixed_low),
        ],
        axis=0,
    )
    ring_places = places.reshape(2, 2, RINGS).swapaxes(1, 2).reshape(-1)
    other_parts = (latent_normed, keyval_grad, grad_attn, attended, ring_places)
    own_first, sent_first, gain_attn_part = first_back(
        place, block_input, other_input, projected_grad, first_weight
    )
    grad_first = own_first + other_x(sent_first).astype(f32)
    small_rows = jnp.concatenate(
        [
            jnp.zeros((ROPE, D), f32),
            gain_attn_part,
            gain_ffn_part[None],
            jnp.pad(
                gain_latent_part.reshape(blocks, latent_depth),
                ((0, 0), (0, depth - latent_depth)),
            ).reshape(1, D),
            grad_router,
            jnp.zeros((128 - ROPE - 3 - experts, D), f32),
        ],
        axis=0,
    )
    first_parts = (first_normed, projected_grad, small_rows, places)
    outs[1] = after(outs[1], projected_grad)
    out_turned = turn_corner(outs, "x")
    first_sent = first_grads(*first_parts, 8, 8, None, (out_turned[1],))
    first_arrived = other_core(first_sent)
    other_arrived = other_core(other_grads(*other_parts, 8, 8, None, (first_sent,)))
    shared_grads = lax.all_to_all(
        add_low(after(shared_kept, projected_grad), shared_came),
        "dp",
        split_axis=0,
        concat_axis=0,
        tiled=True,
    )
    far = first_grads(*first_parts, 4, 4, first_arrived, (shared_grads,))
    other_kept = other_grads(*other_parts, 0, 8, other_arrived, (far,))
    from_y = other_y(far)
    sent_in = expert_grads(
        (every_gate_grad, every_up_grad), every_row, units, 1, None, bf16, (far,)
    )
    arrived_in = other_core(sent_in)
    out_own, out_beside, out_across = close_plane(out_turned)
    out_total = wide_sum(after(out_own, sent_in), out_beside, out_across)
    block_output = mixed + ring_sum(
        [out_total[r * local_rows : (r + 1) * local_rows] for r in range(RINGS)], bf16
    )
    near = first_grads(*first_parts, 0, 4, first_arrived)
    other_summed = ring_sum(
        [other_kept[2 * r * depth : 2 * (r + 1) * depth] for r in range(RINGS)], bf16
    )
    grad_expert_down = expert_grads(
        (every_hidden,), every_grad, units, 0, arrived_down, f32, (from_y,)
    )
    grad_expert_in = expert_grads(
        (every_gate_grad, every_up_grad), every_row, units, 0, arrived_in, f32, (near,)
    )
    first_closed = close_ring(near, from_y, grad_expert_in)
    other_closed = other_summed[:depth] + other_y(
        other_summed[depth:].astype(bf16)
    ).astype(f32)
    grad_shared_in, grad_shared_down = unpack_shared(shared_grads, shared, (from_y,))
    grad_expert_gate_up = grad_expert_in.swapaxes(2, 3)
    grad_expert_down = grad_expert_down[0]
    nope_width = heads * NOPE
    span = heads * (ROPE // 2)
    grad_query_weight = jnp.concatenate(
        [
            first_closed[:, :nope_width].reshape(depth, heads, NOPE),
            first_closed[:, nope_width : nope_width + span].reshape(depth, heads, -1),
            first_closed[:, nope_width + span : query_width].reshape(depth, heads, -1),
        ],
        axis=2,
    ).reshape(depth, query_width)
    both = first_closed[:, query_width:]
    both = both + other_x(both)
    grad_latent_weight = both[:, : KVR + ROPE]
    small_grads = both[:, KVR + ROPE :].T
    keyval_columns = w_keyval.shape[1] * latent_depth // depth
    grad_keyval_weight = (
        other_closed[:, :keyval_columns]
        .reshape(-1, latent_depth, keyval_columns)
        .transpose(1, 0, 2)
        .reshape(latent_depth, -1)
    )
    grad_output_weight = other_closed[:, keyval_columns:].T
    own_inputs = block_input.astype(f32)
    own_scale = rms_scale(own_inputs)
    own_unit = own_inputs * own_scale
    grad_input = grad_mixed + rms_back(grad_first * attn_gain_wide, own_unit, own_scale)
    return (
        block_output,
        grad_input,
        small_grads[0],
        grad_query_weight,
        grad_latent_weight,
        small_grads[2, :latent_depth],
        grad_keyval_weight,
        grad_output_weight,
        small_grads[1],
        small_grads[3 : 3 + experts].T,
        grad_shared_in,
        grad_shared_down,
        grad_expert_gate_up,
        grad_expert_down,
    )


def solution(mesh):
    in_specs = (
        P(("dp", "tensor"), None),
        P("dp", None),
        P("dp"),
        P("dp", None),
        P("dp"),
        P("dp", "tensor"),
        P("dp", None),
        P("dp"),
        P("dp", "tensor"),
        P("tensor", "dp"),
        P("dp"),
        P("dp", None),
        P(None, "dp", "tensor"),
        P("tensor", "dp"),
        P("dp", None, None, "tensor"),
        P("dp", "tensor", None),
        P(("dp", "tensor"), None),
    )
    out_specs = (
        P(("dp", "tensor"), None),
        P(("dp", "tensor"), None),
        P("dp"),
        P("dp", "tensor"),
        P("dp", None),
        P("dp"),
        P("dp", "tensor"),
        P("tensor", "dp"),
        P("dp"),
        P("dp", None),
        P(None, "dp", "tensor"),
        P("tensor", "dp"),
        P("dp", None, None, "tensor"),
        P("dp", "tensor", None),
    )
    body = gather_body if mesh.shape["dp"] == 16 else exchange_body
    return jax.shard_map(body, mesh=mesh, in_specs=in_specs, out_specs=out_specs, check_vma=False)
```

```python
import functools
import math

import jax
import jax.numpy as jnp
from jax import lax
from jax.experimental import pallas as pl
from jax.experimental.pallas import tpu as pltpu
from jax.sharding import PartitionSpec as P

D = 2048
NOPE = 128
ROPE = 64
VD = 128
KVR = 512
TOP = 6


EPSILON = 1e-06


def rms_scale(values):
    return lax.rsqrt(jnp.mean(values * values, axis=-1, keepdims=True) + EPSILON)


def rms_back(grad_unit, unit_rows, row_scale):
    return row_scale * (
        grad_unit - unit_rows * jnp.mean(grad_unit * unit_rows, axis=-1, keepdims=True)
    )


def rotary_tables(segment_row, width):
    count = segment_row.shape[0]
    position = jnp.arange(count, dtype=jnp.int32)
    same = segment_row[:, None] == segment_row[None, :]
    start = jnp.min(jnp.where(same, position[None, :], count), axis=1)
    offset = (position - start).astype(jnp.float32)
    freq = jnp.exp(jnp.arange(width // 2, dtype=jnp.float32) * (-2.0 * math.log(10000.0) / width))
    angle = offset[:, None] * freq[None, :]
    return (jnp.cos(angle), jnp.sin(angle))


def rotate(values, cosine, sine):
    half = values.shape[-1] // 2
    first = values[..., :half]
    second = values[..., half:]
    return jnp.concatenate(
        [first * cosine - second * sine, second * cosine + first * sine], axis=-1
    )


def rotate_back(grads, cosine, sine):
    half = grads.shape[-1] // 2
    first = grads[..., :half]
    second = grads[..., half:]
    return jnp.concatenate(
        [first * cosine + second * sine, second * cosine - first * sine], axis=-1
    )


def allowed_pairs(segment_row, count):
    position = jnp.arange(segment_row.shape[0], dtype=jnp.int32)
    live = position < count
    same = segment_row[:, None] == segment_row[None, :]
    causal = position[None, :] <= position[:, None]
    return same & causal & live[:, None] & live[None, :] | (position[:, None] == position[None, :])


def attention_scores(query_rows, key_nope, key_rope, allowed, scale):
    scores = jnp.einsum(
        "ihd,jhd->hij", query_rows[..., :NOPE], key_nope, preferred_element_type=jnp.float32
    )
    scores = scores + jnp.einsum(
        "ihd,jd->hij", query_rows[..., NOPE:], key_rope, preferred_element_type=jnp.float32
    )
    return jnp.where(allowed[None], scores * scale, -1e30)


def swiglu_back(gate, upper, grad_hidden, axis):
    sigmoid = jax.nn.sigmoid(gate)
    grad_gate = grad_hidden * upper * sigmoid * (1.0 + gate * (1.0 - sigmoid))
    grad_upper = grad_hidden * gate * sigmoid
    return jnp.stack([grad_gate, grad_upper], axis=axis)


def slot_layout(routes, experts, capacity):
    tokens = routes.shape[0]
    flat = routes.reshape(-1)
    onehot = (flat[:, None] == jnp.arange(experts, dtype=jnp.int32)[None, :]).astype(jnp.int32)
    rank = jnp.arange(flat.shape[0], dtype=jnp.int32)
    earlier = (rank[None, :] < rank[:, None]).astype(jnp.bfloat16)
    before = jnp.dot(
        earlier, onehot.astype(jnp.bfloat16), preferred_element_type=jnp.float32
    ).astype(jnp.int32)
    slot_index = jnp.sum(before * onehot, axis=1)
    target = flat * capacity + slot_index
    token_ids = jnp.arange(flat.shape[0], dtype=jnp.int32) // routes.shape[1]
    owner = jnp.full((experts * capacity,), tokens, jnp.int32).at[target].set(token_ids)
    return (slot_index, target, owner)


def to_expert_major(arrived, groups, local_experts):
    capacity = arrived.shape[1]
    width = arrived.shape[2]
    return (
        arrived.reshape(groups, local_experts, capacity, width)
        .transpose(1, 0, 2, 3)
        .reshape(local_experts, groups * capacity, width)
    )


def from_expert_major(results, groups):
    local_experts = results.shape[0]
    width = results.shape[2]
    capacity = results.shape[1] // groups
    return (
        results.reshape(local_experts, groups, capacity, width)
        .transpose(1, 0, 2, 3)
        .reshape(groups * local_experts, capacity, width)
    )


def exchange_body(
    block_input,
    segments,
    counts,
    routes,
    attn_gain,
    w_query,
    w_latent,
    latent_gain,
    w_keyval,
    w_output,
    ffn_gain,
    w_router,
    shared_gate_up,
    shared_down,
    expert_gate_up,
    expert_down,
    cotangent,
):
    gathered = (
        lax.all_gather(attn_gain, "dp", axis=0, tiled=True),
        lax.all_gather(w_query, "dp", axis=0, tiled=True),
        lax.all_gather(w_latent, "dp", axis=0, tiled=True),
        lax.all_gather(latent_gain, "dp", axis=0, tiled=True),
        lax.all_gather(w_keyval, "dp", axis=0, tiled=True),
        lax.all_gather(w_output, "dp", axis=1, tiled=True),
        lax.all_gather(ffn_gain, "dp", axis=0, tiled=True),
        lax.all_gather(w_router, "dp", axis=0, tiled=True),
        lax.all_gather(shared_gate_up, "dp", axis=1, tiled=True),
        lax.all_gather(shared_down, "dp", axis=1, tiled=True),
    )
    (
        full_attn_gain,
        query_weight,
        latent_weight,
        full_latent_gain,
        keyval_weight,
        output_weight,
        full_ffn_gain,
        router_weight,
        shared_in,
        shared_out,
    ) = gathered
    tensor_rank = lax.axis_index("tensor")
    dp_size = lax.axis_size("dp")
    rows_all = lax.all_gather(block_input, "tensor", axis=0, tiled=True)
    tokens = rows_all.shape[0]
    local_rows = block_input.shape[0]
    heads = query_weight.shape[1] // (NOPE + ROPE)
    experts = router_weight.shape[1]
    local_experts = expert_gate_up.shape[0]
    capacity = 2 * tokens * TOP // experts
    scale = (NOPE + ROPE) ** (-0.5)
    start = tensor_rank * local_rows
    cosine, sine = rotary_tables(segments[0], ROPE)
    allowed = allowed_pairs(segments[0], counts[0])
    attn_gain_wide = full_attn_gain.astype(jnp.float32)
    latent_gain_wide = full_latent_gain.astype(jnp.float32)
    ffn_gain_wide = full_ffn_gain.astype(jnp.float32)
    inputs = rows_all.astype(jnp.float32)
    first_scale = rms_scale(inputs)
    first_unit = inputs * first_scale
    first_normed = (first_unit * attn_gain_wide).astype(jnp.bfloat16)
    query = jnp.dot(first_normed, query_weight, preferred_element_type=jnp.float32).reshape(
        tokens, heads, NOPE + ROPE
    )
    query_rows = jnp.concatenate(
        [query[..., :NOPE], rotate(query[..., NOPE:], cosine[:, None, :], sine[:, None, :])],
        axis=-1,
    ).astype(jnp.bfloat16)
    latent_all = jnp.dot(first_normed, latent_weight, preferred_element_type=jnp.float32)
    latent = latent_all[:, :KVR]
    key_rope = rotate(latent_all[:, KVR:], cosine, sine).astype(jnp.bfloat16)
    latent_scale = rms_scale(latent)
    latent_unit = latent * latent_scale
    latent_normed = (latent_unit * latent_gain_wide).astype(jnp.bfloat16)
    keyval = (
        jnp.dot(latent_normed, keyval_weight, preferred_element_type=jnp.float32)
        .astype(jnp.bfloat16)
        .reshape(tokens, heads, NOPE + VD)
    )
    key_nope = keyval[..., :NOPE]
    values = keyval[..., NOPE:]
    scores = attention_scores(query_rows, key_nope, key_rope, allowed, scale)
    row_max = jnp.max(scores, axis=-1, keepdims=True)
    log_total = row_max + jnp.log(jnp.sum(jnp.exp(scores - row_max), axis=-1, keepdims=True))
    weights_low = jnp.exp(scores - log_total).astype(jnp.bfloat16)
    attended = (
        jnp.einsum("hij,jhd->ihd", weights_low, values, preferred_element_type=jnp.float32)
        .astype(jnp.bfloat16)
        .reshape(tokens, heads * VD)
    )
    attn_part = jnp.dot(attended, output_weight, preferred_element_type=jnp.float32)
    mixed = inputs + lax.psum(attn_part, "tensor")
    second_scale = rms_scale(mixed)
    second_unit = mixed * second_scale
    second_normed = (second_unit * ffn_gain_wide).astype(jnp.bfloat16)
    logits = jnp.dot(second_normed, router_weight, preferred_element_type=jnp.float32)
    probabilities = jax.nn.softmax(logits, axis=-1)
    gate_values = jnp.take_along_axis(probabilities, routes, axis=1)
    shared_pre = jnp.einsum(
        "td,gdf->tgf", second_normed, shared_in, preferred_element_type=jnp.float32
    )
    shared_hidden = (jax.nn.silu(shared_pre[:, 0]) * shared_pre[:, 1]).astype(jnp.bfloat16)
    shared_part = jnp.dot(shared_hidden, shared_out, preferred_element_type=jnp.float32)
    slot_index, target, owner = slot_layout(routes, experts, capacity)
    owner_grid = owner.reshape(experts, capacity)
    padded_rows = jnp.concatenate([second_normed, jnp.zeros((1, D), jnp.bfloat16)], axis=0)
    outgoing = padded_rows[owner_grid]
    arrived = lax.all_to_all(outgoing, "dp", split_axis=0, concat_axis=0, tiled=True)
    expert_rows = to_expert_major(arrived, dp_size, local_experts)
    expert_pre = jnp.einsum(
        "erd,egdf->ergf", expert_rows, expert_gate_up, preferred_element_type=jnp.float32
    )
    expert_hidden = (jax.nn.silu(expert_pre[:, :, 0]) * expert_pre[:, :, 1]).astype(jnp.bfloat16)
    expert_result = jnp.einsum(
        "erf,efd->erd", expert_hidden, expert_down, preferred_element_type=jnp.float32
    )
    returning = from_expert_major(expert_result, dp_size)
    returned = lax.all_to_all(
        returning.astype(jnp.bfloat16), "dp", split_axis=0, concat_axis=0, tiled=True
    ).astype(returning.dtype)
    padded_back = jnp.concatenate([returned.reshape(-1, D), jnp.zeros((1, D), jnp.float32)], axis=0)
    picked = padded_back[target].reshape(tokens, TOP, D)
    routed_part = jnp.sum(gate_values[:, :, None] * picked, axis=1)
    branch_sum = lax.psum_scatter(
        (shared_part + routed_part).astype(jnp.bfloat16), "tensor", scatter_dimension=0, tiled=True
    ).astype(jnp.float32)
    block_output = lax.dynamic_slice_in_dim(mixed, start, local_rows, 0) + branch_sum
    grad_rows = lax.all_gather(cotangent, "tensor", axis=0, tiled=True)
    grad_out = grad_rows.astype(jnp.float32)
    grad_shared_hidden = jnp.dot(grad_rows, shared_out.T, preferred_element_type=jnp.float32)
    grad_shared_out = jnp.dot(shared_hidden.T, grad_rows, preferred_element_type=jnp.float32)
    grad_shared_pre = swiglu_back(shared_pre[:, 0], shared_pre[:, 1], grad_shared_hidden, 1).astype(
        jnp.bfloat16
    )
    grad_shared_in = jnp.einsum(
        "td,tgf->gdf", second_normed, grad_shared_pre, preferred_element_type=jnp.float32
    )
    grad_second = jnp.einsum(
        "tgf,gdf->td", grad_shared_pre, shared_in, preferred_element_type=jnp.float32
    )
    gate_by_slot = (
        jnp.zeros((experts * capacity + 1,), jnp.float32).at[target].set(gate_values.reshape(-1))
    )
    slot_ids = jnp.arange(experts * capacity, dtype=jnp.int32).reshape(experts, capacity)
    padded_grad = jnp.concatenate([grad_out, jnp.zeros((1, D), jnp.float32)], axis=0)
    grad_outgoing = (gate_by_slot[slot_ids][..., None] * padded_grad[owner_grid]).astype(
        jnp.bfloat16
    )
    grad_arrived = lax.all_to_all(grad_outgoing, "dp", split_axis=0, concat_axis=0, tiled=True)
    grad_expert_rows = to_expert_major(grad_arrived, dp_size, local_experts)
    grad_expert_hidden = jnp.einsum(
        "erd,efd->erf", grad_expert_rows, expert_down, preferred_element_type=jnp.float32
    )
    grad_expert_down = jnp.einsum(
        "erf,erd->efd", expert_hidden, grad_expert_rows, preferred_element_type=jnp.float32
    )
    grad_expert_pre = swiglu_back(
        expert_pre[:, :, 0], expert_pre[:, :, 1], grad_expert_hidden, 2
    ).astype(jnp.bfloat16)
    grad_expert_gate_up = jnp.einsum(
        "erd,ergf->egdf", expert_rows, grad_expert_pre, preferred_element_type=jnp.float32
    )
    grad_expert_input = jnp.einsum(
        "ergf,egdf->erd", grad_expert_pre, expert_gate_up, preferred_element_type=jnp.float32
    )
    grad_returning = from_expert_major(grad_expert_input, dp_size)
    grad_returned = lax.all_to_all(
        grad_returning.astype(jnp.bfloat16), "dp", split_axis=0, concat_axis=0, tiled=True
    ).astype(grad_returning.dtype)
    padded_grad_back = jnp.concatenate(
        [grad_returned.reshape(-1, D), jnp.zeros((1, D), jnp.float32)], axis=0
    )
    grad_second = grad_second + jnp.sum(padded_grad_back[target].reshape(tokens, TOP, D), axis=1)
    grad_gates = jnp.sum(grad_out[:, None, :] * picked, axis=-1)
    grad_second, grad_gates = (
        lax.psum(grad_second.astype(jnp.bfloat16), "tensor").astype(jnp.float32),
        lax.psum(grad_gates.astype(jnp.bfloat16), "tensor").astype(jnp.float32),
    )
    chosen = (routes[:, :, None] == jnp.arange(experts, dtype=jnp.int32)[None, None, :]).astype(
        jnp.float32
    )
    grad_probabilities = jnp.sum(chosen * grad_gates[:, :, None], axis=1)
    grad_logits = probabilities * (
        grad_probabilities - jnp.sum(probabilities * grad_probabilities, axis=-1, keepdims=True)
    )
    grad_logits_low = grad_logits.astype(jnp.bfloat16)
    grad_router = jnp.dot(second_normed.T, grad_logits_low, preferred_element_type=jnp.float32)
    grad_second = grad_second + jnp.dot(
        grad_logits_low, router_weight.T, preferred_element_type=jnp.float32
    )
    gain_ffn_grad = jnp.sum(grad_second * second_unit, axis=0)
    grad_mixed = grad_out + rms_back(grad_second * ffn_gain_wide, second_unit, second_scale)
    grad_attn_low = grad_mixed.astype(jnp.bfloat16)
    grad_output_weight = jnp.dot(attended.T, grad_attn_low, preferred_element_type=jnp.float32)
    grad_attended = (
        jnp.dot(grad_attn_low, output_weight.T, preferred_element_type=jnp.float32)
        .astype(jnp.bfloat16)
        .reshape(tokens, heads, VD)
    )
    scores = attention_scores(query_rows, key_nope, key_rope, allowed, scale)
    weights = jnp.exp(scores - log_total)
    weights_low = weights.astype(jnp.bfloat16)
    grad_weights = jnp.einsum(
        "ihd,jhd->hij", grad_attended, values, preferred_element_type=jnp.float32
    )
    grad_values = jnp.einsum(
        "hij,ihd->jhd", weights_low, grad_attended, preferred_element_type=jnp.float32
    )
    grad_scores = (
        weights * (grad_weights - jnp.sum(weights * grad_weights, axis=-1, keepdims=True))
    ).astype(jnp.bfloat16)
    grad_query_nope = (
        jnp.einsum("hij,jhd->ihd", grad_scores, key_nope, preferred_element_type=jnp.float32)
        * scale
    )
    grad_query_rope = (
        jnp.einsum("hij,jd->ihd", grad_scores, key_rope, preferred_element_type=jnp.float32) * scale
    )
    grad_key_nope = (
        jnp.einsum(
            "hij,ihd->jhd", grad_scores, query_rows[..., :NOPE], preferred_element_type=jnp.float32
        )
        * scale
    )
    grad_key_rope = (
        jnp.einsum(
            "hij,ihd->jd", grad_scores, query_rows[..., NOPE:], preferred_element_type=jnp.float32
        )
        * scale
    )
    grad_query = (
        jnp.concatenate(
            [grad_query_nope, rotate_back(grad_query_rope, cosine[:, None, :], sine[:, None, :])],
            axis=-1,
        )
        .astype(jnp.bfloat16)
        .reshape(tokens, heads * (NOPE + ROPE))
    )
    grad_query_weight = jnp.dot(first_normed.T, grad_query, preferred_element_type=jnp.float32)
    grad_first = jnp.dot(grad_query, query_weight.T, preferred_element_type=jnp.float32)
    grad_keyval = (
        jnp.concatenate([grad_key_nope, grad_values], axis=-1)
        .astype(jnp.bfloat16)
        .reshape(tokens, heads * (NOPE + VD))
    )
    grad_keyval_weight = jnp.dot(latent_normed.T, grad_keyval, preferred_element_type=jnp.float32)
    grad_latent_normed = jnp.dot(grad_keyval, keyval_weight.T, preferred_element_type=jnp.float32)
    gain_latent_part = jnp.sum(grad_latent_normed * latent_unit, axis=0)
    grad_latent = rms_back(grad_latent_normed * latent_gain_wide, latent_unit, latent_scale)
    grad_latent_all = jnp.concatenate(
        [grad_latent, rotate_back(grad_key_rope, cosine, sine)], axis=-1
    )
    grad_first, grad_latent_all, gain_latent_grad = (
        lax.psum(grad_first.astype(jnp.bfloat16), "tensor").astype(jnp.float32),
        lax.psum(grad_latent_all.astype(jnp.bfloat16), "tensor").astype(jnp.float32),
        lax.psum(gain_latent_part.astype(jnp.bfloat16), "tensor").astype(jnp.float32),
    )
    grad_latent_low = grad_latent_all.astype(jnp.bfloat16)
    grad_latent_weight = jnp.dot(
        first_normed.T, grad_latent_low, preferred_element_type=jnp.float32
    )
    grad_first = grad_first + jnp.dot(
        grad_latent_low, latent_weight.T, preferred_element_type=jnp.float32
    )
    gain_attn_grad = jnp.sum(grad_first * first_unit, axis=0)
    grad_inputs = grad_mixed + rms_back(grad_first * attn_gain_wide, first_unit, first_scale)
    grad_local = lax.dynamic_slice_in_dim(grad_inputs, start, local_rows, 0)
    summed = (
        lax.psum_scatter(gain_attn_grad, "dp", scatter_dimension=0, tiled=True),
        lax.psum_scatter(grad_query_weight, "dp", scatter_dimension=0, tiled=True),
        lax.psum_scatter(grad_latent_weight, "dp", scatter_dimension=0, tiled=True),
        lax.psum_scatter(gain_latent_grad, "dp", scatter_dimension=0, tiled=True),
        lax.psum_scatter(grad_keyval_weight, "dp", scatter_dimension=0, tiled=True),
        lax.psum_scatter(grad_output_weight, "dp", scatter_dimension=1, tiled=True),
        lax.psum_scatter(gain_ffn_grad, "dp", scatter_dimension=0, tiled=True),
        lax.psum_scatter(grad_router, "dp", scatter_dimension=0, tiled=True),
        lax.psum_scatter(grad_shared_in, "dp", scatter_dimension=1, tiled=True),
        lax.psum_scatter(grad_shared_out, "dp", scatter_dimension=1, tiled=True),
    )
    return (
        block_output,
        grad_local,
        summed[0],
        summed[1],
        summed[2],
        summed[3],
        summed[4],
        summed[5],
        summed[6],
        summed[7],
        summed[8],
        summed[9],
        grad_expert_gate_up,
        grad_expert_down,
    )


RINGS = 4


def ring_step(values):
    return lax.ppermute(values, "dp", [(i, (i + RINGS) % 16) for i in range(16)])


def other_y(values):
    return lax.ppermute(values, "dp", [(i, i ^ 2) for i in range(16)])


def other_core(values):
    return lax.ppermute(values, "dp", [(i, i ^ 1) for i in range(16)])


def other_x(values):
    return lax.ppermute(values, "tensor", [(0, 1), (1, 0)])


def fence_kernel(*refs):
    pass


def after(values, *others):
    anywhere = pl.BlockSpec(memory_space=pl.ANY)
    return pl.pallas_call(
        fence_kernel,
        out_shape=jax.ShapeDtypeStruct(values.shape, values.dtype),
        in_specs=[anywhere] * (1 + len(others)),
        out_specs=anywhere,
        input_output_aliases={0: 0},
    )(values, *others)


def gather_whole(rows, early):
    ring = [rows, ring_step(rows)]
    ring.append(ring_step(ring[1]))
    ring.append(ring_step(after(ring[2], early)))
    over_x = [other_x(part) for part in ring]
    groups = []
    for k in (0, 2):
        held = jnp.concatenate(ring[k : k + 2], axis=0)
        across = jnp.concatenate(over_x[k : k + 2], axis=0)
        beside = other_y(held)
        groups.append((held, beside, across, other_y(across) if k else other_x(beside)))
    return groups, ring, over_x


def gather_rows(rows, corners):
    held = [rows, ring_step(rows)]
    first = (other_y(rows), other_x(rows))
    held.append(ring_step(after(held[1], *first)))
    held.append(ring_step(held[2]))
    groups = []
    for k, current in enumerate((held[0], held[1], jnp.concatenate(held[2:], axis=0))):
        beside, across = (other_y(current), other_x(current)) if k else first
        corner = other_x(beside) if corners[k] == "x" else other_y(across)
        groups.append((current, beside, across, corner))
    return held, groups


def add_low(first, second):
    return (first.astype(jnp.float32) + second.astype(jnp.float32)).astype(jnp.bfloat16)


def turn_corner(plane, direction):
    own, beside, across, corner = plane
    if direction == "x":
        return own, add_low(beside, other_x(corner)), across
    return own, beside, add_low(across, other_y(corner))


def close_plane(turned):
    own, beside, across = turned
    return own, other_y(beside), other_x(across)


def wide_sum(*values):
    total = values[0].astype(jnp.float32)
    for value in values[1:]:
        total = total + value.astype(jnp.float32)
    return total


def ring_sum(parts, low):
    moving = parts[1]
    for distance in (2, 3, 0):
        moving = ring_step(moving.astype(low)).astype(jnp.float32) + parts[distance].astype(
            jnp.float32
        )
    return moving


def ring_shards(shard):
    held = [shard]
    for _ in range(RINGS - 1):
        held.append(ring_step(held[-1]))
    return held


def gather_weight(shard, early):
    held, besides = [shard], []
    for distance in range(RINGS):
        beside = other_y(after(held[1], *early) if distance == 1 else held[distance])
        besides.append(beside)
        if distance < RINGS - 1:
            source = after(held[distance], besides[distance - 1]) if distance else shard
            held.append(ring_step(source))
    chunks = []
    for distance, (current, beside) in enumerate(zip(held, besides)):
        for flip_y, chunk in ((0, current), (1, beside)):
            for flip_core, piece in ((0, chunk), (1, other_core(chunk))):
                chunks.append(((distance, flip_y, flip_core), piece))
    return chunks, held, besides


def place_of(coords, key):
    z, y, core = coords
    distance, flip_y, flip_core = key
    return (
        lax.rem(z + RINGS - distance, RINGS) * 4
        + (1 - y if flip_y else y) * 2
        + (1 - core if flip_core else core)
    )


def weight_keys():
    return [
        (distance, flip_y, flip_core)
        for flip_core in (0, 1)
        for flip_y in (0, 1)
        for distance in range(RINGS)
    ]


def scatter_blocks(grads, low):
    half = grads.shape[0] // 2
    total = grads[:half].astype(jnp.float32) + other_core(grads[half:].astype(low)).astype(
        jnp.float32
    )
    quarter = half // 2
    total = total[:quarter] + other_y(total[quarter:].astype(low)).astype(jnp.float32)
    size = quarter // RINGS
    return ring_sum([total[r * size : (r + 1) * size] for r in range(RINGS)], low)


def pick_blocks(values, order):
    chosen = order[:, None] == jnp.arange(values.shape[0], dtype=jnp.int32)[None, :]
    chosen = chosen.reshape(chosen.shape + (1,) * (values.ndim - 1))
    return jnp.sum(jnp.where(chosen, values[None], 0.0), axis=1)


def wide_dot(left, right):
    return jnp.dot(left, right, preferred_element_type=jnp.float32)


def dot_turned(left, right):
    return lax.dot_general(left, right, (((1,), (1,)), ((), ())), preferred_element_type=jnp.float32)


def dot_rows(left, right):
    return lax.dot_general(left, right, (((0,), (0,)), ((), ())), preferred_element_type=jnp.float32)


TILE = 256


def whole(array):
    return pl.BlockSpec(array.shape, lambda *i: (0,) * array.ndim)


def in_vmem(count):
    return [pl.BlockSpec(memory_space=pltpu.VMEM)] * count


def in_place(count):
    return [pl.BlockSpec(memory_space=pl.ANY)] * count


def head_scores(heads, h, nope_ref, turned_ref, keyval_ref, key_ref, masks):
    span = ROPE // 2 * heads
    column = pl.ds(pl.multiple_of(h * NOPE, NOPE), NOPE)
    key_column = pl.ds(pl.multiple_of(h * (NOPE + VD), NOPE), NOPE)
    scores = dot_turned(nope_ref[:, column], keyval_ref[:, key_column])
    for k in (0, 1):
        part = turned_ref[:, k * span : (k + 1) * span]
        part = jnp.where(masks, part, jnp.zeros_like(part))
        scores += dot_turned(part, key_ref[:, k * span : (k + 1) * span])
    return scores * (NOPE + ROPE) ** (-0.5)


def head_lanes(heads, h):
    span = ROPE // 2 * heads
    lane = lax.broadcasted_iota(jnp.int32, (1, span), 1)
    return (lane >= h * (ROPE // 2)) & (lane < (h + 1) * (ROPE // 2))


def allowed_rows(count, segment_row, segment_column):
    tokens = segment_row.shape[1]
    column = lax.broadcasted_iota(jnp.int32, (tokens, tokens), 0)
    row = lax.broadcasted_iota(jnp.int32, (tokens, tokens), 1)
    live = (column < count) & (row < count) & (row <= column)
    return (segment_row == segment_column) & live | (column == row)


def attend_kernel(
    keys,
    extra,
    heads,
    sizes,
    place_ref,
    segment_row_ref,
    segment_column_ref,
    cosine_ref,
    sine_ref,
    own_ref,
    other_ref,
    *refs,
):
    depth, query_width, used, latent_depth, keyval_part, first_width = sizes
    chunks = refs[: len(keys)]
    (
        own_out,
        sent_out,
        first_ref,
        keyval_weight_ref,
        output_ref,
        normed_ref,
        nope_ref,
        turned_ref,
        latent_ref,
        key_ref,
        keyval_ref,
        total_ref,
        attended_ref,
        gains_ref,
        latent_gain_ref,
        semaphores,
    ) = refs[len(keys) + extra :]
    f32, bf16 = jnp.float32, jnp.bfloat16
    local_rows = own_ref.shape[0]
    tokens = 2 * local_rows
    coords = (place_ref[0], place_ref[1], place_ref[2])
    x = place_ref[3]
    copies = []
    parts = depth // latent_depth
    for key, chunk in zip(keys, chunks):
        block = place_of(coords, key)
        rows = pl.ds(pl.multiple_of(block * depth, depth), depth)
        small_rows = pl.ds(pl.multiple_of(block * latent_depth, latent_depth), latent_depth)
        moves = [(chunk.at[:, pl.ds(0, first_width)], first_ref.at[rows])]
        for k in range(parts):
            moves.append(
                (
                    chunk.at[
                        pl.ds(k * latent_depth, latent_depth), pl.ds(first_width, keyval_part)
                    ],
                    keyval_weight_ref.at[small_rows, pl.ds(k * keyval_part, keyval_part)],
                )
            )
        moves.append(
            (
                chunk.at[:, pl.ds(first_width + keyval_part, heads * VD)],
                output_ref.at[rows],
            )
        )
        for source, target in moves:
            copies.append(pltpu.make_async_copy(source, target, semaphores.at[len(copies)]))
    for copy in copies:
        copy.start()
    for copy in copies:
        copy.wait()

    edge = query_width + KVR
    spread = jnp.transpose(first_ref[:, edge:].astype(f32))[used - edge : used - edge + 8]
    gains_ref[...] = spread
    gain = spread[0:1]
    source = lax.broadcasted_iota(jnp.int32, (D, KVR), 0)
    target = lax.broadcasted_iota(jnp.int32, (D, KVR), 1)
    wanted = target // latent_depth * depth + target % latent_depth
    chosen = jnp.where(source == wanted, 1.0, 0.0).astype(bf16)
    latent_gain = wide_dot(spread.astype(bf16), chosen)[2:3]
    latent_gain_ref[...] = latent_gain
    for ref, start in ((own_ref, x * local_rows), (other_ref, (1 - x) * local_rows)):
        rows = ref[...].astype(f32)
        unit = rows * lax.rsqrt(jnp.mean(rows * rows, axis=1, keepdims=True) + EPSILON)
        normed_ref[pl.ds(pl.multiple_of(start, local_rows), local_rows), :] = (unit * gain).astype(
            bf16
        )
    nope_width = heads * NOPE
    span = heads * (ROPE // 2)
    half = nope_width // 2
    for k in (0, 1):
        nope_ref[:, k * half : (k + 1) * half] = wide_dot(
            normed_ref[...], first_ref[:, k * half : (k + 1) * half]
        ).astype(bf16)
    turning = wide_dot(normed_ref[...], first_ref[:, nope_width : nope_width + 2 * span])
    cosine, sine = cosine_ref[...], sine_ref[...]
    first, second = turning[:, :span], turning[:, span:]
    turned_ref[:, :span] = (first * cosine - second * sine).astype(bf16)
    turned_ref[:, span:] = (second * cosine + first * sine).astype(bf16)
    latent = wide_dot(normed_ref[...], first_ref[:, query_width : query_width + KVR])
    latent_ref[...] = latent
    tail = wide_dot(normed_ref[...], first_ref[:, query_width + KVR :])
    lane = lax.broadcasted_iota(jnp.int32, (1, tail.shape[1]), 1)
    swapped = jnp.where(
        lane < ROPE // 2,
        -pltpu.roll(tail, tail.shape[1] - ROPE // 2, 1),
        pltpu.roll(tail, ROPE // 2, 1),
    )
    width = tail.shape[1]
    turned_key = tail * cosine[:, :width] + swapped * sine[:, :width]
    turned_key = jnp.where(lane < ROPE, turned_key, 0.0).astype(bf16)
    source = lax.broadcasted_iota(jnp.int32, (width, 2 * span), 0)
    target = lax.broadcasted_iota(jnp.int32, (width, 2 * span), 1)
    wanted = target % (ROPE // 2) + jnp.where(target < span, 0, ROPE // 2)
    key_ref[...] = wide_dot(turned_key, (source == wanted).astype(bf16)).astype(bf16)
    unit = latent * lax.rsqrt(jnp.mean(latent * latent, axis=1, keepdims=True) + EPSILON)
    latent_normed = (unit * latent_gain).astype(bf16)
    half = keyval_ref.shape[1] // 4
    for k in range(4):
        keyval_ref[:, k * half : (k + 1) * half] = wide_dot(
            latent_normed, keyval_weight_ref[:, k * half : (k + 1) * half]
        ).astype(bf16)
    allowed = allowed_rows(place_ref[4], segment_row_ref[...], segment_column_ref[...])
    total_lane = lax.broadcasted_iota(jnp.int32, total_ref.shape, 1)
    total_ref[...] = jnp.zeros_like(total_ref)

    def one_head(h, _):
        scores = head_scores(
            heads, h, nope_ref, turned_ref, keyval_ref, key_ref, head_lanes(heads, h)
        )
        scores = jnp.where(allowed, scores, -1e30)
        most = jnp.max(scores, axis=1, keepdims=True)
        total = most + jnp.log(jnp.sum(jnp.exp(scores - most), axis=1, keepdims=True))
        weights = jnp.exp(scores - total).astype(bf16)
        total_ref[...] += jnp.where(total_lane == h, total, 0.0)
        value_column = pl.ds(pl.multiple_of(h * (NOPE + VD) + NOPE, NOPE), VD)
        attended_ref[:, pl.ds(pl.multiple_of(h * VD, VD), VD)] = wide_dot(
            weights, keyval_ref[:, value_column]
        ).astype(bf16)
        return 0

    lax.fori_loop(0, heads, one_head, 0)
    own = pl.ds(pl.multiple_of(x * local_rows, local_rows), local_rows)
    other = pl.ds(pl.multiple_of((1 - x) * local_rows, local_rows), local_rows)
    pieces = 4
    size = output_ref.shape[0] // pieces
    for k in range(pieces):
        columns = slice(k * size, (k + 1) * size)
        own_out[:, columns] = dot_turned(attended_ref[own, :], output_ref[columns, :])
        sent_out[:, columns] = dot_turned(attended_ref[other, :], output_ref[columns, :]).astype(
            bf16
        )


def attend_forward(place, segments, cosine, sine, own, other, chunks, heads, sizes, others):
    depth, query_width, used, latent_depth, keyval_part, first_width = sizes
    f32, bf16 = jnp.float32, jnp.bfloat16
    keys = [key for key, _ in chunks]
    local_rows = own.shape[0]
    tokens = 2 * local_rows
    span = heads * (ROPE // 2)
    shapes = [
        ((local_rows, D), f32),
        ((local_rows, D), bf16),
        ((D, first_width), bf16),
        ((KVR, heads * (NOPE + VD)), bf16),
        ((D, heads * VD), bf16),
        ((tokens, D), bf16),
        ((tokens, heads * NOPE), bf16),
        ((tokens, 2 * span), bf16),
        ((tokens, KVR), f32),
        ((tokens, 2 * span), bf16),
        ((tokens, heads * (NOPE + VD)), bf16),
        ((tokens, 128), f32),
        ((tokens, heads * VD), bf16),
        ((8, D), f32),
        ((1, KVR), f32),
    ]
    return pl.pallas_call(
        functools.partial(attend_kernel, keys, len(others), heads, sizes),
        out_shape=[jax.ShapeDtypeStruct(*shape) for shape in shapes],
        in_specs=[pl.BlockSpec(memory_space=pltpu.SMEM)]
        + in_vmem(6)
        + in_place(len(chunks) + len(others)),
        out_specs=in_vmem(len(shapes)),
        scratch_shapes=[
            pltpu.SemaphoreType.DMA((len(chunks) * (2 + depth // latent_depth),))
        ],
        compiler_params=pltpu.CompilerParams(vmem_limit_bytes=48 * 1024 * 1024),
        cost_estimate=pl.CostEstimate(
            flops=2 * tokens * D * (first_width + heads * VD + 1024),
            bytes_accessed=4 * D * (first_width + 1536),
            transcendentals=2 * heads * tokens * tokens,
        ),
    )(
        place,
        segments,
        segments.T,
        cosine,
        sine,
        own,
        other,
        *[piece for _, piece in chunks],
        *others,
    )


def attend_back_kernel(
    heads,
    place_ref,
    segment_row_ref,
    segment_column_ref,
    cosine_ref,
    sine_ref,
    own_ref,
    other_ref,
    keyval_weight_ref,
    output_ref,
    nope_ref,
    turned_ref,
    latent_ref,
    key_ref,
    keyval_ref,
    total_ref,
    latent_gain_ref,
    projected_ref,
    keyval_grad_ref,
    latent_out,
    gain_ref,
    grad_ref,
    turn_ref,
    back_ref,
):
    f32, bf16 = jnp.float32, jnp.bfloat16
    local_rows = own_ref.shape[0]
    x = place_ref[3]
    span = heads * (ROPE // 2)
    nope_width = heads * NOPE
    query_width = nope_width + 2 * span
    scale = (NOPE + ROPE) ** (-0.5)
    for ref, start in ((own_ref, x * local_rows), (other_ref, (1 - x) * local_rows)):
        rows = pl.ds(pl.multiple_of(start, local_rows), local_rows)
        for k in (0, 1):
            half = slice(k * nope_width // 2, (k + 1) * nope_width // 2)
            grad_ref[rows, half] = wide_dot(ref[...], output_ref[:, half]).astype(bf16)
    allowed = allowed_rows(place_ref[4], segment_row_ref[...], segment_column_ref[...])
    total_lane = lax.broadcasted_iota(jnp.int32, total_ref.shape, 1)
    turn_ref[...] = jnp.zeros_like(turn_ref)
    back_ref[...] = jnp.zeros_like(back_ref)

    def one_head(h, _):
        mask = head_lanes(heads, h)
        scores = head_scores(heads, h, nope_ref, turned_ref, keyval_ref, key_ref, mask)
        total = jnp.sum(jnp.where(total_lane == h, total_ref[...], 0.0), axis=1, keepdims=True)
        weights = jnp.exp(jnp.where(allowed, scores, -1e30) - total)
        weights_low = weights.astype(bf16)
        column = pl.ds(pl.multiple_of(h * NOPE, NOPE), NOPE)
        key_column = pl.ds(pl.multiple_of(h * (NOPE + VD), NOPE), NOPE)
        value_column = pl.ds(pl.multiple_of(h * (NOPE + VD) + NOPE, NOPE), VD)
        grads = grad_ref[:, column]
        grad_weights = dot_turned(grads, keyval_ref[:, value_column])
        keyval_grad_ref[:, value_column] = dot_rows(weights_low, grads).astype(bf16)
        grad_scores = (
            weights * (grad_weights - jnp.sum(weights * grad_weights, axis=1, keepdims=True))
        ).astype(bf16)
        projected_ref[:, column] = (
            scale * wide_dot(grad_scores, keyval_ref[:, key_column])
        ).astype(bf16)
        keyval_grad_ref[:, key_column] = (
            scale * dot_rows(grad_scores, nope_ref[:, column])
        ).astype(bf16)
        for k in (0, 1):
            part = slice(k * span, (k + 1) * span)
            turn = wide_dot(grad_scores, key_ref[:, part])
            turn_ref[:, part] += jnp.where(mask, turn, 0.0)
            own = turned_ref[:, part]
            own = jnp.where(mask, own, jnp.zeros_like(own))
            back_ref[:, part] += dot_rows(grad_scores, own)
        return 0

    lax.fori_loop(0, heads, one_head, 0)
    cosine, sine = cosine_ref[...], sine_ref[...]
    first, second = scale * turn_ref[:, :span], scale * turn_ref[:, span:]
    projected_ref[:, nope_width : nope_width + span] = (first * cosine + second * sine).astype(bf16)
    projected_ref[:, nope_width + span : query_width] = (second * cosine - first * sine).astype(
        bf16
    )
    folded = []
    for k in (0, 1):
        part = scale * back_ref[:, k * span : (k + 1) * span]
        shift = span // 2
        while shift >= ROPE // 2:
            part = part + pltpu.roll(part, shift, 1)
            shift //= 2
        folded.append(part)
    width = projected_ref.shape[1] - query_width - KVR
    lane = lax.broadcasted_iota(jnp.int32, (1, width), 1)
    first = (folded[0] * cosine + folded[1] * sine)[:, :width]
    second = (folded[1] * cosine - folded[0] * sine)[:, :width]
    projected_ref[:, query_width + KVR :] = jnp.where(
        lane < ROPE // 2, first, jnp.where(lane < ROPE, second, 0.0)
    ).astype(bf16)
    gain = latent_gain_ref[...]
    latent = latent_ref[...]
    row_scale = lax.rsqrt(jnp.mean(latent * latent, axis=1, keepdims=True) + EPSILON)
    unit = latent * row_scale
    latent_out[...] = (unit * gain).astype(bf16)
    grad_normed = dot_turned(keyval_grad_ref[...], keyval_weight_ref[...])
    gain_ref[...] = jnp.sum(grad_normed * unit, axis=0, keepdims=True)
    grad_unit = grad_normed * gain
    projected_ref[:, query_width : query_width + KVR] = (
        row_scale * (grad_unit - unit * jnp.mean(grad_unit * unit, axis=1, keepdims=True))
    ).astype(bf16)


def attend_back(place, segments, cosine, sine, own, other, saved, heads, first_width, others):
    f32, bf16 = jnp.float32, jnp.bfloat16
    keyval = saved[6]
    tokens = 2 * own.shape[0]
    span = heads * (ROPE // 2)
    return pl.pallas_call(
        lambda *refs: attend_back_kernel(heads, *refs[:16], *refs[16 + len(others) :]),
        out_shape=[
            jax.ShapeDtypeStruct((tokens, first_width), bf16),
            jax.ShapeDtypeStruct((tokens, keyval.shape[1]), bf16),
            jax.ShapeDtypeStruct((tokens, KVR), bf16),
            jax.ShapeDtypeStruct((1, KVR), f32),
        ],
        in_specs=[pl.BlockSpec(memory_space=pltpu.SMEM)] + in_vmem(15) + in_place(len(others)),
        out_specs=in_vmem(4),
        scratch_shapes=[
            pltpu.VMEM((tokens, heads * NOPE), bf16),
            pltpu.VMEM((tokens, 2 * span), f32),
            pltpu.VMEM((tokens, 2 * span), f32),
        ],
        compiler_params=pltpu.CompilerParams(vmem_limit_bytes=48 * 1024 * 1024),
        cost_estimate=pl.CostEstimate(
            flops=2 * tokens * D * 3000,
            bytes_accessed=2 * D * 1536,
            transcendentals=heads * tokens * tokens,
        ),
    )(
        place,
        segments,
        segments.T,
        cosine,
        sine,
        own,
        other,
        *saved,
        *others,
    )


def first_grads_kernel(extra, places_ref, left_ref, right_ref, small_ref, *refs):
    out_ref = refs[-1]
    size = left_ref.shape[1]
    edge = right_ref.shape[1] - small_ref.shape[0]
    result = dot_rows(left_ref[...], right_ref[...])
    for value, some in (
        (result[:, :edge], slice(0, edge)),
        (result[:, edge:] + jnp.transpose(small_ref[...]), slice(edge, right_ref.shape[1])),
    ):
        if extra:
            value = value + refs[0][:, some].astype(jnp.float32)
        out_ref[:, some] = value.astype(jnp.bfloat16)


def other_grads_kernel(first, extra, places_ref, latent_ref, keyval_ref, grad_ref, attended_ref, *refs):
    out_ref, keyval_all = refs[-2:]
    step = pl.program_id(0)
    size = grad_ref.shape[1]
    latent_size = latent_ref.shape[1] // places_ref.shape[0]
    parts = size // latent_size
    columns = keyval_ref.shape[1] // parts

    @pl.when(step == 0)
    def _():
        for k in range(parts):
            some = slice(k * columns, (k + 1) * columns)
            keyval_all[:, some] = dot_rows(latent_ref[...], keyval_ref[:, some])

    start = pl.multiple_of(places_ref[first + step] * latent_size, latent_size)
    strip = keyval_all[pl.ds(start, latent_size), :]
    keyval = jnp.concatenate([strip[:, k * columns : (k + 1) * columns] for k in range(parts)], axis=0)
    output = dot_rows(grad_ref[...], attended_ref[...])
    for value, some in (
        (keyval, slice(0, columns)),
        (output, slice(columns, columns + output.shape[1])),
    ):
        if extra:
            value = value + refs[0][:, some].astype(jnp.float32)
        out_ref[:, some] = value.astype(jnp.bfloat16)


def still(array):
    return pl.BlockSpec(array.shape, lambda i, where: (0, 0))


def grads_call(
    kernel, specs, operands, scratch, size, width, places, first, count, arrived, others
):
    extra = [] if arrived is None else [arrived]
    return pl.pallas_call(
        lambda *refs: kernel(
            len(extra),
            *refs[: 1 + len(operands) + len(extra)],
            *refs[1 + len(operands) + len(extra) + len(others) :],
        ),
        grid_spec=pltpu.PrefetchScalarGridSpec(
            num_scalar_prefetch=1,
            grid=(count,),
            in_specs=specs
            + [pl.BlockSpec((size, width), lambda i, where: (first + i, 0))] * len(extra)
            + in_place(len(others)),
            out_specs=pl.BlockSpec((size, width), lambda i, where: (i, 0)),
            scratch_shapes=scratch,
        ),
        out_shape=jax.ShapeDtypeStruct((count * size, width), jnp.bfloat16),
        compiler_params=pltpu.CompilerParams(vmem_limit_bytes=32 * 1024 * 1024),
        cost_estimate=pl.CostEstimate(
            flops=1024 * count * size * width,
            bytes_accessed=4 * count * size * width,
            transcendentals=0,
        ),
    )(places, *operands, *extra, *others)


def first_grads(left, right, small, places, first, count, arrived=None, others=()):
    rows, width = right.shape
    size = left.shape[1] // places.shape[0]
    specs = [
        pl.BlockSpec((rows, size), lambda i, where: (0, where[first + i])),
        still(right),
        pl.BlockSpec((small.shape[0], size), lambda i, where: (0, where[first + i])),
    ]
    return grads_call(
        first_grads_kernel,
        specs,
        (left, right, small),
        [],
        size,
        width,
        places,
        first,
        count,
        arrived,
        others,
    )


def other_grads(latent, keyval, grad, attended, places, first, count, arrived=None, others=()):
    rows = grad.shape[0]
    blocks = places.shape[0]
    size = grad.shape[1] // blocks
    parts = size // (latent.shape[1] // blocks)
    width = keyval.shape[1] // parts + attended.shape[1]
    specs = [
        still(latent),
        still(keyval),
        pl.BlockSpec((rows, size), lambda i, where: (0, where[first + i])),
        still(attended),
    ]
    scratch = [pltpu.VMEM((latent.shape[1], keyval.shape[1]), jnp.float32)]
    return grads_call(
        functools.partial(other_grads_kernel, first),
        specs,
        (latent, keyval, grad, attended),
        scratch,
        size,
        width,
        places,
        first,
        count,
        arrived,
        others,
    )


def first_back_kernel(place_ref, own_ref, other_ref, grad_ref, weight_ref, own_out, sent_out, gain_ref):
    local_rows = own_ref.shape[0]
    x = place_ref[3]
    size = weight_ref.shape[0] // 4
    for ref, start, out in (
        (own_ref, x * local_rows, own_out),
        (other_ref, (1 - x) * local_rows, sent_out),
    ):
        rows = ref[...].astype(jnp.float32)
        unit = rows * lax.rsqrt(jnp.mean(rows * rows, axis=1, keepdims=True) + EPSILON)
        grads = grad_ref[pl.ds(pl.multiple_of(start, local_rows), local_rows), :]
        for k in range(4):
            some = slice(k * size, (k + 1) * size)
            part = dot_turned(grads, weight_ref[some, :])
            out[:, some] = part.astype(out.dtype)
            gain = jnp.sum(part * unit[:, some], axis=0, keepdims=True)
            if ref is own_ref:
                gain_ref[:, some] = gain
            else:
                gain_ref[:, some] += gain


def first_back(place, own, other, grads, weight):
    f32, bf16 = jnp.float32, jnp.bfloat16
    depth = weight.shape[0]
    return pl.pallas_call(
        first_back_kernel,
        out_shape=[
            jax.ShapeDtypeStruct(own.shape, f32),
            jax.ShapeDtypeStruct(own.shape, bf16),
            jax.ShapeDtypeStruct((1, depth), f32),
        ],
        in_specs=[pl.BlockSpec(memory_space=pltpu.SMEM)] + in_vmem(4),
        out_specs=in_vmem(3),
        compiler_params=pltpu.CompilerParams(vmem_limit_bytes=32 * 1024 * 1024),
        cost_estimate=pl.CostEstimate(
            flops=4 * own.shape[0] * weight.shape[0] * weight.shape[1],
            bytes_accessed=2 * weight.shape[0] * weight.shape[1],
            transcendentals=0,
        ),
    )(place, own, other, grads, weight)


def close_ring(near, arrived, last):
    size = near.shape[0] // RINGS
    total = near.astype(jnp.float32) + arrived.astype(jnp.float32)
    parts = [total[r * size : (r + 1) * size] for r in range(RINGS)]
    parts[0] = after(parts[0], last)
    return ring_sum(parts, jnp.bfloat16)


def pack_kernel(heads, query_ref, latent_ref, small_ref, keyval_ref, output_ref, out_ref):
    half = ROPE // 2
    head = NOPE + ROPE
    nope_width = heads * NOPE
    for h in range(heads):
        start = h * head
        out_ref[:, h * NOPE : (h + 1) * NOPE] = query_ref[:, start : start + NOPE]
        for k in (0, 1):
            to = nope_width + k * heads * half + h * half
            out_ref[:, to : to + half] = query_ref[
                :, start + NOPE + k * half : start + NOPE + (k + 1) * half
            ]
    at = heads * head
    edge = at + KVR
    out_ref[:, at:edge] = latent_ref[:, :KVR]
    out_ref[:, edge : edge + 128] = jnp.concatenate([latent_ref[:, KVR:], small_ref[...]], axis=1)
    at = edge + 128
    size = keyval_ref.shape[0]
    parts = out_ref.shape[0] // size
    part = keyval_ref.shape[1] // parts
    for k in range(parts):
        out_ref[k * size : (k + 1) * size, at : at + part] = keyval_ref[
            :, k * part : (k + 1) * part
        ]
    out_ref[:, at + part :] = jnp.transpose(output_ref[...].astype(jnp.float32)).astype(
        jnp.bfloat16
    )


def pack_weights(query, latent, small, keyval, output):
    depth, query_width = query.shape
    heads = query_width // (NOPE + ROPE)
    width = query_width + KVR + 128 + keyval.size // depth + output.shape[0]
    return pl.pallas_call(
        functools.partial(pack_kernel, heads),
        out_shape=jax.ShapeDtypeStruct((depth, width), jnp.bfloat16),
        in_specs=in_vmem(5),
        out_specs=pl.BlockSpec(memory_space=pltpu.VMEM),
    )(query, latent, small, keyval, output)


def load_pieces(pieces, starts, target, semaphores):
    size = target.shape[0] // len(pieces)
    copies = [
        pltpu.make_async_copy(
            piece.at[pl.ds(start, size)], target.at[pl.ds(k * size, size)], semaphores.at[k]
        )
        for k, (piece, start) in enumerate(zip(pieces, starts))
    ]
    for copy in copies:
        copy.start()
    for copy in copies:
        copy.wait()


def shared_stride(shared):
    return -(-shared // 32) * 32


def pack_shared_kernel(blocks, shared, in_ref, down_ref, out_ref):
    stride = shared_stride(shared)
    out_ref[...] = jnp.zeros_like(out_ref)
    for k in range(3):
        if k < 2:
            units = jnp.transpose(in_ref[k].astype(jnp.float32)).astype(jnp.bfloat16)
        else:
            units = down_ref[...]
        for b in range(blocks):
            out_ref[b, k * stride : k * stride + shared] = units[b * shared : (b + 1) * shared]


def pack_shared(shared_in, shared_down, blocks, others):
    depth = shared_in.shape[1]
    shared = shared_down.shape[0] // blocks
    return pl.pallas_call(
        lambda in_ref, down_ref, *refs: pack_shared_kernel(
            blocks, shared, in_ref, down_ref, refs[-1]
        ),
        out_shape=jax.ShapeDtypeStruct((blocks, 3 * shared_stride(shared), depth), jnp.bfloat16),
        in_specs=in_vmem(2) + in_place(len(others)),
        out_specs=pl.BlockSpec(memory_space=pltpu.VMEM),
    )(shared_in, shared_down, *others)


def unpack_shared_kernel(shared, packed_ref, in_ref, down_ref, units_ref):
    stride = shared_stride(shared)
    blocks = packed_ref.shape[0]
    for k in range(3):
        target = down_ref if k == 2 else units_ref
        for b in range(blocks):
            target[b * shared : (b + 1) * shared, :] = packed_ref[
                b, k * stride : k * stride + shared
            ].astype(jnp.float32)
        if k < 2:
            in_ref[k] = jnp.transpose(units_ref[...])


def unpack_shared(packed, shared, others):
    blocks, _, depth = packed.shape
    return pl.pallas_call(
        lambda packed_ref, *refs: unpack_shared_kernel(shared, packed_ref, *refs[len(others) :]),
        out_shape=[
            jax.ShapeDtypeStruct((2, depth, blocks * shared), jnp.float32),
            jax.ShapeDtypeStruct((blocks * shared, depth), jnp.float32),
        ],
        in_specs=in_vmem(1) + in_place(len(others)),
        out_specs=in_vmem(2),
        scratch_shapes=[pltpu.VMEM((blocks * shared, depth), jnp.float32)],
    )(packed, *others)


def pack_units_kernel(units, shared, own_in, other_in, own_down, other_down, near, far, *refs):
    outs = refs[-3:]
    hole = -(-units // TILE) * TILE
    stride = shared_stride(shared)
    columns = outs[0].shape[1]
    size = near.shape[2]
    for k, out in enumerate(outs):
        first = own_in[0, k] if k < 2 else own_down[0]
        second = other_in[0, k] if k < 2 else other_down[0]
        out[:units] = first
        out[units:hole] = jnp.zeros((hole - units, columns), jnp.bfloat16)
        out[hole : hole + units] = second
        out[hole + units : 2 * hole] = jnp.zeros((hole - units, columns), jnp.bfloat16)
        out[2 * hole :] = jnp.zeros((TILE, columns), jnp.bfloat16)
        for b in range(columns // size):
            part = slice(b * size, (b + 1) * size)
            for at, ref in ((2 * hole, near), (2 * hole + stride, far)):
                out[at : at + shared, part] = ref[b, k * stride : k * stride + shared]


def pack_units(own_in, other_in, own_down, other_down, near, far, shared, others):
    units, depth = own_down.shape[1:]
    size = near.shape[2]
    height = 2 * (-(-units // TILE) * TILE) + TILE
    columns = 2 * size
    in_spec = pl.BlockSpec((1, 2, units, columns), lambda i: (0, 0, 0, i))
    down_spec = pl.BlockSpec((1, units, columns), lambda i: (0, 0, i))
    narrow = pl.BlockSpec((2,) + near.shape[1:], lambda i: (i, 0, 0))
    return pl.pallas_call(
        functools.partial(pack_units_kernel, units, shared),
        grid=(depth // columns,),
        in_specs=[in_spec, in_spec, down_spec, down_spec, narrow, narrow]
        + in_place(len(others)),
        out_specs=[pl.BlockSpec((height, columns), lambda i: (0, i))] * 3,
        out_shape=[jax.ShapeDtypeStruct((height, depth), jnp.bfloat16)] * 3,
        compiler_params=pltpu.CompilerParams(vmem_limit_bytes=32 * 1024 * 1024),
        cost_estimate=pl.CostEstimate(
            flops=0, bytes_accessed=12 * height * depth, transcendentals=0
        ),
    )(own_in, other_in, own_down, other_down, near, far, *others)


def expert_grads_kernel(units, count, extra, right_ref, *refs):
    out = refs[-1]
    for k in range(count):

        @pl.when(pl.program_id(0) == k)
        def _():
            result = dot_rows(refs[k][...], right_ref[...])[:units]
            if extra:
                result += refs[count][0, 0].astype(jnp.float32)
            out[0, 0] = result.astype(out.dtype)


def expert_grads(lefts, right, units, column, arrived, kind, others=()):
    total, depth = right.shape
    wide = -(-units // TILE) * TILE
    extra = [] if arrived is None else [arrived]
    out = pl.BlockSpec((1, 1, units, 2 * TILE), lambda k, i: (0, k, 0, i))
    side = pl.BlockSpec((total, wide), lambda k, i: (0, column))
    return pl.pallas_call(
        functools.partial(expert_grads_kernel, units, len(lefts), len(extra)),
        grid=(len(lefts), depth // (2 * TILE)),
        in_specs=[pl.BlockSpec((total, 2 * TILE), lambda k, i: (0, i))]
        + [side] * len(lefts)
        + [out] * len(extra)
        + in_place(len(others)),
        out_specs=out,
        out_shape=jax.ShapeDtypeStruct((1, len(lefts), units, depth), kind),
        compiler_params=pltpu.CompilerParams(vmem_limit_bytes=48 * 1024 * 1024),
        cost_estimate=pl.CostEstimate(
            flops=2 * len(lefts) * total * depth * wide,
            bytes_accessed=2 * len(lefts) * total * (depth + wide) + 8 * depth * units,
            transcendentals=0,
        ),
    )(right, *lefts, *extra, *others)


def side_grads_kernel(shared, rows_ref, cots_ref, gate_ref, up_ref, hidden_ref, logit_ref, *outs):
    kept_ref, sent_ref, router_ref = outs
    stride = shared_stride(shared)
    size = kept_ref.shape[2]
    for k, (left, right) in enumerate(
        ((gate_ref, rows_ref), (up_ref, rows_ref), (hidden_ref, cots_ref))
    ):
        result = dot_rows(left[...], right[...])
        for b in range(kept_ref.shape[0]):
            part = slice(b * size, (b + 1) * size)
            kept_ref[b, k * stride : (k + 1) * stride] = result[:stride, part]
            sent_ref[b, k * stride : (k + 1) * stride] = result[
                stride : 2 * stride, part
            ].astype(jnp.bfloat16)
    router_ref[...] = dot_rows(logit_ref[...], rows_ref[...])


def side_grads(rows, cots, gate, up, hidden, logits, shared, blocks, others):
    total, depth = rows.shape
    column = gate.shape[1] // TILE - 1
    size = depth // blocks
    stride = shared_stride(shared)
    wide = pl.BlockSpec((total, 2 * TILE), lambda i: (0, i))
    side = pl.BlockSpec((total, TILE), lambda i: (0, column))
    packed = pl.BlockSpec((2 * TILE // size, 3 * stride, size), lambda i: (i, 0, 0))
    return pl.pallas_call(
        lambda *refs: side_grads_kernel(shared, *refs[:6], *refs[6 + len(others) :]),
        grid=(depth // (2 * TILE),),
        in_specs=[wide, wide, side, side, side, whole(logits)] + in_place(len(others)),
        out_specs=[packed, packed, pl.BlockSpec((logits.shape[1], 2 * TILE), lambda i: (0, i))],
        out_shape=[
            jax.ShapeDtypeStruct((blocks, 3 * stride, size), jnp.float32),
            jax.ShapeDtypeStruct((blocks, 3 * stride, size), jnp.bfloat16),
            jax.ShapeDtypeStruct((logits.shape[1], depth), jnp.float32),
        ],
        compiler_params=pltpu.CompilerParams(vmem_limit_bytes=48 * 1024 * 1024),
        cost_estimate=pl.CostEstimate(
            flops=8 * total * depth * TILE,
            bytes_accessed=4 * total * depth,
            transcendentals=0,
        ),
    )(rows, cots, gate, up, hidden, logits, *others)


def down_kernel(starts, *refs):
    count = len(starts)
    pieces, weight_ref = refs[:count], refs[count]
    grads_ref, rows_ref, semaphores = refs[-3:]

    @pl.when(pl.program_id(0) == 0)
    def _():
        load_pieces(pieces, starts, rows_ref, semaphores)

    size = rows_ref.shape[0] // 2
    for k in range(2):
        part = slice(k * size, (k + 1) * size)
        grads_ref[part, :] = dot_turned(rows_ref[part, :], weight_ref[...]).astype(jnp.bfloat16)


def down_grads(part, pieces, size, down, kept, others):
    count = len(pieces)
    depth = down.shape[1]
    width = down.shape[0]
    rows = count * size
    return pl.pallas_call(
        functools.partial(down_kernel, tuple(start for _, start in pieces)),
        grid=(width // TILE,),
        in_specs=in_place(count)
        + [pl.BlockSpec((TILE, depth), lambda i: (i, 0))]
        + in_place(len(kept) + len(others)),
        out_specs=[
            pl.BlockSpec((rows, TILE), lambda i: (part, i)),
            pl.BlockSpec((rows, depth), lambda i: (part, 0)),
        ],
        out_shape=[
            jax.ShapeDtypeStruct((2 * rows, width), jnp.bfloat16),
            jax.ShapeDtypeStruct((2 * rows, depth), jnp.bfloat16),
        ],
        scratch_shapes=[pltpu.SemaphoreType.DMA((count,))],
        input_output_aliases={count + 1 + k: k for k in range(len(kept))},
        compiler_params=pltpu.CompilerParams(vmem_limit_bytes=48 * 1024 * 1024),
        cost_estimate=pl.CostEstimate(
            flops=2 * rows * depth * width,
            bytes_accessed=2 * (2 * rows * depth + depth * width + rows * width),
            transcendentals=0,
        ),
    )(*[array for array, _ in pieces], down, *kept, *others)


def out_kernel(pieces, hidden_ref, weight_ref, *refs):
    outs, done_ref = refs[-1 - pieces : -1], refs[-1]
    size = hidden_ref.shape[0] // (RINGS * pieces)
    done_ref[...] = jnp.zeros_like(done_ref)
    for r in range(RINGS):
        part = hidden_ref[r * pieces * size : (r + 1) * pieces * size, :]
        result = wide_dot(part, weight_ref[...]).astype(jnp.bfloat16)
        for k in range(pieces):
            outs[k][r * size : (r + 1) * size, :] = result[k * size : (k + 1) * size]


def out_rows(pieces, half, hidden, down, kept, others):
    rows, width = hidden.shape
    depth = down.shape[1]
    steps = depth // (2 * TILE)
    results = pl.pallas_call(
        functools.partial(out_kernel, pieces),
        grid=(steps,),
        in_specs=[whole(hidden), pl.BlockSpec((width, TILE), lambda i: (0, half * steps + i))]
        + in_place(len(kept) + len(others)),
        out_specs=[pl.BlockSpec((rows // pieces, TILE), lambda i: (0, half * steps + i))] * pieces
        + [pl.BlockSpec((8, 128), lambda i: (0, 0))],
        out_shape=[jax.ShapeDtypeStruct((rows // pieces, depth), jnp.bfloat16)] * pieces
        + [jax.ShapeDtypeStruct((8, 128), jnp.float32)],
        input_output_aliases={2 + k: k for k in range(len(kept))},
        compiler_params=pltpu.CompilerParams(vmem_limit_bytes=48 * 1024 * 1024),
        cost_estimate=pl.CostEstimate(
            flops=rows * depth * width,
            bytes_accessed=rows * depth + depth * width + 2 * rows * width,
            transcendentals=0,
        ),
    )(hidden, down, *kept, *others)
    return results[:-1], results[-1]


def mlp_kernel(tiles, starts, others, experts_ref, routed_ref, *refs):
    pieces = len(starts)
    row_refs = refs[:pieces]
    router_ref, gate_col, up_col, down_grad, gate_row, up_row = refs[pieces : pieces + 6]
    outs = refs[pieces + 6 + others :]
    grad_refs = outs[:pieces]
    rows_out, hidden_out, gate_out, up_out, logit_out = outs[pieces : pieces + 5]
    gate_all, up_all, prob_ref, scale_ref, sum_ref, semaphores = outs[pieces + 5 :]
    step = pl.program_id(0)
    third = tiles // 2
    total = rows_out.shape[0]
    size = total // pieces
    lane = lax.broadcasted_iota(jnp.int32, (1, router_ref.shape[1]), 1) - experts_ref[3]

    @pl.when(step == 0)
    def _():
        load_pieces(row_refs, starts, rows_out, semaphores)
        logits = wide_dot(rows_out[...], router_ref[...])
        logits = jnp.where((lane >= 0) & (lane < experts_ref[2]), logits, -1e30)
        raised = jnp.exp(logits - jnp.max(logits, axis=1, keepdims=True))
        chances = raised / jnp.sum(raised, axis=1, keepdims=True)
        prob_ref[...] = chances
        for k in (0, 1):
            chance = jnp.sum(jnp.where(lane == experts_ref[k], chances, 0.0), axis=1, keepdims=True)
            scale_ref[k] = routed_ref[:, k : k + 1] * chance
        scale_ref[2] = jnp.ones_like(scale_ref[2])
        sum_ref[...] = jnp.zeros_like(sum_ref)

    @pl.when(step < tiles)
    def _():
        columns = pl.ds(pl.multiple_of(step * TILE, TILE), TILE)
        kind = step // third
        half = total // 2
        for k in (0, 1):
            part = slice(k * half, (k + 1) * half)
            pre_gate = dot_turned(rows_out[part, :], gate_col[...])
            pre_up = dot_turned(rows_out[part, :], up_col[...])
            grads = down_grad[part, :].astype(jnp.float32)
            scale = scale_ref[kind, part, :]
            sigmoid = 1.0 / (1.0 + jnp.exp(-pre_gate))
            silu = pre_gate * sigmoid
            hidden = (silu * pre_up).astype(jnp.bfloat16).astype(jnp.float32)
            sum_ref[kind, part, :] += jnp.sum(hidden * grads, axis=1, keepdims=True)
            grad_hidden = scale * grads
            low_gate = (grad_hidden * pre_up * (sigmoid + silu * (1.0 - sigmoid))).astype(
                jnp.bfloat16
            )
            low_up = (grad_hidden * silu).astype(jnp.bfloat16)
            gate_all[part, columns] = low_gate
            up_all[part, columns] = low_up
            hidden_out[part, :] = (scale * hidden).astype(jnp.bfloat16)
            gate_out[part, :] = low_gate
            up_out[part, :] = low_up

    @pl.when(step == tiles - 1)
    def _():
        grad_logits = jnp.zeros_like(prob_ref)
        for k in (0, 1):
            own = jnp.where(lane == experts_ref[k], 1.0, 0.0)
            grad_logits += scale_ref[k] * sum_ref[k] * (own - prob_ref[...])
        logit_out[...] = grad_logits.astype(jnp.bfloat16)

    @pl.when(step >= tiles)
    def _():
        some = pl.ds(pl.multiple_of((step - tiles) * 2 * TILE, TILE), 2 * TILE)
        grads = wide_dot(gate_all[...], gate_row[...]) + wide_dot(up_all[...], up_row[...])
        grads += dot_turned(logit_out[...], router_ref[some, :])
        grads = grads.astype(jnp.bfloat16)
        for k in range(pieces):
            grad_refs[k][...] = grads[k * size : (k + 1) * size]


def mlp_plane(distance, experts, routed, rows, down_grad, router, weights, kept, others):
    gate, up = weights
    pieces = len(rows)
    width, depth = gate.shape
    size = routed.shape[0] // pieces
    tiles, columns = width // TILE, depth // (2 * TILE)
    total = pieces * size
    low = jnp.bfloat16

    def early(i):
        return jnp.minimum(i, tiles - 1)

    def late(i):
        return jnp.maximum(i - tiles, 0)

    tile_spec = pl.BlockSpec((total, TILE), lambda i: (distance, early(i)))
    anywhere = pl.BlockSpec(memory_space=pl.ANY)
    first_kept = 2 + pieces + 6
    results = pl.pallas_call(
        functools.partial(
            mlp_kernel, tiles, tuple(start for _, start in rows), len(kept) + len(others)
        ),
        grid=(tiles + columns,),
        in_specs=[pl.BlockSpec(memory_space=pltpu.SMEM), whole(routed)]
        + [anywhere] * pieces
        + [
            pl.BlockSpec((depth, 128), lambda i: (0, router.shape[1] // 128 - 1)),
            pl.BlockSpec((TILE, depth), lambda i: (early(i), 0)),
            pl.BlockSpec((TILE, depth), lambda i: (early(i), 0)),
            tile_spec,
            pl.BlockSpec((width, 2 * TILE), lambda i: (0, late(i))),
            pl.BlockSpec((width, 2 * TILE), lambda i: (0, late(i))),
        ]
        + [anywhere] * (len(kept) + len(others)),
        out_specs=[pl.BlockSpec((size, 2 * TILE), lambda i: (0, late(i)))] * pieces
        + [
            pl.BlockSpec((total, depth), lambda i: (distance, 0)),
            tile_spec,
            tile_spec,
            tile_spec,
            pl.BlockSpec((total, 128), lambda i: (distance, 0)),
        ],
        out_shape=[jax.ShapeDtypeStruct((size, depth), low)] * pieces
        + [
            jax.ShapeDtypeStruct((RINGS * total, many), low)
            for many in (depth, width, width, width, 128)
        ],
        scratch_shapes=[pltpu.VMEM((total, width), low)] * 2
        + [
            pltpu.VMEM((total, 128), jnp.float32),
            pltpu.VMEM((3, total, 1), jnp.float32),
            pltpu.VMEM((3, total, 1), jnp.float32),
            pltpu.SemaphoreType.DMA((pieces,)),
        ],
        input_output_aliases={first_kept + k: pieces + k for k in range(len(kept))},
        compiler_params=pltpu.CompilerParams(vmem_limit_bytes=48 * 1024 * 1024),
        cost_estimate=pl.CostEstimate(
            flops=2 * total * depth * width * 4,
            bytes_accessed=2 * (4 * depth * width + 3 * total * depth + 4 * total * width),
            transcendentals=total * width,
        ),
    )(experts, routed, *[array for array, _ in rows], router, gate, up, down_grad, gate, up, *kept, *others)
    return results[:pieces], results[pieces:]


def gather_body(
    block_input,
    segments,
    counts,
    routes,
    attn_gain,
    w_query,
    w_latent,
    latent_gain,
    w_keyval,
    w_output,
    ffn_gain,
    w_router,
    shared_gate_up,
    shared_down,
    expert_gate_up,
    expert_down,
    cotangent,
):
    f32 = jnp.float32
    bf16 = jnp.bfloat16
    blocks = 16
    index = lax.axis_index("dp")
    x = lax.axis_index("tensor")
    coords = jnp.stack([index // 4, (index // 2) % 2, index % 2]).astype(jnp.int32)
    core = coords[2]
    place = jnp.concatenate([coords, x.astype(jnp.int32)[None], counts])
    local_rows = block_input.shape[0]
    tokens = 2 * local_rows
    depth = w_query.shape[0]
    query_width = w_query.shape[1]
    heads = query_width // (NOPE + ROPE)
    experts = w_router.shape[1]
    units = expert_gate_up.shape[3]
    shared = shared_gate_up.shape[2] // blocks
    latent_depth = w_keyval.shape[0]

    used = query_width + KVR + ROPE
    small = jnp.concatenate(
        [
            attn_gain[:, None],
            ffn_gain[:, None],
            jnp.pad(latent_gain, (0, depth - latent_depth))[:, None],
            w_router,
            routes.reshape(depth, -1).astype(bf16),
            jnp.zeros((depth, 128 - ROPE - 3 - experts - 2 * TOP), bf16),
        ],
        axis=1,
    )
    first_width = query_width + KVR + 128
    shards = pack_weights(w_query, w_latent, small, w_keyval, w_output)
    other_input = other_x(block_input)
    expert_in = expert_gate_up.swapaxes(2, 3)
    expert_in_other = other_core(expert_in)
    expert_down_other = other_core(expert_down)
    chunks, held, besides = gather_weight(
        shards, (expert_in_other, expert_down_other, other_input)
    )
    shared_near = lax.all_to_all(
        pack_shared(shared_gate_up, shared_down, blocks, (held[3],)),
        "dp",
        split_axis=0,
        concat_axis=0,
        tiled=True,
    )
    shared_far = other_core(shared_near)

    grad_groups, grad_ring, grad_across = gather_whole(
        after(cotangent, held[3], besides[2]), besides[3]
    )

    cosine, sine = rotary_tables(segments[0], ROPE)
    cosine = jnp.tile(cosine, (1, heads))
    sine = jnp.tile(sine, (1, heads))
    sizes = (depth, query_width, used, latent_depth, w_keyval.shape[1] * latent_depth // depth, first_width)
    (
        own_part,
        sent_part,
        first_weight,
        keyval_weight,
        output_turned,
        first_normed,
        nope,
        turned_query,
        latent,
        key,
        keyval,
        total,
        attended,
        gains,
        latent_gain_row,
    ) = attend_forward(
        place,
        segments,
        cosine,
        sine,
        block_input,
        other_input,
        chunks,
        heads,
        sizes,
        (grad_ring[2], grad_across[0], grad_across[1]),
    )
    attn_gain_wide, ffn_gain_wide = gains[0], gains[1]
    mixed = block_input.astype(f32) + own_part + other_x(sent_part).astype(f32)
    second_scale = rms_scale(mixed)
    second_unit = mixed * second_scale
    second_normed = (second_unit * ffn_gain_wide).astype(bf16)

    routes_at = used + 3 + experts
    routes_all = first_weight[:, routes_at : routes_at + 2 * TOP].reshape(blocks * tokens, TOP)
    chip_experts = jnp.stack([index, index + 1 - 2 * core]).astype(jnp.int32)
    routed_all = jnp.any(
        routes_all[None] == chip_experts[:, None, None].astype(bf16), axis=2
    ).astype(f32)
    order = jnp.stack(
        [
            place_of(coords, (distance, flip_y, 0)) * 2 + (1 - x if flip_x else x)
            for distance in range(RINGS)
            for flip_x, flip_y in ((0, 0), (0, 1), (1, 0), (1, 1))
        ]
    )
    routed = jnp.stack(
        [
            pick_blocks(one.reshape(blocks * 2, local_rows), order).reshape(RINGS, -1)
            for one in routed_all
        ],
        axis=2,
    )

    corners = "yxyx"
    row_ring, row_groups = gather_rows(second_normed, "yyx")
    row_planes = [
        [(array, 0) for array in row_groups[0]],
        [(array, 0) for array in row_groups[1]],
        [(array, 0) for array in row_groups[2]],
        [(array, local_rows) for array in row_groups[2]],
    ]

    gate_weight, up_weight, down_weight = pack_units(
        expert_in,
        expert_in_other,
        expert_down,
        expert_down_other,
        shared_near,
        shared_far,
        shared,
        (second_normed,),
    )
    half_kept = down_grads(
        0,
        [(array, r * local_rows) for r in (0, 1) for array in grad_groups[0]],
        local_rows,
        down_weight,
        (),
        (row_ring[1],),
    )
    down_grad, every_grad = down_grads(
        1,
        [(array, r * local_rows) for r in (0, 1) for array in grad_groups[1]],
        local_rows,
        down_weight,
        half_kept,
        (row_ring[2],),
    )
    expert_ids = jnp.concatenate(
        [chip_experts, jnp.array([experts, used + 3 - query_width - KVR], jnp.int32)]
    )
    kept = []
    planes = []
    turned, closed = [None] * RINGS, [None] * RINGS
    for distance in range(RINGS):
        others = [row_ring[3]] if distance == 0 else []
        if distance == 1:
            others = list(row_groups[2][1:3])
        elif distance == 3:
            others = list(turned[0][1:])
        grads, kept = mlp_plane(
            distance,
            expert_ids,
            routed[distance],
            row_planes[distance],
            down_grad,
            first_weight,
            (gate_weight, up_weight),
            kept,
            others,
        )
        planes.append(list(grads))
        if distance:
            before = planes[distance - 1]
            k = 1 if corners[distance - 1] == "x" else 2
            before[k] = after(before[k], grads[3])
            turned[distance - 1] = turn_corner(before, corners[distance - 1])
            closed[distance - 1] = close_plane(turned[distance - 1])
    turned[3] = turn_corner(planes[3], corners[3])
    first_part = closed[1]
    closed[1] = (after(first_part[0], planes[3][3]),) + tuple(first_part[1:])
    every_row, every_hidden, every_gate_grad, every_up_grad, logit_grads = kept
    first_total = wide_sum(*closed[1]).astype(bf16)
    shared_kept, shared_sent, logit_rows = side_grads(
        every_row,
        every_grad,
        every_gate_grad,
        every_up_grad,
        every_hidden,
        logit_grads,
        shared,
        blocks,
        (first_total,),
    )
    sent_down = expert_grads((every_hidden,), every_grad, units, 1, None, bf16, (shared_sent,))
    half_outs, half_done = out_rows(4, 0, every_hidden, down_weight, (), (sent_down,))
    moving = ring_step(first_total)
    moving = ring_step(wide_sum(moving, *closed[2]).astype(bf16))
    own, beside, across = turned[3]
    own = after(own, sent_down)
    grad_close = close_plane((own, after(beside, shared_sent), across))
    grad_second = wide_sum(
        ring_step(wide_sum(moving, *grad_close).astype(bf16)),
        after(closed[0][0], half_done),
        *closed[0][1:],
    )

    arrived_down = other_core(sent_down)
    router_at = used + 3 - query_width - KVR
    grad_router = logit_rows[router_at : router_at + experts]
    shared_came = other_core(shared_sent)

    gain_ffn_part = jnp.sum(grad_second * second_unit, axis=0)
    grad_mixed = cotangent.astype(f32) + rms_back(
        grad_second * ffn_gain_wide, second_unit, second_scale
    )
    grad_mixed_low = grad_mixed.astype(bf16)
    other_grad = other_x(grad_mixed_low)
    outs, outs_done = out_rows(4, 1, every_hidden, down_weight, half_outs, (grad_mixed_low,))
    outs = list(outs)
    outs[2] = after(outs[2], other_grad)
    outs[3] = after(outs[3], other_grad)


    places = jnp.stack([place_of(coords, key_of) for key_of in weight_keys()]).astype(jnp.int32)
    projected_grad, keyval_grad, latent_normed, gain_latent_part = attend_back(
        place,
        segments,
        cosine,
        sine,
        grad_mixed_low,
        other_grad,
        (keyval_weight, output_turned, nope, turned_query, latent, key, keyval, total, latent_gain_row),
        heads,
        first_width,
        (arrived_down, shared_came, outs_done),
    )
    grad_attn = jnp.concatenate(
        [
            jnp.where(x == 0, grad_mixed_low, other_grad),
            jnp.where(x == 0, other_grad, grad_mixed_low),
        ],
        axis=0,
    )
    ring_places = places.reshape(2, 2, RINGS).swapaxes(1, 2).reshape(-1)
    other_parts = (latent_normed, keyval_grad, grad_attn, attended, ring_places)
    own_first, sent_first, gain_attn_part = first_back(
        place, block_input, other_input, projected_grad, first_weight
    )
    grad_first = own_first + other_x(sent_first).astype(f32)
    small_rows = jnp.concatenate(
        [
            jnp.zeros((ROPE, D), f32),
            gain_attn_part,
            gain_ffn_part[None],
            jnp.pad(
                gain_latent_part.reshape(blocks, latent_depth),
                ((0, 0), (0, depth - latent_depth)),
            ).reshape(1, D),
            grad_router,
            jnp.zeros((128 - ROPE - 3 - experts, D), f32),
        ],
        axis=0,
    )
    first_parts = (first_normed, projected_grad, small_rows, places)
    first_sent = first_grads(*first_parts, 8, 8, None)
    first_arrived = other_core(first_sent)
    other_arrived = other_core(other_grads(*other_parts, 8, 8, None, (first_sent,)))
    far = first_grads(*first_parts, 4, 4, first_arrived)
    other_kept = other_grads(*other_parts, 0, 8, other_arrived, (far,))
    shared_grads = lax.all_to_all(
        add_low(after(shared_kept, projected_grad), shared_came),
        "dp",
        split_axis=0,
        concat_axis=0,
        tiled=True,
    )
    from_y = other_y(far)
    arrived_in = other_core(
        expert_grads((every_gate_grad, every_up_grad), every_row, units, 1, None, bf16, (far,))
    )
    outs[1] = after(outs[1], from_y)
    near = first_grads(*first_parts, 0, 4, first_arrived, (shared_grads,))
    other_summed = ring_sum(
        [other_kept[2 * r * depth : 2 * (r + 1) * depth] for r in range(RINGS)], bf16
    )
    grad_expert_down = expert_grads(
        (every_hidden,), every_grad, units, 0, arrived_down, f32, (from_y,)
    )
    grad_expert_in = expert_grads(
        (every_gate_grad, every_up_grad), every_row, units, 0, arrived_in, f32, (near,)
    )
    first_closed = close_ring(near, from_y, grad_expert_in)
    out_own, out_beside, out_across = close_plane(turn_corner(outs, "x"))
    out_total = wide_sum(after(out_own, first_closed), out_beside, out_across)
    block_output = mixed + ring_sum(
        [out_total[r * local_rows : (r + 1) * local_rows] for r in range(RINGS)], bf16
    )
    other_closed = other_summed[:depth] + other_y(
        other_summed[depth:].astype(bf16)
    ).astype(f32)
    grad_shared_in, grad_shared_down = unpack_shared(shared_grads, shared, (from_y,))
    grad_expert_gate_up = grad_expert_in.swapaxes(2, 3)
    grad_expert_down = grad_expert_down[0]
    nope_width = heads * NOPE
    span = heads * (ROPE // 2)
    grad_query_weight = jnp.concatenate(
        [
            first_closed[:, :nope_width].reshape(depth, heads, NOPE),
            first_closed[:, nope_width : nope_width + span].reshape(depth, heads, -1),
            first_closed[:, nope_width + span : query_width].reshape(depth, heads, -1),
        ],
        axis=2,
    ).reshape(depth, query_width)
    both = first_closed[:, query_width:]
    both = both + other_x(both)
    grad_latent_weight = both[:, : KVR + ROPE]
    small_grads = both[:, KVR + ROPE :].T
    keyval_columns = w_keyval.shape[1] * latent_depth // depth
    grad_keyval_weight = (
        other_closed[:, :keyval_columns]
        .reshape(-1, latent_depth, keyval_columns)
        .transpose(1, 0, 2)
        .reshape(latent_depth, -1)
    )
    grad_output_weight = other_closed[:, keyval_columns:].T
    own_inputs = block_input.astype(f32)
    own_scale = rms_scale(own_inputs)
    own_unit = own_inputs * own_scale
    grad_input = grad_mixed + rms_back(grad_first * attn_gain_wide, own_unit, own_scale)
    return (
        block_output,
        grad_input,
        small_grads[0],
        grad_query_weight,
        grad_latent_weight,
        small_grads[2, :latent_depth],
        grad_keyval_weight,
        grad_output_weight,
        small_grads[1],
        small_grads[3 : 3 + experts].T,
        grad_shared_in,
        grad_shared_down,
        grad_expert_gate_up,
        grad_expert_down,
    )


def solution(mesh):
    in_specs = (
        P(("dp", "tensor"), None),
        P("dp", None),
        P("dp"),
        P("dp", None),
        P("dp"),
        P("dp", "tensor"),
        P("dp", None),
        P("dp"),
        P("dp", "tensor"),
        P("tensor", "dp"),
        P("dp"),
        P("dp", None),
        P(None, "dp", "tensor"),
        P("tensor", "dp"),
        P("dp", None, None, "tensor"),
        P("dp", "tensor", None),
        P(("dp", "tensor"), None),
    )
    out_specs = (
        P(("dp", "tensor"), None),
        P(("dp", "tensor"), None),
        P("dp"),
        P("dp", "tensor"),
        P("dp", None),
        P("dp"),
        P("dp", "tensor"),
        P("tensor", "dp"),
        P("dp"),
        P("dp", None),
        P(None, "dp", "tensor"),
        P("tensor", "dp"),
        P("dp", None, None, "tensor"),
        P("dp", "tensor", None),
    )
    body = gather_body if mesh.shape["dp"] == 16 else exchange_body
    return jax.shard_map(body, mesh=mesh, in_specs=in_specs, out_specs=out_specs, check_vma=False)
```

```python
import functools
import math

import jax
import jax.numpy as jnp
from jax import lax
from jax.experimental import pallas as pl
from jax.experimental.pallas import tpu as pltpu
from jax.sharding import PartitionSpec as P

D = 2048
NOPE = 128
ROPE = 64
VD = 128
KVR = 512
TOP = 6


EPSILON = 1e-06


def rms_scale(values):
    return lax.rsqrt(jnp.mean(values * values, axis=-1, keepdims=True) + EPSILON)


def rms_back(grad_unit, unit_rows, row_scale):
    return row_scale * (
        grad_unit - unit_rows * jnp.mean(grad_unit * unit_rows, axis=-1, keepdims=True)
    )


def rotary_tables(segment_row, width):
    count = segment_row.shape[0]
    position = jnp.arange(count, dtype=jnp.int32)
    same = segment_row[:, None] == segment_row[None, :]
    start = jnp.min(jnp.where(same, position[None, :], count), axis=1)
    offset = (position - start).astype(jnp.float32)
    freq = jnp.exp(jnp.arange(width // 2, dtype=jnp.float32) * (-2.0 * math.log(10000.0) / width))
    angle = offset[:, None] * freq[None, :]
    return (jnp.cos(angle), jnp.sin(angle))


def rotate(values, cosine, sine):
    half = values.shape[-1] // 2
    first = values[..., :half]
    second = values[..., half:]
    return jnp.concatenate(
        [first * cosine - second * sine, second * cosine + first * sine], axis=-1
    )


def rotate_back(grads, cosine, sine):
    half = grads.shape[-1] // 2
    first = grads[..., :half]
    second = grads[..., half:]
    return jnp.concatenate(
        [first * cosine + second * sine, second * cosine - first * sine], axis=-1
    )


def allowed_pairs(segment_row, count):
    position = jnp.arange(segment_row.shape[0], dtype=jnp.int32)
    live = position < count
    same = segment_row[:, None] == segment_row[None, :]
    causal = position[None, :] <= position[:, None]
    return same & causal & live[:, None] & live[None, :] | (position[:, None] == position[None, :])


def attention_scores(query_rows, key_nope, key_rope, allowed, scale):
    scores = jnp.einsum(
        "ihd,jhd->hij", query_rows[..., :NOPE], key_nope, preferred_element_type=jnp.float32
    )
    scores = scores + jnp.einsum(
        "ihd,jd->hij", query_rows[..., NOPE:], key_rope, preferred_element_type=jnp.float32
    )
    return jnp.where(allowed[None], scores * scale, -1e30)


def swiglu_back(gate, upper, grad_hidden, axis):
    sigmoid = jax.nn.sigmoid(gate)
    grad_gate = grad_hidden * upper * sigmoid * (1.0 + gate * (1.0 - sigmoid))
    grad_upper = grad_hidden * gate * sigmoid
    return jnp.stack([grad_gate, grad_upper], axis=axis)


def slot_layout(routes, experts, capacity):
    tokens = routes.shape[0]
    flat = routes.reshape(-1)
    onehot = (flat[:, None] == jnp.arange(experts, dtype=jnp.int32)[None, :]).astype(jnp.int32)
    rank = jnp.arange(flat.shape[0], dtype=jnp.int32)
    earlier = (rank[None, :] < rank[:, None]).astype(jnp.bfloat16)
    before = jnp.dot(
        earlier, onehot.astype(jnp.bfloat16), preferred_element_type=jnp.float32
    ).astype(jnp.int32)
    slot_index = jnp.sum(before * onehot, axis=1)
    target = flat * capacity + slot_index
    token_ids = jnp.arange(flat.shape[0], dtype=jnp.int32) // routes.shape[1]
    owner = jnp.full((experts * capacity,), tokens, jnp.int32).at[target].set(token_ids)
    return (slot_index, target, owner)


def to_expert_major(arrived, groups, local_experts):
    capacity = arrived.shape[1]
    width = arrived.shape[2]
    return (
        arrived.reshape(groups, local_experts, capacity, width)
        .transpose(1, 0, 2, 3)
        .reshape(local_experts, groups * capacity, width)
    )


def from_expert_major(results, groups):
    local_experts = results.shape[0]
    width = results.shape[2]
    capacity = results.shape[1] // groups
    return (
        results.reshape(local_experts, groups, capacity, width)
        .transpose(1, 0, 2, 3)
        .reshape(groups * local_experts, capacity, width)
    )


def exchange_body(
    block_input,
    segments,
    counts,
    routes,
    attn_gain,
    w_query,
    w_latent,
    latent_gain,
    w_keyval,
    w_output,
    ffn_gain,
    w_router,
    shared_gate_up,
    shared_down,
    expert_gate_up,
    expert_down,
    cotangent,
):
    gathered = (
        lax.all_gather(attn_gain, "dp", axis=0, tiled=True),
        lax.all_gather(w_query, "dp", axis=0, tiled=True),
        lax.all_gather(w_latent, "dp", axis=0, tiled=True),
        lax.all_gather(latent_gain, "dp", axis=0, tiled=True),
        lax.all_gather(w_keyval, "dp", axis=0, tiled=True),
        lax.all_gather(w_output, "dp", axis=1, tiled=True),
        lax.all_gather(ffn_gain, "dp", axis=0, tiled=True),
        lax.all_gather(w_router, "dp", axis=0, tiled=True),
        lax.all_gather(shared_gate_up, "dp", axis=1, tiled=True),
        lax.all_gather(shared_down, "dp", axis=1, tiled=True),
    )
    (
        full_attn_gain,
        query_weight,
        latent_weight,
        full_latent_gain,
        keyval_weight,
        output_weight,
        full_ffn_gain,
        router_weight,
        shared_in,
        shared_out,
    ) = gathered
    tensor_rank = lax.axis_index("tensor")
    dp_size = lax.axis_size("dp")
    rows_all = lax.all_gather(block_input, "tensor", axis=0, tiled=True)
    tokens = rows_all.shape[0]
    local_rows = block_input.shape[0]
    heads = query_weight.shape[1] // (NOPE + ROPE)
    experts = router_weight.shape[1]
    local_experts = expert_gate_up.shape[0]
    capacity = 2 * tokens * TOP // experts
    scale = (NOPE + ROPE) ** (-0.5)
    start = tensor_rank * local_rows
    cosine, sine = rotary_tables(segments[0], ROPE)
    allowed = allowed_pairs(segments[0], counts[0])
    attn_gain_wide = full_attn_gain.astype(jnp.float32)
    latent_gain_wide = full_latent_gain.astype(jnp.float32)
    ffn_gain_wide = full_ffn_gain.astype(jnp.float32)
    inputs = rows_all.astype(jnp.float32)
    first_scale = rms_scale(inputs)
    first_unit = inputs * first_scale
    first_normed = (first_unit * attn_gain_wide).astype(jnp.bfloat16)
    query = jnp.dot(first_normed, query_weight, preferred_element_type=jnp.float32).reshape(
        tokens, heads, NOPE + ROPE
    )
    query_rows = jnp.concatenate(
        [query[..., :NOPE], rotate(query[..., NOPE:], cosine[:, None, :], sine[:, None, :])],
        axis=-1,
    ).astype(jnp.bfloat16)
    latent_all = jnp.dot(first_normed, latent_weight, preferred_element_type=jnp.float32)
    latent = latent_all[:, :KVR]
    key_rope = rotate(latent_all[:, KVR:], cosine, sine).astype(jnp.bfloat16)
    latent_scale = rms_scale(latent)
    latent_unit = latent * latent_scale
    latent_normed = (latent_unit * latent_gain_wide).astype(jnp.bfloat16)
    keyval = (
        jnp.dot(latent_normed, keyval_weight, preferred_element_type=jnp.float32)
        .astype(jnp.bfloat16)
        .reshape(tokens, heads, NOPE + VD)
    )
    key_nope = keyval[..., :NOPE]
    values = keyval[..., NOPE:]
    scores = attention_scores(query_rows, key_nope, key_rope, allowed, scale)
    row_max = jnp.max(scores, axis=-1, keepdims=True)
    log_total = row_max + jnp.log(jnp.sum(jnp.exp(scores - row_max), axis=-1, keepdims=True))
    weights_low = jnp.exp(scores - log_total).astype(jnp.bfloat16)
    attended = (
        jnp.einsum("hij,jhd->ihd", weights_low, values, preferred_element_type=jnp.float32)
        .astype(jnp.bfloat16)
        .reshape(tokens, heads * VD)
    )
    attn_part = jnp.dot(attended, output_weight, preferred_element_type=jnp.float32)
    mixed = inputs + lax.psum(attn_part, "tensor")
    second_scale = rms_scale(mixed)
    second_unit = mixed * second_scale
    second_normed = (second_unit * ffn_gain_wide).astype(jnp.bfloat16)
    logits = jnp.dot(second_normed, router_weight, preferred_element_type=jnp.float32)
    probabilities = jax.nn.softmax(logits, axis=-1)
    gate_values = jnp.take_along_axis(probabilities, routes, axis=1)
    shared_pre = jnp.einsum(
        "td,gdf->tgf", second_normed, shared_in, preferred_element_type=jnp.float32
    )
    shared_hidden = (jax.nn.silu(shared_pre[:, 0]) * shared_pre[:, 1]).astype(jnp.bfloat16)
    shared_part = jnp.dot(shared_hidden, shared_out, preferred_element_type=jnp.float32)
    slot_index, target, owner = slot_layout(routes, experts, capacity)
    owner_grid = owner.reshape(experts, capacity)
    padded_rows = jnp.concatenate([second_normed, jnp.zeros((1, D), jnp.bfloat16)], axis=0)
    outgoing = padded_rows[owner_grid]
    arrived = lax.all_to_all(outgoing, "dp", split_axis=0, concat_axis=0, tiled=True)
    expert_rows = to_expert_major(arrived, dp_size, local_experts)
    expert_pre = jnp.einsum(
        "erd,egdf->ergf", expert_rows, expert_gate_up, preferred_element_type=jnp.float32
    )
    expert_hidden = (jax.nn.silu(expert_pre[:, :, 0]) * expert_pre[:, :, 1]).astype(jnp.bfloat16)
    expert_result = jnp.einsum(
        "erf,efd->erd", expert_hidden, expert_down, preferred_element_type=jnp.float32
    )
    returning = from_expert_major(expert_result, dp_size)
    returned = lax.all_to_all(
        returning.astype(jnp.bfloat16), "dp", split_axis=0, concat_axis=0, tiled=True
    ).astype(returning.dtype)
    padded_back = jnp.concatenate([returned.reshape(-1, D), jnp.zeros((1, D), jnp.float32)], axis=0)
    picked = padded_back[target].reshape(tokens, TOP, D)
    routed_part = jnp.sum(gate_values[:, :, None] * picked, axis=1)
    branch_sum = lax.psum_scatter(
        (shared_part + routed_part).astype(jnp.bfloat16), "tensor", scatter_dimension=0, tiled=True
    ).astype(jnp.float32)
    block_output = lax.dynamic_slice_in_dim(mixed, start, local_rows, 0) + branch_sum
    grad_rows = lax.all_gather(cotangent, "tensor", axis=0, tiled=True)
    grad_out = grad_rows.astype(jnp.float32)
    grad_shared_hidden = jnp.dot(grad_rows, shared_out.T, preferred_element_type=jnp.float32)
    grad_shared_out = jnp.dot(shared_hidden.T, grad_rows, preferred_element_type=jnp.float32)
    grad_shared_pre = swiglu_back(shared_pre[:, 0], shared_pre[:, 1], grad_shared_hidden, 1).astype(
        jnp.bfloat16
    )
    grad_shared_in = jnp.einsum(
        "td,tgf->gdf", second_normed, grad_shared_pre, preferred_element_type=jnp.float32
    )
    grad_second = jnp.einsum(
        "tgf,gdf->td", grad_shared_pre, shared_in, preferred_element_type=jnp.float32
    )
    gate_by_slot = (
        jnp.zeros((experts * capacity + 1,), jnp.float32).at[target].set(gate_values.reshape(-1))
    )
    slot_ids = jnp.arange(experts * capacity, dtype=jnp.int32).reshape(experts, capacity)
    padded_grad = jnp.concatenate([grad_out, jnp.zeros((1, D), jnp.float32)], axis=0)
    grad_outgoing = (gate_by_slot[slot_ids][..., None] * padded_grad[owner_grid]).astype(
        jnp.bfloat16
    )
    grad_arrived = lax.all_to_all(grad_outgoing, "dp", split_axis=0, concat_axis=0, tiled=True)
    grad_expert_rows = to_expert_major(grad_arrived, dp_size, local_experts)
    grad_expert_hidden = jnp.einsum(
        "erd,efd->erf", grad_expert_rows, expert_down, preferred_element_type=jnp.float32
    )
    grad_expert_down = jnp.einsum(
        "erf,erd->efd", expert_hidden, grad_expert_rows, preferred_element_type=jnp.float32
    )
    grad_expert_pre = swiglu_back(
        expert_pre[:, :, 0], expert_pre[:, :, 1], grad_expert_hidden, 2
    ).astype(jnp.bfloat16)
    grad_expert_gate_up = jnp.einsum(
        "erd,ergf->egdf", expert_rows, grad_expert_pre, preferred_element_type=jnp.float32
    )
    grad_expert_input = jnp.einsum(
        "ergf,egdf->erd", grad_expert_pre, expert_gate_up, preferred_element_type=jnp.float32
    )
    grad_returning = from_expert_major(grad_expert_input, dp_size)
    grad_returned = lax.all_to_all(
        grad_returning.astype(jnp.bfloat16), "dp", split_axis=0, concat_axis=0, tiled=True
    ).astype(grad_returning.dtype)
    padded_grad_back = jnp.concatenate(
        [grad_returned.reshape(-1, D), jnp.zeros((1, D), jnp.float32)], axis=0
    )
    grad_second = grad_second + jnp.sum(padded_grad_back[target].reshape(tokens, TOP, D), axis=1)
    grad_gates = jnp.sum(grad_out[:, None, :] * picked, axis=-1)
    grad_second, grad_gates = (
        lax.psum(grad_second.astype(jnp.bfloat16), "tensor").astype(jnp.float32),
        lax.psum(grad_gates.astype(jnp.bfloat16), "tensor").astype(jnp.float32),
    )
    chosen = (routes[:, :, None] == jnp.arange(experts, dtype=jnp.int32)[None, None, :]).astype(
        jnp.float32
    )
    grad_probabilities = jnp.sum(chosen * grad_gates[:, :, None], axis=1)
    grad_logits = probabilities * (
        grad_probabilities - jnp.sum(probabilities * grad_probabilities, axis=-1, keepdims=True)
    )
    grad_logits_low = grad_logits.astype(jnp.bfloat16)
    grad_router = jnp.dot(second_normed.T, grad_logits_low, preferred_element_type=jnp.float32)
    grad_second = grad_second + jnp.dot(
        grad_logits_low, router_weight.T, preferred_element_type=jnp.float32
    )
    gain_ffn_grad = jnp.sum(grad_second * second_unit, axis=0)
    grad_mixed = grad_out + rms_back(grad_second * ffn_gain_wide, second_unit, second_scale)
    grad_attn_low = grad_mixed.astype(jnp.bfloat16)
    grad_output_weight = jnp.dot(attended.T, grad_attn_low, preferred_element_type=jnp.float32)
    grad_attended = (
        jnp.dot(grad_attn_low, output_weight.T, preferred_element_type=jnp.float32)
        .astype(jnp.bfloat16)
        .reshape(tokens, heads, VD)
    )
    scores = attention_scores(query_rows, key_nope, key_rope, allowed, scale)
    weights = jnp.exp(scores - log_total)
    weights_low = weights.astype(jnp.bfloat16)
    grad_weights = jnp.einsum(
        "ihd,jhd->hij", grad_attended, values, preferred_element_type=jnp.float32
    )
    grad_values = jnp.einsum(
        "hij,ihd->jhd", weights_low, grad_attended, preferred_element_type=jnp.float32
    )
    grad_scores = (
        weights * (grad_weights - jnp.sum(weights * grad_weights, axis=-1, keepdims=True))
    ).astype(jnp.bfloat16)
    grad_query_nope = (
        jnp.einsum("hij,jhd->ihd", grad_scores, key_nope, preferred_element_type=jnp.float32)
        * scale
    )
    grad_query_rope = (
        jnp.einsum("hij,jd->ihd", grad_scores, key_rope, preferred_element_type=jnp.float32) * scale
    )
    grad_key_nope = (
        jnp.einsum(
            "hij,ihd->jhd", grad_scores, query_rows[..., :NOPE], preferred_element_type=jnp.float32
        )
        * scale
    )
    grad_key_rope = (
        jnp.einsum(
            "hij,ihd->jd", grad_scores, query_rows[..., NOPE:], preferred_element_type=jnp.float32
        )
        * scale
    )
    grad_query = (
        jnp.concatenate(
            [grad_query_nope, rotate_back(grad_query_rope, cosine[:, None, :], sine[:, None, :])],
            axis=-1,
        )
        .astype(jnp.bfloat16)
        .reshape(tokens, heads * (NOPE + ROPE))
    )
    grad_query_weight = jnp.dot(first_normed.T, grad_query, preferred_element_type=jnp.float32)
    grad_first = jnp.dot(grad_query, query_weight.T, preferred_element_type=jnp.float32)
    grad_keyval = (
        jnp.concatenate([grad_key_nope, grad_values], axis=-1)
        .astype(jnp.bfloat16)
        .reshape(tokens, heads * (NOPE + VD))
    )
    grad_keyval_weight = jnp.dot(latent_normed.T, grad_keyval, preferred_element_type=jnp.float32)
    grad_latent_normed = jnp.dot(grad_keyval, keyval_weight.T, preferred_element_type=jnp.float32)
    gain_latent_part = jnp.sum(grad_latent_normed * latent_unit, axis=0)
    grad_latent = rms_back(grad_latent_normed * latent_gain_wide, latent_unit, latent_scale)
    grad_latent_all = jnp.concatenate(
        [grad_latent, rotate_back(grad_key_rope, cosine, sine)], axis=-1
    )
    grad_first, grad_latent_all, gain_latent_grad = (
        lax.psum(grad_first.astype(jnp.bfloat16), "tensor").astype(jnp.float32),
        lax.psum(grad_latent_all.astype(jnp.bfloat16), "tensor").astype(jnp.float32),
        lax.psum(gain_latent_part.astype(jnp.bfloat16), "tensor").astype(jnp.float32),
    )
    grad_latent_low = grad_latent_all.astype(jnp.bfloat16)
    grad_latent_weight = jnp.dot(
        first_normed.T, grad_latent_low, preferred_element_type=jnp.float32
    )
    grad_first = grad_first + jnp.dot(
        grad_latent_low, latent_weight.T, preferred_element_type=jnp.float32
    )
    gain_attn_grad = jnp.sum(grad_first * first_unit, axis=0)
    grad_inputs = grad_mixed + rms_back(grad_first * attn_gain_wide, first_unit, first_scale)
    grad_local = lax.dynamic_slice_in_dim(grad_inputs, start, local_rows, 0)
    summed = (
        lax.psum_scatter(gain_attn_grad, "dp", scatter_dimension=0, tiled=True),
        lax.psum_scatter(grad_query_weight, "dp", scatter_dimension=0, tiled=True),
        lax.psum_scatter(grad_latent_weight, "dp", scatter_dimension=0, tiled=True),
        lax.psum_scatter(gain_latent_grad, "dp", scatter_dimension=0, tiled=True),
        lax.psum_scatter(grad_keyval_weight, "dp", scatter_dimension=0, tiled=True),
        lax.psum_scatter(grad_output_weight, "dp", scatter_dimension=1, tiled=True),
        lax.psum_scatter(gain_ffn_grad, "dp", scatter_dimension=0, tiled=True),
        lax.psum_scatter(grad_router, "dp", scatter_dimension=0, tiled=True),
        lax.psum_scatter(grad_shared_in, "dp", scatter_dimension=1, tiled=True),
        lax.psum_scatter(grad_shared_out, "dp", scatter_dimension=1, tiled=True),
    )
    return (
        block_output,
        grad_local,
        summed[0],
        summed[1],
        summed[2],
        summed[3],
        summed[4],
        summed[5],
        summed[6],
        summed[7],
        summed[8],
        summed[9],
        grad_expert_gate_up,
        grad_expert_down,
    )


RINGS = 4


def ring_step(values):
    return lax.ppermute(values, "dp", [(i, (i + RINGS) % 16) for i in range(16)])


def other_y(values):
    return lax.ppermute(values, "dp", [(i, i ^ 2) for i in range(16)])


def other_core(values):
    return lax.ppermute(values, "dp", [(i, i ^ 1) for i in range(16)])


def other_x(values):
    return lax.ppermute(values, "tensor", [(0, 1), (1, 0)])


def fence_kernel(*refs):
    pass


def after(values, *others):
    anywhere = pl.BlockSpec(memory_space=pl.ANY)
    return pl.pallas_call(
        fence_kernel,
        out_shape=jax.ShapeDtypeStruct(values.shape, values.dtype),
        in_specs=[anywhere] * (1 + len(others)),
        out_specs=anywhere,
        input_output_aliases={0: 0},
    )(values, *others)


def gather_whole(rows, early):
    ring = [rows, ring_step(rows)]
    ring.append(ring_step(ring[1]))
    ring.append(ring_step(after(ring[2], early)))
    over_x = [other_x(part) for part in ring]
    groups = []
    for k in (0, 2):
        held = jnp.concatenate(ring[k : k + 2], axis=0)
        across = jnp.concatenate(over_x[k : k + 2], axis=0)
        beside = other_y(held)
        groups.append((held, beside, across, other_y(across) if k else other_x(beside)))
    return groups, ring, over_x


def gather_rows(rows, corners):
    held = [rows, ring_step(rows)]
    first = (other_y(rows), other_x(rows))
    held.append(ring_step(after(held[1], *first)))
    held.append(ring_step(held[2]))
    groups = []
    for k, current in enumerate((held[0], held[1], jnp.concatenate(held[2:], axis=0))):
        beside, across = (other_y(current), other_x(current)) if k else first
        corner = other_x(beside) if corners[k] == "x" else other_y(across)
        groups.append((current, beside, across, corner))
    return held, groups


def add_low(first, second):
    return (first.astype(jnp.float32) + second.astype(jnp.float32)).astype(jnp.bfloat16)


def turn_corner(plane, direction):
    own, beside, across, corner = plane
    if direction == "x":
        return own, add_low(beside, other_x(corner)), across
    return own, beside, add_low(across, other_y(corner))


def close_plane(turned):
    own, beside, across = turned
    return own, other_y(beside), other_x(across)


def wide_sum(*values):
    total = values[0].astype(jnp.float32)
    for value in values[1:]:
        total = total + value.astype(jnp.float32)
    return total


def ring_sum(parts, low):
    moving = parts[1]
    for distance in (2, 3, 0):
        moving = ring_step(moving.astype(low)).astype(jnp.float32) + parts[distance].astype(
            jnp.float32
        )
    return moving


def ring_shards(shard):
    held = [shard]
    for _ in range(RINGS - 1):
        held.append(ring_step(held[-1]))
    return held


def gather_weight(shard, early):
    held, besides = [shard], []
    for distance in range(RINGS):
        beside = other_y(after(held[1], *early) if distance == 1 else held[distance])
        besides.append(beside)
        if distance < RINGS - 1:
            source = after(held[distance], besides[distance - 1]) if distance else shard
            held.append(ring_step(source))
    chunks = []
    for distance, (current, beside) in enumerate(zip(held, besides)):
        for flip_y, chunk in ((0, current), (1, beside)):
            for flip_core, piece in ((0, chunk), (1, other_core(chunk))):
                chunks.append(((distance, flip_y, flip_core), piece))
    return chunks, held, besides


def place_of(coords, key):
    z, y, core = coords
    distance, flip_y, flip_core = key
    return (
        lax.rem(z + RINGS - distance, RINGS) * 4
        + (1 - y if flip_y else y) * 2
        + (1 - core if flip_core else core)
    )


def weight_keys():
    return [
        (distance, flip_y, flip_core)
        for flip_core in (0, 1)
        for flip_y in (0, 1)
        for distance in range(RINGS)
    ]


def scatter_blocks(grads, low):
    half = grads.shape[0] // 2
    total = grads[:half].astype(jnp.float32) + other_core(grads[half:].astype(low)).astype(
        jnp.float32
    )
    quarter = half // 2
    total = total[:quarter] + other_y(total[quarter:].astype(low)).astype(jnp.float32)
    size = quarter // RINGS
    return ring_sum([total[r * size : (r + 1) * size] for r in range(RINGS)], low)


def pick_blocks(values, order):
    chosen = order[:, None] == jnp.arange(values.shape[0], dtype=jnp.int32)[None, :]
    chosen = chosen.reshape(chosen.shape + (1,) * (values.ndim - 1))
    return jnp.sum(jnp.where(chosen, values[None], 0.0), axis=1)


def wide_dot(left, right):
    return jnp.dot(left, right, preferred_element_type=jnp.float32)


def dot_turned(left, right):
    return lax.dot_general(left, right, (((1,), (1,)), ((), ())), preferred_element_type=jnp.float32)


def dot_rows(left, right):
    return lax.dot_general(left, right, (((0,), (0,)), ((), ())), preferred_element_type=jnp.float32)


TILE = 256


def whole(array):
    return pl.BlockSpec(array.shape, lambda *i: (0,) * array.ndim)


def in_vmem(count):
    return [pl.BlockSpec(memory_space=pltpu.VMEM)] * count


def in_place(count):
    return [pl.BlockSpec(memory_space=pl.ANY)] * count


def head_scores(heads, h, nope_ref, turned_ref, keyval_ref, key_ref, masks):
    span = ROPE // 2 * heads
    column = pl.ds(pl.multiple_of(h * NOPE, NOPE), NOPE)
    key_column = pl.ds(pl.multiple_of(h * (NOPE + VD), NOPE), NOPE)
    scores = dot_turned(nope_ref[:, column], keyval_ref[:, key_column])
    for k in (0, 1):
        part = turned_ref[:, k * span : (k + 1) * span]
        part = jnp.where(masks, part, jnp.zeros_like(part))
        scores += dot_turned(part, key_ref[:, k * span : (k + 1) * span])
    return scores * (NOPE + ROPE) ** (-0.5)


def head_lanes(heads, h):
    span = ROPE // 2 * heads
    lane = lax.broadcasted_iota(jnp.int32, (1, span), 1)
    return (lane >= h * (ROPE // 2)) & (lane < (h + 1) * (ROPE // 2))


def allowed_rows(count, segment_row, segment_column):
    tokens = segment_row.shape[1]
    column = lax.broadcasted_iota(jnp.int32, (tokens, tokens), 0)
    row = lax.broadcasted_iota(jnp.int32, (tokens, tokens), 1)
    live = (column < count) & (row < count) & (row <= column)
    return (segment_row == segment_column) & live | (column == row)


def attend_kernel(
    keys,
    extra,
    heads,
    sizes,
    place_ref,
    segment_row_ref,
    segment_column_ref,
    cosine_ref,
    sine_ref,
    own_ref,
    other_ref,
    *refs,
):
    depth, query_width, used, latent_depth, keyval_part, first_width = sizes
    chunks = refs[: len(keys)]
    (
        own_out,
        sent_out,
        first_ref,
        keyval_weight_ref,
        output_ref,
        normed_ref,
        nope_ref,
        turned_ref,
        latent_ref,
        key_ref,
        keyval_ref,
        total_ref,
        attended_ref,
        gains_ref,
        latent_gain_ref,
        semaphores,
    ) = refs[len(keys) + extra :]
    f32, bf16 = jnp.float32, jnp.bfloat16
    local_rows = own_ref.shape[0]
    tokens = 2 * local_rows
    coords = (place_ref[0], place_ref[1], place_ref[2])
    x = place_ref[3]
    copies = []
    parts = depth // latent_depth
    for key, chunk in zip(keys, chunks):
        block = place_of(coords, key)
        rows = pl.ds(pl.multiple_of(block * depth, depth), depth)
        small_rows = pl.ds(pl.multiple_of(block * latent_depth, latent_depth), latent_depth)
        moves = [(chunk.at[:, pl.ds(0, first_width)], first_ref.at[rows])]
        for k in range(parts):
            moves.append(
                (
                    chunk.at[
                        pl.ds(k * latent_depth, latent_depth), pl.ds(first_width, keyval_part)
                    ],
                    keyval_weight_ref.at[small_rows, pl.ds(k * keyval_part, keyval_part)],
                )
            )
        moves.append(
            (
                chunk.at[:, pl.ds(first_width + keyval_part, heads * VD)],
                output_ref.at[rows],
            )
        )
        for source, target in moves:
            copies.append(pltpu.make_async_copy(source, target, semaphores.at[len(copies)]))
    for copy in copies:
        copy.start()
    for copy in copies:
        copy.wait()

    edge = query_width + KVR
    spread = jnp.transpose(first_ref[:, edge:].astype(f32))[used - edge : used - edge + 8]
    gains_ref[...] = spread
    gain = spread[0:1]
    source = lax.broadcasted_iota(jnp.int32, (D, KVR), 0)
    target = lax.broadcasted_iota(jnp.int32, (D, KVR), 1)
    wanted = target // latent_depth * depth + target % latent_depth
    chosen = jnp.where(source == wanted, 1.0, 0.0).astype(bf16)
    latent_gain = wide_dot(spread.astype(bf16), chosen)[2:3]
    latent_gain_ref[...] = latent_gain
    for ref, start in ((own_ref, x * local_rows), (other_ref, (1 - x) * local_rows)):
        rows = ref[...].astype(f32)
        unit = rows * lax.rsqrt(jnp.mean(rows * rows, axis=1, keepdims=True) + EPSILON)
        normed_ref[pl.ds(pl.multiple_of(start, local_rows), local_rows), :] = (unit * gain).astype(
            bf16
        )
    nope_width = heads * NOPE
    span = heads * (ROPE // 2)
    half = nope_width // 2
    for k in (0, 1):
        nope_ref[:, k * half : (k + 1) * half] = wide_dot(
            normed_ref[...], first_ref[:, k * half : (k + 1) * half]
        ).astype(bf16)
    turning = wide_dot(normed_ref[...], first_ref[:, nope_width : nope_width + 2 * span])
    cosine, sine = cosine_ref[...], sine_ref[...]
    first, second = turning[:, :span], turning[:, span:]
    turned_ref[:, :span] = (first * cosine - second * sine).astype(bf16)
    turned_ref[:, span:] = (second * cosine + first * sine).astype(bf16)
    latent = wide_dot(normed_ref[...], first_ref[:, query_width : query_width + KVR])
    latent_ref[...] = latent
    tail = wide_dot(normed_ref[...], first_ref[:, query_width + KVR :])
    lane = lax.broadcasted_iota(jnp.int32, (1, tail.shape[1]), 1)
    swapped = jnp.where(
        lane < ROPE // 2,
        -pltpu.roll(tail, tail.shape[1] - ROPE // 2, 1),
        pltpu.roll(tail, ROPE // 2, 1),
    )
    width = tail.shape[1]
    turned_key = tail * cosine[:, :width] + swapped * sine[:, :width]
    turned_key = jnp.where(lane < ROPE, turned_key, 0.0).astype(bf16)
    source = lax.broadcasted_iota(jnp.int32, (width, 2 * span), 0)
    target = lax.broadcasted_iota(jnp.int32, (width, 2 * span), 1)
    wanted = target % (ROPE // 2) + jnp.where(target < span, 0, ROPE // 2)
    key_ref[...] = wide_dot(turned_key, (source == wanted).astype(bf16)).astype(bf16)
    unit = latent * lax.rsqrt(jnp.mean(latent * latent, axis=1, keepdims=True) + EPSILON)
    latent_normed = (unit * latent_gain).astype(bf16)
    half = keyval_ref.shape[1] // 4
    for k in range(4):
        keyval_ref[:, k * half : (k + 1) * half] = wide_dot(
            latent_normed, keyval_weight_ref[:, k * half : (k + 1) * half]
        ).astype(bf16)
    allowed = allowed_rows(place_ref[4], segment_row_ref[...], segment_column_ref[...])
    total_lane = lax.broadcasted_iota(jnp.int32, total_ref.shape, 1)
    total_ref[...] = jnp.zeros_like(total_ref)

    def one_head(h, _):
        scores = head_scores(
            heads, h, nope_ref, turned_ref, keyval_ref, key_ref, head_lanes(heads, h)
        )
        scores = jnp.where(allowed, scores, -1e30)
        most = jnp.max(scores, axis=1, keepdims=True)
        total = most + jnp.log(jnp.sum(jnp.exp(scores - most), axis=1, keepdims=True))
        weights = jnp.exp(scores - total).astype(bf16)
        total_ref[...] += jnp.where(total_lane == h, total, 0.0)
        value_column = pl.ds(pl.multiple_of(h * (NOPE + VD) + NOPE, NOPE), VD)
        attended_ref[:, pl.ds(pl.multiple_of(h * VD, VD), VD)] = wide_dot(
            weights, keyval_ref[:, value_column]
        ).astype(bf16)
        return 0

    lax.fori_loop(0, heads, one_head, 0)
    own = pl.ds(pl.multiple_of(x * local_rows, local_rows), local_rows)
    other = pl.ds(pl.multiple_of((1 - x) * local_rows, local_rows), local_rows)
    pieces = 4
    size = output_ref.shape[0] // pieces
    for k in range(pieces):
        columns = slice(k * size, (k + 1) * size)
        own_out[:, columns] = dot_turned(attended_ref[own, :], output_ref[columns, :])
        sent_out[:, columns] = dot_turned(attended_ref[other, :], output_ref[columns, :]).astype(
            bf16
        )


def attend_forward(place, segments, cosine, sine, own, other, chunks, heads, sizes, others):
    depth, query_width, used, latent_depth, keyval_part, first_width = sizes
    f32, bf16 = jnp.float32, jnp.bfloat16
    keys = [key for key, _ in chunks]
    local_rows = own.shape[0]
    tokens = 2 * local_rows
    span = heads * (ROPE // 2)
    shapes = [
        ((local_rows, D), f32),
        ((local_rows, D), bf16),
        ((D, first_width), bf16),
        ((KVR, heads * (NOPE + VD)), bf16),
        ((D, heads * VD), bf16),
        ((tokens, D), bf16),
        ((tokens, heads * NOPE), bf16),
        ((tokens, 2 * span), bf16),
        ((tokens, KVR), f32),
        ((tokens, 2 * span), bf16),
        ((tokens, heads * (NOPE + VD)), bf16),
        ((tokens, 128), f32),
        ((tokens, heads * VD), bf16),
        ((8, D), f32),
        ((1, KVR), f32),
    ]
    return pl.pallas_call(
        functools.partial(attend_kernel, keys, len(others), heads, sizes),
        out_shape=[jax.ShapeDtypeStruct(*shape) for shape in shapes],
        in_specs=[pl.BlockSpec(memory_space=pltpu.SMEM)]
        + in_vmem(6)
        + in_place(len(chunks) + len(others)),
        out_specs=in_vmem(len(shapes)),
        scratch_shapes=[
            pltpu.SemaphoreType.DMA((len(chunks) * (2 + depth // latent_depth),))
        ],
        compiler_params=pltpu.CompilerParams(vmem_limit_bytes=48 * 1024 * 1024),
        cost_estimate=pl.CostEstimate(
            flops=2 * tokens * D * (first_width + heads * VD + 1024),
            bytes_accessed=4 * D * (first_width + 1536),
            transcendentals=2 * heads * tokens * tokens,
        ),
    )(
        place,
        segments,
        segments.T,
        cosine,
        sine,
        own,
        other,
        *[piece for _, piece in chunks],
        *others,
    )


def attend_back_kernel(
    heads,
    place_ref,
    segment_row_ref,
    segment_column_ref,
    cosine_ref,
    sine_ref,
    own_ref,
    other_ref,
    keyval_weight_ref,
    output_ref,
    nope_ref,
    turned_ref,
    latent_ref,
    key_ref,
    keyval_ref,
    total_ref,
    latent_gain_ref,
    projected_ref,
    keyval_grad_ref,
    latent_out,
    gain_ref,
    grad_ref,
    turn_ref,
    back_ref,
):
    f32, bf16 = jnp.float32, jnp.bfloat16
    local_rows = own_ref.shape[0]
    x = place_ref[3]
    span = heads * (ROPE // 2)
    nope_width = heads * NOPE
    query_width = nope_width + 2 * span
    scale = (NOPE + ROPE) ** (-0.5)
    for ref, start in ((own_ref, x * local_rows), (other_ref, (1 - x) * local_rows)):
        rows = pl.ds(pl.multiple_of(start, local_rows), local_rows)
        for k in (0, 1):
            half = slice(k * nope_width // 2, (k + 1) * nope_width // 2)
            grad_ref[rows, half] = wide_dot(ref[...], output_ref[:, half]).astype(bf16)
    allowed = allowed_rows(place_ref[4], segment_row_ref[...], segment_column_ref[...])
    total_lane = lax.broadcasted_iota(jnp.int32, total_ref.shape, 1)
    turn_ref[...] = jnp.zeros_like(turn_ref)
    back_ref[...] = jnp.zeros_like(back_ref)

    def one_head(h, _):
        mask = head_lanes(heads, h)
        scores = head_scores(heads, h, nope_ref, turned_ref, keyval_ref, key_ref, mask)
        total = jnp.sum(jnp.where(total_lane == h, total_ref[...], 0.0), axis=1, keepdims=True)
        weights = jnp.exp(jnp.where(allowed, scores, -1e30) - total)
        weights_low = weights.astype(bf16)
        column = pl.ds(pl.multiple_of(h * NOPE, NOPE), NOPE)
        key_column = pl.ds(pl.multiple_of(h * (NOPE + VD), NOPE), NOPE)
        value_column = pl.ds(pl.multiple_of(h * (NOPE + VD) + NOPE, NOPE), VD)
        grads = grad_ref[:, column]
        grad_weights = dot_turned(grads, keyval_ref[:, value_column])
        keyval_grad_ref[:, value_column] = dot_rows(weights_low, grads).astype(bf16)
        grad_scores = (
            weights * (grad_weights - jnp.sum(weights * grad_weights, axis=1, keepdims=True))
        ).astype(bf16)
        projected_ref[:, column] = (
            scale * wide_dot(grad_scores, keyval_ref[:, key_column])
        ).astype(bf16)
        keyval_grad_ref[:, key_column] = (
            scale * dot_rows(grad_scores, nope_ref[:, column])
        ).astype(bf16)
        for k in (0, 1):
            part = slice(k * span, (k + 1) * span)
            turn = wide_dot(grad_scores, key_ref[:, part])
            turn_ref[:, part] += jnp.where(mask, turn, 0.0)
            own = turned_ref[:, part]
            own = jnp.where(mask, own, jnp.zeros_like(own))
            back_ref[:, part] += dot_rows(grad_scores, own)
        return 0

    lax.fori_loop(0, heads, one_head, 0)
    cosine, sine = cosine_ref[...], sine_ref[...]
    first, second = scale * turn_ref[:, :span], scale * turn_ref[:, span:]
    projected_ref[:, nope_width : nope_width + span] = (first * cosine + second * sine).astype(bf16)
    projected_ref[:, nope_width + span : query_width] = (second * cosine - first * sine).astype(
        bf16
    )
    folded = []
    for k in (0, 1):
        part = scale * back_ref[:, k * span : (k + 1) * span]
        shift = span // 2
        while shift >= ROPE // 2:
            part = part + pltpu.roll(part, shift, 1)
            shift //= 2
        folded.append(part)
    width = projected_ref.shape[1] - query_width - KVR
    lane = lax.broadcasted_iota(jnp.int32, (1, width), 1)
    first = (folded[0] * cosine + folded[1] * sine)[:, :width]
    second = (folded[1] * cosine - folded[0] * sine)[:, :width]
    projected_ref[:, query_width + KVR :] = jnp.where(
        lane < ROPE // 2, first, jnp.where(lane < ROPE, second, 0.0)
    ).astype(bf16)
    gain = latent_gain_ref[...]
    latent = latent_ref[...]
    row_scale = lax.rsqrt(jnp.mean(latent * latent, axis=1, keepdims=True) + EPSILON)
    unit = latent * row_scale
    latent_out[...] = (unit * gain).astype(bf16)
    grad_normed = dot_turned(keyval_grad_ref[...], keyval_weight_ref[...])
    gain_ref[...] = jnp.sum(grad_normed * unit, axis=0, keepdims=True)
    grad_unit = grad_normed * gain
    projected_ref[:, query_width : query_width + KVR] = (
        row_scale * (grad_unit - unit * jnp.mean(grad_unit * unit, axis=1, keepdims=True))
    ).astype(bf16)


def attend_back(place, segments, cosine, sine, own, other, saved, heads, first_width, others):
    f32, bf16 = jnp.float32, jnp.bfloat16
    keyval = saved[6]
    tokens = 2 * own.shape[0]
    span = heads * (ROPE // 2)
    return pl.pallas_call(
        lambda *refs: attend_back_kernel(heads, *refs[:16], *refs[16 + len(others) :]),
        out_shape=[
            jax.ShapeDtypeStruct((tokens, first_width), bf16),
            jax.ShapeDtypeStruct((tokens, keyval.shape[1]), bf16),
            jax.ShapeDtypeStruct((tokens, KVR), bf16),
            jax.ShapeDtypeStruct((1, KVR), f32),
        ],
        in_specs=[pl.BlockSpec(memory_space=pltpu.SMEM)] + in_vmem(15) + in_place(len(others)),
        out_specs=in_vmem(4),
        scratch_shapes=[
            pltpu.VMEM((tokens, heads * NOPE), bf16),
            pltpu.VMEM((tokens, 2 * span), f32),
            pltpu.VMEM((tokens, 2 * span), f32),
        ],
        compiler_params=pltpu.CompilerParams(vmem_limit_bytes=48 * 1024 * 1024),
        cost_estimate=pl.CostEstimate(
            flops=2 * tokens * D * 3000,
            bytes_accessed=2 * D * 1536,
            transcendentals=heads * tokens * tokens,
        ),
    )(
        place,
        segments,
        segments.T,
        cosine,
        sine,
        own,
        other,
        *saved,
        *others,
    )


def first_grads_kernel(extra, places_ref, left_ref, right_ref, small_ref, *refs):
    out_ref = refs[-1]
    size = left_ref.shape[1]
    edge = right_ref.shape[1] - small_ref.shape[0]
    result = dot_rows(left_ref[...], right_ref[...])
    for value, some in (
        (result[:, :edge], slice(0, edge)),
        (result[:, edge:] + jnp.transpose(small_ref[...]), slice(edge, right_ref.shape[1])),
    ):
        if extra:
            value = value + refs[0][:, some].astype(jnp.float32)
        out_ref[:, some] = value.astype(jnp.bfloat16)


def other_grads_kernel(first, extra, places_ref, latent_ref, keyval_ref, grad_ref, attended_ref, *refs):
    out_ref, keyval_all = refs[-2:]
    step = pl.program_id(0)
    size = grad_ref.shape[1]
    latent_size = latent_ref.shape[1] // places_ref.shape[0]
    parts = size // latent_size
    columns = keyval_ref.shape[1] // parts

    @pl.when(step == 0)
    def _():
        for k in range(parts):
            some = slice(k * columns, (k + 1) * columns)
            keyval_all[:, some] = dot_rows(latent_ref[...], keyval_ref[:, some])

    start = pl.multiple_of(places_ref[first + step] * latent_size, latent_size)
    strip = keyval_all[pl.ds(start, latent_size), :]
    keyval = jnp.concatenate([strip[:, k * columns : (k + 1) * columns] for k in range(parts)], axis=0)
    output = dot_rows(grad_ref[...], attended_ref[...])
    for value, some in (
        (keyval, slice(0, columns)),
        (output, slice(columns, columns + output.shape[1])),
    ):
        if extra:
            value = value + refs[0][:, some].astype(jnp.float32)
        out_ref[:, some] = value.astype(jnp.bfloat16)


def still(array):
    return pl.BlockSpec(array.shape, lambda i, where: (0, 0))


def grads_call(
    kernel, specs, operands, scratch, size, width, places, first, count, arrived, others
):
    extra = [] if arrived is None else [arrived]
    return pl.pallas_call(
        lambda *refs: kernel(
            len(extra),
            *refs[: 1 + len(operands) + len(extra)],
            *refs[1 + len(operands) + len(extra) + len(others) :],
        ),
        grid_spec=pltpu.PrefetchScalarGridSpec(
            num_scalar_prefetch=1,
            grid=(count,),
            in_specs=specs
            + [pl.BlockSpec((size, width), lambda i, where: (first + i, 0))] * len(extra)
            + in_place(len(others)),
            out_specs=pl.BlockSpec((size, width), lambda i, where: (i, 0)),
            scratch_shapes=scratch,
        ),
        out_shape=jax.ShapeDtypeStruct((count * size, width), jnp.bfloat16),
        compiler_params=pltpu.CompilerParams(vmem_limit_bytes=32 * 1024 * 1024),
        cost_estimate=pl.CostEstimate(
            flops=1024 * count * size * width,
            bytes_accessed=4 * count * size * width,
            transcendentals=0,
        ),
    )(places, *operands, *extra, *others)


def first_grads(left, right, small, places, first, count, arrived=None, others=()):
    rows, width = right.shape
    size = left.shape[1] // places.shape[0]
    specs = [
        pl.BlockSpec((rows, size), lambda i, where: (0, where[first + i])),
        still(right),
        pl.BlockSpec((small.shape[0], size), lambda i, where: (0, where[first + i])),
    ]
    return grads_call(
        first_grads_kernel,
        specs,
        (left, right, small),
        [],
        size,
        width,
        places,
        first,
        count,
        arrived,
        others,
    )


def other_grads(latent, keyval, grad, attended, places, first, count, arrived=None, others=()):
    rows = grad.shape[0]
    blocks = places.shape[0]
    size = grad.shape[1] // blocks
    parts = size // (latent.shape[1] // blocks)
    width = keyval.shape[1] // parts + attended.shape[1]
    specs = [
        still(latent),
        still(keyval),
        pl.BlockSpec((rows, size), lambda i, where: (0, where[first + i])),
        still(attended),
    ]
    scratch = [pltpu.VMEM((latent.shape[1], keyval.shape[1]), jnp.float32)]
    return grads_call(
        functools.partial(other_grads_kernel, first),
        specs,
        (latent, keyval, grad, attended),
        scratch,
        size,
        width,
        places,
        first,
        count,
        arrived,
        others,
    )


def first_back_kernel(place_ref, own_ref, other_ref, grad_ref, weight_ref, own_out, sent_out, gain_ref):
    local_rows = own_ref.shape[0]
    x = place_ref[3]
    size = weight_ref.shape[0] // 4
    for ref, start, out in (
        (own_ref, x * local_rows, own_out),
        (other_ref, (1 - x) * local_rows, sent_out),
    ):
        rows = ref[...].astype(jnp.float32)
        unit = rows * lax.rsqrt(jnp.mean(rows * rows, axis=1, keepdims=True) + EPSILON)
        grads = grad_ref[pl.ds(pl.multiple_of(start, local_rows), local_rows), :]
        for k in range(4):
            some = slice(k * size, (k + 1) * size)
            part = dot_turned(grads, weight_ref[some, :])
            out[:, some] = part.astype(out.dtype)
            gain = jnp.sum(part * unit[:, some], axis=0, keepdims=True)
            if ref is own_ref:
                gain_ref[:, some] = gain
            else:
                gain_ref[:, some] += gain


def first_back(place, own, other, grads, weight):
    f32, bf16 = jnp.float32, jnp.bfloat16
    depth = weight.shape[0]
    return pl.pallas_call(
        first_back_kernel,
        out_shape=[
            jax.ShapeDtypeStruct(own.shape, f32),
            jax.ShapeDtypeStruct(own.shape, bf16),
            jax.ShapeDtypeStruct((1, depth), f32),
        ],
        in_specs=[pl.BlockSpec(memory_space=pltpu.SMEM)] + in_vmem(4),
        out_specs=in_vmem(3),
        compiler_params=pltpu.CompilerParams(vmem_limit_bytes=32 * 1024 * 1024),
        cost_estimate=pl.CostEstimate(
            flops=4 * own.shape[0] * weight.shape[0] * weight.shape[1],
            bytes_accessed=2 * weight.shape[0] * weight.shape[1],
            transcendentals=0,
        ),
    )(place, own, other, grads, weight)


def close_ring(near, arrived, last):
    size = near.shape[0] // RINGS
    total = near.astype(jnp.float32) + arrived.astype(jnp.float32)
    parts = [total[r * size : (r + 1) * size] for r in range(RINGS)]
    parts[0] = after(parts[0], last)
    return ring_sum(parts, jnp.bfloat16)


def pack_kernel(heads, query_ref, latent_ref, small_ref, keyval_ref, output_ref, out_ref):
    half = ROPE // 2
    head = NOPE + ROPE
    nope_width = heads * NOPE
    for h in range(heads):
        start = h * head
        out_ref[:, h * NOPE : (h + 1) * NOPE] = query_ref[:, start : start + NOPE]
        for k in (0, 1):
            to = nope_width + k * heads * half + h * half
            out_ref[:, to : to + half] = query_ref[
                :, start + NOPE + k * half : start + NOPE + (k + 1) * half
            ]
    at = heads * head
    edge = at + KVR
    out_ref[:, at:edge] = latent_ref[:, :KVR]
    out_ref[:, edge : edge + 128] = jnp.concatenate([latent_ref[:, KVR:], small_ref[...]], axis=1)
    at = edge + 128
    size = keyval_ref.shape[0]
    parts = out_ref.shape[0] // size
    part = keyval_ref.shape[1] // parts
    for k in range(parts):
        out_ref[k * size : (k + 1) * size, at : at + part] = keyval_ref[
            :, k * part : (k + 1) * part
        ]
    out_ref[:, at + part :] = jnp.transpose(output_ref[...].astype(jnp.float32)).astype(
        jnp.bfloat16
    )


def pack_weights(query, latent, small, keyval, output):
    depth, query_width = query.shape
    heads = query_width // (NOPE + ROPE)
    width = query_width + KVR + 128 + keyval.size // depth + output.shape[0]
    return pl.pallas_call(
        functools.partial(pack_kernel, heads),
        out_shape=jax.ShapeDtypeStruct((depth, width), jnp.bfloat16),
        in_specs=in_vmem(5),
        out_specs=pl.BlockSpec(memory_space=pltpu.VMEM),
    )(query, latent, small, keyval, output)


def load_pieces(pieces, starts, target, semaphores):
    size = target.shape[0] // len(pieces)
    copies = [
        pltpu.make_async_copy(
            piece.at[pl.ds(start, size)], target.at[pl.ds(k * size, size)], semaphores.at[k]
        )
        for k, (piece, start) in enumerate(zip(pieces, starts))
    ]
    for copy in copies:
        copy.start()
    for copy in copies:
        copy.wait()


def shared_stride(shared):
    return -(-shared // 32) * 32


def pack_shared_kernel(blocks, shared, in_ref, down_ref, out_ref):
    stride = shared_stride(shared)
    out_ref[...] = jnp.zeros_like(out_ref)
    for k in range(3):
        if k < 2:
            units = jnp.transpose(in_ref[k].astype(jnp.float32)).astype(jnp.bfloat16)
        else:
            units = down_ref[...]
        for b in range(blocks):
            out_ref[b, k * stride : k * stride + shared] = units[b * shared : (b + 1) * shared]


def pack_shared(shared_in, shared_down, blocks, others):
    depth = shared_in.shape[1]
    shared = shared_down.shape[0] // blocks
    return pl.pallas_call(
        lambda in_ref, down_ref, *refs: pack_shared_kernel(
            blocks, shared, in_ref, down_ref, refs[-1]
        ),
        out_shape=jax.ShapeDtypeStruct((blocks, 3 * shared_stride(shared), depth), jnp.bfloat16),
        in_specs=in_vmem(2) + in_place(len(others)),
        out_specs=pl.BlockSpec(memory_space=pltpu.VMEM),
    )(shared_in, shared_down, *others)


def unpack_shared_kernel(shared, packed_ref, in_ref, down_ref, units_ref):
    stride = shared_stride(shared)
    blocks = packed_ref.shape[0]
    for k in range(3):
        target = down_ref if k == 2 else units_ref
        for b in range(blocks):
            target[b * shared : (b + 1) * shared, :] = packed_ref[
                b, k * stride : k * stride + shared
            ].astype(jnp.float32)
        if k < 2:
            in_ref[k] = jnp.transpose(units_ref[...])


def unpack_shared(packed, shared, others):
    blocks, _, depth = packed.shape
    return pl.pallas_call(
        lambda packed_ref, *refs: unpack_shared_kernel(shared, packed_ref, *refs[len(others) :]),
        out_shape=[
            jax.ShapeDtypeStruct((2, depth, blocks * shared), jnp.float32),
            jax.ShapeDtypeStruct((blocks * shared, depth), jnp.float32),
        ],
        in_specs=in_vmem(1) + in_place(len(others)),
        out_specs=in_vmem(2),
        scratch_shapes=[pltpu.VMEM((blocks * shared, depth), jnp.float32)],
    )(packed, *others)


def pack_units_kernel(units, shared, own_in, other_in, own_down, other_down, near, far, *refs):
    outs = refs[-3:]
    hole = -(-units // TILE) * TILE
    stride = shared_stride(shared)
    columns = outs[0].shape[1]
    size = near.shape[2]
    for k, out in enumerate(outs):
        first = own_in[0, k] if k < 2 else own_down[0]
        second = other_in[0, k] if k < 2 else other_down[0]
        out[:units] = first
        out[units:hole] = jnp.zeros((hole - units, columns), jnp.bfloat16)
        out[hole : hole + units] = second
        out[hole + units : 2 * hole] = jnp.zeros((hole - units, columns), jnp.bfloat16)
        out[2 * hole :] = jnp.zeros((TILE, columns), jnp.bfloat16)
        for b in range(columns // size):
            part = slice(b * size, (b + 1) * size)
            for at, ref in ((2 * hole, near), (2 * hole + stride, far)):
                out[at : at + shared, part] = ref[b, k * stride : k * stride + shared]


def pack_units(own_in, other_in, own_down, other_down, near, far, shared, others):
    units, depth = own_down.shape[1:]
    size = near.shape[2]
    height = 2 * (-(-units // TILE) * TILE) + TILE
    columns = 2 * size
    in_spec = pl.BlockSpec((1, 2, units, columns), lambda i: (0, 0, 0, i))
    down_spec = pl.BlockSpec((1, units, columns), lambda i: (0, 0, i))
    narrow = pl.BlockSpec((2,) + near.shape[1:], lambda i: (i, 0, 0))
    return pl.pallas_call(
        functools.partial(pack_units_kernel, units, shared),
        grid=(depth // columns,),
        in_specs=[in_spec, in_spec, down_spec, down_spec, narrow, narrow]
        + in_place(len(others)),
        out_specs=[pl.BlockSpec((height, columns), lambda i: (0, i))] * 3,
        out_shape=[jax.ShapeDtypeStruct((height, depth), jnp.bfloat16)] * 3,
        compiler_params=pltpu.CompilerParams(vmem_limit_bytes=32 * 1024 * 1024),
        cost_estimate=pl.CostEstimate(
            flops=0, bytes_accessed=12 * height * depth, transcendentals=0
        ),
    )(own_in, other_in, own_down, other_down, near, far, *others)


def expert_grads_kernel(units, count, extra, right_ref, *refs):
    out = refs[-1]
    for k in range(count):

        @pl.when(pl.program_id(0) == k)
        def _():
            result = dot_rows(refs[k][...], right_ref[...])[:units]
            if extra:
                result += refs[count][0, 0].astype(jnp.float32)
            out[0, 0] = result.astype(out.dtype)


def expert_grads(lefts, right, units, column, arrived, kind, others=()):
    total, depth = right.shape
    wide = -(-units // TILE) * TILE
    extra = [] if arrived is None else [arrived]
    out = pl.BlockSpec((1, 1, units, 2 * TILE), lambda k, i: (0, k, 0, i))
    side = pl.BlockSpec((total, wide), lambda k, i: (0, column))
    return pl.pallas_call(
        functools.partial(expert_grads_kernel, units, len(lefts), len(extra)),
        grid=(len(lefts), depth // (2 * TILE)),
        in_specs=[pl.BlockSpec((total, 2 * TILE), lambda k, i: (0, i))]
        + [side] * len(lefts)
        + [out] * len(extra)
        + in_place(len(others)),
        out_specs=out,
        out_shape=jax.ShapeDtypeStruct((1, len(lefts), units, depth), kind),
        compiler_params=pltpu.CompilerParams(vmem_limit_bytes=48 * 1024 * 1024),
        cost_estimate=pl.CostEstimate(
            flops=2 * len(lefts) * total * depth * wide,
            bytes_accessed=2 * len(lefts) * total * (depth + wide) + 8 * depth * units,
            transcendentals=0,
        ),
    )(right, *lefts, *extra, *others)


def side_grads_kernel(shared, rows_ref, cots_ref, gate_ref, up_ref, hidden_ref, logit_ref, *outs):
    kept_ref, sent_ref, router_ref = outs
    stride = shared_stride(shared)
    size = kept_ref.shape[2]
    for k, (left, right) in enumerate(
        ((gate_ref, rows_ref), (up_ref, rows_ref), (hidden_ref, cots_ref))
    ):
        result = dot_rows(left[...], right[...])
        for b in range(kept_ref.shape[0]):
            part = slice(b * size, (b + 1) * size)
            kept_ref[b, k * stride : (k + 1) * stride] = result[:stride, part]
            sent_ref[b, k * stride : (k + 1) * stride] = result[
                stride : 2 * stride, part
            ].astype(jnp.bfloat16)
    router_ref[...] = dot_rows(logit_ref[...], rows_ref[...])


def side_grads(rows, cots, gate, up, hidden, logits, shared, blocks, others):
    total, depth = rows.shape
    column = gate.shape[1] // TILE - 1
    size = depth // blocks
    stride = shared_stride(shared)
    wide = pl.BlockSpec((total, 2 * TILE), lambda i: (0, i))
    side = pl.BlockSpec((total, TILE), lambda i: (0, column))
    packed = pl.BlockSpec((2 * TILE // size, 3 * stride, size), lambda i: (i, 0, 0))
    return pl.pallas_call(
        lambda *refs: side_grads_kernel(shared, *refs[:6], *refs[6 + len(others) :]),
        grid=(depth // (2 * TILE),),
        in_specs=[wide, wide, side, side, side, whole(logits)] + in_place(len(others)),
        out_specs=[packed, packed, pl.BlockSpec((logits.shape[1], 2 * TILE), lambda i: (0, i))],
        out_shape=[
            jax.ShapeDtypeStruct((blocks, 3 * stride, size), jnp.float32),
            jax.ShapeDtypeStruct((blocks, 3 * stride, size), jnp.bfloat16),
            jax.ShapeDtypeStruct((logits.shape[1], depth), jnp.float32),
        ],
        compiler_params=pltpu.CompilerParams(vmem_limit_bytes=48 * 1024 * 1024),
        cost_estimate=pl.CostEstimate(
            flops=8 * total * depth * TILE,
            bytes_accessed=4 * total * depth,
            transcendentals=0,
        ),
    )(rows, cots, gate, up, hidden, logits, *others)


def down_kernel(starts, *refs):
    count = len(starts)
    pieces, weight_ref = refs[:count], refs[count]
    grads_ref, rows_ref, semaphores = refs[-3:]

    @pl.when(pl.program_id(0) == 0)
    def _():
        load_pieces(pieces, starts, rows_ref, semaphores)

    size = rows_ref.shape[0] // 2
    for k in range(2):
        part = slice(k * size, (k + 1) * size)
        grads_ref[part, :] = dot_turned(rows_ref[part, :], weight_ref[...]).astype(jnp.bfloat16)


def down_grads(part, pieces, size, down, kept, others):
    count = len(pieces)
    depth = down.shape[1]
    width = down.shape[0]
    rows = count * size
    return pl.pallas_call(
        functools.partial(down_kernel, tuple(start for _, start in pieces)),
        grid=(width // TILE,),
        in_specs=in_place(count)
        + [pl.BlockSpec((TILE, depth), lambda i: (i, 0))]
        + in_place(len(kept) + len(others)),
        out_specs=[
            pl.BlockSpec((rows, TILE), lambda i: (part, i)),
            pl.BlockSpec((rows, depth), lambda i: (part, 0)),
        ],
        out_shape=[
            jax.ShapeDtypeStruct((2 * rows, width), jnp.bfloat16),
            jax.ShapeDtypeStruct((2 * rows, depth), jnp.bfloat16),
        ],
        scratch_shapes=[pltpu.SemaphoreType.DMA((count,))],
        input_output_aliases={count + 1 + k: k for k in range(len(kept))},
        compiler_params=pltpu.CompilerParams(vmem_limit_bytes=48 * 1024 * 1024),
        cost_estimate=pl.CostEstimate(
            flops=2 * rows * depth * width,
            bytes_accessed=2 * (2 * rows * depth + depth * width + rows * width),
            transcendentals=0,
        ),
    )(*[array for array, _ in pieces], down, *kept, *others)


def out_kernel(pieces, hidden_ref, weight_ref, *refs):
    outs, done_ref = refs[-1 - pieces : -1], refs[-1]
    size = hidden_ref.shape[0] // (RINGS * pieces)
    done_ref[...] = jnp.zeros_like(done_ref)
    for r in range(RINGS):
        part = hidden_ref[r * pieces * size : (r + 1) * pieces * size, :]
        result = wide_dot(part, weight_ref[...]).astype(jnp.bfloat16)
        for k in range(pieces):
            outs[k][r * size : (r + 1) * size, :] = result[k * size : (k + 1) * size]


def out_rows(pieces, half, hidden, down, kept, others):
    rows, width = hidden.shape
    depth = down.shape[1]
    steps = depth // (2 * TILE)
    results = pl.pallas_call(
        functools.partial(out_kernel, pieces),
        grid=(steps,),
        in_specs=[whole(hidden), pl.BlockSpec((width, TILE), lambda i: (0, half * steps + i))]
        + in_place(len(kept) + len(others)),
        out_specs=[pl.BlockSpec((rows // pieces, TILE), lambda i: (0, half * steps + i))] * pieces
        + [pl.BlockSpec((8, 128), lambda i: (0, 0))],
        out_shape=[jax.ShapeDtypeStruct((rows // pieces, depth), jnp.bfloat16)] * pieces
        + [jax.ShapeDtypeStruct((8, 128), jnp.float32)],
        input_output_aliases={2 + k: k for k in range(len(kept))},
        compiler_params=pltpu.CompilerParams(vmem_limit_bytes=48 * 1024 * 1024),
        cost_estimate=pl.CostEstimate(
            flops=rows * depth * width,
            bytes_accessed=rows * depth + depth * width + 2 * rows * width,
            transcendentals=0,
        ),
    )(hidden, down, *kept, *others)
    return results[:-1], results[-1]


def mlp_kernel(tiles, starts, others, experts_ref, routed_ref, *refs):
    pieces = len(starts)
    row_refs = refs[:pieces]
    router_ref, gate_col, up_col, down_grad, gate_row, up_row = refs[pieces : pieces + 6]
    outs = refs[pieces + 6 + others :]
    grad_refs = outs[:pieces]
    rows_out, hidden_out, gate_out, up_out, logit_out = outs[pieces : pieces + 5]
    gate_all, up_all, prob_ref, scale_ref, sum_ref, semaphores = outs[pieces + 5 :]
    step = pl.program_id(0)
    third = tiles // 2
    total = rows_out.shape[0]
    size = total // pieces
    lane = lax.broadcasted_iota(jnp.int32, (1, router_ref.shape[1]), 1) - experts_ref[3]

    @pl.when(step == 0)
    def _():
        load_pieces(row_refs, starts, rows_out, semaphores)
        logits = wide_dot(rows_out[...], router_ref[...])
        logits = jnp.where((lane >= 0) & (lane < experts_ref[2]), logits, -1e30)
        raised = jnp.exp(logits - jnp.max(logits, axis=1, keepdims=True))
        chances = raised / jnp.sum(raised, axis=1, keepdims=True)
        prob_ref[...] = chances
        for k in (0, 1):
            chance = jnp.sum(jnp.where(lane == experts_ref[k], chances, 0.0), axis=1, keepdims=True)
            scale_ref[k] = routed_ref[:, k : k + 1] * chance
        scale_ref[2] = jnp.ones_like(scale_ref[2])
        sum_ref[...] = jnp.zeros_like(sum_ref)

    @pl.when(step < tiles)
    def _():
        columns = pl.ds(pl.multiple_of(step * TILE, TILE), TILE)
        kind = step // third
        half = total // 2
        for k in (0, 1):
            part = slice(k * half, (k + 1) * half)
            pre_gate = dot_turned(rows_out[part, :], gate_col[...])
            pre_up = dot_turned(rows_out[part, :], up_col[...])
            grads = down_grad[part, :].astype(jnp.float32)
            scale = scale_ref[kind, part, :]
            sigmoid = 1.0 / (1.0 + jnp.exp(-pre_gate))
            silu = pre_gate * sigmoid
            hidden = (silu * pre_up).astype(jnp.bfloat16).astype(jnp.float32)
            sum_ref[kind, part, :] += jnp.sum(hidden * grads, axis=1, keepdims=True)
            grad_hidden = scale * grads
            low_gate = (grad_hidden * pre_up * (sigmoid + silu * (1.0 - sigmoid))).astype(
                jnp.bfloat16
            )
            low_up = (grad_hidden * silu).astype(jnp.bfloat16)
            gate_all[part, columns] = low_gate
            up_all[part, columns] = low_up
            hidden_out[part, :] = (scale * hidden).astype(jnp.bfloat16)
            gate_out[part, :] = low_gate
            up_out[part, :] = low_up

    @pl.when(step == tiles - 1)
    def _():
        grad_logits = jnp.zeros_like(prob_ref)
        for k in (0, 1):
            own = jnp.where(lane == experts_ref[k], 1.0, 0.0)
            grad_logits += scale_ref[k] * sum_ref[k] * (own - prob_ref[...])
        logit_out[...] = grad_logits.astype(jnp.bfloat16)

    @pl.when(step >= tiles)
    def _():
        some = pl.ds(pl.multiple_of((step - tiles) * 2 * TILE, TILE), 2 * TILE)
        grads = wide_dot(gate_all[...], gate_row[...]) + wide_dot(up_all[...], up_row[...])
        grads += dot_turned(logit_out[...], router_ref[some, :])
        grads = grads.astype(jnp.bfloat16)
        for k in range(pieces):
            grad_refs[k][...] = grads[k * size : (k + 1) * size]


def mlp_plane(distance, experts, routed, rows, down_grad, router, weights, kept, others):
    gate, up = weights
    pieces = len(rows)
    width, depth = gate.shape
    size = routed.shape[0] // pieces
    tiles, columns = width // TILE, depth // (2 * TILE)
    total = pieces * size
    low = jnp.bfloat16

    def early(i):
        return jnp.minimum(i, tiles - 1)

    def late(i):
        return jnp.maximum(i - tiles, 0)

    tile_spec = pl.BlockSpec((total, TILE), lambda i: (distance, early(i)))
    anywhere = pl.BlockSpec(memory_space=pl.ANY)
    first_kept = 2 + pieces + 6
    results = pl.pallas_call(
        functools.partial(
            mlp_kernel, tiles, tuple(start for _, start in rows), len(kept) + len(others)
        ),
        grid=(tiles + columns,),
        in_specs=[pl.BlockSpec(memory_space=pltpu.SMEM), whole(routed)]
        + [anywhere] * pieces
        + [
            pl.BlockSpec((depth, 128), lambda i: (0, router.shape[1] // 128 - 1)),
            pl.BlockSpec((TILE, depth), lambda i: (early(i), 0)),
            pl.BlockSpec((TILE, depth), lambda i: (early(i), 0)),
            tile_spec,
            pl.BlockSpec((width, 2 * TILE), lambda i: (0, late(i))),
            pl.BlockSpec((width, 2 * TILE), lambda i: (0, late(i))),
        ]
        + [anywhere] * (len(kept) + len(others)),
        out_specs=[pl.BlockSpec((size, 2 * TILE), lambda i: (0, late(i)))] * pieces
        + [
            pl.BlockSpec((total, depth), lambda i: (distance, 0)),
            tile_spec,
            tile_spec,
            tile_spec,
            pl.BlockSpec((total, 128), lambda i: (distance, 0)),
        ],
        out_shape=[jax.ShapeDtypeStruct((size, depth), low)] * pieces
        + [
            jax.ShapeDtypeStruct((RINGS * total, many), low)
            for many in (depth, width, width, width, 128)
        ],
        scratch_shapes=[pltpu.VMEM((total, width), low)] * 2
        + [
            pltpu.VMEM((total, 128), jnp.float32),
            pltpu.VMEM((3, total, 1), jnp.float32),
            pltpu.VMEM((3, total, 1), jnp.float32),
            pltpu.SemaphoreType.DMA((pieces,)),
        ],
        input_output_aliases={first_kept + k: pieces + k for k in range(len(kept))},
        compiler_params=pltpu.CompilerParams(vmem_limit_bytes=48 * 1024 * 1024),
        cost_estimate=pl.CostEstimate(
            flops=2 * total * depth * width * 4,
            bytes_accessed=2 * (4 * depth * width + 3 * total * depth + 4 * total * width),
            transcendentals=total * width,
        ),
    )(experts, routed, *[array for array, _ in rows], router, gate, up, down_grad, gate, up, *kept, *others)
    return results[:pieces], results[pieces:]


def gather_body(
    block_input,
    segments,
    counts,
    routes,
    attn_gain,
    w_query,
    w_latent,
    latent_gain,
    w_keyval,
    w_output,
    ffn_gain,
    w_router,
    shared_gate_up,
    shared_down,
    expert_gate_up,
    expert_down,
    cotangent,
):
    f32 = jnp.float32
    bf16 = jnp.bfloat16
    blocks = 16
    index = lax.axis_index("dp")
    x = lax.axis_index("tensor")
    coords = jnp.stack([index // 4, (index // 2) % 2, index % 2]).astype(jnp.int32)
    core = coords[2]
    place = jnp.concatenate([coords, x.astype(jnp.int32)[None], counts])
    local_rows = block_input.shape[0]
    tokens = 2 * local_rows
    depth = w_query.shape[0]
    query_width = w_query.shape[1]
    heads = query_width // (NOPE + ROPE)
    experts = w_router.shape[1]
    units = expert_gate_up.shape[3]
    shared = shared_gate_up.shape[2] // blocks
    latent_depth = w_keyval.shape[0]

    used = query_width + KVR + ROPE
    small = jnp.concatenate(
        [
            attn_gain[:, None],
            ffn_gain[:, None],
            jnp.pad(latent_gain, (0, depth - latent_depth))[:, None],
            w_router,
            routes.reshape(depth, -1).astype(bf16),
            jnp.zeros((depth, 128 - ROPE - 3 - experts - 2 * TOP), bf16),
        ],
        axis=1,
    )
    first_width = query_width + KVR + 128
    shards = pack_weights(w_query, w_latent, small, w_keyval, w_output)
    other_input = other_x(block_input)
    expert_in = expert_gate_up.swapaxes(2, 3)
    expert_in_other = other_core(expert_in)
    expert_down_other = other_core(expert_down)
    chunks, held, besides = gather_weight(
        shards, (expert_in_other, expert_down_other, other_input)
    )
    shared_near = lax.all_to_all(
        pack_shared(shared_gate_up, shared_down, blocks, (held[3],)),
        "dp",
        split_axis=0,
        concat_axis=0,
        tiled=True,
    )
    shared_far = other_core(shared_near)

    grad_groups, grad_ring, grad_across = gather_whole(
        after(cotangent, held[3], besides[2]), besides[3]
    )

    cosine, sine = rotary_tables(segments[0], ROPE)
    cosine = jnp.tile(cosine, (1, heads))
    sine = jnp.tile(sine, (1, heads))
    sizes = (depth, query_width, used, latent_depth, w_keyval.shape[1] * latent_depth // depth, first_width)
    (
        own_part,
        sent_part,
        first_weight,
        keyval_weight,
        output_turned,
        first_normed,
        nope,
        turned_query,
        latent,
        key,
        keyval,
        total,
        attended,
        gains,
        latent_gain_row,
    ) = attend_forward(
        place,
        segments,
        cosine,
        sine,
        block_input,
        other_input,
        chunks,
        heads,
        sizes,
        (grad_ring[2], grad_across[0], grad_across[1]),
    )
    attn_gain_wide, ffn_gain_wide = gains[0], gains[1]
    mixed = block_input.astype(f32) + own_part + other_x(sent_part).astype(f32)
    second_scale = rms_scale(mixed)
    second_unit = mixed * second_scale
    second_normed = (second_unit * ffn_gain_wide).astype(bf16)

    routes_at = used + 3 + experts
    routes_all = first_weight[:, routes_at : routes_at + 2 * TOP].reshape(blocks * tokens, TOP)
    chip_experts = jnp.stack([index, index + 1 - 2 * core]).astype(jnp.int32)
    routed_all = jnp.any(
        routes_all[None] == chip_experts[:, None, None].astype(bf16), axis=2
    ).astype(f32)
    order = jnp.stack(
        [
            place_of(coords, (distance, flip_y, 0)) * 2 + (1 - x if flip_x else x)
            for distance in range(RINGS)
            for flip_x, flip_y in ((0, 0), (0, 1), (1, 0), (1, 1))
        ]
    )
    routed = jnp.stack(
        [
            pick_blocks(one.reshape(blocks * 2, local_rows), order).reshape(RINGS, -1)
            for one in routed_all
        ],
        axis=2,
    )

    corners = "yxyx"
    row_ring, row_groups = gather_rows(second_normed, "yyx")
    row_planes = [
        [(array, 0) for array in row_groups[0]],
        [(array, 0) for array in row_groups[1]],
        [(array, 0) for array in row_groups[2]],
        [(array, local_rows) for array in row_groups[2]],
    ]

    gate_weight, up_weight, down_weight = pack_units(
        expert_in,
        expert_in_other,
        expert_down,
        expert_down_other,
        shared_near,
        shared_far,
        shared,
        (second_normed,),
    )
    half_kept = down_grads(
        0,
        [(array, r * local_rows) for r in (0, 1) for array in grad_groups[0]],
        local_rows,
        down_weight,
        (),
        (row_ring[1],),
    )
    down_grad, every_grad = down_grads(
        1,
        [(array, r * local_rows) for r in (0, 1) for array in grad_groups[1]],
        local_rows,
        down_weight,
        half_kept,
        (row_ring[2],),
    )
    expert_ids = jnp.concatenate(
        [chip_experts, jnp.array([experts, used + 3 - query_width - KVR], jnp.int32)]
    )
    kept = []
    planes = []
    turned, closed = [None] * RINGS, [None] * RINGS
    for distance in range(RINGS):
        others = [row_ring[3]] if distance == 0 else []
        if distance == 1:
            others = list(row_groups[2][1:3])
        elif distance == 3:
            others = list(turned[0][1:])
        grads, kept = mlp_plane(
            distance,
            expert_ids,
            routed[distance],
            row_planes[distance],
            down_grad,
            first_weight,
            (gate_weight, up_weight),
            kept,
            others,
        )
        planes.append(list(grads))
        if distance:
            before = planes[distance - 1]
            k = 1 if corners[distance - 1] == "x" else 2
            before[k] = after(before[k], grads[3])
            turned[distance - 1] = turn_corner(before, corners[distance - 1])
            closed[distance - 1] = close_plane(turned[distance - 1])
    turned[3] = turn_corner(planes[3], corners[3])
    first_part = closed[1]
    closed[1] = (after(first_part[0], planes[3][3]),) + tuple(first_part[1:])
    every_row, every_hidden, every_gate_grad, every_up_grad, logit_grads = kept
    first_total = wide_sum(*closed[1]).astype(bf16)
    shared_kept, shared_sent, logit_rows = side_grads(
        every_row,
        every_grad,
        every_gate_grad,
        every_up_grad,
        every_hidden,
        logit_grads,
        shared,
        blocks,
        (first_total,),
    )
    sent_down = expert_grads((every_hidden,), every_grad, units, 1, None, bf16, (shared_sent,))
    half_outs, half_done = out_rows(4, 0, every_hidden, down_weight, (), (sent_down,))
    moving = ring_step(first_total)
    moving = ring_step(wide_sum(moving, *closed[2]).astype(bf16))
    own, beside, across = turned[3]
    own = after(own, sent_down)
    grad_close = close_plane((own, after(beside, shared_sent), across))
    grad_second = wide_sum(
        ring_step(wide_sum(moving, *grad_close).astype(bf16)),
        after(closed[0][0], half_done),
        *closed[0][1:],
    )

    arrived_down = other_core(sent_down)
    router_at = used + 3 - query_width - KVR
    grad_router = logit_rows[router_at : router_at + experts]
    shared_came = other_core(shared_sent)

    gain_ffn_part = jnp.sum(grad_second * second_unit, axis=0)
    grad_mixed = cotangent.astype(f32) + rms_back(
        grad_second * ffn_gain_wide, second_unit, second_scale
    )
    grad_mixed_low = grad_mixed.astype(bf16)
    other_grad = other_x(grad_mixed_low)
    outs, outs_done = out_rows(4, 1, every_hidden, down_weight, half_outs, (grad_mixed_low,))
    outs = list(outs)
    outs[2] = after(outs[2], other_grad)
    outs[3] = after(outs[3], other_grad)


    places = jnp.stack([place_of(coords, key_of) for key_of in weight_keys()]).astype(jnp.int32)
    projected_grad, keyval_grad, latent_normed, gain_latent_part = attend_back(
        place,
        segments,
        cosine,
        sine,
        grad_mixed_low,
        other_grad,
        (keyval_weight, output_turned, nope, turned_query, latent, key, keyval, total, latent_gain_row),
        heads,
        first_width,
        (arrived_down, shared_came, outs_done),
    )
    grad_attn = jnp.concatenate(
        [
            jnp.where(x == 0, grad_mixed_low, other_grad),
            jnp.where(x == 0, other_grad, grad_mixed_low),
        ],
        axis=0,
    )
    ring_places = places.reshape(2, 2, RINGS).swapaxes(1, 2).reshape(-1)
    other_parts = (latent_normed, keyval_grad, grad_attn, attended, ring_places)
    own_first, sent_first, gain_attn_part = first_back(
        place, block_input, other_input, projected_grad, first_weight
    )
    grad_first = own_first + other_x(sent_first).astype(f32)
    small_rows = jnp.concatenate(
        [
            jnp.zeros((ROPE, D), f32),
            gain_attn_part,
            gain_ffn_part[None],
            jnp.pad(
                gain_latent_part.reshape(blocks, latent_depth),
                ((0, 0), (0, depth - latent_depth)),
            ).reshape(1, D),
            grad_router,
            jnp.zeros((128 - ROPE - 3 - experts, D), f32),
        ],
        axis=0,
    )
    first_parts = (first_normed, projected_grad, small_rows, places)
    first_sent = first_grads(*first_parts, 8, 8, None)
    first_arrived = other_core(first_sent)
    other_arrived = other_core(other_grads(*other_parts, 8, 8, None, (first_sent,)))
    far = first_grads(*first_parts, 4, 4, first_arrived)
    other_kept = other_grads(*other_parts, 0, 8, other_arrived, (far,))
    shared_grads = lax.all_to_all(
        add_low(after(shared_kept, projected_grad), shared_came),
        "dp",
        split_axis=0,
        concat_axis=0,
        tiled=True,
    )
    from_y = other_y(far)
    arrived_in = other_core(
        expert_grads((every_gate_grad, every_up_grad), every_row, units, 1, None, bf16, (far,))
    )
    outs[1] = after(outs[1], from_y)
    near = first_grads(*first_parts, 0, 4, first_arrived, (shared_grads,))
    other_summed = ring_sum(
        [other_kept[2 * r * depth : 2 * (r + 1) * depth] for r in range(RINGS)], bf16
    )
    grad_expert_down = expert_grads(
        (every_hidden,), every_grad, units, 0, arrived_down, f32, (from_y,)
    )
    grad_expert_in = expert_grads(
        (every_gate_grad, every_up_grad), every_row, units, 0, arrived_in, f32, (near,)
    )
    first_closed = close_ring(near, from_y, from_y)
    out_own, out_beside, out_across = close_plane(turn_corner(outs, "x"))
    out_total = wide_sum(after(out_own, first_closed), out_beside, out_across)
    out_parts = [out_total[r * local_rows : (r + 1) * local_rows] for r in range(RINGS)]
    out_parts[2] = after(out_parts[2], grad_expert_in)
    block_output = mixed + ring_sum(out_parts, bf16)
    other_closed = other_summed[:depth] + other_y(
        other_summed[depth:].astype(bf16)
    ).astype(f32)
    grad_shared_in, grad_shared_down = unpack_shared(shared_grads, shared, (from_y,))
    grad_expert_gate_up = grad_expert_in.swapaxes(2, 3)
    grad_expert_down = grad_expert_down[0]
    nope_width = heads * NOPE
    span = heads * (ROPE // 2)
    grad_query_weight = jnp.concatenate(
        [
            first_closed[:, :nope_width].reshape(depth, heads, NOPE),
            first_closed[:, nope_width : nope_width + span].reshape(depth, heads, -1),
            first_closed[:, nope_width + span : query_width].reshape(depth, heads, -1),
        ],
        axis=2,
    ).reshape(depth, query_width)
    both = first_closed[:, query_width:]
    both = both + other_x(both)
    grad_latent_weight = both[:, : KVR + ROPE]
    small_grads = both[:, KVR + ROPE :].T
    keyval_columns = w_keyval.shape[1] * latent_depth // depth
    grad_keyval_weight = (
        other_closed[:, :keyval_columns]
        .reshape(-1, latent_depth, keyval_columns)
        .transpose(1, 0, 2)
        .reshape(latent_depth, -1)
    )
    grad_output_weight = other_closed[:, keyval_columns:].T
    own_inputs = block_input.astype(f32)
    own_scale = rms_scale(own_inputs)
    own_unit = own_inputs * own_scale
    grad_input = grad_mixed + rms_back(grad_first * attn_gain_wide, own_unit, own_scale)
    return (
        block_output,
        grad_input,
        small_grads[0],
        grad_query_weight,
        grad_latent_weight,
        small_grads[2, :latent_depth],
        grad_keyval_weight,
        grad_output_weight,
        small_grads[1],
        small_grads[3 : 3 + experts].T,
        grad_shared_in,
        grad_shared_down,
        grad_expert_gate_up,
        grad_expert_down,
    )


def solution(mesh):
    in_specs = (
        P(("dp", "tensor"), None),
        P("dp", None),
        P("dp"),
        P("dp", None),
        P("dp"),
        P("dp", "tensor"),
        P("dp", None),
        P("dp"),
        P("dp", "tensor"),
        P("tensor", "dp"),
        P("dp"),
        P("dp", None),
        P(None, "dp", "tensor"),
        P("tensor", "dp"),
        P("dp", None, None, "tensor"),
        P("dp", "tensor", None),
        P(("dp", "tensor"), None),
    )
    out_specs = (
        P(("dp", "tensor"), None),
        P(("dp", "tensor"), None),
        P("dp"),
        P("dp", "tensor"),
        P("dp", None),
        P("dp"),
        P("dp", "tensor"),
        P("tensor", "dp"),
        P("dp"),
        P("dp", None),
        P(None, "dp", "tensor"),
        P("tensor", "dp"),
        P("dp", None, None, "tensor"),
        P("dp", "tensor", None),
    )
    body = gather_body if mesh.shape["dp"] == 16 else exchange_body
    return jax.shard_map(body, mesh=mesh, in_specs=in_specs, out_specs=out_specs, check_vma=False)
```
